32 devices in a mesh: fsdp: 8 (over z, y), ctx: 4 (over x, core).
Axes of the slice: x: 2, y: 2, z: 4, core: 2. Of those that a mesh axis runs over, the one named last changes fastest.
Arguments:
- hidden: bfloat16 [16, 1024, 896], P('fsdp', 'ctx'), may hold values from -6 to 6
- segments: int32 [16, 1024], P('fsdp'), may hold values from 0 to 2, as said below
- attn_gain: bfloat16 [896], P(('fsdp', 'ctx')), may hold values from 0.099609375 to 1.8984375
- qkv_weight: bfloat16 [896, 1152], P(('fsdp', 'ctx')), may hold values from -0.1875 to 0.1875
- qkv_bias: bfloat16 [1152], P(('fsdp', 'ctx')), may hold values from -0.29882812 to 0.29882812
- out_weight: bfloat16 [896, 896], P(None, ('fsdp', 'ctx')), may hold values from -0.75 to 0.75
- mlp_gain: bfloat16 [896], P(('fsdp', 'ctx')), may hold values from 0.099609375 to 1.8984375
- gate_weight: bfloat16 [896, 4864], P(('fsdp', 'ctx')), may hold values from -0.1875 to 0.1875
- up_weight: bfloat16 [896, 4864], P(('fsdp', 'ctx')), may hold values from -0.1875 to 0.1875
- down_weight: bfloat16 [4864, 896], P(None, ('fsdp', 'ctx')), may hold values from -0.078125 to 0.078125
- cotangent: bfloat16 [16, 1024, 896], P('fsdp', 'ctx'), may hold values from -6 to 6
Outputs:
- output: bfloat16 [16, 1024, 896], P('fsdp', 'ctx')
- input_grad: bfloat16 [16, 1024, 896], P('fsdp', 'ctx')
- attn_gain_grad: float32 [896], P(('fsdp', 'ctx'))
- qkv_weight_grad: float32 [896, 1152], P(('fsdp', 'ctx'))
- qkv_bias_grad: float32 [1024], P(('fsdp', 'ctx'))
- value_bias_grad: float32 [128], P(('fsdp', 'ctx'))
- out_weight_grad: float32 [896, 896], P(None, ('fsdp', 'ctx'))
- mlp_gain_grad: float32 [896], P(('fsdp', 'ctx'))
- gate_weight_grad: float32 [896, 4864], P(('fsdp', 'ctx'))
- up_weight_grad: float32 [896, 4864], P(('fsdp', 'ctx'))
- down_weight_grad: float32 [4864, 896], P(None, ('fsdp', 'ctx'))
The draws below stay inside these ranges and needn't reach their ends.
Inputs may be any that keep to these rules, and one draw needn't show every extreme that they name: `segments`: along a sequence the numbers never fall; each of 0, 1 and 2 occurs, and document 1 holds positions 256 to 768.
All inputs are finite; a program needn't handle non-finite values.
Results may differ from the reference program's by a relative error of at most 0.029.
Values may be sent and summed in bfloat16 or wider, within the bound.
No kernel may reach another device: no remote copies, remote signals or barrier semaphores. Data moves between devices by JAX's collectives and lax.ppermute only.
A program may use at most 384 MiB of HBM per device.

```python
import jax
import jax.numpy as jnp
from jax import lax

D = 896
HQ = 14
KV = 2
HD = 64
FF = 4864
QKV = 1152
LEN = 1024
SEQS = 16


def draw_segments(key, part):
    key = jax.random.fold_in(key, 7)
    first_key, last_key = jax.random.split(key)
    begin_pos = jax.random.randint(first_key, (SEQS, 1), 1, LEN // 4)
    finish_pos = jax.random.randint(last_key, (SEQS, 1), 3 * LEN // 4 + 1, LEN)
    position_index = jnp.arange(LEN, dtype=jnp.int32)[None, :]
    return (position_index >= begin_pos).astype(jnp.int32) + (position_index >= finish_pos).astype(jnp.int32)


def spiked(values, stream_key, source, target, blocks, factor):
    owner, partner = [(jnp.arange(values.shape[dim]) // (values.shape[dim] // blocks)).reshape([-1 if axis == dim else 1 for axis in range(values.ndim)]) for dim in (source, target)]
    chosen = jax.random.permutation(stream_key, blocks)[partner]
    strong = (owner == chosen) | (owner == (partner + blocks // 2) % blocks)
    return jnp.where(strong, factor * values, values)


def block_levels(rng, shape, cuts, least, top_value):
    def one(dim, blocks):
        heights = jax.random.uniform(jax.random.fold_in(jax.random.fold_in(rng, 6), dim), (blocks,), jnp.float32, least / len(cuts), top_value / len(cuts))
        return jnp.repeat(jnp.exp(heights), shape[dim] // blocks).reshape((-1,) + (1,) * (len(shape) - dim - 1))

    factor_of = one(*cuts[0])
    for cut in cuts[1:]:
        factor_of = factor_of * one(*cut)
    return factor_of


def gaussian(rng, dims, deviation, most, pieces=(), held_as=jnp.bfloat16):
    loudness = block_levels(rng, dims, pieces, -0.22, 0.18) if pieces else 1.0
    entries = jax.random.normal(rng, dims, jnp.float32) * deviation * loudness
    return jnp.minimum(jnp.maximum(entries, -most), most).astype(held_as)


def heavy_noise(own_key, dims, scale, reach, cuts, heavy, kind=jnp.bfloat16):
    entries = scale * jax.random.normal(own_key, dims, jnp.float32)
    if cuts:
        entries = entries * block_levels(own_key, dims, cuts, -0.22, 0.18)
    return jnp.clip(spiked(entries, jax.random.fold_in(own_key, 3), *heavy), -reach, reach).astype(kind)


def setup_inputs(seed: int = 0) -> dict:
    arg_keys = jax.random.split(jax.random.key(seed), 12)
    return {
        "hidden": gaussian(arg_keys[0], (SEQS, LEN, D), 1.0, 6.0, ((0, 8), (1, 4))),
        "segments": draw_segments(jax.random.fold_in(arg_keys[11], 71), 0),
        "attn_gain": jnp.clip(1.0 + 0.18 * jax.random.normal(arg_keys[2], (D,), jnp.float32), 0.099609375, 1.8984375).astype(jnp.bfloat16),
        "qkv_weight": gaussian(arg_keys[3], (D, QKV), D ** -0.5, 0.1875, ((0, 32),)),
        "qkv_bias": gaussian(arg_keys[4], (QKV,), 0.05, 0.29882812, ((0, 32),)),
        "out_weight": gaussian(arg_keys[5], (HQ * HD, D), (max(HQ * HD // 16, 1)) ** -0.5, 0.75, ((1, 32),)),
        "mlp_gain": jnp.clip(1.0 + 0.18 * jax.random.normal(arg_keys[6], (D,), jnp.float32), 0.099609375, 1.8984375).astype(jnp.bfloat16),
        "gate_weight": gaussian(arg_keys[7], (D, FF), D ** -0.5, 0.1875, ((0, 32),)),
        "up_weight": gaussian(arg_keys[8], (D, FF), D ** -0.5, 0.1875, ((0, 32),)),
        "down_weight": gaussian(arg_keys[9], (FF, D), FF ** -0.5, 0.078125, ((1, 32),)),
        "cotangent": heavy_noise(arg_keys[10], (SEQS, LEN, D), 1.0, 6.0, ((0, 8), (1, 4)), (0, 2, 8, 2.0)),
    }


@jax.custom_vjp
def low(v):
    return lax.optimization_barrier(v.astype(jnp.bfloat16)).astype(jnp.float32)

@jax.custom_vjp
def low_back(v):
    return v

def low_keep(v):
    return (low(v), None)

def low_pass(kept, grad):
    return (grad,)

def back_keep(v):
    return (v, None)

def back_low(kept, grad):
    return (low(grad),)
low.defvjp(low_keep, low_pass)
low_back.defvjp(back_keep, back_low)
epsilon = 1e-06
rope_base = 1000000.0
masked_score = -1e+30

def rms_norm(values, gain_vec):
    inverse = lax.rsqrt(lax.optimization_barrier(jnp.mean(values * values, axis=-1, keepdims=True)) + epsilon)
    return values * inverse * gain_vec

def doc_positions(segment_row):
    position_index = jnp.arange(segment_row.shape[0], dtype=jnp.int32)
    changed = jnp.concatenate([jnp.ones((1,), jnp.bool_), segment_row[1:] != segment_row[:-1]])
    starts = lax.cummax(jnp.where(changed, position_index, 0).astype(jnp.int32), axis=0)
    return position_index - starts

def rotary_tables(positions, width):
    half_width = width // 2
    frequency = rope_base ** (-jnp.arange(half_width, dtype=jnp.float32) * 2.0 / width)
    angle_grid = positions.astype(jnp.float32)[:, None] * frequency[None, :]
    return (jnp.cos(angle_grid)[:, None, :], jnp.sin(angle_grid)[:, None, :])

def rotate(values, cosine, sine_table):
    half_width = values.shape[-1] // 2
    lead_half = values[..., :half_width]
    tail_half = values[..., half_width:]
    return jnp.concatenate([lead_half * cosine - tail_half * sine_table, tail_half * cosine + lead_half * sine_table], axis=-1)

def forward(tokens_in, attn_gain, qkv_weight, qkv_bias, out_weight, mlp_gain, gate_weight, up_weight, down_weight, segment_row):
    length = tokens_in.shape[0]
    group_size = HQ // KV
    q_width = HQ * HD
    kv_width = KV * HD
    highest = lax.Precision.HIGHEST
    normed = low(rms_norm(tokens_in, attn_gain))
    joined_rows = low_back(jnp.dot(normed, qkv_weight, precision=highest) + qkv_bias)
    cosine, sine_table = rotary_tables(doc_positions(segment_row), HD)
    queries = low(rotate(joined_rows[:, :q_width].reshape(length, HQ, HD), cosine, sine_table))
    key_rows = low(rotate(joined_rows[:, q_width:q_width + kv_width].reshape(length, KV, HD), cosine, sine_table))
    values = low(joined_rows[:, q_width + kv_width:].reshape(length, KV, HD))
    grouped = queries.reshape(length, KV, group_size, HD)
    raw_scores = low_back(jnp.einsum('qkgd,skd->kgqs', grouped, key_rows, precision=highest))
    position_index = jnp.arange(length, dtype=jnp.int32)
    allowed = (position_index[:, None] >= position_index[None, :]) & (segment_row[:, None] == segment_row[None, :])
    scores = jnp.where(allowed[None, None], raw_scores * HD ** (-0.5), masked_score)
    probability = low(jax.nn.softmax(scores, axis=-1))
    mixed_heads = jnp.einsum('kgqs,skd->qkgd', probability, values, precision=highest)
    attended = low(low_back(mixed_heads.reshape(length, q_width)))
    residual = tokens_in + low_back(jnp.dot(attended, out_weight, precision=highest))
    normed_post = low(rms_norm(residual, mlp_gain))
    gate_proj = low_back(jnp.dot(normed_post, gate_weight, precision=highest))
    up_proj = low_back(jnp.dot(normed_post, up_weight, precision=highest))
    activated = low(jax.nn.silu(gate_proj) * up_proj)
    return residual + jnp.dot(activated, down_weight, precision=highest)

def reference(hidden, segments, attn_gain, qkv_weight, qkv_bias, out_weight, mlp_gain, gate_weight, up_weight, down_weight, cotangent):
    weights = tuple((weight_arg.astype(jnp.float32) for weight_arg in (attn_gain, qkv_weight, qkv_bias, out_weight, mlp_gain, gate_weight, up_weight, down_weight)))

    def one_sequence(totals, step_item):
        tokens, segment_row, seed_grad = step_item

        def layer(tokens_in, *weight_list):
            return forward(tokens_in, *weight_list, segment_row)
        result, pullback = jax.vjp(layer, tokens.astype(jnp.float32), *weights)
        grads = pullback(seed_grad.astype(jnp.float32))
        totals = tuple((running + grad_one for running, grad_one in zip(totals, grads[1:])))
        return (totals, (result.astype(jnp.bfloat16), grads[0].astype(jnp.bfloat16)))
    zeros = tuple((jnp.zeros_like(weight_arg) for weight_arg in weights))
    totals, (outputs, input_grads) = lax.scan(one_sequence, zeros, (hidden, segments, cotangent))
    split_at = (HQ + KV) * HD
    bias_total = totals[2]
    return (outputs, input_grads, totals[0], totals[1], bias_total[:split_at], bias_total[split_at:]) + tuple(totals[3:])
```

```python
import functools

import jax
import jax.numpy as jnp
from jax import lax
from jax.experimental import pallas as pl
from jax.experimental.pallas import tpu as pltpu
from jax.sharding import Mesh
from jax.sharding import PartitionSpec as P

HD = 64
LANES = 128
EPSILON = 1e-06
ROPE_BASE = 1000000.0
MASKED = -1e30
SCALE = HD ** (-0.5)
TILE = 256
MIB = 1 << 20
F32 = jnp.float32
BF16 = jnp.bfloat16
AXES = ("fsdp", "cx", "cc")
CTX = ("cx", "cc")


def dot_nn(a, b):
    return lax.dot_general(a, b, (((1,), (0,)), ((), ())), preferred_element_type=F32)


def dot_nt(a, b):
    return lax.dot_general(a, b, (((1,), (1,)), ((), ())), preferred_element_type=F32)


def dot_tn(a, b):
    return lax.dot_general(a, b, (((0,), (0,)), ((), ())), preferred_element_type=F32)


def lane_of(shape):
    return lax.broadcasted_iota(jnp.int32, shape, len(shape) - 1)


def swap_halves(block):
    lead = lane_of(block.shape) % HD < HD // 2
    return jnp.where(
        lead, pltpu.roll(block, LANES - HD // 2, 1), pltpu.roll(block, HD // 2, 1)
    )


def other_head(block):
    return jnp.concatenate([block[:, HD:], block[:, :HD]], axis=1)


def prep_kernel(x_ref, gain_ref, w_ref, bias_ref, cos_ref, sin_ref, normed_ref, q_ref, kv_ref):
    x = x_ref[...].astype(F32)
    width = q_ref.shape[1]
    inverse = lax.rsqrt(jnp.mean(x * x, axis=-1, keepdims=True) + EPSILON)
    normed = (x * inverse * gain_ref[...]).astype(BF16)
    normed_ref[...] = normed
    joined = dot_nn(normed, w_ref[...]) + bias_ref[...]
    cosine, sine = cos_ref[...], sin_ref[...]
    for begin in range(0, width + LANES, LANES):
        block = joined[:, begin : begin + LANES]
        turned = block * cosine + swap_halves(block) * sine
        if begin < width:
            q_ref[:, begin : begin + LANES] = (turned * SCALE).astype(BF16)
        else:
            kv_ref[:, :LANES] = turned.astype(BF16)
    kv_ref[:, LANES:] = joined[:, width + LANES :].astype(BF16)


def prep(x, gain, w_qkv, bias, cosine, sine, rows):
    count, dim = x.shape
    joint = w_qkv.shape[1]
    width = joint - 2 * LANES
    row_block = lambda cols: pl.BlockSpec((rows, cols), lambda i: (i, 0))
    whole = lambda shape: pl.BlockSpec(shape, lambda i: (0, 0))
    return pl.pallas_call(
        prep_kernel,
        grid=(count // rows,),
        in_specs=[
            row_block(dim),
            whole((1, dim)),
            whole((dim, joint)),
            whole((1, joint)),
            row_block(LANES),
            row_block(LANES),
        ],
        out_specs=[row_block(dim), row_block(width), row_block(2 * LANES)],
        out_shape=[
            jax.ShapeDtypeStruct((count, dim), BF16),
            jax.ShapeDtypeStruct((count, width), BF16),
            jax.ShapeDtypeStruct((count, 2 * LANES), BF16),
        ],
        compiler_params=pltpu.CompilerParams(vmem_limit_bytes=40 * MIB),
        cost_estimate=pl.CostEstimate(
            flops=2 * count * dim * joint, bytes_accessed=4 * count * dim + 2 * dim * joint, transcendentals=0
        ),
        name="norm_project_rotate",
    )(x, gain, w_qkv, bias, cosine, sine)


def attend_kernel(offset_ref, q_ref, kv_ref, start_ref, out_ref):
    rows, width = q_ref.shape
    length = kv_ref.shape[1]
    heads = width // HD
    group = heads // 2
    key = kv_ref[0, :, :LANES]
    value = kv_ref[0, :, LANES:]
    keys = (key, other_head(key))
    values = (value, other_head(value))
    upper_key = lane_of((length, LANES)) >= HD
    upper = lane_of((rows, LANES)) >= HD
    query_at = offset_ref[0] + lax.broadcasted_iota(jnp.int32, (rows, length), 0)
    key_at = lax.broadcasted_iota(jnp.int32, (rows, length), 1)
    allowed = (key_at <= query_at) & (key_at >= start_ref[:, :1])
    bias = jnp.where(allowed, 0.0, MASKED)
    one = jnp.ones((), BF16)
    for pair in range(heads // 2):
        at = slice(pair * LANES, (pair + 1) * LANES)
        both = q_ref[:, at]
        parts = []
        for place in range(2):
            owner = (2 * pair + place) // group
            moved = int(owner != place)
            side = upper if place else ~upper
            side_key = upper_key if place else ~upper_key
            query = jnp.where(side, both, jnp.zeros_like(both))
            score = dot_nt(query, keys[moved]) + bias
            top = jnp.max(score, axis=1, keepdims=True)
            weight = jnp.exp(score - top).astype(BF16)
            mixed = dot_nn(weight, jnp.where(side_key, values[moved], one))
            parts.append(mixed / pltpu.roll(mixed, HD, 1))
        out_ref[:, at] = jnp.where(upper, parts[1], parts[0]).astype(BF16)


def attend(offset, q, kv, start, rows):
    count, width = q.shape
    length = kv.shape[1]
    heads = width // HD
    row_block = lambda cols: pl.BlockSpec((rows, cols), lambda i: (i, 0))
    return pl.pallas_call(
        attend_kernel,
        grid=(count // rows,),
        in_specs=[
            pl.BlockSpec(memory_space=pltpu.SMEM),
            row_block(width),
            pl.BlockSpec((1, length, 2 * LANES), lambda i: (i, 0, 0)),
            row_block(LANES),
        ],
        out_specs=row_block(width),
        out_shape=jax.ShapeDtypeStruct((count, width), BF16),
        compiler_params=pltpu.CompilerParams(vmem_limit_bytes=48 * MIB),
        cost_estimate=pl.CostEstimate(
            flops=8 * count * length * LANES * heads,
            bytes_accessed=4 * count * width,
            transcendentals=count * length * heads,
        ),
        name="attention_forward",
    )(offset, q, kv, start)


def attend_back_kernel(
    offset_ref, q_ref, kv_ref, back_ref, start_ref, cos_ref, sin_ref, dq_ref, dkv_ref, dk_sum, dv_sum
):
    rows, width = q_ref.shape
    length = kv_ref.shape[1]
    heads = width // HD
    group = heads // 2
    key = kv_ref[0, :, :LANES]
    value = kv_ref[0, :, LANES:]
    keys = (key, other_head(key))
    values = (value, other_head(value))
    key_t = key.astype(F32).T.astype(BF16)
    keys_t = (key_t, jnp.concatenate([key_t[HD:], key_t[:HD]], axis=0))
    upper = lane_of((rows, LANES)) >= HD
    upper_t = lax.broadcasted_iota(jnp.int32, (LANES, rows), 0) >= HD
    query_at = offset_ref[0] + lax.broadcasted_iota(jnp.int32, (length, rows), 1)
    key_at = lax.broadcasted_iota(jnp.int32, (length, rows), 0)
    allowed = (key_at <= query_at) & (key_at >= start_ref[0, :1, :])
    bias = jnp.where(allowed, 0.0, MASKED)
    cosine, sine = cos_ref[...], sin_ref[...]
    dk_sum[...] = jnp.zeros_like(dk_sum)
    dv_sum[...] = jnp.zeros_like(dv_sum)
    for pair in range(heads // 2):
        at = slice(pair * LANES, (pair + 1) * LANES)
        both = q_ref[:, at]
        back_both = back_ref[:, at]
        parts = []
        for place in range(2):
            owner = (2 * pair + place) // group
            moved = int(owner != place)
            side = upper if place else ~upper
            query = jnp.where(side, both, jnp.zeros_like(both))
            back = jnp.where(side, back_both, jnp.zeros_like(back_both))
            score = dot_nt(keys[moved], query) + bias
            weight = jnp.exp(score - jnp.max(score, axis=0, keepdims=True))
            prob = weight * (1.0 / jnp.sum(weight, axis=0, keepdims=True))
            dv_sum[owner] += dot_nn(prob.astype(BF16), back)
            d_prob = dot_nt(values[moved], back)
            level = jnp.sum(prob * d_prob, axis=0, keepdims=True)
            d_score = (prob * (d_prob - level)).astype(BF16)
            dk_sum[owner] += dot_nn(d_score, query)
            parts.append(dot_nn(keys_t[moved], d_score))
        d_query = jnp.where(upper_t, parts[1], parts[0]).T * SCALE
        dq_ref[:, at] = (d_query * cosine - swap_halves(d_query) * sine).astype(BF16)
    lower_key = lane_of((length, LANES)) < HD
    for total, begin in ((dk_sum, 0), (dv_sum, LANES)):
        first, second = total[0], total[1]
        first = first + pltpu.roll(first, HD, 1)
        second = second + pltpu.roll(second, HD, 1)
        dkv_ref[0, :, begin : begin + LANES] = jnp.where(lower_key, first, second).astype(BF16)


def attend_back(offset, q, kv, back, start, cosine, sine, rows):
    count, width = q.shape
    length = kv.shape[1]
    heads = width // HD
    row_block = lambda cols: pl.BlockSpec((rows, cols), lambda i: (i, 0))
    key_block = pl.BlockSpec((1, length, 2 * LANES), lambda i: (i, 0, 0))
    return pl.pallas_call(
        attend_back_kernel,
        grid=(count // rows,),
        in_specs=[
            pl.BlockSpec(memory_space=pltpu.SMEM),
            row_block(width),
            key_block,
            row_block(width),
            pl.BlockSpec((1, 8, rows), lambda i: (i, 0, 0)),
            row_block(LANES),
            row_block(LANES),
        ],
        out_specs=[row_block(width), key_block],
        out_shape=[
            jax.ShapeDtypeStruct((count, width), BF16),
            jax.ShapeDtypeStruct(kv.shape, BF16),
        ],
        scratch_shapes=[
            pltpu.VMEM((2, length, LANES), F32),
            pltpu.VMEM((2, length, LANES), F32),
        ],
        compiler_params=pltpu.CompilerParams(vmem_limit_bytes=48 * MIB),
        cost_estimate=pl.CostEstimate(
            flops=20 * count * length * LANES * heads,
            bytes_accessed=8 * count * width,
            transcendentals=count * length * heads,
        ),
        name="attention_backward",
    )(offset, q, kv, back, start, cosine, sine)


def mlp_kernel(
    columns, normed_ref, cot_ref, w_ref, own_ref, away_ref, d_own_ref, d_away_ref, grad_ref,
    normed_t, cot_t, out_sum, d_sum,
):
    step = pl.program_id(0)
    last = pl.num_programs(0) - 1
    half = own_ref.shape[0]

    @pl.when(step == 0)
    def _():
        normed_t[...] = normed_ref[...].T
        cot_t[...] = cot_ref[...].T
        out_sum[...] = jnp.zeros_like(out_sum)
        d_sum[...] = jnp.zeros_like(d_sum)

    def work(size):
        w_gate = w_ref[:, :size]
        w_up = w_ref[:, size : 2 * size]
        w_down = w_ref[:, 2 * size : 3 * size]
        normed = normed_ref[...]
        gate = dot_nn(normed, w_gate)
        up = dot_nn(normed, w_up)
        d_act = dot_nn(cot_ref[...], w_down)
        sigmoid = 1.0 / (1.0 + jnp.exp(-gate))
        swish = gate * sigmoid
        act = (swish * up).astype(BF16)
        d_gate = (d_act * up * sigmoid * (1.0 + gate * (1.0 - sigmoid))).astype(BF16)
        d_up = (d_act * swish).astype(BF16)
        out_sum[...] += dot_nt(act, w_down)
        d_sum[...] += dot_nt(d_gate, w_gate) + dot_nt(d_up, w_up)
        grad_ref[:, :size] = dot_nn(normed_t[...], d_gate).astype(BF16)
        grad_ref[:, size : 2 * size] = dot_nn(normed_t[...], d_up).astype(BF16)
        grad_ref[:, 2 * size : 3 * size] = dot_nn(cot_t[...], act).astype(BF16)

    rest = columns % TILE
    if rest:
        pl.when(step < last)(functools.partial(work, TILE))
        pl.when(step == last)(functools.partial(work, rest))
    else:
        work(TILE)

    @pl.when(step == last)
    def _():
        own_ref[...] = out_sum[:half]
        away_ref[...] = out_sum[half:].astype(BF16)
        d_own_ref[...] = d_sum[:half]
        d_away_ref[...] = d_sum[half:].astype(BF16)


def mlp(normed, cot, weights):
    count, dim = normed.shape
    half = count // 2
    columns = weights.shape[1] // 3
    whole = lambda shape: pl.BlockSpec(shape, lambda i: (0, 0))
    tile = pl.BlockSpec((dim, 3 * TILE), lambda i: (0, i))
    return pl.pallas_call(
        functools.partial(mlp_kernel, columns),
        grid=(pl.cdiv(columns, TILE),),
        in_specs=[whole((count, dim)), whole((count, dim)), tile],
        out_specs=[whole((half, dim))] * 4 + [tile],
        out_shape=[
            jax.ShapeDtypeStruct((half, dim), F32),
            jax.ShapeDtypeStruct((half, dim), BF16),
            jax.ShapeDtypeStruct((half, dim), F32),
            jax.ShapeDtypeStruct((half, dim), BF16),
            jax.ShapeDtypeStruct(weights.shape, BF16),
        ],
        scratch_shapes=[
            pltpu.VMEM((dim, count), BF16),
            pltpu.VMEM((dim, count), BF16),
            pltpu.VMEM((count, dim), F32),
            pltpu.VMEM((count, dim), F32),
        ],
        compiler_params=pltpu.CompilerParams(vmem_limit_bytes=56 * MIB),
        cost_estimate=pl.CostEstimate(
            flops=18 * count * dim * columns,
            bytes_accessed=12 * dim * columns + 16 * count * dim,
            transcendentals=count * columns,
        ),
        name="feed_forward",
    )(normed, cot, weights)


class Split:
    def __init__(self, over):
        self.over = over
        self.rest = ("fsdp", "cc" if over == "cx" else "cx")

    def swap(self, value):
        return lax.ppermute(value, self.over, [(0, 1), (1, 0)])

    def exchange(self, halves):
        cx, cc = lax.axis_index("cx"), lax.axis_index("cc")
        if self.over == "cc":
            mine = jnp.where(cc == 0, halves[0], halves[1])
            theirs = self.swap(jnp.where(cc == 0, halves[1], halves[0]))
            first = cc == 0
        else:
            mine = lax.ppermute(jnp.where(cc == 0, halves[0], halves[1]), CTX, self._turn())
            theirs = lax.ppermute(jnp.where(cc == 0, halves[1], halves[0]), CTX, self._turn_over())
            first = cx == 0
        return jnp.where(
            first,
            jnp.concatenate([mine, theirs], axis=0),
            jnp.concatenate([theirs, mine], axis=0),
        )

    def exchange_back(self, value):
        cx, cc = lax.axis_index("cx"), lax.axis_index("cc")
        rows = value.shape[0] // 2
        low, high = value[:rows], value[rows:]
        if self.over == "cc":
            mine = jnp.where(cc == 0, low, high)
            theirs = self.swap(jnp.where(cc == 0, high, low))
        else:
            mine = lax.ppermute(jnp.where(cx == 0, low, high), CTX, self._turn())
            back = [(to, came) for came, to in self._turn_over()]
            theirs = lax.ppermute(jnp.where(cx == 0, high, low), CTX, back)
        return (jnp.where(cc == 0, mine, theirs), jnp.where(cc == 0, theirs, mine))

    @staticmethod
    def _turn():
        return [(2 * x + c, 2 * c + x) for x in range(2) for c in range(2)]

    @staticmethod
    def _turn_over():
        return [(2 * x + c, 2 * (1 - c) + x) for x in range(2) for c in range(2)]


def interleave(parts):
    columns = parts[0].shape[1]
    pieces = []
    for begin in range(0, columns, TILE):
        pieces += [part[:, begin : begin + TILE] for part in parts]
    return jnp.concatenate(pieces, axis=1)


def separate(value):
    columns = value.shape[1] // 3
    pieces = ([], [], [])
    begin = 0
    for at in range(0, columns, TILE):
        size = min(TILE, columns - at)
        for place in range(3):
            pieces[place].append(value[:, begin : begin + size])
            begin += size
    return tuple(jnp.concatenate(piece, axis=1) for piece in pieces)


def norm_back(values, inverse, gain, incoming):
    scaled = incoming * gain
    gain_grad = jnp.sum(incoming * values * inverse, axis=0)
    mean_term = jnp.mean(scaled * values, axis=-1, keepdims=True)
    return (inverse * scaled - values * inverse**3 * mean_term, gain_grad)


def on_device(
    split,
    hidden,
    segments,
    attn_gain,
    qkv_weight,
    qkv_bias,
    out_weight,
    mlp_gain,
    gate_weight,
    up_weight,
    down_weight,
    cotangent,
):
    seqs, rows, dim = hidden.shape
    length = segments.shape[1]
    count = seqs * rows
    shard = attn_gain.shape[0]
    world = dim // shard
    joint = qkv_weight.shape[1]
    width = joint - 2 * LANES
    ff = gate_weight.shape[1]
    block = lax.axis_index("cx") * lax.axis_size("cc") + lax.axis_index("cc")
    offset = block * rows

    padded = -(-(shard + 1) // 16) * 16
    small = jnp.concatenate([attn_gain, mlp_gain, qkv_bias])
    spare = joint + width
    first_rows = jnp.concatenate([qkv_weight, out_weight.T], axis=1)
    small_row = jnp.pad(small, (0, spare - small.shape[0]))[None]
    first_shard = jnp.pad(
        jnp.concatenate([first_rows, small_row], axis=0), ((0, padded - shard - 1), (0, 0))
    )
    first_all = lax.all_gather(first_shard, AXES, axis=0, tiled=False)
    first_weights = first_all[:, :shard].reshape(dim, spare)
    w_qkv, w_out_t = first_weights[:, :joint], first_weights[:, joint:]
    extras = first_all[:, shard, : small.shape[0]].astype(F32)
    gain_attn = extras[:, :shard].reshape(1, dim)
    gain_mlp = extras[:, shard : 2 * shard].reshape(1, dim)
    bias = extras[:, 2 * shard :].reshape(1, joint)

    columns = ff // 2
    down_t = down_weight.T
    halves = [
        interleave([part[:, h * columns : (h + 1) * columns] for part in (gate_weight, up_weight, down_t)])
        for h in range(2)
    ]
    mlp_shard = split.exchange(halves)
    mlp_weights = lax.all_gather(mlp_shard, split.rest, axis=0, tiled=True)

    at_row = lax.dynamic_slice_in_dim(segments, offset, rows, axis=1)
    zeros_before = jnp.sum((segments < 1).astype(jnp.int32), axis=1, keepdims=True)
    ones_before = jnp.sum((segments < 2).astype(jnp.int32), axis=1, keepdims=True)
    start = jnp.where(at_row == 0, 0, jnp.where(at_row == 1, zeros_before, ones_before))
    position = (offset + jnp.arange(rows, dtype=jnp.int32)[None, :] - start).reshape(count)
    lane = jnp.arange(LANES, dtype=jnp.int32)
    frequency = ROPE_BASE ** (-(lane % (HD // 2)).astype(F32) * 2.0 / HD)
    angle = position.astype(F32)[:, None] * frequency[None, :]
    cosine = jnp.cos(angle)
    sine = jnp.where(lane % HD < HD // 2, -1.0, 1.0)[None, :] * jnp.sin(angle)
    start_column = jnp.broadcast_to(start.reshape(count, 1), (count, LANES))
    start_row = jnp.broadcast_to(start[:, None, :], (seqs, 8, rows))
    offset_arg = offset.reshape(1).astype(jnp.int32)

    x = hidden.reshape(count, dim)
    cot = cotangent.reshape(count, dim)
    cot_all = jnp.concatenate([cot, split.swap(cot)], axis=0)
    normed, q, kv = prep(x, gain_attn, w_qkv, bias, cosine, sine, rows)
    kv_all = lax.all_gather(kv.reshape(seqs, rows, 2 * LANES), CTX, axis=1, tiled=True)
    attended = attend(offset_arg, q, kv_all, start_column, rows)
    x32 = x.astype(F32)
    resid = x32 + dot_nt(attended, w_out_t)
    inv_mlp = lax.rsqrt(jnp.mean(resid * resid, axis=-1, keepdims=True) + EPSILON)
    normed_post = (resid * inv_mlp * gain_mlp).astype(BF16)

    normed_all = jnp.concatenate([normed_post, split.swap(normed_post)], axis=0)
    out_own, out_away, d_own, d_away, mlp_grad = mlp(normed_all, cot_all, mlp_weights)
    d_normed_post = d_own + split.swap(d_away).astype(F32)
    output = (resid + out_own + split.swap(out_away).astype(F32)).astype(BF16)
    mlp_grad_shard = lax.psum_scatter(
        mlp_grad.reshape(world // 2, 2 * shard, 3 * columns), split.rest, scatter_dimension=0, tiled=False
    )

    cot32 = cot.astype(F32)
    d_middle, mlp_gain_grad = norm_back(resid, inv_mlp, gain_mlp, d_normed_post)
    d_resid = cot32 + d_middle
    d_branch = d_resid.astype(BF16)
    out_grad_t = dot_tn(d_branch, attended)
    d_attended = dot_nn(d_branch, w_out_t).astype(BF16)
    dq, dkv_all = attend_back(offset_arg, q, kv_all, d_attended, start_row, cosine, sine, rows)
    dkv = lax.psum_scatter(dkv_all, CTX, scatter_dimension=1, tiled=True)
    dkv = dkv.reshape(count, 2 * LANES).astype(F32)
    dk = dkv[:, :LANES]
    partner = jnp.concatenate(
        [dk[:, HD // 2 : HD], dk[:, : HD // 2], dk[:, HD + HD // 2 :], dk[:, HD : HD + HD // 2]], axis=1
    )
    dk = dk * cosine - partner * sine
    d_joined = jnp.concatenate([dq, dk.astype(BF16), dkv[:, LANES:].astype(BF16)], axis=1)
    qkv_grad = dot_tn(normed, d_joined)
    bias_grad = jnp.sum(d_joined.astype(F32), axis=0)
    d_normed = dot_nt(d_joined, w_qkv)
    inv_attn = lax.rsqrt(jnp.mean(x32 * x32, axis=-1, keepdims=True) + EPSILON)
    d_input, attn_gain_grad = norm_back(x32, inv_attn, gain_attn, d_normed)
    input_grad = (d_resid + d_input).astype(BF16)

    split_at = width + LANES
    small_grads = jnp.concatenate(
        [
            attn_gain_grad.reshape(world, -1),
            mlp_gain_grad.reshape(world, -1),
            bias_grad[:split_at].reshape(world, -1),
            bias_grad[split_at:].reshape(world, -1),
        ],
        axis=1,
    ).astype(BF16)
    small_count = small_grads.shape[1]
    first_grad = jnp.concatenate([qkv_grad.astype(BF16), out_grad_t.astype(BF16)], axis=1)
    first_grad = jnp.concatenate(
        [
            first_grad.reshape(world, shard, spare),
            jnp.pad(small_grads, ((0, 0), (0, spare - small_count)))[:, None, :],
            jnp.zeros((world, padded - shard - 1, spare), BF16),
        ],
        axis=1,
    )
    first_sum = lax.psum_scatter(first_grad, AXES, scatter_dimension=0, tiled=True)[0].astype(F32)
    small_sum = first_sum[shard, :small_count]
    cut = (shard, 2 * shard, 2 * shard + split_at // world)

    low, high = split.exchange_back(lax.optimization_barrier(mlp_grad_shard))
    low, high = separate(low), separate(high)
    gate_grad, up_grad, down_grad_t = (
        jnp.concatenate([a, b], axis=1).astype(F32) for a, b in zip(low, high)
    )
    return (
        output.reshape(hidden.shape),
        input_grad.reshape(hidden.shape),
        small_sum[: cut[0]],
        first_sum[:shard, :joint],
        small_sum[cut[1] : cut[2]],
        small_sum[cut[2] :],
        first_sum[:shard, joint:].T,
        small_sum[cut[0] : cut[1]],
        gate_grad,
        up_grad,
        down_grad_t.T,
    )


def solution(mesh):
    fsdp, ctx = mesh.shape["fsdp"], mesh.shape["ctx"]
    inner = Mesh(mesh.devices.reshape(fsdp, 2, ctx // 2), AXES)
    tokens = P("fsdp", CTX, None)
    vector = P(AXES)
    by_row = P(AXES, None)
    by_column = P(None, AXES)
    return jax.shard_map(
        functools.partial(on_device, Split("cx")),
        mesh=inner,
        in_specs=(
            tokens,
            P("fsdp", None),
            vector,
            by_row,
            vector,
            by_column,
            vector,
            by_row,
            by_row,
            by_column,
            tokens,
        ),
        out_specs=(
            tokens,
            tokens,
            vector,
            by_row,
            vector,
            vector,
            by_column,
            vector,
            by_row,
            by_row,
            by_column,
        ),
        check_vma=False,
    )
```

```python
import functools

import jax
import jax.numpy as jnp
from jax import lax
from jax.experimental import pallas as pl
from jax.experimental.pallas import tpu as pltpu
from jax.sharding import Mesh
from jax.sharding import PartitionSpec as P

HD = 64
LANES = 128
EPSILON = 1e-06
ROPE_BASE = 1000000.0
MASKED = -1e30
SCALE = HD ** (-0.5)
TILE = 256
MIB = 1 << 20
F32 = jnp.float32
BF16 = jnp.bfloat16
AXES = ("fsdp", "cx", "cc")
CTX = ("cx", "cc")


def dot_nn(a, b):
    return lax.dot_general(a, b, (((1,), (0,)), ((), ())), preferred_element_type=F32)


def dot_nt(a, b):
    return lax.dot_general(a, b, (((1,), (1,)), ((), ())), preferred_element_type=F32)


def dot_tn(a, b):
    return lax.dot_general(a, b, (((0,), (0,)), ((), ())), preferred_element_type=F32)


def lane_of(shape):
    return lax.broadcasted_iota(jnp.int32, shape, len(shape) - 1)


def swap_halves(block):
    lead = lane_of(block.shape) % HD < HD // 2
    return jnp.where(
        lead, pltpu.roll(block, LANES - HD // 2, 1), pltpu.roll(block, HD // 2, 1)
    )


def other_head(block):
    return jnp.concatenate([block[:, HD:], block[:, :HD]], axis=1)


def prep_kernel(
    x_ref, gain_ref, order_ref, w_low_ref, w_high_ref, bias_ref, cos_ref, sin_ref, normed_ref, q_ref, kv_ref
):
    x = x_ref[...].astype(F32)
    width = q_ref.shape[1]
    joint = bias_ref.shape[1]
    middle = w_low_ref.shape[0]
    inverse = lax.rsqrt(jnp.mean(x * x, axis=-1, keepdims=True) + EPSILON)
    normed = (x * inverse * gain_ref[...]).astype(BF16)
    ordered = dot_nn(normed, order_ref[...]).astype(BF16)
    normed_ref[...] = ordered
    joined = dot_nn(ordered[:, :middle], w_low_ref[:, :joint])
    joined = joined + dot_nn(ordered[:, middle:], w_high_ref[:, :joint]) + bias_ref[...]
    cosine, sine = cos_ref[...], sin_ref[...]
    for begin in range(0, width + LANES, LANES):
        block = joined[:, begin : begin + LANES]
        turned = block * cosine + swap_halves(block) * sine
        if begin < width:
            q_ref[:, begin : begin + LANES] = (turned * SCALE).astype(BF16)
        else:
            kv_ref[:, :LANES] = turned.astype(BF16)
    kv_ref[:, LANES:] = joined[:, width + LANES :].astype(BF16)


def rows_of(rows, cols):
    return pl.BlockSpec((rows, cols), lambda i: (i, 0))


def whole(value):
    return pl.BlockSpec(value.shape, lambda i: (0,) * value.ndim)


def prep(x, gain, order, weights, bias, cosine, sine, rows):
    count, dim = x.shape
    ordered = order.shape[1]
    joint = bias.shape[1]
    width = joint - 2 * LANES
    return pl.pallas_call(
        prep_kernel,
        grid=(count // rows,),
        in_specs=[
            rows_of(rows, dim),
            whole(gain),
            whole(order),
            whole(weights[0]),
            whole(weights[1]),
            whole(bias),
            rows_of(rows, LANES),
            rows_of(rows, LANES),
        ],
        out_specs=[rows_of(rows, ordered), rows_of(rows, width), rows_of(rows, 2 * LANES)],
        out_shape=[
            jax.ShapeDtypeStruct((count, ordered), BF16),
            jax.ShapeDtypeStruct((count, width), BF16),
            jax.ShapeDtypeStruct((count, 2 * LANES), BF16),
        ],
        compiler_params=pltpu.CompilerParams(vmem_limit_bytes=40 * MIB),
        cost_estimate=pl.CostEstimate(
            flops=2 * count * ordered * (joint + dim), bytes_accessed=12 * MIB, transcendentals=0
        ),
        name="norm_project_rotate",
    )(x, gain, order, weights[0], weights[1], bias, cosine, sine)


def back_in_order(value, order):
    high = value.astype(BF16)
    low = (value - high.astype(F32)).astype(BF16)
    return dot_nt(high, order) + dot_nt(low, order)


def out_kernel(attended_ref, x_ref, w_low_ref, w_high_ref, order_ref, gain_ref, resid_ref, normed_ref):
    width = attended_ref.shape[1]
    joint = w_low_ref.shape[1] - width
    attended = attended_ref[...]
    branch = jnp.concatenate(
        [dot_nt(attended, w_low_ref[:, joint:]), dot_nt(attended, w_high_ref[:, joint:])], axis=1
    )
    resid = x_ref[...].astype(F32) + back_in_order(branch, order_ref[...])
    inverse = lax.rsqrt(jnp.mean(resid * resid, axis=-1, keepdims=True) + EPSILON)
    resid_ref[...] = resid
    normed_ref[...] = (resid * inverse * gain_ref[...]).astype(BF16)


def project_out(attended, x, weights, order, gain, rows):
    count, dim = x.shape
    return pl.pallas_call(
        out_kernel,
        grid=(count // rows,),
        in_specs=[
            rows_of(rows, attended.shape[1]),
            rows_of(rows, dim),
            whole(weights[0]),
            whole(weights[1]),
            whole(order),
            whole(gain),
        ],
        out_specs=[rows_of(rows, dim), rows_of(rows, dim)],
        out_shape=[jax.ShapeDtypeStruct((count, dim), F32), jax.ShapeDtypeStruct((count, dim), BF16)],
        compiler_params=pltpu.CompilerParams(vmem_limit_bytes=40 * MIB),
        cost_estimate=pl.CostEstimate(flops=6 * count * dim * dim, bytes_accessed=8 * MIB, transcendentals=0),
        name="project_out_norm",
    )(attended, x, weights[0], weights[1], order, gain)


def fold_rows(value):
    return jnp.sum(value.reshape(-1, 8, value.shape[1]), axis=0)


def norm_back(values, inverse, gain, incoming):
    scaled = incoming * gain
    mean_term = jnp.mean(scaled * values, axis=-1, keepdims=True)
    return inverse * scaled - values * inverse**3 * mean_term


def out_back_kernel(
    own_ref, came_ref, resid_ref, cot_ref, w_low_ref, w_high_ref, order_ref, gain_ref,
    d_resid_ref, d_branch_ref, d_attended_ref, gain_grad_ref,
):
    width = d_attended_ref.shape[1]
    joint = w_low_ref.shape[1] - width
    middle = w_low_ref.shape[0]
    d_normed = own_ref[...] + came_ref[...].astype(F32)
    resid = resid_ref[...]
    inverse = lax.rsqrt(jnp.mean(resid * resid, axis=-1, keepdims=True) + EPSILON)
    d_resid = cot_ref[...].astype(F32) + norm_back(resid, inverse, gain_ref[...], d_normed)
    d_resid_ref[...] = d_resid
    d_branch = dot_nn(d_resid.astype(BF16), order_ref[...]).astype(BF16)
    d_branch_ref[...] = d_branch
    d_attended = dot_nn(d_branch[:, :middle], w_low_ref[:, joint:])
    d_attended = d_attended + dot_nn(d_branch[:, middle:], w_high_ref[:, joint:])
    d_attended_ref[...] = d_attended.astype(BF16)
    sums = fold_rows(d_normed * resid * inverse)

    @pl.when(pl.program_id(0) == 0)
    def _():
        gain_grad_ref[...] = sums

    @pl.when(pl.program_id(0) > 0)
    def _():
        gain_grad_ref[...] += sums


def project_out_back(own, came, resid, cot, weights, order, gain, rows):
    count, dim = resid.shape
    ordered = order.shape[1]
    width = dim
    return pl.pallas_call(
        out_back_kernel,
        grid=(count // rows,),
        in_specs=[
            rows_of(rows, dim),
            rows_of(rows, dim),
            rows_of(rows, dim),
            rows_of(rows, dim),
            whole(weights[0]),
            whole(weights[1]),
            whole(order),
            whole(gain),
        ],
        out_specs=[
            rows_of(rows, dim),
            rows_of(rows, ordered),
            rows_of(rows, width),
            pl.BlockSpec((8, dim), lambda i: (0, 0)),
        ],
        out_shape=[
            jax.ShapeDtypeStruct((count, dim), F32),
            jax.ShapeDtypeStruct((count, ordered), BF16),
            jax.ShapeDtypeStruct((count, width), BF16),
            jax.ShapeDtypeStruct((8, dim), F32),
        ],
        compiler_params=pltpu.CompilerParams(vmem_limit_bytes=40 * MIB),
        cost_estimate=pl.CostEstimate(flops=4 * count * dim * dim, bytes_accessed=12 * MIB, transcendentals=0),
        name="norm_back_project",
    )(own, came, resid, cot, weights[0], weights[1], order, gain)


def input_back_kernel(
    dq_ref, dkv_ref, x_ref, d_resid_ref, w_low_ref, w_high_ref, order_ref, gain_ref, cos_ref, sin_ref,
    d_joined_ref, input_grad_ref, gain_grad_ref, bias_grad_ref,
):
    width = dq_ref.shape[1]
    joint = d_joined_ref.shape[1]
    dk = dkv_ref[:, :LANES].astype(F32)
    dk = dk * cos_ref[...] - swap_halves(dk) * sin_ref[...]
    d_joined = jnp.concatenate([dq_ref[...], dk.astype(BF16), dkv_ref[:, LANES:].astype(BF16)], axis=1)
    d_joined_ref[...] = d_joined
    d_normed = jnp.concatenate(
        [dot_nt(d_joined, w_low_ref[:, :joint]), dot_nt(d_joined, w_high_ref[:, :joint])], axis=1
    )
    d_normed = back_in_order(d_normed, order_ref[...])
    x = x_ref[...].astype(F32)
    inverse = lax.rsqrt(jnp.mean(x * x, axis=-1, keepdims=True) + EPSILON)
    input_grad_ref[...] = (d_resid_ref[...] + norm_back(x, inverse, gain_ref[...], d_normed)).astype(BF16)
    gain_sums = fold_rows(d_normed * x * inverse)
    bias_sums = fold_rows(d_joined.astype(F32))

    @pl.when(pl.program_id(0) == 0)
    def _():
        gain_grad_ref[...] = gain_sums
        bias_grad_ref[...] = bias_sums

    @pl.when(pl.program_id(0) > 0)
    def _():
        gain_grad_ref[...] += gain_sums
        bias_grad_ref[...] += bias_sums


def input_back(dq, dkv, x, d_resid, weights, order, gain, cosine, sine, rows):
    count, dim = x.shape
    width = dq.shape[1]
    joint = width + 2 * LANES
    return pl.pallas_call(
        input_back_kernel,
        grid=(count // rows,),
        in_specs=[
            rows_of(rows, width),
            rows_of(rows, 2 * LANES),
            rows_of(rows, dim),
            rows_of(rows, dim),
            whole(weights[0]),
            whole(weights[1]),
            whole(order),
            whole(gain),
            rows_of(rows, LANES),
            rows_of(rows, LANES),
        ],
        out_specs=[
            rows_of(rows, joint),
            rows_of(rows, dim),
            pl.BlockSpec((8, dim), lambda i: (0, 0)),
            pl.BlockSpec((8, joint), lambda i: (0, 0)),
        ],
        out_shape=[
            jax.ShapeDtypeStruct((count, joint), BF16),
            jax.ShapeDtypeStruct((count, dim), BF16),
            jax.ShapeDtypeStruct((8, dim), F32),
            jax.ShapeDtypeStruct((8, joint), F32),
        ],
        compiler_params=pltpu.CompilerParams(vmem_limit_bytes=40 * MIB),
        cost_estimate=pl.CostEstimate(flops=6 * count * dim * joint, bytes_accessed=12 * MIB, transcendentals=0),
        name="input_gradient",
    )(dq, dkv, x, d_resid, weights[0], weights[1], order, gain, cosine, sine)


def attend_kernel(offset_ref, q_ref, kv_ref, start_ref, out_ref):
    rows, width = q_ref.shape
    length = kv_ref.shape[1]
    heads = width // HD
    group = heads // 2
    key = kv_ref[0, :, :LANES]
    value = kv_ref[0, :, LANES:]
    keys = (key, other_head(key))
    values = (value, other_head(value))
    upper_key = lane_of((length, LANES)) >= HD
    upper = lane_of((rows, LANES)) >= HD
    query_at = offset_ref[0] * rows + lax.broadcasted_iota(jnp.int32, (rows, length), 0)
    key_at = jnp.concatenate(
        [
            (offset_ref[0] ^ place) * rows + lax.broadcasted_iota(jnp.int32, (rows, rows), 1)
            for place in range(length // rows)
        ],
        axis=1,
    )
    allowed = (key_at <= query_at) & (key_at >= start_ref[:, :1])
    bias = jnp.where(allowed, 0.0, MASKED)
    one = jnp.ones((), BF16)
    for pair in range(heads // 2):
        at = slice(pair * LANES, (pair + 1) * LANES)
        both = q_ref[:, at]
        parts = []
        for place in range(2):
            owner = (2 * pair + place) // group
            moved = int(owner != place)
            side = upper if place else ~upper
            side_key = upper_key if place else ~upper_key
            query = jnp.where(side, both, jnp.zeros_like(both))
            score = dot_nt(query, keys[moved]) + bias
            top = jnp.max(score, axis=1, keepdims=True)
            weight = jnp.exp(score - top).astype(BF16)
            mixed = dot_nn(weight, jnp.where(side_key, values[moved], one))
            parts.append(mixed / pltpu.roll(mixed, HD, 1))
        out_ref[:, at] = jnp.where(upper, parts[1], parts[0]).astype(BF16)


def attend(offset, q, kv, start, rows):
    count, width = q.shape
    length = kv.shape[1]
    heads = width // HD
    row_block = lambda cols: pl.BlockSpec((rows, cols), lambda i: (i, 0))
    return pl.pallas_call(
        attend_kernel,
        grid=(count // rows,),
        in_specs=[
            pl.BlockSpec(memory_space=pltpu.SMEM),
            row_block(width),
            pl.BlockSpec((1, length, 2 * LANES), lambda i: (i, 0, 0)),
            row_block(LANES),
        ],
        out_specs=row_block(width),
        out_shape=jax.ShapeDtypeStruct((count, width), BF16),
        compiler_params=pltpu.CompilerParams(vmem_limit_bytes=48 * MIB),
        cost_estimate=pl.CostEstimate(
            flops=8 * count * length * LANES * heads,
            bytes_accessed=4 * count * width,
            transcendentals=count * length * heads,
        ),
        name="attention_forward",
    )(offset, q, kv, start)


def attend_back_kernel(
    offset_ref, q_ref, kv_ref, back_ref, start_ref, cos_ref, sin_ref, dq_ref, dkv_ref, dk_sum, dv_sum
):
    rows, width = q_ref.shape
    length = kv_ref.shape[1]
    heads = width // HD
    group = heads // 2
    key = kv_ref[0, :, :LANES]
    value = kv_ref[0, :, LANES:]
    keys = (key, other_head(key))
    values = (value, other_head(value))
    key_t = key.astype(F32).T.astype(BF16)
    keys_t = (key_t, jnp.concatenate([key_t[HD:], key_t[:HD]], axis=0))
    upper = lane_of((rows, LANES)) >= HD
    upper_t = lax.broadcasted_iota(jnp.int32, (LANES, rows), 0) >= HD
    query_at = offset_ref[0] * rows + lax.broadcasted_iota(jnp.int32, (length, rows), 1)
    key_at = jnp.concatenate(
        [
            (offset_ref[0] ^ place) * rows + lax.broadcasted_iota(jnp.int32, (rows, rows), 0)
            for place in range(length // rows)
        ],
        axis=0,
    )
    allowed = (key_at <= query_at) & (key_at >= start_ref[0, :1, :])
    bias = jnp.where(allowed, 0.0, MASKED)
    cosine, sine = cos_ref[...], sin_ref[...]
    dk_sum[...] = jnp.zeros_like(dk_sum)
    dv_sum[...] = jnp.zeros_like(dv_sum)
    for pair in range(heads // 2):
        at = slice(pair * LANES, (pair + 1) * LANES)
        both = q_ref[:, at]
        back_both = back_ref[:, at]
        parts = []
        for place in range(2):
            owner = (2 * pair + place) // group
            moved = int(owner != place)
            side = upper if place else ~upper
            query = jnp.where(side, both, jnp.zeros_like(both))
            back = jnp.where(side, back_both, jnp.zeros_like(back_both))
            score = dot_nt(keys[moved], query) + bias
            weight = jnp.exp(score - jnp.max(score, axis=0, keepdims=True))
            prob = weight * (1.0 / jnp.sum(weight, axis=0, keepdims=True))
            dv_sum[owner] += dot_nn(prob.astype(BF16), back)
            d_prob = dot_nt(values[moved], back)
            level = jnp.sum(prob * d_prob, axis=0, keepdims=True)
            d_score = (prob * (d_prob - level)).astype(BF16)
            dk_sum[owner] += dot_nn(d_score, query)
            parts.append(dot_nn(keys_t[moved], d_score))
        d_query = jnp.where(upper_t, parts[1], parts[0]).T * SCALE
        dq_ref[:, at] = (d_query * cosine - swap_halves(d_query) * sine).astype(BF16)
    lower_key = lane_of((length, LANES)) < HD
    for total, begin in ((dk_sum, 0), (dv_sum, LANES)):
        first, second = total[0], total[1]
        first = first + pltpu.roll(first, HD, 1)
        second = second + pltpu.roll(second, HD, 1)
        dkv_ref[0, :, begin : begin + LANES] = jnp.where(lower_key, first, second).astype(BF16)


def attend_back(offset, q, kv, back, start, cosine, sine, rows):
    count, width = q.shape
    length = kv.shape[1]
    heads = width // HD
    row_block = lambda cols: pl.BlockSpec((rows, cols), lambda i: (i, 0))
    key_block = pl.BlockSpec((1, length, 2 * LANES), lambda i: (i, 0, 0))
    return pl.pallas_call(
        attend_back_kernel,
        grid=(count // rows,),
        in_specs=[
            pl.BlockSpec(memory_space=pltpu.SMEM),
            row_block(width),
            key_block,
            row_block(width),
            pl.BlockSpec((1, 8, rows), lambda i: (i, 0, 0)),
            row_block(LANES),
            row_block(LANES),
        ],
        out_specs=[row_block(width), key_block],
        out_shape=[
            jax.ShapeDtypeStruct((count, width), BF16),
            jax.ShapeDtypeStruct(kv.shape, BF16),
        ],
        scratch_shapes=[
            pltpu.VMEM((2, length, LANES), F32),
            pltpu.VMEM((2, length, LANES), F32),
        ],
        compiler_params=pltpu.CompilerParams(vmem_limit_bytes=48 * MIB),
        cost_estimate=pl.CostEstimate(
            flops=20 * count * length * LANES * heads,
            bytes_accessed=8 * count * width,
            transcendentals=count * length * heads,
        ),
        name="attention_backward",
    )(offset, q, kv, back, start, cosine, sine)


def mlp_kernel(
    columns, normed_ref, cot_ref, w_ref, own_ref, away_ref, d_own_ref, d_away_ref, grad_ref,
    normed_t, cot_t, out_sum, d_sum,
):
    step = pl.program_id(0)
    last = pl.num_programs(0) - 1
    half = own_ref.shape[0]

    @pl.when(step == 0)
    def _():
        normed_t[...] = normed_ref[...].T
        cot_t[...] = cot_ref[...].T
        out_sum[...] = jnp.zeros_like(out_sum)
        d_sum[...] = jnp.zeros_like(d_sum)

    def work(size):
        w_gate = w_ref[:, :size]
        w_up = w_ref[:, size : 2 * size]
        w_down = w_ref[:, 2 * size : 3 * size]
        normed = normed_ref[...]
        gate = dot_nn(normed, w_gate)
        up = dot_nn(normed, w_up)
        d_act = dot_nn(cot_ref[...], w_down)
        sigmoid = 1.0 / (1.0 + jnp.exp(-gate))
        swish = gate * sigmoid
        act = (swish * up).astype(BF16)
        d_gate = (d_act * up * sigmoid * (1.0 + gate * (1.0 - sigmoid))).astype(BF16)
        d_up = (d_act * swish).astype(BF16)
        out_sum[...] += dot_nt(act, w_down)
        d_sum[...] += dot_nt(d_gate, w_gate) + dot_nt(d_up, w_up)
        grad_ref[:, :size] = dot_nn(normed_t[...], d_gate).astype(BF16)
        grad_ref[:, size : 2 * size] = dot_nn(normed_t[...], d_up).astype(BF16)
        grad_ref[:, 2 * size : 3 * size] = dot_nn(cot_t[...], act).astype(BF16)

    rest = columns % TILE
    if rest:
        pl.when(step < last)(functools.partial(work, TILE))
        pl.when(step == last)(functools.partial(work, rest))
    else:
        work(TILE)

    @pl.when(step == last)
    def _():
        own_ref[...] = out_sum[:half]
        away_ref[...] = out_sum[half:].astype(BF16)
        d_own_ref[...] = d_sum[:half]
        d_away_ref[...] = d_sum[half:].astype(BF16)


def mlp(normed, cot, weights):
    count, dim = normed.shape
    half = count // 2
    columns = weights.shape[1] // 3
    full = lambda shape: pl.BlockSpec(shape, lambda i: (0, 0))
    tile = pl.BlockSpec((dim, 3 * TILE), lambda i: (0, i))
    return pl.pallas_call(
        functools.partial(mlp_kernel, columns),
        grid=(pl.cdiv(columns, TILE),),
        in_specs=[full((count, dim)), full((count, dim)), tile],
        out_specs=[full((half, dim))] * 4 + [tile],
        out_shape=[
            jax.ShapeDtypeStruct((half, dim), F32),
            jax.ShapeDtypeStruct((half, dim), BF16),
            jax.ShapeDtypeStruct((half, dim), F32),
            jax.ShapeDtypeStruct((half, dim), BF16),
            jax.ShapeDtypeStruct(weights.shape, BF16),
        ],
        scratch_shapes=[
            pltpu.VMEM((dim, count), BF16),
            pltpu.VMEM((dim, count), BF16),
            pltpu.VMEM((count, dim), F32),
            pltpu.VMEM((count, dim), F32),
        ],
        compiler_params=pltpu.CompilerParams(vmem_limit_bytes=56 * MIB),
        cost_estimate=pl.CostEstimate(
            flops=18 * count * dim * columns,
            bytes_accessed=12 * dim * columns + 16 * count * dim,
            transcendentals=count * columns,
        ),
        name="feed_forward",
    )(normed, cot, weights)


class Split:
    def __init__(self, over):
        self.over = over
        self.rest = ("fsdp", "cc" if over == "cx" else "cx")

    def swap(self, value):
        return lax.ppermute(value, self.over, [(0, 1), (1, 0)])

    def exchange(self, halves):
        cx, cc = lax.axis_index("cx"), lax.axis_index("cc")
        if self.over == "cc":
            mine = jnp.where(cc == 0, halves[0], halves[1])
            theirs = self.swap(jnp.where(cc == 0, halves[1], halves[0]))
            first = cc == 0
        else:
            mine = lax.ppermute(jnp.where(cc == 0, halves[0], halves[1]), CTX, self._turn())
            theirs = lax.ppermute(jnp.where(cc == 0, halves[1], halves[0]), CTX, self._turn_over())
            first = cx == 0
        return jnp.where(
            first,
            jnp.concatenate([mine, theirs], axis=0),
            jnp.concatenate([theirs, mine], axis=0),
        )

    def exchange_back(self, value):
        cx, cc = lax.axis_index("cx"), lax.axis_index("cc")
        rows = value.shape[0] // 2
        low, high = value[:rows], value[rows:]
        if self.over == "cc":
            mine = jnp.where(cc == 0, low, high)
            theirs = self.swap(jnp.where(cc == 0, high, low))
        else:
            mine = lax.ppermute(jnp.where(cx == 0, low, high), CTX, self._turn())
            back = [(to, came) for came, to in self._turn_over()]
            theirs = lax.ppermute(jnp.where(cx == 0, high, low), CTX, back)
        return (jnp.where(cc == 0, mine, theirs), jnp.where(cc == 0, theirs, mine))

    @staticmethod
    def _turn():
        return [(2 * x + c, 2 * c + x) for x in range(2) for c in range(2)]

    @staticmethod
    def _turn_over():
        return [(2 * x + c, 2 * (1 - c) + x) for x in range(2) for c in range(2)]


def interleave(parts):
    columns = parts[0].shape[1]
    pieces = []
    for begin in range(0, columns, TILE):
        pieces += [part[:, begin : begin + TILE] for part in parts]
    return jnp.concatenate(pieces, axis=1)


def separate(value):
    columns = value.shape[1] // 3
    pieces = ([], [], [])
    begin = 0
    for at in range(0, columns, TILE):
        size = min(TILE, columns - at)
        for place in range(3):
            pieces[place].append(value[:, begin : begin + size])
            begin += size
    return tuple(jnp.concatenate(piece, axis=1) for piece in pieces)


def bit_swap(value, axis, bit):
    size = lax.axis_size(axis)
    return lax.ppermute(value, axis, [(i, i ^ (1 << bit)) for i in range(size)])


class Doubling:
    def __init__(self, fsdp):
        bits = fsdp.bit_length() - 1
        self.steps = [("fsdp", bit) for bit in reversed(range(bits))] + [("cx", 0), ("cc", 0)]
        weight = {"cc": 1, "cx": 2}
        self.offsets = [0]
        for axis, bit in self.steps:
            jump = weight[axis] if axis in weight else 4 << bit
            self.offsets += [offset ^ jump for offset in self.offsets]

    def gather(self, value):
        for axis, bit in self.steps[:-1]:
            value = jnp.concatenate([value, bit_swap(value, axis, bit)], axis=0)
        return value, bit_swap(value, *self.steps[-1])

    def scatter_sum(self, value):
        for axis, bit in reversed(self.steps):
            middle = value.shape[0] // 2
            came = bit_swap(value[middle:], axis, bit)
            value = (value[:middle].astype(F32) + came.astype(F32)).astype(BF16)
        return value


def on_device(
    split,
    doubling,
    hidden,
    segments,
    attn_gain,
    qkv_weight,
    qkv_bias,
    out_weight,
    mlp_gain,
    gate_weight,
    up_weight,
    down_weight,
    cotangent,
):
    seqs, rows, dim = hidden.shape
    count = seqs * rows
    shard = attn_gain.shape[0]
    world = dim // shard
    joint = qkv_weight.shape[1]
    width = joint - 2 * LANES
    ff = gate_weight.shape[1]
    block = lax.axis_index("cx") * lax.axis_size("cc") + lax.axis_index("cc")
    me = lax.axis_index("fsdp") * lax.axis_size(CTX) + block
    offset = block * rows

    columns = ff // 2
    down_t = down_weight.T
    halves = [
        interleave([part[:, h * columns : (h + 1) * columns] for part in (gate_weight, up_weight, down_t)])
        for h in range(2)
    ]
    mlp_shard = split.exchange(halves)
    mlp_weights = lax.all_gather(mlp_shard, split.rest, axis=0, tiled=True)

    padded = -(-(shard + 1) // 16) * 16
    small = jnp.concatenate([attn_gain, mlp_gain, qkv_bias])
    small_row = jnp.pad(small, (0, joint + width - small.shape[0]))[None]
    first_shard = jnp.concatenate(
        [
            jnp.concatenate([qkv_weight, out_weight.T], axis=1),
            small_row,
            jnp.zeros((padded - shard - 1, joint + width), BF16),
        ],
        axis=0,
    )
    weights = doubling.gather(first_shard)

    owner = me ^ jnp.array(doubling.offsets, jnp.int32)
    within = jnp.arange(padded, dtype=jnp.int32)
    target = jnp.where(within[None, :] < shard, owner[:, None] * shard + within[None, :], -1).reshape(1, -1)
    order = (jnp.arange(dim, dtype=jnp.int32)[:, None] == target).astype(BF16)
    by_owner = (owner[None, :] == jnp.arange(world, dtype=jnp.int32)[:, None]).astype(BF16)
    extras = jnp.concatenate(
        [part.reshape(world // 2, padded, -1)[:, shard, : small.shape[0]] for part in weights], axis=0
    )
    extras = dot_nn(by_owner, extras)
    gain_attn = extras[:, :shard].reshape(1, dim)
    gain_mlp = extras[:, shard : 2 * shard].reshape(1, dim)
    bias = extras[:, 2 * shard :].reshape(1, joint)

    at_row = lax.dynamic_slice_in_dim(segments, offset, rows, axis=1)
    zeros_before = jnp.sum((segments < 1).astype(jnp.int32), axis=1, keepdims=True)
    ones_before = jnp.sum((segments < 2).astype(jnp.int32), axis=1, keepdims=True)
    start = jnp.where(at_row == 0, 0, jnp.where(at_row == 1, zeros_before, ones_before))
    position = (offset + jnp.arange(rows, dtype=jnp.int32)[None, :] - start).reshape(count)
    lane = jnp.arange(LANES, dtype=jnp.int32)
    frequency = ROPE_BASE ** (-(lane % (HD // 2)).astype(F32) * 2.0 / HD)
    angle = position.astype(F32)[:, None] * frequency[None, :]
    cosine = jnp.cos(angle)
    sine = jnp.where(lane % HD < HD // 2, -1.0, 1.0)[None, :] * jnp.sin(angle)
    start_column = jnp.broadcast_to(start.reshape(count, 1), (count, LANES))
    start_row = jnp.broadcast_to(start[:, None, :], (seqs, 8, rows))
    block_arg = block.reshape(1).astype(jnp.int32)

    x = hidden.reshape(count, dim)
    cot = cotangent.reshape(count, dim)
    normed, q, kv = prep(x, gain_attn, order, weights, bias, cosine, sine, rows)
    kv = kv.reshape(seqs, rows, 2 * LANES)
    kv_x = bit_swap(kv, "cx", 0)
    kv_c, kv_xc = bit_swap(kv, "cc", 0), bit_swap(kv_x, "cc", 0)
    kv_all = jnp.concatenate([kv, kv_c, kv_x, kv_xc], axis=1)
    kv_all, cot_out = lax.optimization_barrier((kv_all, cot))
    cot_all = jnp.concatenate([cot, split.swap(cot_out)], axis=0)
    attended = attend(block_arg, q, kv_all, start_column, rows)
    resid, normed_post = project_out(attended, x, weights, order, gain_mlp, rows)

    normed_all = jnp.concatenate([normed_post, split.swap(normed_post)], axis=0)
    out_own, out_away, d_own, d_away, mlp_grad = mlp(normed_all, cot_all, mlp_weights)
    mlp_grad_shard = lax.psum_scatter(
        mlp_grad.reshape(world // 2, 2 * shard, 3 * columns), split.rest, scatter_dimension=0, tiled=False
    )

    d_came = split.swap(d_away)
    d_resid, d_branch, d_attended, mlp_gain_grad = project_out_back(
        d_own, d_came, resid, cot, weights, order, gain_mlp, rows
    )
    d_attended, out_away = lax.optimization_barrier((d_attended, out_away))
    output = (resid + out_own + split.swap(out_away).astype(F32)).astype(BF16)
    out_sum = doubling.scatter_sum(dot_tn(d_branch, attended).astype(BF16))
    dq, dkv = attend_back(block_arg, q, kv_all, d_attended, start_row, cosine, sine, rows)
    for axis in CTX:
        middle = dkv.shape[1] // 2
        came = bit_swap(dkv[:, middle:], axis, 0)
        dkv = (dkv[:, :middle].astype(F32) + came.astype(F32)).astype(BF16)
    d_joined, input_grad, attn_gain_grad, bias_grad = input_back(
        dq, dkv.reshape(count, 2 * LANES), x, d_resid, weights, order, gain_attn, cosine, sine, rows
    )

    split_at = width + LANES
    bias_grad = jnp.sum(bias_grad, axis=0)
    small_grads = jnp.concatenate(
        [
            jnp.sum(attn_gain_grad, axis=0).reshape(world, -1),
            jnp.sum(mlp_gain_grad, axis=0).reshape(world, -1),
            bias_grad[:split_at].reshape(world, -1),
            bias_grad[split_at:].reshape(world, -1),
        ],
        axis=1,
    ).astype(BF16)
    small_count = small_grads.shape[1]
    small_grads = jnp.pad(small_grads, ((0, 0), (0, joint - small_count)))
    place = jnp.where(within[None, :] == shard, owner[:, None], -1).reshape(1, -1)
    spread = (jnp.arange(world, dtype=jnp.int32)[:, None] == place).astype(BF16)
    qkv_grad = dot_tn(
        jnp.concatenate([normed, spread], axis=0), jnp.concatenate([d_joined, small_grads], axis=0)
    ).astype(BF16)
    qkv_sum = doubling.scatter_sum(qkv_grad).astype(F32)
    small_sum = qkv_sum[shard, :small_count]
    cut = (shard, 2 * shard, 2 * shard + split_at // world)

    low, high = split.exchange_back(lax.optimization_barrier(mlp_grad_shard))
    low, high = separate(low), separate(high)
    gate_grad, up_grad, down_grad_t = (
        jnp.concatenate([a, b], axis=1).astype(F32) for a, b in zip(low, high)
    )
    return (
        output.reshape(hidden.shape),
        input_grad.reshape(hidden.shape),
        small_sum[: cut[0]],
        qkv_sum[:shard],
        small_sum[cut[1] : cut[2]],
        small_sum[cut[2] :],
        out_sum[:shard].astype(F32).T,
        small_sum[cut[0] : cut[1]],
        gate_grad,
        up_grad,
        down_grad_t.T,
    )


def solution(mesh):
    fsdp, ctx = mesh.shape["fsdp"], mesh.shape["ctx"]
    inner = Mesh(mesh.devices.reshape(fsdp, 2, ctx // 2), AXES)
    tokens = P("fsdp", CTX, None)
    vector = P(AXES)
    by_row = P(AXES, None)
    by_column = P(None, AXES)
    return jax.shard_map(
        functools.partial(on_device, Split("cx"), Doubling(fsdp)),
        mesh=inner,
        in_specs=(
            tokens,
            P("fsdp", None),
            vector,
            by_row,
            vector,
            by_column,
            vector,
            by_row,
            by_row,
            by_column,
            tokens,
        ),
        out_specs=(
            tokens,
            tokens,
            vector,
            by_row,
            vector,
            vector,
            by_column,
            vector,
            by_row,
            by_row,
            by_column,
        ),
        check_vma=False,
    )
```

```python
import functools

import jax
import jax.numpy as jnp
from jax import lax
from jax.experimental import pallas as pl
from jax.experimental.pallas import tpu as pltpu
from jax.sharding import Mesh
from jax.sharding import PartitionSpec as P

HD = 64
LANES = 128
EPSILON = 1e-06
ROPE_BASE = 1000000.0
MASKED = -1e30
SCALE = HD ** (-0.5)
TILE = 256
MIB = 1 << 20
F32 = jnp.float32
BF16 = jnp.bfloat16
AXES = ("fsdp", "cx", "cc")
CTX = ("cx", "cc")


def dot_nn(a, b):
    return lax.dot_general(a, b, (((1,), (0,)), ((), ())), preferred_element_type=F32)


def dot_nt(a, b):
    return lax.dot_general(a, b, (((1,), (1,)), ((), ())), preferred_element_type=F32)


def dot_tn(a, b):
    return lax.dot_general(a, b, (((0,), (0,)), ((), ())), preferred_element_type=F32)


def lane_of(shape):
    return lax.broadcasted_iota(jnp.int32, shape, len(shape) - 1)


def swap_halves(block):
    lead = lane_of(block.shape) % HD < HD // 2
    return jnp.where(
        lead, pltpu.roll(block, LANES - HD // 2, 1), pltpu.roll(block, HD // 2, 1)
    )


def other_head(block):
    return jnp.concatenate([block[:, HD:], block[:, :HD]], axis=1)


def prep_kernel(
    x_ref, gain_ref, order_ref, w_low_ref, w_high_ref, bias_ref, cos_ref, sin_ref, normed_ref, q_ref, kv_ref
):
    x = x_ref[...].astype(F32)
    width = q_ref.shape[1]
    joint = bias_ref.shape[1]
    middle = w_low_ref.shape[0]
    inverse = lax.rsqrt(jnp.mean(x * x, axis=-1, keepdims=True) + EPSILON)
    normed = (x * inverse * gain_ref[...]).astype(BF16)
    ordered = dot_nn(normed, order_ref[...]).astype(BF16)
    normed_ref[...] = ordered
    joined = dot_nn(ordered[:, :middle], w_low_ref[:, :joint])
    joined = joined + dot_nn(ordered[:, middle:], w_high_ref[:, :joint]) + bias_ref[...]
    cosine, sine = cos_ref[...], sin_ref[...]
    for begin in range(0, width + LANES, LANES):
        block = joined[:, begin : begin + LANES]
        turned = block * cosine + swap_halves(block) * sine
        if begin < width:
            q_ref[:, begin : begin + LANES] = (turned * SCALE).astype(BF16)
        else:
            kv_ref[:, :LANES] = turned.astype(BF16)
    kv_ref[:, LANES:] = joined[:, width + LANES :].astype(BF16)


def rows_of(rows, cols):
    return pl.BlockSpec((rows, cols), lambda i: (i, 0))


def whole(value):
    return pl.BlockSpec(value.shape, lambda i: (0,) * value.ndim)


def prep(x, gain, order, weights, bias, cosine, sine, rows):
    count, dim = x.shape
    ordered = order.shape[1]
    joint = bias.shape[1]
    width = joint - 2 * LANES
    return pl.pallas_call(
        prep_kernel,
        grid=(count // rows,),
        in_specs=[
            rows_of(rows, dim),
            whole(gain),
            whole(order),
            whole(weights[0]),
            whole(weights[1]),
            whole(bias),
            rows_of(rows, LANES),
            rows_of(rows, LANES),
        ],
        out_specs=[rows_of(rows, ordered), rows_of(rows, width), rows_of(rows, 2 * LANES)],
        out_shape=[
            jax.ShapeDtypeStruct((count, ordered), BF16),
            jax.ShapeDtypeStruct((count, width), BF16),
            jax.ShapeDtypeStruct((count, 2 * LANES), BF16),
        ],
        compiler_params=pltpu.CompilerParams(vmem_limit_bytes=40 * MIB),
        cost_estimate=pl.CostEstimate(
            flops=2 * count * ordered * (joint + dim), bytes_accessed=12 * MIB, transcendentals=0
        ),
        name="norm_project_rotate",
    )(x, gain, order, weights[0], weights[1], bias, cosine, sine)


def back_in_order(value, order):
    high = value.astype(BF16)
    low = (value - high.astype(F32)).astype(BF16)
    return dot_nt(high, order) + dot_nt(low, order)


def out_kernel(attended_ref, x_ref, w_low_ref, w_high_ref, order_ref, gain_ref, resid_ref, normed_ref):
    width = attended_ref.shape[1]
    joint = w_low_ref.shape[1] - width
    attended = attended_ref[...]
    branch = jnp.concatenate(
        [dot_nt(attended, w_low_ref[:, joint:]), dot_nt(attended, w_high_ref[:, joint:])], axis=1
    )
    resid = x_ref[...].astype(F32) + back_in_order(branch, order_ref[...])
    inverse = lax.rsqrt(jnp.mean(resid * resid, axis=-1, keepdims=True) + EPSILON)
    resid_ref[...] = resid
    normed_ref[...] = (resid * inverse * gain_ref[...]).astype(BF16)


def project_out(attended, x, weights, order, gain, rows, seq):
    dim = x.shape[1]
    count = rows
    return pl.pallas_call(
        out_kernel,
        grid=(1,),
        in_specs=[
            rows_of(rows, attended.shape[1]),
            pl.BlockSpec((rows, dim), lambda i: (seq, 0)),
            whole(weights[0]),
            whole(weights[1]),
            whole(order),
            whole(gain),
        ],
        out_specs=[rows_of(rows, dim), rows_of(rows, dim)],
        out_shape=[jax.ShapeDtypeStruct((count, dim), F32), jax.ShapeDtypeStruct((count, dim), BF16)],
        compiler_params=pltpu.CompilerParams(vmem_limit_bytes=40 * MIB),
        cost_estimate=pl.CostEstimate(flops=6 * count * dim * dim, bytes_accessed=8 * MIB, transcendentals=0),
        name="project_out_norm",
    )(attended, x, weights[0], weights[1], order, gain)


def fold_rows(value):
    return jnp.sum(value.reshape(-1, 8, value.shape[1]), axis=0)


def norm_back(values, inverse, gain, incoming):
    scaled = incoming * gain
    mean_term = jnp.mean(scaled * values, axis=-1, keepdims=True)
    return inverse * scaled - values * inverse**3 * mean_term


def out_back_kernel(
    own_ref, core_ref, x_ref, resid_ref, cot_ref, w_low_ref, w_high_ref, order_ref, gain_ref,
    d_resid_ref, d_branch_ref, d_attended_ref, gain_grad_ref,
):
    width = d_attended_ref.shape[1]
    joint = w_low_ref.shape[1] - width
    middle = w_low_ref.shape[0]
    d_normed = own_ref[...] + core_ref[...].astype(F32) + x_ref[...].astype(F32)
    resid = resid_ref[...]
    inverse = lax.rsqrt(jnp.mean(resid * resid, axis=-1, keepdims=True) + EPSILON)
    d_resid = cot_ref[...].astype(F32) + norm_back(resid, inverse, gain_ref[...], d_normed)
    d_resid_ref[...] = d_resid
    d_branch = dot_nn(d_resid.astype(BF16), order_ref[...]).astype(BF16)
    d_branch_ref[...] = d_branch
    d_attended = dot_nn(d_branch[:, :middle], w_low_ref[:, joint:])
    d_attended = d_attended + dot_nn(d_branch[:, middle:], w_high_ref[:, joint:])
    d_attended_ref[...] = d_attended.astype(BF16)
    gain_grad_ref[...] = fold_rows(d_normed * resid * inverse)


def project_out_back(terms, resid, cot, weights, order, gain, rows, seq):
    count, dim = resid.shape
    ordered = order.shape[1]
    width = dim
    return pl.pallas_call(
        out_back_kernel,
        grid=(1,),
        in_specs=[
            rows_of(rows, dim),
            rows_of(rows, dim),
            rows_of(rows, dim),
            rows_of(rows, dim),
            pl.BlockSpec((rows, dim), lambda i: (seq, 0)),
            whole(weights[0]),
            whole(weights[1]),
            whole(order),
            whole(gain),
        ],
        out_specs=[
            rows_of(rows, dim),
            rows_of(rows, ordered),
            rows_of(rows, width),
            pl.BlockSpec((8, dim), lambda i: (0, 0)),
        ],
        out_shape=[
            jax.ShapeDtypeStruct((count, dim), F32),
            jax.ShapeDtypeStruct((count, ordered), BF16),
            jax.ShapeDtypeStruct((count, width), BF16),
            jax.ShapeDtypeStruct((8, dim), F32),
        ],
        compiler_params=pltpu.CompilerParams(vmem_limit_bytes=40 * MIB),
        cost_estimate=pl.CostEstimate(flops=4 * count * dim * dim, bytes_accessed=12 * MIB, transcendentals=0),
        name="norm_back_project",
    )(*terms, resid, cot, weights[0], weights[1], order, gain)


def input_back_kernel(
    dq_ref, own_ref, core_ref, from_x_ref, x_ref, d_resid_ref, w_low_ref, w_high_ref, order_ref, gain_ref, cos_ref, sin_ref,
    d_joined_ref, input_grad_ref, gain_grad_ref, bias_grad_ref,
):
    width = dq_ref.shape[1]
    joint = d_joined_ref.shape[1]
    dkv = own_ref[...] + core_ref[...].astype(F32) + from_x_ref[...].astype(F32)
    dk = dkv[:, :LANES]
    dk = dk * cos_ref[...] - swap_halves(dk) * sin_ref[...]
    d_joined = jnp.concatenate([dq_ref[...], dk.astype(BF16), dkv[:, LANES:].astype(BF16)], axis=1)
    d_joined_ref[...] = d_joined
    d_normed = jnp.concatenate(
        [dot_nt(d_joined, w_low_ref[:, :joint]), dot_nt(d_joined, w_high_ref[:, :joint])], axis=1
    )
    d_normed = back_in_order(d_normed, order_ref[...])
    x = x_ref[...].astype(F32)
    inverse = lax.rsqrt(jnp.mean(x * x, axis=-1, keepdims=True) + EPSILON)
    input_grad_ref[...] = (d_resid_ref[...] + norm_back(x, inverse, gain_ref[...], d_normed)).astype(BF16)
    gain_grad_ref[...] = fold_rows(d_normed * x * inverse)
    bias_grad_ref[...] = fold_rows(d_joined.astype(F32))


def input_back(dq, terms, x, d_resid, weights, order, gain, cosine, sine, rows, seq):
    count, dim = d_resid.shape
    width = dq.shape[1]
    joint = width + 2 * LANES
    return pl.pallas_call(
        input_back_kernel,
        grid=(1,),
        in_specs=[
            rows_of(rows, width),
            rows_of(rows, 2 * LANES),
            rows_of(rows, 2 * LANES),
            rows_of(rows, 2 * LANES),
            pl.BlockSpec((rows, dim), lambda i: (seq, 0)),
            rows_of(rows, dim),
            whole(weights[0]),
            whole(weights[1]),
            whole(order),
            whole(gain),
            pl.BlockSpec((rows, LANES), lambda i: (seq, 0)),
            pl.BlockSpec((rows, LANES), lambda i: (seq, 0)),
        ],
        out_specs=[
            rows_of(rows, joint),
            rows_of(rows, dim),
            pl.BlockSpec((8, dim), lambda i: (0, 0)),
            pl.BlockSpec((8, joint), lambda i: (0, 0)),
        ],
        out_shape=[
            jax.ShapeDtypeStruct((count, joint), BF16),
            jax.ShapeDtypeStruct((count, dim), BF16),
            jax.ShapeDtypeStruct((8, dim), F32),
            jax.ShapeDtypeStruct((8, joint), F32),
        ],
        compiler_params=pltpu.CompilerParams(vmem_limit_bytes=40 * MIB),
        cost_estimate=pl.CostEstimate(flops=6 * count * dim * joint, bytes_accessed=12 * MIB, transcendentals=0),
        name="input_gradient",
    )(dq, *terms, x, d_resid, weights[0], weights[1], order, gain, cosine, sine)


def seq_rows(seq, rows, cols):
    return pl.BlockSpec((rows, cols), lambda i: (seq, 0))


def piece_of(seq, rows):
    return pl.BlockSpec((1, rows, 2 * LANES), lambda i: (seq, 0, 0))


def keys_and_values(piece_refs):
    joint = jnp.concatenate([ref[0] for ref in piece_refs], axis=0)
    key, value = joint[:, :LANES], joint[:, LANES:]
    return (key, other_head(key)), (value, other_head(value))


def attend_kernel(block_ref, q_ref, kv_0, kv_1, kv_2, kv_3, start_ref, out_ref):
    rows, width = q_ref.shape
    length = 4 * rows
    heads = width // HD
    group = heads // 2
    keys, values = keys_and_values((kv_0, kv_1, kv_2, kv_3))
    upper_key = lane_of((length, LANES)) >= HD
    upper = lane_of((rows, LANES)) >= HD
    query_at = block_ref[0] * rows + lax.broadcasted_iota(jnp.int32, (rows, length), 0)
    key_at = jnp.concatenate(
        [
            (block_ref[0] ^ place) * rows + lax.broadcasted_iota(jnp.int32, (rows, rows), 1)
            for place in range(4)
        ],
        axis=1,
    )
    allowed = (key_at <= query_at) & (key_at >= start_ref[:, :1])
    bias = jnp.where(allowed, 0.0, MASKED)
    one = jnp.ones((), BF16)
    for pair in range(heads // 2):
        at = slice(pair * LANES, (pair + 1) * LANES)
        both = q_ref[:, at]
        parts = []
        for place in range(2):
            owner = (2 * pair + place) // group
            moved = int(owner != place)
            side = upper if place else ~upper
            side_key = upper_key if place else ~upper_key
            query = jnp.where(side, both, jnp.zeros_like(both))
            score = dot_nt(query, keys[moved]) + bias
            top = jnp.max(score, axis=1, keepdims=True)
            weight = jnp.exp(score - top).astype(BF16)
            mixed = dot_nn(weight, jnp.where(side_key, values[moved], one))
            parts.append(mixed / pltpu.roll(mixed, HD, 1))
        out_ref[:, at] = jnp.where(upper, parts[1], parts[0]).astype(BF16)


def attend(block, q, kv_pieces, start, rows, seq):
    width = q.shape[1]
    heads = width // HD
    return pl.pallas_call(
        attend_kernel,
        grid=(1,),
        in_specs=[
            pl.BlockSpec(memory_space=pltpu.SMEM),
            seq_rows(seq, rows, width),
            *[piece_of(seq, rows)] * 4,
            seq_rows(seq, rows, LANES),
        ],
        out_specs=seq_rows(0, rows, width),
        out_shape=jax.ShapeDtypeStruct((rows, width), BF16),
        compiler_params=pltpu.CompilerParams(vmem_limit_bytes=48 * MIB),
        cost_estimate=pl.CostEstimate(
            flops=32 * rows * rows * LANES * heads,
            bytes_accessed=4 * rows * width,
            transcendentals=4 * rows * rows * heads,
        ),
        name="attention_forward",
    )(block, q, *kv_pieces, start)


def attend_back_kernel(
    block_ref, q_ref, kv_0, kv_1, kv_2, kv_3, back_ref, start_ref, cos_ref, sin_ref,
    dq_ref, own_ref, core_ref, x_ref, dk_sum, dv_sum,
):
    rows, width = q_ref.shape
    length = 4 * rows
    heads = width // HD
    group = heads // 2
    keys, values = keys_and_values((kv_0, kv_1, kv_2, kv_3))
    key_t = keys[0].astype(F32).T.astype(BF16)
    keys_t = (key_t, jnp.concatenate([key_t[HD:], key_t[:HD]], axis=0))
    upper = lane_of((rows, LANES)) >= HD
    upper_t = lax.broadcasted_iota(jnp.int32, (LANES, rows), 0) >= HD
    query_at = block_ref[0] * rows + lax.broadcasted_iota(jnp.int32, (length, rows), 1)
    key_at = jnp.concatenate(
        [
            (block_ref[0] ^ place) * rows + lax.broadcasted_iota(jnp.int32, (rows, rows), 0)
            for place in range(4)
        ],
        axis=0,
    )
    allowed = (key_at <= query_at) & (key_at >= start_ref[0, :1, :])
    bias = jnp.where(allowed, 0.0, MASKED)
    cosine, sine = cos_ref[...], sin_ref[...]
    dk_sum[...] = jnp.zeros_like(dk_sum)
    dv_sum[...] = jnp.zeros_like(dv_sum)
    for pair in range(heads // 2):
        at = slice(pair * LANES, (pair + 1) * LANES)
        both = q_ref[:, at]
        back_both = back_ref[:, at]
        parts = []
        for place in range(2):
            owner = (2 * pair + place) // group
            moved = int(owner != place)
            side = upper if place else ~upper
            query = jnp.where(side, both, jnp.zeros_like(both))
            back = jnp.where(side, back_both, jnp.zeros_like(back_both))
            score = dot_nt(keys[moved], query) + bias
            weight = jnp.exp(score - jnp.max(score, axis=0, keepdims=True))
            prob = weight * (1.0 / jnp.sum(weight, axis=0, keepdims=True))
            dv_sum[owner] += dot_nn(prob.astype(BF16), back)
            d_prob = dot_nt(values[moved], back)
            level = jnp.sum(prob * d_prob, axis=0, keepdims=True)
            d_score = (prob * (d_prob - level)).astype(BF16)
            dk_sum[owner] += dot_nn(d_score, query)
            parts.append(dot_nn(keys_t[moved], d_score))
        d_query = jnp.where(upper_t, parts[1], parts[0]).T * SCALE
        dq_ref[:, at] = (d_query * cosine - swap_halves(d_query) * sine).astype(BF16)
    lower_key = lane_of((length, LANES)) < HD
    for total, begin in ((dk_sum, 0), (dv_sum, LANES)):
        first, second = total[0], total[1]
        first = first + pltpu.roll(first, HD, 1)
        second = second + pltpu.roll(second, HD, 1)
        both = jnp.where(lower_key, first, second)
        cols = slice(begin, begin + LANES)
        own_ref[:, cols] = both[:rows]
        core_ref[:rows, cols] = both[rows : 2 * rows].astype(BF16)
        core_ref[rows:, cols] = both[3 * rows :].astype(BF16)
        x_ref[:, cols] = both[2 * rows : 3 * rows]


def parts_of(rows, cols):
    specs = [seq_rows(0, rows, cols), seq_rows(0, 2 * rows, cols), seq_rows(0, rows, cols)]
    shapes = [
        jax.ShapeDtypeStruct((rows, cols), F32),
        jax.ShapeDtypeStruct((2 * rows, cols), BF16),
        jax.ShapeDtypeStruct((rows, cols), F32),
    ]
    return specs, shapes


def attend_back(block, q, kv_pieces, back, start, cosine, sine, rows, seq):
    width = q.shape[1]
    length = 4 * rows
    heads = width // HD
    specs, shapes = parts_of(rows, 2 * LANES)
    return pl.pallas_call(
        attend_back_kernel,
        grid=(1,),
        in_specs=[
            pl.BlockSpec(memory_space=pltpu.SMEM),
            seq_rows(seq, rows, width),
            *[piece_of(seq, rows)] * 4,
            seq_rows(0, rows, width),
            pl.BlockSpec((1, 8, rows), lambda i: (seq, 0, 0)),
            seq_rows(seq, rows, LANES),
            seq_rows(seq, rows, LANES),
        ],
        out_specs=[seq_rows(0, rows, width), *specs],
        out_shape=[jax.ShapeDtypeStruct((rows, width), BF16), *shapes],
        scratch_shapes=[
            pltpu.VMEM((2, length, LANES), F32),
            pltpu.VMEM((2, length, LANES), F32),
        ],
        compiler_params=pltpu.CompilerParams(vmem_limit_bytes=48 * MIB),
        cost_estimate=pl.CostEstimate(
            flops=80 * rows * rows * LANES * heads,
            bytes_accessed=8 * rows * width,
            transcendentals=4 * rows * rows * heads,
        ),
        name="attention_backward",
    )(block, q, *kv_pieces, back, start, cosine, sine)


def mlp_kernel(
    n_0, n_1, n_2, n_3, c_0, c_1, c_2, c_3, gate_ref, up_ref, down_ref,
    own_ref, core_ref, x_ref, d_own_ref, d_core_ref, d_x_ref, kept_ref,
    normed, cot, out_sum, d_sum,
):
    step = pl.program_id(0)
    rows = own_ref.shape[0]

    @pl.when(step == 0)
    def _():
        for place, (n_ref, c_ref) in enumerate(zip((n_0, n_1, n_2, n_3), (c_0, c_1, c_2, c_3))):
            normed[place * rows : (place + 1) * rows] = n_ref[...]
            cot[place * rows : (place + 1) * rows] = c_ref[...]
        out_sum[...] = jnp.zeros_like(out_sum)
        d_sum[...] = jnp.zeros_like(d_sum)

    for begin in range(0, 4 * rows, 2 * rows):
        at = slice(begin, begin + 2 * rows)
        w_gate, w_up, w_down = gate_ref[...], up_ref[...], down_ref[...]
        gate = dot_nn(normed[at], w_gate)
        up = dot_nn(normed[at], w_up)
        d_act = dot_nn(cot[at], w_down)
        sigmoid = 1.0 / (1.0 + jnp.exp(-gate))
        swish = gate * sigmoid
        act = (swish * up).astype(BF16)
        d_gate = (d_act * up * sigmoid * (1.0 + gate * (1.0 - sigmoid))).astype(BF16)
        d_up = (d_act * swish).astype(BF16)
        kept_ref[0, at] = d_gate
        kept_ref[1, at] = d_up
        kept_ref[2, at] = act
        out_sum[at] += dot_nt(act, w_down)
        d_sum[at] += dot_nt(d_gate, w_gate) + dot_nt(d_up, w_up)

    @pl.when(step == pl.num_programs(0) - 1)
    def _():
        for total, own, core, x in ((out_sum, own_ref, core_ref, x_ref), (d_sum, d_own_ref, d_core_ref, d_x_ref)):
            own[...] = total[:rows]
            core[:rows] = total[rows : 2 * rows].astype(BF16)
            core[rows:] = total[3 * rows :].astype(BF16)
            x[...] = total[2 * rows : 3 * rows]


def mlp(normed, cot, weights, seq):
    rows, dim = normed[0].shape
    columns = weights.shape[1] // 3
    tiles = columns // TILE
    specs, shapes = parts_of(rows, dim)
    return pl.pallas_call(
        mlp_kernel,
        grid=(tiles,),
        in_specs=[
            *[seq_rows(0, rows, dim)] * 4,
            *[seq_rows(seq, rows, dim)] * 4,
            pl.BlockSpec((dim, TILE), lambda i: (0, i)),
            pl.BlockSpec((dim, TILE), lambda i: (0, tiles + i)),
            pl.BlockSpec((dim, TILE), lambda i: (0, 2 * tiles + i)),
        ],
        out_specs=[*specs, *specs, pl.BlockSpec((3, 4 * rows, TILE), lambda i: (0, 0, i))],
        out_shape=[*shapes, *shapes, jax.ShapeDtypeStruct((3, 4 * rows, columns), BF16)],
        scratch_shapes=[
            pltpu.VMEM((4 * rows, dim), BF16),
            pltpu.VMEM((4 * rows, dim), BF16),
            pltpu.VMEM((4 * rows, dim), F32),
            pltpu.VMEM((4 * rows, dim), F32),
        ],
        compiler_params=pltpu.CompilerParams(vmem_limit_bytes=56 * MIB),
        cost_estimate=pl.CostEstimate(
            flops=48 * rows * dim * columns,
            bytes_accessed=6 * dim * columns + 24 * rows * columns,
            transcendentals=4 * rows * columns,
        ),
        name="feed_forward",
    )(*normed, *cot, weights, weights, weights)


def mlp_grad_kernel(*refs):
    normed_refs, cot_refs, kept_refs, grad_ref, turned = refs[:8], refs[8:16], refs[16:18], refs[18], refs[19]
    step = pl.program_id(0)
    rows = normed_refs[0].shape[0]
    count = 4 * rows

    def turn(sources):
        for place, ref in enumerate(sources):
            turned[:, place * rows : (place + 1) * rows] = ref[...].T

    pl.when(step == 0)(functools.partial(turn, normed_refs))
    pl.when(step == 2)(functools.partial(turn, cot_refs))
    total = dot_nn(turned[:, :count], kept_refs[0][0]) + dot_nn(turned[:, count:], kept_refs[1][0])
    grad_ref[...] = total.astype(BF16)


def mlp_grad(normed, cot, kept):
    rows, dim = normed[0][0].shape
    columns = kept[0].shape[2]
    kept_block = pl.BlockSpec((1, 4 * rows, columns), lambda i: (i, 0, 0))
    return pl.pallas_call(
        mlp_grad_kernel,
        grid=(3,),
        in_specs=[
            *[seq_rows(0, rows, dim)] * 8,
            *[seq_rows(0, rows, dim)] * 4,
            *[seq_rows(1, rows, dim)] * 4,
            kept_block,
            kept_block,
        ],
        out_specs=pl.BlockSpec((dim, columns), lambda i: (0, i)),
        out_shape=jax.ShapeDtypeStruct((dim, 3 * columns), BF16),
        scratch_shapes=[pltpu.VMEM((dim, 8 * rows), BF16)],
        compiler_params=pltpu.CompilerParams(vmem_limit_bytes=60 * MIB),
        cost_estimate=pl.CostEstimate(
            flops=48 * rows * dim * columns,
            bytes_accessed=6 * dim * columns + 48 * rows * columns,
            transcendentals=0,
        ),
        name="feed_forward_gradients",
    )(*normed[0], *normed[1], *cot, *cot, *kept)


def pack_kernel(block_ref, gate_ref, up_ref, down_ref, *refs):
    out_refs, scratch = refs[:4], refs[4]
    shard, ff = gate_ref.shape
    quarter = scratch.shape[2] // 4
    for place, ref in enumerate((gate_ref, up_ref, down_ref)):
        scratch[place, :, :ff] = ref[...].astype(F32)
        scratch[place, :, ff:] = jnp.zeros((shard, 4 * quarter - ff), F32)
    for place, out_ref in enumerate(out_refs):
        begin = pl.multiple_of((block_ref[0] ^ place) * quarter, LANES)
        for part in range(3):
            out_ref[:, part * quarter : (part + 1) * quarter] = scratch[part, :, pl.ds(begin, quarter)].astype(BF16)


def pack(block, gate, up, down_t, quarter):
    shard = gate.shape[0]
    return pl.pallas_call(
        pack_kernel,
        in_specs=[pl.BlockSpec(memory_space=pltpu.SMEM)] + [pl.BlockSpec(memory_space=pltpu.VMEM)] * 3,
        out_specs=[pl.BlockSpec(memory_space=pltpu.VMEM)] * 4,
        out_shape=[jax.ShapeDtypeStruct((shard, 3 * quarter), BF16)] * 4,
        scratch_shapes=[pltpu.VMEM((3, shard, 4 * quarter), F32)],
        name="pack_columns",
    )(block, gate, up, down_t)


def pick(options, index):
    value = options[0]
    for place in range(1, len(options)):
        value = jnp.where(index == place, options[place], value)
    return value


def assemble_kernel(block_ref, *refs):
    pieces, out_ref, scratch = refs[:4], refs[4], refs[5]
    shard = pieces[0].shape[0]
    values = [ref[...].astype(F32) for ref in pieces]
    for owner in range(4):
        scratch[owner * shard : (owner + 1) * shard] = pick(values, block_ref[0] ^ owner)
    out_ref[...] = scratch[...].astype(BF16)


def assemble(block, pieces):
    shard, columns = pieces[0].shape
    return pl.pallas_call(
        assemble_kernel,
        in_specs=[pl.BlockSpec(memory_space=pltpu.SMEM)] + [pl.BlockSpec(memory_space=pltpu.VMEM)] * 4,
        out_specs=pl.BlockSpec(memory_space=pltpu.VMEM),
        out_shape=jax.ShapeDtypeStruct((4 * shard, columns), BF16),
        scratch_shapes=[pltpu.VMEM((4 * shard, columns), F32)],
        name="assemble_rows",
    )(block, *pieces)


def cut_kernel(block_ref, value_ref, *refs):
    out_refs, scratch = refs[:4], refs[4]
    shard = out_refs[0].shape[0]
    scratch[...] = value_ref[...].astype(F32)
    values = [scratch[owner * shard : (owner + 1) * shard] for owner in range(4)]
    for place, out_ref in enumerate(out_refs):
        out_ref[...] = pick(values, block_ref[0] ^ place).astype(BF16)


def cut(block, value):
    shard, columns = value.shape[0] // 4, value.shape[1]
    return pl.pallas_call(
        cut_kernel,
        in_specs=[pl.BlockSpec(memory_space=pltpu.SMEM), pl.BlockSpec(memory_space=pltpu.VMEM)],
        out_specs=[pl.BlockSpec(memory_space=pltpu.VMEM)] * 4,
        out_shape=[jax.ShapeDtypeStruct((shard, columns), BF16)] * 4,
        scratch_shapes=[pltpu.VMEM(value.shape, F32)],
        name="cut_rows",
    )(block, value)


def unpack_kernel(block_ref, *refs):
    pieces, out_refs, scratch = refs[:4], refs[4:7], refs[7]
    ff = out_refs[0].shape[1]
    quarter = scratch.shape[2] // 4
    for place, ref in enumerate(pieces):
        begin = pl.multiple_of((block_ref[0] ^ place) * quarter, LANES)
        for part in range(3):
            scratch[part, :, pl.ds(begin, quarter)] = ref[:, part * quarter : (part + 1) * quarter].astype(F32)
    for part, out_ref in enumerate(out_refs):
        out_ref[...] = scratch[part, :, :ff]


def unpack(block, pieces, ff):
    shard, columns = pieces[0].shape
    return pl.pallas_call(
        unpack_kernel,
        in_specs=[pl.BlockSpec(memory_space=pltpu.SMEM)] + [pl.BlockSpec(memory_space=pltpu.VMEM)] * 4,
        out_specs=[pl.BlockSpec(memory_space=pltpu.VMEM)] * 3,
        out_shape=[jax.ShapeDtypeStruct((shard, ff), F32)] * 3,
        scratch_shapes=[pltpu.VMEM((3, shard, columns // 3 * 4), F32)],
        name="unpack_columns",
    )(block, *pieces)


def bit_swap(value, axis, bit=0):
    size = lax.axis_size(axis)
    return lax.ppermute(value, axis, [(i, i ^ (1 << bit)) for i in range(size)])


def ctx_swap(value, jump):
    return lax.ppermute(value, CTX, [(i, i ^ jump) for i in range(4)])


def after(first, *values):
    return lax.optimization_barrier((first, *values))


def gather_four(value):
    from_x = bit_swap(value, "cx")
    return [value, bit_swap(value, "cc"), from_x, bit_swap(from_x, "cc")]


def sum_four(own, core, x):
    rows = own.shape[0]
    from_core = bit_swap(core, "cc")
    x = (x + from_core[rows:].astype(F32)).astype(BF16)
    return own, from_core, bit_swap(x, "cx")


class Doubling:
    def __init__(self, fsdp):
        bits = fsdp.bit_length() - 1
        self.steps = [("fsdp", bit) for bit in reversed(range(bits))] + [("cx", 0), ("cc", 0)]
        weight = {"cc": 1, "cx": 2}
        self.offsets = [0]
        for axis, bit in self.steps:
            jump = weight[axis] if axis in weight else 4 << bit
            self.offsets += [offset ^ jump for offset in self.offsets]

    def gather(self, value, before_x):
        for axis, bit in self.steps[:-1]:
            if axis == "cx":
                value, before_x = after(value, before_x)
            value = jnp.concatenate([value, bit_swap(value, axis, bit)], axis=0)
        return (value, bit_swap(value, *self.steps[-1])), before_x

    def scatter_sum(self, value):
        for axis, bit in reversed(self.steps):
            middle = value.shape[0] // 2
            came = bit_swap(value[middle:], axis, bit)
            value = (value[:middle].astype(F32) + came.astype(F32)).astype(BF16)
        return value


def on_device(
    doubling,
    hidden,
    segments,
    attn_gain,
    qkv_weight,
    qkv_bias,
    out_weight,
    mlp_gain,
    gate_weight,
    up_weight,
    down_weight,
    cotangent,
):
    seqs, rows, dim = hidden.shape
    count = seqs * rows
    shard = attn_gain.shape[0]
    world = dim // shard
    joint = qkv_weight.shape[1]
    width = joint - 2 * LANES
    ff = gate_weight.shape[1]
    block = lax.axis_index("cx") * lax.axis_size("cc") + lax.axis_index("cc")
    me = lax.axis_index("fsdp") * lax.axis_size(CTX) + block
    offset = block * rows
    block_arg = block.reshape(1).astype(jnp.int32)
    x = hidden.reshape(count, dim)
    cot = cotangent.reshape(count, dim)

    quarter = -(-ff // (4 * TILE)) * TILE
    pieces = pack(block_arg, gate_weight, up_weight, down_weight.T, quarter)
    pieces = [pieces[0]] + [ctx_swap(pieces[jump], jump) for jump in range(1, 4)]
    mlp_shard = assemble(block_arg, pieces)
    mlp_weights = lax.all_gather(mlp_shard, "fsdp", axis=0, tiled=True)
    _, cot_late = after(pieces[3], cot)
    cot_x = bit_swap(cot_late, "cx")

    padded = -(-(shard + 1) // 16) * 16
    small = jnp.concatenate([attn_gain, mlp_gain, qkv_bias])
    small_row = jnp.pad(small, (0, joint + width - small.shape[0]))[None]
    first_shard = jnp.concatenate(
        [
            jnp.concatenate([qkv_weight, out_weight.T], axis=1),
            small_row,
            jnp.zeros((padded - shard - 1, joint + width), BF16),
        ],
        axis=0,
    )
    weights, cot_x = doubling.gather(first_shard, cot_x)
    cot_all = [cot, bit_swap(cot_late, "cc"), cot_x, bit_swap(cot_x, "cc")]

    owner = me ^ jnp.array(doubling.offsets, jnp.int32)
    within = jnp.arange(padded, dtype=jnp.int32)
    target = jnp.where(within[None, :] < shard, owner[:, None] * shard + within[None, :], -1).reshape(1, -1)
    order = (jnp.arange(dim, dtype=jnp.int32)[:, None] == target).astype(BF16)
    by_owner = (owner[None, :] == jnp.arange(world, dtype=jnp.int32)[:, None]).astype(BF16)
    extras = jnp.concatenate(
        [part.reshape(world // 2, padded, -1)[:, shard, : small.shape[0]] for part in weights], axis=0
    )
    extras = dot_nn(by_owner, extras)
    gain_attn = extras[:, :shard].reshape(1, dim)
    gain_mlp = extras[:, shard : 2 * shard].reshape(1, dim)
    bias = extras[:, 2 * shard :].reshape(1, joint)

    at_row = lax.dynamic_slice_in_dim(segments, offset, rows, axis=1)
    zeros_before = jnp.sum((segments < 1).astype(jnp.int32), axis=1, keepdims=True)
    ones_before = jnp.sum((segments < 2).astype(jnp.int32), axis=1, keepdims=True)
    start = jnp.where(at_row == 0, 0, jnp.where(at_row == 1, zeros_before, ones_before))
    position = (offset + jnp.arange(rows, dtype=jnp.int32)[None, :] - start).reshape(count)
    lane = jnp.arange(LANES, dtype=jnp.int32)
    frequency = ROPE_BASE ** (-(lane % (HD // 2)).astype(F32) * 2.0 / HD)
    angle = position.astype(F32)[:, None] * frequency[None, :]
    cosine = jnp.cos(angle)
    sine = jnp.where(lane % HD < HD // 2, -1.0, 1.0)[None, :] * jnp.sin(angle)
    start_column = jnp.broadcast_to(start.reshape(count, 1), (count, LANES))
    start_row = jnp.broadcast_to(start[:, None, :], (seqs, 8, rows))

    normed, q, kv = prep(x, gain_attn, order, weights, bias, cosine, sine, rows)
    kv_all = gather_four(kv.reshape(seqs, rows, 2 * LANES))
    attended, resid, normed_all = [], [], []
    for seq in range(seqs):
        attended.append(attend(block_arg, q, kv_all, start_column, rows, seq))
        resid_one, normed_one = project_out(attended[seq], x, weights, order, gain_mlp, rows, seq)
        resid.append(resid_one)
        normed_all.append(gather_four(normed_one))

    out_parts, d_terms, kept = [], [], []
    for seq in range(seqs):
        result = mlp(normed_all[seq], cot_all, mlp_weights, seq)
        out_parts.append(result[:3])
        d_terms.append(sum_four(*result[3:6]))
        kept.append(result[6])
    grads = mlp_grad(normed_all, cot_all, kept)
    grads = lax.psum_scatter(
        grads.reshape(world // 4, 4 * shard, 3 * quarter), "fsdp", scatter_dimension=0, tiled=False
    )

    d_resid, d_branch, d_attended, mlp_gain_grad = [], [], [], []
    for seq in range(seqs):
        result = project_out_back(d_terms[seq], resid[seq], cot, weights, order, gain_mlp, rows, seq)
        for place, value in zip((d_resid, d_branch, d_attended, mlp_gain_grad), result):
            place.append(value)
    out_grad = dot_tn(jnp.concatenate(d_branch, axis=0), jnp.concatenate(attended, axis=0)).astype(BF16)
    out_sum = doubling.scatter_sum(out_grad)
    dq, dkv_terms = [], []
    for seq in range(seqs):
        result = attend_back(block_arg, q, kv_all, d_attended[seq], start_row, cosine, sine, rows, seq)
        dq.append(result[0])
        dkv_terms.append(sum_four(*result[1:]))
    d_joined, input_grad, attn_gain_grad, bias_grad = [], [], [], []
    for seq in range(seqs):
        result = input_back(
            dq[seq], dkv_terms[seq], x, d_resid[seq], weights, order, gain_attn, cosine, sine, rows, seq
        )
        for place, value in zip((d_joined, input_grad, attn_gain_grad, bias_grad), result):
            place.append(value)

    output = []
    for seq in range(seqs):
        _, *parts = after(d_attended[seq], *out_parts[seq])
        own, from_core, from_x = sum_four(*parts)
        output.append(
            (resid[seq] + own + from_core[:rows].astype(F32) + from_x.astype(F32)).astype(BF16)
        )

    split_at = width + LANES
    bias_grad = jnp.sum(sum(bias_grad), axis=0)
    small_grads = jnp.concatenate(
        [
            jnp.sum(sum(attn_gain_grad), axis=0).reshape(world, -1),
            jnp.sum(sum(mlp_gain_grad), axis=0).reshape(world, -1),
            bias_grad[:split_at].reshape(world, -1),
            bias_grad[split_at:].reshape(world, -1),
        ],
        axis=1,
    ).astype(BF16)
    small_count = small_grads.shape[1]
    small_grads = jnp.pad(small_grads, ((0, 0), (0, joint - small_count)))
    place = jnp.where(within[None, :] == shard, owner[:, None], -1).reshape(1, -1)
    spread = (jnp.arange(world, dtype=jnp.int32)[:, None] == place).astype(BF16)
    qkv_grad = dot_tn(
        jnp.concatenate([normed, spread], axis=0), jnp.concatenate([*d_joined, small_grads], axis=0)
    ).astype(BF16)
    qkv_sum = doubling.scatter_sum(qkv_grad).astype(F32)
    small_sum = qkv_sum[shard, :small_count]
    at = (shard, 2 * shard, 2 * shard + split_at // world)

    pieces = cut(block_arg, lax.optimization_barrier(grads))
    pieces = [pieces[0]] + [ctx_swap(pieces[jump], jump) for jump in range(1, 4)]
    gate_grad, up_grad, down_grad_t = unpack(block_arg, pieces, ff)
    return (
        jnp.stack(output),
        jnp.stack(input_grad),
        small_sum[: at[0]],
        qkv_sum[:shard],
        small_sum[at[1] : at[2]],
        small_sum[at[2] :],
        out_sum[:shard].astype(F32).T,
        small_sum[at[0] : at[1]],
        gate_grad,
        up_grad,
        down_grad_t.T,
    )


def solution(mesh):
    fsdp, ctx = mesh.shape["fsdp"], mesh.shape["ctx"]
    inner = Mesh(mesh.devices.reshape(fsdp, 2, ctx // 2), AXES)
    tokens = P("fsdp", CTX, None)
    vector = P(AXES)
    by_row = P(AXES, None)
    by_column = P(None, AXES)
    return jax.shard_map(
        functools.partial(on_device, Doubling(fsdp)),
        mesh=inner,
        in_specs=(
            tokens,
            P("fsdp", None),
            vector,
            by_row,
            vector,
            by_column,
            vector,
            by_row,
            by_row,
            by_column,
            tokens,
        ),
        out_specs=(
            tokens,
            tokens,
            vector,
            by_row,
            vector,
            vector,
            by_column,
            vector,
            by_row,
            by_row,
            by_column,
        ),
        check_vma=False,
    )
```

```python
import functools

import jax
import jax.numpy as jnp
from jax import lax
from jax.experimental import pallas as pl
from jax.experimental.pallas import tpu as pltpu
from jax.sharding import Mesh
from jax.sharding import PartitionSpec as P

HD = 64
LANES = 128
EPSILON = 1e-06
ROPE_BASE = 1000000.0
MASKED = -1e30
SCALE = HD ** (-0.5)
TILE = 256
MIB = 1 << 20
F32 = jnp.float32
BF16 = jnp.bfloat16
AXES = ("fsdp", "cx", "cc")
CTX = ("cx", "cc")


def dot_nn(a, b):
    return lax.dot_general(a, b, (((1,), (0,)), ((), ())), preferred_element_type=F32)


def dot_nt(a, b):
    return lax.dot_general(a, b, (((1,), (1,)), ((), ())), preferred_element_type=F32)


def dot_tn(a, b):
    return lax.dot_general(a, b, (((0,), (0,)), ((), ())), preferred_element_type=F32)


def lane_of(shape):
    return lax.broadcasted_iota(jnp.int32, shape, len(shape) - 1)


def swap_halves(block):
    lead = lane_of(block.shape) % HD < HD // 2
    return jnp.where(
        lead, pltpu.roll(block, LANES - HD // 2, 1), pltpu.roll(block, HD // 2, 1)
    )


def other_head(block):
    return jnp.concatenate([block[:, HD:], block[:, :HD]], axis=1)


def prep_kernel(
    x_ref, gain_ref, order_ref, w_low_ref, w_high_ref, bias_ref, cos_ref, sin_ref, normed_ref, q_ref, kv_ref
):
    x = x_ref[...].astype(F32)
    width = q_ref.shape[1]
    joint = bias_ref.shape[1]
    middle = w_low_ref.shape[0]
    inverse = lax.rsqrt(jnp.mean(x * x, axis=-1, keepdims=True) + EPSILON)
    normed = (x * inverse * gain_ref[...]).astype(BF16)
    ordered = dot_nn(normed, order_ref[...]).astype(BF16)
    normed_ref[...] = ordered
    joined = dot_nn(ordered[:, :middle], w_low_ref[:, :joint])
    joined = joined + dot_nn(ordered[:, middle:], w_high_ref[:, :joint]) + bias_ref[...]
    cosine, sine = cos_ref[...], sin_ref[...]
    for begin in range(0, width + LANES, LANES):
        block = joined[:, begin : begin + LANES]
        turned = block * cosine + swap_halves(block) * sine
        if begin < width:
            q_ref[:, begin : begin + LANES] = (turned * SCALE).astype(BF16)
        else:
            kv_ref[:, :LANES] = turned.astype(BF16)
    kv_ref[:, LANES:] = joined[:, width + LANES :].astype(BF16)


def rows_of(rows, cols):
    return pl.BlockSpec((rows, cols), lambda i: (i, 0))


def whole(value):
    return pl.BlockSpec(value.shape, lambda i: (0,) * value.ndim)


def prep(x, gain, order, weights, bias, cosine, sine, rows):
    count, dim = x.shape
    ordered = order.shape[1]
    joint = bias.shape[1]
    width = joint - 2 * LANES
    return pl.pallas_call(
        prep_kernel,
        grid=(count // rows,),
        in_specs=[
            rows_of(rows, dim),
            whole(gain),
            whole(order),
            whole(weights[0]),
            whole(weights[1]),
            whole(bias),
            rows_of(rows, LANES),
            rows_of(rows, LANES),
        ],
        out_specs=[rows_of(rows, ordered), rows_of(rows, width), rows_of(rows, 2 * LANES)],
        out_shape=[
            jax.ShapeDtypeStruct((count, ordered), BF16),
            jax.ShapeDtypeStruct((count, width), BF16),
            jax.ShapeDtypeStruct((count, 2 * LANES), BF16),
        ],
        compiler_params=pltpu.CompilerParams(vmem_limit_bytes=40 * MIB),
        cost_estimate=pl.CostEstimate(
            flops=2 * count * ordered * (joint + dim), bytes_accessed=12 * MIB, transcendentals=0
        ),
        name="norm_project_rotate",
    )(x, gain, order, weights[0], weights[1], bias, cosine, sine)


def back_in_order(value, order):
    high = value.astype(BF16)
    low = (value - high.astype(F32)).astype(BF16)
    return dot_nt(high, order) + dot_nt(low, order)


def out_kernel(attended_ref, x_ref, w_low_ref, w_high_ref, order_ref, gain_ref, resid_ref, normed_ref):
    width = attended_ref.shape[1]
    joint = w_low_ref.shape[1] - width
    attended = attended_ref[...]
    branch = jnp.concatenate(
        [dot_nt(attended, w_low_ref[:, joint:]), dot_nt(attended, w_high_ref[:, joint:])], axis=1
    )
    resid = x_ref[...].astype(F32) + back_in_order(branch, order_ref[...])
    inverse = lax.rsqrt(jnp.mean(resid * resid, axis=-1, keepdims=True) + EPSILON)
    resid_ref[...] = resid
    normed_ref[...] = (resid * inverse * gain_ref[...]).astype(BF16)


def project_out(attended, x, weights, order, gain, rows, seq):
    dim = x.shape[1]
    count = rows
    return pl.pallas_call(
        out_kernel,
        grid=(1,),
        in_specs=[
            rows_of(rows, attended.shape[1]),
            pl.BlockSpec((rows, dim), lambda i: (seq, 0)),
            whole(weights[0]),
            whole(weights[1]),
            whole(order),
            whole(gain),
        ],
        out_specs=[rows_of(rows, dim), rows_of(rows, dim)],
        out_shape=[jax.ShapeDtypeStruct((count, dim), F32), jax.ShapeDtypeStruct((count, dim), BF16)],
        compiler_params=pltpu.CompilerParams(vmem_limit_bytes=40 * MIB),
        cost_estimate=pl.CostEstimate(flops=6 * count * dim * dim, bytes_accessed=8 * MIB, transcendentals=0),
        name="project_out_norm",
    )(attended, x, weights[0], weights[1], order, gain)


def fold_rows(value):
    return jnp.sum(value.reshape(-1, 8, value.shape[1]), axis=0)


def norm_back(values, inverse, gain, incoming):
    scaled = incoming * gain
    mean_term = jnp.mean(scaled * values, axis=-1, keepdims=True)
    return inverse * scaled - values * inverse**3 * mean_term


def total_of(own_ref, *away_refs):
    total = own_ref[...]
    for ref in away_refs:
        total = total + ref[...].astype(F32)
    return total


def out_back_kernel(
    own_ref, core_ref, x_ref, far_ref, resid_ref, cot_ref, w_low_ref, w_high_ref, order_ref, gain_ref,
    d_resid_ref, d_branch_ref, d_attended_ref, gain_grad_ref,
):
    width = d_attended_ref.shape[1]
    joint = w_low_ref.shape[1] - width
    middle = w_low_ref.shape[0]
    d_normed = total_of(own_ref, core_ref, x_ref, far_ref)
    resid = resid_ref[...]
    inverse = lax.rsqrt(jnp.mean(resid * resid, axis=-1, keepdims=True) + EPSILON)
    d_resid = cot_ref[...].astype(F32) + norm_back(resid, inverse, gain_ref[...], d_normed)
    d_resid_ref[...] = d_resid
    d_branch = dot_nn(d_resid.astype(BF16), order_ref[...]).astype(BF16)
    d_branch_ref[...] = d_branch
    d_attended = dot_nn(d_branch[:, :middle], w_low_ref[:, joint:])
    d_attended = d_attended + dot_nn(d_branch[:, middle:], w_high_ref[:, joint:])
    d_attended_ref[...] = d_attended.astype(BF16)
    gain_grad_ref[...] = fold_rows(d_normed * resid * inverse)


def project_out_back(terms, resid, cot, weights, order, gain, rows, seq):
    count, dim = resid.shape
    ordered = order.shape[1]
    width = dim
    return pl.pallas_call(
        out_back_kernel,
        grid=(1,),
        in_specs=[
            rows_of(rows, dim),
            rows_of(rows, dim),
            rows_of(rows, dim),
            rows_of(rows, dim),
            rows_of(rows, dim),
            pl.BlockSpec((rows, dim), lambda i: (seq, 0)),
            whole(weights[0]),
            whole(weights[1]),
            whole(order),
            whole(gain),
        ],
        out_specs=[
            rows_of(rows, dim),
            rows_of(rows, ordered),
            rows_of(rows, width),
            pl.BlockSpec((8, dim), lambda i: (0, 0)),
        ],
        out_shape=[
            jax.ShapeDtypeStruct((count, dim), F32),
            jax.ShapeDtypeStruct((count, ordered), BF16),
            jax.ShapeDtypeStruct((count, width), BF16),
            jax.ShapeDtypeStruct((8, dim), F32),
        ],
        compiler_params=pltpu.CompilerParams(vmem_limit_bytes=40 * MIB),
        cost_estimate=pl.CostEstimate(flops=4 * count * dim * dim, bytes_accessed=12 * MIB, transcendentals=0),
        name="norm_back_project",
    )(*terms, resid, cot, weights[0], weights[1], order, gain)


def input_back_kernel(
    dq_ref, own_ref, core_ref, from_x_ref, far_ref, x_ref, d_resid_ref, w_low_ref, w_high_ref, order_ref,
    gain_ref, cos_ref, sin_ref, d_kv_ref, input_grad_ref, gain_grad_ref, bias_grad_ref,
):
    joint = dq_ref.shape[1] + d_kv_ref.shape[1]
    dkv = total_of(own_ref, core_ref, from_x_ref, far_ref)
    dk = dkv[:, :LANES]
    dk = dk * cos_ref[...] - swap_halves(dk) * sin_ref[...]
    d_kv = jnp.concatenate([dk.astype(BF16), dkv[:, LANES:].astype(BF16)], axis=1)
    d_kv_ref[...] = d_kv
    d_joined = jnp.concatenate([dq_ref[...], d_kv], axis=1)
    d_normed = jnp.concatenate(
        [dot_nt(d_joined, w_low_ref[:, :joint]), dot_nt(d_joined, w_high_ref[:, :joint])], axis=1
    )
    d_normed = back_in_order(d_normed, order_ref[...])
    x = x_ref[...].astype(F32)
    inverse = lax.rsqrt(jnp.mean(x * x, axis=-1, keepdims=True) + EPSILON)
    input_grad_ref[...] = (d_resid_ref[...] + norm_back(x, inverse, gain_ref[...], d_normed)).astype(BF16)
    gain_grad_ref[...] = fold_rows(d_normed * x * inverse)
    bias_grad_ref[...] = fold_rows(d_joined.astype(F32))


def input_back(dq, terms, x, d_resid, weights, order, gain, cosine, sine, rows, seq):
    count, dim = d_resid.shape
    width = dq.shape[1]
    joint = width + 2 * LANES
    return pl.pallas_call(
        input_back_kernel,
        grid=(1,),
        in_specs=[
            rows_of(rows, width),
            rows_of(rows, 2 * LANES),
            rows_of(rows, 2 * LANES),
            rows_of(rows, 2 * LANES),
            rows_of(rows, 2 * LANES),
            pl.BlockSpec((rows, dim), lambda i: (seq, 0)),
            rows_of(rows, dim),
            whole(weights[0]),
            whole(weights[1]),
            whole(order),
            whole(gain),
            pl.BlockSpec((rows, LANES), lambda i: (seq, 0)),
            pl.BlockSpec((rows, LANES), lambda i: (seq, 0)),
        ],
        out_specs=[
            rows_of(rows, 2 * LANES),
            rows_of(rows, dim),
            pl.BlockSpec((8, dim), lambda i: (0, 0)),
            pl.BlockSpec((8, joint), lambda i: (0, 0)),
        ],
        out_shape=[
            jax.ShapeDtypeStruct((count, 2 * LANES), BF16),
            jax.ShapeDtypeStruct((count, dim), BF16),
            jax.ShapeDtypeStruct((8, dim), F32),
            jax.ShapeDtypeStruct((8, joint), F32),
        ],
        compiler_params=pltpu.CompilerParams(vmem_limit_bytes=40 * MIB),
        cost_estimate=pl.CostEstimate(flops=6 * count * dim * joint, bytes_accessed=12 * MIB, transcendentals=0),
        name="input_gradient",
    )(dq, *terms, x, d_resid, weights[0], weights[1], order, gain, cosine, sine)


def seq_rows(seq, rows, cols):
    return pl.BlockSpec((rows, cols), lambda i: (seq, 0))


def piece_of(seq, rows):
    return pl.BlockSpec((1, rows, 2 * LANES), lambda i: (seq, 0, 0))


def keys_and_values(piece_refs):
    joint = jnp.concatenate([ref[0] for ref in piece_refs], axis=0)
    key, value = joint[:, :LANES], joint[:, LANES:]
    return (key, other_head(key)), (value, other_head(value))


def attend_kernel(block_ref, q_ref, kv_0, kv_1, kv_2, kv_3, start_ref, out_ref):
    rows, width = q_ref.shape
    length = 4 * rows
    heads = width // HD
    group = heads // 2
    keys, values = keys_and_values((kv_0, kv_1, kv_2, kv_3))
    upper_key = lane_of((length, LANES)) >= HD
    upper = lane_of((rows, LANES)) >= HD
    query_at = block_ref[0] * rows + lax.broadcasted_iota(jnp.int32, (rows, length), 0)
    key_at = jnp.concatenate(
        [
            (block_ref[0] ^ place) * rows + lax.broadcasted_iota(jnp.int32, (rows, rows), 1)
            for place in range(4)
        ],
        axis=1,
    )
    allowed = (key_at <= query_at) & (key_at >= start_ref[:, :1])
    bias = jnp.where(allowed, 0.0, MASKED)
    one = jnp.ones((), BF16)
    for pair in range(heads // 2):
        at = slice(pair * LANES, (pair + 1) * LANES)
        both = q_ref[:, at]
        parts = []
        for place in range(2):
            owner = (2 * pair + place) // group
            moved = int(owner != place)
            side = upper if place else ~upper
            side_key = upper_key if place else ~upper_key
            query = jnp.where(side, both, jnp.zeros_like(both))
            score = dot_nt(query, keys[moved]) + bias
            top = jnp.max(score, axis=1, keepdims=True)
            weight = jnp.exp(score - top).astype(BF16)
            mixed = dot_nn(weight, jnp.where(side_key, values[moved], one))
            parts.append(mixed / pltpu.roll(mixed, HD, 1))
        out_ref[:, at] = jnp.where(upper, parts[1], parts[0]).astype(BF16)


def attend(block, q, kv_pieces, start, rows, seq):
    width = q.shape[1]
    heads = width // HD
    return pl.pallas_call(
        attend_kernel,
        grid=(1,),
        in_specs=[
            pl.BlockSpec(memory_space=pltpu.SMEM),
            seq_rows(seq, rows, width),
            *[piece_of(seq, rows)] * 4,
            seq_rows(seq, rows, LANES),
        ],
        out_specs=seq_rows(0, rows, width),
        out_shape=jax.ShapeDtypeStruct((rows, width), BF16),
        compiler_params=pltpu.CompilerParams(vmem_limit_bytes=48 * MIB),
        cost_estimate=pl.CostEstimate(
            flops=32 * rows * rows * LANES * heads,
            bytes_accessed=4 * rows * width,
            transcendentals=4 * rows * rows * heads,
        ),
        name="attention_forward",
    )(block, q, *kv_pieces, start)


def attend_back_kernel(
    block_ref, q_ref, kv_0, kv_1, kv_2, kv_3, back_ref, start_ref, cos_ref, sin_ref,
    dq_ref, own_ref, core_ref, x_ref, far_ref, dk_sum, dv_sum,
):
    rows, width = q_ref.shape
    length = 4 * rows
    heads = width // HD
    group = heads // 2
    keys, values = keys_and_values((kv_0, kv_1, kv_2, kv_3))
    key_t = keys[0].astype(F32).T.astype(BF16)
    keys_t = (key_t, jnp.concatenate([key_t[HD:], key_t[:HD]], axis=0))
    upper = lane_of((rows, LANES)) >= HD
    upper_t = lax.broadcasted_iota(jnp.int32, (LANES, rows), 0) >= HD
    query_at = block_ref[0] * rows + lax.broadcasted_iota(jnp.int32, (length, rows), 1)
    key_at = jnp.concatenate(
        [
            (block_ref[0] ^ place) * rows + lax.broadcasted_iota(jnp.int32, (rows, rows), 0)
            for place in range(4)
        ],
        axis=0,
    )
    allowed = (key_at <= query_at) & (key_at >= start_ref[0, :1, :])
    bias = jnp.where(allowed, 0.0, MASKED)
    cosine, sine = cos_ref[...], sin_ref[...]
    dk_sum[...] = jnp.zeros_like(dk_sum)
    dv_sum[...] = jnp.zeros_like(dv_sum)
    for pair in range(heads // 2):
        at = slice(pair * LANES, (pair + 1) * LANES)
        both = q_ref[:, at]
        back_both = back_ref[:, at]
        parts = []
        for place in range(2):
            owner = (2 * pair + place) // group
            moved = int(owner != place)
            side = upper if place else ~upper
            query = jnp.where(side, both, jnp.zeros_like(both))
            back = jnp.where(side, back_both, jnp.zeros_like(back_both))
            score = dot_nt(keys[moved], query) + bias
            weight = jnp.exp(score - jnp.max(score, axis=0, keepdims=True))
            prob = weight * (1.0 / jnp.sum(weight, axis=0, keepdims=True))
            dv_sum[owner] += dot_nn(prob.astype(BF16), back)
            d_prob = dot_nt(values[moved], back)
            level = jnp.sum(prob * d_prob, axis=0, keepdims=True)
            d_score = (prob * (d_prob - level)).astype(BF16)
            dk_sum[owner] += dot_nn(d_score, query)
            parts.append(dot_nn(keys_t[moved], d_score))
        d_query = jnp.where(upper_t, parts[1], parts[0]).T * SCALE
        dq_ref[:, at] = (d_query * cosine - swap_halves(d_query) * sine).astype(BF16)
    lower_key = lane_of((length, LANES)) < HD
    for total, begin in ((dk_sum, 0), (dv_sum, LANES)):
        first, second = total[0], total[1]
        first = first + pltpu.roll(first, HD, 1)
        second = second + pltpu.roll(second, HD, 1)
        both = jnp.where(lower_key, first, second)
        cols = slice(begin, begin + LANES)
        own_ref[:, cols] = both[:rows]
        for place, ref in enumerate((core_ref, x_ref, far_ref)):
            ref[:, cols] = both[(place + 1) * rows : (place + 2) * rows].astype(BF16)


def direct_parts_of(rows, cols):
    shapes = [jax.ShapeDtypeStruct((rows, cols), F32)] + [jax.ShapeDtypeStruct((rows, cols), BF16)] * 3
    return [seq_rows(0, rows, cols)] * 4, shapes


def parts_of(rows, cols):
    specs = [seq_rows(0, rows, cols), seq_rows(0, 2 * rows, cols), seq_rows(0, rows, cols)]
    shapes = [
        jax.ShapeDtypeStruct((rows, cols), F32),
        jax.ShapeDtypeStruct((2 * rows, cols), BF16),
        jax.ShapeDtypeStruct((rows, cols), F32),
    ]
    return specs, shapes


def attend_back(block, q, kv_pieces, back, start, cosine, sine, rows, seq):
    width = q.shape[1]
    length = 4 * rows
    heads = width // HD
    specs, shapes = direct_parts_of(rows, 2 * LANES)
    return pl.pallas_call(
        attend_back_kernel,
        grid=(1,),
        in_specs=[
            pl.BlockSpec(memory_space=pltpu.SMEM),
            seq_rows(seq, rows, width),
            *[piece_of(seq, rows)] * 4,
            seq_rows(0, rows, width),
            pl.BlockSpec((1, 8, rows), lambda i: (seq, 0, 0)),
            seq_rows(seq, rows, LANES),
            seq_rows(seq, rows, LANES),
        ],
        out_specs=[seq_rows(0, rows, width), *specs],
        out_shape=[jax.ShapeDtypeStruct((rows, width), BF16), *shapes],
        scratch_shapes=[
            pltpu.VMEM((2, length, LANES), F32),
            pltpu.VMEM((2, length, LANES), F32),
        ],
        compiler_params=pltpu.CompilerParams(vmem_limit_bytes=48 * MIB),
        cost_estimate=pl.CostEstimate(
            flops=80 * rows * rows * LANES * heads,
            bytes_accessed=8 * rows * width,
            transcendentals=4 * rows * rows * heads,
        ),
        name="attention_backward",
    )(block, q, *kv_pieces, back, start, cosine, sine)


def mlp_kernel(
    n_0, n_1, n_2, n_3, c_0, c_1, c_2, c_3, w_ref,
    own_ref, core_ref, x_ref, d_own_ref, d_core_ref, d_x_ref, d_far_ref, kept_ref, turned_ref,
    normed_all, cot_all,
):
    step = pl.program_id(0)
    rows = own_ref.shape[0]
    columns = w_ref.shape[1] // 3

    @pl.when(step == 0)
    def _():
        for place, (n_ref, c_ref) in enumerate(zip((n_0, n_1, n_2, n_3), (c_0, c_1, c_2, c_3))):
            normed_all[place // 2, (place % 2) * rows : (place % 2 + 1) * rows] = n_ref[...]
            cot_all[place // 2, (place % 2) * rows : (place % 2 + 1) * rows] = c_ref[...]

    normed, cot = normed_all[step], cot_all[step]
    for begin in range(0, columns, TILE):
        at = slice(begin, begin + TILE)
        gate = dot_nn(normed, w_ref[:, begin : begin + TILE])
        up = dot_nn(normed, w_ref[:, columns + begin : columns + begin + TILE])
        d_act = dot_nn(cot, w_ref[:, 2 * columns + begin : 2 * columns + begin + TILE])
        sigmoid = 0.5 * jnp.tanh(0.5 * gate) + 0.5
        swish = gate * sigmoid
        kept_ref[0, :, at] = (d_act * up * (sigmoid + swish * (1.0 - sigmoid))).astype(BF16)
        kept_ref[1, :, at] = (d_act * swish).astype(BF16)
        kept_ref[2, :, at] = (swish * up).astype(BF16)
    turned_ref[0] = normed.T
    turned_ref[1] = cot.T
    out = dot_nt(kept_ref[2], w_ref[:, 2 * columns :])
    d_normed = dot_nt(kept_ref[0], w_ref[:, :columns]) + dot_nt(kept_ref[1], w_ref[:, columns : 2 * columns])

    @pl.when(step == 0)
    def _():
        own_ref[...] = out[:rows]
        core_ref[:rows] = out[rows:].astype(BF16)
        d_own_ref[...] = d_normed[:rows]
        d_core_ref[...] = d_normed[rows:].astype(BF16)

    @pl.when(step == 1)
    def _():
        x_ref[...] = out[:rows]
        core_ref[rows:] = out[rows:].astype(BF16)
        d_x_ref[...] = d_normed[:rows].astype(BF16)
        d_far_ref[...] = d_normed[rows:].astype(BF16)


def mlp(normed, cot, weights, seq):
    rows, dim = normed[0].shape
    columns = weights.shape[1] // 3
    specs, shapes = parts_of(rows, dim)
    d_specs, d_shapes = direct_parts_of(rows, dim)
    once = lambda at: pl.BlockSpec((rows, dim), lambda i: (at, 0), pipeline_mode=pl.Buffered(1))
    return pl.pallas_call(
        mlp_kernel,
        grid=(2,),
        in_specs=[
            *[once(0)] * 4,
            *[once(seq)] * 4,
            pl.BlockSpec(weights.shape, lambda i: (0, 0), pipeline_mode=pl.Buffered(1)),
        ],
        out_specs=[
            *specs,
            *d_specs,
            pl.BlockSpec((3, 2 * rows, columns), lambda i: (0, i, 0)),
            pl.BlockSpec((2, dim, 2 * rows), lambda i: (0, 0, i)),
        ],
        out_shape=[
            *shapes,
            *d_shapes,
            jax.ShapeDtypeStruct((3, 4 * rows, columns), BF16),
            jax.ShapeDtypeStruct((2, dim, 4 * rows), BF16),
        ],
        scratch_shapes=[
            pltpu.VMEM((2, 2 * rows, dim), BF16),
            pltpu.VMEM((2, 2 * rows, dim), BF16),
        ],
        compiler_params=pltpu.CompilerParams(vmem_limit_bytes=58 * MIB),
        cost_estimate=pl.CostEstimate(
            flops=48 * rows * dim * columns,
            bytes_accessed=6 * dim * columns + 24 * rows * columns,
            transcendentals=4 * rows * columns,
        ),
        name="feed_forward",
    )(*normed, *cot, weights)


def mlp_grad_kernel(turned_0, turned_1, kept_0, kept_1, grad_ref):
    grad_ref[...] = (dot_nn(turned_0[0], kept_0[0]) + dot_nn(turned_1[0], kept_1[0])).astype(BF16)


def mlp_grad(turned, kept):
    _, dim, count = turned[0].shape
    columns = kept[0].shape[2]
    turned_block = pl.BlockSpec((1, dim, count), lambda i: (i // 2, 0, 0))
    kept_block = pl.BlockSpec((1, count, columns), lambda i: (i, 0, 0))
    return pl.pallas_call(
        mlp_grad_kernel,
        grid=(3,),
        in_specs=[turned_block, turned_block, kept_block, kept_block],
        out_specs=pl.BlockSpec((dim, columns), lambda i: (0, i)),
        out_shape=jax.ShapeDtypeStruct((dim, 3 * columns), BF16),
        compiler_params=pltpu.CompilerParams(vmem_limit_bytes=58 * MIB),
        cost_estimate=pl.CostEstimate(
            flops=12 * count * dim * columns,
            bytes_accessed=6 * dim * columns + 12 * count * columns,
            transcendentals=0,
        ),
        name="feed_forward_gradients",
    )(*turned, *kept)


def pack_kernel(block_ref, gate_ref, up_ref, down_ref, *refs):
    out_refs, scratch = refs[:4], refs[4]
    shard, ff = gate_ref.shape
    quarter = scratch.shape[2] // 4
    for place, ref in enumerate((gate_ref, up_ref, down_ref)):
        scratch[place, :, :ff] = ref[...].astype(F32)
        scratch[place, :, ff:] = jnp.zeros((shard, 4 * quarter - ff), F32)
    for place, out_ref in enumerate(out_refs):
        begin = pl.multiple_of((block_ref[0] ^ place) * quarter, LANES)
        for part in range(3):
            out_ref[:, part * quarter : (part + 1) * quarter] = scratch[part, :, pl.ds(begin, quarter)].astype(BF16)


def pack(block, gate, up, down_t, quarter):
    shard = gate.shape[0]
    return pl.pallas_call(
        pack_kernel,
        in_specs=[pl.BlockSpec(memory_space=pltpu.SMEM)] + [pl.BlockSpec(memory_space=pltpu.VMEM)] * 3,
        out_specs=[pl.BlockSpec(memory_space=pltpu.VMEM)] * 4,
        out_shape=[jax.ShapeDtypeStruct((shard, 3 * quarter), BF16)] * 4,
        scratch_shapes=[pltpu.VMEM((3, shard, 4 * quarter), F32)],
        name="pack_columns",
    )(block, gate, up, down_t)


def pick(options, index):
    value = options[0]
    for place in range(1, len(options)):
        value = jnp.where(index == place, options[place], value)
    return value


def assemble_kernel(block_ref, *refs):
    pieces, out_ref, scratch = refs[:4], refs[4], refs[5]
    shard = pieces[0].shape[0]
    values = [ref[...].astype(F32) for ref in pieces]
    for owner in range(4):
        scratch[owner * shard : (owner + 1) * shard] = pick(values, block_ref[0] ^ owner)
    out_ref[...] = scratch[...].astype(BF16)


def assemble(block, pieces):
    shard, columns = pieces[0].shape
    return pl.pallas_call(
        assemble_kernel,
        in_specs=[pl.BlockSpec(memory_space=pltpu.SMEM)] + [pl.BlockSpec(memory_space=pltpu.VMEM)] * 4,
        out_specs=pl.BlockSpec(memory_space=pltpu.VMEM),
        out_shape=jax.ShapeDtypeStruct((4 * shard, columns), BF16),
        scratch_shapes=[pltpu.VMEM((4 * shard, columns), F32)],
        name="assemble_rows",
    )(block, *pieces)


def cut_kernel(block_ref, value_ref, *refs):
    out_refs, scratch = refs[:4], refs[4]
    shard = out_refs[0].shape[0]
    scratch[...] = value_ref[...].astype(F32)
    values = [scratch[owner * shard : (owner + 1) * shard] for owner in range(4)]
    for place, out_ref in enumerate(out_refs):
        out_ref[...] = pick(values, block_ref[0] ^ place).astype(BF16)


def cut(block, value):
    shard, columns = value.shape[0] // 4, value.shape[1]
    return pl.pallas_call(
        cut_kernel,
        in_specs=[pl.BlockSpec(memory_space=pltpu.SMEM), pl.BlockSpec(memory_space=pltpu.VMEM)],
        out_specs=[pl.BlockSpec(memory_space=pltpu.VMEM)] * 4,
        out_shape=[jax.ShapeDtypeStruct((shard, columns), BF16)] * 4,
        scratch_shapes=[pltpu.VMEM(value.shape, F32)],
        name="cut_rows",
    )(block, value)


def unpack_kernel(block_ref, *refs):
    pieces, out_refs, scratch = refs[:4], refs[4:7], refs[7]
    ff = out_refs[0].shape[1]
    quarter = scratch.shape[2] // 4
    for place, ref in enumerate(pieces):
        begin = pl.multiple_of((block_ref[0] ^ place) * quarter, LANES)
        for part in range(3):
            scratch[part, :, pl.ds(begin, quarter)] = ref[:, part * quarter : (part + 1) * quarter].astype(F32)
    for part, out_ref in enumerate(out_refs):
        out_ref[...] = scratch[part, :, :ff]


def unpack(block, pieces, ff):
    shard, columns = pieces[0].shape
    return pl.pallas_call(
        unpack_kernel,
        in_specs=[pl.BlockSpec(memory_space=pltpu.SMEM)] + [pl.BlockSpec(memory_space=pltpu.VMEM)] * 4,
        out_specs=[pl.BlockSpec(memory_space=pltpu.VMEM)] * 3,
        out_shape=[jax.ShapeDtypeStruct((shard, ff), F32)] * 3,
        scratch_shapes=[pltpu.VMEM((3, shard, columns // 3 * 4), F32)],
        name="unpack_columns",
    )(block, *pieces)


def bit_swap(value, axis, bit=0):
    size = lax.axis_size(axis)
    return lax.ppermute(value, axis, [(i, i ^ (1 << bit)) for i in range(size)])


def ctx_swap(value, jump):
    return lax.ppermute(value, CTX, [(i, i ^ jump) for i in range(4)])


def after(first, *values):
    return lax.optimization_barrier((first, *values))


def gather_four(value):
    from_x = bit_swap(value, "cx")
    return [value, bit_swap(value, "cc"), from_x, bit_swap(from_x, "cc")]


def gather_direct(value):
    return [value] + [ctx_swap(value, jump) for jump in range(1, 4)]


def sum_direct(own, *away):
    return [own] + [ctx_swap(value, jump + 1) for jump, value in enumerate(away)]


class Doubling:
    def __init__(self, fsdp):
        bits = fsdp.bit_length() - 1
        self.steps = [("fsdp", bit) for bit in reversed(range(bits))] + [("cx", 0), ("cc", 0)]
        weight = {"cc": 1, "cx": 2}
        self.offsets = [0]
        for axis, bit in self.steps:
            jump = weight[axis] if axis in weight else 4 << bit
            self.offsets += [offset ^ jump for offset in self.offsets]

    def gather(self, value, steps):
        for axis, bit in steps:
            value = jnp.concatenate([value, bit_swap(value, axis, bit)], axis=0)
        return value


def halve(value, axis, bit=0):
    middle = value.shape[0] // 2
    came = bit_swap(value[middle:], axis, bit)
    return (value[:middle].astype(F32) + came.astype(F32)).astype(BF16)


def on_device(
    doubling,
    hidden,
    segments,
    attn_gain,
    qkv_weight,
    qkv_bias,
    out_weight,
    mlp_gain,
    gate_weight,
    up_weight,
    down_weight,
    cotangent,
):
    seqs, rows, dim = hidden.shape
    count = seqs * rows
    shard = attn_gain.shape[0]
    world = dim // shard
    joint = qkv_weight.shape[1]
    width = joint - 2 * LANES
    ff = gate_weight.shape[1]
    block = lax.axis_index("cx") * lax.axis_size("cc") + lax.axis_index("cc")
    me = lax.axis_index("fsdp") * lax.axis_size(CTX) + block
    offset = block * rows
    block_arg = block.reshape(1).astype(jnp.int32)
    x = hidden.reshape(count, dim)
    cot = cotangent.reshape(count, dim)

    padded = -(-(shard + 1) // 16) * 16
    small = jnp.concatenate([attn_gain, mlp_gain, qkv_bias])
    small_row = jnp.pad(small, (0, joint + width - small.shape[0]))[None]
    first_shard = jnp.concatenate(
        [
            jnp.concatenate([qkv_weight, out_weight.T], axis=1),
            small_row,
            jnp.zeros((padded - shard - 1, joint + width), BF16),
        ],
        axis=0,
    )
    far = len(doubling.steps) - 3
    first = doubling.gather(first_shard, doubling.steps[:far])

    quarter = -(-ff // (4 * TILE)) * TILE
    pieces = pack(block_arg, gate_weight, up_weight, down_weight.T, quarter)
    pieces = [pieces[0]] + [ctx_swap(pieces[jump], jump) for jump in range(1, 4)]
    mlp_shard = assemble(block_arg, pieces)
    first, mlp_shard = after(first, mlp_shard)
    mlp_weights = lax.all_gather(mlp_shard, "fsdp", axis=0, tiled=True)

    cot_x = bit_swap(after(first, cot)[1], "cx")
    first = doubling.gather(first, doubling.steps[far : far + 1])
    first, cot_x = after(first, cot_x)
    first = doubling.gather(first, doubling.steps[far + 1 : -1])
    weights = (first, bit_swap(first, *doubling.steps[-1]))
    cot_all = [cot, bit_swap(cot, "cc"), cot_x, bit_swap(cot_x, "cc")]

    owner = me ^ jnp.array(doubling.offsets, jnp.int32)
    within = jnp.arange(padded, dtype=jnp.int32)
    target = jnp.where(within[None, :] < shard, owner[:, None] * shard + within[None, :], -1).reshape(1, -1)
    order = (jnp.arange(dim, dtype=jnp.int32)[:, None] == target).astype(BF16)
    by_owner = (owner[None, :] == jnp.arange(world, dtype=jnp.int32)[:, None]).astype(BF16)
    extras = jnp.concatenate(
        [part.reshape(world // 2, padded, -1)[:, shard, : small.shape[0]] for part in weights], axis=0
    )
    extras = dot_nn(by_owner, extras)
    gain_attn = extras[:, :shard].reshape(1, dim)
    gain_mlp = extras[:, shard : 2 * shard].reshape(1, dim)
    bias = extras[:, 2 * shard :].reshape(1, joint)

    at_row = lax.dynamic_slice_in_dim(segments, offset, rows, axis=1)
    zeros_before = jnp.sum((segments < 1).astype(jnp.int32), axis=1, keepdims=True)
    ones_before = jnp.sum((segments < 2).astype(jnp.int32), axis=1, keepdims=True)
    start = jnp.where(at_row == 0, 0, jnp.where(at_row == 1, zeros_before, ones_before))
    position = (offset + jnp.arange(rows, dtype=jnp.int32)[None, :] - start).reshape(count)
    lane = jnp.arange(LANES, dtype=jnp.int32)
    frequency = ROPE_BASE ** (-(lane % (HD // 2)).astype(F32) * 2.0 / HD)
    angle = position.astype(F32)[:, None] * frequency[None, :]
    cosine = jnp.cos(angle)
    sine = jnp.where(lane % HD < HD // 2, -1.0, 1.0)[None, :] * jnp.sin(angle)
    start_column = jnp.broadcast_to(start.reshape(count, 1), (count, LANES))
    start_row = jnp.broadcast_to(start[:, None, :], (seqs, 8, rows))

    normed, q, kv = prep(x, gain_attn, order, weights, bias, cosine, sine, rows)
    kv_all = gather_four(kv.reshape(seqs, rows, 2 * LANES))
    attended, resid, normed_all = [], [], []
    for seq in range(seqs):
        attended.append(attend(block_arg, q, kv_all, start_column, rows, seq))
        resid_one, normed_one = project_out(attended[seq], x, weights, order, gain_mlp, rows, seq)
        resid.append(resid_one)
        normed_all.append(gather_direct(normed_one))

    out_parts, d_terms, kept, turned = [], [], [], []
    for seq in range(seqs):
        result = mlp(normed_all[seq], cot_all, mlp_weights, seq)
        out_parts.append(result[:3])
        d_terms.append(sum_direct(*result[3:7]))
        kept.append(result[7])
        turned.append(result[8])
    grads = mlp_grad(turned, kept)
    grads, d_terms[0], d_terms[1] = after(grads, *d_terms)
    grads = lax.psum_scatter(
        grads.reshape(world // 4, 4 * shard, 3 * quarter), "fsdp", scatter_dimension=0, tiled=False
    )

    d_resid, d_branch, d_attended, mlp_gain_grad = [], [], [], []
    for seq in range(seqs):
        result = project_out_back(d_terms[seq], resid[seq], cot, weights, order, gain_mlp, rows, seq)
        for place, value in zip((d_resid, d_branch, d_attended, mlp_gain_grad), result):
            place.append(value)
    out_grad = dot_tn(jnp.concatenate(d_branch, axis=0), jnp.concatenate(attended, axis=0)).astype(BF16)
    out_grad = halve(out_grad, "cc")
    out_core = [bit_swap(part[1], "cc") for part in out_parts]
    out_x = jnp.concatenate(
        [(part[2] + core[rows:].astype(F32)).astype(BF16) for part, core in zip(out_parts, out_core)], axis=0
    )
    out_x = bit_swap(after(d_attended[0], out_x)[1], "cx")
    dq, dkv_terms = [], []
    for seq in range(seqs):
        if seq == 1:
            d_attended[1], out_grad, out_x = after(d_attended[1], out_grad, out_x)
            out_grad = halve(out_grad, "cx")
        result = attend_back(block_arg, q, kv_all, d_attended[seq], start_row, cosine, sine, rows, seq)
        dq.append(result[0])
        dkv_terms.append(sum_direct(*result[1:]))
    dq[1], out_grad = after(dq[1], out_grad)
    q_grad = dot_tn(normed, jnp.concatenate(dq, axis=0)).astype(BF16)
    q_grad = halve(halve(q_grad, "cc"), "cx")
    d_kv, input_grad, attn_gain_grad, bias_grad = [], [], [], []
    for seq in range(seqs):
        result = input_back(
            dq[seq], dkv_terms[seq], x, d_resid[seq], weights, order, gain_attn, cosine, sine, rows, seq
        )
        for place, value in zip((d_kv, input_grad, attn_gain_grad, bias_grad), result):
            place.append(value)

    output = []
    for seq in range(seqs):
        came = out_core[seq][:rows].astype(F32) + out_x[seq * rows : (seq + 1) * rows].astype(F32)
        output.append((resid[seq] + out_parts[seq][0] + came).astype(BF16))

    split_at = width + LANES
    bias_grad = jnp.sum(sum(bias_grad), axis=0)
    small_grads = jnp.concatenate(
        [
            jnp.sum(sum(attn_gain_grad), axis=0).reshape(world, -1),
            jnp.sum(sum(mlp_gain_grad), axis=0).reshape(world, -1),
            bias_grad[:split_at].reshape(world, -1),
            bias_grad[split_at:].reshape(world, -1),
        ],
        axis=1,
    ).astype(BF16)
    small_count = small_grads.shape[1]
    small_grads = jnp.pad(small_grads, ((0, 0), (0, 2 * LANES - small_count)))
    place = jnp.where(within[None, :] == shard, owner[:, None], -1).reshape(1, -1)
    spread = (jnp.arange(world, dtype=jnp.int32)[:, None] == place).astype(BF16)
    kv_grad = dot_tn(
        jnp.concatenate([normed, spread], axis=0), jnp.concatenate([*d_kv, small_grads], axis=0)
    ).astype(BF16)
    kv_grad = halve(halve(kv_grad, "cc"), "cx")
    first_sum = jnp.concatenate([q_grad, kv_grad, out_grad], axis=1)
    for axis, bit in reversed(doubling.steps[:-2]):
        first_sum = halve(first_sum, axis, bit)
    first_sum = first_sum.astype(F32)
    qkv_sum, out_sum = first_sum[:, :joint], first_sum[:, joint:]
    small_sum = qkv_sum[shard, width : width + small_count]
    at = (shard, 2 * shard, 2 * shard + split_at // world)

    pieces = cut(block_arg, lax.optimization_barrier(grads))
    pieces = [pieces[0]] + [ctx_swap(pieces[jump], jump) for jump in range(1, 4)]
    gate_grad, up_grad, down_grad_t = unpack(block_arg, pieces, ff)
    return (
        jnp.stack(output),
        jnp.stack(input_grad),
        small_sum[: at[0]],
        qkv_sum[:shard],
        small_sum[at[1] : at[2]],
        small_sum[at[2] :],
        out_sum[:shard].T,
        small_sum[at[0] : at[1]],
        gate_grad,
        up_grad,
        down_grad_t.T,
    )


def solution(mesh):
    fsdp, ctx = mesh.shape["fsdp"], mesh.shape["ctx"]
    inner = Mesh(mesh.devices.reshape(fsdp, 2, ctx // 2), AXES)
    tokens = P("fsdp", CTX, None)
    vector = P(AXES)
    by_row = P(AXES, None)
    by_column = P(None, AXES)
    return jax.shard_map(
        functools.partial(on_device, Doubling(fsdp)),
        mesh=inner,
        in_specs=(
            tokens,
            P("fsdp", None),
            vector,
            by_row,
            vector,
            by_column,
            vector,
            by_row,
            by_row,
            by_column,
            tokens,
        ),
        out_specs=(
            tokens,
            tokens,
            vector,
            by_row,
            vector,
            vector,
            by_column,
            vector,
            by_row,
            by_row,
            by_column,
        ),
        check_vma=False,
    )
```

```python
import functools

import jax
import jax.numpy as jnp
from jax import lax
from jax.experimental import pallas as pl
from jax.experimental.pallas import tpu as pltpu
from jax.sharding import Mesh
from jax.sharding import PartitionSpec as P

HD = 64
LANES = 128
EPSILON = 1e-06
ROPE_BASE = 1000000.0
MASKED = -1e30
SCALE = HD ** (-0.5)
TILE = 256
MIB = 1 << 20
F32 = jnp.float32
BF16 = jnp.bfloat16
AXES = ("fz", "fy", "cx", "cc")
FSDP = ("fz", "fy")
CTX = ("cx", "cc")
TOKENS = ("fy", "cx")
WEIGHTS = ("fz", "cc")


def dot_nn(a, b):
    return lax.dot_general(a, b, (((1,), (0,)), ((), ())), preferred_element_type=F32)


def dot_nt(a, b):
    return lax.dot_general(a, b, (((1,), (1,)), ((), ())), preferred_element_type=F32)


def dot_tn(a, b):
    return lax.dot_general(a, b, (((0,), (0,)), ((), ())), preferred_element_type=F32)


def lane_of(shape):
    return lax.broadcasted_iota(jnp.int32, shape, len(shape) - 1)


def swap_halves(block):
    lead = lane_of(block.shape) % HD < HD // 2
    return jnp.where(
        lead, pltpu.roll(block, LANES - HD // 2, 1), pltpu.roll(block, HD // 2, 1)
    )


def other_head(block):
    return jnp.concatenate([block[:, HD:], block[:, :HD]], axis=1)


def prep_kernel(
    x_ref, gain_ref, order_ref, w_low_ref, w_high_ref, bias_ref, cos_ref, sin_ref, normed_ref, q_ref, kv_ref
):
    x = x_ref[...].astype(F32)
    width = q_ref.shape[1]
    joint = bias_ref.shape[1]
    middle = w_low_ref.shape[0]
    inverse = lax.rsqrt(jnp.mean(x * x, axis=-1, keepdims=True) + EPSILON)
    normed = (x * inverse * gain_ref[...]).astype(BF16)
    ordered = dot_nn(normed, order_ref[...]).astype(BF16)
    normed_ref[...] = ordered
    joined = dot_nn(ordered[:, :middle], w_low_ref[:, :joint])
    joined = joined + dot_nn(ordered[:, middle:], w_high_ref[:, :joint]) + bias_ref[...]
    cosine, sine = cos_ref[...], sin_ref[...]
    for begin in range(0, width + LANES, LANES):
        block = joined[:, begin : begin + LANES]
        turned = block * cosine + swap_halves(block) * sine
        if begin < width:
            q_ref[:, begin : begin + LANES] = (turned * SCALE).astype(BF16)
        else:
            kv_ref[:, :LANES] = turned.astype(BF16)
    kv_ref[:, LANES:] = joined[:, width + LANES :].astype(BF16)


def rows_of(rows, cols):
    return pl.BlockSpec((rows, cols), lambda i: (i, 0))


def whole(value):
    return pl.BlockSpec(value.shape, lambda i: (0,) * value.ndim)


def prep(x, gain, order, weights, bias, cosine, sine, rows):
    count, dim = x.shape
    ordered = order.shape[1]
    joint = bias.shape[1]
    width = joint - 2 * LANES
    return pl.pallas_call(
        prep_kernel,
        grid=(count // rows,),
        in_specs=[
            rows_of(rows, dim),
            whole(gain),
            whole(order),
            whole(weights[0]),
            whole(weights[1]),
            whole(bias),
            rows_of(rows, LANES),
            rows_of(rows, LANES),
        ],
        out_specs=[rows_of(rows, ordered), rows_of(rows, width), rows_of(rows, 2 * LANES)],
        out_shape=[
            jax.ShapeDtypeStruct((count, ordered), BF16),
            jax.ShapeDtypeStruct((count, width), BF16),
            jax.ShapeDtypeStruct((count, 2 * LANES), BF16),
        ],
        compiler_params=pltpu.CompilerParams(vmem_limit_bytes=40 * MIB),
        cost_estimate=pl.CostEstimate(
            flops=2 * count * ordered * (joint + dim), bytes_accessed=12 * MIB, transcendentals=0
        ),
        name="norm_project_rotate",
    )(x, gain, order, weights[0], weights[1], bias, cosine, sine)


def back_in_order(value, order):
    high = value.astype(BF16)
    low = (value - high.astype(F32)).astype(BF16)
    return dot_nt(high, order) + dot_nt(low, order)


def out_kernel(attended_ref, x_ref, w_low_ref, w_high_ref, order_ref, gain_ref, resid_ref, normed_ref):
    width = attended_ref.shape[1]
    joint = w_low_ref.shape[1] - width
    attended = attended_ref[...]
    branch = jnp.concatenate(
        [dot_nt(attended, w_low_ref[:, joint:]), dot_nt(attended, w_high_ref[:, joint:])], axis=1
    )
    resid = x_ref[...].astype(F32) + back_in_order(branch, order_ref[...])
    inverse = lax.rsqrt(jnp.mean(resid * resid, axis=-1, keepdims=True) + EPSILON)
    resid_ref[...] = resid
    normed_ref[...] = (resid * inverse * gain_ref[...]).astype(BF16)


def project_out(attended, x, weights, order, gain, rows, seq):
    dim = x.shape[1]
    count = rows
    return pl.pallas_call(
        out_kernel,
        grid=(1,),
        in_specs=[
            rows_of(rows, attended.shape[1]),
            pl.BlockSpec((rows, dim), lambda i: (seq, 0)),
            whole(weights[0]),
            whole(weights[1]),
            whole(order),
            whole(gain),
        ],
        out_specs=[rows_of(rows, dim), rows_of(rows, dim)],
        out_shape=[jax.ShapeDtypeStruct((count, dim), F32), jax.ShapeDtypeStruct((count, dim), BF16)],
        compiler_params=pltpu.CompilerParams(vmem_limit_bytes=40 * MIB),
        cost_estimate=pl.CostEstimate(flops=6 * count * dim * dim, bytes_accessed=8 * MIB, transcendentals=0),
        name="project_out_norm",
    )(attended, x, weights[0], weights[1], order, gain)


def fold_rows(value):
    return jnp.sum(value.reshape(-1, 8, value.shape[1]), axis=0)


def norm_back(values, inverse, gain, incoming):
    scaled = incoming * gain
    mean_term = jnp.mean(scaled * values, axis=-1, keepdims=True)
    return inverse * scaled - values * inverse**3 * mean_term


def total_of(own_ref, *away_refs):
    total = own_ref[...]
    for ref in away_refs:
        total = total + ref[...].astype(F32)
    return total


def out_back_kernel(
    own_ref, core_ref, x_ref, far_ref, resid_ref, cot_ref, w_low_ref, w_high_ref, order_ref, gain_ref,
    d_resid_ref, d_branch_ref, d_attended_ref, gain_grad_ref,
):
    width = d_attended_ref.shape[1]
    joint = w_low_ref.shape[1] - width
    middle = w_low_ref.shape[0]
    d_normed = total_of(own_ref, core_ref, x_ref, far_ref)
    resid = resid_ref[...]
    inverse = lax.rsqrt(jnp.mean(resid * resid, axis=-1, keepdims=True) + EPSILON)
    d_resid = cot_ref[...].astype(F32) + norm_back(resid, inverse, gain_ref[...], d_normed)
    d_resid_ref[...] = d_resid
    d_branch = dot_nn(d_resid.astype(BF16), order_ref[...]).astype(BF16)
    d_branch_ref[...] = d_branch
    d_attended = dot_nn(d_branch[:, :middle], w_low_ref[:, joint:])
    d_attended = d_attended + dot_nn(d_branch[:, middle:], w_high_ref[:, joint:])
    d_attended_ref[...] = d_attended.astype(BF16)
    gain_grad_ref[...] = fold_rows(d_normed * resid * inverse)


def project_out_back(terms, resid, cot, weights, order, gain, rows, seq):
    count, dim = resid.shape
    ordered = order.shape[1]
    width = dim
    return pl.pallas_call(
        out_back_kernel,
        grid=(1,),
        in_specs=[
            rows_of(rows, dim),
            rows_of(rows, dim),
            rows_of(rows, dim),
            rows_of(rows, dim),
            rows_of(rows, dim),
            pl.BlockSpec((rows, dim), lambda i: (seq, 0)),
            whole(weights[0]),
            whole(weights[1]),
            whole(order),
            whole(gain),
        ],
        out_specs=[
            rows_of(rows, dim),
            rows_of(rows, ordered),
            rows_of(rows, width),
            pl.BlockSpec((8, dim), lambda i: (0, 0)),
        ],
        out_shape=[
            jax.ShapeDtypeStruct((count, dim), F32),
            jax.ShapeDtypeStruct((count, ordered), BF16),
            jax.ShapeDtypeStruct((count, width), BF16),
            jax.ShapeDtypeStruct((8, dim), F32),
        ],
        compiler_params=pltpu.CompilerParams(vmem_limit_bytes=40 * MIB),
        cost_estimate=pl.CostEstimate(flops=4 * count * dim * dim, bytes_accessed=12 * MIB, transcendentals=0),
        name="norm_back_project",
    )(*terms, resid, cot, weights[0], weights[1], order, gain)


def input_back_kernel(
    dq_ref, own_ref, core_ref, from_x_ref, far_ref, x_ref, d_resid_ref, w_low_ref, w_high_ref, order_ref,
    gain_ref, cos_ref, sin_ref, d_kv_ref, input_grad_ref, gain_grad_ref, bias_grad_ref,
):
    joint = dq_ref.shape[1] + d_kv_ref.shape[1]
    dkv = total_of(own_ref, core_ref, from_x_ref, far_ref)
    dk = dkv[:, :LANES]
    dk = dk * cos_ref[...] - swap_halves(dk) * sin_ref[...]
    d_kv = jnp.concatenate([dk.astype(BF16), dkv[:, LANES:].astype(BF16)], axis=1)
    d_kv_ref[...] = d_kv
    d_joined = jnp.concatenate([dq_ref[...], d_kv], axis=1)
    d_normed = jnp.concatenate(
        [dot_nt(d_joined, w_low_ref[:, :joint]), dot_nt(d_joined, w_high_ref[:, :joint])], axis=1
    )
    d_normed = back_in_order(d_normed, order_ref[...])
    x = x_ref[...].astype(F32)
    inverse = lax.rsqrt(jnp.mean(x * x, axis=-1, keepdims=True) + EPSILON)
    input_grad_ref[...] = (d_resid_ref[...] + norm_back(x, inverse, gain_ref[...], d_normed)).astype(BF16)
    gain_grad_ref[...] = fold_rows(d_normed * x * inverse)
    bias_grad_ref[...] = fold_rows(d_joined.astype(F32))


def input_back(dq, terms, x, d_resid, weights, order, gain, cosine, sine, rows, seq):
    count, dim = d_resid.shape
    width = dq.shape[1]
    joint = width + 2 * LANES
    return pl.pallas_call(
        input_back_kernel,
        grid=(1,),
        in_specs=[
            rows_of(rows, width),
            rows_of(rows, 2 * LANES),
            rows_of(rows, 2 * LANES),
            rows_of(rows, 2 * LANES),
            rows_of(rows, 2 * LANES),
            pl.BlockSpec((rows, dim), lambda i: (seq, 0)),
            rows_of(rows, dim),
            whole(weights[0]),
            whole(weights[1]),
            whole(order),
            whole(gain),
            pl.BlockSpec((rows, LANES), lambda i: (seq, 0)),
            pl.BlockSpec((rows, LANES), lambda i: (seq, 0)),
        ],
        out_specs=[
            rows_of(rows, 2 * LANES),
            rows_of(rows, dim),
            pl.BlockSpec((8, dim), lambda i: (0, 0)),
            pl.BlockSpec((8, joint), lambda i: (0, 0)),
        ],
        out_shape=[
            jax.ShapeDtypeStruct((count, 2 * LANES), BF16),
            jax.ShapeDtypeStruct((count, dim), BF16),
            jax.ShapeDtypeStruct((8, dim), F32),
            jax.ShapeDtypeStruct((8, joint), F32),
        ],
        compiler_params=pltpu.CompilerParams(vmem_limit_bytes=40 * MIB),
        cost_estimate=pl.CostEstimate(flops=6 * count * dim * joint, bytes_accessed=12 * MIB, transcendentals=0),
        name="input_gradient",
    )(dq, *terms, x, d_resid, weights[0], weights[1], order, gain, cosine, sine)


def seq_rows(seq, rows, cols):
    return pl.BlockSpec((rows, cols), lambda i: (seq, 0))


def piece_of(seq, rows):
    return pl.BlockSpec((1, rows, 2 * LANES), lambda i: (seq, 0, 0))


def keys_and_values(piece_refs):
    joint = jnp.concatenate([ref[0] for ref in piece_refs], axis=0)
    key, value = joint[:, :LANES], joint[:, LANES:]
    return (key, other_head(key)), (value, other_head(value))


def attend_kernel(block_ref, q_ref, kv_0, kv_1, kv_2, kv_3, start_ref, out_ref):
    rows, width = q_ref.shape
    length = 4 * rows
    heads = width // HD
    group = heads // 2
    keys, values = keys_and_values((kv_0, kv_1, kv_2, kv_3))
    upper_key = lane_of((length, LANES)) >= HD
    upper = lane_of((rows, LANES)) >= HD
    query_at = block_ref[0] * rows + lax.broadcasted_iota(jnp.int32, (rows, length), 0)
    key_at = jnp.concatenate(
        [
            (block_ref[0] ^ place) * rows + lax.broadcasted_iota(jnp.int32, (rows, rows), 1)
            for place in range(4)
        ],
        axis=1,
    )
    allowed = (key_at <= query_at) & (key_at >= start_ref[:, :1])
    bias = jnp.where(allowed, 0.0, MASKED)
    one = jnp.ones((), BF16)
    for pair in range(heads // 2):
        at = slice(pair * LANES, (pair + 1) * LANES)
        both = q_ref[:, at]
        parts = []
        for place in range(2):
            owner = (2 * pair + place) // group
            moved = int(owner != place)
            side = upper if place else ~upper
            side_key = upper_key if place else ~upper_key
            query = jnp.where(side, both, jnp.zeros_like(both))
            score = dot_nt(query, keys[moved]) + bias
            top = jnp.max(score, axis=1, keepdims=True)
            weight = jnp.exp(score - top).astype(BF16)
            mixed = dot_nn(weight, jnp.where(side_key, values[moved], one))
            parts.append(mixed / pltpu.roll(mixed, HD, 1))
        out_ref[:, at] = jnp.where(upper, parts[1], parts[0]).astype(BF16)


def attend(block, q, kv_pieces, start, rows, seq):
    width = q.shape[1]
    heads = width // HD
    return pl.pallas_call(
        attend_kernel,
        grid=(1,),
        in_specs=[
            pl.BlockSpec(memory_space=pltpu.SMEM),
            seq_rows(seq, rows, width),
            *[piece_of(seq, rows)] * 4,
            seq_rows(seq, rows, LANES),
        ],
        out_specs=seq_rows(0, rows, width),
        out_shape=jax.ShapeDtypeStruct((rows, width), BF16),
        compiler_params=pltpu.CompilerParams(vmem_limit_bytes=48 * MIB),
        cost_estimate=pl.CostEstimate(
            flops=32 * rows * rows * LANES * heads,
            bytes_accessed=4 * rows * width,
            transcendentals=4 * rows * rows * heads,
        ),
        name="attention_forward",
    )(block, q, *kv_pieces, start)


def attend_back_kernel(
    block_ref, q_ref, kv_0, kv_1, kv_2, kv_3, back_ref, start_ref, cos_ref, sin_ref,
    dq_ref, own_ref, core_ref, x_ref, far_ref, dk_sum, dv_sum,
):
    rows, width = q_ref.shape
    length = 4 * rows
    heads = width // HD
    group = heads // 2
    keys, values = keys_and_values((kv_0, kv_1, kv_2, kv_3))
    key_t = keys[0].astype(F32).T.astype(BF16)
    keys_t = (key_t, jnp.concatenate([key_t[HD:], key_t[:HD]], axis=0))
    upper = lane_of((rows, LANES)) >= HD
    upper_t = lax.broadcasted_iota(jnp.int32, (LANES, rows), 0) >= HD
    query_at = block_ref[0] * rows + lax.broadcasted_iota(jnp.int32, (length, rows), 1)
    key_at = jnp.concatenate(
        [
            (block_ref[0] ^ place) * rows + lax.broadcasted_iota(jnp.int32, (rows, rows), 0)
            for place in range(4)
        ],
        axis=0,
    )
    allowed = (key_at <= query_at) & (key_at >= start_ref[0, :1, :])
    bias = jnp.where(allowed, 0.0, MASKED)
    cosine, sine = cos_ref[...], sin_ref[...]
    dk_sum[...] = jnp.zeros_like(dk_sum)
    dv_sum[...] = jnp.zeros_like(dv_sum)
    for pair in range(heads // 2):
        at = slice(pair * LANES, (pair + 1) * LANES)
        both = q_ref[:, at]
        back_both = back_ref[:, at]
        parts = []
        for place in range(2):
            owner = (2 * pair + place) // group
            moved = int(owner != place)
            side = upper if place else ~upper
            query = jnp.where(side, both, jnp.zeros_like(both))
            back = jnp.where(side, back_both, jnp.zeros_like(back_both))
            score = dot_nt(keys[moved], query) + bias
            weight = jnp.exp(score - jnp.max(score, axis=0, keepdims=True))
            prob = weight * (1.0 / jnp.sum(weight, axis=0, keepdims=True))
            dv_sum[owner] += dot_nn(prob.astype(BF16), back)
            d_prob = dot_nt(values[moved], back)
            level = jnp.sum(prob * d_prob, axis=0, keepdims=True)
            d_score = (prob * (d_prob - level)).astype(BF16)
            dk_sum[owner] += dot_nn(d_score, query)
            parts.append(dot_nn(keys_t[moved], d_score))
        d_query = jnp.where(upper_t, parts[1], parts[0]).T * SCALE
        dq_ref[:, at] = (d_query * cosine - swap_halves(d_query) * sine).astype(BF16)
    lower_key = lane_of((length, LANES)) < HD
    for total, begin in ((dk_sum, 0), (dv_sum, LANES)):
        first, second = total[0], total[1]
        first = first + pltpu.roll(first, HD, 1)
        second = second + pltpu.roll(second, HD, 1)
        both = jnp.where(lower_key, first, second)
        cols = slice(begin, begin + LANES)
        own_ref[:, cols] = both[:rows]
        for place, ref in enumerate((core_ref, x_ref, far_ref)):
            ref[:, cols] = both[(place + 1) * rows : (place + 2) * rows].astype(BF16)


def parts_of(rows, cols):
    shapes = [jax.ShapeDtypeStruct((rows, cols), F32)] + [jax.ShapeDtypeStruct((rows, cols), BF16)] * 3
    return [seq_rows(0, rows, cols)] * 4, shapes


def attend_back(block, q, kv_pieces, back, start, cosine, sine, rows, seq):
    width = q.shape[1]
    length = 4 * rows
    heads = width // HD
    specs, shapes = parts_of(rows, 2 * LANES)
    return pl.pallas_call(
        attend_back_kernel,
        grid=(1,),
        in_specs=[
            pl.BlockSpec(memory_space=pltpu.SMEM),
            seq_rows(seq, rows, width),
            *[piece_of(seq, rows)] * 4,
            seq_rows(0, rows, width),
            pl.BlockSpec((1, 8, rows), lambda i: (seq, 0, 0)),
            seq_rows(seq, rows, LANES),
            seq_rows(seq, rows, LANES),
        ],
        out_specs=[seq_rows(0, rows, width), *specs],
        out_shape=[jax.ShapeDtypeStruct((rows, width), BF16), *shapes],
        scratch_shapes=[
            pltpu.VMEM((2, length, LANES), F32),
            pltpu.VMEM((2, length, LANES), F32),
        ],
        compiler_params=pltpu.CompilerParams(vmem_limit_bytes=48 * MIB),
        cost_estimate=pl.CostEstimate(
            flops=80 * rows * rows * LANES * heads,
            bytes_accessed=8 * rows * width,
            transcendentals=4 * rows * rows * heads,
        ),
        name="attention_backward",
    )(block, q, *kv_pieces, back, start, cosine, sine)


def mlp_kernel(
    n_0, n_1, n_2, n_3, c_0, c_1, c_2, c_3, w_ref,
    own_ref, out_1, out_2, out_3, d_own_ref, d_1, d_2, d_3, kept_ref, turned_ref,
    normed_all, cot_all,
):
    step = pl.program_id(0)
    rows = own_ref.shape[0]
    columns = w_ref.shape[1] // 3

    @pl.when(step == 0)
    def _():
        for place, (n_ref, c_ref) in enumerate(zip((n_0, n_1, n_2, n_3), (c_0, c_1, c_2, c_3))):
            normed_all[place // 2, (place % 2) * rows : (place % 2 + 1) * rows] = n_ref[...]
            cot_all[place // 2, (place % 2) * rows : (place % 2 + 1) * rows] = c_ref[...]

    normed, cot = normed_all[step], cot_all[step]
    for begin in range(0, columns, TILE):
        at = slice(begin, begin + TILE)
        gate = dot_nn(normed, w_ref[:, begin : begin + TILE])
        up = dot_nn(normed, w_ref[:, columns + begin : columns + begin + TILE])
        d_act = dot_nn(cot, w_ref[:, 2 * columns + begin : 2 * columns + begin + TILE])
        sigmoid = 0.5 * jnp.tanh(0.5 * gate) + 0.5
        swish = gate * sigmoid
        kept_ref[0, :, at] = (d_act * up * (sigmoid + swish * (1.0 - sigmoid))).astype(BF16)
        kept_ref[1, :, at] = (d_act * swish).astype(BF16)
        kept_ref[2, :, at] = (swish * up).astype(BF16)
    turned_ref[0] = normed.T
    turned_ref[1] = cot.T
    out = dot_nt(kept_ref[2], w_ref[:, 2 * columns :])
    d_normed = dot_nt(kept_ref[0], w_ref[:, :columns]) + dot_nt(kept_ref[1], w_ref[:, columns : 2 * columns])

    @pl.when(step == 0)
    def _():
        own_ref[...] = out[:rows]
        out_1[...] = out[rows:].astype(BF16)
        d_own_ref[...] = d_normed[:rows]
        d_1[...] = d_normed[rows:].astype(BF16)

    @pl.when(step == 1)
    def _():
        out_2[...] = out[:rows].astype(BF16)
        out_3[...] = out[rows:].astype(BF16)
        d_2[...] = d_normed[:rows].astype(BF16)
        d_3[...] = d_normed[rows:].astype(BF16)


def mlp(normed, cot, weights, seq):
    rows, dim = normed[0].shape
    columns = weights.shape[1] // 3
    specs, shapes = parts_of(rows, dim)
    once = lambda at: pl.BlockSpec((rows, dim), lambda i: (at, 0), pipeline_mode=pl.Buffered(1))
    return pl.pallas_call(
        mlp_kernel,
        grid=(2,),
        in_specs=[
            *[once(0)] * 4,
            *[once(seq)] * 4,
            pl.BlockSpec(weights.shape, lambda i: (0, 0), pipeline_mode=pl.Buffered(1)),
        ],
        out_specs=[
            *specs,
            *specs,
            pl.BlockSpec((3, 2 * rows, columns), lambda i: (0, i, 0)),
            pl.BlockSpec((2, dim, 2 * rows), lambda i: (0, 0, i)),
        ],
        out_shape=[
            *shapes,
            *shapes,
            jax.ShapeDtypeStruct((3, 4 * rows, columns), BF16),
            jax.ShapeDtypeStruct((2, dim, 4 * rows), BF16),
        ],
        scratch_shapes=[
            pltpu.VMEM((2, 2 * rows, dim), BF16),
            pltpu.VMEM((2, 2 * rows, dim), BF16),
        ],
        compiler_params=pltpu.CompilerParams(vmem_limit_bytes=58 * MIB),
        cost_estimate=pl.CostEstimate(
            flops=48 * rows * dim * columns,
            bytes_accessed=6 * dim * columns + 24 * rows * columns,
            transcendentals=4 * rows * columns,
        ),
        name="feed_forward",
    )(*normed, *cot, weights)


def mlp_grad_kernel(turned_0, turned_1, kept_0, kept_1, grad_ref):
    grad_ref[...] = (dot_nn(turned_0[0], kept_0[0]) + dot_nn(turned_1[0], kept_1[0])).astype(BF16)


def mlp_grad(turned, kept):
    _, dim, count = turned[0].shape
    columns = kept[0].shape[2]
    turned_block = pl.BlockSpec((1, dim, count), lambda i: (i // 2, 0, 0))
    kept_block = pl.BlockSpec((1, count, columns), lambda i: (i, 0, 0))
    return pl.pallas_call(
        mlp_grad_kernel,
        grid=(3,),
        in_specs=[turned_block, turned_block, kept_block, kept_block],
        out_specs=pl.BlockSpec((dim, columns), lambda i: (0, i)),
        out_shape=jax.ShapeDtypeStruct((dim, 3 * columns), BF16),
        compiler_params=pltpu.CompilerParams(vmem_limit_bytes=58 * MIB),
        cost_estimate=pl.CostEstimate(
            flops=12 * count * dim * columns,
            bytes_accessed=6 * dim * columns + 12 * count * columns,
            transcendentals=0,
        ),
        name="feed_forward_gradients",
    )(*turned, *kept)


def pack_kernel(block_ref, gate_ref, up_ref, down_ref, *refs):
    out_refs, scratch = refs[:4], refs[4]
    shard, ff = gate_ref.shape
    quarter = scratch.shape[2] // 4
    for place, ref in enumerate((gate_ref, up_ref, down_ref)):
        scratch[place, :, :ff] = ref[...].astype(F32)
        scratch[place, :, ff:] = jnp.zeros((shard, 4 * quarter - ff), F32)
    for place, out_ref in enumerate(out_refs):
        begin = pl.multiple_of((block_ref[0] ^ place) * quarter, LANES)
        for part in range(3):
            out_ref[:, part * quarter : (part + 1) * quarter] = scratch[part, :, pl.ds(begin, quarter)].astype(BF16)


def pack(block, gate, up, down_t, quarter):
    shard = gate.shape[0]
    return pl.pallas_call(
        pack_kernel,
        in_specs=[pl.BlockSpec(memory_space=pltpu.SMEM)] + [pl.BlockSpec(memory_space=pltpu.VMEM)] * 3,
        out_specs=[pl.BlockSpec(memory_space=pltpu.VMEM)] * 4,
        out_shape=[jax.ShapeDtypeStruct((shard, 3 * quarter), BF16)] * 4,
        scratch_shapes=[pltpu.VMEM((3, shard, 4 * quarter), F32)],
        name="pack_columns",
    )(block, gate, up, down_t)


def pick(options, index):
    value = options[0]
    for place in range(1, len(options)):
        value = jnp.where(index == place, options[place], value)
    return value


def assemble_kernel(block_ref, *refs):
    pieces, out_ref, scratch = refs[:4], refs[4], refs[5]
    shard = pieces[0].shape[0]
    values = [ref[...].astype(F32) for ref in pieces]
    for owner in range(4):
        scratch[owner * shard : (owner + 1) * shard] = pick(values, block_ref[0] ^ owner)
    out_ref[...] = scratch[...].astype(BF16)


def assemble(block, pieces):
    shard, columns = pieces[0].shape
    return pl.pallas_call(
        assemble_kernel,
        in_specs=[pl.BlockSpec(memory_space=pltpu.SMEM)] + [pl.BlockSpec(memory_space=pltpu.VMEM)] * 4,
        out_specs=pl.BlockSpec(memory_space=pltpu.VMEM),
        out_shape=jax.ShapeDtypeStruct((4 * shard, columns), BF16),
        scratch_shapes=[pltpu.VMEM((4 * shard, columns), F32)],
        name="assemble_rows",
    )(block, *pieces)


def cut_kernel(block_ref, value_ref, *refs):
    out_refs, scratch = refs[:4], refs[4]
    shard = out_refs[0].shape[0]
    scratch[...] = value_ref[...].astype(F32)
    values = [scratch[owner * shard : (owner + 1) * shard] for owner in range(4)]
    for place, out_ref in enumerate(out_refs):
        out_ref[...] = pick(values, block_ref[0] ^ place).astype(BF16)


def cut(block, value):
    shard, columns = value.shape[0] // 4, value.shape[1]
    return pl.pallas_call(
        cut_kernel,
        in_specs=[pl.BlockSpec(memory_space=pltpu.SMEM), pl.BlockSpec(memory_space=pltpu.VMEM)],
        out_specs=[pl.BlockSpec(memory_space=pltpu.VMEM)] * 4,
        out_shape=[jax.ShapeDtypeStruct((shard, columns), BF16)] * 4,
        scratch_shapes=[pltpu.VMEM(value.shape, F32)],
        name="cut_rows",
    )(block, value)


def unpack_kernel(block_ref, *refs):
    pieces, out_refs, scratch = refs[:4], refs[4:7], refs[7]
    ff = out_refs[0].shape[1]
    quarter = scratch.shape[2] // 4
    for place, ref in enumerate(pieces):
        begin = pl.multiple_of((block_ref[0] ^ place) * quarter, LANES)
        for part in range(3):
            scratch[part, :, pl.ds(begin, quarter)] = ref[:, part * quarter : (part + 1) * quarter].astype(F32)
    for part, out_ref in enumerate(out_refs):
        out_ref[...] = scratch[part, :, :ff]


def unpack(block, pieces, ff):
    shard, columns = pieces[0].shape
    return pl.pallas_call(
        unpack_kernel,
        in_specs=[pl.BlockSpec(memory_space=pltpu.SMEM)] + [pl.BlockSpec(memory_space=pltpu.VMEM)] * 4,
        out_specs=[pl.BlockSpec(memory_space=pltpu.VMEM)] * 3,
        out_shape=[jax.ShapeDtypeStruct((shard, ff), F32)] * 3,
        scratch_shapes=[pltpu.VMEM((3, shard, columns // 3 * 4), F32)],
        name="unpack_columns",
    )(block, *pieces)


def bit_swap(value, axis, bit=0):
    size = lax.axis_size(axis)
    return lax.ppermute(value, axis, [(i, i ^ (1 << bit)) for i in range(size)])


def jump_swap(value, axes, jump):
    return lax.ppermute(value, axes, [(i, i ^ jump) for i in range(4)])


def to_plane(value, slot):
    high, low = slot >> 1, slot & 1
    pairs = [
        (4 * y + 2 * x + c, 4 * (c ^ low) + 2 * (x ^ high) + y) for y in range(2) for x in range(2) for c in range(2)
    ]
    return lax.ppermute(value, TOKENS + ("cc",), pairs)


def from_plane(value, slot):
    high, low = slot >> 1, slot & 1
    pairs = [
        (4 * y + 2 * x + c, 4 * c + 2 * (x ^ high) + (y ^ low)) for y in range(2) for x in range(2) for c in range(2)
    ]
    return lax.ppermute(value, TOKENS + ("cc",), pairs)


def after(first, *values):
    return lax.optimization_barrier((first, *values))


def gather_four(value, axes):
    from_first = bit_swap(value, axes[0])
    return [value, bit_swap(value, axes[1]), from_first, bit_swap(from_first, axes[1])]


def gather_direct(value, axes):
    return [value] + [jump_swap(value, axes, jump) for jump in range(1, 4)]


def sum_direct(axes, own, *away):
    return [own] + [jump_swap(value, axes, jump + 1) for jump, value in enumerate(away)]


class Doubling:
    def __init__(self, size):
        bits = size.bit_length() - 1
        self.steps = [("fz", bit) for bit in reversed(range(bits))] + [("fy", 0), ("cx", 0), ("cc", 0)]
        weight = {"cc": 1, "cx": 2, "fy": 4, "fz": 8}
        self.offsets = [0]
        for axis, bit in self.steps:
            jump = weight[axis] << bit
            self.offsets += [offset ^ jump for offset in self.offsets]

    def gather(self, value, steps):
        for axis, bit in steps:
            value = jnp.concatenate([value, bit_swap(value, axis, bit)], axis=0)
        return value


def halve(value, axis, bit=0):
    middle = value.shape[0] // 2
    came = bit_swap(value[middle:], axis, bit)
    return (value[:middle].astype(F32) + came.astype(F32)).astype(BF16)


def on_device(
    doubling,
    hidden,
    segments,
    attn_gain,
    qkv_weight,
    qkv_bias,
    out_weight,
    mlp_gain,
    gate_weight,
    up_weight,
    down_weight,
    cotangent,
):
    seqs, rows, dim = hidden.shape
    count = seqs * rows
    shard = attn_gain.shape[0]
    world = dim // shard
    joint = qkv_weight.shape[1]
    width = joint - 2 * LANES
    ff = gate_weight.shape[1]
    block = lax.axis_index("cx") * lax.axis_size("cc") + lax.axis_index("cc")
    me = lax.axis_index(FSDP) * lax.axis_size(CTX) + block
    offset = block * rows
    block_arg = block.reshape(1).astype(jnp.int32)
    plane_arg = (lax.axis_index("cx") * 2 + lax.axis_index("fy")).reshape(1).astype(jnp.int32)
    x = hidden.reshape(count, dim)
    cot = cotangent.reshape(count, dim)

    padded = -(-(shard + 1) // 16) * 16
    small = jnp.concatenate([attn_gain, mlp_gain, qkv_bias])
    small_row = jnp.pad(small, (0, joint + width - small.shape[0]))[None]
    first_shard = jnp.concatenate(
        [
            jnp.concatenate([qkv_weight, out_weight.T], axis=1),
            small_row,
            jnp.zeros((padded - shard - 1, joint + width), BF16),
        ],
        axis=0,
    )
    first = doubling.gather(first_shard, doubling.steps[:1])

    quarter = -(-ff // (4 * TILE)) * TILE
    pieces = pack(block_arg, gate_weight, up_weight, down_weight.T, quarter)
    pieces = [to_plane(piece, slot) for slot, piece in enumerate(pieces)]
    first, *pieces = after(first, *pieces)
    mlp_shard = assemble(plane_arg, pieces)
    mlp_weights = lax.all_gather(mlp_shard, WEIGHTS, axis=0, tiled=True)

    first = doubling.gather(first, doubling.steps[1:-1])
    first, cot_late = after(first, cot)
    weights = (first, bit_swap(first, *doubling.steps[-1]))
    cot_all = gather_four(cot_late, TOKENS)

    owner = me ^ jnp.array(doubling.offsets, jnp.int32)
    within = jnp.arange(padded, dtype=jnp.int32)
    target = jnp.where(within[None, :] < shard, owner[:, None] * shard + within[None, :], -1).reshape(1, -1)
    order = (jnp.arange(dim, dtype=jnp.int32)[:, None] == target).astype(BF16)
    by_owner = (owner[None, :] == jnp.arange(world, dtype=jnp.int32)[:, None]).astype(BF16)
    extras = jnp.concatenate(
        [part.reshape(world // 2, padded, -1)[:, shard, : small.shape[0]] for part in weights], axis=0
    )
    extras = dot_nn(by_owner, extras)
    gain_attn = extras[:, :shard].reshape(1, dim)
    gain_mlp = extras[:, shard : 2 * shard].reshape(1, dim)
    bias = extras[:, 2 * shard :].reshape(1, joint)

    at_row = lax.dynamic_slice_in_dim(segments, offset, rows, axis=1)
    zeros_before = jnp.sum((segments < 1).astype(jnp.int32), axis=1, keepdims=True)
    ones_before = jnp.sum((segments < 2).astype(jnp.int32), axis=1, keepdims=True)
    start = jnp.where(at_row == 0, 0, jnp.where(at_row == 1, zeros_before, ones_before))
    position = (offset + jnp.arange(rows, dtype=jnp.int32)[None, :] - start).reshape(count)
    lane = jnp.arange(LANES, dtype=jnp.int32)
    frequency = ROPE_BASE ** (-(lane % (HD // 2)).astype(F32) * 2.0 / HD)
    angle = position.astype(F32)[:, None] * frequency[None, :]
    cosine = jnp.cos(angle)
    sine = jnp.where(lane % HD < HD // 2, -1.0, 1.0)[None, :] * jnp.sin(angle)
    start_column = jnp.broadcast_to(start.reshape(count, 1), (count, LANES))
    start_row = jnp.broadcast_to(start[:, None, :], (seqs, 8, rows))

    normed, q, kv = prep(x, gain_attn, order, weights, bias, cosine, sine, rows)
    kv_all = gather_four(kv.reshape(seqs, rows, 2 * LANES), CTX)
    attended, resid, normed_all = [], [], []
    for seq in range(seqs):
        attended.append(attend(block_arg, q, kv_all, start_column, rows, seq))
        resid_one, normed_one = project_out(attended[seq], x, weights, order, gain_mlp, rows, seq)
        resid.append(resid_one)
        normed_all.append(gather_direct(normed_one, TOKENS))

    out_parts, d_terms, kept, turned = [], [], [], []
    for seq in range(seqs):
        result = mlp(normed_all[seq], cot_all, mlp_weights, seq)
        out_parts.append(result[:4])
        d_terms.append(sum_direct(TOKENS, *result[4:8]))
        kept.append(result[8])
        turned.append(result[9])
    grads = mlp_grad(turned, kept)
    grads, d_terms[0], d_terms[1] = after(grads, *d_terms)
    grads = lax.psum_scatter(
        grads.reshape(world // 4, 4 * shard, 3 * quarter), WEIGHTS, scatter_dimension=0, tiled=False
    )

    d_resid, d_branch, d_attended, mlp_gain_grad = [], [], [], []
    for seq in range(seqs):
        result = project_out_back(d_terms[seq], resid[seq], cot, weights, order, gain_mlp, rows, seq)
        for place, value in zip((d_resid, d_branch, d_attended, mlp_gain_grad), result):
            place.append(value)
    out_grad = dot_tn(jnp.concatenate(d_branch, axis=0), jnp.concatenate(attended, axis=0)).astype(BF16)
    out_grad = halve(out_grad, "cc")
    out_terms = [sum_direct(TOKENS, *after(d_terms[1][1], *part)[1:]) for part in out_parts]
    dq, dkv_terms = [], []
    for seq in range(seqs):
        if seq == 1:
            d_attended[1], out_grad, out_terms[0] = after(d_attended[1], out_grad, out_terms[0])
            out_grad = halve(out_grad, "cx")
        result = attend_back(block_arg, q, kv_all, d_attended[seq], start_row, cosine, sine, rows, seq)
        dq.append(result[0])
        dkv_terms.append(sum_direct(CTX, *result[1:]))
    dq[1], out_grad, out_terms[1] = after(dq[1], out_grad, out_terms[1])
    q_grad = dot_tn(normed, jnp.concatenate(dq, axis=0)).astype(BF16)
    q_grad = halve(q_grad, "cc")
    dkv_terms[0], q_grad = after(dkv_terms[0], q_grad)
    q_grad = halve(q_grad, "cx")
    d_kv, input_grad, attn_gain_grad, bias_grad = [], [], [], []
    for seq in range(seqs):
        result = input_back(
            dq[seq], dkv_terms[seq], x, d_resid[seq], weights, order, gain_attn, cosine, sine, rows, seq
        )
        for place, value in zip((d_kv, input_grad, attn_gain_grad, bias_grad), result):
            place.append(value)
    d_kv[1], q_grad = after(d_kv[1], q_grad)

    output = []
    for seq in range(seqs):
        own, *away = out_terms[seq]
        output.append((resid[seq] + own + sum(term.astype(F32) for term in away)).astype(BF16))

    split_at = width + LANES
    bias_grad = jnp.sum(sum(bias_grad), axis=0)
    small_grads = jnp.concatenate(
        [
            jnp.sum(sum(attn_gain_grad), axis=0).reshape(world, -1),
            jnp.sum(sum(mlp_gain_grad), axis=0).reshape(world, -1),
            bias_grad[:split_at].reshape(world, -1),
            bias_grad[split_at:].reshape(world, -1),
        ],
        axis=1,
    ).astype(BF16)
    small_count = small_grads.shape[1]
    small_grads = jnp.pad(small_grads, ((0, 0), (0, 2 * LANES - small_count)))
    place = jnp.where(within[None, :] == shard, owner[:, None], -1).reshape(1, -1)
    spread = (jnp.arange(world, dtype=jnp.int32)[:, None] == place).astype(BF16)
    kv_grad = dot_tn(
        jnp.concatenate([normed, spread], axis=0), jnp.concatenate([*d_kv, small_grads], axis=0)
    ).astype(BF16)
    kv_grad = halve(halve(kv_grad, "cc"), "cx")
    first_sum = jnp.concatenate([q_grad, kv_grad, out_grad], axis=1)
    for axis, bit in reversed(doubling.steps[:-2]):
        first_sum = halve(first_sum, axis, bit)
    first_sum = first_sum.astype(F32)
    qkv_sum, out_sum = first_sum[:, :joint], first_sum[:, joint:]
    small_sum = qkv_sum[shard, width : width + small_count]
    at = (shard, 2 * shard, 2 * shard + split_at // world)

    pieces = cut(plane_arg, lax.optimization_barrier(grads))
    pieces = [from_plane(piece, slot) for slot, piece in enumerate(pieces)]
    gate_grad, up_grad, down_grad_t = unpack(block_arg, pieces, ff)
    return (
        jnp.stack(output),
        jnp.stack(input_grad),
        small_sum[: at[0]],
        qkv_sum[:shard],
        small_sum[at[1] : at[2]],
        small_sum[at[2] :],
        out_sum[:shard].T,
        small_sum[at[0] : at[1]],
        gate_grad,
        up_grad,
        down_grad_t.T,
    )


def solution(mesh):
    fsdp, ctx = mesh.shape["fsdp"], mesh.shape["ctx"]
    inner = Mesh(mesh.devices.reshape(fsdp // 2, 2, 2, ctx // 2), AXES)
    tokens = P(FSDP, CTX, None)
    vector = P(AXES)
    by_row = P(AXES, None)
    by_column = P(None, AXES)
    return jax.shard_map(
        functools.partial(on_device, Doubling(fsdp // 2)),
        mesh=inner,
        in_specs=(
            tokens,
            P(FSDP, None),
            vector,
            by_row,
            vector,
            by_column,
            vector,
            by_row,
            by_row,
            by_column,
            tokens,
        ),
        out_specs=(
            tokens,
            tokens,
            vector,
            by_row,
            vector,
            vector,
            by_column,
            vector,
            by_row,
            by_row,
            by_column,
        ),
        check_vma=False,
    )
```

```python
import functools

import jax
import jax.numpy as jnp
from jax import lax
from jax.experimental import pallas as pl
from jax.experimental.pallas import tpu as pltpu
from jax.sharding import Mesh
from jax.sharding import PartitionSpec as P

HD = 64
LANES = 128
EPSILON = 1e-06
ROPE_BASE = 1000000.0
MASKED = -1e30
SCALE = HD ** (-0.5)
TILE = 256
MIB = 1 << 20
VMEM_LIMIT = 60 * MIB
F32 = jnp.float32
BF16 = jnp.bfloat16
AXES = ("fz", "fy", "cx", "cc")
FSDP = ("fz", "fy")
CTX = ("cx", "cc")
TOKENS = ("fy", "cx")
WEIGHTS = ("fz", "cc")


def dot_nn(a, b):
    return lax.dot_general(a, b, (((1,), (0,)), ((), ())), preferred_element_type=F32)


def dot_nt(a, b):
    return lax.dot_general(a, b, (((1,), (1,)), ((), ())), preferred_element_type=F32)


def dot_tn(a, b):
    return lax.dot_general(a, b, (((0,), (0,)), ((), ())), preferred_element_type=F32)


def lane_of(shape):
    return lax.broadcasted_iota(jnp.int32, shape, len(shape) - 1)


def swap_halves(block):
    lead = lane_of(block.shape) % HD < HD // 2
    return jnp.where(
        lead, pltpu.roll(block, LANES - HD // 2, 1), pltpu.roll(block, HD // 2, 1)
    )


def other_head(block):
    return jnp.concatenate([block[:, HD:], block[:, :HD]], axis=1)


def read_out(extras, first, piece, total):
    owners, columns = extras.shape
    at = lax.broadcasted_iota(jnp.int32, (columns, total), 1) % piece + first
    chosen = (lax.broadcasted_iota(jnp.int32, (columns, total), 0) == at).astype(BF16)
    spread = dot_nn(extras, chosen)
    owner = lax.broadcasted_iota(jnp.int32, (owners, total), 1) // piece
    mine = owner == lax.broadcasted_iota(jnp.int32, (owners, total), 0)
    return jnp.sum(jnp.where(mine, spread, 0.0), axis=0, keepdims=True)


def prep_kernel(
    x_ref, order_ref, spread_ref, w_low_ref, w_high_ref, cos_ref, sin_ref,
    normed_ref, q_ref, kv_ref, gain_ref, gain_mlp_ref,
):
    x = x_ref[...].astype(F32)
    dim = x.shape[1]
    width = q_ref.shape[1]
    joint = w_low_ref.shape[1]
    middle = w_low_ref.shape[0]
    owners = spread_ref.shape[0]
    extras = dot_nn(spread_ref[:, :middle], w_low_ref[:, :LANES])
    extras = (extras + dot_nn(spread_ref[:, middle:], w_high_ref[:, :LANES])).astype(BF16)
    shard = dim // owners
    gain = read_out(extras, 0, shard, dim)
    gain_ref[...] = gain
    gain_mlp_ref[...] = read_out(extras, shard, shard, dim)
    bias = read_out(extras, 2 * shard, joint // owners, joint)
    inverse = lax.rsqrt(jnp.mean(x * x, axis=-1, keepdims=True) + EPSILON)
    normed = (x * inverse * gain).astype(BF16)
    ordered = dot_nn(normed, order_ref[...]).astype(BF16)
    normed_ref[...] = ordered
    joined = dot_nn(ordered[:, :middle], w_low_ref[...])
    joined = joined + dot_nn(ordered[:, middle:], w_high_ref[...]) + bias
    cosine, sine = cos_ref[...], sin_ref[...]
    for begin in range(0, width + LANES, LANES):
        block = joined[:, begin : begin + LANES]
        turned = block * cosine + swap_halves(block) * sine
        if begin < width:
            q_ref[:, begin : begin + LANES] = (turned * SCALE).astype(BF16)
        else:
            kv_ref[:, :LANES] = turned.astype(BF16)
    kv_ref[:, LANES:] = joined[:, width + LANES :].astype(BF16)


def rows_of(rows, cols):
    return pl.BlockSpec((rows, cols), lambda i: (i, 0))


def whole(value):
    return pl.BlockSpec(value.shape, lambda i: (0,) * value.ndim)


def prep(x, order, spread, weights, cosine, sine, rows):
    count, dim = x.shape
    ordered = order.shape[1]
    joint = weights[0].shape[1]
    width = joint - 2 * LANES
    row = pl.BlockSpec((1, dim), lambda i: (0, 0))
    return pl.pallas_call(
        prep_kernel,
        grid=(count // rows,),
        in_specs=[
            rows_of(rows, dim),
            whole(order),
            whole(spread),
            whole(weights[0]),
            whole(weights[1]),
            rows_of(rows, LANES),
            rows_of(rows, LANES),
        ],
        out_specs=[rows_of(rows, ordered), rows_of(rows, width), rows_of(rows, 2 * LANES), row, row],
        out_shape=[
            jax.ShapeDtypeStruct((count, ordered), BF16),
            jax.ShapeDtypeStruct((count, width), BF16),
            jax.ShapeDtypeStruct((count, 2 * LANES), BF16),
            jax.ShapeDtypeStruct((1, dim), F32),
            jax.ShapeDtypeStruct((1, dim), F32),
        ],
        compiler_params=pltpu.CompilerParams(vmem_limit_bytes=VMEM_LIMIT),
        cost_estimate=pl.CostEstimate(
            flops=2 * count * ordered * (joint + dim), bytes_accessed=12 * MIB, transcendentals=0
        ),
        name="norm_project_rotate",
    )(x, order, spread, weights[0], weights[1], cosine, sine)


def back_in_order(value, order):
    high = value.astype(BF16)
    low = (value - high.astype(F32)).astype(BF16)
    return dot_nt(high, order) + dot_nt(low, order)


def out_kernel(attended_ref, x_ref, w_low_ref, w_high_ref, order_ref, gain_ref, resid_ref, normed_ref):
    attended = attended_ref[...]
    branch = jnp.concatenate([dot_nt(attended, w_low_ref[...]), dot_nt(attended, w_high_ref[...])], axis=1)
    resid = x_ref[...].astype(F32) + back_in_order(branch, order_ref[...])
    inverse = lax.rsqrt(jnp.mean(resid * resid, axis=-1, keepdims=True) + EPSILON)
    resid_ref[...] = resid
    normed_ref[...] = (resid * inverse * gain_ref[...]).astype(BF16)


def project_out(attended, x, weights, order, gain, rows, seq):
    dim = x.shape[1]
    count = rows
    return pl.pallas_call(
        out_kernel,
        grid=(1,),
        in_specs=[
            rows_of(rows, attended.shape[1]),
            pl.BlockSpec((rows, dim), lambda i: (seq, 0)),
            whole(weights[0]),
            whole(weights[1]),
            whole(order),
            whole(gain),
        ],
        out_specs=[rows_of(rows, dim), rows_of(rows, dim)],
        out_shape=[jax.ShapeDtypeStruct((count, dim), F32), jax.ShapeDtypeStruct((count, dim), BF16)],
        compiler_params=pltpu.CompilerParams(vmem_limit_bytes=VMEM_LIMIT),
        cost_estimate=pl.CostEstimate(flops=6 * count * dim * dim, bytes_accessed=8 * MIB, transcendentals=0),
        name="project_out_norm",
    )(attended, x, weights[0], weights[1], order, gain)


def fold_rows(value):
    return jnp.sum(value.reshape(-1, 8, value.shape[1]), axis=0)


def norm_back(values, inverse, gain, incoming):
    scaled = incoming * gain
    mean_term = jnp.mean(scaled * values, axis=-1, keepdims=True)
    return inverse * scaled - values * inverse**3 * mean_term


def total_of(own_ref, *away_refs):
    total = own_ref[...]
    for ref in away_refs:
        total = total + ref[...].astype(F32)
    return total


def out_back_kernel(
    own_ref, core_ref, x_ref, far_ref, resid_ref, cot_ref, w_low_ref, w_high_ref, order_ref, gain_ref,
    d_resid_ref, d_branch_ref, d_attended_ref, gain_grad_ref,
):
    middle = w_low_ref.shape[0]
    d_normed = total_of(own_ref, core_ref, x_ref, far_ref)
    resid = resid_ref[...]
    inverse = lax.rsqrt(jnp.mean(resid * resid, axis=-1, keepdims=True) + EPSILON)
    d_resid = cot_ref[...].astype(F32) + norm_back(resid, inverse, gain_ref[...], d_normed)
    d_resid_ref[...] = d_resid
    d_branch = dot_nn(d_resid.astype(BF16), order_ref[...]).astype(BF16)
    d_branch_ref[...] = d_branch
    d_attended = dot_nn(d_branch[:, :middle], w_low_ref[...])
    d_attended = d_attended + dot_nn(d_branch[:, middle:], w_high_ref[...])
    d_attended_ref[...] = d_attended.astype(BF16)
    gain_grad_ref[...] = fold_rows(d_normed * resid * inverse)


def project_out_back(terms, resid, cot, weights, order, gain, rows, seq):
    count, dim = resid.shape
    ordered = order.shape[1]
    width = dim
    return pl.pallas_call(
        out_back_kernel,
        grid=(1,),
        in_specs=[
            rows_of(rows, dim),
            rows_of(rows, dim),
            rows_of(rows, dim),
            rows_of(rows, dim),
            rows_of(rows, dim),
            pl.BlockSpec((rows, dim), lambda i: (seq, 0)),
            whole(weights[0]),
            whole(weights[1]),
            whole(order),
            whole(gain),
        ],
        out_specs=[
            rows_of(rows, dim),
            rows_of(rows, ordered),
            rows_of(rows, width),
            pl.BlockSpec((8, dim), lambda i: (0, 0)),
        ],
        out_shape=[
            jax.ShapeDtypeStruct((count, dim), F32),
            jax.ShapeDtypeStruct((count, ordered), BF16),
            jax.ShapeDtypeStruct((count, width), BF16),
            jax.ShapeDtypeStruct((8, dim), F32),
        ],
        compiler_params=pltpu.CompilerParams(vmem_limit_bytes=VMEM_LIMIT),
        cost_estimate=pl.CostEstimate(flops=4 * count * dim * dim, bytes_accessed=12 * MIB, transcendentals=0),
        name="norm_back_project",
    )(*terms, resid, cot, weights[0], weights[1], order, gain)


def input_back_kernel(
    dq_ref, own_ref, core_ref, from_x_ref, far_ref, x_ref, d_resid_ref, w_low_ref, w_high_ref, order_ref,
    gain_ref, cos_ref, sin_ref, d_kv_ref, input_grad_ref, gain_grad_ref, bias_grad_ref,
):
    dkv = total_of(own_ref, core_ref, from_x_ref, far_ref)
    dk = dkv[:, :LANES]
    dk = dk * cos_ref[...] - swap_halves(dk) * sin_ref[...]
    d_kv = jnp.concatenate([dk.astype(BF16), dkv[:, LANES:].astype(BF16)], axis=1)
    d_kv_ref[...] = d_kv
    d_joined = jnp.concatenate([dq_ref[...], d_kv], axis=1)
    d_normed = jnp.concatenate(
        [dot_nt(d_joined, w_low_ref[...]), dot_nt(d_joined, w_high_ref[...])], axis=1
    )
    d_normed = back_in_order(d_normed, order_ref[...])
    x = x_ref[...].astype(F32)
    inverse = lax.rsqrt(jnp.mean(x * x, axis=-1, keepdims=True) + EPSILON)
    input_grad_ref[...] = (d_resid_ref[...] + norm_back(x, inverse, gain_ref[...], d_normed)).astype(BF16)
    gain_grad_ref[...] = fold_rows(d_normed * x * inverse)
    bias_grad_ref[...] = fold_rows(d_joined.astype(F32))


def input_back(dq, terms, x, d_resid, weights, order, gain, cosine, sine, rows, seq):
    count, dim = d_resid.shape
    width = dq.shape[1]
    joint = width + 2 * LANES
    return pl.pallas_call(
        input_back_kernel,
        grid=(1,),
        in_specs=[
            rows_of(rows, width),
            rows_of(rows, 2 * LANES),
            rows_of(rows, 2 * LANES),
            rows_of(rows, 2 * LANES),
            rows_of(rows, 2 * LANES),
            pl.BlockSpec((rows, dim), lambda i: (seq, 0)),
            rows_of(rows, dim),
            whole(weights[0]),
            whole(weights[1]),
            whole(order),
            whole(gain),
            pl.BlockSpec((rows, LANES), lambda i: (seq, 0)),
            pl.BlockSpec((rows, LANES), lambda i: (seq, 0)),
        ],
        out_specs=[
            rows_of(rows, 2 * LANES),
            rows_of(rows, dim),
            pl.BlockSpec((8, dim), lambda i: (0, 0)),
            pl.BlockSpec((8, joint), lambda i: (0, 0)),
        ],
        out_shape=[
            jax.ShapeDtypeStruct((count, 2 * LANES), BF16),
            jax.ShapeDtypeStruct((count, dim), BF16),
            jax.ShapeDtypeStruct((8, dim), F32),
            jax.ShapeDtypeStruct((8, joint), F32),
        ],
        compiler_params=pltpu.CompilerParams(vmem_limit_bytes=VMEM_LIMIT),
        cost_estimate=pl.CostEstimate(flops=6 * count * dim * joint, bytes_accessed=12 * MIB, transcendentals=0),
        name="input_gradient",
    )(dq, *terms, x, d_resid, weights[0], weights[1], order, gain, cosine, sine)


def seq_rows(seq, rows, cols):
    return pl.BlockSpec((rows, cols), lambda i: (seq, 0))


def piece_of(seq, rows):
    return pl.BlockSpec((1, rows, 2 * LANES), lambda i: (seq, 0, 0))


def keys_and_values(piece_refs):
    joint = jnp.concatenate([ref[0] for ref in piece_refs], axis=0)
    key, value = joint[:, :LANES], joint[:, LANES:]
    return (key, other_head(key)), (value, other_head(value))


def attend_kernel(block_ref, q_ref, kv_0, kv_1, kv_2, kv_3, start_ref, out_ref):
    rows, width = q_ref.shape
    length = 4 * rows
    heads = width // HD
    group = heads // 2
    keys, values = keys_and_values((kv_0, kv_1, kv_2, kv_3))
    upper_key = lane_of((length, LANES)) >= HD
    upper = lane_of((rows, LANES)) >= HD
    query_at = block_ref[0] * rows + lax.broadcasted_iota(jnp.int32, (rows, length), 0)
    key_at = jnp.concatenate(
        [
            (block_ref[0] ^ place) * rows + lax.broadcasted_iota(jnp.int32, (rows, rows), 1)
            for place in range(4)
        ],
        axis=1,
    )
    allowed = (key_at <= query_at) & (key_at >= start_ref[:, :1])
    bias = jnp.where(allowed, 0.0, MASKED)
    one = jnp.ones((), BF16)
    for pair in range(heads // 2):
        at = slice(pair * LANES, (pair + 1) * LANES)
        both = q_ref[:, at]
        parts = []
        for place in range(2):
            owner = (2 * pair + place) // group
            moved = int(owner != place)
            side = upper if place else ~upper
            side_key = upper_key if place else ~upper_key
            query = jnp.where(side, both, jnp.zeros_like(both))
            score = dot_nt(query, keys[moved]) + bias
            top = jnp.max(score, axis=1, keepdims=True)
            weight = jnp.exp(score - top).astype(BF16)
            mixed = dot_nn(weight, jnp.where(side_key, values[moved], one))
            parts.append(mixed / pltpu.roll(mixed, HD, 1))
        out_ref[:, at] = jnp.where(upper, parts[1], parts[0]).astype(BF16)


def attend(block, q, kv_pieces, start, rows, seq):
    width = q.shape[1]
    heads = width // HD
    return pl.pallas_call(
        attend_kernel,
        grid=(1,),
        in_specs=[
            pl.BlockSpec(memory_space=pltpu.SMEM),
            seq_rows(seq, rows, width),
            *[piece_of(seq, rows)] * 4,
            seq_rows(seq, rows, LANES),
        ],
        out_specs=seq_rows(0, rows, width),
        out_shape=jax.ShapeDtypeStruct((rows, width), BF16),
        compiler_params=pltpu.CompilerParams(vmem_limit_bytes=VMEM_LIMIT),
        cost_estimate=pl.CostEstimate(
            flops=32 * rows * rows * LANES * heads,
            bytes_accessed=4 * rows * width,
            transcendentals=4 * rows * rows * heads,
        ),
        name="attention_forward",
    )(block, q, *kv_pieces, start)


def attend_back_kernel(
    block_ref, q_ref, kv_0, kv_1, kv_2, kv_3, back_ref, start_ref, cos_ref, sin_ref,
    dq_ref, own_ref, core_ref, x_ref, far_ref, dk_sum, dv_sum,
):
    rows, width = q_ref.shape
    length = 4 * rows
    heads = width // HD
    group = heads // 2
    keys, values = keys_and_values((kv_0, kv_1, kv_2, kv_3))
    key_t = keys[0].astype(F32).T.astype(BF16)
    keys_t = (key_t, jnp.concatenate([key_t[HD:], key_t[:HD]], axis=0))
    upper = lane_of((rows, LANES)) >= HD
    upper_t = lax.broadcasted_iota(jnp.int32, (LANES, rows), 0) >= HD
    query_at = block_ref[0] * rows + lax.broadcasted_iota(jnp.int32, (length, rows), 1)
    key_at = jnp.concatenate(
        [
            (block_ref[0] ^ place) * rows + lax.broadcasted_iota(jnp.int32, (rows, rows), 0)
            for place in range(4)
        ],
        axis=0,
    )
    allowed = (key_at <= query_at) & (key_at >= start_ref[0, :1, :])
    bias = jnp.where(allowed, 0.0, MASKED)
    cosine, sine = cos_ref[...], sin_ref[...]
    dk_sum[...] = jnp.zeros_like(dk_sum)
    dv_sum[...] = jnp.zeros_like(dv_sum)
    for pair in range(heads // 2):
        at = slice(pair * LANES, (pair + 1) * LANES)
        both = q_ref[:, at]
        back_both = back_ref[:, at]
        parts = []
        for place in range(2):
            owner = (2 * pair + place) // group
            moved = int(owner != place)
            side = upper if place else ~upper
            query = jnp.where(side, both, jnp.zeros_like(both))
            back = jnp.where(side, back_both, jnp.zeros_like(back_both))
            score = dot_nt(keys[moved], query) + bias
            weight = jnp.exp(score - jnp.max(score, axis=0, keepdims=True))
            prob = weight * (1.0 / jnp.sum(weight, axis=0, keepdims=True))
            dv_sum[owner] += dot_nn(prob.astype(BF16), back)
            d_prob = dot_nt(values[moved], back)
            level = jnp.sum(prob * d_prob, axis=0, keepdims=True)
            d_score = (prob * (d_prob - level)).astype(BF16)
            dk_sum[owner] += dot_nn(d_score, query)
            parts.append(dot_nn(keys_t[moved], d_score))
        d_query = jnp.where(upper_t, parts[1], parts[0]).T * SCALE
        dq_ref[:, at] = (d_query * cosine - swap_halves(d_query) * sine).astype(BF16)
    lower_key = lane_of((length, LANES)) < HD
    for total, begin in ((dk_sum, 0), (dv_sum, LANES)):
        first, second = total[0], total[1]
        first = first + pltpu.roll(first, HD, 1)
        second = second + pltpu.roll(second, HD, 1)
        both = jnp.where(lower_key, first, second)
        cols = slice(begin, begin + LANES)
        own_ref[:, cols] = both[:rows]
        for place, ref in enumerate((core_ref, x_ref, far_ref)):
            ref[:, cols] = both[(place + 1) * rows : (place + 2) * rows].astype(BF16)


def parts_of(rows, cols):
    shapes = [jax.ShapeDtypeStruct((rows, cols), F32)] + [jax.ShapeDtypeStruct((rows, cols), BF16)] * 3
    return [seq_rows(0, rows, cols)] * 4, shapes


def attend_back(block, q, kv_pieces, back, start, cosine, sine, rows, seq):
    width = q.shape[1]
    length = 4 * rows
    heads = width // HD
    specs, shapes = parts_of(rows, 2 * LANES)
    return pl.pallas_call(
        attend_back_kernel,
        grid=(1,),
        in_specs=[
            pl.BlockSpec(memory_space=pltpu.SMEM),
            seq_rows(seq, rows, width),
            *[piece_of(seq, rows)] * 4,
            seq_rows(0, rows, width),
            pl.BlockSpec((1, 8, rows), lambda i: (seq, 0, 0)),
            seq_rows(seq, rows, LANES),
            seq_rows(seq, rows, LANES),
        ],
        out_specs=[seq_rows(0, rows, width), *specs],
        out_shape=[jax.ShapeDtypeStruct((rows, width), BF16), *shapes],
        scratch_shapes=[
            pltpu.VMEM((2, length, LANES), F32),
            pltpu.VMEM((2, length, LANES), F32),
        ],
        compiler_params=pltpu.CompilerParams(vmem_limit_bytes=VMEM_LIMIT),
        cost_estimate=pl.CostEstimate(
            flops=80 * rows * rows * LANES * heads,
            bytes_accessed=8 * rows * width,
            transcendentals=4 * rows * rows * heads,
        ),
        name="attention_backward",
    )(block, q, *kv_pieces, back, start, cosine, sine)


def mlp_kernel(
    n_0, n_1, n_2, n_3, c_0, c_1, c_2, c_3, w_ref,
    own_ref, out_1, out_2, out_3, d_own_ref, d_1, d_2, d_3, kept_ref, turned_ref,
    normed_all, cot_all,
):
    step = pl.program_id(0)
    rows = own_ref.shape[0]
    columns = w_ref.shape[1] // 3

    @pl.when(step == 0)
    def _():
        for place, (n_ref, c_ref) in enumerate(zip((n_0, n_1, n_2, n_3), (c_0, c_1, c_2, c_3))):
            normed_all[place // 2, (place % 2) * rows : (place % 2 + 1) * rows] = n_ref[...]
            cot_all[place // 2, (place % 2) * rows : (place % 2 + 1) * rows] = c_ref[...]

    normed, cot = normed_all[step], cot_all[step]
    for begin in range(0, columns, TILE):
        at = slice(begin, begin + TILE)
        gate = dot_nn(normed, w_ref[:, begin : begin + TILE])
        up = dot_nn(normed, w_ref[:, columns + begin : columns + begin + TILE])
        d_act = dot_nn(cot, w_ref[:, 2 * columns + begin : 2 * columns + begin + TILE])
        sigmoid = 0.5 * jnp.tanh(0.5 * gate) + 0.5
        swish = gate * sigmoid
        kept_ref[0, :, at] = (d_act * up * (sigmoid + swish * (1.0 - sigmoid))).astype(BF16)
        kept_ref[1, :, at] = (d_act * swish).astype(BF16)
        kept_ref[2, :, at] = (swish * up).astype(BF16)
    turned_ref[0] = normed.T
    turned_ref[1] = cot.T
    out = dot_nt(kept_ref[2], w_ref[:, 2 * columns :])
    d_normed = dot_nt(kept_ref[0], w_ref[:, :columns]) + dot_nt(kept_ref[1], w_ref[:, columns : 2 * columns])

    @pl.when(step == 0)
    def _():
        own_ref[...] = out[:rows]
        out_1[...] = out[rows:].astype(BF16)
        d_own_ref[...] = d_normed[:rows]
        d_1[...] = d_normed[rows:].astype(BF16)

    @pl.when(step == 1)
    def _():
        out_2[...] = out[:rows].astype(BF16)
        out_3[...] = out[rows:].astype(BF16)
        d_2[...] = d_normed[:rows].astype(BF16)
        d_3[...] = d_normed[rows:].astype(BF16)


def mlp(normed, cot, weights, seq):
    rows, dim = normed[0].shape
    columns = weights.shape[1] // 3
    specs, shapes = parts_of(rows, dim)
    once = lambda at: pl.BlockSpec((rows, dim), lambda i: (at, 0), pipeline_mode=pl.Buffered(1))
    return pl.pallas_call(
        mlp_kernel,
        grid=(2,),
        in_specs=[
            *[once(0)] * 4,
            *[once(seq)] * 3,
            once(0),
            pl.BlockSpec(weights.shape, lambda i: (0, 0), pipeline_mode=pl.Buffered(1)),
        ],
        out_specs=[
            *specs,
            *specs,
            pl.BlockSpec((3, 2 * rows, columns), lambda i: (0, i, 0)),
            pl.BlockSpec((2, dim, 2 * rows), lambda i: (0, 0, i)),
        ],
        out_shape=[
            *shapes,
            *shapes,
            jax.ShapeDtypeStruct((3, 4 * rows, columns), BF16),
            jax.ShapeDtypeStruct((2, dim, 4 * rows), BF16),
        ],
        scratch_shapes=[
            pltpu.VMEM((2, 2 * rows, dim), BF16),
            pltpu.VMEM((2, 2 * rows, dim), BF16),
        ],
        compiler_params=pltpu.CompilerParams(vmem_limit_bytes=VMEM_LIMIT),
        cost_estimate=pl.CostEstimate(
            flops=48 * rows * dim * columns,
            bytes_accessed=6 * dim * columns + 24 * rows * columns,
            transcendentals=4 * rows * columns,
        ),
        name="feed_forward",
    )(*normed, *cot, weights)


def mlp_grad_kernel(turned_0, turned_1, kept_0, kept_1, grad_ref):
    grad_ref[...] = (dot_nn(turned_0[0], kept_0[0]) + dot_nn(turned_1[0], kept_1[0])).astype(BF16)


def mlp_grad(turned, kept):
    _, dim, count = turned[0].shape
    columns = kept[0].shape[2]
    turned_block = pl.BlockSpec((1, dim, count), lambda i: (i // 2, 0, 0))
    kept_block = pl.BlockSpec((1, count, columns), lambda i: (i, 0, 0))
    return pl.pallas_call(
        mlp_grad_kernel,
        grid=(3,),
        in_specs=[turned_block, turned_block, kept_block, kept_block],
        out_specs=pl.BlockSpec((dim, columns), lambda i: (0, i)),
        out_shape=jax.ShapeDtypeStruct((dim, 3 * columns), BF16),
        compiler_params=pltpu.CompilerParams(vmem_limit_bytes=VMEM_LIMIT),
        cost_estimate=pl.CostEstimate(
            flops=12 * count * dim * columns,
            bytes_accessed=6 * dim * columns + 12 * count * columns,
            transcendentals=0,
        ),
        name="feed_forward_gradients",
    )(*turned, *kept)


def pack_kernel(block_ref, gate_ref, up_ref, down_ref, *refs):
    out_refs, scratch = refs[:4], refs[4]
    shard, ff = gate_ref.shape
    quarter = scratch.shape[2] // 4
    for place, ref in enumerate((gate_ref, up_ref, down_ref)):
        scratch[place, :, :ff] = ref[...].astype(F32)
        scratch[place, :, ff:] = jnp.zeros((shard, 4 * quarter - ff), F32)
    for place, out_ref in enumerate(out_refs):
        begin = pl.multiple_of((block_ref[0] ^ place) * quarter, LANES)
        for part in range(3):
            out_ref[:, part * quarter : (part + 1) * quarter] = scratch[part, :, pl.ds(begin, quarter)].astype(BF16)


def pack(block, gate, up, down_t, quarter):
    shard = gate.shape[0]
    return pl.pallas_call(
        pack_kernel,
        in_specs=[pl.BlockSpec(memory_space=pltpu.SMEM)] + [pl.BlockSpec(memory_space=pltpu.VMEM)] * 3,
        out_specs=[pl.BlockSpec(memory_space=pltpu.VMEM)] * 4,
        out_shape=[jax.ShapeDtypeStruct((shard, 3 * quarter), BF16)] * 4,
        scratch_shapes=[pltpu.VMEM((3, shard, 4 * quarter), F32)],
        compiler_params=pltpu.CompilerParams(vmem_limit_bytes=VMEM_LIMIT),
        name="pack_columns",
    )(block, gate, up, down_t)


def pick(options, index):
    value = options[0]
    for place in range(1, len(options)):
        value = jnp.where(index == place, options[place], value)
    return value


def assemble_kernel(block_ref, *refs):
    pieces, out_ref, scratch = refs[:4], refs[4], refs[5]
    shard = pieces[0].shape[0]
    values = [ref[...].astype(F32) for ref in pieces]
    for owner in range(4):
        scratch[owner * shard : (owner + 1) * shard] = pick(values, block_ref[0] ^ owner)
    out_ref[...] = scratch[...].astype(BF16)


def assemble(block, pieces):
    shard, columns = pieces[0].shape
    return pl.pallas_call(
        assemble_kernel,
        in_specs=[pl.BlockSpec(memory_space=pltpu.SMEM)] + [pl.BlockSpec(memory_space=pltpu.VMEM)] * 4,
        out_specs=pl.BlockSpec(memory_space=pltpu.VMEM),
        out_shape=jax.ShapeDtypeStruct((4 * shard, columns), BF16),
        scratch_shapes=[pltpu.VMEM((4 * shard, columns), F32)],
        compiler_params=pltpu.CompilerParams(vmem_limit_bytes=VMEM_LIMIT),
        name="assemble_rows",
    )(block, *pieces)


def cut_kernel(block_ref, value_ref, *refs):
    out_refs, scratch = refs[:4], refs[4]
    shard = out_refs[0].shape[0]
    scratch[...] = value_ref[...].astype(F32)
    values = [scratch[owner * shard : (owner + 1) * shard] for owner in range(4)]
    for place, out_ref in enumerate(out_refs):
        out_ref[...] = pick(values, block_ref[0] ^ place).astype(BF16)


def cut(block, value):
    shard, columns = value.shape[0] // 4, value.shape[1]
    return pl.pallas_call(
        cut_kernel,
        in_specs=[pl.BlockSpec(memory_space=pltpu.SMEM), pl.BlockSpec(memory_space=pltpu.VMEM)],
        out_specs=[pl.BlockSpec(memory_space=pltpu.VMEM)] * 4,
        out_shape=[jax.ShapeDtypeStruct((shard, columns), BF16)] * 4,
        scratch_shapes=[pltpu.VMEM(value.shape, F32)],
        compiler_params=pltpu.CompilerParams(vmem_limit_bytes=VMEM_LIMIT),
        name="cut_rows",
    )(block, value)


def unpack_kernel(block_ref, *refs):
    pieces, out_refs, scratch = refs[:4], refs[4:7], refs[7]
    ff = out_refs[0].shape[1]
    quarter = scratch.shape[2] // 4
    for place, ref in enumerate(pieces):
        begin = pl.multiple_of((block_ref[0] ^ place) * quarter, LANES)
        for part in range(3):
            scratch[part, :, pl.ds(begin, quarter)] = ref[:, part * quarter : (part + 1) * quarter].astype(F32)
    for part, out_ref in enumerate(out_refs):
        out_ref[...] = scratch[part, :, :ff]


def unpack(block, pieces, ff):
    shard, columns = pieces[0].shape
    return pl.pallas_call(
        unpack_kernel,
        in_specs=[pl.BlockSpec(memory_space=pltpu.SMEM)] + [pl.BlockSpec(memory_space=pltpu.VMEM)] * 4,
        out_specs=[pl.BlockSpec(memory_space=pltpu.VMEM)] * 3,
        out_shape=[jax.ShapeDtypeStruct((shard, ff), F32)] * 3,
        scratch_shapes=[pltpu.VMEM((3, shard, columns // 3 * 4), F32)],
        compiler_params=pltpu.CompilerParams(vmem_limit_bytes=VMEM_LIMIT),
        name="unpack_columns",
    )(block, *pieces)


def bit_swap(value, axis, bit=0):
    size = lax.axis_size(axis)
    return lax.ppermute(value, axis, [(i, i ^ (1 << bit)) for i in range(size)])


def jump_swap(value, axes, jump):
    return lax.ppermute(value, axes, [(i, i ^ jump) for i in range(4)])


def to_plane(value, slot):
    high, low = slot >> 1, slot & 1
    pairs = [
        (4 * y + 2 * x + c, 4 * (c ^ low) + 2 * (x ^ high) + y) for y in range(2) for x in range(2) for c in range(2)
    ]
    return lax.ppermute(value, TOKENS + ("cc",), pairs)


def from_plane(value, slot):
    high, low = slot >> 1, slot & 1
    pairs = [
        (4 * y + 2 * x + c, 4 * c + 2 * (x ^ high) + (y ^ low)) for y in range(2) for x in range(2) for c in range(2)
    ]
    return lax.ppermute(value, TOKENS + ("cc",), pairs)


def after(first, *values):
    return lax.optimization_barrier((first, *values))


def gather_four(value, axes):
    from_first = bit_swap(value, axes[0])
    return [value, bit_swap(value, axes[1]), from_first, bit_swap(from_first, axes[1])]


def gather_direct(value, axes):
    return [value] + [jump_swap(value, axes, jump) for jump in range(1, 4)]


def sum_direct(axes, own, *away):
    return [own] + [jump_swap(value, axes, jump + 1) for jump, value in enumerate(away)]


def doubling_offsets(steps):
    weight = {"cc": 1, "cx": 2, "fy": 4, "fz": 8}
    offsets = [0]
    for axis, bit in steps:
        offsets += [offset ^ (weight[axis] << bit) for offset in offsets]
    return jnp.array(offsets, jnp.int32)


def double(value, axis, bit=0):
    return jnp.concatenate([value, bit_swap(value, axis, bit)], axis=0)


def halve(value, axis, bit=0):
    middle = value.shape[0] // 2
    came = bit_swap(value[middle:], axis, bit)
    return (value[:middle].astype(F32) + came.astype(F32)).astype(BF16)


def on_device(
    hidden,
    segments,
    attn_gain,
    qkv_weight,
    qkv_bias,
    out_weight,
    mlp_gain,
    gate_weight,
    up_weight,
    down_weight,
    cotangent,
):
    seqs, rows, dim = hidden.shape
    count = seqs * rows
    shard = attn_gain.shape[0]
    world = dim // shard
    joint = qkv_weight.shape[1]
    width = joint - 2 * LANES
    ff = gate_weight.shape[1]
    block = lax.axis_index("cx") * lax.axis_size("cc") + lax.axis_index("cc")
    me = lax.axis_index(FSDP) * lax.axis_size(CTX) + block
    offset = block * rows
    block_arg = block.reshape(1).astype(jnp.int32)
    plane_arg = (lax.axis_index("cx") * 2 + lax.axis_index("fy")).reshape(1).astype(jnp.int32)
    x = hidden.reshape(count, dim)
    cot = cotangent.reshape(count, dim)

    far = [("fz", bit) for bit in reversed(range((lax.axis_size("fz")).bit_length() - 1))]
    padded = -(-(shard + 1) // 16) * 16
    small = jnp.concatenate([attn_gain, mlp_gain, qkv_bias])
    small_row = jnp.pad(small, (0, joint + width - small.shape[0]))[None]
    first = jnp.concatenate(
        [
            jnp.concatenate([qkv_weight, out_weight.T], axis=1),
            small_row,
            jnp.zeros((padded - shard - 1, joint + width), BF16),
        ],
        axis=0,
    )
    for axis, bit in far:
        first = double(first, axis, bit)

    quarter = -(-ff // (4 * TILE)) * TILE
    pieces = pack(block_arg, gate_weight, up_weight, down_weight.T, quarter)
    pieces = [to_plane(piece, slot) for slot, piece in enumerate(pieces)]
    first, *pieces = after(first, *pieces)
    mlp_shard = assemble(plane_arg, pieces)
    mlp_weights = lax.all_gather(mlp_shard, WEIGHTS, axis=0, tiled=True)

    within = jnp.arange(padded, dtype=jnp.int32)

    def arrival(steps):
        owner = me ^ doubling_offsets(steps)
        target = jnp.where(within[None, :] < shard, owner[:, None] * shard + within[None, :], -1).reshape(1, -1)
        return owner, (jnp.arange(dim, dtype=jnp.int32)[:, None] == target).astype(BF16)

    owner, order = arrival(far + [("fy", 0), ("cx", 0), ("cc", 0)])
    _, out_order = arrival(far + [("cx", 0), ("fy", 0), ("cc", 0)])
    place = jnp.where(within[None, :] == shard, owner[:, None], -1).reshape(1, -1)
    spread = (jnp.arange(world, dtype=jnp.int32)[:, None] == place).astype(BF16)

    first, order, out_order, spread = after(first, order, out_order, spread)
    w_joint, w_out = double(first[:, :joint], "fy"), double(first[:, joint:], "cx")
    w_joint, w_out = double(w_joint, "cx"), double(w_out, "fy")
    w_joint, w_out, cot_late = after(w_joint, w_out, cot)
    w_joint, w_out = (w_joint, bit_swap(w_joint, "cc")), (w_out, bit_swap(w_out, "cc"))
    cot_x, cot_y = bit_swap(cot_late, "cx"), bit_swap(cot_late, "fy")
    cot_far = [bit_swap(cot_x[:rows], "fy"), bit_swap(cot_y[rows:], "cx")]

    at_row = lax.dynamic_slice_in_dim(segments, offset, rows, axis=1)
    zeros_before = jnp.sum((segments < 1).astype(jnp.int32), axis=1, keepdims=True)
    ones_before = jnp.sum((segments < 2).astype(jnp.int32), axis=1, keepdims=True)
    start = jnp.where(at_row == 0, 0, jnp.where(at_row == 1, zeros_before, ones_before))
    position = (offset + jnp.arange(rows, dtype=jnp.int32)[None, :] - start).reshape(count)
    lane = jnp.arange(LANES, dtype=jnp.int32)
    frequency = ROPE_BASE ** (-(lane % (HD // 2)).astype(F32) * 2.0 / HD)
    angle = position.astype(F32)[:, None] * frequency[None, :]
    cosine = jnp.cos(angle)
    sine = jnp.where(lane % HD < HD // 2, -1.0, 1.0)[None, :] * jnp.sin(angle)
    start_column = jnp.broadcast_to(start.reshape(count, 1), (count, LANES))
    start_row = jnp.broadcast_to(start[:, None, :], (seqs, 8, rows))

    normed, q, kv, gain_attn, gain_mlp = prep(x, order, spread, w_joint, cosine, sine, rows)
    kv_all = gather_four(kv.reshape(seqs, rows, 2 * LANES), CTX)
    attended, resid, normed_all = [], [], []
    for seq in range(seqs):
        attended.append(attend(block_arg, q, kv_all, start_column, rows, seq))
        resid_one, normed_one = project_out(attended[seq], x, w_out, out_order, gain_mlp, rows, seq)
        resid.append(resid_one)
        normed_all.append(gather_direct(normed_one, TOKENS))

    out_parts, d_terms, kept, turned = [], [], [], []
    for seq in range(seqs):
        result = mlp(normed_all[seq], [cot, cot_x, cot_y, cot_far[seq]], mlp_weights, seq)
        out_parts.append(result[:4])
        d_terms.append(sum_direct(TOKENS, *result[4:8]))
        kept.append(result[8])
        turned.append(result[9])
    grads = mlp_grad(turned, kept)
    grads, d_terms[0], d_terms[1] = after(grads, *d_terms)
    grads = lax.psum_scatter(
        grads.reshape(world // 4, 4 * shard, 3 * quarter), WEIGHTS, scatter_dimension=0, tiled=False
    )

    d_resid, d_branch, d_attended, mlp_gain_grad = [], [], [], []
    for seq in range(seqs):
        result = project_out_back(d_terms[seq], resid[seq], cot, w_out, out_order, gain_mlp, rows, seq)
        for place, value in zip((d_resid, d_branch, d_attended, mlp_gain_grad), result):
            place.append(value)
    out_grad = dot_tn(jnp.concatenate(d_branch, axis=0), jnp.concatenate(attended, axis=0)).astype(BF16)
    out_grad = halve(out_grad, "cc")
    out_terms = [sum_direct(TOKENS, *after(d_terms[1][1], *part)[1:]) for part in out_parts]
    dq, dkv_terms = [], []
    for seq in range(seqs):
        if seq == 1:
            d_attended[1], out_grad = after(d_attended[1], out_grad)
            out_grad = halve(out_grad, "fy")
        result = attend_back(block_arg, q, kv_all, d_attended[seq], start_row, cosine, sine, rows, seq)
        dq.append(result[0])
        dkv_terms.append(sum_direct(CTX, *result[1:]))
    dq[1], out_grad = after(dq[1], out_grad)
    q_grad = dot_tn(normed, jnp.concatenate(dq, axis=0)).astype(BF16)
    q_grad = halve(q_grad, "cc")
    dkv_terms[0], q_grad, out_terms[0], out_terms[1] = after(dkv_terms[0], q_grad, *out_terms)
    q_grad, out_grad = halve(q_grad, "cx"), halve(out_grad, "cx")
    d_kv, input_grad, attn_gain_grad, bias_grad = [], [], [], []
    for seq in range(seqs):
        result = input_back(
            dq[seq], dkv_terms[seq], x, d_resid[seq], w_joint, order, gain_attn, cosine, sine, rows, seq
        )
        for place, value in zip((d_kv, input_grad, attn_gain_grad, bias_grad), result):
            place.append(value)
    pieces = cut(plane_arg, lax.optimization_barrier(grads))
    pieces = [from_plane(piece, slot) for slot, piece in enumerate(pieces)]
    d_kv[1], q_grad, out_grad, *pieces = after(d_kv[1], q_grad, out_grad, *pieces)
    gate_grad, up_grad, down_grad_t = unpack(block_arg, pieces, ff)

    output = []
    for seq in range(seqs):
        own, *away = out_terms[seq]
        output.append((resid[seq] + own + sum(term.astype(F32) for term in away)).astype(BF16))

    split_at = width + LANES
    bias_grad = jnp.sum(sum(bias_grad), axis=0)
    small_grads = jnp.concatenate(
        [
            jnp.sum(sum(attn_gain_grad), axis=0).reshape(world, -1),
            jnp.sum(sum(mlp_gain_grad), axis=0).reshape(world, -1),
            bias_grad[:split_at].reshape(world, -1),
            bias_grad[split_at:].reshape(world, -1),
        ],
        axis=1,
    ).astype(BF16)
    small_count = small_grads.shape[1]
    small_grads = jnp.pad(small_grads, ((0, 0), (0, 2 * LANES - small_count)))
    kv_grad = dot_tn(
        jnp.concatenate([normed, spread], axis=0), jnp.concatenate([*d_kv, small_grads], axis=0)
    ).astype(BF16)
    kv_grad = halve(halve(kv_grad, "cc"), "cx")
    joint_grad = halve(jnp.concatenate([q_grad, kv_grad], axis=1), "fy")
    first_sum = jnp.concatenate([joint_grad, out_grad], axis=1)
    for axis, bit in reversed(far):
        first_sum = halve(first_sum, axis, bit)
    first_sum = first_sum.astype(F32)
    qkv_sum, out_sum = first_sum[:, :joint], first_sum[:, joint:]
    small_sum = qkv_sum[shard, width : width + small_count]
    at = (shard, 2 * shard, 2 * shard + split_at // world)

    return (
        jnp.stack(output),
        jnp.stack(input_grad),
        small_sum[: at[0]],
        qkv_sum[:shard],
        small_sum[at[1] : at[2]],
        small_sum[at[2] :],
        out_sum[:shard].T,
        small_sum[at[0] : at[1]],
        gate_grad,
        up_grad,
        down_grad_t.T,
    )


def solution(mesh):
    fsdp, ctx = mesh.shape["fsdp"], mesh.shape["ctx"]
    inner = Mesh(mesh.devices.reshape(fsdp // 2, 2, 2, ctx // 2), AXES)
    tokens = P(FSDP, CTX, None)
    vector = P(AXES)
    by_row = P(AXES, None)
    by_column = P(None, AXES)
    return jax.shard_map(
        on_device,
        mesh=inner,
        in_specs=(
            tokens,
            P(FSDP, None),
            vector,
            by_row,
            vector,
            by_column,
            vector,
            by_row,
            by_row,
            by_column,
            tokens,
        ),
        out_specs=(
            tokens,
            tokens,
            vector,
            by_row,
            vector,
            vector,
            by_column,
            vector,
            by_row,
            by_row,
            by_column,
        ),
        check_vma=False,
    )
```

```python
import functools

import jax
import jax.numpy as jnp
from jax import lax
from jax.experimental import pallas as pl
from jax.experimental.pallas import tpu as pltpu
from jax.sharding import Mesh
from jax.sharding import PartitionSpec as P

HD = 64
LANES = 128
EPSILON = 1e-06
ROPE_BASE = 1000000.0
MASKED = -1e30
SCALE = HD ** (-0.5)
TILE = 256
MIB = 1 << 20
VMEM_LIMIT = 60 * MIB
F32 = jnp.float32
BF16 = jnp.bfloat16
AXES = ("fz", "fy", "cx", "cc")
FSDP = ("fz", "fy")
CTX = ("cx", "cc")
TOKENS = ("fy", "cx")
WEIGHTS = ("fz", "cc")


def dot_nn(a, b):
    return lax.dot_general(a, b, (((1,), (0,)), ((), ())), preferred_element_type=F32)


def dot_nt(a, b):
    return lax.dot_general(a, b, (((1,), (1,)), ((), ())), preferred_element_type=F32)


def dot_tn(a, b):
    return lax.dot_general(a, b, (((0,), (0,)), ((), ())), preferred_element_type=F32)


def lane_of(shape):
    return lax.broadcasted_iota(jnp.int32, shape, len(shape) - 1)


def swap_halves(block):
    lead = lane_of(block.shape) % HD < HD // 2
    return jnp.where(
        lead, pltpu.roll(block, LANES - HD // 2, 1), pltpu.roll(block, HD // 2, 1)
    )


def other_head(block):
    return jnp.concatenate([block[:, HD:], block[:, :HD]], axis=1)


def read_out(extras, first, piece, total):
    owners, columns = extras.shape
    at = lax.broadcasted_iota(jnp.int32, (columns, total), 1) % piece + first
    chosen = (lax.broadcasted_iota(jnp.int32, (columns, total), 0) == at).astype(BF16)
    spread = dot_nn(extras, chosen)
    owner = lax.broadcasted_iota(jnp.int32, (owners, total), 1) // piece
    mine = owner == lax.broadcasted_iota(jnp.int32, (owners, total), 0)
    return jnp.sum(jnp.where(mine, spread, 0.0), axis=0, keepdims=True)


def prep_kernel(
    x_ref, order_ref, spread_ref, w_low_ref, w_high_ref, cos_ref, sin_ref,
    normed_ref, q_ref, kv_ref, gain_ref, gain_mlp_ref,
):
    x = x_ref[...].astype(F32)
    dim = x.shape[1]
    width = q_ref.shape[1]
    joint = w_low_ref.shape[1]
    middle = w_low_ref.shape[0]
    owners = spread_ref.shape[0]
    extras = dot_nn(spread_ref[:, :middle], w_low_ref[:, :LANES])
    extras = (extras + dot_nn(spread_ref[:, middle:], w_high_ref[:, :LANES])).astype(BF16)
    shard = dim // owners
    gain = read_out(extras, 0, shard, dim)
    gain_ref[...] = gain
    gain_mlp_ref[...] = read_out(extras, shard, shard, dim)
    bias = read_out(extras, 2 * shard, joint // owners, joint)
    inverse = lax.rsqrt(jnp.mean(x * x, axis=-1, keepdims=True) + EPSILON)
    normed = (x * inverse * gain).astype(BF16)
    ordered = dot_nn(normed, order_ref[...]).astype(BF16)
    normed_ref[...] = ordered
    joined = dot_nn(ordered[:, :middle], w_low_ref[...])
    joined = joined + dot_nn(ordered[:, middle:], w_high_ref[...]) + bias
    cosine, sine = cos_ref[...], sin_ref[...]
    for begin in range(0, width + LANES, LANES):
        block = joined[:, begin : begin + LANES]
        turned = block * cosine + swap_halves(block) * sine
        if begin < width:
            q_ref[:, begin : begin + LANES] = (turned * SCALE).astype(BF16)
        else:
            kv_ref[:, :LANES] = turned.astype(BF16)
    kv_ref[:, LANES:] = joined[:, width + LANES :].astype(BF16)


def rows_of(rows, cols):
    return pl.BlockSpec((rows, cols), lambda i: (i, 0))


def whole(value):
    return pl.BlockSpec(value.shape, lambda i: (0,) * value.ndim)


def prep(x, order, spread, weights, cosine, sine, rows):
    count, dim = x.shape
    ordered = order.shape[1]
    joint = weights[0].shape[1]
    width = joint - 2 * LANES
    row = pl.BlockSpec((1, dim), lambda i: (0, 0))
    return pl.pallas_call(
        prep_kernel,
        grid=(count // rows,),
        in_specs=[
            rows_of(rows, dim),
            whole(order),
            whole(spread),
            whole(weights[0]),
            whole(weights[1]),
            rows_of(rows, LANES),
            rows_of(rows, LANES),
        ],
        out_specs=[rows_of(rows, ordered), rows_of(rows, width), rows_of(rows, 2 * LANES), row, row],
        out_shape=[
            jax.ShapeDtypeStruct((count, ordered), BF16),
            jax.ShapeDtypeStruct((count, width), BF16),
            jax.ShapeDtypeStruct((count, 2 * LANES), BF16),
            jax.ShapeDtypeStruct((1, dim), F32),
            jax.ShapeDtypeStruct((1, dim), F32),
        ],
        compiler_params=pltpu.CompilerParams(vmem_limit_bytes=VMEM_LIMIT),
        cost_estimate=pl.CostEstimate(
            flops=2 * count * ordered * (joint + dim), bytes_accessed=12 * MIB, transcendentals=0
        ),
        name="norm_project_rotate",
    )(x, order, spread, weights[0], weights[1], cosine, sine)


def back_in_order(value, order):
    high = value.astype(BF16)
    low = (value - high.astype(F32)).astype(BF16)
    return dot_nt(high, order) + dot_nt(low, order)


def out_kernel(attended_ref, x_ref, w_low_ref, w_high_ref, order_ref, gain_ref, resid_ref, normed_ref):
    attended = attended_ref[...]
    branch = jnp.concatenate([dot_nt(attended, w_low_ref[...]), dot_nt(attended, w_high_ref[...])], axis=1)
    resid = x_ref[...].astype(F32) + back_in_order(branch, order_ref[...])
    inverse = lax.rsqrt(jnp.mean(resid * resid, axis=-1, keepdims=True) + EPSILON)
    resid_ref[...] = resid
    normed_ref[...] = (resid * inverse * gain_ref[...]).astype(BF16)


def project_out(attended, x, weights, order, gain, rows, seq):
    dim = x.shape[1]
    count = rows
    return pl.pallas_call(
        out_kernel,
        grid=(1,),
        in_specs=[
            rows_of(rows, attended.shape[1]),
            pl.BlockSpec((rows, dim), lambda i: (seq, 0)),
            whole(weights[0]),
            whole(weights[1]),
            whole(order),
            whole(gain),
        ],
        out_specs=[rows_of(rows, dim), rows_of(rows, dim)],
        out_shape=[jax.ShapeDtypeStruct((count, dim), F32), jax.ShapeDtypeStruct((count, dim), BF16)],
        compiler_params=pltpu.CompilerParams(vmem_limit_bytes=VMEM_LIMIT),
        cost_estimate=pl.CostEstimate(flops=6 * count * dim * dim, bytes_accessed=8 * MIB, transcendentals=0),
        name="project_out_norm",
    )(attended, x, weights[0], weights[1], order, gain)


def fold_rows(value):
    return jnp.sum(value.reshape(-1, 8, value.shape[1]), axis=0)


def norm_back(values, inverse, gain, incoming):
    scaled = incoming * gain
    mean_term = jnp.mean(scaled * values, axis=-1, keepdims=True)
    return inverse * scaled - values * inverse**3 * mean_term


def total_of(own_ref, *away_refs):
    total = own_ref[...]
    for ref in away_refs:
        total = total + ref[...].astype(F32)
    return total


def out_back_kernel(
    own_ref, core_ref, x_ref, far_ref, resid_ref, cot_ref, w_low_ref, w_high_ref, order_ref, gain_ref,
    d_resid_ref, d_branch_ref, d_attended_ref, gain_grad_ref,
):
    middle = w_low_ref.shape[0]
    d_normed = total_of(own_ref, core_ref, x_ref, far_ref)
    resid = resid_ref[...]
    inverse = lax.rsqrt(jnp.mean(resid * resid, axis=-1, keepdims=True) + EPSILON)
    d_resid = cot_ref[...].astype(F32) + norm_back(resid, inverse, gain_ref[...], d_normed)
    d_resid_ref[...] = d_resid
    d_branch = dot_nn(d_resid.astype(BF16), order_ref[...]).astype(BF16)
    d_branch_ref[...] = d_branch
    d_attended = dot_nn(d_branch[:, :middle], w_low_ref[...])
    d_attended = d_attended + dot_nn(d_branch[:, middle:], w_high_ref[...])
    d_attended_ref[...] = d_attended.astype(BF16)
    gain_grad_ref[...] = fold_rows(d_normed * resid * inverse)


def project_out_back(terms, resid, cot, weights, order, gain, rows, seq):
    count, dim = resid.shape
    ordered = order.shape[1]
    width = dim
    return pl.pallas_call(
        out_back_kernel,
        grid=(1,),
        in_specs=[
            rows_of(rows, dim),
            rows_of(rows, dim),
            rows_of(rows, dim),
            rows_of(rows, dim),
            rows_of(rows, dim),
            pl.BlockSpec((rows, dim), lambda i: (seq, 0)),
            whole(weights[0]),
            whole(weights[1]),
            whole(order),
            whole(gain),
        ],
        out_specs=[
            rows_of(rows, dim),
            rows_of(rows, ordered),
            rows_of(rows, width),
            pl.BlockSpec((8, dim), lambda i: (0, 0)),
        ],
        out_shape=[
            jax.ShapeDtypeStruct((count, dim), F32),
            jax.ShapeDtypeStruct((count, ordered), BF16),
            jax.ShapeDtypeStruct((count, width), BF16),
            jax.ShapeDtypeStruct((8, dim), F32),
        ],
        compiler_params=pltpu.CompilerParams(vmem_limit_bytes=VMEM_LIMIT),
        cost_estimate=pl.CostEstimate(flops=4 * count * dim * dim, bytes_accessed=12 * MIB, transcendentals=0),
        name="norm_back_project",
    )(*terms, resid, cot, weights[0], weights[1], order, gain)


def input_back_kernel(
    dq_ref, own_ref, core_ref, from_x_ref, far_ref, x_ref, d_resid_ref, w_low_ref, w_high_ref, order_ref,
    gain_ref, cos_ref, sin_ref, d_kv_ref, input_grad_ref, gain_grad_ref, bias_grad_ref,
):
    dkv = total_of(own_ref, core_ref, from_x_ref, far_ref)
    dk = dkv[:, :LANES]
    dk = dk * cos_ref[...] - swap_halves(dk) * sin_ref[...]
    d_kv = jnp.concatenate([dk.astype(BF16), dkv[:, LANES:].astype(BF16)], axis=1)
    d_kv_ref[...] = d_kv
    d_joined = jnp.concatenate([dq_ref[...], d_kv], axis=1)
    d_normed = jnp.concatenate(
        [dot_nt(d_joined, w_low_ref[...]), dot_nt(d_joined, w_high_ref[...])], axis=1
    )
    d_normed = back_in_order(d_normed, order_ref[...])
    x = x_ref[...].astype(F32)
    inverse = lax.rsqrt(jnp.mean(x * x, axis=-1, keepdims=True) + EPSILON)
    input_grad_ref[...] = (d_resid_ref[...] + norm_back(x, inverse, gain_ref[...], d_normed)).astype(BF16)
    gain_grad_ref[...] = fold_rows(d_normed * x * inverse)
    bias_grad_ref[...] = fold_rows(d_joined.astype(F32))


def input_back(dq, terms, x, d_resid, weights, order, gain, cosine, sine, rows, seq):
    count, dim = d_resid.shape
    width = dq.shape[1]
    joint = width + 2 * LANES
    return pl.pallas_call(
        input_back_kernel,
        grid=(1,),
        in_specs=[
            rows_of(rows, width),
            rows_of(rows, 2 * LANES),
            rows_of(rows, 2 * LANES),
            rows_of(rows, 2 * LANES),
            rows_of(rows, 2 * LANES),
            pl.BlockSpec((rows, dim), lambda i: (seq, 0)),
            rows_of(rows, dim),
            whole(weights[0]),
            whole(weights[1]),
            whole(order),
            whole(gain),
            pl.BlockSpec((rows, LANES), lambda i: (seq, 0)),
            pl.BlockSpec((rows, LANES), lambda i: (seq, 0)),
        ],
        out_specs=[
            rows_of(rows, 2 * LANES),
            rows_of(rows, dim),
            pl.BlockSpec((8, dim), lambda i: (0, 0)),
            pl.BlockSpec((8, joint), lambda i: (0, 0)),
        ],
        out_shape=[
            jax.ShapeDtypeStruct((count, 2 * LANES), BF16),
            jax.ShapeDtypeStruct((count, dim), BF16),
            jax.ShapeDtypeStruct((8, dim), F32),
            jax.ShapeDtypeStruct((8, joint), F32),
        ],
        compiler_params=pltpu.CompilerParams(vmem_limit_bytes=VMEM_LIMIT),
        cost_estimate=pl.CostEstimate(flops=6 * count * dim * joint, bytes_accessed=12 * MIB, transcendentals=0),
        name="input_gradient",
    )(dq, *terms, x, d_resid, weights[0], weights[1], order, gain, cosine, sine)


def seq_rows(seq, rows, cols):
    return pl.BlockSpec((rows, cols), lambda i: (seq, 0))


def piece_of(seq, rows):
    return pl.BlockSpec((1, rows, 2 * LANES), lambda i: (seq, 0, 0))


def keys_and_values(piece_refs):
    joint = jnp.concatenate([ref[0] for ref in piece_refs], axis=0)
    key, value = joint[:, :LANES], joint[:, LANES:]
    return (key, other_head(key)), (value, other_head(value))


def attend_kernel(block_ref, q_ref, kv_0, kv_1, kv_2, kv_3, start_ref, out_ref):
    rows, width = q_ref.shape
    length = 4 * rows
    heads = width // HD
    group = heads // 2
    keys, values = keys_and_values((kv_0, kv_1, kv_2, kv_3))
    upper_key = lane_of((length, LANES)) >= HD
    upper = lane_of((rows, LANES)) >= HD
    query_at = block_ref[0] * rows + lax.broadcasted_iota(jnp.int32, (rows, length), 0)
    key_at = jnp.concatenate(
        [
            (block_ref[0] ^ place) * rows + lax.broadcasted_iota(jnp.int32, (rows, rows), 1)
            for place in range(4)
        ],
        axis=1,
    )
    allowed = (key_at <= query_at) & (key_at >= start_ref[:, :1])
    bias = jnp.where(allowed, 0.0, MASKED)
    one = jnp.ones((), BF16)
    for pair in range(heads // 2):
        at = slice(pair * LANES, (pair + 1) * LANES)
        both = q_ref[:, at]
        parts = []
        for place in range(2):
            owner = (2 * pair + place) // group
            moved = int(owner != place)
            side = upper if place else ~upper
            side_key = upper_key if place else ~upper_key
            query = jnp.where(side, both, jnp.zeros_like(both))
            score = dot_nt(query, keys[moved]) + bias
            top = jnp.max(score, axis=1, keepdims=True)
            weight = jnp.exp(score - top).astype(BF16)
            mixed = dot_nn(weight, jnp.where(side_key, values[moved], one))
            parts.append(mixed / pltpu.roll(mixed, HD, 1))
        out_ref[:, at] = jnp.where(upper, parts[1], parts[0]).astype(BF16)


def attend(block, q, kv_pieces, start, rows, seq):
    width = q.shape[1]
    heads = width // HD
    return pl.pallas_call(
        attend_kernel,
        grid=(1,),
        in_specs=[
            pl.BlockSpec(memory_space=pltpu.SMEM),
            seq_rows(seq, rows, width),
            *[piece_of(seq, rows)] * 4,
            seq_rows(seq, rows, LANES),
        ],
        out_specs=seq_rows(0, rows, width),
        out_shape=jax.ShapeDtypeStruct((rows, width), BF16),
        compiler_params=pltpu.CompilerParams(vmem_limit_bytes=VMEM_LIMIT),
        cost_estimate=pl.CostEstimate(
            flops=32 * rows * rows * LANES * heads,
            bytes_accessed=4 * rows * width,
            transcendentals=4 * rows * rows * heads,
        ),
        name="attention_forward",
    )(block, q, *kv_pieces, start)


def attend_back_kernel(
    block_ref, q_ref, kv_0, kv_1, kv_2, kv_3, back_ref, start_ref, cos_ref, sin_ref,
    dq_ref, own_ref, core_ref, x_ref, far_ref, dk_sum, dv_sum,
):
    rows, width = q_ref.shape
    length = 4 * rows
    heads = width // HD
    group = heads // 2
    keys, values = keys_and_values((kv_0, kv_1, kv_2, kv_3))
    key_t = keys[0].astype(F32).T.astype(BF16)
    keys_t = (key_t, jnp.concatenate([key_t[HD:], key_t[:HD]], axis=0))
    upper = lane_of((rows, LANES)) >= HD
    upper_t = lax.broadcasted_iota(jnp.int32, (LANES, rows), 0) >= HD
    query_at = block_ref[0] * rows + lax.broadcasted_iota(jnp.int32, (length, rows), 1)
    key_at = jnp.concatenate(
        [
            (block_ref[0] ^ place) * rows + lax.broadcasted_iota(jnp.int32, (rows, rows), 0)
            for place in range(4)
        ],
        axis=0,
    )
    allowed = (key_at <= query_at) & (key_at >= start_ref[0, :1, :])
    bias = jnp.where(allowed, 0.0, MASKED)
    cosine, sine = cos_ref[...], sin_ref[...]
    dk_sum[...] = jnp.zeros_like(dk_sum)
    dv_sum[...] = jnp.zeros_like(dv_sum)
    for pair in range(heads // 2):
        at = slice(pair * LANES, (pair + 1) * LANES)
        both = q_ref[:, at]
        back_both = back_ref[:, at]
        parts = []
        for place in range(2):
            owner = (2 * pair + place) // group
            moved = int(owner != place)
            side = upper if place else ~upper
            query = jnp.where(side, both, jnp.zeros_like(both))
            back = jnp.where(side, back_both, jnp.zeros_like(back_both))
            score = dot_nt(keys[moved], query) + bias
            weight = jnp.exp(score - jnp.max(score, axis=0, keepdims=True))
            prob = weight * (1.0 / jnp.sum(weight, axis=0, keepdims=True))
            dv_sum[owner] += dot_nn(prob.astype(BF16), back)
            d_prob = dot_nt(values[moved], back)
            level = jnp.sum(prob * d_prob, axis=0, keepdims=True)
            d_score = (prob * (d_prob - level)).astype(BF16)
            dk_sum[owner] += dot_nn(d_score, query)
            parts.append(dot_nn(keys_t[moved], d_score))
        d_query = jnp.where(upper_t, parts[1], parts[0]).T * SCALE
        dq_ref[:, at] = (d_query * cosine - swap_halves(d_query) * sine).astype(BF16)
    lower_key = lane_of((length, LANES)) < HD
    for total, begin in ((dk_sum, 0), (dv_sum, LANES)):
        first, second = total[0], total[1]
        first = first + pltpu.roll(first, HD, 1)
        second = second + pltpu.roll(second, HD, 1)
        both = jnp.where(lower_key, first, second)
        cols = slice(begin, begin + LANES)
        own_ref[:, cols] = both[:rows]
        for place, ref in enumerate((core_ref, x_ref, far_ref)):
            ref[:, cols] = both[(place + 1) * rows : (place + 2) * rows].astype(BF16)


def parts_of(rows, cols):
    shapes = [jax.ShapeDtypeStruct((rows, cols), F32)] + [jax.ShapeDtypeStruct((rows, cols), BF16)] * 3
    return [seq_rows(0, rows, cols)] * 4, shapes


def attend_back(block, q, kv_pieces, back, start, cosine, sine, rows, seq):
    width = q.shape[1]
    length = 4 * rows
    heads = width // HD
    specs, shapes = parts_of(rows, 2 * LANES)
    return pl.pallas_call(
        attend_back_kernel,
        grid=(1,),
        in_specs=[
            pl.BlockSpec(memory_space=pltpu.SMEM),
            seq_rows(seq, rows, width),
            *[piece_of(seq, rows)] * 4,
            seq_rows(0, rows, width),
            pl.BlockSpec((1, 8, rows), lambda i: (seq, 0, 0)),
            seq_rows(seq, rows, LANES),
            seq_rows(seq, rows, LANES),
        ],
        out_specs=[seq_rows(0, rows, width), *specs],
        out_shape=[jax.ShapeDtypeStruct((rows, width), BF16), *shapes],
        scratch_shapes=[
            pltpu.VMEM((2, length, LANES), F32),
            pltpu.VMEM((2, length, LANES), F32),
        ],
        compiler_params=pltpu.CompilerParams(vmem_limit_bytes=VMEM_LIMIT),
        cost_estimate=pl.CostEstimate(
            flops=80 * rows * rows * LANES * heads,
            bytes_accessed=8 * rows * width,
            transcendentals=4 * rows * rows * heads,
        ),
        name="attention_backward",
    )(block, q, *kv_pieces, back, start, cosine, sine)


def mlp_kernel(
    n_0, n_1, n_2, n_3, c_0, c_1, c_2, c_3, w_ref,
    own_ref, out_1, out_2, out_3, d_own_ref, d_1, d_2, d_3, kept_ref, turned_ref,
    normed_all, cot_all,
):
    step = pl.program_id(0)
    rows = own_ref.shape[0]
    columns = w_ref.shape[1] // 3

    @pl.when(step == 0)
    def _():
        for place, (n_ref, c_ref) in enumerate(zip((n_0, n_1, n_2, n_3), (c_0, c_1, c_2, c_3))):
            normed_all[place // 2, (place % 2) * rows : (place % 2 + 1) * rows] = n_ref[...]
            cot_all[place // 2, (place % 2) * rows : (place % 2 + 1) * rows] = c_ref[...]

    normed, cot = normed_all[step], cot_all[step]
    for begin in range(0, columns, TILE):
        at = slice(begin, begin + TILE)
        gate = dot_nn(normed, w_ref[:, begin : begin + TILE])
        up = dot_nn(normed, w_ref[:, columns + begin : columns + begin + TILE])
        d_act = dot_nn(cot, w_ref[:, 2 * columns + begin : 2 * columns + begin + TILE])
        sigmoid = 0.5 * jnp.tanh(0.5 * gate) + 0.5
        swish = gate * sigmoid
        kept_ref[0, :, at] = (d_act * up * (sigmoid + swish * (1.0 - sigmoid))).astype(BF16)
        kept_ref[1, :, at] = (d_act * swish).astype(BF16)
        kept_ref[2, :, at] = (swish * up).astype(BF16)
    turned_ref[0] = normed.T
    turned_ref[1] = cot.T
    out = dot_nt(kept_ref[2], w_ref[:, 2 * columns :])
    d_normed = dot_nt(kept_ref[0], w_ref[:, :columns]) + dot_nt(kept_ref[1], w_ref[:, columns : 2 * columns])

    @pl.when(step == 0)
    def _():
        own_ref[...] = out[:rows]
        out_1[...] = out[rows:].astype(BF16)
        d_own_ref[...] = d_normed[:rows]
        d_1[...] = d_normed[rows:].astype(BF16)

    @pl.when(step == 1)
    def _():
        out_2[...] = out[:rows].astype(BF16)
        out_3[...] = out[rows:].astype(BF16)
        d_2[...] = d_normed[:rows].astype(BF16)
        d_3[...] = d_normed[rows:].astype(BF16)


def mlp(normed, cot, weights, seq):
    rows, dim = normed[0].shape
    columns = weights.shape[1] // 3
    specs, shapes = parts_of(rows, dim)
    once = lambda at: pl.BlockSpec((rows, dim), lambda i: (at, 0), pipeline_mode=pl.Buffered(1))
    return pl.pallas_call(
        mlp_kernel,
        grid=(2,),
        in_specs=[
            *[once(0)] * 4,
            *[once(seq)] * 3,
            once(0),
            pl.BlockSpec(weights.shape, lambda i: (0, 0), pipeline_mode=pl.Buffered(1)),
        ],
        out_specs=[
            *specs,
            *specs,
            pl.BlockSpec((3, 2 * rows, columns), lambda i: (0, i, 0)),
            pl.BlockSpec((2, dim, 2 * rows), lambda i: (0, 0, i)),
        ],
        out_shape=[
            *shapes,
            *shapes,
            jax.ShapeDtypeStruct((3, 4 * rows, columns), BF16),
            jax.ShapeDtypeStruct((2, dim, 4 * rows), BF16),
        ],
        scratch_shapes=[
            pltpu.VMEM((2, 2 * rows, dim), BF16),
            pltpu.VMEM((2, 2 * rows, dim), BF16),
        ],
        compiler_params=pltpu.CompilerParams(vmem_limit_bytes=VMEM_LIMIT),
        cost_estimate=pl.CostEstimate(
            flops=48 * rows * dim * columns,
            bytes_accessed=6 * dim * columns + 24 * rows * columns,
            transcendentals=4 * rows * columns,
        ),
        name="feed_forward",
    )(*normed, *cot, weights)


def mlp_grad_kernel(turned_0, turned_1, kept_0, kept_1, grad_ref):
    grad_ref[...] = (dot_nn(turned_0[0], kept_0[0]) + dot_nn(turned_1[0], kept_1[0])).astype(BF16)


def mlp_grad(turned, kept):
    _, dim, count = turned[0].shape
    columns = kept[0].shape[2]
    turned_block = pl.BlockSpec((1, dim, count), lambda i: (i // 2, 0, 0))
    kept_block = pl.BlockSpec((1, count, columns), lambda i: (i, 0, 0))
    return pl.pallas_call(
        mlp_grad_kernel,
        grid=(3,),
        in_specs=[turned_block, turned_block, kept_block, kept_block],
        out_specs=pl.BlockSpec((dim, columns), lambda i: (0, i)),
        out_shape=jax.ShapeDtypeStruct((dim, 3 * columns), BF16),
        compiler_params=pltpu.CompilerParams(vmem_limit_bytes=VMEM_LIMIT),
        cost_estimate=pl.CostEstimate(
            flops=12 * count * dim * columns,
            bytes_accessed=6 * dim * columns + 12 * count * columns,
            transcendentals=0,
        ),
        name="feed_forward_gradients",
    )(*turned, *kept)


def pack_kernel(block_ref, gate_ref, up_ref, down_ref, *refs):
    out_refs, scratch = refs[:4], refs[4]
    shard, ff = gate_ref.shape
    quarter = scratch.shape[2] // 4
    for place, ref in enumerate((gate_ref, up_ref, down_ref)):
        scratch[place, :, :ff] = ref[...].astype(F32)
        scratch[place, :, ff:] = jnp.zeros((shard, 4 * quarter - ff), F32)
    for place, out_ref in enumerate(out_refs):
        begin = pl.multiple_of((block_ref[0] ^ place) * quarter, LANES)
        for part in range(3):
            out_ref[:, part * quarter : (part + 1) * quarter] = scratch[part, :, pl.ds(begin, quarter)].astype(BF16)


def pack(block, gate, up, down_t, quarter):
    shard = gate.shape[0]
    return pl.pallas_call(
        pack_kernel,
        in_specs=[pl.BlockSpec(memory_space=pltpu.SMEM)] + [pl.BlockSpec(memory_space=pltpu.VMEM)] * 3,
        out_specs=[pl.BlockSpec(memory_space=pltpu.VMEM)] * 4,
        out_shape=[jax.ShapeDtypeStruct((shard, 3 * quarter), BF16)] * 4,
        scratch_shapes=[pltpu.VMEM((3, shard, 4 * quarter), F32)],
        compiler_params=pltpu.CompilerParams(vmem_limit_bytes=VMEM_LIMIT),
        name="pack_columns",
    )(block, gate, up, down_t)


def pick(options, index):
    value = options[0]
    for place in range(1, len(options)):
        value = jnp.where(index == place, options[place], value)
    return value


def assemble_kernel(block_ref, *refs):
    pieces, out_ref, scratch = refs[:4], refs[4], refs[5]
    shard = pieces[0].shape[0]
    values = [ref[...].astype(F32) for ref in pieces]
    for owner in range(4):
        scratch[owner * shard : (owner + 1) * shard] = pick(values, block_ref[0] ^ owner)
    out_ref[...] = scratch[...].astype(BF16)


def assemble(block, pieces):
    shard, columns = pieces[0].shape
    return pl.pallas_call(
        assemble_kernel,
        in_specs=[pl.BlockSpec(memory_space=pltpu.SMEM)] + [pl.BlockSpec(memory_space=pltpu.VMEM)] * 4,
        out_specs=pl.BlockSpec(memory_space=pltpu.VMEM),
        out_shape=jax.ShapeDtypeStruct((4 * shard, columns), BF16),
        scratch_shapes=[pltpu.VMEM((4 * shard, columns), F32)],
        compiler_params=pltpu.CompilerParams(vmem_limit_bytes=VMEM_LIMIT),
        name="assemble_rows",
    )(block, *pieces)


def cut_kernel(block_ref, value_ref, *refs):
    out_refs, scratch = refs[:4], refs[4]
    shard = out_refs[0].shape[0]
    scratch[...] = value_ref[...].astype(F32)
    values = [scratch[owner * shard : (owner + 1) * shard] for owner in range(4)]
    for place, out_ref in enumerate(out_refs):
        out_ref[...] = pick(values, block_ref[0] ^ place).astype(BF16)


def cut(block, value):
    shard, columns = value.shape[0] // 4, value.shape[1]
    return pl.pallas_call(
        cut_kernel,
        in_specs=[pl.BlockSpec(memory_space=pltpu.SMEM), pl.BlockSpec(memory_space=pltpu.VMEM)],
        out_specs=[pl.BlockSpec(memory_space=pltpu.VMEM)] * 4,
        out_shape=[jax.ShapeDtypeStruct((shard, columns), BF16)] * 4,
        scratch_shapes=[pltpu.VMEM(value.shape, F32)],
        compiler_params=pltpu.CompilerParams(vmem_limit_bytes=VMEM_LIMIT),
        name="cut_rows",
    )(block, value)


def unpack_kernel(block_ref, *refs):
    pieces, out_refs, scratch = refs[:4], refs[4:7], refs[7]
    ff = out_refs[0].shape[1]
    quarter = scratch.shape[2] // 4
    for place, ref in enumerate(pieces):
        begin = pl.multiple_of((block_ref[0] ^ place) * quarter, LANES)
        for part in range(3):
            scratch[part, :, pl.ds(begin, quarter)] = ref[:, part * quarter : (part + 1) * quarter].astype(F32)
    for part, out_ref in enumerate(out_refs):
        out_ref[...] = scratch[part, :, :ff]


def unpack(block, pieces, ff):
    shard, columns = pieces[0].shape
    return pl.pallas_call(
        unpack_kernel,
        in_specs=[pl.BlockSpec(memory_space=pltpu.SMEM)] + [pl.BlockSpec(memory_space=pltpu.VMEM)] * 4,
        out_specs=[pl.BlockSpec(memory_space=pltpu.VMEM)] * 3,
        out_shape=[jax.ShapeDtypeStruct((shard, ff), F32)] * 3,
        scratch_shapes=[pltpu.VMEM((3, shard, columns // 3 * 4), F32)],
        compiler_params=pltpu.CompilerParams(vmem_limit_bytes=VMEM_LIMIT),
        name="unpack_columns",
    )(block, *pieces)


def bit_swap(value, axis, bit=0):
    size = lax.axis_size(axis)
    return lax.ppermute(value, axis, [(i, i ^ (1 << bit)) for i in range(size)])


def jump_swap(value, axes, jump):
    return lax.ppermute(value, axes, [(i, i ^ jump) for i in range(4)])


def to_plane(value, slot):
    high, low = slot >> 1, slot & 1
    pairs = [
        (4 * y + 2 * x + c, 4 * (c ^ low) + 2 * (x ^ high) + y) for y in range(2) for x in range(2) for c in range(2)
    ]
    return lax.ppermute(value, TOKENS + ("cc",), pairs)


def from_plane(value, slot):
    high, low = slot >> 1, slot & 1
    pairs = [
        (4 * y + 2 * x + c, 4 * c + 2 * (x ^ high) + (y ^ low)) for y in range(2) for x in range(2) for c in range(2)
    ]
    return lax.ppermute(value, TOKENS + ("cc",), pairs)


def after(first, *values):
    return lax.optimization_barrier((first, *values))


def gather_four(value, axes):
    from_first = bit_swap(value, axes[0])
    return [value, bit_swap(value, axes[1]), from_first, bit_swap(from_first, axes[1])]


def gather_direct(value, axes):
    return [value] + [jump_swap(value, axes, jump) for jump in range(1, 4)]


def sum_direct(axes, own, *away):
    return [own] + [jump_swap(value, axes, jump + 1) for jump, value in enumerate(away)]


def doubling_offsets(steps):
    weight = {"cc": 1, "cx": 2, "fy": 4, "fz": 8}
    offsets = [0]
    for axis, bit in steps:
        offsets += [offset ^ (weight[axis] << bit) for offset in offsets]
    return jnp.array(offsets, jnp.int32)


def double(value, axis, bit=0):
    return jnp.concatenate([value, bit_swap(value, axis, bit)], axis=0)


def halve(value, axis, bit=0):
    middle = value.shape[0] // 2
    came = bit_swap(value[middle:], axis, bit)
    return (value[:middle].astype(F32) + came.astype(F32)).astype(BF16)


def on_device(
    hidden,
    segments,
    attn_gain,
    qkv_weight,
    qkv_bias,
    out_weight,
    mlp_gain,
    gate_weight,
    up_weight,
    down_weight,
    cotangent,
):
    seqs, rows, dim = hidden.shape
    count = seqs * rows
    shard = attn_gain.shape[0]
    world = dim // shard
    joint = qkv_weight.shape[1]
    width = joint - 2 * LANES
    ff = gate_weight.shape[1]
    block = lax.axis_index("cx") * lax.axis_size("cc") + lax.axis_index("cc")
    me = lax.axis_index(FSDP) * lax.axis_size(CTX) + block
    offset = block * rows
    block_arg = block.reshape(1).astype(jnp.int32)
    plane_arg = (lax.axis_index("cx") * 2 + lax.axis_index("fy")).reshape(1).astype(jnp.int32)
    x = hidden.reshape(count, dim)
    cot = cotangent.reshape(count, dim)

    cot_x, cot_y = bit_swap(cot, "cx"), bit_swap(cot, "fy")

    far = [("fz", bit) for bit in reversed(range((lax.axis_size("fz")).bit_length() - 1))]
    padded = -(-(shard + 1) // 16) * 16
    small = jnp.concatenate([attn_gain, mlp_gain, qkv_bias])
    small_row = jnp.pad(small, (0, joint + width - small.shape[0]))[None]
    first = jnp.concatenate(
        [
            jnp.concatenate([qkv_weight, out_weight.T], axis=1),
            small_row,
            jnp.zeros((padded - shard - 1, joint + width), BF16),
        ],
        axis=0,
    )
    for axis, bit in far:
        first = double(first, axis, bit)

    quarter = -(-ff // (4 * TILE)) * TILE
    pieces = pack(block_arg, gate_weight, up_weight, down_weight.T, quarter)
    pieces = [to_plane(piece, slot) for slot, piece in enumerate(pieces)]
    within = jnp.arange(padded, dtype=jnp.int32)

    def arrival(steps):
        owner = me ^ doubling_offsets(steps)
        target = jnp.where(within[None, :] < shard, owner[:, None] * shard + within[None, :], -1).reshape(1, -1)
        return owner, (jnp.arange(dim, dtype=jnp.int32)[:, None] == target).astype(BF16)

    owner, order = arrival(far + [("fy", 0), ("cx", 0), ("cc", 0)])
    _, out_order = arrival(far + [("cx", 0), ("fy", 0), ("cc", 0)])
    place = jnp.where(within[None, :] == shard, owner[:, None], -1).reshape(1, -1)
    spread = (jnp.arange(world, dtype=jnp.int32)[:, None] == place).astype(BF16)

    at_row = lax.dynamic_slice_in_dim(segments, offset, rows, axis=1)
    zeros_before = jnp.sum((segments < 1).astype(jnp.int32), axis=1, keepdims=True)
    ones_before = jnp.sum((segments < 2).astype(jnp.int32), axis=1, keepdims=True)
    start = jnp.where(at_row == 0, 0, jnp.where(at_row == 1, zeros_before, ones_before))
    position = (offset + jnp.arange(rows, dtype=jnp.int32)[None, :] - start).reshape(count)
    lane = jnp.arange(LANES, dtype=jnp.int32)
    frequency = ROPE_BASE ** (-(lane % (HD // 2)).astype(F32) * 2.0 / HD)
    angle = position.astype(F32)[:, None] * frequency[None, :]
    cosine = jnp.cos(angle)
    sine = jnp.where(lane % HD < HD // 2, -1.0, 1.0)[None, :] * jnp.sin(angle)
    start_column = jnp.broadcast_to(start.reshape(count, 1), (count, LANES))
    start_row = jnp.broadcast_to(start[:, None, :], (seqs, 8, rows))

    w_joint, w_out = double(first[:, :joint], "fy"), double(first[:, joint:], "cx")
    w_joint, w_out, cot_x, cot_y, order, out_order, spread, cosine, sine, start_column, *pieces = after(
        w_joint, w_out, cot_x, cot_y, order, out_order, spread, cosine, sine, start_column, *pieces
    )
    mlp_shard = assemble(plane_arg, pieces)
    mlp_weights = lax.all_gather(mlp_shard, WEIGHTS, axis=0, tiled=True)
    w_joint, w_out = double(w_joint, "cx"), double(w_out, "fy")
    w_joint, w_out = (w_joint, bit_swap(w_joint, "cc")), (w_out, bit_swap(w_out, "cc"))

    normed, q, kv, gain_attn, gain_mlp = prep(x, order, spread, w_joint, cosine, sine, rows)
    kv_all = gather_four(kv.reshape(seqs, rows, 2 * LANES), CTX)
    kv_all[3], far_0, far_1 = after(kv_all[3], cot_x[:rows], cot_y[rows:])
    cot_far = [bit_swap(far_0, "fy"), bit_swap(far_1, "cx")]
    attended, resid, normed_all = [], [], []
    for seq in range(seqs):
        turn = block_arg if seq == 0 else after(attended[0], block_arg)[1]
        attended.append(attend(turn, q, kv_all, start_column, rows, seq))
        if seq == 1:
            attended[1], *cot_far = after(attended[1], *cot_far)
        resid_one, normed_one = project_out(attended[seq], x, w_out, out_order, gain_mlp, rows, seq)
        resid.append(resid_one)
        normed_all.append(gather_direct(normed_one, TOKENS))

    out_parts, d_terms, kept, turned = [], [], [], []
    for seq in range(seqs):
        if seq == 1:
            out_parts[0], normed_all[1] = lax.optimization_barrier((out_parts[0], normed_all[1]))
        result = mlp(normed_all[seq], [cot, cot_x, cot_y, cot_far[seq]], mlp_weights, seq)
        out_parts.append(result[:4])
        d_terms.append(sum_direct(TOKENS, *result[4:8]))
        kept.append(result[8])
        turned.append(result[9])
    turned[1], *d_terms[0] = after(turned[1], *d_terms[0])
    grads = mlp_grad(turned, kept)
    grads, d_terms[0], d_terms[1] = after(grads, *d_terms)
    grads = lax.psum_scatter(
        grads.reshape(world // 4, 4 * shard, 3 * quarter), WEIGHTS, scatter_dimension=0, tiled=False
    )

    d_resid, d_branch, d_attended, mlp_gain_grad = [], [], [], []
    for seq in range(seqs):
        if seq == 1:
            d_resid[0], d_terms[1][0] = after(d_resid[0], d_terms[1][0])
        result = project_out_back(d_terms[seq], resid[seq], cot, w_out, out_order, gain_mlp, rows, seq)
        for place, value in zip((d_resid, d_branch, d_attended, mlp_gain_grad), result):
            place.append(value)
    out_grad = dot_tn(jnp.concatenate(d_branch, axis=0), jnp.concatenate(attended, axis=0)).astype(BF16)
    out_grad = halve(out_grad, "cc")
    out_terms = [sum_direct(TOKENS, *after(d_terms[1][1], *part)[1:]) for part in out_parts]
    d_attended[0], out_terms[0] = after(d_attended[0], out_terms[0])
    dq, dkv_terms = [], []
    for seq in range(seqs):
        if seq == 1:
            dq[0], d_attended[1], out_grad, out_terms[1] = after(dq[0], d_attended[1], out_grad, out_terms[1])
            out_grad = halve(out_grad, "fy")
        result = attend_back(block_arg, q, kv_all, d_attended[seq], start_row, cosine, sine, rows, seq)
        dq.append(result[0])
        dkv_terms.append(sum_direct(CTX, *result[1:]))
    dq[1], out_grad, *dkv_terms[0] = after(dq[1], out_grad, *dkv_terms[0])
    q_grad = dot_tn(normed, jnp.concatenate(dq, axis=0)).astype(BF16)
    q_grad = halve(q_grad, "cc")
    d_kv, input_grad, attn_gain_grad, bias_grad = [], [], [], []
    for seq in range(seqs):
        if seq == 1:
            q_grad, *dkv_terms[1] = after(q_grad, *dkv_terms[1])
            q_grad, out_grad = halve(q_grad, "cx"), halve(out_grad, "cx")
        result = input_back(
            dq[seq], dkv_terms[seq], x, d_resid[seq], w_joint, order, gain_attn, cosine, sine, rows, seq
        )
        for place, value in zip((d_kv, input_grad, attn_gain_grad, bias_grad), result):
            place.append(value)
    d_kv[1], q_grad, out_grad = after(d_kv[1], q_grad, out_grad)
    pieces = cut(plane_arg, lax.optimization_barrier(grads))
    pieces = [from_plane(piece, slot) for slot, piece in enumerate(pieces)]

    output = []
    for seq in range(seqs):
        own, *away = out_terms[seq]
        output.append((resid[seq] + own + sum(term.astype(F32) for term in away)).astype(BF16))

    split_at = width + LANES
    bias_grad = jnp.sum(sum(bias_grad), axis=0)
    small_grads = jnp.concatenate(
        [
            jnp.sum(sum(attn_gain_grad), axis=0).reshape(world, -1),
            jnp.sum(sum(mlp_gain_grad), axis=0).reshape(world, -1),
            bias_grad[:split_at].reshape(world, -1),
            bias_grad[split_at:].reshape(world, -1),
        ],
        axis=1,
    ).astype(BF16)
    small_count = small_grads.shape[1]
    small_grads = jnp.pad(small_grads, ((0, 0), (0, 2 * LANES - small_count)))
    kv_grad = dot_tn(
        jnp.concatenate([normed, spread], axis=0), jnp.concatenate([*d_kv, small_grads], axis=0)
    ).astype(BF16)
    kv_grad = halve(halve(kv_grad, "cc"), "cx")
    joint_grad = halve(jnp.concatenate([q_grad, kv_grad], axis=1), "fy")
    joint_grad, *pieces = after(joint_grad, *pieces)
    gate_grad, up_grad, down_grad_t = unpack(block_arg, pieces, ff)
    first_sum = jnp.concatenate([joint_grad, out_grad], axis=1)
    for axis, bit in reversed(far):
        first_sum = halve(first_sum, axis, bit)
    first_sum = first_sum.astype(F32)
    qkv_sum, out_sum = first_sum[:, :joint], first_sum[:, joint:]
    small_sum = qkv_sum[shard, width : width + small_count]
    at = (shard, 2 * shard, 2 * shard + split_at // world)

    return (
        jnp.stack(output),
        jnp.stack(input_grad),
        small_sum[: at[0]],
        qkv_sum[:shard],
        small_sum[at[1] : at[2]],
        small_sum[at[2] :],
        out_sum[:shard].T,
        small_sum[at[0] : at[1]],
        gate_grad,
        up_grad,
        down_grad_t.T,
    )


def solution(mesh):
    fsdp, ctx = mesh.shape["fsdp"], mesh.shape["ctx"]
    inner = Mesh(mesh.devices.reshape(fsdp // 2, 2, 2, ctx // 2), AXES)
    tokens = P(FSDP, CTX, None)
    vector = P(AXES)
    by_row = P(AXES, None)
    by_column = P(None, AXES)
    return jax.shard_map(
        on_device,
        mesh=inner,
        in_specs=(
            tokens,
            P(FSDP, None),
            vector,
            by_row,
            vector,
            by_column,
            vector,
            by_row,
            by_row,
            by_column,
            tokens,
        ),
        out_specs=(
            tokens,
            tokens,
            vector,
            by_row,
            vector,
            vector,
            by_column,
            vector,
            by_row,
            by_row,
            by_column,
        ),
        check_vma=False,
    )
```

```python
import functools

import jax
import jax.numpy as jnp
from jax import lax
from jax.experimental import pallas as pl
from jax.experimental.pallas import tpu as pltpu
from jax.sharding import Mesh
from jax.sharding import PartitionSpec as P

HD = 64
LANES = 128
EPSILON = 1e-06
ROPE_BASE = 1000000.0
MASKED = -1e30
SCALE = HD ** (-0.5)
TILE = 256
MIB = 1 << 20
VMEM_LIMIT = 60 * MIB
F32 = jnp.float32
BF16 = jnp.bfloat16
AXES = ("fz", "fy", "cx", "cc")
FSDP = ("fz", "fy")
CTX = ("cx", "cc")
TOKENS = ("fy", "cx")
WEIGHTS = ("fz", "cc")


def dot_nn(a, b):
    return lax.dot_general(a, b, (((1,), (0,)), ((), ())), preferred_element_type=F32)


def dot_nt(a, b):
    return lax.dot_general(a, b, (((1,), (1,)), ((), ())), preferred_element_type=F32)


def dot_tn(a, b):
    return lax.dot_general(a, b, (((0,), (0,)), ((), ())), preferred_element_type=F32)


def lane_of(shape):
    return lax.broadcasted_iota(jnp.int32, shape, len(shape) - 1)


def swap_halves(block):
    lead = lane_of(block.shape) % HD < HD // 2
    return jnp.where(
        lead, pltpu.roll(block, LANES - HD // 2, 1), pltpu.roll(block, HD // 2, 1)
    )


def other_head(block):
    return jnp.concatenate([block[:, HD:], block[:, :HD]], axis=1)


def read_out(extras, first, piece, total):
    owners, columns = extras.shape
    at = lax.broadcasted_iota(jnp.int32, (columns, total), 1) % piece + first
    chosen = (lax.broadcasted_iota(jnp.int32, (columns, total), 0) == at).astype(BF16)
    spread = dot_nn(extras, chosen)
    owner = lax.broadcasted_iota(jnp.int32, (owners, total), 1) // piece
    mine = owner == lax.broadcasted_iota(jnp.int32, (owners, total), 0)
    return jnp.sum(jnp.where(mine, spread, 0.0), axis=0, keepdims=True)


def prep_kernel(
    x_ref, order_ref, spread_ref, w_low_ref, w_high_ref, cos_ref, sin_ref,
    normed_ref, q_ref, kv_ref, gain_ref, gain_mlp_ref, bias_ref,
):
    x = x_ref[...].astype(F32)
    dim = x.shape[1]
    width = q_ref.shape[1]
    joint = w_low_ref.shape[1]
    middle = w_low_ref.shape[0]
    owners = spread_ref.shape[0]

    @pl.when(pl.program_id(0) == 0)
    def _():
        extras = dot_nn(spread_ref[:, :middle], w_low_ref[:, :LANES])
        extras = (extras + dot_nn(spread_ref[:, middle:], w_high_ref[:, :LANES])).astype(BF16)
        shard = dim // owners
        gain_ref[...] = read_out(extras, 0, shard, dim)
        gain_mlp_ref[...] = read_out(extras, shard, shard, dim)
        bias_ref[...] = read_out(extras, 2 * shard, joint // owners, joint)

    gain, bias = gain_ref[...], bias_ref[...]
    inverse = lax.rsqrt(jnp.mean(x * x, axis=-1, keepdims=True) + EPSILON)
    normed = (x * inverse * gain).astype(BF16)
    ordered = dot_nn(normed, order_ref[...]).astype(BF16)
    normed_ref[...] = ordered
    joined = dot_nn(ordered[:, :middle], w_low_ref[...])
    joined = joined + dot_nn(ordered[:, middle:], w_high_ref[...]) + bias
    cosine, sine = cos_ref[...], sin_ref[...]
    for begin in range(0, width + LANES, LANES):
        block = joined[:, begin : begin + LANES]
        turned = block * cosine + swap_halves(block) * sine
        if begin < width:
            q_ref[:, begin : begin + LANES] = (turned * SCALE).astype(BF16)
        else:
            kv_ref[:, :LANES] = turned.astype(BF16)
    kv_ref[:, LANES:] = joined[:, width + LANES :].astype(BF16)


def rows_of(rows, cols):
    return pl.BlockSpec((rows, cols), lambda i: (i, 0))


def whole(value):
    return pl.BlockSpec(value.shape, lambda i: (0,) * value.ndim)


def prep(x, order, spread, weights, cosine, sine, rows):
    count, dim = x.shape
    ordered = order.shape[1]
    joint = weights[0].shape[1]
    width = joint - 2 * LANES
    row = pl.BlockSpec((1, dim), lambda i: (0, 0))
    return pl.pallas_call(
        prep_kernel,
        grid=(count // rows,),
        in_specs=[
            rows_of(rows, dim),
            whole(order),
            whole(spread),
            whole(weights[0]),
            whole(weights[1]),
            rows_of(rows, LANES),
            rows_of(rows, LANES),
        ],
        out_specs=[rows_of(rows, ordered), rows_of(rows, width), rows_of(rows, 2 * LANES), row, row],
        out_shape=[
            jax.ShapeDtypeStruct((count, ordered), BF16),
            jax.ShapeDtypeStruct((count, width), BF16),
            jax.ShapeDtypeStruct((count, 2 * LANES), BF16),
            jax.ShapeDtypeStruct((1, dim), F32),
            jax.ShapeDtypeStruct((1, dim), F32),
        ],
        scratch_shapes=[pltpu.VMEM((1, joint), F32)],
        compiler_params=pltpu.CompilerParams(vmem_limit_bytes=VMEM_LIMIT),
        cost_estimate=pl.CostEstimate(
            flops=2 * count * ordered * (joint + dim), bytes_accessed=12 * MIB, transcendentals=0
        ),
        name="norm_project_rotate",
    )(x, order, spread, weights[0], weights[1], cosine, sine)


def back_in_order(value, order):
    high = value.astype(BF16)
    low = (value - high.astype(F32)).astype(BF16)
    return dot_nt(high, order) + dot_nt(low, order)


def out_kernel(attended_ref, x_ref, w_low_ref, w_high_ref, order_ref, gain_ref, resid_ref, normed_ref):
    attended = attended_ref[...]
    branch = jnp.concatenate([dot_nt(attended, w_low_ref[...]), dot_nt(attended, w_high_ref[...])], axis=1)
    resid = x_ref[...].astype(F32) + back_in_order(branch, order_ref[...])
    inverse = lax.rsqrt(jnp.mean(resid * resid, axis=-1, keepdims=True) + EPSILON)
    resid_ref[...] = resid
    normed_ref[...] = (resid * inverse * gain_ref[...]).astype(BF16)


def project_out(attended, x, weights, order, gain, rows, seq):
    dim = x.shape[1]
    count = rows
    return pl.pallas_call(
        out_kernel,
        grid=(1,),
        in_specs=[
            rows_of(rows, attended.shape[1]),
            pl.BlockSpec((rows, dim), lambda i: (seq, 0)),
            whole(weights[0]),
            whole(weights[1]),
            whole(order),
            whole(gain),
        ],
        out_specs=[rows_of(rows, dim), rows_of(rows, dim)],
        out_shape=[jax.ShapeDtypeStruct((count, dim), F32), jax.ShapeDtypeStruct((count, dim), BF16)],
        compiler_params=pltpu.CompilerParams(vmem_limit_bytes=VMEM_LIMIT),
        cost_estimate=pl.CostEstimate(flops=6 * count * dim * dim, bytes_accessed=8 * MIB, transcendentals=0),
        name="project_out_norm",
    )(attended, x, weights[0], weights[1], order, gain)


def fold_rows(value):
    return jnp.sum(value.reshape(-1, 8, value.shape[1]), axis=0)


def norm_back(values, inverse, gain, incoming):
    scaled = incoming * gain
    mean_term = jnp.mean(scaled * values, axis=-1, keepdims=True)
    return inverse * scaled - values * inverse**3 * mean_term


def total_of(own_ref, *away_refs):
    total = own_ref[...]
    for ref in away_refs:
        total = total + ref[...].astype(F32)
    return total


def out_back_kernel(*refs):
    terms, resids = refs[:8], refs[8:10]
    cot_ref, w_low_ref, w_high_ref, order_ref, gain_ref = refs[10:15]
    d_resid_ref, d_branch_ref, d_attended_ref, gain_grad_ref = refs[15:]
    middle = w_low_ref.shape[0]
    d_normed = jnp.concatenate([total_of(*terms[:4]), total_of(*terms[4:])], axis=0)
    resid = jnp.concatenate([ref[...] for ref in resids], axis=0)
    inverse = lax.rsqrt(jnp.mean(resid * resid, axis=-1, keepdims=True) + EPSILON)
    d_resid = cot_ref[...].astype(F32) + norm_back(resid, inverse, gain_ref[...], d_normed)
    d_resid_ref[...] = d_resid
    d_branch = dot_nn(d_resid.astype(BF16), order_ref[...]).astype(BF16)
    d_branch_ref[...] = d_branch
    d_attended = dot_nn(d_branch[:, :middle], w_low_ref[...])
    d_attended = d_attended + dot_nn(d_branch[:, middle:], w_high_ref[...])
    d_attended_ref[...] = d_attended.astype(BF16)
    gain_grad_ref[...] = fold_rows(d_normed * resid * inverse)


def call_whole(kernel, operands, out_shape, flops, name):
    return pl.pallas_call(
        kernel,
        in_specs=[pl.BlockSpec(memory_space=pltpu.VMEM)] * len(operands),
        out_specs=[pl.BlockSpec(memory_space=pltpu.VMEM)] * len(out_shape),
        out_shape=out_shape,
        compiler_params=pltpu.CompilerParams(vmem_limit_bytes=VMEM_LIMIT),
        cost_estimate=pl.CostEstimate(flops=flops, bytes_accessed=16 * MIB, transcendentals=0),
        name=name,
    )(*operands)


def project_out_back(terms, resid, cot, weights, order, gain):
    count, dim = cot.shape
    ordered = order.shape[1]
    return call_whole(
        out_back_kernel,
        (*terms[0], *terms[1], *resid, cot, *weights, order, gain),
        [
            jax.ShapeDtypeStruct((count, dim), F32),
            jax.ShapeDtypeStruct((count, ordered), BF16),
            jax.ShapeDtypeStruct((count, weights[0].shape[1]), BF16),
            jax.ShapeDtypeStruct((8, dim), F32),
        ],
        4 * count * dim * dim,
        "norm_back_project",
    )


def input_back_kernel(*refs):
    dqs, terms = refs[:2], refs[2:10]
    x_ref, d_resid_ref, w_low_ref, w_high_ref, order_ref, gain_ref, cos_ref, sin_ref = refs[10:18]
    d_kv_ref, input_grad_ref, gain_grad_ref, bias_grad_ref = refs[18:]
    dkv = jnp.concatenate([total_of(*terms[:4]), total_of(*terms[4:])], axis=0)
    dk = dkv[:, :LANES]
    dk = dk * cos_ref[...] - swap_halves(dk) * sin_ref[...]
    d_kv = jnp.concatenate([dk.astype(BF16), dkv[:, LANES:].astype(BF16)], axis=1)
    d_kv_ref[...] = d_kv
    dq = jnp.concatenate([ref[...] for ref in dqs], axis=0)
    d_joined = jnp.concatenate([dq, d_kv], axis=1)
    d_normed = jnp.concatenate([dot_nt(d_joined, w_low_ref[...]), dot_nt(d_joined, w_high_ref[...])], axis=1)
    d_normed = back_in_order(d_normed, order_ref[...])
    x = x_ref[...].astype(F32)
    inverse = lax.rsqrt(jnp.mean(x * x, axis=-1, keepdims=True) + EPSILON)
    input_grad_ref[...] = (d_resid_ref[...] + norm_back(x, inverse, gain_ref[...], d_normed)).astype(BF16)
    gain_grad_ref[...] = fold_rows(d_normed * x * inverse)
    bias_grad_ref[...] = fold_rows(d_joined.astype(F32))


def input_back(dq, terms, x, d_resid, weights, order, gain, cosine, sine):
    count, dim = x.shape
    joint = dq[0].shape[1] + 2 * LANES
    return call_whole(
        input_back_kernel,
        (*dq, *terms[0], *terms[1], x, d_resid, *weights, order, gain, cosine, sine),
        [
            jax.ShapeDtypeStruct((count, 2 * LANES), BF16),
            jax.ShapeDtypeStruct((count, dim), BF16),
            jax.ShapeDtypeStruct((8, dim), F32),
            jax.ShapeDtypeStruct((8, joint), F32),
        ],
        6 * count * dim * joint,
        "input_gradient",
    )


def seq_rows(seq, rows, cols):
    return pl.BlockSpec((rows, cols), lambda i: (seq, 0))


def piece_of(seq, rows):
    return pl.BlockSpec((1, rows, 2 * LANES), lambda i: (seq, 0, 0))


def keys_and_values(piece_refs):
    joint = jnp.concatenate([ref[0] for ref in piece_refs], axis=0)
    key, value = joint[:, :LANES], joint[:, LANES:]
    return (key, other_head(key)), (value, other_head(value))


def attend_kernel(block_ref, q_ref, kv_0, kv_1, kv_2, kv_3, start_ref, out_ref):
    rows, width = q_ref.shape
    length = 4 * rows
    heads = width // HD
    group = heads // 2
    keys, values = keys_and_values((kv_0, kv_1, kv_2, kv_3))
    upper_key = lane_of((length, LANES)) >= HD
    upper = lane_of((rows, LANES)) >= HD
    query_at = block_ref[0] * rows + lax.broadcasted_iota(jnp.int32, (rows, length), 0)
    key_at = jnp.concatenate(
        [
            (block_ref[0] ^ place) * rows + lax.broadcasted_iota(jnp.int32, (rows, rows), 1)
            for place in range(4)
        ],
        axis=1,
    )
    allowed = (key_at <= query_at) & (key_at >= start_ref[:, :1])
    bias = jnp.where(allowed, 0.0, MASKED)
    one = jnp.ones((), BF16)
    for pair in range(heads // 2):
        at = slice(pair * LANES, (pair + 1) * LANES)
        both = q_ref[:, at]
        parts = []
        for place in range(2):
            owner = (2 * pair + place) // group
            moved = int(owner != place)
            side = upper if place else ~upper
            side_key = upper_key if place else ~upper_key
            query = jnp.where(side, both, jnp.zeros_like(both))
            score = dot_nt(query, keys[moved]) + bias
            top = jnp.max(score, axis=1, keepdims=True)
            weight = jnp.exp(score - top).astype(BF16)
            mixed = dot_nn(weight, jnp.where(side_key, values[moved], one))
            parts.append(mixed / pltpu.roll(mixed, HD, 1))
        out_ref[:, at] = jnp.where(upper, parts[1], parts[0]).astype(BF16)


def attend(block, q, kv_pieces, start, rows, seq):
    width = q.shape[1]
    heads = width // HD
    return pl.pallas_call(
        attend_kernel,
        grid=(1,),
        in_specs=[
            pl.BlockSpec(memory_space=pltpu.SMEM),
            seq_rows(seq, rows, width),
            *[piece_of(seq, rows)] * 4,
            seq_rows(seq, rows, LANES),
        ],
        out_specs=seq_rows(0, rows, width),
        out_shape=jax.ShapeDtypeStruct((rows, width), BF16),
        compiler_params=pltpu.CompilerParams(vmem_limit_bytes=VMEM_LIMIT),
        cost_estimate=pl.CostEstimate(
            flops=32 * rows * rows * LANES * heads,
            bytes_accessed=4 * rows * width,
            transcendentals=4 * rows * rows * heads,
        ),
        name="attention_forward",
    )(block, q, *kv_pieces, start)


def attend_back_kernel(
    block_ref, q_ref, kv_0, kv_1, kv_2, kv_3, back_ref, start_ref, cos_ref, sin_ref,
    dq_ref, own_ref, core_ref, x_ref, far_ref, dk_sum, dv_sum,
):
    rows, width = q_ref.shape
    length = 4 * rows
    heads = width // HD
    group = heads // 2
    keys, values = keys_and_values((kv_0, kv_1, kv_2, kv_3))
    key_t = keys[0].astype(F32).T.astype(BF16)
    keys_t = (key_t, jnp.concatenate([key_t[HD:], key_t[:HD]], axis=0))
    upper = lane_of((rows, LANES)) >= HD
    upper_t = lax.broadcasted_iota(jnp.int32, (LANES, rows), 0) >= HD
    query_at = block_ref[0] * rows + lax.broadcasted_iota(jnp.int32, (length, rows), 1)
    key_at = jnp.concatenate(
        [
            (block_ref[0] ^ place) * rows + lax.broadcasted_iota(jnp.int32, (rows, rows), 0)
            for place in range(4)
        ],
        axis=0,
    )
    allowed = (key_at <= query_at) & (key_at >= start_ref[0, :1, :])
    bias = jnp.where(allowed, 0.0, MASKED)
    cosine, sine = cos_ref[...], sin_ref[...]
    dk_sum[...] = jnp.zeros_like(dk_sum)
    dv_sum[...] = jnp.zeros_like(dv_sum)
    for pair in range(heads // 2):
        at = slice(pair * LANES, (pair + 1) * LANES)
        both = q_ref[:, at]
        back_both = back_ref[:, at]
        parts = []
        for place in range(2):
            owner = (2 * pair + place) // group
            moved = int(owner != place)
            side = upper if place else ~upper
            query = jnp.where(side, both, jnp.zeros_like(both))
            back = jnp.where(side, back_both, jnp.zeros_like(back_both))
            score = dot_nt(keys[moved], query) + bias
            weight = jnp.exp(score - jnp.max(score, axis=0, keepdims=True))
            prob = weight * (1.0 / jnp.sum(weight, axis=0, keepdims=True))
            dv_sum[owner] += dot_nn(prob.astype(BF16), back)
            d_prob = dot_nt(values[moved], back)
            level = jnp.sum(prob * d_prob, axis=0, keepdims=True)
            d_score = (prob * (d_prob - level)).astype(BF16)
            dk_sum[owner] += dot_nn(d_score, query)
            parts.append(dot_nn(keys_t[moved], d_score))
        d_query = jnp.where(upper_t, parts[1], parts[0]).T * SCALE
        dq_ref[:, at] = (d_query * cosine - swap_halves(d_query) * sine).astype(BF16)
    lower_key = lane_of((length, LANES)) < HD
    for total, begin in ((dk_sum, 0), (dv_sum, LANES)):
        first, second = total[0], total[1]
        first = first + pltpu.roll(first, HD, 1)
        second = second + pltpu.roll(second, HD, 1)
        both = jnp.where(lower_key, first, second)
        cols = slice(begin, begin + LANES)
        own_ref[:, cols] = both[:rows]
        for place, ref in enumerate((core_ref, x_ref, far_ref)):
            ref[:, cols] = both[(place + 1) * rows : (place + 2) * rows].astype(BF16)


def parts_of(rows, cols):
    shapes = [jax.ShapeDtypeStruct((rows, cols), F32)] + [jax.ShapeDtypeStruct((rows, cols), BF16)] * 3
    return [seq_rows(0, rows, cols)] * 4, shapes


def attend_back(block, q, kv_pieces, back, start, cosine, sine, rows, seq):
    width = q.shape[1]
    length = 4 * rows
    heads = width // HD
    specs, shapes = parts_of(rows, 2 * LANES)
    return pl.pallas_call(
        attend_back_kernel,
        grid=(1,),
        in_specs=[
            pl.BlockSpec(memory_space=pltpu.SMEM),
            seq_rows(seq, rows, width),
            *[piece_of(seq, rows)] * 4,
            seq_rows(seq, rows, width),
            pl.BlockSpec((1, 8, rows), lambda i: (seq, 0, 0)),
            seq_rows(seq, rows, LANES),
            seq_rows(seq, rows, LANES),
        ],
        out_specs=[seq_rows(0, rows, width), *specs],
        out_shape=[jax.ShapeDtypeStruct((rows, width), BF16), *shapes],
        scratch_shapes=[
            pltpu.VMEM((2, length, LANES), F32),
            pltpu.VMEM((2, length, LANES), F32),
        ],
        compiler_params=pltpu.CompilerParams(vmem_limit_bytes=VMEM_LIMIT),
        cost_estimate=pl.CostEstimate(
            flops=80 * rows * rows * LANES * heads,
            bytes_accessed=8 * rows * width,
            transcendentals=4 * rows * rows * heads,
        ),
        name="attention_backward",
    )(block, q, *kv_pieces, back, start, cosine, sine)


def mlp_kernel(
    n_0, n_1, n_2, n_3, c_0, c_1, c_2, c_3, w_ref,
    own_ref, out_1, out_2, out_3, d_own_ref, d_1, d_2, d_3, kept_ref, turned_ref,
    normed_all, cot_all,
):
    step = pl.program_id(0)
    rows = own_ref.shape[0]
    columns = w_ref.shape[1] // 3

    @pl.when(step == 0)
    def _():
        for place, (n_ref, c_ref) in enumerate(zip((n_0, n_1, n_2, n_3), (c_0, c_1, c_2, c_3))):
            normed_all[place // 2, (place % 2) * rows : (place % 2 + 1) * rows] = n_ref[...]
            cot_all[place // 2, (place % 2) * rows : (place % 2 + 1) * rows] = c_ref[...]

    normed, cot = normed_all[step], cot_all[step]
    for begin in range(0, columns, TILE):
        at = slice(begin, begin + TILE)
        gate = dot_nn(normed, w_ref[:, begin : begin + TILE])
        up = dot_nn(normed, w_ref[:, columns + begin : columns + begin + TILE])
        d_act = dot_nn(cot, w_ref[:, 2 * columns + begin : 2 * columns + begin + TILE])
        sigmoid = 0.5 * jnp.tanh(0.5 * gate) + 0.5
        swish = gate * sigmoid
        kept_ref[0, :, at] = (d_act * up * (sigmoid + swish * (1.0 - sigmoid))).astype(BF16)
        kept_ref[1, :, at] = (d_act * swish).astype(BF16)
        kept_ref[2, :, at] = (swish * up).astype(BF16)
    turned_ref[0] = normed.T
    turned_ref[1] = cot.T
    out = dot_nt(kept_ref[2], w_ref[:, 2 * columns :])
    d_normed = dot_nt(kept_ref[0], w_ref[:, :columns]) + dot_nt(kept_ref[1], w_ref[:, columns : 2 * columns])

    @pl.when(step == 0)
    def _():
        own_ref[...] = out[:rows]
        out_1[...] = out[rows:].astype(BF16)
        d_own_ref[...] = d_normed[:rows]
        d_1[...] = d_normed[rows:].astype(BF16)

    @pl.when(step == 1)
    def _():
        out_2[...] = out[:rows].astype(BF16)
        out_3[...] = out[rows:].astype(BF16)
        d_2[...] = d_normed[:rows].astype(BF16)
        d_3[...] = d_normed[rows:].astype(BF16)


def mlp(normed, cot, weights, seq):
    rows, dim = normed[0].shape
    columns = weights.shape[1] // 3
    specs, shapes = parts_of(rows, dim)
    once = lambda at: pl.BlockSpec((rows, dim), lambda i: (at, 0), pipeline_mode=pl.Buffered(1))
    return pl.pallas_call(
        mlp_kernel,
        grid=(2,),
        in_specs=[
            *[once(0)] * 4,
            *[once(seq)] * 3,
            once(0),
            pl.BlockSpec(weights.shape, lambda i: (0, 0), pipeline_mode=pl.Buffered(1)),
        ],
        out_specs=[
            *specs,
            *specs,
            pl.BlockSpec((3, 2 * rows, columns), lambda i: (0, i, 0)),
            pl.BlockSpec((2, dim, 2 * rows), lambda i: (0, 0, i)),
        ],
        out_shape=[
            *shapes,
            *shapes,
            jax.ShapeDtypeStruct((3, 4 * rows, columns), BF16),
            jax.ShapeDtypeStruct((2, dim, 4 * rows), BF16),
        ],
        scratch_shapes=[
            pltpu.VMEM((2, 2 * rows, dim), BF16),
            pltpu.VMEM((2, 2 * rows, dim), BF16),
        ],
        compiler_params=pltpu.CompilerParams(vmem_limit_bytes=VMEM_LIMIT),
        cost_estimate=pl.CostEstimate(
            flops=48 * rows * dim * columns,
            bytes_accessed=6 * dim * columns + 24 * rows * columns,
            transcendentals=4 * rows * columns,
        ),
        name="feed_forward",
    )(*normed, *cot, weights)


def mlp_grad_kernel(turned_0, turned_1, kept_0, kept_1, grad_ref):
    grad_ref[...] = (dot_nn(turned_0[0], kept_0[0]) + dot_nn(turned_1[0], kept_1[0])).astype(BF16)


def mlp_grad(turned, kept):
    _, dim, count = turned[0].shape
    columns = kept[0].shape[2]
    turned_block = pl.BlockSpec((1, dim, count), lambda i: (i // 2, 0, 0))
    kept_block = pl.BlockSpec((1, count, columns), lambda i: (i, 0, 0))
    return pl.pallas_call(
        mlp_grad_kernel,
        grid=(3,),
        in_specs=[turned_block, turned_block, kept_block, kept_block],
        out_specs=pl.BlockSpec((dim, columns), lambda i: (0, i)),
        out_shape=jax.ShapeDtypeStruct((dim, 3 * columns), BF16),
        compiler_params=pltpu.CompilerParams(vmem_limit_bytes=VMEM_LIMIT),
        cost_estimate=pl.CostEstimate(
            flops=12 * count * dim * columns,
            bytes_accessed=6 * dim * columns + 12 * count * columns,
            transcendentals=0,
        ),
        name="feed_forward_gradients",
    )(*turned, *kept)


def pack_kernel(block_ref, gate_ref, up_ref, down_ref, *refs):
    out_refs, scratch = refs[:4], refs[4]
    shard, ff = gate_ref.shape
    quarter = scratch.shape[2] // 4
    for place, ref in enumerate((gate_ref, up_ref, down_ref)):
        scratch[place, :, :ff] = ref[...].astype(F32)
        scratch[place, :, ff:] = jnp.zeros((shard, 4 * quarter - ff), F32)
    for place, out_ref in enumerate(out_refs):
        begin = pl.multiple_of((block_ref[0] ^ place) * quarter, LANES)
        for part in range(3):
            out_ref[:, part * quarter : (part + 1) * quarter] = scratch[part, :, pl.ds(begin, quarter)].astype(BF16)


def pack(block, gate, up, down_t, quarter):
    shard = gate.shape[0]
    return pl.pallas_call(
        pack_kernel,
        in_specs=[pl.BlockSpec(memory_space=pltpu.SMEM)] + [pl.BlockSpec(memory_space=pltpu.VMEM)] * 3,
        out_specs=[pl.BlockSpec(memory_space=pltpu.VMEM)] * 4,
        out_shape=[jax.ShapeDtypeStruct((shard, 3 * quarter), BF16)] * 4,
        scratch_shapes=[pltpu.VMEM((3, shard, 4 * quarter), F32)],
        compiler_params=pltpu.CompilerParams(vmem_limit_bytes=VMEM_LIMIT),
        name="pack_columns",
    )(block, gate, up, down_t)


def pick(options, index):
    value = options[0]
    for place in range(1, len(options)):
        value = jnp.where(index == place, options[place], value)
    return value


def assemble_kernel(block_ref, *refs):
    pieces, out_ref, scratch = refs[:4], refs[4], refs[5]
    shard = pieces[0].shape[0]
    values = [ref[...].astype(F32) for ref in pieces]
    for owner in range(4):
        scratch[owner * shard : (owner + 1) * shard] = pick(values, block_ref[0] ^ owner)
    out_ref[...] = scratch[...].astype(BF16)


def assemble(block, pieces):
    shard, columns = pieces[0].shape
    return pl.pallas_call(
        assemble_kernel,
        in_specs=[pl.BlockSpec(memory_space=pltpu.SMEM)] + [pl.BlockSpec(memory_space=pltpu.VMEM)] * 4,
        out_specs=pl.BlockSpec(memory_space=pltpu.VMEM),
        out_shape=jax.ShapeDtypeStruct((4 * shard, columns), BF16),
        scratch_shapes=[pltpu.VMEM((4 * shard, columns), F32)],
        compiler_params=pltpu.CompilerParams(vmem_limit_bytes=VMEM_LIMIT),
        name="assemble_rows",
    )(block, *pieces)


def cut_kernel(block_ref, value_ref, *refs):
    out_refs, scratch = refs[:4], refs[4]
    shard = out_refs[0].shape[0]
    scratch[...] = value_ref[...].astype(F32)
    values = [scratch[owner * shard : (owner + 1) * shard] for owner in range(4)]
    for place, out_ref in enumerate(out_refs):
        out_ref[...] = pick(values, block_ref[0] ^ place).astype(BF16)


def cut(block, value):
    shard, columns = value.shape[0] // 4, value.shape[1]
    return pl.pallas_call(
        cut_kernel,
        in_specs=[pl.BlockSpec(memory_space=pltpu.SMEM), pl.BlockSpec(memory_space=pltpu.VMEM)],
        out_specs=[pl.BlockSpec(memory_space=pltpu.VMEM)] * 4,
        out_shape=[jax.ShapeDtypeStruct((shard, columns), BF16)] * 4,
        scratch_shapes=[pltpu.VMEM(value.shape, F32)],
        compiler_params=pltpu.CompilerParams(vmem_limit_bytes=VMEM_LIMIT),
        name="cut_rows",
    )(block, value)


def unpack_kernel(block_ref, *refs):
    pieces, out_refs, scratch = refs[:4], refs[4:7], refs[7]
    ff = out_refs[0].shape[1]
    quarter = scratch.shape[2] // 4
    for place, ref in enumerate(pieces):
        begin = pl.multiple_of((block_ref[0] ^ place) * quarter, LANES)
        for part in range(3):
            scratch[part, :, pl.ds(begin, quarter)] = ref[:, part * quarter : (part + 1) * quarter].astype(F32)
    for part, out_ref in enumerate(out_refs):
        out_ref[...] = scratch[part, :, :ff]


def unpack(block, pieces, ff):
    shard, columns = pieces[0].shape
    return pl.pallas_call(
        unpack_kernel,
        in_specs=[pl.BlockSpec(memory_space=pltpu.SMEM)] + [pl.BlockSpec(memory_space=pltpu.VMEM)] * 4,
        out_specs=[pl.BlockSpec(memory_space=pltpu.VMEM)] * 3,
        out_shape=[jax.ShapeDtypeStruct((shard, ff), F32)] * 3,
        scratch_shapes=[pltpu.VMEM((3, shard, columns // 3 * 4), F32)],
        compiler_params=pltpu.CompilerParams(vmem_limit_bytes=VMEM_LIMIT),
        name="unpack_columns",
    )(block, *pieces)


def bit_swap(value, axis, bit=0):
    size = lax.axis_size(axis)
    return lax.ppermute(value, axis, [(i, i ^ (1 << bit)) for i in range(size)])


def jump_swap(value, axes, jump):
    return lax.ppermute(value, axes, [(i, i ^ jump) for i in range(4)])


def to_plane(value, slot):
    high, low = slot >> 1, slot & 1
    pairs = [
        (4 * y + 2 * x + c, 4 * (c ^ low) + 2 * (x ^ high) + y) for y in range(2) for x in range(2) for c in range(2)
    ]
    return lax.ppermute(value, TOKENS + ("cc",), pairs)


def from_plane(value, slot):
    high, low = slot >> 1, slot & 1
    pairs = [
        (4 * y + 2 * x + c, 4 * c + 2 * (x ^ high) + (y ^ low)) for y in range(2) for x in range(2) for c in range(2)
    ]
    return lax.ppermute(value, TOKENS + ("cc",), pairs)


def after(first, *values):
    return lax.optimization_barrier((first, *values))


def gather_four(value, axes):
    from_first = bit_swap(value, axes[0])
    return [value, bit_swap(value, axes[1]), from_first, bit_swap(from_first, axes[1])]


def gather_direct(value, axes):
    return [value] + [jump_swap(value, axes, jump) for jump in range(1, 4)]


def sum_direct(axes, own, *away):
    return [own] + [jump_swap(value, axes, jump + 1) for jump, value in enumerate(away)]


def doubling_offsets(steps):
    weight = {"cc": 1, "cx": 2, "fy": 4, "fz": 8}
    offsets = [0]
    for axis, bit in steps:
        offsets += [offset ^ (weight[axis] << bit) for offset in offsets]
    return jnp.array(offsets, jnp.int32)


def double(value, axis, bit=0):
    return jnp.concatenate([value, bit_swap(value, axis, bit)], axis=0)


def halve(value, axis, bit=0):
    middle = value.shape[0] // 2
    came = bit_swap(value[middle:], axis, bit)
    return (value[:middle].astype(F32) + came.astype(F32)).astype(BF16)


def on_device(
    hidden,
    segments,
    attn_gain,
    qkv_weight,
    qkv_bias,
    out_weight,
    mlp_gain,
    gate_weight,
    up_weight,
    down_weight,
    cotangent,
):
    seqs, rows, dim = hidden.shape
    count = seqs * rows
    shard = attn_gain.shape[0]
    world = dim // shard
    joint = qkv_weight.shape[1]
    width = joint - 2 * LANES
    ff = gate_weight.shape[1]
    block = lax.axis_index("cx") * lax.axis_size("cc") + lax.axis_index("cc")
    me = lax.axis_index(FSDP) * lax.axis_size(CTX) + block
    offset = block * rows
    block_arg = block.reshape(1).astype(jnp.int32)
    plane_arg = (lax.axis_index("cx") * 2 + lax.axis_index("fy")).reshape(1).astype(jnp.int32)
    x = hidden.reshape(count, dim)
    cot = cotangent.reshape(count, dim)

    far = [("fz", bit) for bit in reversed(range((lax.axis_size("fz")).bit_length() - 1))]
    padded = -(-(shard + 1) // 16) * 16
    small = jnp.concatenate([attn_gain, mlp_gain, qkv_bias])
    small_row = jnp.pad(small, (0, joint + width - small.shape[0]))[None]
    first = jnp.concatenate(
        [
            jnp.concatenate([qkv_weight, out_weight.T], axis=1),
            small_row,
            jnp.zeros((padded - shard - 1, joint + width), BF16),
        ],
        axis=0,
    )
    for axis, bit in far:
        first = double(first, axis, bit)

    quarter = -(-ff // (4 * TILE)) * TILE
    pieces = pack(block_arg, gate_weight, up_weight, down_weight.T, quarter)
    pieces = [to_plane(piece, slot) for slot, piece in enumerate(pieces)]
    within = jnp.arange(padded, dtype=jnp.int32)

    def arrival(steps):
        owner = me ^ doubling_offsets(steps)
        target = jnp.where(within[None, :] < shard, owner[:, None] * shard + within[None, :], -1).reshape(1, -1)
        return owner, (jnp.arange(dim, dtype=jnp.int32)[:, None] == target).astype(BF16)

    owner, order = arrival(far + [("fy", 0), ("cx", 0), ("cc", 0)])
    _, out_order = arrival(far + [("cx", 0), ("fy", 0), ("cc", 0)])
    place = jnp.where(within[None, :] == shard, owner[:, None], -1).reshape(1, -1)
    spread = (jnp.arange(world, dtype=jnp.int32)[:, None] == place).astype(BF16)

    at_row = lax.dynamic_slice_in_dim(segments, offset, rows, axis=1)
    zeros_before = jnp.sum((segments < 1).astype(jnp.int32), axis=1, keepdims=True)
    ones_before = jnp.sum((segments < 2).astype(jnp.int32), axis=1, keepdims=True)
    start = jnp.where(at_row == 0, 0, jnp.where(at_row == 1, zeros_before, ones_before))
    position = (offset + jnp.arange(rows, dtype=jnp.int32)[None, :] - start).reshape(count)
    lane = jnp.arange(LANES, dtype=jnp.int32)
    frequency = ROPE_BASE ** (-(lane % (HD // 2)).astype(F32) * 2.0 / HD)
    angle = position.astype(F32)[:, None] * frequency[None, :]
    cosine = jnp.cos(angle)
    sine = jnp.where(lane % HD < HD // 2, -1.0, 1.0)[None, :] * jnp.sin(angle)
    start_column = jnp.broadcast_to(start.reshape(count, 1), (count, LANES))
    start_row = jnp.broadcast_to(start[:, None, :], (seqs, 8, rows))

    w_joint, w_out = double(first[:, :joint], "fy"), double(first[:, joint:], "cx")
    w_joint, w_out = double(w_joint, "cx"), double(w_out, "fy")
    w_joint, w_out, order, out_order, spread, cosine, sine, start_column, cot_late, *pieces = after(
        w_joint, w_out, order, out_order, spread, cosine, sine, start_column, cot, *pieces
    )
    mlp_shard = assemble(plane_arg, pieces)
    mlp_weights = lax.all_gather(mlp_shard, WEIGHTS, axis=0, tiled=True)
    w_joint, w_out = (w_joint, bit_swap(w_joint, "cc")), (w_out, bit_swap(w_out, "cc"))

    cot_x, cot_y = bit_swap(cot_late, "cx"), bit_swap(cot_late, "fy")

    normed, q, kv, gain_attn, gain_mlp = prep(x, order, spread, w_joint, cosine, sine, rows)
    kv_all = gather_four(kv.reshape(seqs, rows, 2 * LANES), CTX)
    kv_all[3], cot_x, cot_y = after(kv_all[3], cot_x, cot_y)
    far_0, far_1 = cot_x[:rows], cot_y[rows:]
    cot_far = [bit_swap(far_0, "fy"), bit_swap(far_1, "cx")]
    attended, resid, normed_all = [], [], []
    for seq in range(seqs):
        turn = block_arg if seq == 0 else after(attended[0], block_arg)[1]
        attended.append(attend(turn, q, kv_all, start_column, rows, seq))
        if seq == 1:
            attended[1], *cot_far = after(attended[1], *cot_far)
        resid_one, normed_one = project_out(attended[seq], x, w_out, out_order, gain_mlp, rows, seq)
        resid.append(resid_one)
        normed_all.append(gather_direct(normed_one, TOKENS))

    out_parts, d_terms, kept, turned = [], [], [], []
    for seq in range(seqs):
        if seq == 1:
            out_parts[0], normed_all[1] = lax.optimization_barrier((out_parts[0], normed_all[1]))
        result = mlp(normed_all[seq], [cot, cot_x, cot_y, cot_far[seq]], mlp_weights, seq)
        out_parts.append(result[:4])
        d_terms.append(sum_direct(TOKENS, *result[4:8]))
        kept.append(result[8])
        turned.append(result[9])
    turned[1], *d_terms[0] = after(turned[1], *d_terms[0])
    grads = mlp_grad(turned, kept)
    grads, d_terms[0], d_terms[1] = after(grads, *d_terms)
    grads = lax.psum_scatter(
        grads.reshape(world // 4, 4 * shard, 3 * quarter), WEIGHTS, scatter_dimension=0, tiled=False
    )

    d_resid, d_branch, d_attended, mlp_gain_grad = project_out_back(
        d_terms, resid, cot, w_out, out_order, gain_mlp
    )
    out_grad = dot_tn(d_branch, jnp.concatenate(attended, axis=0)).astype(BF16)
    out_grad = halve(out_grad, "cc")
    out_terms = [sum_direct(TOKENS, *after(d_terms[1][1], *part)[1:]) for part in out_parts]
    d_attended, out_terms[0] = after(d_attended, out_terms[0])
    dq, dkv_terms = [], []
    for seq in range(seqs):
        if seq == 1:
            dq[0], d_attended, out_grad, out_terms[1] = after(dq[0], d_attended, out_grad, out_terms[1])
            out_grad = halve(out_grad, "fy")
        result = attend_back(block_arg, q, kv_all, d_attended, start_row, cosine, sine, rows, seq)
        dq.append(result[0])
        dkv_terms.append(sum_direct(CTX, *result[1:]))
    dq[1], out_grad, *dkv_terms[0] = after(dq[1], out_grad, *dkv_terms[0])
    q_grad = dot_tn(normed, jnp.concatenate(dq, axis=0)).astype(BF16)
    q_grad = halve(q_grad, "cc")
    q_grad, *dkv_terms[1] = after(q_grad, *dkv_terms[1])
    q_grad, out_grad = halve(q_grad, "cx"), halve(out_grad, "cx")
    d_kv, input_grad, attn_gain_grad, bias_grad = input_back(
        dq, dkv_terms, x, d_resid, w_joint, order, gain_attn, cosine, sine
    )
    d_kv, q_grad, out_grad = after(d_kv, q_grad, out_grad)

    output = []
    for seq in range(seqs):
        own, *away = out_terms[seq]
        output.append((resid[seq] + own + sum(term.astype(F32) for term in away)).astype(BF16))

    split_at = width + LANES
    bias_grad = jnp.sum(bias_grad, axis=0)
    small_grads = jnp.concatenate(
        [
            jnp.sum(attn_gain_grad, axis=0).reshape(world, -1),
            jnp.sum(mlp_gain_grad, axis=0).reshape(world, -1),
            bias_grad[:split_at].reshape(world, -1),
            bias_grad[split_at:].reshape(world, -1),
        ],
        axis=1,
    ).astype(BF16)
    small_count = small_grads.shape[1]
    small_grads = jnp.pad(small_grads, ((0, 0), (0, 2 * LANES - small_count)))
    kv_grad = dot_tn(
        jnp.concatenate([normed, spread], axis=0), jnp.concatenate([d_kv, small_grads], axis=0)
    ).astype(BF16)
    kv_grad = halve(halve(kv_grad, "cc"), "cx")
    joint_grad = halve(jnp.concatenate([q_grad, kv_grad], axis=1), "fy")
    pieces = cut(plane_arg, lax.optimization_barrier(grads))
    joint_grad, *pieces = after(joint_grad, *pieces)
    pieces = [from_plane(piece, slot) for slot, piece in enumerate(pieces)]
    first_sum = jnp.concatenate([joint_grad, out_grad], axis=1)
    for axis, bit in reversed(far):
        first_sum = halve(first_sum, axis, bit)
    gate_grad, up_grad, down_grad_t = unpack(block_arg, pieces, ff)
    first_sum = first_sum.astype(F32)
    qkv_sum, out_sum = first_sum[:, :joint], first_sum[:, joint:]
    small_sum = qkv_sum[shard, width : width + small_count]
    at = (shard, 2 * shard, 2 * shard + split_at // world)

    return (
        jnp.stack(output),
        input_grad.reshape(hidden.shape),
        small_sum[: at[0]],
        qkv_sum[:shard],
        small_sum[at[1] : at[2]],
        small_sum[at[2] :],
        out_sum[:shard].T,
        small_sum[at[0] : at[1]],
        gate_grad,
        up_grad,
        down_grad_t.T,
    )


def solution(mesh):
    fsdp, ctx = mesh.shape["fsdp"], mesh.shape["ctx"]
    inner = Mesh(mesh.devices.reshape(fsdp // 2, 2, 2, ctx // 2), AXES)
    tokens = P(FSDP, CTX, None)
    vector = P(AXES)
    by_row = P(AXES, None)
    by_column = P(None, AXES)
    return jax.shard_map(
        on_device,
        mesh=inner,
        in_specs=(
            tokens,
            P(FSDP, None),
            vector,
            by_row,
            vector,
            by_column,
            vector,
            by_row,
            by_row,
            by_column,
            tokens,
        ),
        out_specs=(
            tokens,
            tokens,
            vector,
            by_row,
            vector,
            vector,
            by_column,
            vector,
            by_row,
            by_row,
            by_column,
        ),
        check_vma=False,
    )
```

```python
import functools

import jax
import jax.numpy as jnp
from jax import lax
from jax.experimental import pallas as pl
from jax.experimental.pallas import tpu as pltpu
from jax.sharding import Mesh
from jax.sharding import PartitionSpec as P

HD = 64
LANES = 128
EPSILON = 1e-06
ROPE_BASE = 1000000.0
MASKED = -1e30
SCALE = HD ** (-0.5)
TILE = 256
MIB = 1 << 20
VMEM_LIMIT = 60 * MIB
F32 = jnp.float32
BF16 = jnp.bfloat16
AXES = ("fz", "fy", "cx", "cc")
FSDP = ("fz", "fy")
CTX = ("cx", "cc")
TOKENS = ("fy", "cx")
WEIGHTS = ("fz", "cc")


def dot_nn(a, b):
    return lax.dot_general(a, b, (((1,), (0,)), ((), ())), preferred_element_type=F32)


def dot_nt(a, b):
    return lax.dot_general(a, b, (((1,), (1,)), ((), ())), preferred_element_type=F32)


def dot_tn(a, b):
    return lax.dot_general(a, b, (((0,), (0,)), ((), ())), preferred_element_type=F32)


def lane_of(shape):
    return lax.broadcasted_iota(jnp.int32, shape, len(shape) - 1)


def swap_halves(block):
    lead = lane_of(block.shape) % HD < HD // 2
    return jnp.where(
        lead, pltpu.roll(block, LANES - HD // 2, 1), pltpu.roll(block, HD // 2, 1)
    )


def other_head(block):
    return jnp.concatenate([block[:, HD:], block[:, :HD]], axis=1)


def read_out(extras, first, piece, total):
    owners, columns = extras.shape
    at = lax.broadcasted_iota(jnp.int32, (columns, total), 1) % piece + first
    chosen = (lax.broadcasted_iota(jnp.int32, (columns, total), 0) == at).astype(BF16)
    spread = dot_nn(extras, chosen)
    owner = lax.broadcasted_iota(jnp.int32, (owners, total), 1) // piece
    mine = owner == lax.broadcasted_iota(jnp.int32, (owners, total), 0)
    return jnp.sum(jnp.where(mine, spread, 0.0), axis=0, keepdims=True)


def prep_kernel(
    x_ref, order_ref, spread_ref, w_low_ref, w_high_ref, cos_ref, sin_ref,
    normed_ref, q_ref, kv_ref, gain_ref, gain_mlp_ref, bias_ref,
):
    x = x_ref[...].astype(F32)
    dim = x.shape[1]
    width = q_ref.shape[1]
    joint = w_low_ref.shape[1]
    middle = w_low_ref.shape[0]
    owners = spread_ref.shape[0]

    @pl.when(pl.program_id(0) == 0)
    def _():
        extras = dot_nn(spread_ref[:, :middle], w_low_ref[:, :LANES])
        extras = (extras + dot_nn(spread_ref[:, middle:], w_high_ref[:, :LANES])).astype(BF16)
        shard = dim // owners
        gain_ref[...] = read_out(extras, 0, shard, dim)
        gain_mlp_ref[...] = read_out(extras, shard, shard, dim)
        bias_ref[...] = read_out(extras, 2 * shard, joint // owners, joint)

    gain, bias = gain_ref[...], bias_ref[...]
    inverse = lax.rsqrt(jnp.mean(x * x, axis=-1, keepdims=True) + EPSILON)
    normed = (x * inverse * gain).astype(BF16)
    ordered = dot_nn(normed, order_ref[...]).astype(BF16)
    normed_ref[...] = ordered
    joined = dot_nn(ordered[:, :middle], w_low_ref[...])
    joined = joined + dot_nn(ordered[:, middle:], w_high_ref[...]) + bias
    cosine, sine = cos_ref[...], sin_ref[...]
    for begin in range(0, width + LANES, LANES):
        block = joined[:, begin : begin + LANES]
        turned = block * cosine + swap_halves(block) * sine
        if begin < width:
            q_ref[:, begin : begin + LANES] = (turned * SCALE).astype(BF16)
        else:
            kv_ref[:, :LANES] = turned.astype(BF16)
    kv_ref[:, LANES:] = joined[:, width + LANES :].astype(BF16)


def rows_of(rows, cols):
    return pl.BlockSpec((rows, cols), lambda i: (i, 0))


def whole(value):
    return pl.BlockSpec(value.shape, lambda i: (0,) * value.ndim)


def prep(x, order, spread, weights, cosine, sine, rows):
    count, dim = x.shape
    ordered = order.shape[1]
    joint = weights[0].shape[1]
    width = joint - 2 * LANES
    row = pl.BlockSpec((1, dim), lambda i: (0, 0))
    return pl.pallas_call(
        prep_kernel,
        grid=(count // rows,),
        in_specs=[
            rows_of(rows, dim),
            whole(order),
            whole(spread),
            whole(weights[0]),
            whole(weights[1]),
            rows_of(rows, LANES),
            rows_of(rows, LANES),
        ],
        out_specs=[rows_of(rows, ordered), rows_of(rows, width), rows_of(rows, 2 * LANES), row, row],
        out_shape=[
            jax.ShapeDtypeStruct((count, ordered), BF16),
            jax.ShapeDtypeStruct((count, width), BF16),
            jax.ShapeDtypeStruct((count, 2 * LANES), BF16),
            jax.ShapeDtypeStruct((1, dim), F32),
            jax.ShapeDtypeStruct((1, dim), F32),
        ],
        scratch_shapes=[pltpu.VMEM((1, joint), F32)],
        compiler_params=pltpu.CompilerParams(vmem_limit_bytes=VMEM_LIMIT),
        cost_estimate=pl.CostEstimate(
            flops=2 * count * ordered * (joint + dim), bytes_accessed=12 * MIB, transcendentals=0
        ),
        name="norm_project_rotate",
    )(x, order, spread, weights[0], weights[1], cosine, sine)


def back_in_order(value, order):
    high = value.astype(BF16)
    low = (value - high.astype(F32)).astype(BF16)
    return dot_nt(high, order) + dot_nt(low, order)


def out_kernel(attended_ref, x_ref, w_low_ref, w_high_ref, order_ref, gain_ref, resid_ref, normed_ref):
    attended = attended_ref[...]
    branch = jnp.concatenate([dot_nt(attended, w_low_ref[...]), dot_nt(attended, w_high_ref[...])], axis=1)
    resid = x_ref[...].astype(F32) + back_in_order(branch, order_ref[...])
    inverse = lax.rsqrt(jnp.mean(resid * resid, axis=-1, keepdims=True) + EPSILON)
    resid_ref[...] = resid
    normed_ref[...] = (resid * inverse * gain_ref[...]).astype(BF16)


def project_out(attended, x, weights, order, gain, rows, seq):
    dim = x.shape[1]
    count = rows
    return pl.pallas_call(
        out_kernel,
        grid=(1,),
        in_specs=[
            rows_of(rows, attended.shape[1]),
            pl.BlockSpec((rows, dim), lambda i: (seq, 0)),
            whole(weights[0]),
            whole(weights[1]),
            whole(order),
            whole(gain),
        ],
        out_specs=[rows_of(rows, dim), rows_of(rows, dim)],
        out_shape=[jax.ShapeDtypeStruct((count, dim), F32), jax.ShapeDtypeStruct((count, dim), BF16)],
        compiler_params=pltpu.CompilerParams(vmem_limit_bytes=VMEM_LIMIT),
        cost_estimate=pl.CostEstimate(flops=6 * count * dim * dim, bytes_accessed=8 * MIB, transcendentals=0),
        name="project_out_norm",
    )(attended, x, weights[0], weights[1], order, gain)


def fold_rows(value):
    return jnp.sum(value.reshape(-1, 8, value.shape[1]), axis=0)


def norm_back(values, inverse, gain, incoming):
    scaled = incoming * gain
    mean_term = jnp.mean(scaled * values, axis=-1, keepdims=True)
    return inverse * scaled - values * inverse**3 * mean_term


def total_of(own_ref, *away_refs):
    total = own_ref[...]
    for ref in away_refs:
        total = total + ref[...].astype(F32)
    return total


def out_back_kernel(*refs):
    terms, resids = refs[:8], refs[8:10]
    cot_ref, w_low_ref, w_high_ref, order_ref, gain_ref = refs[10:15]
    d_resid_ref, d_branch_ref, d_attended_ref, gain_grad_ref = refs[15:]
    middle = w_low_ref.shape[0]
    d_normed = jnp.concatenate([total_of(*terms[:4]), total_of(*terms[4:])], axis=0)
    resid = jnp.concatenate([ref[...] for ref in resids], axis=0)
    inverse = lax.rsqrt(jnp.mean(resid * resid, axis=-1, keepdims=True) + EPSILON)
    d_resid = cot_ref[...].astype(F32) + norm_back(resid, inverse, gain_ref[...], d_normed)
    d_resid_ref[...] = d_resid
    d_branch = dot_nn(d_resid.astype(BF16), order_ref[...]).astype(BF16)
    d_branch_ref[...] = d_branch
    d_attended = dot_nn(d_branch[:, :middle], w_low_ref[...])
    d_attended = d_attended + dot_nn(d_branch[:, middle:], w_high_ref[...])
    d_attended_ref[...] = d_attended.astype(BF16)
    gain_grad_ref[...] = fold_rows(d_normed * resid * inverse)


def call_whole(kernel, operands, out_shape, flops, name):
    return pl.pallas_call(
        kernel,
        in_specs=[pl.BlockSpec(memory_space=pltpu.VMEM)] * len(operands),
        out_specs=[pl.BlockSpec(memory_space=pltpu.VMEM)] * len(out_shape),
        out_shape=out_shape,
        compiler_params=pltpu.CompilerParams(vmem_limit_bytes=VMEM_LIMIT),
        cost_estimate=pl.CostEstimate(flops=flops, bytes_accessed=16 * MIB, transcendentals=0),
        name=name,
    )(*operands)


def project_out_back(terms, resid, cot, weights, order, gain):
    count, dim = cot.shape
    ordered = order.shape[1]
    return call_whole(
        out_back_kernel,
        (*terms[0], *terms[1], *resid, cot, *weights, order, gain),
        [
            jax.ShapeDtypeStruct((count, dim), F32),
            jax.ShapeDtypeStruct((count, ordered), BF16),
            jax.ShapeDtypeStruct((count, weights[0].shape[1]), BF16),
            jax.ShapeDtypeStruct((8, dim), F32),
        ],
        4 * count * dim * dim,
        "norm_back_project",
    )


def input_back_kernel(*refs):
    dqs, terms = refs[:2], refs[2:10]
    x_ref, d_resid_ref, w_low_ref, w_high_ref, order_ref, gain_ref, cos_ref, sin_ref = refs[10:18]
    d_kv_ref, input_grad_ref, gain_grad_ref, bias_grad_ref = refs[18:]
    dkv = jnp.concatenate([total_of(*terms[:4]), total_of(*terms[4:])], axis=0)
    dk = dkv[:, :LANES]
    dk = dk * cos_ref[...] - swap_halves(dk) * sin_ref[...]
    d_kv = jnp.concatenate([dk.astype(BF16), dkv[:, LANES:].astype(BF16)], axis=1)
    d_kv_ref[...] = d_kv
    dq = jnp.concatenate([ref[...] for ref in dqs], axis=0)
    d_joined = jnp.concatenate([dq, d_kv], axis=1)
    d_normed = jnp.concatenate([dot_nt(d_joined, w_low_ref[...]), dot_nt(d_joined, w_high_ref[...])], axis=1)
    d_normed = back_in_order(d_normed, order_ref[...])
    x = x_ref[...].astype(F32)
    inverse = lax.rsqrt(jnp.mean(x * x, axis=-1, keepdims=True) + EPSILON)
    input_grad_ref[...] = (d_resid_ref[...] + norm_back(x, inverse, gain_ref[...], d_normed)).astype(BF16)
    gain_grad_ref[...] = fold_rows(d_normed * x * inverse)
    bias_grad_ref[...] = fold_rows(d_joined.astype(F32))


def input_back(dq, terms, x, d_resid, weights, order, gain, cosine, sine):
    count, dim = x.shape
    joint = dq[0].shape[1] + 2 * LANES
    return call_whole(
        input_back_kernel,
        (*dq, *terms[0], *terms[1], x, d_resid, *weights, order, gain, cosine, sine),
        [
            jax.ShapeDtypeStruct((count, 2 * LANES), BF16),
            jax.ShapeDtypeStruct((count, dim), BF16),
            jax.ShapeDtypeStruct((8, dim), F32),
            jax.ShapeDtypeStruct((8, joint), F32),
        ],
        6 * count * dim * joint,
        "input_gradient",
    )


def seq_rows(seq, rows, cols):
    return pl.BlockSpec((rows, cols), lambda i: (seq, 0))


def piece_of(seq, rows):
    return pl.BlockSpec((1, rows, 2 * LANES), lambda i: (seq, 0, 0))


def keys_and_values(piece_refs):
    joint = jnp.concatenate([ref[0] for ref in piece_refs], axis=0)
    key, value = joint[:, :LANES], joint[:, LANES:]
    return (key, other_head(key)), (value, other_head(value))


def attend_kernel(block_ref, q_ref, kv_0, kv_1, kv_2, kv_3, start_ref, out_ref):
    rows, width = q_ref.shape
    length = 4 * rows
    heads = width // HD
    group = heads // 2
    keys, values = keys_and_values((kv_0, kv_1, kv_2, kv_3))
    upper_key = lane_of((length, LANES)) >= HD
    upper = lane_of((rows, LANES)) >= HD
    query_at = block_ref[0] * rows + lax.broadcasted_iota(jnp.int32, (rows, length), 0)
    key_at = jnp.concatenate(
        [
            (block_ref[0] ^ place) * rows + lax.broadcasted_iota(jnp.int32, (rows, rows), 1)
            for place in range(4)
        ],
        axis=1,
    )
    allowed = (key_at <= query_at) & (key_at >= start_ref[:, :1])
    bias = jnp.where(allowed, 0.0, MASKED)
    one = jnp.ones((), BF16)
    for pair in range(heads // 2):
        at = slice(pair * LANES, (pair + 1) * LANES)
        both = q_ref[:, at]
        parts = []
        for place in range(2):
            owner = (2 * pair + place) // group
            moved = int(owner != place)
            side = upper if place else ~upper
            side_key = upper_key if place else ~upper_key
            query = jnp.where(side, both, jnp.zeros_like(both))
            score = dot_nt(query, keys[moved]) + bias
            top = jnp.max(score, axis=1, keepdims=True)
            weight = jnp.exp(score - top).astype(BF16)
            mixed = dot_nn(weight, jnp.where(side_key, values[moved], one))
            parts.append(mixed / pltpu.roll(mixed, HD, 1))
        out_ref[:, at] = jnp.where(upper, parts[1], parts[0]).astype(BF16)


def attend(block, q, kv_pieces, start, rows, seq):
    width = q.shape[1]
    heads = width // HD
    return pl.pallas_call(
        attend_kernel,
        grid=(1,),
        in_specs=[
            pl.BlockSpec(memory_space=pltpu.SMEM),
            seq_rows(seq, rows, width),
            *[piece_of(seq, rows)] * 4,
            seq_rows(seq, rows, LANES),
        ],
        out_specs=seq_rows(0, rows, width),
        out_shape=jax.ShapeDtypeStruct((rows, width), BF16),
        compiler_params=pltpu.CompilerParams(vmem_limit_bytes=VMEM_LIMIT),
        cost_estimate=pl.CostEstimate(
            flops=32 * rows * rows * LANES * heads,
            bytes_accessed=4 * rows * width,
            transcendentals=4 * rows * rows * heads,
        ),
        name="attention_forward",
    )(block, q, *kv_pieces, start)


def attend_back_kernel(
    block_ref, q_ref, kv_0, kv_1, kv_2, kv_3, back_ref, start_ref, cos_ref, sin_ref,
    dq_ref, own_ref, core_ref, x_ref, far_ref, dk_sum, dv_sum,
):
    rows, width = q_ref.shape
    length = 4 * rows
    heads = width // HD
    group = heads // 2
    keys, values = keys_and_values((kv_0, kv_1, kv_2, kv_3))
    key_t = keys[0].astype(F32).T.astype(BF16)
    keys_t = (key_t, jnp.concatenate([key_t[HD:], key_t[:HD]], axis=0))
    upper = lane_of((rows, LANES)) >= HD
    upper_t = lax.broadcasted_iota(jnp.int32, (LANES, rows), 0) >= HD
    query_at = block_ref[0] * rows + lax.broadcasted_iota(jnp.int32, (length, rows), 1)
    key_at = jnp.concatenate(
        [
            (block_ref[0] ^ place) * rows + lax.broadcasted_iota(jnp.int32, (rows, rows), 0)
            for place in range(4)
        ],
        axis=0,
    )
    allowed = (key_at <= query_at) & (key_at >= start_ref[0, :1, :])
    bias = jnp.where(allowed, 0.0, MASKED)
    cosine, sine = cos_ref[...], sin_ref[...]
    dk_sum[...] = jnp.zeros_like(dk_sum)
    dv_sum[...] = jnp.zeros_like(dv_sum)
    for pair in range(heads // 2):
        at = slice(pair * LANES, (pair + 1) * LANES)
        both = q_ref[:, at]
        back_both = back_ref[:, at]
        parts = []
        for place in range(2):
            owner = (2 * pair + place) // group
            moved = int(owner != place)
            side = upper if place else ~upper
            query = jnp.where(side, both, jnp.zeros_like(both))
            back = jnp.where(side, back_both, jnp.zeros_like(back_both))
            score = dot_nt(keys[moved], query) + bias
            weight = jnp.exp(score - jnp.max(score, axis=0, keepdims=True))
            prob = weight * (1.0 / jnp.sum(weight, axis=0, keepdims=True))
            dv_sum[owner] += dot_nn(prob.astype(BF16), back)
            d_prob = dot_nt(values[moved], back)
            level = jnp.sum(prob * d_prob, axis=0, keepdims=True)
            d_score = (prob * (d_prob - level)).astype(BF16)
            dk_sum[owner] += dot_nn(d_score, query)
            parts.append(dot_nn(keys_t[moved], d_score))
        d_query = jnp.where(upper_t, parts[1], parts[0]).T * SCALE
        dq_ref[:, at] = (d_query * cosine - swap_halves(d_query) * sine).astype(BF16)
    lower_key = lane_of((length, LANES)) < HD
    for total, begin in ((dk_sum, 0), (dv_sum, LANES)):
        first, second = total[0], total[1]
        first = first + pltpu.roll(first, HD, 1)
        second = second + pltpu.roll(second, HD, 1)
        both = jnp.where(lower_key, first, second)
        cols = slice(begin, begin + LANES)
        own_ref[:, cols] = both[:rows]
        for place, ref in enumerate((core_ref, x_ref, far_ref)):
            ref[:, cols] = both[(place + 1) * rows : (place + 2) * rows].astype(BF16)


def parts_of(rows, cols):
    shapes = [jax.ShapeDtypeStruct((rows, cols), F32)] + [jax.ShapeDtypeStruct((rows, cols), BF16)] * 3
    return [seq_rows(0, rows, cols)] * 4, shapes


def attend_back(block, q, kv_pieces, back, start, cosine, sine, rows, seq):
    width = q.shape[1]
    length = 4 * rows
    heads = width // HD
    specs, shapes = parts_of(rows, 2 * LANES)
    return pl.pallas_call(
        attend_back_kernel,
        grid=(1,),
        in_specs=[
            pl.BlockSpec(memory_space=pltpu.SMEM),
            seq_rows(seq, rows, width),
            *[piece_of(seq, rows)] * 4,
            seq_rows(seq, rows, width),
            pl.BlockSpec((1, 8, rows), lambda i: (seq, 0, 0)),
            seq_rows(seq, rows, LANES),
            seq_rows(seq, rows, LANES),
        ],
        out_specs=[seq_rows(0, rows, width), *specs],
        out_shape=[jax.ShapeDtypeStruct((rows, width), BF16), *shapes],
        scratch_shapes=[
            pltpu.VMEM((2, length, LANES), F32),
            pltpu.VMEM((2, length, LANES), F32),
        ],
        compiler_params=pltpu.CompilerParams(vmem_limit_bytes=VMEM_LIMIT),
        cost_estimate=pl.CostEstimate(
            flops=80 * rows * rows * LANES * heads,
            bytes_accessed=8 * rows * width,
            transcendentals=4 * rows * rows * heads,
        ),
        name="attention_backward",
    )(block, q, *kv_pieces, back, start, cosine, sine)


def mlp_kernel(
    n_0, n_1, n_2, n_3, c_0, c_1, c_2, c_3, w_ref,
    own_ref, out_1, out_2, out_3, d_own_ref, d_1, d_2, d_3, kept_ref, turned_ref,
    normed_all, cot_all,
):
    step = pl.program_id(0)
    rows = own_ref.shape[0]
    columns = w_ref.shape[1] // 3

    @pl.when(step == 0)
    def _():
        for place, (n_ref, c_ref) in enumerate(zip((n_0, n_1, n_2, n_3), (c_0, c_1, c_2, c_3))):
            normed_all[place // 2, (place % 2) * rows : (place % 2 + 1) * rows] = n_ref[...]
            cot_all[place // 2, (place % 2) * rows : (place % 2 + 1) * rows] = c_ref[...]

    normed, cot = normed_all[step], cot_all[step]
    for begin in range(0, columns, TILE):
        at = slice(begin, begin + TILE)
        gate = dot_nn(normed, w_ref[:, begin : begin + TILE])
        up = dot_nn(normed, w_ref[:, columns + begin : columns + begin + TILE])
        d_act = dot_nn(cot, w_ref[:, 2 * columns + begin : 2 * columns + begin + TILE])
        sigmoid = 0.5 * jnp.tanh(0.5 * gate) + 0.5
        swish = gate * sigmoid
        kept_ref[0, :, at] = (d_act * up * (sigmoid + swish * (1.0 - sigmoid))).astype(BF16)
        kept_ref[1, :, at] = (d_act * swish).astype(BF16)
        kept_ref[2, :, at] = (swish * up).astype(BF16)
    turned_ref[0] = normed.T
    turned_ref[1] = cot.T
    out = dot_nt(kept_ref[2], w_ref[:, 2 * columns :])
    d_normed = dot_nt(kept_ref[0], w_ref[:, :columns]) + dot_nt(kept_ref[1], w_ref[:, columns : 2 * columns])

    @pl.when(step == 0)
    def _():
        own_ref[...] = out[:rows]
        out_1[...] = out[rows:].astype(BF16)
        d_own_ref[...] = d_normed[:rows]
        d_1[...] = d_normed[rows:].astype(BF16)

    @pl.when(step == 1)
    def _():
        out_2[...] = out[:rows].astype(BF16)
        out_3[...] = out[rows:].astype(BF16)
        d_2[...] = d_normed[:rows].astype(BF16)
        d_3[...] = d_normed[rows:].astype(BF16)


def mlp(normed, cot, weights, seq):
    rows, dim = normed[0].shape
    columns = weights.shape[1] // 3
    specs, shapes = parts_of(rows, dim)
    once = lambda at: pl.BlockSpec((rows, dim), lambda i: (at, 0), pipeline_mode=pl.Buffered(1))
    return pl.pallas_call(
        mlp_kernel,
        grid=(2,),
        in_specs=[
            *[once(0)] * 4,
            *[once(seq)] * 3,
            once(0),
            pl.BlockSpec(weights.shape, lambda i: (0, 0), pipeline_mode=pl.Buffered(1)),
        ],
        out_specs=[
            *specs,
            *specs,
            pl.BlockSpec((3, 2 * rows, columns), lambda i: (0, i, 0)),
            pl.BlockSpec((2, dim, 2 * rows), lambda i: (0, 0, i)),
        ],
        out_shape=[
            *shapes,
            *shapes,
            jax.ShapeDtypeStruct((3, 4 * rows, columns), BF16),
            jax.ShapeDtypeStruct((2, dim, 4 * rows), BF16),
        ],
        scratch_shapes=[
            pltpu.VMEM((2, 2 * rows, dim), BF16),
            pltpu.VMEM((2, 2 * rows, dim), BF16),
        ],
        compiler_params=pltpu.CompilerParams(vmem_limit_bytes=VMEM_LIMIT),
        cost_estimate=pl.CostEstimate(
            flops=48 * rows * dim * columns,
            bytes_accessed=6 * dim * columns + 24 * rows * columns,
            transcendentals=4 * rows * columns,
        ),
        name="feed_forward",
    )(*normed, *cot, weights)


def mlp_grad_kernel(turned_0, turned_1, kept_0, kept_1, grad_ref):
    grad_ref[...] = (dot_nn(turned_0[0], kept_0[0]) + dot_nn(turned_1[0], kept_1[0])).astype(BF16)


def mlp_grad(turned, kept):
    _, dim, count = turned[0].shape
    columns = kept[0].shape[2]
    turned_block = pl.BlockSpec((1, dim, count), lambda i: (i // 2, 0, 0))
    kept_block = pl.BlockSpec((1, count, columns), lambda i: (i, 0, 0))
    return pl.pallas_call(
        mlp_grad_kernel,
        grid=(3,),
        in_specs=[turned_block, turned_block, kept_block, kept_block],
        out_specs=pl.BlockSpec((dim, columns), lambda i: (0, i)),
        out_shape=jax.ShapeDtypeStruct((dim, 3 * columns), BF16),
        compiler_params=pltpu.CompilerParams(vmem_limit_bytes=VMEM_LIMIT),
        cost_estimate=pl.CostEstimate(
            flops=12 * count * dim * columns,
            bytes_accessed=6 * dim * columns + 12 * count * columns,
            transcendentals=0,
        ),
        name="feed_forward_gradients",
    )(*turned, *kept)


def pack_kernel(block_ref, gate_ref, up_ref, down_ref, *refs):
    out_refs, scratch = refs[:4], refs[4]
    shard, ff = gate_ref.shape
    quarter = scratch.shape[2] // 4
    for place, ref in enumerate((gate_ref, up_ref, down_ref)):
        scratch[place, :, :ff] = ref[...].astype(F32)
        scratch[place, :, ff:] = jnp.zeros((shard, 4 * quarter - ff), F32)
    for place, out_ref in enumerate(out_refs):
        begin = pl.multiple_of((block_ref[0] ^ place) * quarter, LANES)
        for part in range(3):
            out_ref[:, part * quarter : (part + 1) * quarter] = scratch[part, :, pl.ds(begin, quarter)].astype(BF16)


def pack(block, gate, up, down_t, quarter):
    shard = gate.shape[0]
    return pl.pallas_call(
        pack_kernel,
        in_specs=[pl.BlockSpec(memory_space=pltpu.SMEM)] + [pl.BlockSpec(memory_space=pltpu.VMEM)] * 3,
        out_specs=[pl.BlockSpec(memory_space=pltpu.VMEM)] * 4,
        out_shape=[jax.ShapeDtypeStruct((shard, 3 * quarter), BF16)] * 4,
        scratch_shapes=[pltpu.VMEM((3, shard, 4 * quarter), F32)],
        compiler_params=pltpu.CompilerParams(vmem_limit_bytes=VMEM_LIMIT),
        name="pack_columns",
    )(block, gate, up, down_t)


def pick(options, index):
    value = options[0]
    for place in range(1, len(options)):
        value = jnp.where(index == place, options[place], value)
    return value


def assemble_kernel(block_ref, *refs):
    pieces, out_ref, scratch = refs[:4], refs[4], refs[5]
    shard = pieces[0].shape[0]
    values = [ref[...].astype(F32) for ref in pieces]
    for owner in range(4):
        scratch[owner * shard : (owner + 1) * shard] = pick(values, block_ref[0] ^ owner)
    out_ref[...] = scratch[...].astype(BF16)


def assemble(block, pieces):
    shard, columns = pieces[0].shape
    return pl.pallas_call(
        assemble_kernel,
        in_specs=[pl.BlockSpec(memory_space=pltpu.SMEM)] + [pl.BlockSpec(memory_space=pltpu.VMEM)] * 4,
        out_specs=pl.BlockSpec(memory_space=pltpu.VMEM),
        out_shape=jax.ShapeDtypeStruct((4 * shard, columns), BF16),
        scratch_shapes=[pltpu.VMEM((4 * shard, columns), F32)],
        compiler_params=pltpu.CompilerParams(vmem_limit_bytes=VMEM_LIMIT),
        name="assemble_rows",
    )(block, *pieces)


def cut_kernel(block_ref, value_ref, *refs):
    out_refs, scratch = refs[:4], refs[4]
    shard = out_refs[0].shape[0]
    scratch[...] = value_ref[...].astype(F32)
    values = [scratch[owner * shard : (owner + 1) * shard] for owner in range(4)]
    for place, out_ref in enumerate(out_refs):
        out_ref[...] = pick(values, block_ref[0] ^ place).astype(BF16)


def cut(block, value):
    shard, columns = value.shape[0] // 4, value.shape[1]
    return pl.pallas_call(
        cut_kernel,
        in_specs=[pl.BlockSpec(memory_space=pltpu.SMEM), pl.BlockSpec(memory_space=pltpu.VMEM)],
        out_specs=[pl.BlockSpec(memory_space=pltpu.VMEM)] * 4,
        out_shape=[jax.ShapeDtypeStruct((shard, columns), BF16)] * 4,
        scratch_shapes=[pltpu.VMEM(value.shape, F32)],
        compiler_params=pltpu.CompilerParams(vmem_limit_bytes=VMEM_LIMIT),
        name="cut_rows",
    )(block, value)


def unpack_kernel(block_ref, *refs):
    pieces, out_refs, scratch = refs[:4], refs[4:7], refs[7]
    ff = out_refs[0].shape[1]
    quarter = scratch.shape[2] // 4
    for place, ref in enumerate(pieces):
        begin = pl.multiple_of((block_ref[0] ^ place) * quarter, LANES)
        for part in range(3):
            scratch[part, :, pl.ds(begin, quarter)] = ref[:, part * quarter : (part + 1) * quarter].astype(F32)
    for part, out_ref in enumerate(out_refs):
        out_ref[...] = scratch[part, :, :ff]


def unpack(block, pieces, ff):
    shard, columns = pieces[0].shape
    return pl.pallas_call(
        unpack_kernel,
        in_specs=[pl.BlockSpec(memory_space=pltpu.SMEM)] + [pl.BlockSpec(memory_space=pltpu.VMEM)] * 4,
        out_specs=[pl.BlockSpec(memory_space=pltpu.VMEM)] * 3,
        out_shape=[jax.ShapeDtypeStruct((shard, ff), F32)] * 3,
        scratch_shapes=[pltpu.VMEM((3, shard, columns // 3 * 4), F32)],
        compiler_params=pltpu.CompilerParams(vmem_limit_bytes=VMEM_LIMIT),
        name="unpack_columns",
    )(block, *pieces)


def bit_swap(value, axis, bit=0):
    size = lax.axis_size(axis)
    return lax.ppermute(value, axis, [(i, i ^ (1 << bit)) for i in range(size)])


def jump_swap(value, axes, jump):
    return lax.ppermute(value, axes, [(i, i ^ jump) for i in range(4)])


def to_plane(value, slot):
    high, low = slot >> 1, slot & 1
    pairs = [
        (4 * y + 2 * x + c, 4 * (c ^ low) + 2 * (x ^ high) + y) for y in range(2) for x in range(2) for c in range(2)
    ]
    return lax.ppermute(value, TOKENS + ("cc",), pairs)


def from_plane(value, slot):
    high, low = slot >> 1, slot & 1
    pairs = [
        (4 * y + 2 * x + c, 4 * c + 2 * (x ^ high) + (y ^ low)) for y in range(2) for x in range(2) for c in range(2)
    ]
    return lax.ppermute(value, TOKENS + ("cc",), pairs)


def after(first, *values):
    return lax.optimization_barrier((first, *values))


def gather_four(value, axes):
    from_first = bit_swap(value, axes[0])
    return [value, bit_swap(value, axes[1]), from_first, bit_swap(from_first, axes[1])]


def gather_direct(value, axes):
    return [value] + [jump_swap(value, axes, jump) for jump in range(1, 4)]


def sum_direct(axes, own, *away):
    return [own] + [jump_swap(value, axes, jump + 1) for jump, value in enumerate(away)]


def doubling_offsets(steps):
    weight = {"cc": 1, "cx": 2, "fy": 4, "fz": 8}
    offsets = [0]
    for axis, bit in steps:
        offsets += [offset ^ (weight[axis] << bit) for offset in offsets]
    return jnp.array(offsets, jnp.int32)


def double(value, axis, bit=0):
    return jnp.concatenate([value, bit_swap(value, axis, bit)], axis=0)


def halve(value, axis, bit=0):
    middle = value.shape[0] // 2
    came = bit_swap(value[middle:], axis, bit)
    return (value[:middle].astype(F32) + came.astype(F32)).astype(BF16)


def on_device(
    hidden,
    segments,
    attn_gain,
    qkv_weight,
    qkv_bias,
    out_weight,
    mlp_gain,
    gate_weight,
    up_weight,
    down_weight,
    cotangent,
):
    seqs, rows, dim = hidden.shape
    count = seqs * rows
    shard = attn_gain.shape[0]
    world = dim // shard
    joint = qkv_weight.shape[1]
    width = joint - 2 * LANES
    ff = gate_weight.shape[1]
    block = lax.axis_index("cx") * lax.axis_size("cc") + lax.axis_index("cc")
    me = lax.axis_index(FSDP) * lax.axis_size(CTX) + block
    offset = block * rows
    block_arg = block.reshape(1).astype(jnp.int32)
    plane_arg = (lax.axis_index("cx") * 2 + lax.axis_index("fy")).reshape(1).astype(jnp.int32)
    x = hidden.reshape(count, dim)
    cot = cotangent.reshape(count, dim)

    cot_x, cot_y = bit_swap(cot, "cx"), bit_swap(cot, "fy")

    far = [("fz", bit) for bit in reversed(range((lax.axis_size("fz")).bit_length() - 1))]
    padded = -(-(shard + 1) // 16) * 16
    small = jnp.concatenate([attn_gain, mlp_gain, qkv_bias])
    small_row = jnp.pad(small, (0, joint + width - small.shape[0]))[None]
    first = jnp.concatenate(
        [
            jnp.concatenate([qkv_weight, out_weight.T], axis=1),
            small_row,
            jnp.zeros((padded - shard - 1, joint + width), BF16),
        ],
        axis=0,
    )
    for axis, bit in far:
        first = double(first, axis, bit)

    quarter = -(-ff // (4 * TILE)) * TILE
    pieces = pack(block_arg, gate_weight, up_weight, down_weight.T, quarter)
    pieces = [to_plane(piece, slot) for slot, piece in enumerate(pieces)]
    within = jnp.arange(padded, dtype=jnp.int32)

    def arrival(steps):
        owner = me ^ doubling_offsets(steps)
        target = jnp.where(within[None, :] < shard, owner[:, None] * shard + within[None, :], -1).reshape(1, -1)
        return owner, (jnp.arange(dim, dtype=jnp.int32)[:, None] == target).astype(BF16)

    owner, order = arrival(far + [("fy", 0), ("cx", 0), ("cc", 0)])
    _, out_order = arrival(far + [("cx", 0), ("fy", 0), ("cc", 0)])
    place = jnp.where(within[None, :] == shard, owner[:, None], -1).reshape(1, -1)
    spread = (jnp.arange(world, dtype=jnp.int32)[:, None] == place).astype(BF16)

    at_row = lax.dynamic_slice_in_dim(segments, offset, rows, axis=1)
    zeros_before = jnp.sum((segments < 1).astype(jnp.int32), axis=1, keepdims=True)
    ones_before = jnp.sum((segments < 2).astype(jnp.int32), axis=1, keepdims=True)
    start = jnp.where(at_row == 0, 0, jnp.where(at_row == 1, zeros_before, ones_before))
    position = (offset + jnp.arange(rows, dtype=jnp.int32)[None, :] - start).reshape(count)
    lane = jnp.arange(LANES, dtype=jnp.int32)
    frequency = ROPE_BASE ** (-(lane % (HD // 2)).astype(F32) * 2.0 / HD)
    angle = position.astype(F32)[:, None] * frequency[None, :]
    cosine = jnp.cos(angle)
    sine = jnp.where(lane % HD < HD // 2, -1.0, 1.0)[None, :] * jnp.sin(angle)
    start_column = jnp.broadcast_to(start.reshape(count, 1), (count, LANES))
    start_row = jnp.broadcast_to(start[:, None, :], (seqs, 8, rows))

    first, cot_x, cot_y = after(first, cot_x, cot_y)
    w_joint, w_out = double(first[:, :joint], "fy"), double(first[:, joint:], "cx")
    w_joint, w_out, order, out_order, spread, cosine, sine, start_column, *pieces = after(
        w_joint, w_out, order, out_order, spread, cosine, sine, start_column, *pieces
    )
    mlp_shard = assemble(plane_arg, pieces)
    mlp_weights = lax.all_gather(mlp_shard, WEIGHTS, axis=0, tiled=True)
    w_joint, w_out = after(double(w_joint, "cx"), double(w_out, "fy"))
    w_joint, w_out = (w_joint, bit_swap(w_joint, "cc")), (w_out, bit_swap(w_out, "cc"))

    normed, q, kv, gain_attn, gain_mlp = prep(x, order, spread, w_joint, cosine, sine, rows)
    kv_all = gather_four(kv.reshape(seqs, rows, 2 * LANES), CTX)
    kv_all[3], far_0, far_1 = after(kv_all[3], cot_x[:rows], cot_y[rows:])
    cot_far = [bit_swap(far_0, "fy"), bit_swap(far_1, "cx")]
    attended, resid, normed_all = [], [], []
    for seq in range(seqs):
        turn = block_arg if seq == 0 else after(attended[0], block_arg)[1]
        attended.append(attend(turn, q, kv_all, start_column, rows, seq))
        if seq == 1:
            attended[1], *cot_far = after(attended[1], *cot_far)
        resid_one, normed_one = project_out(attended[seq], x, w_out, out_order, gain_mlp, rows, seq)
        resid.append(resid_one)
        normed_all.append(gather_direct(normed_one, TOKENS))

    out_parts, d_terms, kept, turned = [], [], [], []
    for seq in range(seqs):
        if seq == 1:
            out_parts[0], normed_all[1] = lax.optimization_barrier((out_parts[0], normed_all[1]))
        result = mlp(normed_all[seq], [cot, cot_x, cot_y, cot_far[seq]], mlp_weights, seq)
        out_parts.append(result[:4])
        d_terms.append(sum_direct(TOKENS, *result[4:8]))
        kept.append(result[8])
        turned.append(result[9])
    turned[1], *d_terms[0] = after(turned[1], *d_terms[0])
    grads = mlp_grad(turned, kept)
    grads, d_terms[0], d_terms[1] = after(grads, *d_terms)
    grads = lax.psum_scatter(
        grads.reshape(world // 4, 4 * shard, 3 * quarter), WEIGHTS, scatter_dimension=0, tiled=False
    )

    d_resid, d_branch, d_attended, mlp_gain_grad = project_out_back(
        d_terms, resid, cot, w_out, out_order, gain_mlp
    )
    out_grad = dot_tn(d_branch, jnp.concatenate(attended, axis=0)).astype(BF16)
    out_grad = halve(out_grad, "cc")
    out_terms = [sum_direct(TOKENS, *after(d_terms[1][1], *part)[1:]) for part in out_parts]
    d_attended, out_terms[0] = after(d_attended, out_terms[0])
    dq, dkv_terms = [], []
    for seq in range(seqs):
        if seq == 1:
            dq[0], d_attended, out_grad, out_terms[1] = after(dq[0], d_attended, out_grad, out_terms[1])
            out_grad = halve(out_grad, "fy")
        result = attend_back(block_arg, q, kv_all, d_attended, start_row, cosine, sine, rows, seq)
        dq.append(result[0])
        dkv_terms.append(sum_direct(CTX, *result[1:]))
    dq[1], out_grad, *dkv_terms[0] = after(dq[1], out_grad, *dkv_terms[0])
    q_grad = dot_tn(normed, jnp.concatenate(dq, axis=0)).astype(BF16)
    q_grad = halve(q_grad, "cc")
    pieces = cut(plane_arg, lax.optimization_barrier(grads))
    dkv_terms[1], pieces, q_grad = lax.optimization_barrier((dkv_terms[1], pieces, q_grad))
    q_grad, out_grad = halve(q_grad, "cx"), halve(out_grad, "cx")
    d_kv, input_grad, attn_gain_grad, bias_grad = input_back(
        dq, dkv_terms, x, d_resid, w_joint, order, gain_attn, cosine, sine
    )
    d_kv, q_grad = after(d_kv, q_grad)

    output = []
    for seq in range(seqs):
        own, *away = out_terms[seq]
        output.append((resid[seq] + own + sum(term.astype(F32) for term in away)).astype(BF16))

    split_at = width + LANES
    bias_grad = jnp.sum(bias_grad, axis=0)
    small_grads = jnp.concatenate(
        [
            jnp.sum(attn_gain_grad, axis=0).reshape(world, -1),
            jnp.sum(mlp_gain_grad, axis=0).reshape(world, -1),
            bias_grad[:split_at].reshape(world, -1),
            bias_grad[split_at:].reshape(world, -1),
        ],
        axis=1,
    ).astype(BF16)
    small_count = small_grads.shape[1]
    small_grads = jnp.pad(small_grads, ((0, 0), (0, 2 * LANES - small_count)))
    kv_grad = dot_tn(
        jnp.concatenate([normed, spread], axis=0), jnp.concatenate([d_kv, small_grads], axis=0)
    ).astype(BF16)
    kv_grad, *pieces = after(halve(kv_grad, "cc"), *pieces)
    kv_grad = halve(kv_grad, "cx")
    joint_grad = halve(jnp.concatenate([q_grad, kv_grad], axis=1), "fy")
    pieces = [from_plane(piece, slot) for slot, piece in enumerate(pieces)]
    first_sum = jnp.concatenate([joint_grad, out_grad], axis=1)
    for axis, bit in reversed(far):
        first_sum = halve(first_sum, axis, bit)
    gate_grad, up_grad, down_grad_t = unpack(block_arg, pieces, ff)
    first_sum = first_sum.astype(F32)
    qkv_sum, out_sum = first_sum[:, :joint], first_sum[:, joint:]
    small_sum = qkv_sum[shard, width : width + small_count]
    at = (shard, 2 * shard, 2 * shard + split_at // world)

    return (
        jnp.stack(output),
        input_grad.reshape(hidden.shape),
        small_sum[: at[0]],
        qkv_sum[:shard],
        small_sum[at[1] : at[2]],
        small_sum[at[2] :],
        out_sum[:shard].T,
        small_sum[at[0] : at[1]],
        gate_grad,
        up_grad,
        down_grad_t.T,
    )


def solution(mesh):
    fsdp, ctx = mesh.shape["fsdp"], mesh.shape["ctx"]
    inner = Mesh(mesh.devices.reshape(fsdp // 2, 2, 2, ctx // 2), AXES)
    tokens = P(FSDP, CTX, None)
    vector = P(AXES)
    by_row = P(AXES, None)
    by_column = P(None, AXES)
    return jax.shard_map(
        on_device,
        mesh=inner,
        in_specs=(
            tokens,
            P(FSDP, None),
            vector,
            by_row,
            vector,
            by_column,
            vector,
            by_row,
            by_row,
            by_column,
            tokens,
        ),
        out_specs=(
            tokens,
            tokens,
            vector,
            by_row,
            vector,
            vector,
            by_column,
            vector,
            by_row,
            by_row,
            by_column,
        ),
        check_vma=False,
    )
```

```python
import functools

import jax
import jax.numpy as jnp
from jax import lax
from jax.experimental import pallas as pl
from jax.experimental.pallas import tpu as pltpu
from jax.sharding import Mesh
from jax.sharding import PartitionSpec as P

HD = 64
LANES = 128
EPSILON = 1e-06
ROPE_BASE = 1000000.0
MASKED = -1e30
SCALE = HD ** (-0.5)
TILE = 256
MIB = 1 << 20
VMEM_LIMIT = 60 * MIB
F32 = jnp.float32
BF16 = jnp.bfloat16
AXES = ("fz", "fy", "cx", "cc")
FSDP = ("fz", "fy")
CTX = ("cx", "cc")
TOKENS = ("fy", "cx")
WEIGHTS = ("fz", "cc")


def dot_nn(a, b):
    return lax.dot_general(a, b, (((1,), (0,)), ((), ())), preferred_element_type=F32)


def dot_nt(a, b):
    return lax.dot_general(a, b, (((1,), (1,)), ((), ())), preferred_element_type=F32)


def dot_tn(a, b):
    return lax.dot_general(a, b, (((0,), (0,)), ((), ())), preferred_element_type=F32)


def lane_of(shape):
    return lax.broadcasted_iota(jnp.int32, shape, len(shape) - 1)


def swap_halves(block):
    lead = lane_of(block.shape) % HD < HD // 2
    return jnp.where(
        lead, pltpu.roll(block, LANES - HD // 2, 1), pltpu.roll(block, HD // 2, 1)
    )


def other_head(block):
    return jnp.concatenate([block[:, HD:], block[:, :HD]], axis=1)


def read_out(extras, first, piece, total):
    owners, columns = extras.shape
    at = lax.broadcasted_iota(jnp.int32, (columns, total), 1) % piece + first
    chosen = (lax.broadcasted_iota(jnp.int32, (columns, total), 0) == at).astype(BF16)
    spread = dot_nn(extras, chosen)
    owner = lax.broadcasted_iota(jnp.int32, (owners, total), 1) // piece
    mine = owner == lax.broadcasted_iota(jnp.int32, (owners, total), 0)
    return jnp.sum(jnp.where(mine, spread, 0.0), axis=0, keepdims=True)


def prep_kernel(
    x_ref, order_ref, spread_ref, w_low_ref, w_high_ref, cos_ref, sin_ref,
    normed_ref, q_ref, kv_ref, gain_ref, gain_mlp_ref, bias_ref,
):
    x = x_ref[...].astype(F32)
    dim = x.shape[1]
    width = q_ref.shape[1]
    joint = w_low_ref.shape[1]
    middle = w_low_ref.shape[0]
    owners = spread_ref.shape[0]

    @pl.when(pl.program_id(0) == 0)
    def _():
        extras = dot_nn(spread_ref[:, :middle], w_low_ref[:, :LANES])
        extras = (extras + dot_nn(spread_ref[:, middle:], w_high_ref[:, :LANES])).astype(BF16)
        shard = dim // owners
        gain_ref[...] = read_out(extras, 0, shard, dim)
        gain_mlp_ref[...] = read_out(extras, shard, shard, dim)
        bias_ref[...] = read_out(extras, 2 * shard, joint // owners, joint)

    gain, bias = gain_ref[...], bias_ref[...]
    inverse = lax.rsqrt(jnp.mean(x * x, axis=-1, keepdims=True) + EPSILON)
    normed = (x * inverse * gain).astype(BF16)
    ordered = dot_nn(normed, order_ref[...]).astype(BF16)
    normed_ref[...] = ordered
    joined = dot_nn(ordered[:, :middle], w_low_ref[...])
    joined = joined + dot_nn(ordered[:, middle:], w_high_ref[...]) + bias
    cosine, sine = cos_ref[...], sin_ref[...]
    for begin in range(0, width + LANES, LANES):
        block = joined[:, begin : begin + LANES]
        turned = block * cosine + swap_halves(block) * sine
        if begin < width:
            q_ref[:, begin : begin + LANES] = (turned * SCALE).astype(BF16)
        else:
            kv_ref[:, :LANES] = turned.astype(BF16)
    kv_ref[:, LANES:] = joined[:, width + LANES :].astype(BF16)


def rows_of(rows, cols):
    return pl.BlockSpec((rows, cols), lambda i: (i, 0))


def whole(value):
    return pl.BlockSpec(value.shape, lambda i: (0,) * value.ndim)


def prep(x, order, spread, weights, cosine, sine, rows):
    count, dim = x.shape
    ordered = order.shape[1]
    joint = weights[0].shape[1]
    width = joint - 2 * LANES
    row = pl.BlockSpec((1, dim), lambda i: (0, 0))
    return pl.pallas_call(
        prep_kernel,
        grid=(count // rows,),
        in_specs=[
            rows_of(rows, dim),
            whole(order),
            whole(spread),
            whole(weights[0]),
            whole(weights[1]),
            rows_of(rows, LANES),
            rows_of(rows, LANES),
        ],
        out_specs=[rows_of(rows, ordered), rows_of(rows, width), rows_of(rows, 2 * LANES), row, row],
        out_shape=[
            jax.ShapeDtypeStruct((count, ordered), BF16),
            jax.ShapeDtypeStruct((count, width), BF16),
            jax.ShapeDtypeStruct((count, 2 * LANES), BF16),
            jax.ShapeDtypeStruct((1, dim), F32),
            jax.ShapeDtypeStruct((1, dim), F32),
        ],
        scratch_shapes=[pltpu.VMEM((1, joint), F32)],
        compiler_params=pltpu.CompilerParams(vmem_limit_bytes=VMEM_LIMIT),
        cost_estimate=pl.CostEstimate(
            flops=2 * count * ordered * (joint + dim), bytes_accessed=12 * MIB, transcendentals=0
        ),
        name="norm_project_rotate",
    )(x, order, spread, weights[0], weights[1], cosine, sine)


def back_in_order(value, order):
    high = value.astype(BF16)
    low = (value - high.astype(F32)).astype(BF16)
    return dot_nt(high, order) + dot_nt(low, order)


def out_kernel(attended_ref, x_ref, w_low_ref, w_high_ref, order_ref, gain_ref, resid_ref, normed_ref):
    attended = attended_ref[...]
    branch = jnp.concatenate([dot_nt(attended, w_low_ref[...]), dot_nt(attended, w_high_ref[...])], axis=1)
    resid = x_ref[...].astype(F32) + back_in_order(branch, order_ref[...])
    inverse = lax.rsqrt(jnp.mean(resid * resid, axis=-1, keepdims=True) + EPSILON)
    resid_ref[...] = resid
    normed_ref[...] = (resid * inverse * gain_ref[...]).astype(BF16)


def project_out(attended, x, weights, order, gain, rows, seq):
    dim = x.shape[1]
    count = rows
    return pl.pallas_call(
        out_kernel,
        grid=(1,),
        in_specs=[
            rows_of(rows, attended.shape[1]),
            pl.BlockSpec((rows, dim), lambda i: (seq, 0)),
            whole(weights[0]),
            whole(weights[1]),
            whole(order),
            whole(gain),
        ],
        out_specs=[rows_of(rows, dim), rows_of(rows, dim)],
        out_shape=[jax.ShapeDtypeStruct((count, dim), F32), jax.ShapeDtypeStruct((count, dim), BF16)],
        compiler_params=pltpu.CompilerParams(vmem_limit_bytes=VMEM_LIMIT),
        cost_estimate=pl.CostEstimate(flops=6 * count * dim * dim, bytes_accessed=8 * MIB, transcendentals=0),
        name="project_out_norm",
    )(attended, x, weights[0], weights[1], order, gain)


def sum_rows(value):
    return jnp.sum(value, axis=0, keepdims=True)


def norm_back(values, inverse, gain, incoming):
    scaled = incoming * gain
    mean_term = jnp.mean(scaled * values, axis=-1, keepdims=True)
    return inverse * scaled - values * inverse**3 * mean_term


def total_of(own_ref, *away_refs):
    total = own_ref[...]
    for ref in away_refs:
        total = total + ref[...].astype(F32)
    return total


def out_back_kernel(*refs):
    terms, resids = refs[:8], refs[8:10]
    cot_ref, w_low_ref, w_high_ref, order_ref, gain_ref = refs[10:15]
    d_resid_ref, d_branch_ref, d_attended_ref, gain_grad_ref = refs[15:]
    middle = w_low_ref.shape[0]
    d_normed = jnp.concatenate([total_of(*terms[:4]), total_of(*terms[4:])], axis=0)
    resid = jnp.concatenate([ref[...] for ref in resids], axis=0)
    inverse = lax.rsqrt(jnp.mean(resid * resid, axis=-1, keepdims=True) + EPSILON)
    d_resid = cot_ref[...].astype(F32) + norm_back(resid, inverse, gain_ref[...], d_normed)
    d_resid_ref[...] = d_resid
    d_branch = dot_nn(d_resid.astype(BF16), order_ref[...]).astype(BF16)
    d_branch_ref[...] = d_branch
    d_attended = dot_nn(d_branch[:, :middle], w_low_ref[...])
    d_attended = d_attended + dot_nn(d_branch[:, middle:], w_high_ref[...])
    d_attended_ref[...] = d_attended.astype(BF16)
    gain_grad_ref[...] = sum_rows(d_normed * resid * inverse)


def call_whole(kernel, operands, out_shape, flops, name):
    return pl.pallas_call(
        kernel,
        in_specs=[pl.BlockSpec(memory_space=pltpu.VMEM)] * len(operands),
        out_specs=[pl.BlockSpec(memory_space=pltpu.VMEM)] * len(out_shape),
        out_shape=out_shape,
        compiler_params=pltpu.CompilerParams(vmem_limit_bytes=VMEM_LIMIT),
        cost_estimate=pl.CostEstimate(flops=flops, bytes_accessed=16 * MIB, transcendentals=0),
        name=name,
    )(*operands)


def project_out_back(terms, resid, cot, weights, order, gain):
    count, dim = cot.shape
    ordered = order.shape[1]
    return call_whole(
        out_back_kernel,
        (*terms[0], *terms[1], *resid, cot, *weights, order, gain),
        [
            jax.ShapeDtypeStruct((count, dim), F32),
            jax.ShapeDtypeStruct((count, ordered), BF16),
            jax.ShapeDtypeStruct((count, weights[0].shape[1]), BF16),
            jax.ShapeDtypeStruct((1, dim), F32),
        ],
        4 * count * dim * dim,
        "norm_back_project",
    )


def input_back_kernel(*refs):
    dqs, terms = refs[:2], refs[2:10]
    x_ref, d_resid_ref, w_low_ref, w_high_ref, order_ref, gain_ref, cos_ref, sin_ref = refs[10:18]
    d_kv_ref, input_grad_ref, gain_grad_ref, bias_grad_ref = refs[18:]
    dkv = jnp.concatenate([total_of(*terms[:4]), total_of(*terms[4:])], axis=0)
    dk = dkv[:, :LANES]
    dk = dk * cos_ref[...] - swap_halves(dk) * sin_ref[...]
    d_kv = jnp.concatenate([dk.astype(BF16), dkv[:, LANES:].astype(BF16)], axis=1)
    d_kv_ref[...] = d_kv
    dq = jnp.concatenate([ref[...] for ref in dqs], axis=0)
    d_joined = jnp.concatenate([dq, d_kv], axis=1)
    d_normed = jnp.concatenate([dot_nt(d_joined, w_low_ref[...]), dot_nt(d_joined, w_high_ref[...])], axis=1)
    d_normed = back_in_order(d_normed, order_ref[...])
    x = x_ref[...].astype(F32)
    inverse = lax.rsqrt(jnp.mean(x * x, axis=-1, keepdims=True) + EPSILON)
    input_grad_ref[...] = (d_resid_ref[...] + norm_back(x, inverse, gain_ref[...], d_normed)).astype(BF16)
    gain_grad_ref[...] = sum_rows(d_normed * x * inverse)
    bias_grad_ref[...] = sum_rows(d_joined.astype(F32))


def input_back(dq, terms, x, d_resid, weights, order, gain, cosine, sine):
    count, dim = x.shape
    joint = dq[0].shape[1] + 2 * LANES
    return call_whole(
        input_back_kernel,
        (*dq, *terms[0], *terms[1], x, d_resid, *weights, order, gain, cosine, sine),
        [
            jax.ShapeDtypeStruct((count, 2 * LANES), BF16),
            jax.ShapeDtypeStruct((count, dim), BF16),
            jax.ShapeDtypeStruct((1, dim), F32),
            jax.ShapeDtypeStruct((1, joint), F32),
        ],
        6 * count * dim * joint,
        "input_gradient",
    )


def seq_rows(seq, rows, cols):
    return pl.BlockSpec((rows, cols), lambda i: (seq, 0))


def piece_of(seq, rows):
    return pl.BlockSpec((1, rows, 2 * LANES), lambda i: (seq, 0, 0))


def keys_and_values(piece_refs):
    joint = jnp.concatenate([ref[0] for ref in piece_refs], axis=0)
    key, value = joint[:, :LANES], joint[:, LANES:]
    return (key, other_head(key)), (value, other_head(value))


def attend_kernel(block_ref, q_ref, kv_0, kv_1, kv_2, kv_3, start_ref, out_ref):
    rows, width = q_ref.shape
    length = 4 * rows
    heads = width // HD
    group = heads // 2
    keys, values = keys_and_values((kv_0, kv_1, kv_2, kv_3))
    upper_key = lane_of((length, LANES)) >= HD
    upper = lane_of((rows, LANES)) >= HD
    query_at = block_ref[0] * rows + lax.broadcasted_iota(jnp.int32, (rows, length), 0)
    key_at = jnp.concatenate(
        [
            (block_ref[0] ^ place) * rows + lax.broadcasted_iota(jnp.int32, (rows, rows), 1)
            for place in range(4)
        ],
        axis=1,
    )
    allowed = (key_at <= query_at) & (key_at >= start_ref[:, :1])
    bias = jnp.where(allowed, 0.0, MASKED)
    one = jnp.ones((), BF16)
    for pair in range(heads // 2):
        at = slice(pair * LANES, (pair + 1) * LANES)
        both = q_ref[:, at]
        parts = []
        for place in range(2):
            owner = (2 * pair + place) // group
            moved = int(owner != place)
            side = upper if place else ~upper
            side_key = upper_key if place else ~upper_key
            query = jnp.where(side, both, jnp.zeros_like(both))
            score = dot_nt(query, keys[moved]) + bias
            top = jnp.max(score, axis=1, keepdims=True)
            weight = jnp.exp(score - top).astype(BF16)
            mixed = dot_nn(weight, jnp.where(side_key, values[moved], one))
            parts.append(mixed / pltpu.roll(mixed, HD, 1))
        out_ref[:, at] = jnp.where(upper, parts[1], parts[0]).astype(BF16)


def attend(block, q, kv_pieces, start, rows, seq):
    width = q.shape[1]
    heads = width // HD
    return pl.pallas_call(
        attend_kernel,
        grid=(1,),
        in_specs=[
            pl.BlockSpec(memory_space=pltpu.SMEM),
            seq_rows(seq, rows, width),
            *[piece_of(seq, rows)] * 4,
            seq_rows(seq, rows, LANES),
        ],
        out_specs=seq_rows(0, rows, width),
        out_shape=jax.ShapeDtypeStruct((rows, width), BF16),
        compiler_params=pltpu.CompilerParams(vmem_limit_bytes=VMEM_LIMIT),
        cost_estimate=pl.CostEstimate(
            flops=32 * rows * rows * LANES * heads,
            bytes_accessed=4 * rows * width,
            transcendentals=4 * rows * rows * heads,
        ),
        name="attention_forward",
    )(block, q, *kv_pieces, start)


def attend_back_kernel(
    block_ref, q_ref, kv_0, kv_1, kv_2, kv_3, back_ref, start_ref, cos_ref, sin_ref,
    dq_ref, own_ref, core_ref, x_ref, far_ref, dk_sum, dv_sum,
):
    rows, width = q_ref.shape
    length = 4 * rows
    heads = width // HD
    group = heads // 2
    keys, values = keys_and_values((kv_0, kv_1, kv_2, kv_3))
    key_t = keys[0].astype(F32).T.astype(BF16)
    keys_t = (key_t, jnp.concatenate([key_t[HD:], key_t[:HD]], axis=0))
    upper = lane_of((rows, LANES)) >= HD
    upper_t = lax.broadcasted_iota(jnp.int32, (LANES, rows), 0) >= HD
    query_at = block_ref[0] * rows + lax.broadcasted_iota(jnp.int32, (length, rows), 1)
    key_at = jnp.concatenate(
        [
            (block_ref[0] ^ place) * rows + lax.broadcasted_iota(jnp.int32, (rows, rows), 0)
            for place in range(4)
        ],
        axis=0,
    )
    allowed = (key_at <= query_at) & (key_at >= start_ref[0, :1, :])
    bias = jnp.where(allowed, 0.0, MASKED)
    cosine, sine = cos_ref[...], sin_ref[...]
    dk_sum[...] = jnp.zeros_like(dk_sum)
    dv_sum[...] = jnp.zeros_like(dv_sum)
    for pair in range(heads // 2):
        at = slice(pair * LANES, (pair + 1) * LANES)
        both = q_ref[:, at]
        back_both = back_ref[:, at]
        parts = []
        for place in range(2):
            owner = (2 * pair + place) // group
            moved = int(owner != place)
            side = upper if place else ~upper
            query = jnp.where(side, both, jnp.zeros_like(both))
            back = jnp.where(side, back_both, jnp.zeros_like(back_both))
            score = dot_nt(keys[moved], query) + bias
            weight = jnp.exp(score - jnp.max(score, axis=0, keepdims=True))
            prob = weight * (1.0 / jnp.sum(weight, axis=0, keepdims=True))
            dv_sum[owner] += dot_nn(prob.astype(BF16), back)
            d_prob = dot_nt(values[moved], back)
            level = jnp.sum(prob * d_prob, axis=0, keepdims=True)
            d_score = (prob * (d_prob - level)).astype(BF16)
            dk_sum[owner] += dot_nn(d_score, query)
            parts.append(dot_nn(keys_t[moved], d_score))
        d_query = jnp.where(upper_t, parts[1], parts[0]).T * SCALE
        dq_ref[:, at] = (d_query * cosine - swap_halves(d_query) * sine).astype(BF16)
    lower_key = lane_of((length, LANES)) < HD
    for total, begin in ((dk_sum, 0), (dv_sum, LANES)):
        first, second = total[0], total[1]
        first = first + pltpu.roll(first, HD, 1)
        second = second + pltpu.roll(second, HD, 1)
        both = jnp.where(lower_key, first, second)
        cols = slice(begin, begin + LANES)
        own_ref[:, cols] = both[:rows]
        for place, ref in enumerate((core_ref, x_ref, far_ref)):
            ref[:, cols] = both[(place + 1) * rows : (place + 2) * rows].astype(BF16)


def parts_of(rows, cols):
    shapes = [jax.ShapeDtypeStruct((rows, cols), F32)] + [jax.ShapeDtypeStruct((rows, cols), BF16)] * 3
    return [seq_rows(0, rows, cols)] * 4, shapes


def attend_back(block, q, kv_pieces, back, start, cosine, sine, rows, seq):
    width = q.shape[1]
    length = 4 * rows
    heads = width // HD
    specs, shapes = parts_of(rows, 2 * LANES)
    return pl.pallas_call(
        attend_back_kernel,
        grid=(1,),
        in_specs=[
            pl.BlockSpec(memory_space=pltpu.SMEM),
            seq_rows(seq, rows, width),
            *[piece_of(seq, rows)] * 4,
            seq_rows(seq, rows, width),
            pl.BlockSpec((1, 8, rows), lambda i: (seq, 0, 0)),
            seq_rows(seq, rows, LANES),
            seq_rows(seq, rows, LANES),
        ],
        out_specs=[seq_rows(0, rows, width), *specs],
        out_shape=[jax.ShapeDtypeStruct((rows, width), BF16), *shapes],
        scratch_shapes=[
            pltpu.VMEM((2, length, LANES), F32),
            pltpu.VMEM((2, length, LANES), F32),
        ],
        compiler_params=pltpu.CompilerParams(vmem_limit_bytes=VMEM_LIMIT),
        cost_estimate=pl.CostEstimate(
            flops=80 * rows * rows * LANES * heads,
            bytes_accessed=8 * rows * width,
            transcendentals=4 * rows * rows * heads,
        ),
        name="attention_backward",
    )(block, q, *kv_pieces, back, start, cosine, sine)


def mlp_kernel(
    n_0, n_1, n_2, n_3, c_0, c_1, c_2, c_3, w_ref,
    own_ref, out_1, out_2, out_3, d_own_ref, d_1, d_2, d_3, kept_ref, turned_ref,
    normed_all, cot_all,
):
    step = pl.program_id(0)
    rows = own_ref.shape[0]
    columns = w_ref.shape[1] // 3

    @pl.when(step == 0)
    def _():
        for place, (n_ref, c_ref) in enumerate(zip((n_0, n_1, n_2, n_3), (c_0, c_1, c_2, c_3))):
            normed_all[place // 2, (place % 2) * rows : (place % 2 + 1) * rows] = n_ref[...]
            cot_all[place // 2, (place % 2) * rows : (place % 2 + 1) * rows] = c_ref[...]

    normed, cot = normed_all[step], cot_all[step]
    for begin in range(0, columns, TILE):
        at = slice(begin, begin + TILE)
        gate = dot_nn(normed, w_ref[:, begin : begin + TILE])
        up = dot_nn(normed, w_ref[:, columns + begin : columns + begin + TILE])
        d_act = dot_nn(cot, w_ref[:, 2 * columns + begin : 2 * columns + begin + TILE])
        sigmoid = 0.5 * jnp.tanh(0.5 * gate) + 0.5
        swish = gate * sigmoid
        kept_ref[0, :, at] = (d_act * up * (sigmoid + swish * (1.0 - sigmoid))).astype(BF16)
        kept_ref[1, :, at] = (d_act * swish).astype(BF16)
        kept_ref[2, :, at] = (swish * up).astype(BF16)
    turned_ref[0] = normed.T
    turned_ref[1] = cot.T
    out = dot_nt(kept_ref[2], w_ref[:, 2 * columns :])
    d_normed = dot_nt(kept_ref[0], w_ref[:, :columns]) + dot_nt(kept_ref[1], w_ref[:, columns : 2 * columns])

    @pl.when(step == 0)
    def _():
        own_ref[...] = out[:rows]
        out_1[...] = out[rows:].astype(BF16)
        d_own_ref[...] = d_normed[:rows]
        d_1[...] = d_normed[rows:].astype(BF16)

    @pl.when(step == 1)
    def _():
        out_2[...] = out[:rows].astype(BF16)
        out_3[...] = out[rows:].astype(BF16)
        d_2[...] = d_normed[:rows].astype(BF16)
        d_3[...] = d_normed[rows:].astype(BF16)


def mlp(normed, cot, weights, seq):
    rows, dim = normed[0].shape
    columns = weights.shape[1] // 3
    specs, shapes = parts_of(rows, dim)
    once = lambda at: pl.BlockSpec((rows, dim), lambda i: (at, 0), pipeline_mode=pl.Buffered(1))
    return pl.pallas_call(
        mlp_kernel,
        grid=(2,),
        in_specs=[
            *[once(0)] * 4,
            *[once(seq)] * 3,
            once(0),
            pl.BlockSpec(weights.shape, lambda i: (0, 0), pipeline_mode=pl.Buffered(1)),
        ],
        out_specs=[
            *specs,
            *specs,
            pl.BlockSpec((3, 2 * rows, columns), lambda i: (0, i, 0)),
            pl.BlockSpec((2, dim, 2 * rows), lambda i: (0, 0, i)),
        ],
        out_shape=[
            *shapes,
            *shapes,
            jax.ShapeDtypeStruct((3, 4 * rows, columns), BF16),
            jax.ShapeDtypeStruct((2, dim, 4 * rows), BF16),
        ],
        scratch_shapes=[
            pltpu.VMEM((2, 2 * rows, dim), BF16),
            pltpu.VMEM((2, 2 * rows, dim), BF16),
        ],
        compiler_params=pltpu.CompilerParams(vmem_limit_bytes=VMEM_LIMIT),
        cost_estimate=pl.CostEstimate(
            flops=48 * rows * dim * columns,
            bytes_accessed=6 * dim * columns + 24 * rows * columns,
            transcendentals=4 * rows * columns,
        ),
        name="feed_forward",
    )(*normed, *cot, weights)


def mlp_grad_kernel(turned_0, turned_1, kept_0, kept_1, grad_ref):
    grad_ref[...] = (dot_nn(turned_0[0], kept_0[0]) + dot_nn(turned_1[0], kept_1[0])).astype(BF16)


def mlp_grad(turned, kept):
    _, dim, count = turned[0].shape
    columns = kept[0].shape[2]
    turned_block = pl.BlockSpec((1, dim, count), lambda i: (i // 2, 0, 0))
    kept_block = pl.BlockSpec((1, count, columns), lambda i: (i, 0, 0))
    return pl.pallas_call(
        mlp_grad_kernel,
        grid=(3,),
        in_specs=[turned_block, turned_block, kept_block, kept_block],
        out_specs=pl.BlockSpec((dim, columns), lambda i: (0, i)),
        out_shape=jax.ShapeDtypeStruct((dim, 3 * columns), BF16),
        compiler_params=pltpu.CompilerParams(vmem_limit_bytes=VMEM_LIMIT),
        cost_estimate=pl.CostEstimate(
            flops=12 * count * dim * columns,
            bytes_accessed=6 * dim * columns + 12 * count * columns,
            transcendentals=0,
        ),
        name="feed_forward_gradients",
    )(*turned, *kept)


def pack_kernel(block_ref, gate_ref, up_ref, down_ref, *refs):
    out_refs, scratch = refs[:4], refs[4]
    shard, ff = gate_ref.shape
    quarter = scratch.shape[2] // 4
    for place, ref in enumerate((gate_ref, up_ref, down_ref)):
        scratch[place, :, :ff] = ref[...].astype(F32)
        scratch[place, :, ff:] = jnp.zeros((shard, 4 * quarter - ff), F32)
    for place, out_ref in enumerate(out_refs):
        begin = pl.multiple_of((block_ref[0] ^ place) * quarter, LANES)
        for part in range(3):
            out_ref[:, part * quarter : (part + 1) * quarter] = scratch[part, :, pl.ds(begin, quarter)].astype(BF16)


def pack(block, gate, up, down_t, quarter):
    shard = gate.shape[0]
    return pl.pallas_call(
        pack_kernel,
        in_specs=[pl.BlockSpec(memory_space=pltpu.SMEM)] + [pl.BlockSpec(memory_space=pltpu.VMEM)] * 3,
        out_specs=[pl.BlockSpec(memory_space=pltpu.VMEM)] * 4,
        out_shape=[jax.ShapeDtypeStruct((shard, 3 * quarter), BF16)] * 4,
        scratch_shapes=[pltpu.VMEM((3, shard, 4 * quarter), F32)],
        compiler_params=pltpu.CompilerParams(vmem_limit_bytes=VMEM_LIMIT),
        name="pack_columns",
    )(block, gate, up, down_t)


def pick(options, index):
    value = options[0]
    for place in range(1, len(options)):
        value = jnp.where(index == place, options[place], value)
    return value


def assemble_kernel(block_ref, *refs):
    pieces, out_ref, scratch = refs[:4], refs[4], refs[5]
    shard = pieces[0].shape[0]
    values = [ref[...].astype(F32) for ref in pieces]
    for owner in range(4):
        scratch[owner * shard : (owner + 1) * shard] = pick(values, block_ref[0] ^ owner)
    out_ref[...] = scratch[...].astype(BF16)


def assemble(block, pieces):
    shard, columns = pieces[0].shape
    return pl.pallas_call(
        assemble_kernel,
        in_specs=[pl.BlockSpec(memory_space=pltpu.SMEM)] + [pl.BlockSpec(memory_space=pltpu.VMEM)] * 4,
        out_specs=pl.BlockSpec(memory_space=pltpu.VMEM),
        out_shape=jax.ShapeDtypeStruct((4 * shard, columns), BF16),
        scratch_shapes=[pltpu.VMEM((4 * shard, columns), F32)],
        compiler_params=pltpu.CompilerParams(vmem_limit_bytes=VMEM_LIMIT),
        name="assemble_rows",
    )(block, *pieces)


def cut_kernel(block_ref, value_ref, *refs):
    out_refs, scratch = refs[:4], refs[4]
    shard = out_refs[0].shape[0]
    scratch[...] = value_ref[...].astype(F32)
    values = [scratch[owner * shard : (owner + 1) * shard] for owner in range(4)]
    for place, out_ref in enumerate(out_refs):
        out_ref[...] = pick(values, block_ref[0] ^ place).astype(BF16)


def cut(block, value):
    shard, columns = value.shape[0] // 4, value.shape[1]
    return pl.pallas_call(
        cut_kernel,
        in_specs=[pl.BlockSpec(memory_space=pltpu.SMEM), pl.BlockSpec(memory_space=pltpu.VMEM)],
        out_specs=[pl.BlockSpec(memory_space=pltpu.VMEM)] * 4,
        out_shape=[jax.ShapeDtypeStruct((shard, columns), BF16)] * 4,
        scratch_shapes=[pltpu.VMEM(value.shape, F32)],
        compiler_params=pltpu.CompilerParams(vmem_limit_bytes=VMEM_LIMIT),
        name="cut_rows",
    )(block, value)


def unpack_kernel(block_ref, *refs):
    pieces, out_refs, scratch = refs[:4], refs[4:7], refs[7]
    ff = out_refs[0].shape[1]
    quarter = scratch.shape[2] // 4
    for place, ref in enumerate(pieces):
        begin = pl.multiple_of((block_ref[0] ^ place) * quarter, LANES)
        for part in range(3):
            scratch[part, :, pl.ds(begin, quarter)] = ref[:, part * quarter : (part + 1) * quarter].astype(F32)
    for part, out_ref in enumerate(out_refs):
        out_ref[...] = scratch[part, :, :ff]


def unpack(block, pieces, ff):
    shard, columns = pieces[0].shape
    return pl.pallas_call(
        unpack_kernel,
        in_specs=[pl.BlockSpec(memory_space=pltpu.SMEM)] + [pl.BlockSpec(memory_space=pltpu.VMEM)] * 4,
        out_specs=[pl.BlockSpec(memory_space=pltpu.VMEM)] * 3,
        out_shape=[jax.ShapeDtypeStruct((shard, ff), F32)] * 3,
        scratch_shapes=[pltpu.VMEM((3, shard, columns // 3 * 4), F32)],
        compiler_params=pltpu.CompilerParams(vmem_limit_bytes=VMEM_LIMIT),
        name="unpack_columns",
    )(block, *pieces)


def bit_swap(value, axis, bit=0):
    size = lax.axis_size(axis)
    return lax.ppermute(value, axis, [(i, i ^ (1 << bit)) for i in range(size)])


def jump_swap(value, axes, jump):
    return lax.ppermute(value, axes, [(i, i ^ jump) for i in range(4)])


def to_plane(value, slot):
    high, low = slot >> 1, slot & 1
    pairs = [
        (4 * y + 2 * x + c, 4 * (c ^ low) + 2 * (x ^ high) + y) for y in range(2) for x in range(2) for c in range(2)
    ]
    return lax.ppermute(value, TOKENS + ("cc",), pairs)


def from_plane(value, slot):
    high, low = slot >> 1, slot & 1
    pairs = [
        (4 * y + 2 * x + c, 4 * c + 2 * (x ^ high) + (y ^ low)) for y in range(2) for x in range(2) for c in range(2)
    ]
    return lax.ppermute(value, TOKENS + ("cc",), pairs)


def after(first, *values):
    return lax.optimization_barrier((first, *values))


def gather_four(value, axes):
    from_first = bit_swap(value, axes[0])
    return [value, bit_swap(value, axes[1]), from_first, bit_swap(from_first, axes[1])]


def gather_direct(value, axes):
    return [value] + [jump_swap(value, axes, jump) for jump in range(1, 4)]


def sum_direct(axes, own, *away):
    return [own] + [jump_swap(value, axes, jump + 1) for jump, value in enumerate(away)]


def doubling_offsets(steps):
    weight = {"cc": 1, "cx": 2, "fy": 4, "fz": 8}
    offsets = [0]
    for axis, bit in steps:
        offsets += [offset ^ (weight[axis] << bit) for offset in offsets]
    return jnp.array(offsets, jnp.int32)


def double(value, axis, bit=0):
    return jnp.concatenate([value, bit_swap(value, axis, bit)], axis=0)


def halve(value, axis, bit=0):
    middle = value.shape[0] // 2
    came = bit_swap(value[middle:], axis, bit)
    return (value[:middle].astype(F32) + came.astype(F32)).astype(BF16)


def on_device(
    hidden,
    segments,
    attn_gain,
    qkv_weight,
    qkv_bias,
    out_weight,
    mlp_gain,
    gate_weight,
    up_weight,
    down_weight,
    cotangent,
):
    seqs, rows, dim = hidden.shape
    count = seqs * rows
    shard = attn_gain.shape[0]
    world = dim // shard
    joint = qkv_weight.shape[1]
    width = joint - 2 * LANES
    ff = gate_weight.shape[1]
    block = lax.axis_index("cx") * lax.axis_size("cc") + lax.axis_index("cc")
    me = lax.axis_index(FSDP) * lax.axis_size(CTX) + block
    offset = block * rows
    block_arg = block.reshape(1).astype(jnp.int32)
    plane_arg = (lax.axis_index("cx") * 2 + lax.axis_index("fy")).reshape(1).astype(jnp.int32)
    x = hidden.reshape(count, dim)
    cot = cotangent.reshape(count, dim)

    far = [("fz", bit) for bit in reversed(range((lax.axis_size("fz")).bit_length() - 1))]
    padded = -(-(shard + 1) // 16) * 16
    small = jnp.concatenate([attn_gain, mlp_gain, qkv_bias])
    small_row = jnp.pad(small, (0, joint + width - small.shape[0]))[None]
    first = jnp.concatenate(
        [
            jnp.concatenate([qkv_weight, out_weight.T], axis=1),
            small_row,
            jnp.zeros((padded - shard - 1, joint + width), BF16),
        ],
        axis=0,
    )
    for axis, bit in far:
        first = double(first, axis, bit)

    quarter = -(-ff // (4 * TILE)) * TILE
    pieces = pack(block_arg, gate_weight, up_weight, down_weight.T, quarter)
    pieces = [to_plane(piece, slot) for slot, piece in enumerate(pieces)]
    within = jnp.arange(padded, dtype=jnp.int32)

    def arrival(steps):
        owner = me ^ doubling_offsets(steps)
        target = jnp.where(within[None, :] < shard, owner[:, None] * shard + within[None, :], -1).reshape(1, -1)
        return owner, (jnp.arange(dim, dtype=jnp.int32)[:, None] == target).astype(BF16)

    owner, order = arrival(far + [("fy", 0), ("cx", 0), ("cc", 0)])
    _, out_order = arrival(far + [("cx", 0), ("fy", 0), ("cc", 0)])
    place = jnp.where(within[None, :] == shard, owner[:, None], -1).reshape(1, -1)
    spread = (jnp.arange(world, dtype=jnp.int32)[:, None] == place).astype(BF16)

    at_row = lax.dynamic_slice_in_dim(segments, offset, rows, axis=1)
    zeros_before = jnp.sum((segments < 1).astype(jnp.int32), axis=1, keepdims=True)
    ones_before = jnp.sum((segments < 2).astype(jnp.int32), axis=1, keepdims=True)
    start = jnp.where(at_row == 0, 0, jnp.where(at_row == 1, zeros_before, ones_before))
    position = (offset + jnp.arange(rows, dtype=jnp.int32)[None, :] - start).reshape(count)
    lane = jnp.arange(LANES, dtype=jnp.int32)
    frequency = ROPE_BASE ** (-(lane % (HD // 2)).astype(F32) * 2.0 / HD)
    angle = position.astype(F32)[:, None] * frequency[None, :]
    cosine = jnp.cos(angle)
    sine = jnp.where(lane % HD < HD // 2, -1.0, 1.0)[None, :] * jnp.sin(angle)
    start_column = jnp.broadcast_to(start.reshape(count, 1), (count, LANES))
    start_row = jnp.broadcast_to(start[:, None, :], (seqs, 8, rows))

    first, *pieces = after(first, *pieces)
    mlp_shard = assemble(plane_arg, pieces)
    mlp_weights = lax.all_gather(mlp_shard, WEIGHTS, axis=0, tiled=True)

    w_joint, w_out = double(first[:, :joint], "fy"), double(first[:, joint:], "cx")
    cot_x, cot_y = bit_swap(cot, "cx"), bit_swap(cot, "fy")
    w_joint, w_out = double(w_joint, "cx"), double(w_out, "fy")
    w_joint, w_out, cot_x, cot_y, order, out_order, spread, cosine, sine, start_column = after(
        w_joint, w_out, cot_x, cot_y, order, out_order, spread, cosine, sine, start_column
    )
    w_joint, w_out = (w_joint, bit_swap(w_joint, "cc")), (w_out, bit_swap(w_out, "cc"))

    normed, q, kv, gain_attn, gain_mlp = prep(x, order, spread, w_joint, cosine, sine, rows)
    kv_all = gather_four(kv.reshape(seqs, rows, 2 * LANES), CTX)
    kv_all[3], far_0, far_1 = after(kv_all[3], cot_x[:rows], cot_y[rows:])
    cot_far = [bit_swap(far_0, "fy"), bit_swap(far_1, "cx")]
    attended, resid, normed_all = [], [], []
    for seq in range(seqs):
        turn = block_arg if seq == 0 else after(attended[0], block_arg)[1]
        attended.append(attend(turn, q, kv_all, start_column, rows, seq))
        if seq == 1:
            attended[1], *cot_far = after(attended[1], *cot_far)
        resid_one, normed_one = project_out(attended[seq], x, w_out, out_order, gain_mlp, rows, seq)
        resid.append(resid_one)
        normed_all.append(gather_direct(normed_one, TOKENS))

    out_parts, d_terms, kept, turned = [], [], [], []
    for seq in range(seqs):
        if seq == 1:
            out_parts[0], normed_all[1] = lax.optimization_barrier((out_parts[0], normed_all[1]))
        result = mlp(normed_all[seq], [cot, cot_x, cot_y, cot_far[seq]], mlp_weights, seq)
        out_parts.append(result[:4])
        d_terms.append(sum_direct(TOKENS, *result[4:8]))
        kept.append(result[8])
        turned.append(result[9])
    turned[1], *d_terms[0] = after(turned[1], *d_terms[0])
    grads = mlp_grad(turned, kept)
    grads, d_terms[0], d_terms[1] = after(grads, *d_terms)
    grads = lax.psum_scatter(
        grads.reshape(world // 4, 4 * shard, 3 * quarter), WEIGHTS, scatter_dimension=0, tiled=False
    )

    d_resid, d_branch, d_attended, mlp_gain_grad = project_out_back(
        d_terms, resid, cot, w_out, out_order, gain_mlp
    )
    out_grad = dot_tn(d_branch, jnp.concatenate(attended, axis=0)).astype(BF16)
    out_grad = halve(out_grad, "cc")
    out_terms = [sum_direct(TOKENS, *after(d_terms[1][1], *part)[1:]) for part in out_parts]
    d_attended, out_terms[0] = after(d_attended, out_terms[0])
    dq, dkv_terms = [], []
    for seq in range(seqs):
        if seq == 1:
            dq[0], d_attended, out_grad, out_terms[1] = after(dq[0], d_attended, out_grad, out_terms[1])
            out_grad = halve(out_grad, "fy")
        result = attend_back(block_arg, q, kv_all, d_attended, start_row, cosine, sine, rows, seq)
        dq.append(result[0])
        dkv_terms.append(sum_direct(CTX, *result[1:]))
    dq[1], out_grad, *dkv_terms[0] = after(dq[1], out_grad, *dkv_terms[0])
    q_grad = dot_tn(normed, jnp.concatenate(dq, axis=0)).astype(BF16)
    q_grad = halve(q_grad, "cc")
    pieces = cut(plane_arg, lax.optimization_barrier(grads))
    dkv_terms[1], pieces = lax.optimization_barrier((dkv_terms[1], pieces))
    d_kv, input_grad, attn_gain_grad, bias_grad = input_back(
        dq, dkv_terms, x, d_resid, w_joint, order, gain_attn, cosine, sine
    )
    d_kv, q_grad = after(d_kv, q_grad)
    q_grad, out_grad = halve(q_grad, "cx"), halve(out_grad, "cx")

    output = []
    for seq in range(seqs):
        own, *away = out_terms[seq]
        output.append((resid[seq] + own + sum(term.astype(F32) for term in away)).astype(BF16))

    split_at = width + LANES
    bias_grad = bias_grad[0]
    small_grads = jnp.concatenate(
        [
            attn_gain_grad.reshape(world, -1),
            mlp_gain_grad.reshape(world, -1),
            bias_grad[:split_at].reshape(world, -1),
            bias_grad[split_at:].reshape(world, -1),
        ],
        axis=1,
    ).astype(BF16)
    small_count = small_grads.shape[1]
    small_grads = jnp.pad(small_grads, ((0, 0), (0, 2 * LANES - small_count)))
    kv_grad = dot_tn(
        jnp.concatenate([normed, spread], axis=0), jnp.concatenate([d_kv, small_grads], axis=0)
    ).astype(BF16)
    kv_grad = halve(halve(kv_grad, "cc"), "cx")
    pieces = [from_plane(piece, slot) for slot, piece in enumerate(pieces)]
    joint_grad = halve(jnp.concatenate([q_grad, kv_grad], axis=1), "fy")
    first_sum = jnp.concatenate([joint_grad, out_grad], axis=1)
    for axis, bit in reversed(far):
        first_sum = halve(first_sum, axis, bit)
    gate_grad, up_grad, down_grad_t = unpack(block_arg, pieces, ff)
    first_sum = first_sum.astype(F32)
    qkv_sum, out_sum = first_sum[:, :joint], first_sum[:, joint:]
    small_sum = qkv_sum[shard, width : width + small_count]
    at = (shard, 2 * shard, 2 * shard + split_at // world)

    return (
        jnp.stack(output),
        input_grad.reshape(hidden.shape),
        small_sum[: at[0]],
        qkv_sum[:shard],
        small_sum[at[1] : at[2]],
        small_sum[at[2] :],
        out_sum[:shard].T,
        small_sum[at[0] : at[1]],
        gate_grad,
        up_grad,
        down_grad_t.T,
    )


def solution(mesh):
    fsdp, ctx = mesh.shape["fsdp"], mesh.shape["ctx"]
    inner = Mesh(mesh.devices.reshape(fsdp // 2, 2, 2, ctx // 2), AXES)
    tokens = P(FSDP, CTX, None)
    vector = P(AXES)
    by_row = P(AXES, None)
    by_column = P(None, AXES)
    return jax.shard_map(
        on_device,
        mesh=inner,
        in_specs=(
            tokens,
            P(FSDP, None),
            vector,
            by_row,
            vector,
            by_column,
            vector,
            by_row,
            by_row,
            by_column,
            tokens,
        ),
        out_specs=(
            tokens,
            tokens,
            vector,
            by_row,
            vector,
            vector,
            by_column,
            vector,
            by_row,
            by_row,
            by_column,
        ),
        check_vma=False,
    )
```

```python
import functools

import jax
import jax.numpy as jnp
from jax import lax
from jax.experimental import pallas as pl
from jax.experimental.pallas import tpu as pltpu
from jax.sharding import Mesh
from jax.sharding import PartitionSpec as P

HD = 64
LANES = 128
EPSILON = 1e-06
ROPE_BASE = 1000000.0
MASKED = -1e30
SCALE = HD ** (-0.5)
TILE = 256
MIB = 1 << 20
VMEM_LIMIT = 60 * MIB
F32 = jnp.float32
BF16 = jnp.bfloat16
AXES = ("fz", "fy", "cx", "cc")
FSDP = ("fz", "fy")
CTX = ("cx", "cc")
TOKENS = ("fy", "cx")
WEIGHTS = ("fz", "cc")


def dot_nn(a, b):
    return lax.dot_general(a, b, (((1,), (0,)), ((), ())), preferred_element_type=F32)


def dot_nt(a, b):
    return lax.dot_general(a, b, (((1,), (1,)), ((), ())), preferred_element_type=F32)


def dot_tn(a, b):
    return lax.dot_general(a, b, (((0,), (0,)), ((), ())), preferred_element_type=F32)


def lane_of(shape):
    return lax.broadcasted_iota(jnp.int32, shape, len(shape) - 1)


def swap_halves(block):
    lead = lane_of(block.shape) % HD < HD // 2
    return jnp.where(
        lead, pltpu.roll(block, LANES - HD // 2, 1), pltpu.roll(block, HD // 2, 1)
    )


def other_head(block):
    return jnp.concatenate([block[:, HD:], block[:, :HD]], axis=1)


def read_out(extras, first, piece, total):
    owners, columns = extras.shape
    at = lax.broadcasted_iota(jnp.int32, (columns, total), 1) % piece + first
    chosen = (lax.broadcasted_iota(jnp.int32, (columns, total), 0) == at).astype(BF16)
    spread = dot_nn(extras, chosen)
    owner = lax.broadcasted_iota(jnp.int32, (owners, total), 1) // piece
    mine = owner == lax.broadcasted_iota(jnp.int32, (owners, total), 0)
    return jnp.sum(jnp.where(mine, spread, 0.0), axis=0, keepdims=True)


def prep_kernel(
    x_ref, order_ref, spread_ref, w_low_ref, w_high_ref, cos_ref, sin_ref,
    normed_ref, q_ref, kv_ref, gain_ref, gain_mlp_ref, bias_ref,
):
    x = x_ref[...].astype(F32)
    dim = x.shape[1]
    width = q_ref.shape[1]
    joint = w_low_ref.shape[1]
    middle = w_low_ref.shape[0]
    owners = spread_ref.shape[0]

    @pl.when(pl.program_id(0) == 0)
    def _():
        extras = dot_nn(spread_ref[:, :middle], w_low_ref[:, :LANES])
        extras = (extras + dot_nn(spread_ref[:, middle:], w_high_ref[:, :LANES])).astype(BF16)
        shard = dim // owners
        gain_ref[...] = read_out(extras, 0, shard, dim)
        gain_mlp_ref[...] = read_out(extras, shard, shard, dim)
        bias_ref[...] = read_out(extras, 2 * shard, joint // owners, joint)

    gain, bias = gain_ref[...], bias_ref[...]
    inverse = lax.rsqrt(jnp.mean(x * x, axis=-1, keepdims=True) + EPSILON)
    normed = (x * inverse * gain).astype(BF16)
    ordered = dot_nn(normed, order_ref[...]).astype(BF16)
    normed_ref[...] = ordered
    joined = dot_nn(ordered[:, :middle], w_low_ref[...])
    joined = joined + dot_nn(ordered[:, middle:], w_high_ref[...]) + bias
    cosine, sine = cos_ref[...], sin_ref[...]
    for begin in range(0, width + LANES, LANES):
        block = joined[:, begin : begin + LANES]
        turned = block * cosine + swap_halves(block) * sine
        if begin < width:
            q_ref[:, begin : begin + LANES] = (turned * SCALE).astype(BF16)
        else:
            kv_ref[:, :LANES] = turned.astype(BF16)
    kv_ref[:, LANES:] = joined[:, width + LANES :].astype(BF16)


def rows_of(rows, cols):
    return pl.BlockSpec((rows, cols), lambda i: (i, 0))


def whole(value):
    return pl.BlockSpec(value.shape, lambda i: (0,) * value.ndim)


def prep(x, order, spread, weights, cosine, sine, rows):
    count, dim = x.shape
    ordered = order.shape[1]
    joint = weights[0].shape[1]
    width = joint - 2 * LANES
    row = pl.BlockSpec((1, dim), lambda i: (0, 0))
    return pl.pallas_call(
        prep_kernel,
        grid=(count // rows,),
        in_specs=[
            rows_of(rows, dim),
            whole(order),
            whole(spread),
            whole(weights[0]),
            whole(weights[1]),
            rows_of(rows, LANES),
            rows_of(rows, LANES),
        ],
        out_specs=[rows_of(rows, ordered), rows_of(rows, width), rows_of(rows, 2 * LANES), row, row],
        out_shape=[
            jax.ShapeDtypeStruct((count, ordered), BF16),
            jax.ShapeDtypeStruct((count, width), BF16),
            jax.ShapeDtypeStruct((count, 2 * LANES), BF16),
            jax.ShapeDtypeStruct((1, dim), F32),
            jax.ShapeDtypeStruct((1, dim), F32),
        ],
        scratch_shapes=[pltpu.VMEM((1, joint), F32)],
        compiler_params=pltpu.CompilerParams(vmem_limit_bytes=VMEM_LIMIT),
        cost_estimate=pl.CostEstimate(
            flops=2 * count * ordered * (joint + dim), bytes_accessed=12 * MIB, transcendentals=0
        ),
        name="norm_project_rotate",
    )(x, order, spread, weights[0], weights[1], cosine, sine)


def back_in_order(value, order):
    high = value.astype(BF16)
    low = (value - high.astype(F32)).astype(BF16)
    return dot_nt(high, order) + dot_nt(low, order)


def out_kernel(attended_ref, x_ref, w_low_ref, w_high_ref, order_ref, gain_ref, resid_ref, normed_ref):
    attended = attended_ref[...]
    branch = jnp.concatenate([dot_nt(attended, w_low_ref[...]), dot_nt(attended, w_high_ref[...])], axis=1)
    resid = x_ref[...].astype(F32) + back_in_order(branch, order_ref[...])
    inverse = lax.rsqrt(jnp.mean(resid * resid, axis=-1, keepdims=True) + EPSILON)
    resid_ref[...] = resid
    normed_ref[...] = (resid * inverse * gain_ref[...]).astype(BF16)


def project_out(attended, x, weights, order, gain, rows, seq):
    dim = x.shape[1]
    count = rows
    return pl.pallas_call(
        out_kernel,
        grid=(1,),
        in_specs=[
            rows_of(rows, attended.shape[1]),
            pl.BlockSpec((rows, dim), lambda i: (seq, 0)),
            whole(weights[0]),
            whole(weights[1]),
            whole(order),
            whole(gain),
        ],
        out_specs=[rows_of(rows, dim), rows_of(rows, dim)],
        out_shape=[jax.ShapeDtypeStruct((count, dim), F32), jax.ShapeDtypeStruct((count, dim), BF16)],
        compiler_params=pltpu.CompilerParams(vmem_limit_bytes=VMEM_LIMIT),
        cost_estimate=pl.CostEstimate(flops=6 * count * dim * dim, bytes_accessed=8 * MIB, transcendentals=0),
        name="project_out_norm",
    )(attended, x, weights[0], weights[1], order, gain)


def sum_rows(value):
    return jnp.sum(value, axis=0, keepdims=True)


def norm_back(values, inverse, gain, incoming):
    scaled = incoming * gain
    mean_term = jnp.mean(scaled * values, axis=-1, keepdims=True)
    return inverse * scaled - values * inverse**3 * mean_term


def total_of(own_ref, *away_refs):
    total = own_ref[...]
    for ref in away_refs:
        total = total + ref[...].astype(F32)
    return total


def out_back_kernel(*refs):
    terms, resids = refs[:8], refs[8:10]
    cot_ref, w_low_ref, w_high_ref, order_ref, gain_ref = refs[10:15]
    d_resid_ref, d_branch_ref, d_attended_ref, gain_grad_ref = refs[15:]
    middle = w_low_ref.shape[0]
    d_normed = jnp.concatenate([total_of(*terms[:4]), total_of(*terms[4:])], axis=0)
    resid = jnp.concatenate([ref[...] for ref in resids], axis=0)
    inverse = lax.rsqrt(jnp.mean(resid * resid, axis=-1, keepdims=True) + EPSILON)
    d_resid = cot_ref[...].astype(F32) + norm_back(resid, inverse, gain_ref[...], d_normed)
    d_resid_ref[...] = d_resid
    d_branch = dot_nn(d_resid.astype(BF16), order_ref[...]).astype(BF16)
    d_branch_ref[...] = d_branch
    d_attended = dot_nn(d_branch[:, :middle], w_low_ref[...])
    d_attended = d_attended + dot_nn(d_branch[:, middle:], w_high_ref[...])
    d_attended_ref[...] = d_attended.astype(BF16)
    gain_grad_ref[...] = sum_rows(d_normed * resid * inverse)


def call_whole(kernel, operands, out_shape, flops, name):
    return pl.pallas_call(
        kernel,
        in_specs=[pl.BlockSpec(memory_space=pltpu.VMEM)] * len(operands),
        out_specs=[pl.BlockSpec(memory_space=pltpu.VMEM)] * len(out_shape),
        out_shape=out_shape,
        compiler_params=pltpu.CompilerParams(vmem_limit_bytes=VMEM_LIMIT),
        cost_estimate=pl.CostEstimate(flops=flops, bytes_accessed=16 * MIB, transcendentals=0),
        name=name,
    )(*operands)


def project_out_back(terms, resid, cot, weights, order, gain):
    count, dim = cot.shape
    ordered = order.shape[1]
    return call_whole(
        out_back_kernel,
        (*terms[0], *terms[1], *resid, cot, *weights, order, gain),
        [
            jax.ShapeDtypeStruct((count, dim), F32),
            jax.ShapeDtypeStruct((count, ordered), BF16),
            jax.ShapeDtypeStruct((count, weights[0].shape[1]), BF16),
            jax.ShapeDtypeStruct((1, dim), F32),
        ],
        4 * count * dim * dim,
        "norm_back_project",
    )


def input_back_kernel(*refs):
    dqs, terms = refs[:2], refs[2:10]
    x_ref, d_resid_ref, w_low_ref, w_high_ref, order_ref, gain_ref, cos_ref, sin_ref = refs[10:18]
    d_kv_ref, input_grad_ref, gain_grad_ref, bias_grad_ref = refs[18:]
    dkv = jnp.concatenate([total_of(*terms[:4]), total_of(*terms[4:])], axis=0)
    dk = dkv[:, :LANES]
    dk = dk * cos_ref[...] - swap_halves(dk) * sin_ref[...]
    d_kv = jnp.concatenate([dk.astype(BF16), dkv[:, LANES:].astype(BF16)], axis=1)
    d_kv_ref[...] = d_kv
    dq = jnp.concatenate([ref[...] for ref in dqs], axis=0)
    d_joined = jnp.concatenate([dq, d_kv], axis=1)
    d_normed = jnp.concatenate([dot_nt(d_joined, w_low_ref[...]), dot_nt(d_joined, w_high_ref[...])], axis=1)
    d_normed = back_in_order(d_normed, order_ref[...])
    x = x_ref[...].astype(F32)
    inverse = lax.rsqrt(jnp.mean(x * x, axis=-1, keepdims=True) + EPSILON)
    input_grad_ref[...] = (d_resid_ref[...] + norm_back(x, inverse, gain_ref[...], d_normed)).astype(BF16)
    gain_grad_ref[...] = sum_rows(d_normed * x * inverse)
    bias_grad_ref[...] = sum_rows(d_joined.astype(F32))


def input_back(dq, terms, x, d_resid, weights, order, gain, cosine, sine):
    count, dim = x.shape
    joint = dq[0].shape[1] + 2 * LANES
    return call_whole(
        input_back_kernel,
        (*dq, *terms[0], *terms[1], x, d_resid, *weights, order, gain, cosine, sine),
        [
            jax.ShapeDtypeStruct((count, 2 * LANES), BF16),
            jax.ShapeDtypeStruct((count, dim), BF16),
            jax.ShapeDtypeStruct((1, dim), F32),
            jax.ShapeDtypeStruct((1, joint), F32),
        ],
        6 * count * dim * joint,
        "input_gradient",
    )


def seq_rows(seq, rows, cols):
    return pl.BlockSpec((rows, cols), lambda i: (seq, 0))


def piece_of(seq, rows):
    return pl.BlockSpec((1, rows, 2 * LANES), lambda i: (seq, 0, 0))


def keys_and_values(piece_refs):
    joint = jnp.concatenate([ref[0] for ref in piece_refs], axis=0)
    key, value = joint[:, :LANES], joint[:, LANES:]
    return (key, other_head(key)), (value, other_head(value))


def attend_kernel(block_ref, q_ref, kv_0, kv_1, kv_2, kv_3, start_ref, out_ref, level_ref):
    rows, width = q_ref.shape
    length = 4 * rows
    heads = width // HD
    group = heads // 2
    keys, values = keys_and_values((kv_0, kv_1, kv_2, kv_3))
    upper_key = lane_of((length, LANES)) >= HD
    upper = lane_of((rows, LANES)) >= HD
    query_at = block_ref[0] * rows + lax.broadcasted_iota(jnp.int32, (rows, length), 0)
    key_at = jnp.concatenate(
        [
            (block_ref[0] ^ place) * rows + lax.broadcasted_iota(jnp.int32, (rows, rows), 1)
            for place in range(4)
        ],
        axis=1,
    )
    allowed = (key_at <= query_at) & (key_at >= start_ref[:, :1])
    bias = jnp.where(allowed, 0.0, MASKED)
    one = jnp.ones((), BF16)
    lane = lane_of((rows, LANES))
    levels = jnp.zeros((rows, LANES), F32)
    for pair in range(heads // 2):
        at = slice(pair * LANES, (pair + 1) * LANES)
        both = q_ref[:, at]
        parts = []
        for place in range(2):
            owner = (2 * pair + place) // group
            moved = int(owner != place)
            side = upper if place else ~upper
            side_key = upper_key if place else ~upper_key
            query = jnp.where(side, both, jnp.zeros_like(both))
            score = dot_nt(query, keys[moved]) + bias
            top = jnp.max(score, axis=1, keepdims=True)
            weight = jnp.exp(score - top).astype(BF16)
            mixed = dot_nn(weight, jnp.where(side_key, values[moved], one))
            total = pltpu.roll(mixed, HD, 1)
            parts.append(mixed / total)
            level = top + jnp.log(total[:, place * HD : place * HD + 1])
            levels = jnp.where(lane == 2 * pair + place, level, levels)
        out_ref[:, at] = jnp.where(upper, parts[1], parts[0]).astype(BF16)
    level_ref[...] = levels


def attend(block, q, kv_pieces, start, rows, seq):
    width = q.shape[1]
    heads = width // HD
    return pl.pallas_call(
        attend_kernel,
        grid=(1,),
        in_specs=[
            pl.BlockSpec(memory_space=pltpu.SMEM),
            seq_rows(seq, rows, width),
            *[piece_of(seq, rows)] * 4,
            seq_rows(seq, rows, LANES),
        ],
        out_specs=[seq_rows(0, rows, width), seq_rows(0, rows, LANES)],
        out_shape=[jax.ShapeDtypeStruct((rows, width), BF16), jax.ShapeDtypeStruct((rows, LANES), F32)],
        compiler_params=pltpu.CompilerParams(vmem_limit_bytes=VMEM_LIMIT),
        cost_estimate=pl.CostEstimate(
            flops=32 * rows * rows * LANES * heads,
            bytes_accessed=4 * rows * width,
            transcendentals=4 * rows * rows * heads,
        ),
        name="attention_forward",
    )(block, q, *kv_pieces, start)


def attend_back_kernel(
    block_ref, q_ref, kv_0, kv_1, kv_2, kv_3, back_ref, out_ref, level_ref, start_ref, cos_ref, sin_ref,
    dq_ref, own_ref, core_ref, x_ref, far_ref, dk_sum, dv_sum,
):
    rows, width = q_ref.shape
    heads = width // HD
    group = heads // 2
    keys, values = keys_and_values((kv_0, kv_1, kv_2, kv_3))
    key_t = keys[0].astype(F32).T.astype(BF16)
    keys_t = (key_t, jnp.concatenate([key_t[HD:], key_t[:HD]], axis=0))
    upper = lane_of((rows, LANES)) >= HD
    upper_t = lax.broadcasted_iota(jnp.int32, (LANES, rows), 0) >= HD
    query_at = block_ref[0] * rows + lax.broadcasted_iota(jnp.int32, (rows, rows), 1)
    key_at = lax.broadcasted_iota(jnp.int32, (rows, rows), 0)
    biases = []
    for place in range(4):
        at = (block_ref[0] ^ place) * rows + key_at
        biases.append(jnp.where((at <= query_at) & (at >= start_ref[0, :1, :]), 0.0, MASKED))
    head_of = lax.broadcasted_iota(jnp.int32, (width, LANES), 0) // HD
    by_head = (head_of == lane_of((width, LANES))).astype(BF16)
    product = back_ref[...].astype(F32) * out_ref[...].astype(F32)
    product_high = product.astype(BF16)
    product_low = (product - product_high.astype(F32)).astype(BF16)
    row_sums = (dot_nn(product_high, by_head) + dot_nn(product_low, by_head)).T
    levels = level_ref[...].T
    cosine, sine = cos_ref[...], sin_ref[...]
    dk_sum[...] = jnp.zeros_like(dk_sum)
    dv_sum[...] = jnp.zeros_like(dv_sum)
    for pair in range(heads // 2):
        at = slice(pair * LANES, (pair + 1) * LANES)
        both = q_ref[:, at]
        back_both = back_ref[:, at]
        zero = jnp.zeros_like(both)
        sides = (~upper, upper)
        queries = [jnp.where(side, both, zero) for side in sides]
        backs = [jnp.where(side, back_both, zero) for side in sides]
        owners = [(2 * pair + place) // group for place in range(2)]
        d_query_t = [jnp.zeros((LANES, rows), F32) for _ in range(2)]
        for piece in range(4):
            span = slice(piece * rows, (piece + 1) * rows)
            probs, d_scores = [], []
            for place in range(2):
                head = 2 * pair + place
                moved = int(owners[place] != place)
                score = dot_nt(keys[moved][span], queries[place]) + biases[piece]
                prob = jnp.exp(score - levels[head : head + 1])
                d_prob = dot_nt(values[moved][span], backs[place])
                d_score = (prob * (d_prob - row_sums[head : head + 1])).astype(BF16)
                d_query_t[place] = d_query_t[place] + dot_nn(keys_t[moved][:, span], d_score)
                probs.append(prob.astype(BF16))
                d_scores.append(d_score)
            if owners[0] == owners[1]:
                dv_sum[owners[0], span] += dot_nn(
                    jnp.concatenate(probs, axis=1), jnp.concatenate(backs, axis=0)
                )
                dk_sum[owners[0], span] += dot_nn(
                    jnp.concatenate(d_scores, axis=1), jnp.concatenate(queries, axis=0)
                )
            else:
                for place in range(2):
                    dv_sum[owners[place], span] += dot_nn(probs[place], backs[place])
                    dk_sum[owners[place], span] += dot_nn(d_scores[place], queries[place])
        d_query = jnp.where(upper_t, d_query_t[1], d_query_t[0]).T * SCALE
        dq_ref[:, at] = (d_query * cosine - swap_halves(d_query) * sine).astype(BF16)
    lower_key = lane_of((4 * rows, LANES)) < HD
    for total, begin in ((dk_sum, 0), (dv_sum, LANES)):
        first, second = total[0], total[1]
        first = first + pltpu.roll(first, HD, 1)
        second = second + pltpu.roll(second, HD, 1)
        both = jnp.where(lower_key, first, second)
        cols = slice(begin, begin + LANES)
        own_ref[:, cols] = both[:rows]
        for place, ref in enumerate((core_ref, x_ref, far_ref)):
            ref[:, cols] = both[(place + 1) * rows : (place + 2) * rows].astype(BF16)


def parts_of(rows, cols):
    shapes = [jax.ShapeDtypeStruct((rows, cols), F32)] + [jax.ShapeDtypeStruct((rows, cols), BF16)] * 3
    return [seq_rows(0, rows, cols)] * 4, shapes


def attend_back(block, q, kv_pieces, back, out, level, start, cosine, sine, rows, seq):
    width = q.shape[1]
    length = 4 * rows
    heads = width // HD
    specs, shapes = parts_of(rows, 2 * LANES)
    return pl.pallas_call(
        attend_back_kernel,
        grid=(1,),
        in_specs=[
            pl.BlockSpec(memory_space=pltpu.SMEM),
            seq_rows(seq, rows, width),
            *[piece_of(seq, rows)] * 4,
            seq_rows(seq, rows, width),
            seq_rows(0, rows, width),
            seq_rows(0, rows, LANES),
            pl.BlockSpec((1, 8, rows), lambda i: (seq, 0, 0)),
            seq_rows(seq, rows, LANES),
            seq_rows(seq, rows, LANES),
        ],
        out_specs=[seq_rows(0, rows, width), *specs],
        out_shape=[jax.ShapeDtypeStruct((rows, width), BF16), *shapes],
        scratch_shapes=[
            pltpu.VMEM((2, length, LANES), F32),
            pltpu.VMEM((2, length, LANES), F32),
        ],
        compiler_params=pltpu.CompilerParams(vmem_limit_bytes=VMEM_LIMIT),
        cost_estimate=pl.CostEstimate(
            flops=80 * rows * rows * LANES * heads,
            bytes_accessed=8 * rows * width,
            transcendentals=4 * rows * rows * heads,
        ),
        name="attention_backward",
    )(block, q, *kv_pieces, back, out, level, start, cosine, sine)


def mlp_kernel(
    n_0, n_1, n_2, n_3, c_0, c_1, c_2, c_3, w_ref,
    own_ref, out_1, out_2, out_3, d_own_ref, d_1, d_2, d_3, kept_ref, turned_ref,
    normed_all, cot_all,
):
    step = pl.program_id(0)
    rows = own_ref.shape[0]
    columns = w_ref.shape[1] // 3

    @pl.when(step == 0)
    def _():
        for place, (n_ref, c_ref) in enumerate(zip((n_0, n_1, n_2, n_3), (c_0, c_1, c_2, c_3))):
            normed_all[place // 2, (place % 2) * rows : (place % 2 + 1) * rows] = n_ref[...]
            cot_all[place // 2, (place % 2) * rows : (place % 2 + 1) * rows] = c_ref[...]

    normed, cot = normed_all[step], cot_all[step]
    for begin in range(0, columns, TILE):
        at = slice(begin, begin + TILE)
        gate = dot_nn(normed, w_ref[:, begin : begin + TILE])
        up = dot_nn(normed, w_ref[:, columns + begin : columns + begin + TILE])
        d_act = dot_nn(cot, w_ref[:, 2 * columns + begin : 2 * columns + begin + TILE])
        sigmoid = 0.5 * jnp.tanh(0.5 * gate) + 0.5
        swish = gate * sigmoid
        kept_ref[0, :, at] = (d_act * up * (sigmoid + swish * (1.0 - sigmoid))).astype(BF16)
        kept_ref[1, :, at] = (d_act * swish).astype(BF16)
        kept_ref[2, :, at] = (swish * up).astype(BF16)
    turned_ref[0] = normed.T
    turned_ref[1] = cot.T
    out = dot_nt(kept_ref[2], w_ref[:, 2 * columns :])
    d_normed = dot_nt(kept_ref[0], w_ref[:, :columns]) + dot_nt(kept_ref[1], w_ref[:, columns : 2 * columns])

    @pl.when(step == 0)
    def _():
        own_ref[...] = out[:rows]
        out_1[...] = out[rows:].astype(BF16)
        d_own_ref[...] = d_normed[:rows]
        d_1[...] = d_normed[rows:].astype(BF16)

    @pl.when(step == 1)
    def _():
        out_2[...] = out[:rows].astype(BF16)
        out_3[...] = out[rows:].astype(BF16)
        d_2[...] = d_normed[:rows].astype(BF16)
        d_3[...] = d_normed[rows:].astype(BF16)


def mlp(normed, cot, weights, seq):
    rows, dim = normed[0].shape
    columns = weights.shape[1] // 3
    specs, shapes = parts_of(rows, dim)
    once = lambda at: pl.BlockSpec((rows, dim), lambda i: (at, 0), pipeline_mode=pl.Buffered(1))
    return pl.pallas_call(
        mlp_kernel,
        grid=(2,),
        in_specs=[
            *[once(0)] * 4,
            *[once(seq)] * 3,
            once(0),
            pl.BlockSpec(weights.shape, lambda i: (0, 0), pipeline_mode=pl.Buffered(1)),
        ],
        out_specs=[
            *specs,
            *specs,
            pl.BlockSpec((3, 2 * rows, columns), lambda i: (0, i, 0)),
            pl.BlockSpec((2, dim, 2 * rows), lambda i: (0, 0, i)),
        ],
        out_shape=[
            *shapes,
            *shapes,
            jax.ShapeDtypeStruct((3, 4 * rows, columns), BF16),
            jax.ShapeDtypeStruct((2, dim, 4 * rows), BF16),
        ],
        scratch_shapes=[
            pltpu.VMEM((2, 2 * rows, dim), BF16),
            pltpu.VMEM((2, 2 * rows, dim), BF16),
        ],
        compiler_params=pltpu.CompilerParams(vmem_limit_bytes=VMEM_LIMIT),
        cost_estimate=pl.CostEstimate(
            flops=48 * rows * dim * columns,
            bytes_accessed=6 * dim * columns + 24 * rows * columns,
            transcendentals=4 * rows * columns,
        ),
        name="feed_forward",
    )(*normed, *cot, weights)


def mlp_grad_kernel(turned_0, turned_1, kept_0, kept_1, grad_ref):
    grad_ref[...] = (dot_nn(turned_0[0], kept_0[0]) + dot_nn(turned_1[0], kept_1[0])).astype(BF16)


def mlp_grad(turned, kept):
    _, dim, count = turned[0].shape
    columns = kept[0].shape[2]
    turned_block = pl.BlockSpec((1, dim, count), lambda i: (i // 2, 0, 0))
    kept_block = pl.BlockSpec((1, count, columns), lambda i: (i, 0, 0))
    return pl.pallas_call(
        mlp_grad_kernel,
        grid=(3,),
        in_specs=[turned_block, turned_block, kept_block, kept_block],
        out_specs=pl.BlockSpec((dim, columns), lambda i: (0, i)),
        out_shape=jax.ShapeDtypeStruct((dim, 3 * columns), BF16),
        compiler_params=pltpu.CompilerParams(vmem_limit_bytes=VMEM_LIMIT),
        cost_estimate=pl.CostEstimate(
            flops=12 * count * dim * columns,
            bytes_accessed=6 * dim * columns + 12 * count * columns,
            transcendentals=0,
        ),
        name="feed_forward_gradients",
    )(*turned, *kept)


def pack_kernel(block_ref, gate_ref, up_ref, down_ref, *refs):
    out_refs, scratch = refs[:4], refs[4]
    shard, ff = gate_ref.shape
    quarter = scratch.shape[2] // 4
    for place, ref in enumerate((gate_ref, up_ref, down_ref)):
        scratch[place, :, :ff] = ref[...].astype(F32)
        scratch[place, :, ff:] = jnp.zeros((shard, 4 * quarter - ff), F32)
    for place, out_ref in enumerate(out_refs):
        begin = pl.multiple_of((block_ref[0] ^ place) * quarter, LANES)
        for part in range(3):
            out_ref[:, part * quarter : (part + 1) * quarter] = scratch[part, :, pl.ds(begin, quarter)].astype(BF16)


def pack(block, gate, up, down_t, quarter):
    shard = gate.shape[0]
    return pl.pallas_call(
        pack_kernel,
        in_specs=[pl.BlockSpec(memory_space=pltpu.SMEM)] + [pl.BlockSpec(memory_space=pltpu.VMEM)] * 3,
        out_specs=[pl.BlockSpec(memory_space=pltpu.VMEM)] * 4,
        out_shape=[jax.ShapeDtypeStruct((shard, 3 * quarter), BF16)] * 4,
        scratch_shapes=[pltpu.VMEM((3, shard, 4 * quarter), F32)],
        compiler_params=pltpu.CompilerParams(vmem_limit_bytes=VMEM_LIMIT),
        name="pack_columns",
    )(block, gate, up, down_t)


def pick(options, index):
    value = options[0]
    for place in range(1, len(options)):
        value = jnp.where(index == place, options[place], value)
    return value


def assemble_kernel(block_ref, *refs):
    pieces, out_ref, scratch = refs[:4], refs[4], refs[5]
    shard = pieces[0].shape[0]
    values = [ref[...].astype(F32) for ref in pieces]
    for owner in range(4):
        scratch[owner * shard : (owner + 1) * shard] = pick(values, block_ref[0] ^ owner)
    out_ref[...] = scratch[...].astype(BF16)


def assemble(block, pieces):
    shard, columns = pieces[0].shape
    return pl.pallas_call(
        assemble_kernel,
        in_specs=[pl.BlockSpec(memory_space=pltpu.SMEM)] + [pl.BlockSpec(memory_space=pltpu.VMEM)] * 4,
        out_specs=pl.BlockSpec(memory_space=pltpu.VMEM),
        out_shape=jax.ShapeDtypeStruct((4 * shard, columns), BF16),
        scratch_shapes=[pltpu.VMEM((4 * shard, columns), F32)],
        compiler_params=pltpu.CompilerParams(vmem_limit_bytes=VMEM_LIMIT),
        name="assemble_rows",
    )(block, *pieces)


def cut_kernel(block_ref, value_ref, *refs):
    out_refs, scratch = refs[:4], refs[4]
    shard = out_refs[0].shape[0]
    scratch[...] = value_ref[...].astype(F32)
    values = [scratch[owner * shard : (owner + 1) * shard] for owner in range(4)]
    for place, out_ref in enumerate(out_refs):
        out_ref[...] = pick(values, block_ref[0] ^ place).astype(BF16)


def cut(block, value):
    shard, columns = value.shape[0] // 4, value.shape[1]
    return pl.pallas_call(
        cut_kernel,
        in_specs=[pl.BlockSpec(memory_space=pltpu.SMEM), pl.BlockSpec(memory_space=pltpu.VMEM)],
        out_specs=[pl.BlockSpec(memory_space=pltpu.VMEM)] * 4,
        out_shape=[jax.ShapeDtypeStruct((shard, columns), BF16)] * 4,
        scratch_shapes=[pltpu.VMEM(value.shape, F32)],
        compiler_params=pltpu.CompilerParams(vmem_limit_bytes=VMEM_LIMIT),
        name="cut_rows",
    )(block, value)


def unpack_kernel(block_ref, *refs):
    pieces, out_refs, scratch = refs[:4], refs[4:7], refs[7]
    ff = out_refs[0].shape[1]
    quarter = scratch.shape[2] // 4
    for place, ref in enumerate(pieces):
        begin = pl.multiple_of((block_ref[0] ^ place) * quarter, LANES)
        for part in range(3):
            scratch[part, :, pl.ds(begin, quarter)] = ref[:, part * quarter : (part + 1) * quarter].astype(F32)
    for part, out_ref in enumerate(out_refs):
        out_ref[...] = scratch[part, :, :ff]


def unpack(block, pieces, ff):
    shard, columns = pieces[0].shape
    return pl.pallas_call(
        unpack_kernel,
        in_specs=[pl.BlockSpec(memory_space=pltpu.SMEM)] + [pl.BlockSpec(memory_space=pltpu.VMEM)] * 4,
        out_specs=[pl.BlockSpec(memory_space=pltpu.VMEM)] * 3,
        out_shape=[jax.ShapeDtypeStruct((shard, ff), F32)] * 3,
        scratch_shapes=[pltpu.VMEM((3, shard, columns // 3 * 4), F32)],
        compiler_params=pltpu.CompilerParams(vmem_limit_bytes=VMEM_LIMIT),
        name="unpack_columns",
    )(block, *pieces)


def bit_swap(value, axis, bit=0):
    size = lax.axis_size(axis)
    return lax.ppermute(value, axis, [(i, i ^ (1 << bit)) for i in range(size)])


def jump_swap(value, axes, jump):
    return lax.ppermute(value, axes, [(i, i ^ jump) for i in range(4)])


def to_plane(value, slot):
    high, low = slot >> 1, slot & 1
    pairs = [
        (4 * y + 2 * x + c, 4 * (c ^ low) + 2 * (x ^ high) + y) for y in range(2) for x in range(2) for c in range(2)
    ]
    return lax.ppermute(value, TOKENS + ("cc",), pairs)


def from_plane(value, slot):
    high, low = slot >> 1, slot & 1
    pairs = [
        (4 * y + 2 * x + c, 4 * c + 2 * (x ^ high) + (y ^ low)) for y in range(2) for x in range(2) for c in range(2)
    ]
    return lax.ppermute(value, TOKENS + ("cc",), pairs)


def after(first, *values):
    return lax.optimization_barrier((first, *values))


def gather_four(value, axes):
    from_first = bit_swap(value, axes[0])
    return [value, bit_swap(value, axes[1]), from_first, bit_swap(from_first, axes[1])]


def gather_direct(value, axes):
    return [value] + [jump_swap(value, axes, jump) for jump in range(1, 4)]


def sum_direct(axes, own, *away):
    return [own] + [jump_swap(value, axes, jump + 1) for jump, value in enumerate(away)]


def doubling_offsets(steps):
    weight = {"cc": 1, "cx": 2, "fy": 4, "fz": 8}
    offsets = [0]
    for axis, bit in steps:
        offsets += [offset ^ (weight[axis] << bit) for offset in offsets]
    return jnp.array(offsets, jnp.int32)


def double(value, axis, bit=0):
    return jnp.concatenate([value, bit_swap(value, axis, bit)], axis=0)


def halve(value, axis, bit=0):
    middle = value.shape[0] // 2
    came = bit_swap(value[middle:], axis, bit)
    return (value[:middle].astype(F32) + came.astype(F32)).astype(BF16)


def on_device(
    hidden,
    segments,
    attn_gain,
    qkv_weight,
    qkv_bias,
    out_weight,
    mlp_gain,
    gate_weight,
    up_weight,
    down_weight,
    cotangent,
):
    seqs, rows, dim = hidden.shape
    count = seqs * rows
    shard = attn_gain.shape[0]
    world = dim // shard
    joint = qkv_weight.shape[1]
    width = joint - 2 * LANES
    ff = gate_weight.shape[1]
    block = lax.axis_index("cx") * lax.axis_size("cc") + lax.axis_index("cc")
    me = lax.axis_index(FSDP) * lax.axis_size(CTX) + block
    offset = block * rows
    block_arg = block.reshape(1).astype(jnp.int32)
    plane_arg = (lax.axis_index("cx") * 2 + lax.axis_index("fy")).reshape(1).astype(jnp.int32)
    x = hidden.reshape(count, dim)
    cot = cotangent.reshape(count, dim)

    cot_x, cot_y = bit_swap(cot, "cx"), bit_swap(cot, "fy")

    far = [("fz", bit) for bit in reversed(range((lax.axis_size("fz")).bit_length() - 1))]
    padded = -(-(shard + 1) // 16) * 16
    small = jnp.concatenate([attn_gain, mlp_gain, qkv_bias])
    small_row = jnp.pad(small, (0, joint + width - small.shape[0]))[None]
    first = jnp.concatenate(
        [
            jnp.concatenate([qkv_weight, out_weight.T], axis=1),
            small_row,
            jnp.zeros((padded - shard - 1, joint + width), BF16),
        ],
        axis=0,
    )
    for axis, bit in far:
        first = double(first, axis, bit)

    quarter = -(-ff // (4 * TILE)) * TILE
    pieces = pack(block_arg, gate_weight, up_weight, down_weight.T, quarter)
    pieces = [to_plane(piece, slot) for slot, piece in enumerate(pieces)]
    within = jnp.arange(padded, dtype=jnp.int32)

    def arrival(steps):
        owner = me ^ doubling_offsets(steps)
        target = jnp.where(within[None, :] < shard, owner[:, None] * shard + within[None, :], -1).reshape(1, -1)
        return owner, (jnp.arange(dim, dtype=jnp.int32)[:, None] == target).astype(BF16)

    owner, order = arrival(far + [("fy", 0), ("cx", 0), ("cc", 0)])
    _, out_order = arrival(far + [("cx", 0), ("fy", 0), ("cc", 0)])
    place = jnp.where(within[None, :] == shard, owner[:, None], -1).reshape(1, -1)
    spread = (jnp.arange(world, dtype=jnp.int32)[:, None] == place).astype(BF16)

    at_row = lax.dynamic_slice_in_dim(segments, offset, rows, axis=1)
    zeros_before = jnp.sum((segments < 1).astype(jnp.int32), axis=1, keepdims=True)
    ones_before = jnp.sum((segments < 2).astype(jnp.int32), axis=1, keepdims=True)
    start = jnp.where(at_row == 0, 0, jnp.where(at_row == 1, zeros_before, ones_before))
    position = (offset + jnp.arange(rows, dtype=jnp.int32)[None, :] - start).reshape(count)
    lane = jnp.arange(LANES, dtype=jnp.int32)
    frequency = ROPE_BASE ** (-(lane % (HD // 2)).astype(F32) * 2.0 / HD)
    angle = position.astype(F32)[:, None] * frequency[None, :]
    cosine = jnp.cos(angle)
    sine = jnp.where(lane % HD < HD // 2, -1.0, 1.0)[None, :] * jnp.sin(angle)
    start_column = jnp.broadcast_to(start.reshape(count, 1), (count, LANES))
    start_row = jnp.broadcast_to(start[:, None, :], (seqs, 8, rows))

    first, cot_x, cot_y, *pieces = after(first, cot_x, cot_y, *pieces)
    mlp_shard = assemble(plane_arg, pieces)
    mlp_weights = lax.all_gather(mlp_shard, WEIGHTS, axis=0, tiled=True)
    w_joint, w_out = double(first[:, :joint], "fy"), double(first[:, joint:], "cx")
    w_joint, w_out, order, out_order, spread, cosine, sine, start_column = after(
        w_joint, w_out, order, out_order, spread, cosine, sine, start_column
    )
    w_joint, w_out = after(double(w_joint, "cx"), double(w_out, "fy"))
    w_joint, w_out = (w_joint, bit_swap(w_joint, "cc")), (w_out, bit_swap(w_out, "cc"))

    normed, q, kv, gain_attn, gain_mlp = prep(x, order, spread, w_joint, cosine, sine, rows)
    kv_all = gather_four(kv.reshape(seqs, rows, 2 * LANES), CTX)
    kv_all[3], far_0, far_1 = after(kv_all[3], cot_x[:rows], cot_y[rows:])
    cot_far = [bit_swap(far_0, "fy"), bit_swap(far_1, "cx")]
    attended, levels, resid, normed_all = [], [], [], []
    for seq in range(seqs):
        turn = block_arg if seq == 0 else after(attended[0], block_arg)[1]
        attended_one, level_one = attend(turn, q, kv_all, start_column, rows, seq)
        attended.append(attended_one)
        levels.append(level_one)
        if seq == 1:
            attended[1], *cot_far = after(attended[1], *cot_far)
        resid_one, normed_one = project_out(attended[seq], x, w_out, out_order, gain_mlp, rows, seq)
        resid.append(resid_one)
        normed_all.append(gather_direct(normed_one, TOKENS))

    out_parts, d_terms, kept, turned = [], [], [], []
    for seq in range(seqs):
        if seq == 1:
            out_parts[0], normed_all[1] = lax.optimization_barrier((out_parts[0], normed_all[1]))
        result = mlp(normed_all[seq], [cot, cot_x, cot_y, cot_far[seq]], mlp_weights, seq)
        out_parts.append(result[:4])
        d_terms.append(sum_direct(TOKENS, *result[4:8]))
        kept.append(result[8])
        turned.append(result[9])
    turned[1], *d_terms[0] = after(turned[1], *d_terms[0])
    grads = mlp_grad(turned, kept)
    grads, d_terms[0], d_terms[1] = after(grads, *d_terms)
    grads = lax.psum_scatter(
        grads.reshape(world // 4, 4 * shard, 3 * quarter), WEIGHTS, scatter_dimension=0, tiled=False
    )

    d_resid, d_branch, d_attended, mlp_gain_grad = project_out_back(
        d_terms, resid, cot, w_out, out_order, gain_mlp
    )
    out_grad = dot_tn(d_branch, jnp.concatenate(attended, axis=0)).astype(BF16)
    out_grad = halve(out_grad, "cc")
    out_terms = [sum_direct(TOKENS, *after(d_terms[1][1], *part)[1:]) for part in out_parts]
    d_attended, out_terms[0] = after(d_attended, out_terms[0])
    dq, dkv_terms = [], []
    for seq in range(seqs):
        if seq == 1:
            dq[0], d_attended, out_grad, out_terms[1] = after(dq[0], d_attended, out_grad, out_terms[1])
            out_grad = halve(out_grad, "fy")
        result = attend_back(
            block_arg, q, kv_all, d_attended, attended[seq], levels[seq], start_row, cosine, sine, rows, seq
        )
        dq.append(result[0])
        dkv_terms.append(sum_direct(CTX, *result[1:]))
    dq[1], out_grad, *dkv_terms[0] = after(dq[1], out_grad, *dkv_terms[0])
    q_grad = dot_tn(normed, jnp.concatenate(dq, axis=0)).astype(BF16)
    q_grad = halve(q_grad, "cc")
    pieces = cut(plane_arg, lax.optimization_barrier(grads))
    dkv_terms[1], pieces, q_grad = lax.optimization_barrier((dkv_terms[1], pieces, q_grad))
    q_grad, out_grad = halve(q_grad, "cx"), halve(out_grad, "cx")
    d_kv, input_grad, attn_gain_grad, bias_grad = input_back(
        dq, dkv_terms, x, d_resid, w_joint, order, gain_attn, cosine, sine
    )
    d_kv, q_grad = after(d_kv, q_grad)

    output = []
    for seq in range(seqs):
        own, *away = out_terms[seq]
        output.append((resid[seq] + own + sum(term.astype(F32) for term in away)).astype(BF16))

    split_at = width + LANES
    bias_grad = bias_grad[0]
    small_grads = jnp.concatenate(
        [
            attn_gain_grad.reshape(world, -1),
            mlp_gain_grad.reshape(world, -1),
            bias_grad[:split_at].reshape(world, -1),
            bias_grad[split_at:].reshape(world, -1),
        ],
        axis=1,
    ).astype(BF16)
    small_count = small_grads.shape[1]
    small_grads = jnp.pad(small_grads, ((0, 0), (0, 2 * LANES - small_count)))
    kv_grad = dot_tn(
        jnp.concatenate([normed, spread], axis=0), jnp.concatenate([d_kv, small_grads], axis=0)
    ).astype(BF16)
    kv_grad, *pieces = after(halve(kv_grad, "cc"), *pieces)
    kv_grad = halve(kv_grad, "cx")
    joint_grad = halve(jnp.concatenate([q_grad, kv_grad], axis=1), "fy")
    pieces = [from_plane(piece, slot) for slot, piece in enumerate(pieces)]
    first_sum = jnp.concatenate([joint_grad, out_grad], axis=1)
    for axis, bit in reversed(far):
        first_sum = halve(first_sum, axis, bit)
    gate_grad, up_grad, down_grad_t = unpack(block_arg, pieces, ff)
    first_sum = first_sum.astype(F32)
    qkv_sum, out_sum = first_sum[:, :joint], first_sum[:, joint:]
    small_sum = qkv_sum[shard, width : width + small_count]
    at = (shard, 2 * shard, 2 * shard + split_at // world)

    return (
        jnp.stack(output),
        input_grad.reshape(hidden.shape),
        small_sum[: at[0]],
        qkv_sum[:shard],
        small_sum[at[1] : at[2]],
        small_sum[at[2] :],
        out_sum[:shard].T,
        small_sum[at[0] : at[1]],
        gate_grad,
        up_grad,
        down_grad_t.T,
    )


def solution(mesh):
    fsdp, ctx = mesh.shape["fsdp"], mesh.shape["ctx"]
    inner = Mesh(mesh.devices.reshape(fsdp // 2, 2, 2, ctx // 2), AXES)
    tokens = P(FSDP, CTX, None)
    vector = P(AXES)
    by_row = P(AXES, None)
    by_column = P(None, AXES)
    return jax.shard_map(
        on_device,
        mesh=inner,
        in_specs=(
            tokens,
            P(FSDP, None),
            vector,
            by_row,
            vector,
            by_column,
            vector,
            by_row,
            by_row,
            by_column,
            tokens,
        ),
        out_specs=(
            tokens,
            tokens,
            vector,
            by_row,
            vector,
            vector,
            by_column,
            vector,
            by_row,
            by_row,
            by_column,
        ),
        check_vma=False,
    )
```

```python
import functools

import jax
import jax.numpy as jnp
from jax import lax
from jax.experimental import pallas as pl
from jax.experimental.pallas import tpu as pltpu
from jax.sharding import Mesh
from jax.sharding import PartitionSpec as P

HD = 64
LANES = 128
EPSILON = 1e-06
ROPE_BASE = 1000000.0
MASKED = -1e30
SCALE = HD ** (-0.5)
TILE = 256
MIB = 1 << 20
VMEM_LIMIT = 60 * MIB
F32 = jnp.float32
BF16 = jnp.bfloat16
AXES = ("fz", "fy", "cx", "cc")
FSDP = ("fz", "fy")
CTX = ("cx", "cc")
TOKENS = ("fy", "cx")
WEIGHTS = ("fz", "cc")


def dot_nn(a, b):
    return lax.dot_general(a, b, (((1,), (0,)), ((), ())), preferred_element_type=F32)


def dot_nt(a, b):
    return lax.dot_general(a, b, (((1,), (1,)), ((), ())), preferred_element_type=F32)


def dot_tn(a, b):
    return lax.dot_general(a, b, (((0,), (0,)), ((), ())), preferred_element_type=F32)


def lane_of(shape):
    return lax.broadcasted_iota(jnp.int32, shape, len(shape) - 1)


def swap_halves(block):
    lead = lane_of(block.shape) % HD < HD // 2
    return jnp.where(
        lead, pltpu.roll(block, LANES - HD // 2, 1), pltpu.roll(block, HD // 2, 1)
    )


def other_head(block):
    return jnp.concatenate([block[:, HD:], block[:, :HD]], axis=1)


def read_out(extras, first, piece, total):
    owners, columns = extras.shape
    at = lax.broadcasted_iota(jnp.int32, (columns, total), 1) % piece + first
    chosen = (lax.broadcasted_iota(jnp.int32, (columns, total), 0) == at).astype(BF16)
    spread = dot_nn(extras, chosen)
    owner = lax.broadcasted_iota(jnp.int32, (owners, total), 1) // piece
    mine = owner == lax.broadcasted_iota(jnp.int32, (owners, total), 0)
    return jnp.sum(jnp.where(mine, spread, 0.0), axis=0, keepdims=True)


def prep_kernel(
    x_ref, order_ref, spread_ref, w_low_ref, w_high_ref, cos_ref, sin_ref,
    normed_ref, q_ref, kv_ref, gain_ref, gain_mlp_ref, bias_ref,
):
    x = x_ref[...].astype(F32)
    dim = x.shape[1]
    width = q_ref.shape[1]
    joint = w_low_ref.shape[1]
    middle = w_low_ref.shape[0]
    owners = spread_ref.shape[0]

    @pl.when(pl.program_id(0) == 0)
    def _():
        extras = dot_nn(spread_ref[:, :middle], w_low_ref[:, :LANES])
        extras = (extras + dot_nn(spread_ref[:, middle:], w_high_ref[:, :LANES])).astype(BF16)
        shard = dim // owners
        gain_ref[...] = read_out(extras, 0, shard, dim)
        gain_mlp_ref[...] = read_out(extras, shard, shard, dim)
        bias_ref[...] = read_out(extras, 2 * shard, joint // owners, joint)

    gain, bias = gain_ref[...], bias_ref[...]
    inverse = lax.rsqrt(jnp.mean(x * x, axis=-1, keepdims=True) + EPSILON)
    normed = (x * inverse * gain).astype(BF16)
    ordered = dot_nn(normed, order_ref[...]).astype(BF16)
    normed_ref[...] = ordered
    joined = dot_nn(ordered[:, :middle], w_low_ref[...])
    joined = joined + dot_nn(ordered[:, middle:], w_high_ref[...]) + bias
    cosine, sine = cos_ref[...], sin_ref[...]
    for begin in range(0, width + LANES, LANES):
        block = joined[:, begin : begin + LANES]
        turned = block * cosine + swap_halves(block) * sine
        if begin < width:
            q_ref[:, begin : begin + LANES] = (turned * SCALE).astype(BF16)
        else:
            kv_ref[:, :LANES] = turned.astype(BF16)
    kv_ref[:, LANES:] = joined[:, width + LANES :].astype(BF16)


def rows_of(rows, cols):
    return pl.BlockSpec((rows, cols), lambda i: (i, 0))


def whole(value):
    return pl.BlockSpec(value.shape, lambda i: (0,) * value.ndim)


def prep(x, order, spread, weights, cosine, sine, rows):
    count, dim = x.shape
    ordered = order.shape[1]
    joint = weights[0].shape[1]
    width = joint - 2 * LANES
    row = pl.BlockSpec((1, dim), lambda i: (0, 0))
    return pl.pallas_call(
        prep_kernel,
        grid=(count // rows,),
        in_specs=[
            rows_of(rows, dim),
            whole(order),
            whole(spread),
            whole(weights[0]),
            whole(weights[1]),
            rows_of(rows, LANES),
            rows_of(rows, LANES),
        ],
        out_specs=[rows_of(rows, ordered), rows_of(rows, width), rows_of(rows, 2 * LANES), row, row],
        out_shape=[
            jax.ShapeDtypeStruct((count, ordered), BF16),
            jax.ShapeDtypeStruct((count, width), BF16),
            jax.ShapeDtypeStruct((count, 2 * LANES), BF16),
            jax.ShapeDtypeStruct((1, dim), F32),
            jax.ShapeDtypeStruct((1, dim), F32),
        ],
        scratch_shapes=[pltpu.VMEM((1, joint), F32)],
        compiler_params=pltpu.CompilerParams(vmem_limit_bytes=VMEM_LIMIT),
        cost_estimate=pl.CostEstimate(
            flops=2 * count * ordered * (joint + dim), bytes_accessed=12 * MIB, transcendentals=0
        ),
        name="norm_project_rotate",
    )(x, order, spread, weights[0], weights[1], cosine, sine)


def back_in_order(value, order):
    high = value.astype(BF16)
    low = (value - high.astype(F32)).astype(BF16)
    return dot_nt(high, order) + dot_nt(low, order)


def out_kernel(attended_ref, x_ref, w_low_ref, w_high_ref, order_ref, gain_ref, resid_ref, normed_ref):
    attended = attended_ref[...]
    branch = jnp.concatenate([dot_nt(attended, w_low_ref[...]), dot_nt(attended, w_high_ref[...])], axis=1)
    resid = x_ref[...].astype(F32) + back_in_order(branch, order_ref[...])
    inverse = lax.rsqrt(jnp.mean(resid * resid, axis=-1, keepdims=True) + EPSILON)
    resid_ref[...] = resid
    normed_ref[...] = (resid * inverse * gain_ref[...]).astype(BF16)


def project_out(attended, x, weights, order, gain, rows, seq):
    dim = x.shape[1]
    count = rows
    return pl.pallas_call(
        out_kernel,
        grid=(1,),
        in_specs=[
            rows_of(rows, attended.shape[1]),
            pl.BlockSpec((rows, dim), lambda i: (seq, 0)),
            whole(weights[0]),
            whole(weights[1]),
            whole(order),
            whole(gain),
        ],
        out_specs=[rows_of(rows, dim), rows_of(rows, dim)],
        out_shape=[jax.ShapeDtypeStruct((count, dim), F32), jax.ShapeDtypeStruct((count, dim), BF16)],
        compiler_params=pltpu.CompilerParams(vmem_limit_bytes=VMEM_LIMIT),
        cost_estimate=pl.CostEstimate(flops=6 * count * dim * dim, bytes_accessed=8 * MIB, transcendentals=0),
        name="project_out_norm",
    )(attended, x, weights[0], weights[1], order, gain)


def sum_rows(value):
    return jnp.sum(value, axis=0, keepdims=True)


def norm_back(values, inverse, gain, incoming):
    scaled = incoming * gain
    mean_term = jnp.mean(scaled * values, axis=-1, keepdims=True)
    return inverse * scaled - values * inverse**3 * mean_term


def total_of(own_ref, *away_refs):
    total = own_ref[...]
    for ref in away_refs:
        total = total + ref[...].astype(F32)
    return total


def out_back_kernel(*refs):
    terms, resids = refs[:8], refs[8:10]
    cot_ref, w_low_ref, w_high_ref, order_ref, gain_ref = refs[10:15]
    d_resid_ref, d_branch_ref, d_attended_ref, gain_grad_ref = refs[15:]
    middle = w_low_ref.shape[0]
    d_normed = jnp.concatenate([total_of(*terms[:4]), total_of(*terms[4:])], axis=0)
    resid = jnp.concatenate([ref[...] for ref in resids], axis=0)
    inverse = lax.rsqrt(jnp.mean(resid * resid, axis=-1, keepdims=True) + EPSILON)
    d_resid = cot_ref[...].astype(F32) + norm_back(resid, inverse, gain_ref[...], d_normed)
    d_resid_ref[...] = d_resid
    d_branch = dot_nn(d_resid.astype(BF16), order_ref[...]).astype(BF16)
    d_branch_ref[...] = d_branch
    d_attended = dot_nn(d_branch[:, :middle], w_low_ref[...])
    d_attended = d_attended + dot_nn(d_branch[:, middle:], w_high_ref[...])
    d_attended_ref[...] = d_attended.astype(BF16)
    gain_grad_ref[...] = sum_rows(d_normed * resid * inverse)


def call_whole(kernel, operands, out_shape, flops, name):
    return pl.pallas_call(
        kernel,
        in_specs=[pl.BlockSpec(memory_space=pltpu.VMEM)] * len(operands),
        out_specs=[pl.BlockSpec(memory_space=pltpu.VMEM)] * len(out_shape),
        out_shape=out_shape,
        compiler_params=pltpu.CompilerParams(vmem_limit_bytes=VMEM_LIMIT),
        cost_estimate=pl.CostEstimate(flops=flops, bytes_accessed=16 * MIB, transcendentals=0),
        name=name,
    )(*operands)


def project_out_back(terms, resid, cot, weights, order, gain):
    count, dim = cot.shape
    ordered = order.shape[1]
    return call_whole(
        out_back_kernel,
        (*terms[0], *terms[1], *resid, cot, *weights, order, gain),
        [
            jax.ShapeDtypeStruct((count, dim), F32),
            jax.ShapeDtypeStruct((count, ordered), BF16),
            jax.ShapeDtypeStruct((count, weights[0].shape[1]), BF16),
            jax.ShapeDtypeStruct((1, dim), F32),
        ],
        4 * count * dim * dim,
        "norm_back_project",
    )


def input_back_kernel(*refs):
    dqs, terms = refs[:2], refs[2:10]
    x_ref, d_resid_ref, w_low_ref, w_high_ref, order_ref, gain_ref, cos_ref, sin_ref = refs[10:18]
    d_kv_ref, input_grad_ref, gain_grad_ref, bias_grad_ref = refs[18:]
    dkv = jnp.concatenate([total_of(*terms[:4]), total_of(*terms[4:])], axis=0)
    dk = dkv[:, :LANES]
    dk = dk * cos_ref[...] - swap_halves(dk) * sin_ref[...]
    d_kv = jnp.concatenate([dk.astype(BF16), dkv[:, LANES:].astype(BF16)], axis=1)
    d_kv_ref[...] = d_kv
    dq = jnp.concatenate([ref[...] for ref in dqs], axis=0)
    d_joined = jnp.concatenate([dq, d_kv], axis=1)
    d_normed = jnp.concatenate([dot_nt(d_joined, w_low_ref[...]), dot_nt(d_joined, w_high_ref[...])], axis=1)
    d_normed = back_in_order(d_normed, order_ref[...])
    x = x_ref[...].astype(F32)
    inverse = lax.rsqrt(jnp.mean(x * x, axis=-1, keepdims=True) + EPSILON)
    input_grad_ref[...] = (d_resid_ref[...] + norm_back(x, inverse, gain_ref[...], d_normed)).astype(BF16)
    gain_grad_ref[...] = sum_rows(d_normed * x * inverse)
    bias_grad_ref[...] = sum_rows(d_joined.astype(F32))


def input_back(dq, terms, x, d_resid, weights, order, gain, cosine, sine):
    count, dim = x.shape
    joint = dq[0].shape[1] + 2 * LANES
    return call_whole(
        input_back_kernel,
        (*dq, *terms[0], *terms[1], x, d_resid, *weights, order, gain, cosine, sine),
        [
            jax.ShapeDtypeStruct((count, 2 * LANES), BF16),
            jax.ShapeDtypeStruct((count, dim), BF16),
            jax.ShapeDtypeStruct((1, dim), F32),
            jax.ShapeDtypeStruct((1, joint), F32),
        ],
        6 * count * dim * joint,
        "input_gradient",
    )


def seq_rows(seq, rows, cols):
    return pl.BlockSpec((rows, cols), lambda i: (seq, 0))


def piece_of(seq, rows):
    return pl.BlockSpec((1, rows, 2 * LANES), lambda i: (seq, 0, 0))


def keys_and_values(piece_refs):
    joint = jnp.concatenate([ref[0] for ref in piece_refs], axis=0)
    key, value = joint[:, :LANES], joint[:, LANES:]
    return (key, other_head(key)), (value, other_head(value))


def attend_kernel(block_ref, q_ref, kv_0, kv_1, kv_2, kv_3, start_ref, out_ref, level_ref):
    rows, width = q_ref.shape
    length = 4 * rows
    heads = width // HD
    group = heads // 2
    keys, values = keys_and_values((kv_0, kv_1, kv_2, kv_3))
    upper_key = lane_of((length, LANES)) >= HD
    upper = lane_of((rows, LANES)) >= HD
    query_at = block_ref[0] * rows + lax.broadcasted_iota(jnp.int32, (rows, length), 0)
    key_at = jnp.concatenate(
        [
            (block_ref[0] ^ place) * rows + lax.broadcasted_iota(jnp.int32, (rows, rows), 1)
            for place in range(4)
        ],
        axis=1,
    )
    allowed = (key_at <= query_at) & (key_at >= start_ref[:, :1])
    bias = jnp.where(allowed, 0.0, MASKED)
    one = jnp.ones((), BF16)
    lane = lane_of((rows, LANES))
    levels = jnp.zeros((rows, LANES), F32)
    for pair in range(heads // 2):
        at = slice(pair * LANES, (pair + 1) * LANES)
        both = q_ref[:, at]
        parts = []
        for place in range(2):
            owner = (2 * pair + place) // group
            moved = int(owner != place)
            side = upper if place else ~upper
            side_key = upper_key if place else ~upper_key
            query = jnp.where(side, both, jnp.zeros_like(both))
            score = dot_nt(query, keys[moved]) + bias
            top = jnp.max(score, axis=1, keepdims=True)
            weight = jnp.exp(score - top).astype(BF16)
            mixed = dot_nn(weight, jnp.where(side_key, values[moved], one))
            total = pltpu.roll(mixed, HD, 1)
            parts.append(mixed / total)
            level = top + jnp.log(total[:, place * HD : place * HD + 1])
            levels = jnp.where(lane == 2 * pair + place, level, levels)
        out_ref[:, at] = jnp.where(upper, parts[1], parts[0]).astype(BF16)
    level_ref[...] = levels


def attend(block, q, kv_pieces, start, rows, seq):
    width = q.shape[1]
    heads = width // HD
    return pl.pallas_call(
        attend_kernel,
        grid=(1,),
        in_specs=[
            pl.BlockSpec(memory_space=pltpu.SMEM),
            seq_rows(seq, rows, width),
            *[piece_of(seq, rows)] * 4,
            seq_rows(seq, rows, LANES),
        ],
        out_specs=[seq_rows(0, rows, width), seq_rows(0, rows, LANES)],
        out_shape=[jax.ShapeDtypeStruct((rows, width), BF16), jax.ShapeDtypeStruct((rows, LANES), F32)],
        compiler_params=pltpu.CompilerParams(vmem_limit_bytes=VMEM_LIMIT),
        cost_estimate=pl.CostEstimate(
            flops=32 * rows * rows * LANES * heads,
            bytes_accessed=4 * rows * width,
            transcendentals=4 * rows * rows * heads,
        ),
        name="attention_forward",
    )(block, q, *kv_pieces, start)


def attend_back_kernel(
    block_ref, q_ref, kv_0, kv_1, kv_2, kv_3, back_ref, out_ref, level_ref, start_ref, cos_ref, sin_ref,
    dq_ref, own_ref, core_ref, x_ref, far_ref, dk_sum, dv_sum,
):
    rows, width = q_ref.shape
    heads = width // HD
    group = heads // 2
    keys, values = keys_and_values((kv_0, kv_1, kv_2, kv_3))
    key_t = keys[0].astype(F32).T.astype(BF16)
    keys_t = (key_t, jnp.concatenate([key_t[HD:], key_t[:HD]], axis=0))
    upper = lane_of((rows, LANES)) >= HD
    upper_t = lax.broadcasted_iota(jnp.int32, (LANES, rows), 0) >= HD
    query_at = block_ref[0] * rows + lax.broadcasted_iota(jnp.int32, (rows, rows), 1)
    key_at = lax.broadcasted_iota(jnp.int32, (rows, rows), 0)
    biases = []
    for place in range(4):
        at = (block_ref[0] ^ place) * rows + key_at
        biases.append(jnp.where((at <= query_at) & (at >= start_ref[0, :1, :]), 0.0, MASKED))
    head_of = lax.broadcasted_iota(jnp.int32, (width, LANES), 0) // HD
    by_head = (head_of == lane_of((width, LANES))).astype(BF16)
    product = back_ref[...].astype(F32) * out_ref[...].astype(F32)
    product_high = product.astype(BF16)
    product_low = (product - product_high.astype(F32)).astype(BF16)
    row_sums = (dot_nn(product_high, by_head) + dot_nn(product_low, by_head)).T
    levels = level_ref[...].T
    cosine, sine = cos_ref[...], sin_ref[...]
    dk_sum[...] = jnp.zeros_like(dk_sum)
    dv_sum[...] = jnp.zeros_like(dv_sum)
    for pair in range(heads // 2):
        at = slice(pair * LANES, (pair + 1) * LANES)
        both = q_ref[:, at]
        back_both = back_ref[:, at]
        zero = jnp.zeros_like(both)
        sides = (~upper, upper)
        queries = [jnp.where(side, both, zero) for side in sides]
        backs = [jnp.where(side, back_both, zero) for side in sides]
        owners = [(2 * pair + place) // group for place in range(2)]
        d_query_t = [jnp.zeros((LANES, rows), F32) for _ in range(2)]
        for piece in range(4):
            span = slice(piece * rows, (piece + 1) * rows)
            probs, d_scores = [], []
            for place in range(2):
                head = 2 * pair + place
                moved = int(owners[place] != place)
                score = dot_nt(keys[moved][span], queries[place]) + biases[piece]
                prob = jnp.exp(score - levels[head : head + 1])
                d_prob = dot_nt(values[moved][span], backs[place])
                d_score = (prob * (d_prob - row_sums[head : head + 1])).astype(BF16)
                d_query_t[place] = d_query_t[place] + dot_nn(keys_t[moved][:, span], d_score)
                probs.append(prob.astype(BF16))
                d_scores.append(d_score)
            if owners[0] == owners[1]:
                dv_sum[owners[0], span] += dot_nn(
                    jnp.concatenate(probs, axis=1), jnp.concatenate(backs, axis=0)
                )
                dk_sum[owners[0], span] += dot_nn(
                    jnp.concatenate(d_scores, axis=1), jnp.concatenate(queries, axis=0)
                )
            else:
                for place in range(2):
                    dv_sum[owners[place], span] += dot_nn(probs[place], backs[place])
                    dk_sum[owners[place], span] += dot_nn(d_scores[place], queries[place])
        d_query = jnp.where(upper_t, d_query_t[1], d_query_t[0]).T * SCALE
        dq_ref[:, at] = (d_query * cosine - swap_halves(d_query) * sine).astype(BF16)
    lower_key = lane_of((4 * rows, LANES)) < HD
    for total, begin in ((dk_sum, 0), (dv_sum, LANES)):
        first, second = total[0], total[1]
        first = first + pltpu.roll(first, HD, 1)
        second = second + pltpu.roll(second, HD, 1)
        both = jnp.where(lower_key, first, second)
        cols = slice(begin, begin + LANES)
        own_ref[:, cols] = both[:rows]
        for place, ref in enumerate((core_ref, x_ref, far_ref)):
            ref[:, cols] = both[(place + 1) * rows : (place + 2) * rows].astype(BF16)


def parts_of(rows, cols):
    shapes = [jax.ShapeDtypeStruct((rows, cols), F32)] + [jax.ShapeDtypeStruct((rows, cols), BF16)] * 3
    return [seq_rows(0, rows, cols)] * 4, shapes


def attend_back(block, q, kv_pieces, back, out, level, start, cosine, sine, rows, seq):
    width = q.shape[1]
    length = 4 * rows
    heads = width // HD
    specs, shapes = parts_of(rows, 2 * LANES)
    return pl.pallas_call(
        attend_back_kernel,
        grid=(1,),
        in_specs=[
            pl.BlockSpec(memory_space=pltpu.SMEM),
            seq_rows(seq, rows, width),
            *[piece_of(seq, rows)] * 4,
            seq_rows(seq, rows, width),
            seq_rows(0, rows, width),
            seq_rows(0, rows, LANES),
            pl.BlockSpec((1, 8, rows), lambda i: (seq, 0, 0)),
            seq_rows(seq, rows, LANES),
            seq_rows(seq, rows, LANES),
        ],
        out_specs=[seq_rows(0, rows, width), *specs],
        out_shape=[jax.ShapeDtypeStruct((rows, width), BF16), *shapes],
        scratch_shapes=[
            pltpu.VMEM((2, length, LANES), F32),
            pltpu.VMEM((2, length, LANES), F32),
        ],
        compiler_params=pltpu.CompilerParams(vmem_limit_bytes=VMEM_LIMIT),
        cost_estimate=pl.CostEstimate(
            flops=80 * rows * rows * LANES * heads,
            bytes_accessed=8 * rows * width,
            transcendentals=4 * rows * rows * heads,
        ),
        name="attention_backward",
    )(block, q, *kv_pieces, back, out, level, start, cosine, sine)


def mlp_kernel(
    n_0, n_1, n_2, n_3, c_0, c_1, c_2, c_3, w_ref,
    own_ref, out_1, out_2, out_3, d_own_ref, d_1, d_2, d_3, kept_ref, turned_ref,
    normed_all, cot_all,
):
    step = pl.program_id(0)
    rows = own_ref.shape[0]
    columns = w_ref.shape[1] // 3

    @pl.when(step == 0)
    def _():
        for place, (n_ref, c_ref) in enumerate(zip((n_0, n_1, n_2, n_3), (c_0, c_1, c_2, c_3))):
            normed_all[place // 2, (place % 2) * rows : (place % 2 + 1) * rows] = n_ref[...]
            cot_all[place // 2, (place % 2) * rows : (place % 2 + 1) * rows] = c_ref[...]

    normed, cot = normed_all[step], cot_all[step]
    for begin in range(0, columns, TILE):
        at = slice(begin, begin + TILE)
        gate = dot_nn(normed, w_ref[:, begin : begin + TILE])
        up = dot_nn(normed, w_ref[:, columns + begin : columns + begin + TILE])
        d_act = dot_nn(cot, w_ref[:, 2 * columns + begin : 2 * columns + begin + TILE])
        sigmoid = 0.5 * jnp.tanh(0.5 * gate) + 0.5
        swish = gate * sigmoid
        kept_ref[0, :, at] = (d_act * up * (sigmoid + swish * (1.0 - sigmoid))).astype(BF16)
        kept_ref[1, :, at] = (d_act * swish).astype(BF16)
        kept_ref[2, :, at] = (swish * up).astype(BF16)
    turned_ref[0] = normed.T
    turned_ref[1] = cot.T
    out = dot_nt(kept_ref[2], w_ref[:, 2 * columns :])
    d_normed = dot_nt(kept_ref[0], w_ref[:, :columns]) + dot_nt(kept_ref[1], w_ref[:, columns : 2 * columns])

    @pl.when(step == 0)
    def _():
        own_ref[...] = out[:rows]
        out_1[...] = out[rows:].astype(BF16)
        d_own_ref[...] = d_normed[:rows]
        d_1[...] = d_normed[rows:].astype(BF16)

    @pl.when(step == 1)
    def _():
        out_2[...] = out[:rows].astype(BF16)
        out_3[...] = out[rows:].astype(BF16)
        d_2[...] = d_normed[:rows].astype(BF16)
        d_3[...] = d_normed[rows:].astype(BF16)


def mlp(normed, cot, weights, seq):
    rows, dim = normed[0].shape
    columns = weights.shape[1] // 3
    specs, shapes = parts_of(rows, dim)
    once = lambda at: pl.BlockSpec((rows, dim), lambda i: (at, 0), pipeline_mode=pl.Buffered(1))
    return pl.pallas_call(
        mlp_kernel,
        grid=(2,),
        in_specs=[
            *[once(0)] * 4,
            *[once(seq)] * 3,
            once(0),
            pl.BlockSpec(weights.shape, lambda i: (0, 0), pipeline_mode=pl.Buffered(1)),
        ],
        out_specs=[
            *specs,
            *specs,
            pl.BlockSpec((3, 2 * rows, columns), lambda i: (0, i, 0)),
            pl.BlockSpec((2, dim, 2 * rows), lambda i: (0, 0, i)),
        ],
        out_shape=[
            *shapes,
            *shapes,
            jax.ShapeDtypeStruct((3, 4 * rows, columns), BF16),
            jax.ShapeDtypeStruct((2, dim, 4 * rows), BF16),
        ],
        scratch_shapes=[
            pltpu.VMEM((2, 2 * rows, dim), BF16),
            pltpu.VMEM((2, 2 * rows, dim), BF16),
        ],
        compiler_params=pltpu.CompilerParams(vmem_limit_bytes=VMEM_LIMIT),
        cost_estimate=pl.CostEstimate(
            flops=48 * rows * dim * columns,
            bytes_accessed=6 * dim * columns + 24 * rows * columns,
            transcendentals=4 * rows * columns,
        ),
        name="feed_forward",
    )(*normed, *cot, weights)


def mlp_grad_kernel(turned_0, turned_1, kept_0, kept_1, grad_ref):
    grad_ref[...] = (dot_nn(turned_0[0], kept_0[0]) + dot_nn(turned_1[0], kept_1[0])).astype(BF16)


def mlp_grad(turned, kept):
    _, dim, count = turned[0].shape
    columns = kept[0].shape[2]
    turned_block = pl.BlockSpec((1, dim, count), lambda i: (i // 2, 0, 0))
    kept_block = pl.BlockSpec((1, count, columns), lambda i: (i, 0, 0))
    return pl.pallas_call(
        mlp_grad_kernel,
        grid=(3,),
        in_specs=[turned_block, turned_block, kept_block, kept_block],
        out_specs=pl.BlockSpec((dim, columns), lambda i: (0, i)),
        out_shape=jax.ShapeDtypeStruct((dim, 3 * columns), BF16),
        compiler_params=pltpu.CompilerParams(vmem_limit_bytes=VMEM_LIMIT),
        cost_estimate=pl.CostEstimate(
            flops=12 * count * dim * columns,
            bytes_accessed=6 * dim * columns + 12 * count * columns,
            transcendentals=0,
        ),
        name="feed_forward_gradients",
    )(*turned, *kept)


def pack_kernel(block_ref, gate_ref, up_ref, down_ref, *refs):
    out_refs, scratch = refs[:4], refs[4]
    shard, ff = gate_ref.shape
    quarter = scratch.shape[2] // 4
    for place, ref in enumerate((gate_ref, up_ref, down_ref)):
        scratch[place, :, :ff] = ref[...].astype(F32)
        scratch[place, :, ff:] = jnp.zeros((shard, 4 * quarter - ff), F32)
    for place, out_ref in enumerate(out_refs):
        begin = pl.multiple_of((block_ref[0] ^ place) * quarter, LANES)
        for part in range(3):
            out_ref[:, part * quarter : (part + 1) * quarter] = scratch[part, :, pl.ds(begin, quarter)].astype(BF16)


def pack(block, gate, up, down_t, quarter):
    shard = gate.shape[0]
    return pl.pallas_call(
        pack_kernel,
        in_specs=[pl.BlockSpec(memory_space=pltpu.SMEM)] + [pl.BlockSpec(memory_space=pltpu.VMEM)] * 3,
        out_specs=[pl.BlockSpec(memory_space=pltpu.VMEM)] * 4,
        out_shape=[jax.ShapeDtypeStruct((shard, 3 * quarter), BF16)] * 4,
        scratch_shapes=[pltpu.VMEM((3, shard, 4 * quarter), F32)],
        compiler_params=pltpu.CompilerParams(vmem_limit_bytes=VMEM_LIMIT),
        name="pack_columns",
    )(block, gate, up, down_t)


def pick(options, index):
    value = options[0]
    for place in range(1, len(options)):
        value = jnp.where(index == place, options[place], value)
    return value


def assemble_kernel(block_ref, *refs):
    pieces, out_ref, scratch = refs[:4], refs[4], refs[5]
    shard = pieces[0].shape[0]
    values = [ref[...].astype(F32) for ref in pieces]
    for owner in range(4):
        scratch[owner * shard : (owner + 1) * shard] = pick(values, block_ref[0] ^ owner)
    out_ref[...] = scratch[...].astype(BF16)


def assemble(block, pieces):
    shard, columns = pieces[0].shape
    return pl.pallas_call(
        assemble_kernel,
        in_specs=[pl.BlockSpec(memory_space=pltpu.SMEM)] + [pl.BlockSpec(memory_space=pltpu.VMEM)] * 4,
        out_specs=pl.BlockSpec(memory_space=pltpu.VMEM),
        out_shape=jax.ShapeDtypeStruct((4 * shard, columns), BF16),
        scratch_shapes=[pltpu.VMEM((4 * shard, columns), F32)],
        compiler_params=pltpu.CompilerParams(vmem_limit_bytes=VMEM_LIMIT),
        name="assemble_rows",
    )(block, *pieces)


def cut_kernel(block_ref, value_ref, *refs):
    out_refs, scratch = refs[:4], refs[4]
    shard = out_refs[0].shape[0]
    scratch[...] = value_ref[...].astype(F32)
    values = [scratch[owner * shard : (owner + 1) * shard] for owner in range(4)]
    for place, out_ref in enumerate(out_refs):
        out_ref[...] = pick(values, block_ref[0] ^ place).astype(BF16)


def cut(block, value):
    shard, columns = value.shape[0] // 4, value.shape[1]
    return pl.pallas_call(
        cut_kernel,
        in_specs=[pl.BlockSpec(memory_space=pltpu.SMEM), pl.BlockSpec(memory_space=pltpu.VMEM)],
        out_specs=[pl.BlockSpec(memory_space=pltpu.VMEM)] * 4,
        out_shape=[jax.ShapeDtypeStruct((shard, columns), BF16)] * 4,
        scratch_shapes=[pltpu.VMEM(value.shape, F32)],
        compiler_params=pltpu.CompilerParams(vmem_limit_bytes=VMEM_LIMIT),
        name="cut_rows",
    )(block, value)


def unpack_kernel(block_ref, *refs):
    pieces, out_refs, scratch = refs[:4], refs[4:7], refs[7]
    ff = out_refs[0].shape[1]
    quarter = scratch.shape[2] // 4
    for place, ref in enumerate(pieces):
        begin = pl.multiple_of((block_ref[0] ^ place) * quarter, LANES)
        for part in range(3):
            scratch[part, :, pl.ds(begin, quarter)] = ref[:, part * quarter : (part + 1) * quarter].astype(F32)
    for part, out_ref in enumerate(out_refs):
        out_ref[...] = scratch[part, :, :ff]


def unpack(block, pieces, ff):
    shard, columns = pieces[0].shape
    return pl.pallas_call(
        unpack_kernel,
        in_specs=[pl.BlockSpec(memory_space=pltpu.SMEM)] + [pl.BlockSpec(memory_space=pltpu.VMEM)] * 4,
        out_specs=[pl.BlockSpec(memory_space=pltpu.VMEM)] * 3,
        out_shape=[jax.ShapeDtypeStruct((shard, ff), F32)] * 3,
        scratch_shapes=[pltpu.VMEM((3, shard, columns // 3 * 4), F32)],
        compiler_params=pltpu.CompilerParams(vmem_limit_bytes=VMEM_LIMIT),
        name="unpack_columns",
    )(block, *pieces)


def bit_swap(value, axis, bit=0):
    size = lax.axis_size(axis)
    return lax.ppermute(value, axis, [(i, i ^ (1 << bit)) for i in range(size)])


def jump_swap(value, axes, jump):
    return lax.ppermute(value, axes, [(i, i ^ jump) for i in range(4)])


def to_plane(value, slot):
    high, low = slot >> 1, slot & 1
    pairs = [
        (4 * y + 2 * x + c, 4 * (c ^ low) + 2 * (x ^ high) + y) for y in range(2) for x in range(2) for c in range(2)
    ]
    return lax.ppermute(value, TOKENS + ("cc",), pairs)


def from_plane(value, slot):
    high, low = slot >> 1, slot & 1
    pairs = [
        (4 * y + 2 * x + c, 4 * c + 2 * (x ^ high) + (y ^ low)) for y in range(2) for x in range(2) for c in range(2)
    ]
    return lax.ppermute(value, TOKENS + ("cc",), pairs)


def after(first, *values):
    return lax.optimization_barrier((first, *values))


def gather_four(value, axes):
    from_first = bit_swap(value, axes[0])
    return [value, bit_swap(value, axes[1]), from_first, bit_swap(from_first, axes[1])]


def gather_direct(value, axes):
    return [value] + [jump_swap(value, axes, jump) for jump in range(1, 4)]


def sum_direct(axes, own, *away):
    return [own] + [jump_swap(value, axes, jump + 1) for jump, value in enumerate(away)]


def doubling_offsets(steps):
    weight = {"cc": 1, "cx": 2, "fy": 4, "fz": 8}
    offsets = [0]
    for axis, bit in steps:
        offsets += [offset ^ (weight[axis] << bit) for offset in offsets]
    return jnp.array(offsets, jnp.int32)


def double(value, axis, bit=0):
    return jnp.concatenate([value, bit_swap(value, axis, bit)], axis=0)


def plane_gather(value):
    return jnp.concatenate(gather_direct(value, TOKENS), axis=0)


def plane_sum(value):
    parts = jnp.split(value, 4, axis=0)
    terms = sum_direct(TOKENS, *parts)
    return sum(term.astype(F32) for term in terms).astype(BF16)


def halve(value, axis, bit=0):
    middle = value.shape[0] // 2
    came = bit_swap(value[middle:], axis, bit)
    return (value[:middle].astype(F32) + came.astype(F32)).astype(BF16)


def on_device(
    hidden,
    segments,
    attn_gain,
    qkv_weight,
    qkv_bias,
    out_weight,
    mlp_gain,
    gate_weight,
    up_weight,
    down_weight,
    cotangent,
):
    seqs, rows, dim = hidden.shape
    count = seqs * rows
    shard = attn_gain.shape[0]
    world = dim // shard
    joint = qkv_weight.shape[1]
    width = joint - 2 * LANES
    ff = gate_weight.shape[1]
    block = lax.axis_index("cx") * lax.axis_size("cc") + lax.axis_index("cc")
    me = lax.axis_index(FSDP) * lax.axis_size(CTX) + block
    offset = block * rows
    block_arg = block.reshape(1).astype(jnp.int32)
    plane_arg = (lax.axis_index("cx") * 2 + lax.axis_index("fy")).reshape(1).astype(jnp.int32)
    x = hidden.reshape(count, dim)
    cot = cotangent.reshape(count, dim)

    far = [("fz", bit) for bit in reversed(range((lax.axis_size("fz")).bit_length() - 1))]
    padded = -(-(shard + 1) // 16) * 16
    small = jnp.concatenate([attn_gain, mlp_gain, qkv_bias])
    small_row = jnp.pad(small, (0, joint + width - small.shape[0]))[None]
    first = jnp.concatenate(
        [
            jnp.concatenate([qkv_weight, out_weight.T], axis=1),
            small_row,
            jnp.zeros((padded - shard - 1, joint + width), BF16),
        ],
        axis=0,
    )
    first = double(first, *far[0])

    quarter = -(-ff // (4 * TILE)) * TILE
    first, *pieces = after(first, *pack(block_arg, gate_weight, up_weight, down_weight.T, quarter))
    pieces = [to_plane(piece, slot) for slot, piece in enumerate(pieces)]
    for axis, bit in far[1:]:
        first = double(first, axis, bit)

    within = jnp.arange(padded, dtype=jnp.int32)
    owner = me ^ doubling_offsets(far + [("cx", 0), ("fy", 0), ("cc", 0)])
    target = jnp.where(within[None, :] < shard, owner[:, None] * shard + within[None, :], -1).reshape(1, -1)
    order = (jnp.arange(dim, dtype=jnp.int32)[:, None] == target).astype(BF16)
    place = jnp.where(within[None, :] == shard, owner[:, None], -1).reshape(1, -1)
    spread = (jnp.arange(world, dtype=jnp.int32)[:, None] == place).astype(BF16)

    at_row = lax.dynamic_slice_in_dim(segments, offset, rows, axis=1)
    zeros_before = jnp.sum((segments < 1).astype(jnp.int32), axis=1, keepdims=True)
    ones_before = jnp.sum((segments < 2).astype(jnp.int32), axis=1, keepdims=True)
    start = jnp.where(at_row == 0, 0, jnp.where(at_row == 1, zeros_before, ones_before))
    position = (offset + jnp.arange(rows, dtype=jnp.int32)[None, :] - start).reshape(count)
    lane = jnp.arange(LANES, dtype=jnp.int32)
    frequency = ROPE_BASE ** (-(lane % (HD // 2)).astype(F32) * 2.0 / HD)
    angle = position.astype(F32)[:, None] * frequency[None, :]
    cosine = jnp.cos(angle)
    sine = jnp.where(lane % HD < HD // 2, -1.0, 1.0)[None, :] * jnp.sin(angle)
    start_column = jnp.broadcast_to(start.reshape(count, 1), (count, LANES))
    start_row = jnp.broadcast_to(start[:, None, :], (seqs, 8, rows))

    first, order, spread, cosine, sine, start_column, *pieces = after(
        first, order, spread, cosine, sine, start_column, *pieces
    )
    w_joint = plane_gather(first[:, :joint])
    mlp_shard = assemble(plane_arg, pieces)
    mlp_weights = lax.all_gather(mlp_shard, WEIGHTS, axis=0, tiled=True)
    w_joint = (w_joint, bit_swap(w_joint, "cc"))

    normed, q, kv, gain_attn, gain_mlp = prep(x, order, spread, w_joint, cosine, sine, rows)
    kv, w_out = after(kv, plane_gather(first[:, joint:]))
    kv_all = gather_four(kv.reshape(seqs, rows, 2 * LANES), CTX)

    w_out, cot_late = after(w_out, cot)
    w_out = (w_out, bit_swap(w_out, "cc"))
    cot_x, cot_y = bit_swap(cot_late, "cx"), bit_swap(cot_late, "fy")
    cot_far = [bit_swap(cot_x[:rows], "fy"), bit_swap(cot_y[rows:], "cx")]
    attended, levels, resid, normed_all = [], [], [], []
    for seq in range(seqs):
        turn = block_arg if seq == 0 else after(attended[0], block_arg)[1]
        attended_one, level_one = attend(turn, q, kv_all, start_column, rows, seq)
        attended.append(attended_one)
        levels.append(level_one)
        if seq == 1:
            attended[1], cot_x, cot_y = after(attended[1], cot_x, cot_y)
        resid_one, normed_one = project_out(attended[seq], x, w_out, order, gain_mlp, rows, seq)
        resid.append(resid_one)
        normed_all.append(gather_direct(normed_one, TOKENS))

    out_parts, d_terms, kept, turned = [], [], [], []
    for seq in range(seqs):
        if seq == 1:
            out_parts[0], normed_all[1] = lax.optimization_barrier((out_parts[0], normed_all[1]))
        result = mlp(normed_all[seq], [cot, cot_x, cot_y, cot_far[seq]], mlp_weights, seq)
        out_parts.append(result[:4])
        d_terms.append(sum_direct(TOKENS, *result[4:8]))
        kept.append(result[8])
        turned.append(result[9])
    turned[1], *d_terms[0] = after(turned[1], *d_terms[0])
    grads = mlp_grad(turned, kept)
    grads, d_terms[0], d_terms[1] = after(grads, *d_terms)
    grads = lax.psum_scatter(
        grads.reshape(world // 4, 4 * shard, 3 * quarter), WEIGHTS, scatter_dimension=0, tiled=False
    )

    d_resid, d_branch, d_attended, mlp_gain_grad = project_out_back(
        d_terms, resid, cot, w_out, order, gain_mlp
    )
    out_grad = dot_tn(d_branch, jnp.concatenate(attended, axis=0)).astype(BF16)
    out_grad = halve(out_grad, "cc")
    out_terms = [sum_direct(TOKENS, *after(d_terms[1][1], *part)[1:]) for part in out_parts]
    d_attended, out_terms[0] = after(d_attended, out_terms[0])
    dq, dkv_terms = [], []
    for seq in range(seqs):
        if seq == 1:
            dq[0], d_attended, out_grad, out_terms[1] = after(dq[0], d_attended, out_grad, out_terms[1])
            out_grad = plane_sum(out_grad)
        result = attend_back(
            block_arg, q, kv_all, d_attended, attended[seq], levels[seq], start_row, cosine, sine, rows, seq
        )
        dq.append(result[0])
        dkv_terms.append(sum_direct(CTX, *result[1:]))
    dq[1], out_grad, *dkv_terms[0] = after(dq[1], out_grad, *dkv_terms[0])
    q_grad = dot_tn(normed, jnp.concatenate(dq, axis=0)).astype(BF16)
    q_grad = halve(q_grad, "cc")
    q_grad, *dkv_terms[1] = after(q_grad, *dkv_terms[1])
    q_grad = plane_sum(q_grad)
    d_kv, input_grad, attn_gain_grad, bias_grad = input_back(
        dq, dkv_terms, x, d_resid, w_joint, order, gain_attn, cosine, sine
    )
    d_kv, q_grad = after(d_kv, q_grad)

    output = []
    for seq in range(seqs):
        own, *away = out_terms[seq]
        output.append((resid[seq] + own + sum(term.astype(F32) for term in away)).astype(BF16))

    split_at = width + LANES
    bias_grad = bias_grad[0]
    small_grads = jnp.concatenate(
        [
            attn_gain_grad.reshape(world, -1),
            mlp_gain_grad.reshape(world, -1),
            bias_grad[:split_at].reshape(world, -1),
            bias_grad[split_at:].reshape(world, -1),
        ],
        axis=1,
    ).astype(BF16)
    small_count = small_grads.shape[1]
    small_grads = jnp.pad(small_grads, ((0, 0), (0, 2 * LANES - small_count)))
    kv_grad = dot_tn(
        jnp.concatenate([normed, spread], axis=0), jnp.concatenate([d_kv, small_grads], axis=0)
    ).astype(BF16)
    pieces = cut(plane_arg, lax.optimization_barrier(grads))
    kv_grad, *pieces = after(halve(kv_grad, "cc"), *pieces)
    pieces = [from_plane(piece, slot) for slot, piece in enumerate(pieces)]
    first_sum = jnp.concatenate([q_grad, plane_sum(kv_grad), out_grad], axis=1)
    for axis, bit in reversed(far):
        first_sum = halve(first_sum, axis, bit)
    gate_grad, up_grad, down_grad_t = unpack(block_arg, pieces, ff)
    first_sum = first_sum.astype(F32)
    qkv_sum, out_sum = first_sum[:, :joint], first_sum[:, joint:]
    small_sum = qkv_sum[shard, width : width + small_count]
    at = (shard, 2 * shard, 2 * shard + split_at // world)

    return (
        jnp.stack(output),
        input_grad.reshape(hidden.shape),
        small_sum[: at[0]],
        qkv_sum[:shard],
        small_sum[at[1] : at[2]],
        small_sum[at[2] :],
        out_sum[:shard].T,
        small_sum[at[0] : at[1]],
        gate_grad,
        up_grad,
        down_grad_t.T,
    )


def solution(mesh):
    fsdp, ctx = mesh.shape["fsdp"], mesh.shape["ctx"]
    inner = Mesh(mesh.devices.reshape(fsdp // 2, 2, 2, ctx // 2), AXES)
    tokens = P(FSDP, CTX, None)
    vector = P(AXES)
    by_row = P(AXES, None)
    by_column = P(None, AXES)
    return jax.shard_map(
        on_device,
        mesh=inner,
        in_specs=(
            tokens,
            P(FSDP, None),
            vector,
            by_row,
            vector,
            by_column,
            vector,
            by_row,
            by_row,
            by_column,
            tokens,
        ),
        out_specs=(
            tokens,
            tokens,
            vector,
            by_row,
            vector,
            vector,
            by_column,
            vector,
            by_row,
            by_row,
            by_column,
        ),
        check_vma=False,
    )
```

```python
import functools

import jax
import jax.numpy as jnp
from jax import lax
from jax.experimental import pallas as pl
from jax.experimental.pallas import tpu as pltpu
from jax.sharding import Mesh
from jax.sharding import PartitionSpec as P

HD = 64
LANES = 128
EPSILON = 1e-06
ROPE_BASE = 1000000.0
MASKED = -1e30
SCALE = HD ** (-0.5)
TILE = 256
MIB = 1 << 20
VMEM_LIMIT = 60 * MIB
F32 = jnp.float32
BF16 = jnp.bfloat16
AXES = ("fz", "fy", "cx", "cc")
FSDP = ("fz", "fy")
CTX = ("cx", "cc")
TOKENS = ("fy", "cx")
WEIGHTS = ("fz", "cc")


def dot_nn(a, b):
    return lax.dot_general(a, b, (((1,), (0,)), ((), ())), preferred_element_type=F32)


def dot_nt(a, b):
    return lax.dot_general(a, b, (((1,), (1,)), ((), ())), preferred_element_type=F32)


def dot_tn(a, b):
    return lax.dot_general(a, b, (((0,), (0,)), ((), ())), preferred_element_type=F32)


def lane_of(shape):
    return lax.broadcasted_iota(jnp.int32, shape, len(shape) - 1)


def swap_halves(block):
    lead = lane_of(block.shape) % HD < HD // 2
    return jnp.where(
        lead, pltpu.roll(block, LANES - HD // 2, 1), pltpu.roll(block, HD // 2, 1)
    )


def other_head(block):
    return jnp.concatenate([block[:, HD:], block[:, :HD]], axis=1)


def read_out(extras, first, piece, total):
    owners, columns = extras.shape
    at = lax.broadcasted_iota(jnp.int32, (columns, total), 1) % piece + first
    chosen = (lax.broadcasted_iota(jnp.int32, (columns, total), 0) == at).astype(BF16)
    spread = dot_nn(extras, chosen)
    owner = lax.broadcasted_iota(jnp.int32, (owners, total), 1) // piece
    mine = owner == lax.broadcasted_iota(jnp.int32, (owners, total), 0)
    return jnp.sum(jnp.where(mine, spread, 0.0), axis=0, keepdims=True)


def prep_kernel(
    x_ref, order_ref, spread_ref, w_low_ref, w_high_ref, cos_ref, sin_ref,
    normed_ref, q_ref, kv_ref, gain_ref, gain_mlp_ref, bias_ref,
):
    x = x_ref[...].astype(F32)
    dim = x.shape[1]
    width = q_ref.shape[1]
    joint = w_low_ref.shape[1]
    middle = w_low_ref.shape[0]
    owners = spread_ref.shape[0]

    @pl.when(pl.program_id(0) == 0)
    def _():
        extras = dot_nn(spread_ref[:, :middle], w_low_ref[:, :LANES])
        extras = (extras + dot_nn(spread_ref[:, middle:], w_high_ref[:, :LANES])).astype(BF16)
        shard = dim // owners
        gain_ref[...] = read_out(extras, 0, shard, dim)
        gain_mlp_ref[...] = read_out(extras, shard, shard, dim)
        bias_ref[...] = read_out(extras, 2 * shard, joint // owners, joint)

    gain, bias = gain_ref[...], bias_ref[...]
    inverse = lax.rsqrt(jnp.mean(x * x, axis=-1, keepdims=True) + EPSILON)
    normed = (x * inverse * gain).astype(BF16)
    ordered = dot_nn(normed, order_ref[...]).astype(BF16)
    normed_ref[...] = ordered
    joined = dot_nn(ordered[:, :middle], w_low_ref[...])
    joined = joined + dot_nn(ordered[:, middle:], w_high_ref[...]) + bias
    cosine, sine = cos_ref[...], sin_ref[...]
    for begin in range(0, width + LANES, LANES):
        block = joined[:, begin : begin + LANES]
        turned = block * cosine + swap_halves(block) * sine
        if begin < width:
            q_ref[:, begin : begin + LANES] = (turned * SCALE).astype(BF16)
        else:
            kv_ref[:, :LANES] = turned.astype(BF16)
    kv_ref[:, LANES:] = joined[:, width + LANES :].astype(BF16)


def rows_of(rows, cols):
    return pl.BlockSpec((rows, cols), lambda i: (i, 0))


def whole(value):
    return pl.BlockSpec(value.shape, lambda i: (0,) * value.ndim)


def prep(x, order, spread, weights, cosine, sine, rows):
    count, dim = x.shape
    ordered = order.shape[1]
    joint = weights[0].shape[1]
    width = joint - 2 * LANES
    row = pl.BlockSpec((1, dim), lambda i: (0, 0))
    return pl.pallas_call(
        prep_kernel,
        grid=(count // rows,),
        in_specs=[
            rows_of(rows, dim),
            whole(order),
            whole(spread),
            whole(weights[0]),
            whole(weights[1]),
            rows_of(rows, LANES),
            rows_of(rows, LANES),
        ],
        out_specs=[rows_of(rows, ordered), rows_of(rows, width), rows_of(rows, 2 * LANES), row, row],
        out_shape=[
            jax.ShapeDtypeStruct((count, ordered), BF16),
            jax.ShapeDtypeStruct((count, width), BF16),
            jax.ShapeDtypeStruct((count, 2 * LANES), BF16),
            jax.ShapeDtypeStruct((1, dim), F32),
            jax.ShapeDtypeStruct((1, dim), F32),
        ],
        scratch_shapes=[pltpu.VMEM((1, joint), F32)],
        compiler_params=pltpu.CompilerParams(vmem_limit_bytes=VMEM_LIMIT),
        cost_estimate=pl.CostEstimate(
            flops=2 * count * ordered * (joint + dim), bytes_accessed=12 * MIB, transcendentals=0
        ),
        name="norm_project_rotate",
    )(x, order, spread, weights[0], weights[1], cosine, sine)


def back_in_order(value, order):
    high = value.astype(BF16)
    low = (value - high.astype(F32)).astype(BF16)
    return dot_nt(high, order) + dot_nt(low, order)


def out_kernel(attended_ref, x_ref, w_low_ref, w_high_ref, order_ref, gain_ref, resid_ref, normed_ref):
    attended = attended_ref[...]
    branch = jnp.concatenate([dot_nt(attended, w_low_ref[...]), dot_nt(attended, w_high_ref[...])], axis=1)
    resid = x_ref[...].astype(F32) + back_in_order(branch, order_ref[...])
    inverse = lax.rsqrt(jnp.mean(resid * resid, axis=-1, keepdims=True) + EPSILON)
    resid_ref[...] = resid
    normed_ref[...] = (resid * inverse * gain_ref[...]).astype(BF16)


def project_out(attended, x, weights, order, gain, rows, seq):
    dim = x.shape[1]
    count = rows
    return pl.pallas_call(
        out_kernel,
        grid=(1,),
        in_specs=[
            rows_of(rows, attended.shape[1]),
            pl.BlockSpec((rows, dim), lambda i: (seq, 0)),
            whole(weights[0]),
            whole(weights[1]),
            whole(order),
            whole(gain),
        ],
        out_specs=[rows_of(rows, dim), rows_of(rows, dim)],
        out_shape=[jax.ShapeDtypeStruct((count, dim), F32), jax.ShapeDtypeStruct((count, dim), BF16)],
        compiler_params=pltpu.CompilerParams(vmem_limit_bytes=VMEM_LIMIT),
        cost_estimate=pl.CostEstimate(flops=6 * count * dim * dim, bytes_accessed=8 * MIB, transcendentals=0),
        name="project_out_norm",
    )(attended, x, weights[0], weights[1], order, gain)


def sum_rows(value):
    return jnp.sum(value, axis=0, keepdims=True)


def norm_back(values, inverse, gain, incoming):
    scaled = incoming * gain
    mean_term = jnp.mean(scaled * values, axis=-1, keepdims=True)
    return inverse * scaled - values * inverse**3 * mean_term


def total_of(own_ref, *away_refs):
    total = own_ref[...]
    for ref in away_refs:
        total = total + ref[...].astype(F32)
    return total


def out_back_kernel(
    own_ref, core_ref, x_ref, far_ref, resid_ref, cot_ref, w_low_ref, w_high_ref, order_ref, gain_ref,
    d_resid_ref, d_branch_ref, d_attended_ref, gain_grad_ref,
):
    middle = w_low_ref.shape[0]
    d_normed = total_of(own_ref, core_ref, x_ref, far_ref)
    resid = resid_ref[...]
    inverse = lax.rsqrt(jnp.mean(resid * resid, axis=-1, keepdims=True) + EPSILON)
    d_resid = cot_ref[...].astype(F32) + norm_back(resid, inverse, gain_ref[...], d_normed)
    d_resid_ref[...] = d_resid
    d_branch = dot_nn(d_resid.astype(BF16), order_ref[...]).astype(BF16)
    d_branch_ref[...] = d_branch
    d_attended = dot_nn(d_branch[:, :middle], w_low_ref[...])
    d_attended = d_attended + dot_nn(d_branch[:, middle:], w_high_ref[...])
    d_attended_ref[...] = d_attended.astype(BF16)
    gain_grad_ref[...] = sum_rows(d_normed * resid * inverse)


def project_out_back(terms, resid, cot, weights, order, gain, rows, seq):
    count, dim = resid.shape
    ordered = order.shape[1]
    width = dim
    return pl.pallas_call(
        out_back_kernel,
        grid=(1,),
        in_specs=[
            rows_of(rows, dim),
            rows_of(rows, dim),
            rows_of(rows, dim),
            rows_of(rows, dim),
            rows_of(rows, dim),
            pl.BlockSpec((rows, dim), lambda i: (seq, 0)),
            whole(weights[0]),
            whole(weights[1]),
            whole(order),
            whole(gain),
        ],
        out_specs=[
            rows_of(rows, dim),
            rows_of(rows, ordered),
            rows_of(rows, width),
            pl.BlockSpec((1, dim), lambda i: (0, 0)),
        ],
        out_shape=[
            jax.ShapeDtypeStruct((count, dim), F32),
            jax.ShapeDtypeStruct((count, ordered), BF16),
            jax.ShapeDtypeStruct((count, width), BF16),
            jax.ShapeDtypeStruct((1, dim), F32),
        ],
        compiler_params=pltpu.CompilerParams(vmem_limit_bytes=VMEM_LIMIT),
        cost_estimate=pl.CostEstimate(flops=4 * count * dim * dim, bytes_accessed=12 * MIB, transcendentals=0),
        name="norm_back_project",
    )(*terms, resid, cot, weights[0], weights[1], order, gain)


def call_whole(kernel, operands, out_shape, flops, name):
    return pl.pallas_call(
        kernel,
        in_specs=[pl.BlockSpec(memory_space=pltpu.VMEM)] * len(operands),
        out_specs=[pl.BlockSpec(memory_space=pltpu.VMEM)] * len(out_shape),
        out_shape=out_shape,
        compiler_params=pltpu.CompilerParams(vmem_limit_bytes=VMEM_LIMIT),
        cost_estimate=pl.CostEstimate(flops=flops, bytes_accessed=16 * MIB, transcendentals=0),
        name=name,
    )(*operands)


def input_back_kernel(*refs):
    dqs, terms = refs[:2], refs[2:10]
    x_ref, d_resid_ref, w_low_ref, w_high_ref, order_ref, gain_ref, cos_ref, sin_ref = refs[10:18]
    d_kv_ref, input_grad_ref, gain_grad_ref, bias_grad_ref = refs[18:]
    dkv = jnp.concatenate([total_of(*terms[:4]), total_of(*terms[4:])], axis=0)
    dk = dkv[:, :LANES]
    dk = dk * cos_ref[...] - swap_halves(dk) * sin_ref[...]
    d_kv = jnp.concatenate([dk.astype(BF16), dkv[:, LANES:].astype(BF16)], axis=1)
    d_kv_ref[...] = d_kv
    dq = jnp.concatenate([ref[...] for ref in dqs], axis=0)
    d_joined = jnp.concatenate([dq, d_kv], axis=1)
    d_normed = jnp.concatenate([dot_nt(d_joined, w_low_ref[...]), dot_nt(d_joined, w_high_ref[...])], axis=1)
    d_normed = back_in_order(d_normed, order_ref[...])
    x = x_ref[...].astype(F32)
    inverse = lax.rsqrt(jnp.mean(x * x, axis=-1, keepdims=True) + EPSILON)
    input_grad_ref[...] = (d_resid_ref[...] + norm_back(x, inverse, gain_ref[...], d_normed)).astype(BF16)
    gain_grad_ref[...] = sum_rows(d_normed * x * inverse)
    bias_grad_ref[...] = sum_rows(d_joined.astype(F32))


def input_back(dq, terms, x, d_resid, weights, order, gain, cosine, sine):
    count, dim = x.shape
    joint = dq[0].shape[1] + 2 * LANES
    return call_whole(
        input_back_kernel,
        (*dq, *terms[0], *terms[1], x, d_resid, *weights, order, gain, cosine, sine),
        [
            jax.ShapeDtypeStruct((count, 2 * LANES), BF16),
            jax.ShapeDtypeStruct((count, dim), BF16),
            jax.ShapeDtypeStruct((1, dim), F32),
            jax.ShapeDtypeStruct((1, joint), F32),
        ],
        6 * count * dim * joint,
        "input_gradient",
    )


def seq_rows(seq, rows, cols):
    return pl.BlockSpec((rows, cols), lambda i: (seq, 0))


def piece_of(seq, rows):
    return pl.BlockSpec((1, rows, 2 * LANES), lambda i: (seq, 0, 0))


def keys_and_values(piece_refs):
    joint = jnp.concatenate([ref[0] for ref in piece_refs], axis=0)
    key, value = joint[:, :LANES], joint[:, LANES:]
    return (key, other_head(key)), (value, other_head(value))


def attend_kernel(block_ref, q_ref, kv_0, kv_1, kv_2, kv_3, start_ref, out_ref, level_ref):
    rows, width = q_ref.shape
    length = 4 * rows
    heads = width // HD
    group = heads // 2
    keys, values = keys_and_values((kv_0, kv_1, kv_2, kv_3))
    upper_key = lane_of((length, LANES)) >= HD
    upper = lane_of((rows, LANES)) >= HD
    query_at = block_ref[0] * rows + lax.broadcasted_iota(jnp.int32, (rows, length), 0)
    key_at = jnp.concatenate(
        [
            (block_ref[0] ^ place) * rows + lax.broadcasted_iota(jnp.int32, (rows, rows), 1)
            for place in range(4)
        ],
        axis=1,
    )
    allowed = (key_at <= query_at) & (key_at >= start_ref[:, :1])
    bias = jnp.where(allowed, 0.0, MASKED)
    one = jnp.ones((), BF16)
    lane = lane_of((rows, LANES))
    levels = jnp.zeros((rows, LANES), F32)
    for pair in range(heads // 2):
        at = slice(pair * LANES, (pair + 1) * LANES)
        both = q_ref[:, at]
        parts = []
        for place in range(2):
            owner = (2 * pair + place) // group
            moved = int(owner != place)
            side = upper if place else ~upper
            side_key = upper_key if place else ~upper_key
            query = jnp.where(side, both, jnp.zeros_like(both))
            score = dot_nt(query, keys[moved]) + bias
            top = jnp.max(score, axis=1, keepdims=True)
            weight = jnp.exp(score - top).astype(BF16)
            mixed = dot_nn(weight, jnp.where(side_key, values[moved], one))
            total = pltpu.roll(mixed, HD, 1)
            parts.append(mixed / total)
            level = top + jnp.log(total[:, place * HD : place * HD + 1])
            levels = jnp.where(lane == 2 * pair + place, level, levels)
        out_ref[:, at] = jnp.where(upper, parts[1], parts[0]).astype(BF16)
    level_ref[...] = levels


def attend(block, q, kv_pieces, start, rows, seq):
    width = q.shape[1]
    heads = width // HD
    return pl.pallas_call(
        attend_kernel,
        grid=(1,),
        in_specs=[
            pl.BlockSpec(memory_space=pltpu.SMEM),
            seq_rows(seq, rows, width),
            *[piece_of(seq, rows)] * 4,
            seq_rows(seq, rows, LANES),
        ],
        out_specs=[seq_rows(0, rows, width), seq_rows(0, rows, LANES)],
        out_shape=[jax.ShapeDtypeStruct((rows, width), BF16), jax.ShapeDtypeStruct((rows, LANES), F32)],
        compiler_params=pltpu.CompilerParams(vmem_limit_bytes=VMEM_LIMIT),
        cost_estimate=pl.CostEstimate(
            flops=32 * rows * rows * LANES * heads,
            bytes_accessed=4 * rows * width,
            transcendentals=4 * rows * rows * heads,
        ),
        name="attention_forward",
    )(block, q, *kv_pieces, start)


def attend_back_kernel(
    block_ref, q_ref, kv_0, kv_1, kv_2, kv_3, back_ref, out_ref, level_ref, start_ref, cos_ref, sin_ref,
    dq_ref, own_ref, core_ref, x_ref, far_ref, dk_sum, dv_sum,
):
    rows, width = q_ref.shape
    heads = width // HD
    group = heads // 2
    keys, values = keys_and_values((kv_0, kv_1, kv_2, kv_3))
    key_t = keys[0].astype(F32).T.astype(BF16)
    keys_t = (key_t, jnp.concatenate([key_t[HD:], key_t[:HD]], axis=0))
    upper = lane_of((rows, LANES)) >= HD
    upper_t = lax.broadcasted_iota(jnp.int32, (LANES, rows), 0) >= HD
    query_at = block_ref[0] * rows + lax.broadcasted_iota(jnp.int32, (rows, rows), 1)
    key_at = lax.broadcasted_iota(jnp.int32, (rows, rows), 0)
    biases = []
    for place in range(4):
        at = (block_ref[0] ^ place) * rows + key_at
        biases.append(jnp.where((at <= query_at) & (at >= start_ref[0, :1, :]), 0.0, MASKED))
    head_of = lax.broadcasted_iota(jnp.int32, (width, LANES), 0) // HD
    by_head = (head_of == lane_of((width, LANES))).astype(BF16)
    product = back_ref[...].astype(F32) * out_ref[...].astype(F32)
    product_high = product.astype(BF16)
    product_low = (product - product_high.astype(F32)).astype(BF16)
    row_sums = (dot_nn(product_high, by_head) + dot_nn(product_low, by_head)).T
    levels = level_ref[...].T
    cosine, sine = cos_ref[...], sin_ref[...]
    dk_sum[...] = jnp.zeros_like(dk_sum)
    dv_sum[...] = jnp.zeros_like(dv_sum)
    for pair in range(heads // 2):
        at = slice(pair * LANES, (pair + 1) * LANES)
        both = q_ref[:, at]
        back_both = back_ref[:, at]
        zero = jnp.zeros_like(both)
        sides = (~upper, upper)
        queries = [jnp.where(side, both, zero) for side in sides]
        backs = [jnp.where(side, back_both, zero) for side in sides]
        owners = [(2 * pair + place) // group for place in range(2)]
        d_query_t = [jnp.zeros((LANES, rows), F32) for _ in range(2)]
        for piece in range(4):
            span = slice(piece * rows, (piece + 1) * rows)
            probs, d_scores = [], []
            for place in range(2):
                head = 2 * pair + place
                moved = int(owners[place] != place)
                score = dot_nt(keys[moved][span], queries[place]) + biases[piece]
                prob = jnp.exp(score - levels[head : head + 1])
                d_prob = dot_nt(values[moved][span], backs[place])
                d_score = (prob * (d_prob - row_sums[head : head + 1])).astype(BF16)
                d_query_t[place] = d_query_t[place] + dot_nn(keys_t[moved][:, span], d_score)
                probs.append(prob.astype(BF16))
                d_scores.append(d_score)
            if owners[0] == owners[1]:
                dv_sum[owners[0], span] += dot_nn(
                    jnp.concatenate(probs, axis=1), jnp.concatenate(backs, axis=0)
                )
                dk_sum[owners[0], span] += dot_nn(
                    jnp.concatenate(d_scores, axis=1), jnp.concatenate(queries, axis=0)
                )
            else:
                for place in range(2):
                    dv_sum[owners[place], span] += dot_nn(probs[place], backs[place])
                    dk_sum[owners[place], span] += dot_nn(d_scores[place], queries[place])
        d_query = jnp.where(upper_t, d_query_t[1], d_query_t[0]).T * SCALE
        dq_ref[:, at] = (d_query * cosine - swap_halves(d_query) * sine).astype(BF16)
    lower_key = lane_of((4 * rows, LANES)) < HD
    for total, begin in ((dk_sum, 0), (dv_sum, LANES)):
        first, second = total[0], total[1]
        first = first + pltpu.roll(first, HD, 1)
        second = second + pltpu.roll(second, HD, 1)
        both = jnp.where(lower_key, first, second)
        cols = slice(begin, begin + LANES)
        own_ref[:, cols] = both[:rows]
        for place, ref in enumerate((core_ref, x_ref, far_ref)):
            ref[:, cols] = both[(place + 1) * rows : (place + 2) * rows].astype(BF16)


def parts_of(rows, cols):
    shapes = [jax.ShapeDtypeStruct((rows, cols), F32)] + [jax.ShapeDtypeStruct((rows, cols), BF16)] * 3
    return [seq_rows(0, rows, cols)] * 4, shapes


def attend_back(block, q, kv_pieces, back, out, level, start, cosine, sine, rows, seq):
    width = q.shape[1]
    length = 4 * rows
    heads = width // HD
    specs, shapes = parts_of(rows, 2 * LANES)
    return pl.pallas_call(
        attend_back_kernel,
        grid=(1,),
        in_specs=[
            pl.BlockSpec(memory_space=pltpu.SMEM),
            seq_rows(seq, rows, width),
            *[piece_of(seq, rows)] * 4,
            seq_rows(0, rows, width),
            seq_rows(0, rows, width),
            seq_rows(0, rows, LANES),
            pl.BlockSpec((1, 8, rows), lambda i: (seq, 0, 0)),
            seq_rows(seq, rows, LANES),
            seq_rows(seq, rows, LANES),
        ],
        out_specs=[seq_rows(0, rows, width), *specs],
        out_shape=[jax.ShapeDtypeStruct((rows, width), BF16), *shapes],
        scratch_shapes=[
            pltpu.VMEM((2, length, LANES), F32),
            pltpu.VMEM((2, length, LANES), F32),
        ],
        compiler_params=pltpu.CompilerParams(vmem_limit_bytes=VMEM_LIMIT),
        cost_estimate=pl.CostEstimate(
            flops=80 * rows * rows * LANES * heads,
            bytes_accessed=8 * rows * width,
            transcendentals=4 * rows * rows * heads,
        ),
        name="attention_backward",
    )(block, q, *kv_pieces, back, out, level, start, cosine, sine)


def mlp_kernel(
    n_0, n_1, n_2, n_3, c_0, c_1, c_2, c_3, w_ref,
    own_ref, out_1, out_2, out_3, d_own_ref, d_1, d_2, d_3, kept_ref, turned_ref,
    normed_all, cot_all,
):
    step = pl.program_id(0)
    rows = own_ref.shape[0]
    columns = w_ref.shape[1] // 3

    @pl.when(step == 0)
    def _():
        for place, (n_ref, c_ref) in enumerate(zip((n_0, n_1, n_2, n_3), (c_0, c_1, c_2, c_3))):
            normed_all[place // 2, (place % 2) * rows : (place % 2 + 1) * rows] = n_ref[...]
            cot_all[place // 2, (place % 2) * rows : (place % 2 + 1) * rows] = c_ref[...]

    normed, cot = normed_all[step], cot_all[step]
    for begin in range(0, columns, TILE):
        at = slice(begin, begin + TILE)
        gate = dot_nn(normed, w_ref[:, begin : begin + TILE])
        up = dot_nn(normed, w_ref[:, columns + begin : columns + begin + TILE])
        d_act = dot_nn(cot, w_ref[:, 2 * columns + begin : 2 * columns + begin + TILE])
        sigmoid = 0.5 * jnp.tanh(0.5 * gate) + 0.5
        swish = gate * sigmoid
        kept_ref[0, :, at] = (d_act * up * (sigmoid + swish * (1.0 - sigmoid))).astype(BF16)
        kept_ref[1, :, at] = (d_act * swish).astype(BF16)
        kept_ref[2, :, at] = (swish * up).astype(BF16)
    turned_ref[0] = normed.T
    turned_ref[1] = cot.T
    out = dot_nt(kept_ref[2], w_ref[:, 2 * columns :])
    d_normed = dot_nt(kept_ref[0], w_ref[:, :columns]) + dot_nt(kept_ref[1], w_ref[:, columns : 2 * columns])

    @pl.when(step == 0)
    def _():
        own_ref[...] = out[:rows]
        out_1[...] = out[rows:].astype(BF16)
        d_own_ref[...] = d_normed[:rows]
        d_1[...] = d_normed[rows:].astype(BF16)

    @pl.when(step == 1)
    def _():
        out_2[...] = out[:rows].astype(BF16)
        out_3[...] = out[rows:].astype(BF16)
        d_2[...] = d_normed[:rows].astype(BF16)
        d_3[...] = d_normed[rows:].astype(BF16)


def mlp(normed, cot, weights, seq):
    rows, dim = normed[0].shape
    columns = weights.shape[1] // 3
    specs, shapes = parts_of(rows, dim)
    once = lambda at: pl.BlockSpec((rows, dim), lambda i: (at, 0), pipeline_mode=pl.Buffered(1))
    return pl.pallas_call(
        mlp_kernel,
        grid=(2,),
        in_specs=[
            *[once(0)] * 4,
            *[once(seq)] * 3,
            once(0),
            pl.BlockSpec(weights.shape, lambda i: (0, 0), pipeline_mode=pl.Buffered(1)),
        ],
        out_specs=[
            *specs,
            *specs,
            pl.BlockSpec((3, 2 * rows, columns), lambda i: (0, i, 0)),
            pl.BlockSpec((2, dim, 2 * rows), lambda i: (0, 0, i)),
        ],
        out_shape=[
            *shapes,
            *shapes,
            jax.ShapeDtypeStruct((3, 4 * rows, columns), BF16),
            jax.ShapeDtypeStruct((2, dim, 4 * rows), BF16),
        ],
        scratch_shapes=[
            pltpu.VMEM((2, 2 * rows, dim), BF16),
            pltpu.VMEM((2, 2 * rows, dim), BF16),
        ],
        compiler_params=pltpu.CompilerParams(vmem_limit_bytes=VMEM_LIMIT),
        cost_estimate=pl.CostEstimate(
            flops=48 * rows * dim * columns,
            bytes_accessed=6 * dim * columns + 24 * rows * columns,
            transcendentals=4 * rows * columns,
        ),
        name="feed_forward",
    )(*normed, *cot, weights)


def mlp_grad_kernel(turned_0, turned_1, kept_0, kept_1, grad_ref):
    grad_ref[...] = (dot_nn(turned_0[0], kept_0[0]) + dot_nn(turned_1[0], kept_1[0])).astype(BF16)


def mlp_grad(turned, kept):
    _, dim, count = turned[0].shape
    columns = kept[0].shape[2]
    turned_block = pl.BlockSpec((1, dim, count), lambda i: (i // 2, 0, 0))
    kept_block = pl.BlockSpec((1, count, columns), lambda i: (i, 0, 0))
    return pl.pallas_call(
        mlp_grad_kernel,
        grid=(3,),
        in_specs=[turned_block, turned_block, kept_block, kept_block],
        out_specs=pl.BlockSpec((dim, columns), lambda i: (0, i)),
        out_shape=jax.ShapeDtypeStruct((dim, 3 * columns), BF16),
        compiler_params=pltpu.CompilerParams(vmem_limit_bytes=VMEM_LIMIT),
        cost_estimate=pl.CostEstimate(
            flops=12 * count * dim * columns,
            bytes_accessed=6 * dim * columns + 12 * count * columns,
            transcendentals=0,
        ),
        name="feed_forward_gradients",
    )(*turned, *kept)


def pack_kernel(block_ref, gate_ref, up_ref, down_ref, *refs):
    out_refs, scratch = refs[:4], refs[4]
    shard, ff = gate_ref.shape
    quarter = scratch.shape[2] // 4
    for place, ref in enumerate((gate_ref, up_ref, down_ref)):
        scratch[place, :, :ff] = ref[...].astype(F32)
        scratch[place, :, ff:] = jnp.zeros((shard, 4 * quarter - ff), F32)
    for place, out_ref in enumerate(out_refs):
        begin = pl.multiple_of((block_ref[0] ^ place) * quarter, LANES)
        for part in range(3):
            out_ref[:, part * quarter : (part + 1) * quarter] = scratch[part, :, pl.ds(begin, quarter)].astype(BF16)


def pack(block, gate, up, down_t, quarter):
    shard = gate.shape[0]
    return pl.pallas_call(
        pack_kernel,
        in_specs=[pl.BlockSpec(memory_space=pltpu.SMEM)] + [pl.BlockSpec(memory_space=pltpu.VMEM)] * 3,
        out_specs=[pl.BlockSpec(memory_space=pltpu.VMEM)] * 4,
        out_shape=[jax.ShapeDtypeStruct((shard, 3 * quarter), BF16)] * 4,
        scratch_shapes=[pltpu.VMEM((3, shard, 4 * quarter), F32)],
        compiler_params=pltpu.CompilerParams(vmem_limit_bytes=VMEM_LIMIT),
        name="pack_columns",
    )(block, gate, up, down_t)


def pick(options, index):
    value = options[0]
    for place in range(1, len(options)):
        value = jnp.where(index == place, options[place], value)
    return value


def assemble_kernel(block_ref, *refs):
    pieces, out_ref, scratch = refs[:4], refs[4], refs[5]
    shard = pieces[0].shape[0]
    values = [ref[...].astype(F32) for ref in pieces]
    for owner in range(4):
        scratch[owner * shard : (owner + 1) * shard] = pick(values, block_ref[0] ^ owner)
    out_ref[...] = scratch[...].astype(BF16)


def assemble(block, pieces):
    shard, columns = pieces[0].shape
    return pl.pallas_call(
        assemble_kernel,
        in_specs=[pl.BlockSpec(memory_space=pltpu.SMEM)] + [pl.BlockSpec(memory_space=pltpu.VMEM)] * 4,
        out_specs=pl.BlockSpec(memory_space=pltpu.VMEM),
        out_shape=jax.ShapeDtypeStruct((4 * shard, columns), BF16),
        scratch_shapes=[pltpu.VMEM((4 * shard, columns), F32)],
        compiler_params=pltpu.CompilerParams(vmem_limit_bytes=VMEM_LIMIT),
        name="assemble_rows",
    )(block, *pieces)


def cut_kernel(block_ref, value_ref, *refs):
    out_refs, scratch = refs[:4], refs[4]
    shard = out_refs[0].shape[0]
    scratch[...] = value_ref[...].astype(F32)
    values = [scratch[owner * shard : (owner + 1) * shard] for owner in range(4)]
    for place, out_ref in enumerate(out_refs):
        out_ref[...] = pick(values, block_ref[0] ^ place).astype(BF16)


def cut(block, value):
    shard, columns = value.shape[0] // 4, value.shape[1]
    return pl.pallas_call(
        cut_kernel,
        in_specs=[pl.BlockSpec(memory_space=pltpu.SMEM), pl.BlockSpec(memory_space=pltpu.VMEM)],
        out_specs=[pl.BlockSpec(memory_space=pltpu.VMEM)] * 4,
        out_shape=[jax.ShapeDtypeStruct((shard, columns), BF16)] * 4,
        scratch_shapes=[pltpu.VMEM(value.shape, F32)],
        compiler_params=pltpu.CompilerParams(vmem_limit_bytes=VMEM_LIMIT),
        name="cut_rows",
    )(block, value)


def unpack_kernel(block_ref, *refs):
    pieces, out_refs, scratch = refs[:4], refs[4:7], refs[7]
    ff = out_refs[0].shape[1]
    quarter = scratch.shape[2] // 4
    for place, ref in enumerate(pieces):
        begin = pl.multiple_of((block_ref[0] ^ place) * quarter, LANES)
        for part in range(3):
            scratch[part, :, pl.ds(begin, quarter)] = ref[:, part * quarter : (part + 1) * quarter].astype(F32)
    for part, out_ref in enumerate(out_refs):
        out_ref[...] = scratch[part, :, :ff]


def unpack(block, pieces, ff):
    shard, columns = pieces[0].shape
    return pl.pallas_call(
        unpack_kernel,
        in_specs=[pl.BlockSpec(memory_space=pltpu.SMEM)] + [pl.BlockSpec(memory_space=pltpu.VMEM)] * 4,
        out_specs=[pl.BlockSpec(memory_space=pltpu.VMEM)] * 3,
        out_shape=[jax.ShapeDtypeStruct((shard, ff), F32)] * 3,
        scratch_shapes=[pltpu.VMEM((3, shard, columns // 3 * 4), F32)],
        compiler_params=pltpu.CompilerParams(vmem_limit_bytes=VMEM_LIMIT),
        name="unpack_columns",
    )(block, *pieces)


def bit_swap(value, axis, bit=0):
    size = lax.axis_size(axis)
    return lax.ppermute(value, axis, [(i, i ^ (1 << bit)) for i in range(size)])


def jump_swap(value, axes, jump):
    return lax.ppermute(value, axes, [(i, i ^ jump) for i in range(4)])


def to_plane(value, slot):
    high, low = slot >> 1, slot & 1
    pairs = [
        (4 * y + 2 * x + c, 4 * (c ^ low) + 2 * (x ^ high) + y) for y in range(2) for x in range(2) for c in range(2)
    ]
    return lax.ppermute(value, TOKENS + ("cc",), pairs)


def from_plane(value, slot):
    high, low = slot >> 1, slot & 1
    pairs = [
        (4 * y + 2 * x + c, 4 * c + 2 * (x ^ high) + (y ^ low)) for y in range(2) for x in range(2) for c in range(2)
    ]
    return lax.ppermute(value, TOKENS + ("cc",), pairs)


def after(first, *values):
    return lax.optimization_barrier((first, *values))


def gather_four(value, axes):
    from_first = bit_swap(value, axes[0])
    return [value, bit_swap(value, axes[1]), from_first, bit_swap(from_first, axes[1])]


def gather_direct(value, axes):
    return [value] + [jump_swap(value, axes, jump) for jump in range(1, 4)]


def sum_direct(axes, own, *away):
    return [own] + [jump_swap(value, axes, jump + 1) for jump, value in enumerate(away)]


def doubling_offsets(steps):
    weight = {"cc": 1, "cx": 2, "fy": 4, "fz": 8}
    offsets = [0]
    for axis, bit in steps:
        offsets += [offset ^ (weight[axis] << bit) for offset in offsets]
    return jnp.array(offsets, jnp.int32)


def double(value, axis, bit=0):
    return jnp.concatenate([value, bit_swap(value, axis, bit)], axis=0)


def plane_gather(value):
    return jnp.concatenate(gather_direct(value, TOKENS), axis=0)


def plane_sum(value):
    parts = jnp.split(value, 4, axis=0)
    terms = sum_direct(TOKENS, *parts)
    return sum(term.astype(F32) for term in terms).astype(BF16)


def halve(value, axis, bit=0):
    middle = value.shape[0] // 2
    came = bit_swap(value[middle:], axis, bit)
    return (value[:middle].astype(F32) + came.astype(F32)).astype(BF16)


def on_device(
    hidden,
    segments,
    attn_gain,
    qkv_weight,
    qkv_bias,
    out_weight,
    mlp_gain,
    gate_weight,
    up_weight,
    down_weight,
    cotangent,
):
    seqs, rows, dim = hidden.shape
    count = seqs * rows
    shard = attn_gain.shape[0]
    world = dim // shard
    joint = qkv_weight.shape[1]
    width = joint - 2 * LANES
    ff = gate_weight.shape[1]
    block = lax.axis_index("cx") * lax.axis_size("cc") + lax.axis_index("cc")
    me = lax.axis_index(FSDP) * lax.axis_size(CTX) + block
    offset = block * rows
    block_arg = block.reshape(1).astype(jnp.int32)
    plane_arg = (lax.axis_index("cx") * 2 + lax.axis_index("fy")).reshape(1).astype(jnp.int32)
    x = hidden.reshape(count, dim)
    cot = cotangent.reshape(count, dim)

    cot_x, cot_y = bit_swap(cot, "cx"), bit_swap(cot, "fy")

    far = [("fz", bit) for bit in reversed(range((lax.axis_size("fz")).bit_length() - 1))]
    padded = -(-(shard + 1) // 16) * 16
    small = jnp.concatenate([attn_gain, mlp_gain, qkv_bias])
    small_row = jnp.pad(small, (0, joint + width - small.shape[0]))[None]
    first = jnp.concatenate(
        [
            jnp.concatenate([qkv_weight, out_weight.T], axis=1),
            small_row,
            jnp.zeros((padded - shard - 1, joint + width), BF16),
        ],
        axis=0,
    )
    first = double(first, *far[0])

    quarter = -(-ff // (4 * TILE)) * TILE
    first, *pieces = after(first, *pack(block_arg, gate_weight, up_weight, down_weight.T, quarter))
    pieces = [to_plane(piece, slot) for slot, piece in enumerate(pieces)]
    for axis, bit in far[1:]:
        first = double(first, axis, bit)

    within = jnp.arange(padded, dtype=jnp.int32)
    owner = me ^ doubling_offsets(far + [("cx", 0), ("fy", 0), ("cc", 0)])
    target = jnp.where(within[None, :] < shard, owner[:, None] * shard + within[None, :], -1).reshape(1, -1)
    order = (jnp.arange(dim, dtype=jnp.int32)[:, None] == target).astype(BF16)
    place = jnp.where(within[None, :] == shard, owner[:, None], -1).reshape(1, -1)
    spread = (jnp.arange(world, dtype=jnp.int32)[:, None] == place).astype(BF16)

    at_row = lax.dynamic_slice_in_dim(segments, offset, rows, axis=1)
    zeros_before = jnp.sum((segments < 1).astype(jnp.int32), axis=1, keepdims=True)
    ones_before = jnp.sum((segments < 2).astype(jnp.int32), axis=1, keepdims=True)
    start = jnp.where(at_row == 0, 0, jnp.where(at_row == 1, zeros_before, ones_before))
    position = (offset + jnp.arange(rows, dtype=jnp.int32)[None, :] - start).reshape(count)
    lane = jnp.arange(LANES, dtype=jnp.int32)
    frequency = ROPE_BASE ** (-(lane % (HD // 2)).astype(F32) * 2.0 / HD)
    angle = position.astype(F32)[:, None] * frequency[None, :]
    cosine = jnp.cos(angle)
    sine = jnp.where(lane % HD < HD // 2, -1.0, 1.0)[None, :] * jnp.sin(angle)
    start_column = jnp.broadcast_to(start.reshape(count, 1), (count, LANES))
    start_row = jnp.broadcast_to(start[:, None, :], (seqs, 8, rows))

    first, cot_x, cot_y, order, spread, cosine, sine, start_column, *pieces = after(
        first, cot_x, cot_y, order, spread, cosine, sine, start_column, *pieces
    )
    w_joint = plane_gather(first[:, :joint])
    mlp_shard = assemble(plane_arg, pieces)
    mlp_weights = lax.all_gather(mlp_shard, WEIGHTS, axis=0, tiled=True)
    w_joint, far_0, far_1 = after(w_joint, cot_x[:rows], cot_y[rows:])
    w_joint = (w_joint, bit_swap(w_joint, "cc"))
    cot_far = [bit_swap(far_0, "fy"), bit_swap(far_1, "cx")]

    normed, q, kv, gain_attn, gain_mlp = prep(x, order, spread, w_joint, cosine, sine, rows)
    kv_all = gather_four(kv.reshape(seqs, rows, 2 * LANES), CTX)
    kv_all[3], out_rows, *cot_far = after(kv_all[3], first[:, joint:], *cot_far)
    w_out = plane_gather(out_rows)
    attended, levels, resid, normed_all = [], [], [], []
    for seq in range(seqs):
        turn = block_arg if seq == 0 else after(attended[0], block_arg)[1]
        attended_one, level_one = attend(turn, q, kv_all, start_column, rows, seq)
        if seq == 0:
            attended_one, w_out = after(attended_one, w_out)
            w_out = (w_out, bit_swap(w_out, "cc"))
        attended.append(attended_one)
        levels.append(level_one)
        resid_one, normed_one = project_out(attended[seq], x, w_out, order, gain_mlp, rows, seq)
        resid.append(resid_one)
        normed_all.append(gather_direct(normed_one, TOKENS))

    out_parts, d_terms, kept, turned = [], [], [], []
    for seq in range(seqs):
        if seq == 1:
            out_parts[0], normed_all[1] = lax.optimization_barrier((out_parts[0], normed_all[1]))
        result = mlp(normed_all[seq], [cot, cot_x, cot_y, cot_far[seq]], mlp_weights, seq)
        out_parts.append(result[:4])
        d_terms.append(sum_direct(TOKENS, *result[4:8]))
        kept.append(result[8])
        turned.append(result[9])
    d_resid, d_branch, d_attended, mlp_gain_grad, dq, dkv_terms, out_terms = [], [], [], [], [], [], []
    for seq in range(seqs):
        if seq == 0:
            _, *d_terms[0] = after(kept[1], *d_terms[0])
        else:
            dq[0], d_terms[1][0], *out_terms[0] = after(dq[0], d_terms[1][0], *out_terms[0])
        result = project_out_back(d_terms[seq], resid[seq], cot, w_out, order, gain_mlp, rows, seq)
        for place, value in zip((d_resid, d_branch, d_attended, mlp_gain_grad), result):
            place.append(value)
        out_terms.append(sum_direct(TOKENS, *after(d_terms[seq][1], *out_parts[seq])[1:]))
        if seq == 0:
            _, turned[1] = after(d_resid[0], turned[1])
            grads = mlp_grad(turned, kept)
            grads, d_attended[0], *d_terms[1] = after(grads, d_attended[0], *d_terms[1])
            grads = lax.psum_scatter(
                grads.reshape(world // 4, 4 * shard, 3 * quarter), WEIGHTS, scatter_dimension=0, tiled=False
            )
        else:
            out_grad = dot_tn(jnp.concatenate(d_branch, axis=0), jnp.concatenate(attended, axis=0)).astype(BF16)
            out_grad = halve(out_grad, "cc")
            d_attended[1], *dkv_terms[0] = after(d_attended[1], *dkv_terms[0])
        result = attend_back(
            block_arg, q, kv_all, d_attended[seq], attended[seq], levels[seq], start_row, cosine, sine, rows, seq
        )
        dq.append(result[0])
        dkv_terms.append(sum_direct(CTX, *result[1:]))
    dq[1], out_grad, *out_terms[1] = after(dq[1], out_grad, *out_terms[1])
    q_grad = dot_tn(normed, jnp.concatenate(dq, axis=0)).astype(BF16)
    q_grad = halve(q_grad, "cc")
    q_grad, *dkv_terms[1] = after(q_grad, *dkv_terms[1])
    q_grad = plane_sum(q_grad)
    d_resid = jnp.concatenate(d_resid, axis=0)
    d_kv, input_grad, attn_gain_grad, bias_grad = input_back(
        dq, dkv_terms, x, d_resid, w_joint, order, gain_attn, cosine, sine
    )
    d_kv, q_grad = after(d_kv, q_grad)

    output = []
    for seq in range(seqs):
        own, *away = out_terms[seq]
        output.append((resid[seq] + own + sum(term.astype(F32) for term in away)).astype(BF16))

    split_at = width + LANES
    bias_grad = bias_grad[0]
    small_grads = jnp.concatenate(
        [
            attn_gain_grad.reshape(world, -1),
            sum(mlp_gain_grad).reshape(world, -1),
            bias_grad[:split_at].reshape(world, -1),
            bias_grad[split_at:].reshape(world, -1),
        ],
        axis=1,
    ).astype(BF16)
    small_count = small_grads.shape[1]
    small_grads = jnp.pad(small_grads, ((0, 0), (0, 2 * LANES - small_count)))
    kv_grad = dot_tn(
        jnp.concatenate([normed, spread], axis=0), jnp.concatenate([d_kv, small_grads], axis=0)
    ).astype(BF16)
    pieces = cut(plane_arg, lax.optimization_barrier(grads))
    kv_grad, *pieces = after(halve(kv_grad, "cc"), *pieces)
    pieces = [from_plane(piece, slot) for slot, piece in enumerate(pieces)]
    kv_grad, out_grad = plane_sum(kv_grad), plane_sum(out_grad)
    first_sum = jnp.concatenate([q_grad, kv_grad, out_grad], axis=1)
    for axis, bit in reversed(far):
        first_sum = halve(first_sum, axis, bit)
    gate_grad, up_grad, down_grad_t = unpack(block_arg, pieces, ff)
    first_sum = first_sum.astype(F32)
    qkv_sum, out_sum = first_sum[:, :joint], first_sum[:, joint:]
    small_sum = qkv_sum[shard, width : width + small_count]
    at = (shard, 2 * shard, 2 * shard + split_at // world)

    return (
        jnp.stack(output),
        input_grad.reshape(hidden.shape),
        small_sum[: at[0]],
        qkv_sum[:shard],
        small_sum[at[1] : at[2]],
        small_sum[at[2] :],
        out_sum[:shard].T,
        small_sum[at[0] : at[1]],
        gate_grad,
        up_grad,
        down_grad_t.T,
    )


def solution(mesh):
    fsdp, ctx = mesh.shape["fsdp"], mesh.shape["ctx"]
    inner = Mesh(mesh.devices.reshape(fsdp // 2, 2, 2, ctx // 2), AXES)
    tokens = P(FSDP, CTX, None)
    vector = P(AXES)
    by_row = P(AXES, None)
    by_column = P(None, AXES)
    return jax.shard_map(
        on_device,
        mesh=inner,
        in_specs=(
            tokens,
            P(FSDP, None),
            vector,
            by_row,
            vector,
            by_column,
            vector,
            by_row,
            by_row,
            by_column,
            tokens,
        ),
        out_specs=(
            tokens,
            tokens,
            vector,
            by_row,
            vector,
            vector,
            by_column,
            vector,
            by_row,
            by_row,
            by_column,
        ),
        check_vma=False,
    )
```

```python
import functools

import jax
import jax.numpy as jnp
from jax import lax
from jax.experimental import pallas as pl
from jax.experimental.pallas import tpu as pltpu
from jax.sharding import Mesh
from jax.sharding import PartitionSpec as P

HD = 64
LANES = 128
EPSILON = 1e-06
ROPE_BASE = 1000000.0
MASKED = -1e30
SCALE = HD ** (-0.5)
TILE = 256
MIB = 1 << 20
VMEM_LIMIT = 64 * MIB
F32 = jnp.float32
BF16 = jnp.bfloat16
AXES = ("fz", "fy", "cx", "cc")
FSDP = ("fz", "fy")
CTX = ("cx", "cc")
TOKENS = ("fy", "cx")
WEIGHTS = ("fz", "cc")


def dot_nn(a, b):
    return lax.dot_general(a, b, (((1,), (0,)), ((), ())), preferred_element_type=F32)


def dot_nt(a, b):
    return lax.dot_general(a, b, (((1,), (1,)), ((), ())), preferred_element_type=F32)


def dot_tn(a, b):
    return lax.dot_general(a, b, (((0,), (0,)), ((), ())), preferred_element_type=F32)


def lane_of(shape):
    return lax.broadcasted_iota(jnp.int32, shape, len(shape) - 1)


def swap_halves(block):
    lead = lane_of(block.shape) % HD < HD // 2
    return jnp.where(
        lead, pltpu.roll(block, LANES - HD // 2, 1), pltpu.roll(block, HD // 2, 1)
    )


def other_head(block):
    return jnp.concatenate([block[:, HD:], block[:, :HD]], axis=1)


def read_out(extras, first, piece, total):
    owners, columns = extras.shape
    at = lax.broadcasted_iota(jnp.int32, (columns, total), 1) % piece + first
    chosen = (lax.broadcasted_iota(jnp.int32, (columns, total), 0) == at).astype(BF16)
    spread = dot_nn(extras, chosen)
    owner = lax.broadcasted_iota(jnp.int32, (owners, total), 1) // piece
    mine = owner == lax.broadcasted_iota(jnp.int32, (owners, total), 0)
    return jnp.sum(jnp.where(mine, spread, 0.0), axis=0, keepdims=True)


def prep_kernel(
    x_ref, order_ref, spread_ref, w_low_ref, w_high_ref, cos_ref, sin_ref,
    normed_ref, q_ref, kv_ref, gain_ref, gain_mlp_ref, bias_ref,
):
    x = x_ref[...].astype(F32)
    dim = x.shape[1]
    width = q_ref.shape[1]
    joint = w_low_ref.shape[1]
    middle = w_low_ref.shape[0]
    owners = spread_ref.shape[0]

    @pl.when(pl.program_id(0) == 0)
    def _():
        extras = dot_nn(spread_ref[:, :middle], w_low_ref[:, :LANES])
        extras = (extras + dot_nn(spread_ref[:, middle:], w_high_ref[:, :LANES])).astype(BF16)
        shard = dim // owners
        gain_ref[...] = read_out(extras, 0, shard, dim)
        gain_mlp_ref[...] = read_out(extras, shard, shard, dim)
        bias_ref[...] = read_out(extras, 2 * shard, joint // owners, joint)

    gain, bias = gain_ref[...], bias_ref[...]
    inverse = lax.rsqrt(jnp.mean(x * x, axis=-1, keepdims=True) + EPSILON)
    normed = (x * inverse * gain).astype(BF16)
    ordered = dot_nn(normed, order_ref[...]).astype(BF16)
    normed_ref[...] = ordered
    joined = dot_nn(ordered[:, :middle], w_low_ref[...])
    joined = joined + dot_nn(ordered[:, middle:], w_high_ref[...]) + bias
    cosine, sine = cos_ref[...], sin_ref[...]
    for begin in range(0, width + LANES, LANES):
        block = joined[:, begin : begin + LANES]
        turned = block * cosine + swap_halves(block) * sine
        if begin < width:
            q_ref[:, begin : begin + LANES] = (turned * SCALE).astype(BF16)
        else:
            kv_ref[:, :LANES] = turned.astype(BF16)
    kv_ref[:, LANES:] = joined[:, width + LANES :].astype(BF16)


def rows_of(rows, cols):
    return pl.BlockSpec((rows, cols), lambda i: (i, 0))


def whole(value):
    return pl.BlockSpec(value.shape, lambda i: (0,) * value.ndim)


def prep(x, order, spread, weights, cosine, sine, rows):
    count, dim = x.shape
    ordered = order.shape[1]
    joint = weights[0].shape[1]
    width = joint - 2 * LANES
    row = pl.BlockSpec((1, dim), lambda i: (0, 0))
    return pl.pallas_call(
        prep_kernel,
        grid=(count // rows,),
        in_specs=[
            rows_of(rows, dim),
            whole(order),
            whole(spread),
            whole(weights[0]),
            whole(weights[1]),
            rows_of(rows, LANES),
            rows_of(rows, LANES),
        ],
        out_specs=[rows_of(rows, ordered), rows_of(rows, width), rows_of(rows, 2 * LANES), row, row],
        out_shape=[
            jax.ShapeDtypeStruct((count, ordered), BF16),
            jax.ShapeDtypeStruct((count, width), BF16),
            jax.ShapeDtypeStruct((count, 2 * LANES), BF16),
            jax.ShapeDtypeStruct((1, dim), F32),
            jax.ShapeDtypeStruct((1, dim), F32),
        ],
        scratch_shapes=[pltpu.VMEM((1, joint), F32)],
        compiler_params=pltpu.CompilerParams(vmem_limit_bytes=VMEM_LIMIT),
        cost_estimate=pl.CostEstimate(
            flops=2 * count * ordered * (joint + dim), bytes_accessed=12 * MIB, transcendentals=0
        ),
        name="norm_project_rotate",
    )(x, order, spread, weights[0], weights[1], cosine, sine)


def back_in_order(value, order):
    high = value.astype(BF16)
    low = (value - high.astype(F32)).astype(BF16)
    return dot_nt(high, order) + dot_nt(low, order)


def out_kernel(attended_ref, x_ref, w_low_ref, w_high_ref, order_ref, gain_ref, resid_ref, normed_ref):
    attended = attended_ref[...]
    branch = jnp.concatenate([dot_nt(attended, w_low_ref[...]), dot_nt(attended, w_high_ref[...])], axis=1)
    resid = x_ref[...].astype(F32) + back_in_order(branch, order_ref[...])
    inverse = lax.rsqrt(jnp.mean(resid * resid, axis=-1, keepdims=True) + EPSILON)
    resid_ref[...] = resid
    normed_ref[...] = (resid * inverse * gain_ref[...]).astype(BF16)


def project_out(attended, x, weights, order, gain, rows, seq):
    dim = x.shape[1]
    count = rows
    return pl.pallas_call(
        out_kernel,
        grid=(1,),
        in_specs=[
            rows_of(rows, attended.shape[1]),
            pl.BlockSpec((rows, dim), lambda i: (seq, 0)),
            whole(weights[0]),
            whole(weights[1]),
            whole(order),
            whole(gain),
        ],
        out_specs=[rows_of(rows, dim), rows_of(rows, dim)],
        out_shape=[jax.ShapeDtypeStruct((count, dim), F32), jax.ShapeDtypeStruct((count, dim), BF16)],
        compiler_params=pltpu.CompilerParams(vmem_limit_bytes=VMEM_LIMIT),
        cost_estimate=pl.CostEstimate(flops=6 * count * dim * dim, bytes_accessed=8 * MIB, transcendentals=0),
        name="project_out_norm",
    )(attended, x, weights[0], weights[1], order, gain)


def sum_rows(value):
    return jnp.sum(value, axis=0, keepdims=True)


def norm_back(values, inverse, gain, incoming):
    scaled = incoming * gain
    mean_term = jnp.mean(scaled * values, axis=-1, keepdims=True)
    return inverse * scaled - values * inverse**3 * mean_term


def total_of(own_ref, *away_refs):
    total = own_ref[...]
    for ref in away_refs:
        total = total + ref[...].astype(F32)
    return total


def out_back_kernel(
    own_ref, core_ref, x_ref, far_ref, resid_ref, cot_ref, w_low_ref, w_high_ref, order_ref, gain_ref,
    d_resid_ref, d_branch_ref, d_attended_ref, gain_grad_ref,
):
    middle = w_low_ref.shape[0]
    d_normed = total_of(own_ref, core_ref, x_ref, far_ref)
    resid = resid_ref[...]
    inverse = lax.rsqrt(jnp.mean(resid * resid, axis=-1, keepdims=True) + EPSILON)
    d_resid = cot_ref[...].astype(F32) + norm_back(resid, inverse, gain_ref[...], d_normed)
    d_resid_ref[...] = d_resid
    d_branch = dot_nn(d_resid.astype(BF16), order_ref[...]).astype(BF16)
    d_branch_ref[...] = d_branch
    d_attended = dot_nn(d_branch[:, :middle], w_low_ref[...])
    d_attended = d_attended + dot_nn(d_branch[:, middle:], w_high_ref[...])
    d_attended_ref[...] = d_attended.astype(BF16)
    gain_grad_ref[...] = sum_rows(d_normed * resid * inverse)


def project_out_back(terms, resid, cot, weights, order, gain, rows, seq):
    count, dim = resid.shape
    ordered = order.shape[1]
    width = dim
    return pl.pallas_call(
        out_back_kernel,
        grid=(1,),
        in_specs=[
            rows_of(rows, dim),
            rows_of(rows, dim),
            rows_of(rows, dim),
            rows_of(rows, dim),
            rows_of(rows, dim),
            pl.BlockSpec((rows, dim), lambda i: (seq, 0)),
            whole(weights[0]),
            whole(weights[1]),
            whole(order),
            whole(gain),
        ],
        out_specs=[
            rows_of(rows, dim),
            rows_of(rows, ordered),
            rows_of(rows, width),
            pl.BlockSpec((1, dim), lambda i: (0, 0)),
        ],
        out_shape=[
            jax.ShapeDtypeStruct((count, dim), F32),
            jax.ShapeDtypeStruct((count, ordered), BF16),
            jax.ShapeDtypeStruct((count, width), BF16),
            jax.ShapeDtypeStruct((1, dim), F32),
        ],
        compiler_params=pltpu.CompilerParams(vmem_limit_bytes=VMEM_LIMIT),
        cost_estimate=pl.CostEstimate(flops=4 * count * dim * dim, bytes_accessed=12 * MIB, transcendentals=0),
        name="norm_back_project",
    )(*terms, resid, cot, weights[0], weights[1], order, gain)


def call_whole(kernel, operands, out_shape, flops, name):
    return pl.pallas_call(
        kernel,
        in_specs=[pl.BlockSpec(memory_space=pltpu.VMEM)] * len(operands),
        out_specs=[pl.BlockSpec(memory_space=pltpu.VMEM)] * len(out_shape),
        out_shape=out_shape,
        compiler_params=pltpu.CompilerParams(vmem_limit_bytes=VMEM_LIMIT),
        cost_estimate=pl.CostEstimate(flops=flops, bytes_accessed=16 * MIB, transcendentals=0),
        name=name,
    )(*operands)


def input_back_kernel(*refs):
    dqs, terms = refs[:2], refs[2:10]
    x_ref, d_resid_ref, w_low_ref, w_high_ref, order_ref, gain_ref, cos_ref, sin_ref = refs[10:18]
    d_kv_ref, input_grad_ref, gain_grad_ref, bias_grad_ref = refs[18:]
    dkv = jnp.concatenate([total_of(*terms[:4]), total_of(*terms[4:])], axis=0)
    dk = dkv[:, :LANES]
    dk = dk * cos_ref[...] - swap_halves(dk) * sin_ref[...]
    d_kv = jnp.concatenate([dk.astype(BF16), dkv[:, LANES:].astype(BF16)], axis=1)
    d_kv_ref[...] = d_kv
    dq = jnp.concatenate([ref[...] for ref in dqs], axis=0)
    d_joined = jnp.concatenate([dq, d_kv], axis=1)
    d_normed = jnp.concatenate([dot_nt(d_joined, w_low_ref[...]), dot_nt(d_joined, w_high_ref[...])], axis=1)
    d_normed = back_in_order(d_normed, order_ref[...])
    x = x_ref[...].astype(F32)
    inverse = lax.rsqrt(jnp.mean(x * x, axis=-1, keepdims=True) + EPSILON)
    input_grad_ref[...] = (d_resid_ref[...] + norm_back(x, inverse, gain_ref[...], d_normed)).astype(BF16)
    gain_grad_ref[...] = sum_rows(d_normed * x * inverse)
    bias_grad_ref[...] = sum_rows(d_joined.astype(F32))


def input_back(dq, terms, x, d_resid, weights, order, gain, cosine, sine):
    count, dim = x.shape
    joint = dq[0].shape[1] + 2 * LANES
    return call_whole(
        input_back_kernel,
        (*dq, *terms[0], *terms[1], x, d_resid, *weights, order, gain, cosine, sine),
        [
            jax.ShapeDtypeStruct((count, 2 * LANES), BF16),
            jax.ShapeDtypeStruct((count, dim), BF16),
            jax.ShapeDtypeStruct((1, dim), F32),
            jax.ShapeDtypeStruct((1, joint), F32),
        ],
        6 * count * dim * joint,
        "input_gradient",
    )


def seq_rows(seq, rows, cols):
    return pl.BlockSpec((rows, cols), lambda i: (seq, 0))


def piece_of(seq, rows):
    return pl.BlockSpec((1, rows, 2 * LANES), lambda i: (seq, 0, 0))


def keys_and_values(piece_refs):
    joint = jnp.concatenate([ref[0] for ref in piece_refs], axis=0)
    key, value = joint[:, :LANES], joint[:, LANES:]
    return (key, other_head(key)), (value, other_head(value))


def attend_kernel(block_ref, q_ref, kv_0, kv_1, kv_2, kv_3, start_ref, out_ref, level_ref):
    rows, width = q_ref.shape
    length = 4 * rows
    heads = width // HD
    group = heads // 2
    keys, values = keys_and_values((kv_0, kv_1, kv_2, kv_3))
    upper_key = lane_of((length, LANES)) >= HD
    upper = lane_of((rows, LANES)) >= HD
    query_at = block_ref[0] * rows + lax.broadcasted_iota(jnp.int32, (rows, length), 0)
    key_at = jnp.concatenate(
        [
            (block_ref[0] ^ place) * rows + lax.broadcasted_iota(jnp.int32, (rows, rows), 1)
            for place in range(4)
        ],
        axis=1,
    )
    allowed = (key_at <= query_at) & (key_at >= start_ref[:, :1])
    bias = jnp.where(allowed, 0.0, MASKED)
    one = jnp.ones((), BF16)
    lane = lane_of((rows, LANES))
    levels = jnp.zeros((rows, LANES), F32)
    for pair in range(heads // 2):
        at = slice(pair * LANES, (pair + 1) * LANES)
        both = q_ref[:, at]
        parts = []
        for place in range(2):
            owner = (2 * pair + place) // group
            moved = int(owner != place)
            side = upper if place else ~upper
            side_key = upper_key if place else ~upper_key
            query = jnp.where(side, both, jnp.zeros_like(both))
            score = dot_nt(query, keys[moved]) + bias
            top = jnp.max(score, axis=1, keepdims=True)
            weight = jnp.exp(score - top).astype(BF16)
            mixed = dot_nn(weight, jnp.where(side_key, values[moved], one))
            total = pltpu.roll(mixed, HD, 1)
            parts.append(mixed / total)
            level = top + jnp.log(total[:, place * HD : place * HD + 1])
            levels = jnp.where(lane == 2 * pair + place, level, levels)
        out_ref[:, at] = jnp.where(upper, parts[1], parts[0]).astype(BF16)
    level_ref[...] = levels


def attend(block, q, kv_pieces, start, rows, seq):
    width = q.shape[1]
    heads = width // HD
    return pl.pallas_call(
        attend_kernel,
        grid=(1,),
        in_specs=[
            pl.BlockSpec(memory_space=pltpu.SMEM),
            seq_rows(seq, rows, width),
            *[piece_of(seq, rows)] * 4,
            seq_rows(seq, rows, LANES),
        ],
        out_specs=[seq_rows(0, rows, width), seq_rows(0, rows, LANES)],
        out_shape=[jax.ShapeDtypeStruct((rows, width), BF16), jax.ShapeDtypeStruct((rows, LANES), F32)],
        compiler_params=pltpu.CompilerParams(vmem_limit_bytes=VMEM_LIMIT),
        cost_estimate=pl.CostEstimate(
            flops=32 * rows * rows * LANES * heads,
            bytes_accessed=4 * rows * width,
            transcendentals=4 * rows * rows * heads,
        ),
        name="attention_forward",
    )(block, q, *kv_pieces, start)


def attend_back_kernel(
    block_ref, q_ref, kv_0, kv_1, kv_2, kv_3, back_ref, out_ref, level_ref, start_ref, cos_ref, sin_ref,
    dq_ref, own_ref, core_ref, x_ref, far_ref, dk_sum, dv_sum,
):
    rows, width = q_ref.shape
    heads = width // HD
    group = heads // 2
    keys, values = keys_and_values((kv_0, kv_1, kv_2, kv_3))
    key_t = keys[0].astype(F32).T.astype(BF16)
    keys_t = (key_t, jnp.concatenate([key_t[HD:], key_t[:HD]], axis=0))
    upper = lane_of((rows, LANES)) >= HD
    upper_t = lax.broadcasted_iota(jnp.int32, (LANES, rows), 0) >= HD
    query_at = block_ref[0] * rows + lax.broadcasted_iota(jnp.int32, (rows, rows), 1)
    key_at = lax.broadcasted_iota(jnp.int32, (rows, rows), 0)
    biases = []
    for place in range(4):
        at = (block_ref[0] ^ place) * rows + key_at
        biases.append(jnp.where((at <= query_at) & (at >= start_ref[0, :1, :]), 0.0, MASKED))
    head_of = lax.broadcasted_iota(jnp.int32, (width, LANES), 0) // HD
    by_head = (head_of == lane_of((width, LANES))).astype(BF16)
    product = back_ref[...].astype(F32) * out_ref[...].astype(F32)
    product_high = product.astype(BF16)
    product_low = (product - product_high.astype(F32)).astype(BF16)
    row_sums = (dot_nn(product_high, by_head) + dot_nn(product_low, by_head)).T
    levels = level_ref[...].T
    cosine, sine = cos_ref[...], sin_ref[...]
    dk_sum[...] = jnp.zeros_like(dk_sum)
    dv_sum[...] = jnp.zeros_like(dv_sum)
    for pair in range(heads // 2):
        at = slice(pair * LANES, (pair + 1) * LANES)
        both = q_ref[:, at]
        back_both = back_ref[:, at]
        zero = jnp.zeros_like(both)
        sides = (~upper, upper)
        queries = [jnp.where(side, both, zero) for side in sides]
        backs = [jnp.where(side, back_both, zero) for side in sides]
        owners = [(2 * pair + place) // group for place in range(2)]
        d_query_t = [jnp.zeros((LANES, rows), F32) for _ in range(2)]
        for piece in range(4):
            span = slice(piece * rows, (piece + 1) * rows)
            probs, d_scores = [], []
            for place in range(2):
                head = 2 * pair + place
                moved = int(owners[place] != place)
                score = dot_nt(keys[moved][span], queries[place]) + biases[piece]
                prob = jnp.exp(score - levels[head : head + 1])
                d_prob = dot_nt(values[moved][span], backs[place])
                d_score = (prob * (d_prob - row_sums[head : head + 1])).astype(BF16)
                d_query_t[place] = d_query_t[place] + dot_nn(keys_t[moved][:, span], d_score)
                probs.append(prob.astype(BF16))
                d_scores.append(d_score)
            if owners[0] == owners[1]:
                dv_sum[owners[0], span] += dot_nn(
                    jnp.concatenate(probs, axis=1), jnp.concatenate(backs, axis=0)
                )
                dk_sum[owners[0], span] += dot_nn(
                    jnp.concatenate(d_scores, axis=1), jnp.concatenate(queries, axis=0)
                )
            else:
                for place in range(2):
                    dv_sum[owners[place], span] += dot_nn(probs[place], backs[place])
                    dk_sum[owners[place], span] += dot_nn(d_scores[place], queries[place])
        d_query = jnp.where(upper_t, d_query_t[1], d_query_t[0]).T * SCALE
        dq_ref[:, at] = (d_query * cosine - swap_halves(d_query) * sine).astype(BF16)
    lower_key = lane_of((4 * rows, LANES)) < HD
    for total, begin in ((dk_sum, 0), (dv_sum, LANES)):
        first, second = total[0], total[1]
        first = first + pltpu.roll(first, HD, 1)
        second = second + pltpu.roll(second, HD, 1)
        both = jnp.where(lower_key, first, second)
        cols = slice(begin, begin + LANES)
        own_ref[:, cols] = both[:rows]
        for place, ref in enumerate((core_ref, x_ref, far_ref)):
            ref[:, cols] = both[(place + 1) * rows : (place + 2) * rows].astype(BF16)


def parts_of(rows, cols):
    shapes = [jax.ShapeDtypeStruct((rows, cols), F32)] + [jax.ShapeDtypeStruct((rows, cols), BF16)] * 3
    return [seq_rows(0, rows, cols)] * 4, shapes


def attend_back(block, q, kv_pieces, back, out, level, start, cosine, sine, rows, seq):
    width = q.shape[1]
    length = 4 * rows
    heads = width // HD
    specs, shapes = parts_of(rows, 2 * LANES)
    return pl.pallas_call(
        attend_back_kernel,
        grid=(1,),
        in_specs=[
            pl.BlockSpec(memory_space=pltpu.SMEM),
            seq_rows(seq, rows, width),
            *[piece_of(seq, rows)] * 4,
            seq_rows(0, rows, width),
            seq_rows(0, rows, width),
            seq_rows(0, rows, LANES),
            pl.BlockSpec((1, 8, rows), lambda i: (seq, 0, 0)),
            seq_rows(seq, rows, LANES),
            seq_rows(seq, rows, LANES),
        ],
        out_specs=[seq_rows(0, rows, width), *specs],
        out_shape=[jax.ShapeDtypeStruct((rows, width), BF16), *shapes],
        scratch_shapes=[
            pltpu.VMEM((2, length, LANES), F32),
            pltpu.VMEM((2, length, LANES), F32),
        ],
        compiler_params=pltpu.CompilerParams(vmem_limit_bytes=VMEM_LIMIT),
        cost_estimate=pl.CostEstimate(
            flops=80 * rows * rows * LANES * heads,
            bytes_accessed=8 * rows * width,
            transcendentals=4 * rows * rows * heads,
        ),
        name="attention_backward",
    )(block, q, *kv_pieces, back, out, level, start, cosine, sine)


def mlp_kernel(
    n_0, n_1, n_2, n_3, c_0, c_1, c_2, c_3, w_ref,
    own_ref, out_1, out_2, out_3, d_own_ref, d_1, d_2, d_3, kept_ref, turned_ref,
    normed_all, cot_all,
):
    step = pl.program_id(0)
    rows = own_ref.shape[0]
    columns = w_ref.shape[1] // 3

    @pl.when(step == 0)
    def _():
        for place, (n_ref, c_ref) in enumerate(zip((n_0, n_1, n_2, n_3), (c_0, c_1, c_2, c_3))):
            normed_all[place // 2, (place % 2) * rows : (place % 2 + 1) * rows] = n_ref[...]
            cot_all[place // 2, (place % 2) * rows : (place % 2 + 1) * rows] = c_ref[...]

    normed, cot = normed_all[step], cot_all[step]
    for begin in range(0, columns, TILE):
        at = slice(begin, begin + TILE)
        gate = dot_nn(normed, w_ref[:, begin : begin + TILE])
        up = dot_nn(normed, w_ref[:, columns + begin : columns + begin + TILE])
        d_act = dot_nn(cot, w_ref[:, 2 * columns + begin : 2 * columns + begin + TILE])
        sigmoid = 0.5 * jnp.tanh(0.5 * gate) + 0.5
        swish = gate * sigmoid
        kept_ref[0, :, at] = (d_act * up * (sigmoid + swish * (1.0 - sigmoid))).astype(BF16)
        kept_ref[1, :, at] = (d_act * swish).astype(BF16)
        kept_ref[2, :, at] = (swish * up).astype(BF16)
    turned_ref[0] = normed.T
    turned_ref[1] = cot.T
    out = dot_nt(kept_ref[2], w_ref[:, 2 * columns :])
    d_normed = dot_nt(kept_ref[0], w_ref[:, :columns]) + dot_nt(kept_ref[1], w_ref[:, columns : 2 * columns])

    @pl.when(step == 0)
    def _():
        own_ref[...] = out[:rows]
        out_1[...] = out[rows:].astype(BF16)
        d_own_ref[...] = d_normed[:rows]
        d_1[...] = d_normed[rows:].astype(BF16)

    @pl.when(step == 1)
    def _():
        out_2[...] = out[:rows].astype(BF16)
        out_3[...] = out[rows:].astype(BF16)
        d_2[...] = d_normed[:rows].astype(BF16)
        d_3[...] = d_normed[rows:].astype(BF16)


def mlp(normed, cot, weights, seq):
    rows, dim = normed[0].shape
    columns = weights.shape[1] // 3
    specs, shapes = parts_of(rows, dim)
    once = lambda at: pl.BlockSpec((rows, dim), lambda i: (at, 0), pipeline_mode=pl.Buffered(1))
    return pl.pallas_call(
        mlp_kernel,
        grid=(2,),
        in_specs=[
            *[once(0)] * 4,
            *[once(seq)] * 3,
            once(0),
            pl.BlockSpec(weights.shape, lambda i: (0, 0), pipeline_mode=pl.Buffered(1)),
        ],
        out_specs=[
            *specs,
            *specs,
            pl.BlockSpec((3, 2 * rows, columns), lambda i: (0, i, 0)),
            pl.BlockSpec((2, dim, 2 * rows), lambda i: (0, 0, i)),
        ],
        out_shape=[
            *shapes,
            *shapes,
            jax.ShapeDtypeStruct((3, 4 * rows, columns), BF16),
            jax.ShapeDtypeStruct((2, dim, 4 * rows), BF16),
        ],
        scratch_shapes=[
            pltpu.VMEM((2, 2 * rows, dim), BF16),
            pltpu.VMEM((2, 2 * rows, dim), BF16),
        ],
        compiler_params=pltpu.CompilerParams(vmem_limit_bytes=VMEM_LIMIT),
        cost_estimate=pl.CostEstimate(
            flops=48 * rows * dim * columns,
            bytes_accessed=6 * dim * columns + 24 * rows * columns,
            transcendentals=4 * rows * columns,
        ),
        name="feed_forward",
    )(*normed, *cot, weights)


def mlp_grad_kernel(turned_0, turned_1, kept_0, kept_1, grad_ref):
    grad_ref[...] = (dot_nn(turned_0[0], kept_0[0]) + dot_nn(turned_1[0], kept_1[0])).astype(BF16)


def mlp_grad(turned, kept):
    _, dim, count = turned[0].shape
    columns = kept[0].shape[2]
    turned_block = pl.BlockSpec((1, dim, count), lambda i: (i // 2, 0, 0))
    kept_block = pl.BlockSpec((1, count, columns), lambda i: (i, 0, 0))
    return pl.pallas_call(
        mlp_grad_kernel,
        grid=(3,),
        in_specs=[turned_block, turned_block, kept_block, kept_block],
        out_specs=pl.BlockSpec((dim, columns), lambda i: (0, i)),
        out_shape=jax.ShapeDtypeStruct((dim, 3 * columns), BF16),
        compiler_params=pltpu.CompilerParams(vmem_limit_bytes=VMEM_LIMIT),
        cost_estimate=pl.CostEstimate(
            flops=12 * count * dim * columns,
            bytes_accessed=6 * dim * columns + 12 * count * columns,
            transcendentals=0,
        ),
        name="feed_forward_gradients",
    )(*turned, *kept)


def pack_kernel(block_ref, gate_ref, up_ref, down_ref, *refs):
    out_refs, scratch = refs[:4], refs[4]
    shard, ff = gate_ref.shape
    quarter = scratch.shape[2] // 4
    for place, ref in enumerate((gate_ref, up_ref, down_ref)):
        scratch[place, :, :ff] = ref[...].astype(F32)
        scratch[place, :, ff:] = jnp.zeros((shard, 4 * quarter - ff), F32)
    for place, out_ref in enumerate(out_refs):
        begin = pl.multiple_of((block_ref[0] ^ place) * quarter, LANES)
        for part in range(3):
            out_ref[:, part * quarter : (part + 1) * quarter] = scratch[part, :, pl.ds(begin, quarter)].astype(BF16)


def pack(block, gate, up, down_t, quarter):
    shard = gate.shape[0]
    return pl.pallas_call(
        pack_kernel,
        in_specs=[pl.BlockSpec(memory_space=pltpu.SMEM)] + [pl.BlockSpec(memory_space=pltpu.VMEM)] * 3,
        out_specs=[pl.BlockSpec(memory_space=pltpu.VMEM)] * 4,
        out_shape=[jax.ShapeDtypeStruct((shard, 3 * quarter), BF16)] * 4,
        scratch_shapes=[pltpu.VMEM((3, shard, 4 * quarter), F32)],
        compiler_params=pltpu.CompilerParams(vmem_limit_bytes=VMEM_LIMIT),
        name="pack_columns",
    )(block, gate, up, down_t)


def pick(options, index):
    value = options[0]
    for place in range(1, len(options)):
        value = jnp.where(index == place, options[place], value)
    return value


def assemble_kernel(block_ref, *refs):
    pieces, out_ref, scratch = refs[:4], refs[4], refs[5]
    shard = pieces[0].shape[0]
    values = [ref[...].astype(F32) for ref in pieces]
    for owner in range(4):
        scratch[owner * shard : (owner + 1) * shard] = pick(values, block_ref[0] ^ owner)
    out_ref[...] = scratch[...].astype(BF16)


def assemble(block, pieces):
    shard, columns = pieces[0].shape
    return pl.pallas_call(
        assemble_kernel,
        in_specs=[pl.BlockSpec(memory_space=pltpu.SMEM)] + [pl.BlockSpec(memory_space=pltpu.VMEM)] * 4,
        out_specs=pl.BlockSpec(memory_space=pltpu.VMEM),
        out_shape=jax.ShapeDtypeStruct((4 * shard, columns), BF16),
        scratch_shapes=[pltpu.VMEM((4 * shard, columns), F32)],
        compiler_params=pltpu.CompilerParams(vmem_limit_bytes=VMEM_LIMIT),
        name="assemble_rows",
    )(block, *pieces)


def cut_kernel(block_ref, value_ref, *refs):
    out_refs, scratch = refs[:4], refs[4]
    shard = out_refs[0].shape[0]
    scratch[...] = value_ref[...].astype(F32)
    values = [scratch[owner * shard : (owner + 1) * shard] for owner in range(4)]
    for place, out_ref in enumerate(out_refs):
        out_ref[...] = pick(values, block_ref[0] ^ place).astype(BF16)


def cut(block, value):
    shard, columns = value.shape[0] // 4, value.shape[1]
    return pl.pallas_call(
        cut_kernel,
        in_specs=[pl.BlockSpec(memory_space=pltpu.SMEM), pl.BlockSpec(memory_space=pltpu.VMEM)],
        out_specs=[pl.BlockSpec(memory_space=pltpu.VMEM)] * 4,
        out_shape=[jax.ShapeDtypeStruct((shard, columns), BF16)] * 4,
        scratch_shapes=[pltpu.VMEM(value.shape, F32)],
        compiler_params=pltpu.CompilerParams(vmem_limit_bytes=VMEM_LIMIT),
        name="cut_rows",
    )(block, value)


def unpack_kernel(block_ref, *refs):
    pieces, out_refs, scratch = refs[:4], refs[4:7], refs[7]
    ff = out_refs[0].shape[1]
    quarter = scratch.shape[2] // 4
    for place, ref in enumerate(pieces):
        begin = pl.multiple_of((block_ref[0] ^ place) * quarter, LANES)
        for part in range(3):
            scratch[part, :, pl.ds(begin, quarter)] = ref[:, part * quarter : (part + 1) * quarter].astype(F32)
    for part, out_ref in enumerate(out_refs):
        out_ref[...] = scratch[part, :, :ff]


def unpack(block, pieces, ff):
    shard, columns = pieces[0].shape
    return pl.pallas_call(
        unpack_kernel,
        in_specs=[pl.BlockSpec(memory_space=pltpu.SMEM)] + [pl.BlockSpec(memory_space=pltpu.VMEM)] * 4,
        out_specs=[pl.BlockSpec(memory_space=pltpu.VMEM)] * 3,
        out_shape=[jax.ShapeDtypeStruct((shard, ff), F32)] * 3,
        scratch_shapes=[pltpu.VMEM((3, shard, columns // 3 * 4), F32)],
        compiler_params=pltpu.CompilerParams(vmem_limit_bytes=VMEM_LIMIT),
        name="unpack_columns",
    )(block, *pieces)


def bit_swap(value, axis, bit=0):
    size = lax.axis_size(axis)
    return lax.ppermute(value, axis, [(i, i ^ (1 << bit)) for i in range(size)])


def jump_swap(value, axes, jump):
    return lax.ppermute(value, axes, [(i, i ^ jump) for i in range(4)])


def to_plane(value, slot):
    high, low = slot >> 1, slot & 1
    pairs = [
        (4 * y + 2 * x + c, 4 * (c ^ low) + 2 * (x ^ high) + y) for y in range(2) for x in range(2) for c in range(2)
    ]
    return lax.ppermute(value, TOKENS + ("cc",), pairs)


def from_plane(value, slot):
    high, low = slot >> 1, slot & 1
    pairs = [
        (4 * y + 2 * x + c, 4 * c + 2 * (x ^ high) + (y ^ low)) for y in range(2) for x in range(2) for c in range(2)
    ]
    return lax.ppermute(value, TOKENS + ("cc",), pairs)


def after(first, *values):
    return lax.optimization_barrier((first, *values))


def gather_four(value, axes):
    from_first = bit_swap(value, axes[0])
    return [value, bit_swap(value, axes[1]), from_first, bit_swap(from_first, axes[1])]


def gather_direct(value, axes):
    return [value] + [jump_swap(value, axes, jump) for jump in range(1, 4)]


def sum_direct(axes, own, *away):
    return [own] + [jump_swap(value, axes, jump + 1) for jump, value in enumerate(away)]


def doubling_offsets(steps):
    weight = {"cc": 1, "cx": 2, "fy": 4, "fz": 8}
    offsets = [0]
    for axis, bit in steps:
        offsets += [offset ^ (weight[axis] << bit) for offset in offsets]
    return jnp.array(offsets, jnp.int32)


def double(value, axis, bit=0):
    return jnp.concatenate([value, bit_swap(value, axis, bit)], axis=0)


def plane_gather(value):
    return jnp.concatenate(gather_direct(value, TOKENS), axis=0)


def plane_sum(value):
    parts = jnp.split(value, 4, axis=0)
    terms = sum_direct(TOKENS, *parts)
    return sum(term.astype(F32) for term in terms).astype(BF16)


def halve(value, axis, bit=0):
    middle = value.shape[0] // 2
    came = bit_swap(value[middle:], axis, bit)
    return (value[:middle].astype(F32) + came.astype(F32)).astype(BF16)


def on_device(
    hidden,
    segments,
    attn_gain,
    qkv_weight,
    qkv_bias,
    out_weight,
    mlp_gain,
    gate_weight,
    up_weight,
    down_weight,
    cotangent,
):
    seqs, rows, dim = hidden.shape
    count = seqs * rows
    shard = attn_gain.shape[0]
    world = dim // shard
    joint = qkv_weight.shape[1]
    width = joint - 2 * LANES
    ff = gate_weight.shape[1]
    block = lax.axis_index("cx") * lax.axis_size("cc") + lax.axis_index("cc")
    me = lax.axis_index(FSDP) * lax.axis_size(CTX) + block
    offset = block * rows
    block_arg = block.reshape(1).astype(jnp.int32)
    plane_arg = (lax.axis_index("cx") * 2 + lax.axis_index("fy")).reshape(1).astype(jnp.int32)
    x = hidden.reshape(count, dim)
    cot = cotangent.reshape(count, dim)

    far = [("fz", bit) for bit in reversed(range((lax.axis_size("fz")).bit_length() - 1))]
    padded = -(-(shard + 1) // 16) * 16
    small = jnp.concatenate([attn_gain, mlp_gain, qkv_bias])
    small_row = jnp.pad(small, (0, joint + width - small.shape[0]))[None]
    first = jnp.concatenate(
        [
            jnp.concatenate([qkv_weight, out_weight.T], axis=1),
            small_row,
            jnp.zeros((padded - shard - 1, joint + width), BF16),
        ],
        axis=0,
    )
    first = double(first, *far[0])

    quarter = -(-ff // (4 * TILE)) * TILE
    first, *pieces = after(first, *pack(block_arg, gate_weight, up_weight, down_weight.T, quarter))
    pieces = [to_plane(piece, slot) for slot, piece in enumerate(pieces)]
    for axis, bit in far[1:]:
        first = double(first, axis, bit)

    within = jnp.arange(padded, dtype=jnp.int32)
    owner = me ^ doubling_offsets(far + [("cx", 0), ("fy", 0), ("cc", 0)])
    target = jnp.where(within[None, :] < shard, owner[:, None] * shard + within[None, :], -1).reshape(1, -1)
    order = (jnp.arange(dim, dtype=jnp.int32)[:, None] == target).astype(BF16)
    place = jnp.where(within[None, :] == shard, owner[:, None], -1).reshape(1, -1)
    spread = (jnp.arange(world, dtype=jnp.int32)[:, None] == place).astype(BF16)

    at_row = lax.dynamic_slice_in_dim(segments, offset, rows, axis=1)
    zeros_before = jnp.sum((segments < 1).astype(jnp.int32), axis=1, keepdims=True)
    ones_before = jnp.sum((segments < 2).astype(jnp.int32), axis=1, keepdims=True)
    start = jnp.where(at_row == 0, 0, jnp.where(at_row == 1, zeros_before, ones_before))
    position = (offset + jnp.arange(rows, dtype=jnp.int32)[None, :] - start).reshape(count)
    lane = jnp.arange(LANES, dtype=jnp.int32)
    frequency = ROPE_BASE ** (-(lane % (HD // 2)).astype(F32) * 2.0 / HD)
    angle = position.astype(F32)[:, None] * frequency[None, :]
    cosine = jnp.cos(angle)
    sine = jnp.where(lane % HD < HD // 2, -1.0, 1.0)[None, :] * jnp.sin(angle)
    start_column = jnp.broadcast_to(start.reshape(count, 1), (count, LANES))
    start_row = jnp.broadcast_to(start[:, None, :], (seqs, 8, rows))

    first, order, spread, cosine, sine, start_column, *pieces = after(
        first, order, spread, cosine, sine, start_column, *pieces
    )
    w_joint = plane_gather(first[:, :joint])
    mlp_shard = assemble(plane_arg, pieces)
    mlp_weights = lax.all_gather(mlp_shard, WEIGHTS, axis=0, tiled=True)
    w_joint, cot_late = after(w_joint, cot)
    w_joint = (w_joint, bit_swap(w_joint, "cc"))

    cot_x, cot_y = bit_swap(cot_late, "cx"), bit_swap(cot_late, "fy")

    normed, q, kv, gain_attn, gain_mlp = prep(x, order, spread, w_joint, cosine, sine, rows)
    kv_all = gather_four(kv.reshape(seqs, rows, 2 * LANES), CTX)
    kv_all[3], out_rows, cot_x, cot_y = after(kv_all[3], first[:, joint:], cot_x, cot_y)
    w_out = plane_gather(out_rows)
    attended, levels, resid, normed_all = [], [], [], []
    for seq in range(seqs):
        turn = block_arg if seq == 0 else after(attended[0], block_arg)[1]
        attended_one, level_one = attend(turn, q, kv_all, start_column, rows, seq)
        if seq == 0:
            attended_one, w_out, far_0, far_1 = after(attended_one, w_out, cot_x[:rows], cot_y[rows:])
            cot_far = [bit_swap(far_0, "fy"), bit_swap(far_1, "cx")]
            w_out = (w_out, bit_swap(w_out, "cc"))
        attended.append(attended_one)
        levels.append(level_one)
        resid_one, normed_one = project_out(attended[seq], x, w_out, order, gain_mlp, rows, seq)
        resid.append(resid_one)
        normed_all.append(gather_direct(normed_one, TOKENS))

    out_parts, d_terms, kept, turned = [], [], [], []
    for seq in range(seqs):
        if seq == 1:
            out_parts[0], normed_all[1] = lax.optimization_barrier((out_parts[0], normed_all[1]))
        result = mlp(normed_all[seq], [cot, cot_x, cot_y, cot_far[seq]], mlp_weights, seq)
        out_parts.append(result[:4])
        d_terms.append(sum_direct(TOKENS, *result[4:8]))
        kept.append(result[8])
        turned.append(result[9])
    d_resid, d_branch, d_attended, mlp_gain_grad, dq, dkv_terms, out_terms = [], [], [], [], [], [], []
    for seq in range(seqs):
        if seq == 0:
            _, *d_terms[0] = after(kept[1], *d_terms[0])
        else:
            dq[0], d_terms[1][0], *out_terms[0] = after(dq[0], d_terms[1][0], *out_terms[0])
        result = project_out_back(d_terms[seq], resid[seq], cot, w_out, order, gain_mlp, rows, seq)
        for place, value in zip((d_resid, d_branch, d_attended, mlp_gain_grad), result):
            place.append(value)
        out_terms.append(sum_direct(TOKENS, *after(d_terms[seq][1], *out_parts[seq])[1:]))
        if seq == 0:
            _, turned[1] = after(d_resid[0], turned[1])
            grads = mlp_grad(turned, kept)
            grads, d_attended[0], *d_terms[1] = after(grads, d_attended[0], *d_terms[1])
            grads = lax.psum_scatter(
                grads.reshape(world // 4, 4 * shard, 3 * quarter), WEIGHTS, scatter_dimension=0, tiled=False
            )
        else:
            out_grad = dot_tn(jnp.concatenate(d_branch, axis=0), jnp.concatenate(attended, axis=0)).astype(BF16)
            out_grad = halve(out_grad, "cc")
            d_attended[1], *dkv_terms[0] = after(d_attended[1], *dkv_terms[0])
        result = attend_back(
            block_arg, q, kv_all, d_attended[seq], attended[seq], levels[seq], start_row, cosine, sine, rows, seq
        )
        dq.append(result[0])
        dkv_terms.append(sum_direct(CTX, *result[1:]))
    dq[1], out_grad, *out_terms[1] = after(dq[1], out_grad, *out_terms[1])
    q_grad = dot_tn(normed, jnp.concatenate(dq, axis=0)).astype(BF16)
    q_grad = halve(q_grad, "cc")
    q_grad, *dkv_terms[1] = after(jnp.concatenate([q_grad, out_grad], axis=1), *dkv_terms[1])
    q_grad = plane_sum(q_grad)
    d_resid = jnp.concatenate(d_resid, axis=0)
    d_kv, input_grad, attn_gain_grad, bias_grad = input_back(
        dq, dkv_terms, x, d_resid, w_joint, order, gain_attn, cosine, sine
    )
    d_kv, q_grad = after(d_kv, q_grad)

    output = []
    for seq in range(seqs):
        own, *away = out_terms[seq]
        output.append((resid[seq] + own + sum(term.astype(F32) for term in away)).astype(BF16))

    split_at = width + LANES
    bias_grad = bias_grad[0]
    small_grads = jnp.concatenate(
        [
            attn_gain_grad.reshape(world, -1),
            sum(mlp_gain_grad).reshape(world, -1),
            bias_grad[:split_at].reshape(world, -1),
            bias_grad[split_at:].reshape(world, -1),
        ],
        axis=1,
    ).astype(BF16)
    small_count = small_grads.shape[1]
    small_grads = jnp.pad(small_grads, ((0, 0), (0, 2 * LANES - small_count)))
    kv_grad = dot_tn(
        jnp.concatenate([normed, spread], axis=0), jnp.concatenate([d_kv, small_grads], axis=0)
    ).astype(BF16)
    pieces = cut(plane_arg, lax.optimization_barrier(grads))
    kv_grad, *pieces = after(halve(kv_grad, "cc"), *pieces)
    pieces = [from_plane(piece, slot) for slot, piece in enumerate(pieces)]
    first_sum = jnp.concatenate([q_grad, plane_sum(kv_grad)], axis=1)
    for axis, bit in reversed(far):
        first_sum = halve(first_sum, axis, bit)
    gate_grad, up_grad, down_grad_t = unpack(block_arg, pieces, ff)
    first_sum = first_sum.astype(F32)
    kv_at = 2 * width
    qkv_sum = jnp.concatenate([first_sum[:shard, :width], first_sum[:shard, kv_at:]], axis=1)
    out_sum = first_sum[:, width:kv_at]
    small_sum = first_sum[shard, kv_at : kv_at + small_count]
    at = (shard, 2 * shard, 2 * shard + split_at // world)

    return (
        jnp.stack(output),
        input_grad.reshape(hidden.shape),
        small_sum[: at[0]],
        qkv_sum,
        small_sum[at[1] : at[2]],
        small_sum[at[2] :],
        out_sum[:shard].T,
        small_sum[at[0] : at[1]],
        gate_grad,
        up_grad,
        down_grad_t.T,
    )


def solution(mesh):
    fsdp, ctx = mesh.shape["fsdp"], mesh.shape["ctx"]
    inner = Mesh(mesh.devices.reshape(fsdp // 2, 2, 2, ctx // 2), AXES)
    tokens = P(FSDP, CTX, None)
    vector = P(AXES)
    by_row = P(AXES, None)
    by_column = P(None, AXES)
    return jax.shard_map(
        on_device,
        mesh=inner,
        in_specs=(
            tokens,
            P(FSDP, None),
            vector,
            by_row,
            vector,
            by_column,
            vector,
            by_row,
            by_row,
            by_column,
            tokens,
        ),
        out_specs=(
            tokens,
            tokens,
            vector,
            by_row,
            vector,
            vector,
            by_column,
            vector,
            by_row,
            by_row,
            by_column,
        ),
        check_vma=False,
    )
```

```python
import functools

import jax
import jax.numpy as jnp
from jax import lax
from jax.experimental import pallas as pl
from jax.experimental.pallas import tpu as pltpu
from jax.sharding import Mesh
from jax.sharding import PartitionSpec as P

HD = 64
LANES = 128
EPSILON = 1e-06
ROPE_BASE = 1000000.0
MASKED = -1e30
SCALE = HD ** (-0.5)
TILE = 256
MIB = 1 << 20
VMEM_LIMIT = 60 * MIB
F32 = jnp.float32
BF16 = jnp.bfloat16
AXES = ("fz", "fy", "cx", "cc")
FSDP = ("fz", "fy")
CTX = ("cx", "cc")
TOKENS = ("fy", "cx")
WEIGHTS = ("fz", "cc")


def dot_nn(a, b):
    return lax.dot_general(a, b, (((1,), (0,)), ((), ())), preferred_element_type=F32)


def dot_nt(a, b):
    return lax.dot_general(a, b, (((1,), (1,)), ((), ())), preferred_element_type=F32)


def dot_tn(a, b):
    return lax.dot_general(a, b, (((0,), (0,)), ((), ())), preferred_element_type=F32)


def lane_of(shape):
    return lax.broadcasted_iota(jnp.int32, shape, len(shape) - 1)


def swap_halves(block):
    lead = lane_of(block.shape) % HD < HD // 2
    return jnp.where(
        lead, pltpu.roll(block, LANES - HD // 2, 1), pltpu.roll(block, HD // 2, 1)
    )


def other_head(block):
    return jnp.concatenate([block[:, HD:], block[:, :HD]], axis=1)


def read_out(extras, first, piece, total):
    owners, columns = extras.shape
    at = lax.broadcasted_iota(jnp.int32, (columns, total), 1) % piece + first
    chosen = (lax.broadcasted_iota(jnp.int32, (columns, total), 0) == at).astype(BF16)
    spread = dot_nn(extras, chosen)
    owner = lax.broadcasted_iota(jnp.int32, (owners, total), 1) // piece
    mine = owner == lax.broadcasted_iota(jnp.int32, (owners, total), 0)
    return jnp.sum(jnp.where(mine, spread, 0.0), axis=0, keepdims=True)


def prep_kernel(
    x_ref, order_ref, spread_ref, w_low_ref, w_high_ref, cos_ref, sin_ref,
    normed_ref, q_ref, kv_ref, gain_ref, gain_mlp_ref, bias_ref,
):
    x = x_ref[...].astype(F32)
    dim = x.shape[1]
    width = q_ref.shape[1]
    joint = w_low_ref.shape[1]
    middle = w_low_ref.shape[0]
    owners = spread_ref.shape[0]

    @pl.when(pl.program_id(0) == 0)
    def _():
        extras = dot_nn(spread_ref[:, :middle], w_low_ref[:, :LANES])
        extras = (extras + dot_nn(spread_ref[:, middle:], w_high_ref[:, :LANES])).astype(BF16)
        shard = dim // owners
        gain_ref[...] = read_out(extras, 0, shard, dim)
        gain_mlp_ref[...] = read_out(extras, shard, shard, dim)
        bias_ref[...] = read_out(extras, 2 * shard, joint // owners, joint)

    gain, bias = gain_ref[...], bias_ref[...]
    inverse = lax.rsqrt(jnp.mean(x * x, axis=-1, keepdims=True) + EPSILON)
    normed = (x * inverse * gain).astype(BF16)
    ordered = dot_nn(normed, order_ref[...]).astype(BF16)
    normed_ref[...] = ordered
    joined = dot_nn(ordered[:, :middle], w_low_ref[...])
    joined = joined + dot_nn(ordered[:, middle:], w_high_ref[...]) + bias
    cosine, sine = cos_ref[...], sin_ref[...]
    for begin in range(0, width + LANES, LANES):
        block = joined[:, begin : begin + LANES]
        turned = block * cosine + swap_halves(block) * sine
        if begin < width:
            q_ref[:, begin : begin + LANES] = (turned * SCALE).astype(BF16)
        else:
            kv_ref[:, :LANES] = turned.astype(BF16)
    kv_ref[:, LANES:] = joined[:, width + LANES :].astype(BF16)


def rows_of(rows, cols):
    return pl.BlockSpec((rows, cols), lambda i: (i, 0))


def whole(value):
    return pl.BlockSpec(value.shape, lambda i: (0,) * value.ndim)


def prep(x, order, spread, weights, cosine, sine, rows):
    count, dim = x.shape
    ordered = order.shape[1]
    joint = weights[0].shape[1]
    width = joint - 2 * LANES
    row = pl.BlockSpec((1, dim), lambda i: (0, 0))
    return pl.pallas_call(
        prep_kernel,
        grid=(count // rows,),
        in_specs=[
            rows_of(rows, dim),
            whole(order),
            whole(spread),
            whole(weights[0]),
            whole(weights[1]),
            rows_of(rows, LANES),
            rows_of(rows, LANES),
        ],
        out_specs=[rows_of(rows, ordered), rows_of(rows, width), rows_of(rows, 2 * LANES), row, row],
        out_shape=[
            jax.ShapeDtypeStruct((count, ordered), BF16),
            jax.ShapeDtypeStruct((count, width), BF16),
            jax.ShapeDtypeStruct((count, 2 * LANES), BF16),
            jax.ShapeDtypeStruct((1, dim), F32),
            jax.ShapeDtypeStruct((1, dim), F32),
        ],
        scratch_shapes=[pltpu.VMEM((1, joint), F32)],
        compiler_params=pltpu.CompilerParams(vmem_limit_bytes=VMEM_LIMIT),
        cost_estimate=pl.CostEstimate(
            flops=2 * count * ordered * (joint + dim), bytes_accessed=12 * MIB, transcendentals=0
        ),
        name="norm_project_rotate",
    )(x, order, spread, weights[0], weights[1], cosine, sine)


def back_in_order(value, order):
    high = value.astype(BF16)
    low = (value - high.astype(F32)).astype(BF16)
    return dot_nt(high, order) + dot_nt(low, order)


def out_kernel(attended_ref, x_ref, w_low_ref, w_high_ref, order_ref, gain_ref, resid_ref, normed_ref):
    attended = attended_ref[...]
    branch = jnp.concatenate([dot_nt(attended, w_low_ref[...]), dot_nt(attended, w_high_ref[...])], axis=1)
    resid = x_ref[...].astype(F32) + back_in_order(branch, order_ref[...])
    inverse = lax.rsqrt(jnp.mean(resid * resid, axis=-1, keepdims=True) + EPSILON)
    resid_ref[...] = resid
    normed_ref[...] = (resid * inverse * gain_ref[...]).astype(BF16)


def project_out(attended, x, weights, order, gain, rows, seq):
    dim = x.shape[1]
    count = rows
    return pl.pallas_call(
        out_kernel,
        grid=(1,),
        in_specs=[
            rows_of(rows, attended.shape[1]),
            pl.BlockSpec((rows, dim), lambda i: (seq, 0)),
            whole(weights[0]),
            whole(weights[1]),
            whole(order),
            whole(gain),
        ],
        out_specs=[rows_of(rows, dim), rows_of(rows, dim)],
        out_shape=[jax.ShapeDtypeStruct((count, dim), F32), jax.ShapeDtypeStruct((count, dim), BF16)],
        compiler_params=pltpu.CompilerParams(vmem_limit_bytes=VMEM_LIMIT),
        cost_estimate=pl.CostEstimate(flops=6 * count * dim * dim, bytes_accessed=8 * MIB, transcendentals=0),
        name="project_out_norm",
    )(attended, x, weights[0], weights[1], order, gain)


def sum_rows(value):
    return jnp.sum(value, axis=0, keepdims=True)


def norm_back(values, inverse, gain, incoming):
    scaled = incoming * gain
    mean_term = jnp.mean(scaled * values, axis=-1, keepdims=True)
    return inverse * scaled - values * inverse**3 * mean_term


def total_of(own_ref, *away_refs):
    total = own_ref[...]
    for ref in away_refs:
        total = total + ref[...].astype(F32)
    return total


def out_back_kernel(
    d_ref, resid_ref, cot_ref, w_low_ref, w_high_ref, order_ref, gain_ref,
    d_resid_ref, d_branch_ref, d_attended_ref, gain_grad_ref,
):
    middle = w_low_ref.shape[0]
    d_normed = d_ref[...].astype(F32)
    resid = resid_ref[...]
    inverse = lax.rsqrt(jnp.mean(resid * resid, axis=-1, keepdims=True) + EPSILON)
    d_resid = cot_ref[...].astype(F32) + norm_back(resid, inverse, gain_ref[...], d_normed)
    d_resid_ref[...] = d_resid
    d_branch = dot_nn(d_resid.astype(BF16), order_ref[...]).astype(BF16)
    d_branch_ref[...] = d_branch
    d_attended = dot_nn(d_branch[:, :middle], w_low_ref[...])
    d_attended = d_attended + dot_nn(d_branch[:, middle:], w_high_ref[...])
    d_attended_ref[...] = d_attended.astype(BF16)
    gain_grad_ref[...] = sum_rows(d_normed * resid * inverse)


def project_out_back(d_normed, resid, cot, weights, order, gain, rows, seq):
    count, dim = resid.shape
    ordered = order.shape[1]
    width = dim
    return pl.pallas_call(
        out_back_kernel,
        grid=(1,),
        in_specs=[
            rows_of(rows, dim),
            rows_of(rows, dim),
            pl.BlockSpec((rows, dim), lambda i: (seq, 0)),
            whole(weights[0]),
            whole(weights[1]),
            whole(order),
            whole(gain),
        ],
        out_specs=[
            rows_of(rows, dim),
            rows_of(rows, ordered),
            rows_of(rows, width),
            pl.BlockSpec((1, dim), lambda i: (0, 0)),
        ],
        out_shape=[
            jax.ShapeDtypeStruct((count, dim), F32),
            jax.ShapeDtypeStruct((count, ordered), BF16),
            jax.ShapeDtypeStruct((count, width), BF16),
            jax.ShapeDtypeStruct((1, dim), F32),
        ],
        compiler_params=pltpu.CompilerParams(vmem_limit_bytes=VMEM_LIMIT),
        cost_estimate=pl.CostEstimate(flops=4 * count * dim * dim, bytes_accessed=12 * MIB, transcendentals=0),
        name="norm_back_project",
    )(d_normed, resid, cot, weights[0], weights[1], order, gain)


def call_whole(kernel, operands, out_shape, flops, name):
    return pl.pallas_call(
        kernel,
        in_specs=[pl.BlockSpec(memory_space=pltpu.VMEM)] * len(operands),
        out_specs=[pl.BlockSpec(memory_space=pltpu.VMEM)] * len(out_shape),
        out_shape=out_shape,
        compiler_params=pltpu.CompilerParams(vmem_limit_bytes=VMEM_LIMIT),
        cost_estimate=pl.CostEstimate(flops=flops, bytes_accessed=16 * MIB, transcendentals=0),
        name=name,
    )(*operands)


def input_back_kernel(*refs):
    dqs, terms = refs[:2], refs[2:10]
    x_ref, d_resid_ref, w_low_ref, w_high_ref, order_ref, gain_ref, cos_ref, sin_ref = refs[10:18]
    d_kv_ref, input_grad_ref, gain_grad_ref, bias_grad_ref = refs[18:]
    dkv = jnp.concatenate([total_of(*terms[:4]), total_of(*terms[4:])], axis=0)
    dk = dkv[:, :LANES]
    dk = dk * cos_ref[...] - swap_halves(dk) * sin_ref[...]
    d_kv = jnp.concatenate([dk.astype(BF16), dkv[:, LANES:].astype(BF16)], axis=1)
    d_kv_ref[...] = d_kv
    dq = jnp.concatenate([ref[...] for ref in dqs], axis=0)
    d_joined = jnp.concatenate([dq, d_kv], axis=1)
    d_normed = jnp.concatenate([dot_nt(d_joined, w_low_ref[...]), dot_nt(d_joined, w_high_ref[...])], axis=1)
    d_normed = back_in_order(d_normed, order_ref[...])
    x = x_ref[...].astype(F32)
    inverse = lax.rsqrt(jnp.mean(x * x, axis=-1, keepdims=True) + EPSILON)
    input_grad_ref[...] = (d_resid_ref[...] + norm_back(x, inverse, gain_ref[...], d_normed)).astype(BF16)
    gain_grad_ref[...] = sum_rows(d_normed * x * inverse)
    bias_grad_ref[...] = sum_rows(d_joined.astype(F32))


def input_back(dq, terms, x, d_resid, weights, order, gain, cosine, sine):
    count, dim = x.shape
    joint = dq[0].shape[1] + 2 * LANES
    return call_whole(
        input_back_kernel,
        (*dq, *terms[0], *terms[1], x, d_resid, *weights, order, gain, cosine, sine),
        [
            jax.ShapeDtypeStruct((count, 2 * LANES), BF16),
            jax.ShapeDtypeStruct((count, dim), BF16),
            jax.ShapeDtypeStruct((1, dim), F32),
            jax.ShapeDtypeStruct((1, joint), F32),
        ],
        30 * count * dim * joint,
        "input_gradient",
    )


def seq_rows(seq, rows, cols):
    return pl.BlockSpec((rows, cols), lambda i: (seq, 0))


def piece_of(seq, rows):
    return pl.BlockSpec((1, rows, 2 * LANES), lambda i: (seq, 0, 0))


def keys_and_values(piece_refs):
    joint = jnp.concatenate([ref[0] for ref in piece_refs], axis=0)
    key, value = joint[:, :LANES], joint[:, LANES:]
    return (key, other_head(key)), (value, other_head(value))


def attend_kernel(block_ref, q_ref, kv_0, kv_1, kv_2, kv_3, start_ref, out_ref, level_ref):
    rows, width = q_ref.shape
    length = 4 * rows
    heads = width // HD
    group = heads // 2
    keys, values = keys_and_values((kv_0, kv_1, kv_2, kv_3))
    upper_key = lane_of((length, LANES)) >= HD
    upper = lane_of((rows, LANES)) >= HD
    query_at = block_ref[0] * rows + lax.broadcasted_iota(jnp.int32, (rows, length), 0)
    key_at = jnp.concatenate(
        [
            (block_ref[0] ^ place) * rows + lax.broadcasted_iota(jnp.int32, (rows, rows), 1)
            for place in range(4)
        ],
        axis=1,
    )
    allowed = (key_at <= query_at) & (key_at >= start_ref[:, :1])
    bias = jnp.where(allowed, 0.0, MASKED)
    one = jnp.ones((), BF16)
    lane = lane_of((rows, LANES))
    levels = jnp.zeros((rows, LANES), F32)
    for pair in range(heads // 2):
        at = slice(pair * LANES, (pair + 1) * LANES)
        both = q_ref[:, at]
        parts = []
        for place in range(2):
            owner = (2 * pair + place) // group
            moved = int(owner != place)
            side = upper if place else ~upper
            side_key = upper_key if place else ~upper_key
            query = jnp.where(side, both, jnp.zeros_like(both))
            score = dot_nt(query, keys[moved]) + bias
            top = jnp.max(score, axis=1, keepdims=True)
            weight = jnp.exp(score - top).astype(BF16)
            mixed = dot_nn(weight, jnp.where(side_key, values[moved], one))
            total = pltpu.roll(mixed, HD, 1)
            parts.append(mixed / total)
            level = top + jnp.log(total[:, place * HD : place * HD + 1])
            levels = jnp.where(lane == 2 * pair + place, level, levels)
        out_ref[:, at] = jnp.where(upper, parts[1], parts[0]).astype(BF16)
    level_ref[...] = levels


def attend(block, q, kv_pieces, start, rows, seq):
    width = q.shape[1]
    heads = width // HD
    return pl.pallas_call(
        attend_kernel,
        grid=(1,),
        in_specs=[
            pl.BlockSpec(memory_space=pltpu.SMEM),
            seq_rows(seq, rows, width),
            *[piece_of(seq, rows)] * 4,
            seq_rows(seq, rows, LANES),
        ],
        out_specs=[seq_rows(0, rows, width), seq_rows(0, rows, LANES)],
        out_shape=[jax.ShapeDtypeStruct((rows, width), BF16), jax.ShapeDtypeStruct((rows, LANES), F32)],
        compiler_params=pltpu.CompilerParams(vmem_limit_bytes=VMEM_LIMIT),
        cost_estimate=pl.CostEstimate(
            flops=32 * rows * rows * LANES * heads,
            bytes_accessed=4 * rows * width,
            transcendentals=4 * rows * rows * heads,
        ),
        name="attention_forward",
    )(block, q, *kv_pieces, start)


def attend_back_kernel(
    block_ref, q_ref, kv_0, kv_1, kv_2, kv_3, back_ref, out_ref, level_ref, start_ref, cos_ref, sin_ref,
    dq_ref, own_ref, core_ref, x_ref, far_ref, dk_sum, dv_sum,
):
    rows, width = q_ref.shape
    heads = width // HD
    group = heads // 2
    keys, values = keys_and_values((kv_0, kv_1, kv_2, kv_3))
    key_t = keys[0].astype(F32).T.astype(BF16)
    keys_t = (key_t, jnp.concatenate([key_t[HD:], key_t[:HD]], axis=0))
    upper = lane_of((rows, LANES)) >= HD
    upper_t = lax.broadcasted_iota(jnp.int32, (LANES, rows), 0) >= HD
    query_at = block_ref[0] * rows + lax.broadcasted_iota(jnp.int32, (rows, rows), 1)
    key_at = lax.broadcasted_iota(jnp.int32, (rows, rows), 0)
    biases = []
    for place in range(4):
        at = (block_ref[0] ^ place) * rows + key_at
        biases.append(jnp.where((at <= query_at) & (at >= start_ref[0, :1, :]), 0.0, MASKED))
    head_of = lax.broadcasted_iota(jnp.int32, (width, LANES), 0) // HD
    by_head = (head_of == lane_of((width, LANES))).astype(BF16)
    product = back_ref[...].astype(F32) * out_ref[...].astype(F32)
    product_high = product.astype(BF16)
    product_low = (product - product_high.astype(F32)).astype(BF16)
    row_sums = (dot_nn(product_high, by_head) + dot_nn(product_low, by_head)).T
    levels = level_ref[...].T
    cosine, sine = cos_ref[...], sin_ref[...]
    dk_sum[...] = jnp.zeros_like(dk_sum)
    dv_sum[...] = jnp.zeros_like(dv_sum)
    for pair in range(heads // 2):
        at = slice(pair * LANES, (pair + 1) * LANES)
        both = q_ref[:, at]
        back_both = back_ref[:, at]
        zero = jnp.zeros_like(both)
        sides = (~upper, upper)
        queries = [jnp.where(side, both, zero) for side in sides]
        backs = [jnp.where(side, back_both, zero) for side in sides]
        owners = [(2 * pair + place) // group for place in range(2)]
        d_query_t = [jnp.zeros((LANES, rows), F32) for _ in range(2)]
        for piece in range(4):
            span = slice(piece * rows, (piece + 1) * rows)
            probs, d_scores = [], []
            for place in range(2):
                head = 2 * pair + place
                moved = int(owners[place] != place)
                score = dot_nt(keys[moved][span], queries[place]) + biases[piece]
                prob = jnp.exp(score - levels[head : head + 1])
                d_prob = dot_nt(values[moved][span], backs[place])
                d_score = (prob * (d_prob - row_sums[head : head + 1])).astype(BF16)
                d_query_t[place] = d_query_t[place] + dot_nn(keys_t[moved][:, span], d_score)
                probs.append(prob.astype(BF16))
                d_scores.append(d_score)
            if owners[0] == owners[1]:
                dv_sum[owners[0], span] += dot_nn(
                    jnp.concatenate(probs, axis=1), jnp.concatenate(backs, axis=0)
                )
                dk_sum[owners[0], span] += dot_nn(
                    jnp.concatenate(d_scores, axis=1), jnp.concatenate(queries, axis=0)
                )
            else:
                for place in range(2):
                    dv_sum[owners[place], span] += dot_nn(probs[place], backs[place])
                    dk_sum[owners[place], span] += dot_nn(d_scores[place], queries[place])
        d_query = jnp.where(upper_t, d_query_t[1], d_query_t[0]).T * SCALE
        dq_ref[:, at] = (d_query * cosine - swap_halves(d_query) * sine).astype(BF16)
    lower_key = lane_of((4 * rows, LANES)) < HD
    for total, begin in ((dk_sum, 0), (dv_sum, LANES)):
        first, second = total[0], total[1]
        first = first + pltpu.roll(first, HD, 1)
        second = second + pltpu.roll(second, HD, 1)
        both = jnp.where(lower_key, first, second)
        cols = slice(begin, begin + LANES)
        own_ref[:, cols] = both[:rows]
        for place, ref in enumerate((core_ref, x_ref, far_ref)):
            ref[:, cols] = both[(place + 1) * rows : (place + 2) * rows].astype(BF16)


def parts_of(rows, cols):
    shapes = [jax.ShapeDtypeStruct((rows, cols), F32)] + [jax.ShapeDtypeStruct((rows, cols), BF16)] * 3
    return [seq_rows(0, rows, cols)] * 4, shapes


def attend_back(block, q, kv_pieces, back, out, level, start, cosine, sine, rows, seq):
    width = q.shape[1]
    length = 4 * rows
    heads = width // HD
    specs, shapes = parts_of(rows, 2 * LANES)
    return pl.pallas_call(
        attend_back_kernel,
        grid=(1,),
        in_specs=[
            pl.BlockSpec(memory_space=pltpu.SMEM),
            seq_rows(seq, rows, width),
            *[piece_of(seq, rows)] * 4,
            seq_rows(0, rows, width),
            seq_rows(0, rows, width),
            seq_rows(0, rows, LANES),
            pl.BlockSpec((1, 8, rows), lambda i: (seq, 0, 0)),
            seq_rows(seq, rows, LANES),
            seq_rows(seq, rows, LANES),
        ],
        out_specs=[seq_rows(0, rows, width), *specs],
        out_shape=[jax.ShapeDtypeStruct((rows, width), BF16), *shapes],
        scratch_shapes=[
            pltpu.VMEM((2, length, LANES), F32),
            pltpu.VMEM((2, length, LANES), F32),
        ],
        compiler_params=pltpu.CompilerParams(vmem_limit_bytes=VMEM_LIMIT),
        cost_estimate=pl.CostEstimate(
            flops=80 * rows * rows * LANES * heads,
            bytes_accessed=8 * rows * width,
            transcendentals=4 * rows * rows * heads,
        ),
        name="attention_backward",
    )(block, q, *kv_pieces, back, out, level, start, cosine, sine)


def mlp_kernel(count_normed, plane_ref, *refs):
    normed_refs, refs = refs[:count_normed], refs[count_normed:]
    cot_refs, w_ref, refs = refs[:4], refs[4], refs[5:]
    own_ref, out_1, out_2, out_3, d_ref, kept_ref, turned_ref, normed_all, cot_all = refs
    step = pl.program_id(0)
    rows = own_ref.shape[0]
    columns = w_ref.shape[1] // 3
    plane = plane_ref[0]

    @pl.when(step == 0)
    def _():
        for place in range(4):
            half, at = place // 2, slice((place % 2) * rows, (place % 2 + 1) * rows)
            normed_all[half, at] = normed_refs[place][...] if count_normed == 4 else normed_refs[0][plane ^ place]
            cot_all[half, at] = cot_refs[place][...]

    normed, cot = normed_all[step], cot_all[step]

    def products(begin):
        cols = [slice(part * columns + begin, part * columns + begin + TILE) for part in range(3)]
        return (
            dot_nn(normed, w_ref[:, cols[0]]),
            dot_nn(normed, w_ref[:, cols[1]]),
            dot_nn(cot, w_ref[:, cols[2]]),
        )

    ahead = products(0)
    for begin in range(0, columns, TILE):
        at = slice(begin, begin + TILE)
        gate, up, d_act = ahead
        if begin + TILE < columns:
            ahead = products(begin + TILE)
        sigmoid = 0.5 * jnp.tanh(0.5 * gate) + 0.5
        swish = gate * sigmoid
        kept_ref[0, :, at] = (d_act * up * (sigmoid + swish * (1.0 - sigmoid))).astype(BF16)
        kept_ref[1, :, at] = (d_act * swish).astype(BF16)
        kept_ref[2, :, at] = (swish * up).astype(BF16)
    turned_ref[0] = normed.T
    turned_ref[1] = cot.T
    out = dot_nt(kept_ref[2], w_ref[:, 2 * columns :])
    d_normed = dot_nt(kept_ref[0], w_ref[:, :columns]) + dot_nt(kept_ref[1], w_ref[:, columns : 2 * columns])
    d_ref[plane ^ (2 * step)] = d_normed[:rows].astype(BF16)
    d_ref[plane ^ (2 * step + 1)] = d_normed[rows:].astype(BF16)

    @pl.when(step == 0)
    def _():
        own_ref[...] = out[:rows]
        out_1[...] = out[rows:].astype(BF16)

    @pl.when(step == 1)
    def _():
        out_2[...] = out[:rows].astype(BF16)
        out_3[...] = out[rows:].astype(BF16)


def mlp(plane, normed, cot, weights, seq):
    rows, dim = cot[3].shape
    columns = weights.shape[1] // 3
    specs, shapes = parts_of(rows, dim)
    once = lambda at: pl.BlockSpec((rows, dim), lambda i: (at, 0), pipeline_mode=pl.Buffered(1))
    plane_block = pl.BlockSpec((4, rows, dim), lambda i: (0, 0, 0), pipeline_mode=pl.Buffered(1))
    return pl.pallas_call(
        functools.partial(mlp_kernel, len(normed)),
        grid=(2,),
        in_specs=[
            pl.BlockSpec(memory_space=pltpu.SMEM),
            *([once(0)] * 4 if len(normed) == 4 else [plane_block]),
            *[once(seq)] * 3,
            once(0),
            pl.BlockSpec(weights.shape, lambda i: (0, 0), pipeline_mode=pl.Buffered(1)),
        ],
        out_specs=[
            *specs,
            pl.BlockSpec((4, rows, dim), lambda i: (0, 0, 0)),
            pl.BlockSpec((3, 2 * rows, columns), lambda i: (0, i, 0)),
            pl.BlockSpec((2, dim, 2 * rows), lambda i: (0, 0, i)),
        ],
        out_shape=[
            *shapes,
            jax.ShapeDtypeStruct((4, rows, dim), BF16),
            jax.ShapeDtypeStruct((3, 4 * rows, columns), BF16),
            jax.ShapeDtypeStruct((2, dim, 4 * rows), BF16),
        ],
        scratch_shapes=[
            pltpu.VMEM((2, 2 * rows, dim), BF16),
            pltpu.VMEM((2, 2 * rows, dim), BF16),
        ],
        compiler_params=pltpu.CompilerParams(vmem_limit_bytes=VMEM_LIMIT),
        cost_estimate=pl.CostEstimate(
            flops=48 * rows * dim * columns,
            bytes_accessed=6 * dim * columns + 24 * rows * columns,
            transcendentals=4 * rows * columns,
        ),
        name="feed_forward",
    )(plane, *normed, *cot, weights)


def mlp_grad_kernel(turned_0, turned_1, kept_0, kept_1, grad_ref):
    grad_ref[...] = (dot_nn(turned_0[0], kept_0[0]) + dot_nn(turned_1[0], kept_1[0])).astype(BF16)


def mlp_grad(turned, kept):
    _, dim, count = turned[0].shape
    columns = kept[0].shape[2]
    turned_block = pl.BlockSpec((1, dim, count), lambda i: (i // 2, 0, 0))
    kept_block = pl.BlockSpec((1, count, columns), lambda i: (i, 0, 0))
    return pl.pallas_call(
        mlp_grad_kernel,
        grid=(3,),
        in_specs=[turned_block, turned_block, kept_block, kept_block],
        out_specs=pl.BlockSpec((dim, columns), lambda i: (0, i)),
        out_shape=jax.ShapeDtypeStruct((dim, 3 * columns), BF16),
        compiler_params=pltpu.CompilerParams(vmem_limit_bytes=VMEM_LIMIT),
        cost_estimate=pl.CostEstimate(
            flops=12 * count * dim * columns,
            bytes_accessed=6 * dim * columns + 12 * count * columns,
            transcendentals=0,
        ),
        name="feed_forward_gradients",
    )(*turned, *kept)


def pack_kernel(block_ref, gate_ref, up_ref, down_ref, *refs):
    out_refs, scratch = refs[:4], refs[4]
    shard, ff = gate_ref.shape
    quarter = scratch.shape[2] // 4
    for place, ref in enumerate((gate_ref, up_ref, down_ref)):
        scratch[place, :, :ff] = ref[...].astype(F32)
        scratch[place, :, ff:] = jnp.zeros((shard, 4 * quarter - ff), F32)
    for place, out_ref in enumerate(out_refs):
        begin = pl.multiple_of((block_ref[0] ^ place) * quarter, LANES)
        for part in range(3):
            out_ref[:, part * quarter : (part + 1) * quarter] = scratch[part, :, pl.ds(begin, quarter)].astype(BF16)


def pack(block, gate, up, down_t, quarter):
    shard = gate.shape[0]
    return pl.pallas_call(
        pack_kernel,
        in_specs=[pl.BlockSpec(memory_space=pltpu.SMEM)] + [pl.BlockSpec(memory_space=pltpu.VMEM)] * 3,
        out_specs=[pl.BlockSpec(memory_space=pltpu.VMEM)] * 4,
        out_shape=[jax.ShapeDtypeStruct((shard, 3 * quarter), BF16)] * 4,
        scratch_shapes=[pltpu.VMEM((3, shard, 4 * quarter), F32)],
        compiler_params=pltpu.CompilerParams(vmem_limit_bytes=VMEM_LIMIT),
        name="pack_columns",
    )(block, gate, up, down_t)


def pick(options, index):
    value = options[0]
    for place in range(1, len(options)):
        value = jnp.where(index == place, options[place], value)
    return value


def assemble_kernel(block_ref, *refs):
    pieces, out_ref, scratch = refs[:4], refs[4], refs[5]
    shard = pieces[0].shape[0]
    values = [ref[...].astype(F32) for ref in pieces]
    for owner in range(4):
        scratch[owner * shard : (owner + 1) * shard] = pick(values, block_ref[0] ^ owner)
    out_ref[...] = scratch[...].astype(BF16)


def assemble(block, pieces):
    shard, columns = pieces[0].shape
    return pl.pallas_call(
        assemble_kernel,
        in_specs=[pl.BlockSpec(memory_space=pltpu.SMEM)] + [pl.BlockSpec(memory_space=pltpu.VMEM)] * 4,
        out_specs=pl.BlockSpec(memory_space=pltpu.VMEM),
        out_shape=jax.ShapeDtypeStruct((4 * shard, columns), BF16),
        scratch_shapes=[pltpu.VMEM((4 * shard, columns), F32)],
        compiler_params=pltpu.CompilerParams(vmem_limit_bytes=VMEM_LIMIT),
        name="assemble_rows",
    )(block, *pieces)


def cut_kernel(block_ref, value_ref, *refs):
    out_refs, scratch = refs[:4], refs[4]
    shard = out_refs[0].shape[0]
    scratch[...] = value_ref[...].astype(F32)
    values = [scratch[owner * shard : (owner + 1) * shard] for owner in range(4)]
    for place, out_ref in enumerate(out_refs):
        out_ref[...] = pick(values, block_ref[0] ^ place).astype(BF16)


def cut(block, value):
    shard, columns = value.shape[0] // 4, value.shape[1]
    return pl.pallas_call(
        cut_kernel,
        in_specs=[pl.BlockSpec(memory_space=pltpu.SMEM), pl.BlockSpec(memory_space=pltpu.VMEM)],
        out_specs=[pl.BlockSpec(memory_space=pltpu.VMEM)] * 4,
        out_shape=[jax.ShapeDtypeStruct((shard, columns), BF16)] * 4,
        scratch_shapes=[pltpu.VMEM(value.shape, F32)],
        compiler_params=pltpu.CompilerParams(vmem_limit_bytes=VMEM_LIMIT),
        name="cut_rows",
    )(block, value)


def unpack_kernel(block_ref, *refs):
    pieces, out_refs, scratch = refs[:4], refs[4:7], refs[7]
    ff = out_refs[0].shape[1]
    quarter = scratch.shape[2] // 4
    for place, ref in enumerate(pieces):
        begin = pl.multiple_of((block_ref[0] ^ place) * quarter, LANES)
        for part in range(3):
            scratch[part, :, pl.ds(begin, quarter)] = ref[:, part * quarter : (part + 1) * quarter].astype(F32)
    for part, out_ref in enumerate(out_refs):
        out_ref[...] = scratch[part, :, :ff]


def unpack(block, pieces, ff):
    shard, columns = pieces[0].shape
    return pl.pallas_call(
        unpack_kernel,
        in_specs=[pl.BlockSpec(memory_space=pltpu.SMEM)] + [pl.BlockSpec(memory_space=pltpu.VMEM)] * 4,
        out_specs=[pl.BlockSpec(memory_space=pltpu.VMEM)] * 3,
        out_shape=[jax.ShapeDtypeStruct((shard, ff), F32)] * 3,
        scratch_shapes=[pltpu.VMEM((3, shard, columns // 3 * 4), F32)],
        compiler_params=pltpu.CompilerParams(vmem_limit_bytes=VMEM_LIMIT),
        name="unpack_columns",
    )(block, *pieces)


def bit_swap(value, axis, bit=0):
    size = lax.axis_size(axis)
    return lax.ppermute(value, axis, [(i, i ^ (1 << bit)) for i in range(size)])


def jump_swap(value, axes, jump):
    return lax.ppermute(value, axes, [(i, i ^ jump) for i in range(4)])


def to_plane(value, slot):
    high, low = slot >> 1, slot & 1
    pairs = [
        (4 * y + 2 * x + c, 4 * (c ^ low) + 2 * (x ^ high) + y) for y in range(2) for x in range(2) for c in range(2)
    ]
    return lax.ppermute(value, TOKENS + ("cc",), pairs)


def from_plane(value, slot):
    high, low = slot >> 1, slot & 1
    pairs = [
        (4 * y + 2 * x + c, 4 * c + 2 * (x ^ high) + (y ^ low)) for y in range(2) for x in range(2) for c in range(2)
    ]
    return lax.ppermute(value, TOKENS + ("cc",), pairs)


def after(first, *values):
    return lax.optimization_barrier((first, *values))


def gather_four(value, axes):
    from_first = bit_swap(value, axes[0])
    return [value, bit_swap(value, axes[1]), from_first, bit_swap(from_first, axes[1])]


def gather_direct(value, axes):
    return [value] + [jump_swap(value, axes, jump) for jump in range(1, 4)]


def sum_direct(axes, own, *away):
    return [own] + [jump_swap(value, axes, jump + 1) for jump, value in enumerate(away)]


def doubling_offsets(steps):
    weight = {"cc": 1, "cx": 2, "fy": 4, "fz": 8}
    offsets = [0]
    for axis, bit in steps:
        offsets += [offset ^ (weight[axis] << bit) for offset in offsets]
    return jnp.array(offsets, jnp.int32)


def double(value, axis, bit=0):
    return jnp.concatenate([value, bit_swap(value, axis, bit)], axis=0)


def plane_gather(value):
    return jnp.concatenate(gather_direct(value, TOKENS), axis=0)


def plane_sum(value):
    parts = jnp.split(value, 4, axis=0)
    terms = sum_direct(TOKENS, *parts)
    return sum(term.astype(F32) for term in terms).astype(BF16)


def halve(value, axis, bit=0):
    middle = value.shape[0] // 2
    came = bit_swap(value[middle:], axis, bit)
    return (value[:middle].astype(F32) + came.astype(F32)).astype(BF16)


def on_device(
    hidden,
    segments,
    attn_gain,
    qkv_weight,
    qkv_bias,
    out_weight,
    mlp_gain,
    gate_weight,
    up_weight,
    down_weight,
    cotangent,
):
    seqs, rows, dim = hidden.shape
    count = seqs * rows
    shard = attn_gain.shape[0]
    world = dim // shard
    joint = qkv_weight.shape[1]
    width = joint - 2 * LANES
    ff = gate_weight.shape[1]
    block = lax.axis_index("cx") * lax.axis_size("cc") + lax.axis_index("cc")
    me = lax.axis_index(FSDP) * lax.axis_size(CTX) + block
    offset = block * rows
    block_arg = block.reshape(1).astype(jnp.int32)
    plane_arg = (lax.axis_index("cx") * 2 + lax.axis_index("fy")).reshape(1).astype(jnp.int32)
    x = hidden.reshape(count, dim)
    cot = cotangent.reshape(count, dim)

    cot_x, cot_y = bit_swap(cot, "cx"), bit_swap(cot, "fy")

    far = [("fz", bit) for bit in reversed(range((lax.axis_size("fz")).bit_length() - 1))]
    padded = -(-(shard + 1) // 16) * 16
    small = jnp.concatenate([attn_gain, mlp_gain, qkv_bias])
    small_row = jnp.pad(small, (0, joint + width - small.shape[0]))[None]
    first = jnp.concatenate(
        [
            jnp.concatenate([qkv_weight, out_weight.T], axis=1),
            small_row,
            jnp.zeros((padded - shard - 1, joint + width), BF16),
        ],
        axis=0,
    )
    first = double(first, *far[0])

    quarter = -(-ff // (4 * TILE)) * TILE
    first, *pieces = after(first, *pack(block_arg, gate_weight, up_weight, down_weight.T, quarter))
    pieces = [to_plane(piece, slot) for slot, piece in enumerate(pieces)]
    for axis, bit in far[1:]:
        first = double(first, axis, bit)

    within = jnp.arange(padded, dtype=jnp.int32)
    owner = me ^ doubling_offsets(far + [("cx", 0), ("fy", 0), ("cc", 0)])
    target = jnp.where(within[None, :] < shard, owner[:, None] * shard + within[None, :], -1).reshape(1, -1)
    order = (jnp.arange(dim, dtype=jnp.int32)[:, None] == target).astype(BF16)
    place = jnp.where(within[None, :] == shard, owner[:, None], -1).reshape(1, -1)
    spread = (jnp.arange(world, dtype=jnp.int32)[:, None] == place).astype(BF16)

    at_row = lax.dynamic_slice_in_dim(segments, offset, rows, axis=1)
    zeros_before = jnp.sum((segments < 1).astype(jnp.int32), axis=1, keepdims=True)
    ones_before = jnp.sum((segments < 2).astype(jnp.int32), axis=1, keepdims=True)
    start = jnp.where(at_row == 0, 0, jnp.where(at_row == 1, zeros_before, ones_before))
    position = (offset + jnp.arange(rows, dtype=jnp.int32)[None, :] - start).reshape(count)
    lane = jnp.arange(LANES, dtype=jnp.int32)
    frequency = ROPE_BASE ** (-(lane % (HD // 2)).astype(F32) * 2.0 / HD)
    angle = position.astype(F32)[:, None] * frequency[None, :]
    cosine = jnp.cos(angle)
    sine = jnp.where(lane % HD < HD // 2, -1.0, 1.0)[None, :] * jnp.sin(angle)
    start_column = jnp.broadcast_to(start.reshape(count, 1), (count, LANES))
    start_row = jnp.broadcast_to(start[:, None, :], (seqs, 8, rows))

    first, cot_x, cot_y, order, spread, cosine, sine, start_column, *pieces = after(
        first, cot_x, cot_y, order, spread, cosine, sine, start_column, *pieces
    )
    w_joint = plane_gather(first[:, :joint])
    mlp_shard = assemble(plane_arg, pieces)
    mlp_weights = lax.all_gather(mlp_shard, WEIGHTS, axis=0, tiled=True)
    w_joint, far_0, far_1 = after(w_joint, cot_x[:rows], cot_y[rows:])
    w_joint = (w_joint, bit_swap(w_joint, "cc"))
    cot_far = [bit_swap(far_0, "fy"), bit_swap(far_1, "cx")]

    normed, q, kv, gain_attn, gain_mlp = prep(x, order, spread, w_joint, cosine, sine, rows)
    kv_all = gather_four(kv.reshape(seqs, rows, 2 * LANES), CTX)
    kv_all[3], out_rows = after(kv_all[3], first[:, joint:])
    w_out = plane_gather(out_rows)
    attended, levels, resid, normed_all = [], [], [], []
    for seq in range(seqs):
        turn = block_arg if seq == 0 else after(attended[0], block_arg)[1]
        attended_one, level_one = attend(turn, q, kv_all, start_column, rows, seq)
        if seq == 0:
            attended_one, w_out = after(attended_one, w_out)
            w_out = (w_out, bit_swap(w_out, "cc"))
        else:
            attended_one, *cot_far = after(attended_one, *cot_far)
        attended.append(attended_one)
        levels.append(level_one)
        resid_one, normed_one = project_out(attended[seq], x, w_out, order, gain_mlp, rows, seq)
        resid.append(resid_one)
        if seq == 0:
            normed_all.append(gather_direct(normed_one, TOKENS))
        else:
            normed_all.append([lax.all_gather(normed_one, TOKENS, axis=0, tiled=False)])

    out_parts, d_terms, kept, turned = [], [], [], []
    tokens_arg = lax.axis_index(TOKENS).reshape(1).astype(jnp.int32)
    for seq in range(seqs):
        if seq == 1:
            out_parts[0][0], normed_all[1][0] = after(out_parts[0][0], normed_all[1][0])
        result = mlp(tokens_arg, normed_all[seq], [cot, cot_x, cot_y, cot_far[seq]], mlp_weights, seq)
        out_parts.append(list(result[:4]))
        d_terms.append(lax.psum_scatter(result[4], TOKENS, scatter_dimension=0, tiled=False))
        kept.append(result[5])
        turned.append(result[6])

    d_resid, d_branch, d_attended, mlp_gain_grad, dq, dkv_terms, out_terms = [], [], [], [], [], [], []
    for seq in range(seqs):
        if seq == 0:
            kept[1], d_terms[0] = after(kept[1], d_terms[0])
        else:
            dq[0], d_terms[1], *out_terms[0] = after(dq[0], d_terms[1], *out_terms[0])
        result = project_out_back(d_terms[seq], resid[seq], cot, w_out, order, gain_mlp, rows, seq)
        for place, value in zip((d_resid, d_branch, d_attended, mlp_gain_grad), result):
            place.append(value)
        out_terms.append(sum_direct(TOKENS, *after(d_resid[seq], *out_parts[seq])[1:]))
        if seq == 0:
            _, turned[1] = after(d_resid[0], turned[1])
            grads = mlp_grad(turned, kept)
            grads, d_attended[0], d_terms[1] = after(grads, d_attended[0], d_terms[1])
            grads = lax.psum_scatter(
                grads.reshape(world // 4, 4 * shard, 3 * quarter), WEIGHTS, scatter_dimension=0, tiled=False
            )
        else:
            out_grad = dot_tn(jnp.concatenate(d_branch, axis=0), jnp.concatenate(attended, axis=0)).astype(BF16)
            out_grad = halve(out_grad, "cc")
            d_attended[1], *dkv_terms[0] = after(d_attended[1], *dkv_terms[0])
        result = attend_back(
            block_arg, q, kv_all, d_attended[seq], attended[seq], levels[seq], start_row, cosine, sine, rows, seq
        )
        dq.append(result[0])
        dkv_terms.append(sum_direct(CTX, *result[1:]))
    dq[1], out_grad, *out_terms[1] = after(dq[1], out_grad, *out_terms[1])
    q_grad = dot_tn(normed, jnp.concatenate(dq, axis=0)).astype(BF16)
    q_grad = halve(q_grad, "cc")
    q_grad, *dkv_terms[1] = after(q_grad, *dkv_terms[1])
    q_grad = plane_sum(q_grad)
    d_resid = jnp.concatenate(d_resid, axis=0)
    d_kv, input_grad, attn_gain_grad, bias_grad = input_back(
        dq, dkv_terms, x, d_resid, w_joint, order, gain_attn, cosine, sine
    )
    d_kv, q_grad = after(d_kv, q_grad)

    output = []
    for seq in range(seqs):
        own, *away = out_terms[seq]
        output.append((resid[seq] + own + sum(term.astype(F32) for term in away)).astype(BF16))

    split_at = width + LANES
    bias_grad = bias_grad[0]
    small_grads = jnp.concatenate(
        [
            attn_gain_grad.reshape(world, -1),
            sum(mlp_gain_grad).reshape(world, -1),
            bias_grad[:split_at].reshape(world, -1),
            bias_grad[split_at:].reshape(world, -1),
        ],
        axis=1,
    ).astype(BF16)
    small_count = small_grads.shape[1]
    small_grads = jnp.pad(small_grads, ((0, 0), (0, 2 * LANES - small_count)))
    kv_grad = dot_tn(
        jnp.concatenate([normed, spread], axis=0), jnp.concatenate([d_kv, small_grads], axis=0)
    ).astype(BF16)
    pieces = cut(plane_arg, lax.optimization_barrier(grads))
    kv_grad, *pieces = after(halve(kv_grad, "cc"), *pieces)
    pieces = [from_plane(piece, slot) for slot, piece in enumerate(pieces)]
    kv_grad, out_grad = plane_sum(kv_grad), plane_sum(out_grad)
    first_sum = jnp.concatenate([q_grad, kv_grad, out_grad], axis=1)
    for axis, bit in reversed(far):
        first_sum = halve(first_sum, axis, bit)
    gate_grad, up_grad, down_grad_t = unpack(block_arg, pieces, ff)
    first_sum = first_sum.astype(F32)
    qkv_sum, out_sum = first_sum[:, :joint], first_sum[:, joint:]
    small_sum = qkv_sum[shard, width : width + small_count]
    at = (shard, 2 * shard, 2 * shard + split_at // world)

    return (
        jnp.stack(output),
        input_grad.reshape(hidden.shape),
        small_sum[: at[0]],
        qkv_sum[:shard],
        small_sum[at[1] : at[2]],
        small_sum[at[2] :],
        out_sum[:shard].T,
        small_sum[at[0] : at[1]],
        gate_grad,
        up_grad,
        down_grad_t.T,
    )


def solution(mesh):
    fsdp, ctx = mesh.shape["fsdp"], mesh.shape["ctx"]
    inner = Mesh(mesh.devices.reshape(fsdp // 2, 2, 2, ctx // 2), AXES)
    tokens = P(FSDP, CTX, None)
    vector = P(AXES)
    by_row = P(AXES, None)
    by_column = P(None, AXES)
    return jax.shard_map(
        on_device,
        mesh=inner,
        in_specs=(
            tokens,
            P(FSDP, None),
            vector,
            by_row,
            vector,
            by_column,
            vector,
            by_row,
            by_row,
            by_column,
            tokens,
        ),
        out_specs=(
            tokens,
            tokens,
            vector,
            by_row,
            vector,
            vector,
            by_column,
            vector,
            by_row,
            by_row,
            by_column,
        ),
        check_vma=False,
    )
```

```python
import functools

import jax
import jax.numpy as jnp
from jax import lax
from jax.experimental import pallas as pl
from jax.experimental.pallas import tpu as pltpu
from jax.sharding import Mesh
from jax.sharding import PartitionSpec as P

HD = 64
LANES = 128
EPSILON = 1e-06
ROPE_BASE = 1000000.0
MASKED = -1e30
SCALE = HD ** (-0.5)
TILE = 256
MIB = 1 << 20
VMEM_LIMIT = 60 * MIB
F32 = jnp.float32
BF16 = jnp.bfloat16
AXES = ("fz", "fy", "cx", "cc")
FSDP = ("fz", "fy")
CTX = ("cx", "cc")
TOKENS = ("fy", "cx")
WEIGHTS = ("fz", "cc")


def dot_nn(a, b):
    return lax.dot_general(a, b, (((1,), (0,)), ((), ())), preferred_element_type=F32)


def dot_nt(a, b):
    return lax.dot_general(a, b, (((1,), (1,)), ((), ())), preferred_element_type=F32)


def dot_tn(a, b):
    return lax.dot_general(a, b, (((0,), (0,)), ((), ())), preferred_element_type=F32)


def lane_of(shape):
    return lax.broadcasted_iota(jnp.int32, shape, len(shape) - 1)


def swap_halves(block):
    lead = lane_of(block.shape) % HD < HD // 2
    return jnp.where(
        lead, pltpu.roll(block, LANES - HD // 2, 1), pltpu.roll(block, HD // 2, 1)
    )


def other_head(block):
    return jnp.concatenate([block[:, HD:], block[:, :HD]], axis=1)


def read_out(extras, first, piece, total):
    owners, columns = extras.shape
    at = lax.broadcasted_iota(jnp.int32, (columns, total), 1) % piece + first
    chosen = (lax.broadcasted_iota(jnp.int32, (columns, total), 0) == at).astype(BF16)
    spread = dot_nn(extras, chosen)
    owner = lax.broadcasted_iota(jnp.int32, (owners, total), 1) // piece
    mine = owner == lax.broadcasted_iota(jnp.int32, (owners, total), 0)
    return jnp.sum(jnp.where(mine, spread, 0.0), axis=0, keepdims=True)


def prep_kernel(
    x_ref, order_ref, spread_ref, w_low_ref, w_high_ref, cos_ref, sin_ref,
    normed_ref, q_ref, kv_ref, gain_ref, gain_mlp_ref, bias_ref,
):
    x = x_ref[...].astype(F32)
    dim = x.shape[1]
    width = q_ref.shape[1]
    joint = w_low_ref.shape[1]
    middle = w_low_ref.shape[0]
    owners = spread_ref.shape[0]

    @pl.when(pl.program_id(0) == 0)
    def _():
        extras = dot_nn(spread_ref[:, :middle], w_low_ref[:, :LANES])
        extras = (extras + dot_nn(spread_ref[:, middle:], w_high_ref[:, :LANES])).astype(BF16)
        shard = dim // owners
        gain_ref[...] = read_out(extras, 0, shard, dim)
        gain_mlp_ref[...] = read_out(extras, shard, shard, dim)
        bias_ref[...] = read_out(extras, 2 * shard, joint // owners, joint)

    gain, bias = gain_ref[...], bias_ref[...]
    inverse = lax.rsqrt(jnp.mean(x * x, axis=-1, keepdims=True) + EPSILON)
    normed = (x * inverse * gain).astype(BF16)
    ordered = dot_nn(normed, order_ref[...]).astype(BF16)
    normed_ref[...] = ordered
    joined = dot_nn(ordered[:, :middle], w_low_ref[...])
    joined = joined + dot_nn(ordered[:, middle:], w_high_ref[...]) + bias
    cosine, sine = cos_ref[...], sin_ref[...]
    for begin in range(0, width + LANES, LANES):
        block = joined[:, begin : begin + LANES]
        turned = block * cosine + swap_halves(block) * sine
        if begin < width:
            q_ref[:, begin : begin + LANES] = (turned * SCALE).astype(BF16)
        else:
            kv_ref[:, :LANES] = turned.astype(BF16)
    kv_ref[:, LANES:] = joined[:, width + LANES :].astype(BF16)


def rows_of(rows, cols):
    return pl.BlockSpec((rows, cols), lambda i: (i, 0))


def whole(value):
    return pl.BlockSpec(value.shape, lambda i: (0,) * value.ndim)


def prep(x, order, spread, weights, cosine, sine, rows):
    count, dim = x.shape
    ordered = order.shape[1]
    joint = weights[0].shape[1]
    width = joint - 2 * LANES
    row = pl.BlockSpec((1, dim), lambda i: (0, 0))
    return pl.pallas_call(
        prep_kernel,
        grid=(count // rows,),
        in_specs=[
            rows_of(rows, dim),
            whole(order),
            whole(spread),
            whole(weights[0]),
            whole(weights[1]),
            rows_of(rows, LANES),
            rows_of(rows, LANES),
        ],
        out_specs=[rows_of(rows, ordered), rows_of(rows, width), rows_of(rows, 2 * LANES), row, row],
        out_shape=[
            jax.ShapeDtypeStruct((count, ordered), BF16),
            jax.ShapeDtypeStruct((count, width), BF16),
            jax.ShapeDtypeStruct((count, 2 * LANES), BF16),
            jax.ShapeDtypeStruct((1, dim), F32),
            jax.ShapeDtypeStruct((1, dim), F32),
        ],
        scratch_shapes=[pltpu.VMEM((1, joint), F32)],
        compiler_params=pltpu.CompilerParams(vmem_limit_bytes=VMEM_LIMIT),
        cost_estimate=pl.CostEstimate(
            flops=2 * count * ordered * (joint + dim), bytes_accessed=12 * MIB, transcendentals=0
        ),
        name="norm_project_rotate",
    )(x, order, spread, weights[0], weights[1], cosine, sine)


def back_in_order(value, order):
    high = value.astype(BF16)
    low = (value - high.astype(F32)).astype(BF16)
    return dot_nt(high, order) + dot_nt(low, order)


def out_kernel(attended_ref, x_ref, w_low_ref, w_high_ref, order_ref, gain_ref, resid_ref, normed_ref):
    attended = attended_ref[...]
    branch = jnp.concatenate([dot_nt(attended, w_low_ref[...]), dot_nt(attended, w_high_ref[...])], axis=1)
    resid = x_ref[...].astype(F32) + back_in_order(branch, order_ref[...])
    inverse = lax.rsqrt(jnp.mean(resid * resid, axis=-1, keepdims=True) + EPSILON)
    resid_ref[...] = resid
    normed_ref[...] = (resid * inverse * gain_ref[...]).astype(BF16)


def project_out(attended, x, weights, order, gain, rows, seq):
    dim = x.shape[1]
    count = rows
    return pl.pallas_call(
        out_kernel,
        grid=(1,),
        in_specs=[
            rows_of(rows, attended.shape[1]),
            pl.BlockSpec((rows, dim), lambda i: (seq, 0)),
            whole(weights[0]),
            whole(weights[1]),
            whole(order),
            whole(gain),
        ],
        out_specs=[rows_of(rows, dim), rows_of(rows, dim)],
        out_shape=[jax.ShapeDtypeStruct((count, dim), F32), jax.ShapeDtypeStruct((count, dim), BF16)],
        compiler_params=pltpu.CompilerParams(vmem_limit_bytes=VMEM_LIMIT),
        cost_estimate=pl.CostEstimate(flops=6 * count * dim * dim, bytes_accessed=8 * MIB, transcendentals=0),
        name="project_out_norm",
    )(attended, x, weights[0], weights[1], order, gain)


def sum_rows(value):
    return jnp.sum(value, axis=0, keepdims=True)


def norm_back(values, inverse, gain, incoming):
    scaled = incoming * gain
    mean_term = jnp.mean(scaled * values, axis=-1, keepdims=True)
    return inverse * scaled - values * inverse**3 * mean_term


def total_of(own_ref, *away_refs):
    total = own_ref[...]
    for ref in away_refs:
        total = total + ref[...].astype(F32)
    return total


def out_back_kernel(
    own_ref, core_ref, x_ref, far_ref, resid_ref, cot_ref, w_low_ref, w_high_ref, order_ref, gain_ref,
    d_resid_ref, d_branch_ref, d_attended_ref, gain_grad_ref,
):
    middle = w_low_ref.shape[0]
    d_normed = total_of(own_ref, core_ref, x_ref, far_ref)
    resid = resid_ref[...]
    inverse = lax.rsqrt(jnp.mean(resid * resid, axis=-1, keepdims=True) + EPSILON)
    d_resid = cot_ref[...].astype(F32) + norm_back(resid, inverse, gain_ref[...], d_normed)
    d_resid_ref[...] = d_resid
    d_branch = dot_nn(d_resid.astype(BF16), order_ref[...]).astype(BF16)
    d_branch_ref[...] = d_branch
    d_attended = dot_nn(d_branch[:, :middle], w_low_ref[...])
    d_attended = d_attended + dot_nn(d_branch[:, middle:], w_high_ref[...])
    d_attended_ref[...] = d_attended.astype(BF16)
    gain_grad_ref[...] = sum_rows(d_normed * resid * inverse)


def project_out_back(terms, resid, cot, weights, order, gain, rows, seq):
    count, dim = resid.shape
    ordered = order.shape[1]
    width = dim
    return pl.pallas_call(
        out_back_kernel,
        grid=(1,),
        in_specs=[
            rows_of(rows, dim),
            rows_of(rows, dim),
            rows_of(rows, dim),
            rows_of(rows, dim),
            rows_of(rows, dim),
            pl.BlockSpec((rows, dim), lambda i: (seq, 0)),
            whole(weights[0]),
            whole(weights[1]),
            whole(order),
            whole(gain),
        ],
        out_specs=[
            rows_of(rows, dim),
            rows_of(rows, ordered),
            rows_of(rows, width),
            pl.BlockSpec((1, dim), lambda i: (0, 0)),
        ],
        out_shape=[
            jax.ShapeDtypeStruct((count, dim), F32),
            jax.ShapeDtypeStruct((count, ordered), BF16),
            jax.ShapeDtypeStruct((count, width), BF16),
            jax.ShapeDtypeStruct((1, dim), F32),
        ],
        compiler_params=pltpu.CompilerParams(vmem_limit_bytes=VMEM_LIMIT),
        cost_estimate=pl.CostEstimate(flops=4 * count * dim * dim, bytes_accessed=12 * MIB, transcendentals=0),
        name="norm_back_project",
    )(*terms, resid, cot, weights[0], weights[1], order, gain)


def call_whole(kernel, operands, out_shape, flops, name):
    return pl.pallas_call(
        kernel,
        in_specs=[pl.BlockSpec(memory_space=pltpu.VMEM)] * len(operands),
        out_specs=[pl.BlockSpec(memory_space=pltpu.VMEM)] * len(out_shape),
        out_shape=out_shape,
        compiler_params=pltpu.CompilerParams(vmem_limit_bytes=VMEM_LIMIT),
        cost_estimate=pl.CostEstimate(flops=flops, bytes_accessed=16 * MIB, transcendentals=0),
        name=name,
    )(*operands)


def input_back_kernel(*refs):
    dqs, terms = refs[:2], refs[2:10]
    x_ref, d_resid_ref, w_low_ref, w_high_ref, order_ref, gain_ref, cos_ref, sin_ref = refs[10:18]
    d_kv_ref, input_grad_ref, gain_grad_ref, bias_grad_ref = refs[18:]
    dkv = jnp.concatenate([total_of(*terms[:4]), total_of(*terms[4:])], axis=0)
    dk = dkv[:, :LANES]
    dk = dk * cos_ref[...] - swap_halves(dk) * sin_ref[...]
    d_kv = jnp.concatenate([dk.astype(BF16), dkv[:, LANES:].astype(BF16)], axis=1)
    d_kv_ref[...] = d_kv
    dq = jnp.concatenate([ref[...] for ref in dqs], axis=0)
    d_joined = jnp.concatenate([dq, d_kv], axis=1)
    d_normed = jnp.concatenate([dot_nt(d_joined, w_low_ref[...]), dot_nt(d_joined, w_high_ref[...])], axis=1)
    d_normed = back_in_order(d_normed, order_ref[...])
    x = x_ref[...].astype(F32)
    inverse = lax.rsqrt(jnp.mean(x * x, axis=-1, keepdims=True) + EPSILON)
    input_grad_ref[...] = (d_resid_ref[...] + norm_back(x, inverse, gain_ref[...], d_normed)).astype(BF16)
    gain_grad_ref[...] = sum_rows(d_normed * x * inverse)
    bias_grad_ref[...] = sum_rows(d_joined.astype(F32))


def input_back(dq, terms, x, d_resid, weights, order, gain, cosine, sine):
    count, dim = x.shape
    joint = dq[0].shape[1] + 2 * LANES
    return call_whole(
        input_back_kernel,
        (*dq, *terms[0], *terms[1], x, d_resid, *weights, order, gain, cosine, sine),
        [
            jax.ShapeDtypeStruct((count, 2 * LANES), BF16),
            jax.ShapeDtypeStruct((count, dim), BF16),
            jax.ShapeDtypeStruct((1, dim), F32),
            jax.ShapeDtypeStruct((1, joint), F32),
        ],
        6 * count * dim * joint,
        "input_gradient",
    )


def seq_rows(seq, rows, cols):
    return pl.BlockSpec((rows, cols), lambda i: (seq, 0))


def piece_of(seq, rows):
    return pl.BlockSpec((1, rows, 2 * LANES), lambda i: (seq, 0, 0))


def keys_and_values(piece_refs):
    joint = jnp.concatenate([ref[0] for ref in piece_refs], axis=0)
    key, value = joint[:, :LANES], joint[:, LANES:]
    return (key, other_head(key)), (value, other_head(value))


def attend_kernel(block_ref, q_ref, kv_0, kv_1, kv_2, kv_3, start_ref, out_ref, level_ref):
    rows, width = q_ref.shape
    length = 4 * rows
    heads = width // HD
    group = heads // 2
    keys, values = keys_and_values((kv_0, kv_1, kv_2, kv_3))
    upper_key = lane_of((length, LANES)) >= HD
    upper = lane_of((rows, LANES)) >= HD
    query_at = block_ref[0] * rows + lax.broadcasted_iota(jnp.int32, (rows, length), 0)
    key_at = jnp.concatenate(
        [
            (block_ref[0] ^ place) * rows + lax.broadcasted_iota(jnp.int32, (rows, rows), 1)
            for place in range(4)
        ],
        axis=1,
    )
    allowed = (key_at <= query_at) & (key_at >= start_ref[:, :1])
    bias = jnp.where(allowed, 0.0, MASKED)
    one = jnp.ones((), BF16)
    lane = lane_of((rows, LANES))
    levels = jnp.zeros((rows, LANES), F32)
    for pair in range(heads // 2):
        at = slice(pair * LANES, (pair + 1) * LANES)
        both = q_ref[:, at]
        parts = []
        for place in range(2):
            owner = (2 * pair + place) // group
            moved = int(owner != place)
            side = upper if place else ~upper
            side_key = upper_key if place else ~upper_key
            query = jnp.where(side, both, jnp.zeros_like(both))
            score = dot_nt(query, keys[moved]) + bias
            top = jnp.max(score, axis=1, keepdims=True)
            weight = jnp.exp(score - top).astype(BF16)
            mixed = dot_nn(weight, jnp.where(side_key, values[moved], one))
            total = pltpu.roll(mixed, HD, 1)
            parts.append(mixed / total)
            level = top + jnp.log(total[:, place * HD : place * HD + 1])
            levels = jnp.where(lane == 2 * pair + place, level, levels)
        out_ref[:, at] = jnp.where(upper, parts[1], parts[0]).astype(BF16)
    level_ref[...] = levels


def attend(block, q, kv_pieces, start, rows, seq):
    width = q.shape[1]
    heads = width // HD
    return pl.pallas_call(
        attend_kernel,
        grid=(1,),
        in_specs=[
            pl.BlockSpec(memory_space=pltpu.SMEM),
            seq_rows(seq, rows, width),
            *[piece_of(seq, rows)] * 4,
            seq_rows(seq, rows, LANES),
        ],
        out_specs=[seq_rows(0, rows, width), seq_rows(0, rows, LANES)],
        out_shape=[jax.ShapeDtypeStruct((rows, width), BF16), jax.ShapeDtypeStruct((rows, LANES), F32)],
        compiler_params=pltpu.CompilerParams(vmem_limit_bytes=VMEM_LIMIT),
        cost_estimate=pl.CostEstimate(
            flops=32 * rows * rows * LANES * heads,
            bytes_accessed=4 * rows * width,
            transcendentals=4 * rows * rows * heads,
        ),
        name="attention_forward",
    )(block, q, *kv_pieces, start)


def attend_back_kernel(
    block_ref, q_ref, kv_0, kv_1, kv_2, kv_3, back_ref, out_ref, level_ref, start_ref, cos_ref, sin_ref,
    dq_ref, own_ref, core_ref, x_ref, far_ref, dk_sum, dv_sum,
):
    rows, width = q_ref.shape
    heads = width // HD
    group = heads // 2
    keys, values = keys_and_values((kv_0, kv_1, kv_2, kv_3))
    key_t = keys[0].astype(F32).T.astype(BF16)
    keys_t = (key_t, jnp.concatenate([key_t[HD:], key_t[:HD]], axis=0))
    upper = lane_of((rows, LANES)) >= HD
    upper_t = lax.broadcasted_iota(jnp.int32, (LANES, rows), 0) >= HD
    query_at = block_ref[0] * rows + lax.broadcasted_iota(jnp.int32, (rows, rows), 1)
    key_at = lax.broadcasted_iota(jnp.int32, (rows, rows), 0)
    biases = []
    for place in range(4):
        at = (block_ref[0] ^ place) * rows + key_at
        biases.append(jnp.where((at <= query_at) & (at >= start_ref[0, :1, :]), 0.0, MASKED))
    head_of = lax.broadcasted_iota(jnp.int32, (width, LANES), 0) // HD
    by_head = (head_of == lane_of((width, LANES))).astype(BF16)
    product = back_ref[...].astype(F32) * out_ref[...].astype(F32)
    product_high = product.astype(BF16)
    product_low = (product - product_high.astype(F32)).astype(BF16)
    row_sums = (dot_nn(product_high, by_head) + dot_nn(product_low, by_head)).T
    levels = level_ref[...].T
    cosine, sine = cos_ref[...], sin_ref[...]
    dk_sum[...] = jnp.zeros_like(dk_sum)
    dv_sum[...] = jnp.zeros_like(dv_sum)
    for pair in range(heads // 2):
        at = slice(pair * LANES, (pair + 1) * LANES)
        both = q_ref[:, at]
        back_both = back_ref[:, at]
        zero = jnp.zeros_like(both)
        sides = (~upper, upper)
        queries = [jnp.where(side, both, zero) for side in sides]
        backs = [jnp.where(side, back_both, zero) for side in sides]
        owners = [(2 * pair + place) // group for place in range(2)]
        d_query_t = [jnp.zeros((LANES, rows), F32) for _ in range(2)]
        for piece in range(4):
            span = slice(piece * rows, (piece + 1) * rows)
            probs, d_scores = [], []
            for place in range(2):
                head = 2 * pair + place
                moved = int(owners[place] != place)
                score = dot_nt(keys[moved][span], queries[place]) + biases[piece]
                prob = jnp.exp(score - levels[head : head + 1])
                d_prob = dot_nt(values[moved][span], backs[place])
                d_score = (prob * (d_prob - row_sums[head : head + 1])).astype(BF16)
                d_query_t[place] = d_query_t[place] + dot_nn(keys_t[moved][:, span], d_score)
                probs.append(prob.astype(BF16))
                d_scores.append(d_score)
            if owners[0] == owners[1]:
                dv_sum[owners[0], span] += dot_nn(
                    jnp.concatenate(probs, axis=1), jnp.concatenate(backs, axis=0)
                )
                dk_sum[owners[0], span] += dot_nn(
                    jnp.concatenate(d_scores, axis=1), jnp.concatenate(queries, axis=0)
                )
            else:
                for place in range(2):
                    dv_sum[owners[place], span] += dot_nn(probs[place], backs[place])
                    dk_sum[owners[place], span] += dot_nn(d_scores[place], queries[place])
        d_query = jnp.where(upper_t, d_query_t[1], d_query_t[0]).T * SCALE
        dq_ref[:, at] = (d_query * cosine - swap_halves(d_query) * sine).astype(BF16)
    lower_key = lane_of((4 * rows, LANES)) < HD
    for total, begin in ((dk_sum, 0), (dv_sum, LANES)):
        first, second = total[0], total[1]
        first = first + pltpu.roll(first, HD, 1)
        second = second + pltpu.roll(second, HD, 1)
        both = jnp.where(lower_key, first, second)
        cols = slice(begin, begin + LANES)
        own_ref[:, cols] = both[:rows]
        for place, ref in enumerate((core_ref, x_ref, far_ref)):
            ref[:, cols] = both[(place + 1) * rows : (place + 2) * rows].astype(BF16)


def parts_of(rows, cols):
    shapes = [jax.ShapeDtypeStruct((rows, cols), F32)] + [jax.ShapeDtypeStruct((rows, cols), BF16)] * 3
    return [seq_rows(0, rows, cols)] * 4, shapes


def attend_back(block, q, kv_pieces, back, out, level, start, cosine, sine, rows, seq):
    width = q.shape[1]
    length = 4 * rows
    heads = width // HD
    specs, shapes = parts_of(rows, 2 * LANES)
    return pl.pallas_call(
        attend_back_kernel,
        grid=(1,),
        in_specs=[
            pl.BlockSpec(memory_space=pltpu.SMEM),
            seq_rows(seq, rows, width),
            *[piece_of(seq, rows)] * 4,
            seq_rows(0, rows, width),
            seq_rows(0, rows, width),
            seq_rows(0, rows, LANES),
            pl.BlockSpec((1, 8, rows), lambda i: (seq, 0, 0)),
            seq_rows(seq, rows, LANES),
            seq_rows(seq, rows, LANES),
        ],
        out_specs=[seq_rows(0, rows, width), *specs],
        out_shape=[jax.ShapeDtypeStruct((rows, width), BF16), *shapes],
        scratch_shapes=[
            pltpu.VMEM((2, length, LANES), F32),
            pltpu.VMEM((2, length, LANES), F32),
        ],
        compiler_params=pltpu.CompilerParams(vmem_limit_bytes=VMEM_LIMIT),
        cost_estimate=pl.CostEstimate(
            flops=80 * rows * rows * LANES * heads,
            bytes_accessed=8 * rows * width,
            transcendentals=4 * rows * rows * heads,
        ),
        name="attention_backward",
    )(block, q, *kv_pieces, back, out, level, start, cosine, sine)


def mlp_kernel(
    n_0, n_1, n_2, n_3, c_0, c_1, c_2, c_3, w_ref,
    own_ref, out_1, out_2, out_3, d_own_ref, d_1, d_2, d_3, kept_ref, turned_ref,
    normed_all, cot_all,
):
    step = pl.program_id(0)
    rows = own_ref.shape[0]
    columns = w_ref.shape[1] // 3

    @pl.when(step == 0)
    def _():
        for place, (n_ref, c_ref) in enumerate(zip((n_0, n_1, n_2, n_3), (c_0, c_1, c_2, c_3))):
            normed_all[place // 2, (place % 2) * rows : (place % 2 + 1) * rows] = n_ref[...]
            cot_all[place // 2, (place % 2) * rows : (place % 2 + 1) * rows] = c_ref[...]

    normed, cot = normed_all[step], cot_all[step]
    for begin in range(0, columns, TILE):
        at = slice(begin, begin + TILE)
        gate = dot_nn(normed, w_ref[:, begin : begin + TILE])
        up = dot_nn(normed, w_ref[:, columns + begin : columns + begin + TILE])
        d_act = dot_nn(cot, w_ref[:, 2 * columns + begin : 2 * columns + begin + TILE])
        sigmoid = 0.5 * jnp.tanh(0.5 * gate) + 0.5
        swish = gate * sigmoid
        kept_ref[0, :, at] = (d_act * up * (sigmoid + swish * (1.0 - sigmoid))).astype(BF16)
        kept_ref[1, :, at] = (d_act * swish).astype(BF16)
        kept_ref[2, :, at] = (swish * up).astype(BF16)
    turned_ref[0] = normed.T
    turned_ref[1] = cot.T
    out = dot_nt(kept_ref[2], w_ref[:, 2 * columns :])
    d_normed = dot_nt(kept_ref[0], w_ref[:, :columns]) + dot_nt(kept_ref[1], w_ref[:, columns : 2 * columns])

    @pl.when(step == 0)
    def _():
        own_ref[...] = out[:rows]
        out_1[...] = out[rows:].astype(BF16)
        d_own_ref[...] = d_normed[:rows]
        d_1[...] = d_normed[rows:].astype(BF16)

    @pl.when(step == 1)
    def _():
        out_2[...] = out[:rows].astype(BF16)
        out_3[...] = out[rows:].astype(BF16)
        d_2[...] = d_normed[:rows].astype(BF16)
        d_3[...] = d_normed[rows:].astype(BF16)


def mlp(normed, cot, weights, seq):
    rows, dim = normed[0].shape
    columns = weights.shape[1] // 3
    specs, shapes = parts_of(rows, dim)
    once = lambda at: pl.BlockSpec((rows, dim), lambda i: (at, 0), pipeline_mode=pl.Buffered(1))
    return pl.pallas_call(
        mlp_kernel,
        grid=(2,),
        in_specs=[
            *[once(0)] * 4,
            *[once(seq)] * 3,
            once(0),
            pl.BlockSpec(weights.shape, lambda i: (0, 0), pipeline_mode=pl.Buffered(1)),
        ],
        out_specs=[
            *specs,
            *specs,
            pl.BlockSpec((3, 2 * rows, columns), lambda i: (0, i, 0)),
            pl.BlockSpec((2, dim, 2 * rows), lambda i: (0, 0, i)),
        ],
        out_shape=[
            *shapes,
            *shapes,
            jax.ShapeDtypeStruct((3, 4 * rows, columns), BF16),
            jax.ShapeDtypeStruct((2, dim, 4 * rows), BF16),
        ],
        scratch_shapes=[
            pltpu.VMEM((2, 2 * rows, dim), BF16),
            pltpu.VMEM((2, 2 * rows, dim), BF16),
        ],
        compiler_params=pltpu.CompilerParams(vmem_limit_bytes=VMEM_LIMIT),
        cost_estimate=pl.CostEstimate(
            flops=48 * rows * dim * columns,
            bytes_accessed=6 * dim * columns + 24 * rows * columns,
            transcendentals=4 * rows * columns,
        ),
        name="feed_forward",
    )(*normed, *cot, weights)


def mlp_grad_kernel(turned_0, turned_1, kept_0, kept_1, grad_ref):
    grad_ref[...] = (dot_nn(turned_0[0], kept_0[0]) + dot_nn(turned_1[0], kept_1[0])).astype(BF16)


def mlp_grad(turned, kept):
    _, dim, count = turned[0].shape
    columns = kept[0].shape[2]
    turned_block = pl.BlockSpec((1, dim, count), lambda i: (i // 2, 0, 0))
    kept_block = pl.BlockSpec((1, count, columns), lambda i: (i, 0, 0))
    return pl.pallas_call(
        mlp_grad_kernel,
        grid=(3,),
        in_specs=[turned_block, turned_block, kept_block, kept_block],
        out_specs=pl.BlockSpec((dim, columns), lambda i: (0, i)),
        out_shape=jax.ShapeDtypeStruct((dim, 3 * columns), BF16),
        compiler_params=pltpu.CompilerParams(vmem_limit_bytes=VMEM_LIMIT),
        cost_estimate=pl.CostEstimate(
            flops=12 * count * dim * columns,
            bytes_accessed=6 * dim * columns + 12 * count * columns,
            transcendentals=0,
        ),
        name="feed_forward_gradients",
    )(*turned, *kept)


def pack_kernel(block_ref, gate_ref, up_ref, down_ref, *refs):
    out_refs, scratch = refs[:4], refs[4]
    shard, ff = gate_ref.shape
    quarter = scratch.shape[2] // 4
    for place, ref in enumerate((gate_ref, up_ref, down_ref)):
        scratch[place, :, :ff] = ref[...].astype(F32)
        scratch[place, :, ff:] = jnp.zeros((shard, 4 * quarter - ff), F32)
    for place, out_ref in enumerate(out_refs):
        begin = pl.multiple_of((block_ref[0] ^ place) * quarter, LANES)
        for part in range(3):
            out_ref[:, part * quarter : (part + 1) * quarter] = scratch[part, :, pl.ds(begin, quarter)].astype(BF16)


def pack(block, gate, up, down_t, quarter):
    shard = gate.shape[0]
    return pl.pallas_call(
        pack_kernel,
        in_specs=[pl.BlockSpec(memory_space=pltpu.SMEM)] + [pl.BlockSpec(memory_space=pltpu.VMEM)] * 3,
        out_specs=[pl.BlockSpec(memory_space=pltpu.VMEM)] * 4,
        out_shape=[jax.ShapeDtypeStruct((shard, 3 * quarter), BF16)] * 4,
        scratch_shapes=[pltpu.VMEM((3, shard, 4 * quarter), F32)],
        compiler_params=pltpu.CompilerParams(vmem_limit_bytes=VMEM_LIMIT),
        name="pack_columns",
    )(block, gate, up, down_t)


def pick(options, index):
    value = options[0]
    for place in range(1, len(options)):
        value = jnp.where(index == place, options[place], value)
    return value


def assemble_kernel(block_ref, *refs):
    pieces, out_ref, scratch = refs[:4], refs[4], refs[5]
    shard = pieces[0].shape[0]
    values = [ref[...].astype(F32) for ref in pieces]
    for owner in range(4):
        scratch[owner * shard : (owner + 1) * shard] = pick(values, block_ref[0] ^ owner)
    out_ref[...] = scratch[...].astype(BF16)


def assemble(block, pieces):
    shard, columns = pieces[0].shape
    return pl.pallas_call(
        assemble_kernel,
        in_specs=[pl.BlockSpec(memory_space=pltpu.SMEM)] + [pl.BlockSpec(memory_space=pltpu.VMEM)] * 4,
        out_specs=pl.BlockSpec(memory_space=pltpu.VMEM),
        out_shape=jax.ShapeDtypeStruct((4 * shard, columns), BF16),
        scratch_shapes=[pltpu.VMEM((4 * shard, columns), F32)],
        compiler_params=pltpu.CompilerParams(vmem_limit_bytes=VMEM_LIMIT),
        name="assemble_rows",
    )(block, *pieces)


def cut_kernel(block_ref, value_ref, *refs):
    out_refs, scratch = refs[:4], refs[4]
    shard = out_refs[0].shape[0]
    scratch[...] = value_ref[...].astype(F32)
    values = [scratch[owner * shard : (owner + 1) * shard] for owner in range(4)]
    for place, out_ref in enumerate(out_refs):
        out_ref[...] = pick(values, block_ref[0] ^ place).astype(BF16)


def cut(block, value):
    shard, columns = value.shape[0] // 4, value.shape[1]
    return pl.pallas_call(
        cut_kernel,
        in_specs=[pl.BlockSpec(memory_space=pltpu.SMEM), pl.BlockSpec(memory_space=pltpu.VMEM)],
        out_specs=[pl.BlockSpec(memory_space=pltpu.VMEM)] * 4,
        out_shape=[jax.ShapeDtypeStruct((shard, columns), BF16)] * 4,
        scratch_shapes=[pltpu.VMEM(value.shape, F32)],
        compiler_params=pltpu.CompilerParams(vmem_limit_bytes=VMEM_LIMIT),
        name="cut_rows",
    )(block, value)


def unpack_kernel(block_ref, *refs):
    pieces, out_refs, scratch = refs[:4], refs[4:7], refs[7]
    ff = out_refs[0].shape[1]
    quarter = scratch.shape[2] // 4
    for place, ref in enumerate(pieces):
        begin = pl.multiple_of((block_ref[0] ^ place) * quarter, LANES)
        for part in range(3):
            scratch[part, :, pl.ds(begin, quarter)] = ref[:, part * quarter : (part + 1) * quarter].astype(F32)
    for part, out_ref in enumerate(out_refs):
        out_ref[...] = scratch[part, :, :ff]


def unpack(block, pieces, ff):
    shard, columns = pieces[0].shape
    return pl.pallas_call(
        unpack_kernel,
        in_specs=[pl.BlockSpec(memory_space=pltpu.SMEM)] + [pl.BlockSpec(memory_space=pltpu.VMEM)] * 4,
        out_specs=[pl.BlockSpec(memory_space=pltpu.VMEM)] * 3,
        out_shape=[jax.ShapeDtypeStruct((shard, ff), F32)] * 3,
        scratch_shapes=[pltpu.VMEM((3, shard, columns // 3 * 4), F32)],
        compiler_params=pltpu.CompilerParams(vmem_limit_bytes=VMEM_LIMIT),
        name="unpack_columns",
    )(block, *pieces)


def bit_swap(value, axis, bit=0):
    size = lax.axis_size(axis)
    return lax.ppermute(value, axis, [(i, i ^ (1 << bit)) for i in range(size)])


def jump_swap(value, axes, jump):
    return lax.ppermute(value, axes, [(i, i ^ jump) for i in range(4)])


def to_plane(value, slot):
    high, low = slot >> 1, slot & 1
    pairs = [
        (4 * y + 2 * x + c, 4 * (c ^ low) + 2 * (x ^ high) + y) for y in range(2) for x in range(2) for c in range(2)
    ]
    return lax.ppermute(value, TOKENS + ("cc",), pairs)


def from_plane(value, slot):
    high, low = slot >> 1, slot & 1
    pairs = [
        (4 * y + 2 * x + c, 4 * c + 2 * (x ^ high) + (y ^ low)) for y in range(2) for x in range(2) for c in range(2)
    ]
    return lax.ppermute(value, TOKENS + ("cc",), pairs)


def after(first, *values):
    return lax.optimization_barrier((first, *values))


def gather_four(value, axes):
    from_first = bit_swap(value, axes[0])
    return [value, bit_swap(value, axes[1]), from_first, bit_swap(from_first, axes[1])]


def gather_direct(value, axes):
    return [value] + [jump_swap(value, axes, jump) for jump in range(1, 4)]


def sum_direct(axes, own, *away):
    return [own] + [jump_swap(value, axes, jump + 1) for jump, value in enumerate(away)]


def doubling_offsets(steps):
    weight = {"cc": 1, "cx": 2, "fy": 4, "fz": 8}
    offsets = [0]
    for axis, bit in steps:
        offsets += [offset ^ (weight[axis] << bit) for offset in offsets]
    return jnp.array(offsets, jnp.int32)


def double(value, axis, bit=0):
    return jnp.concatenate([value, bit_swap(value, axis, bit)], axis=0)


def plane_gather(value):
    return jnp.concatenate(gather_direct(value, TOKENS), axis=0)


def plane_sum(value):
    parts = jnp.split(value, 4, axis=0)
    terms = sum_direct(TOKENS, *parts)
    return sum(term.astype(F32) for term in terms).astype(BF16)


def halve(value, axis, bit=0):
    middle = value.shape[0] // 2
    came = bit_swap(value[middle:], axis, bit)
    return (value[:middle].astype(F32) + came.astype(F32)).astype(BF16)


def on_device(
    hidden,
    segments,
    attn_gain,
    qkv_weight,
    qkv_bias,
    out_weight,
    mlp_gain,
    gate_weight,
    up_weight,
    down_weight,
    cotangent,
):
    seqs, rows, dim = hidden.shape
    count = seqs * rows
    shard = attn_gain.shape[0]
    world = dim // shard
    joint = qkv_weight.shape[1]
    width = joint - 2 * LANES
    ff = gate_weight.shape[1]
    block = lax.axis_index("cx") * lax.axis_size("cc") + lax.axis_index("cc")
    me = lax.axis_index(FSDP) * lax.axis_size(CTX) + block
    offset = block * rows
    block_arg = block.reshape(1).astype(jnp.int32)
    plane_arg = (lax.axis_index("cx") * 2 + lax.axis_index("fy")).reshape(1).astype(jnp.int32)
    x = hidden.reshape(count, dim)
    cot = cotangent.reshape(count, dim)

    cot_x, cot_y = bit_swap(cot, "cx"), bit_swap(cot, "fy")

    far = [("fz", bit) for bit in reversed(range((lax.axis_size("fz")).bit_length() - 1))]
    padded = -(-(shard + 1) // 16) * 16
    small = jnp.concatenate([attn_gain, mlp_gain, qkv_bias])
    small_row = jnp.pad(small, (0, joint + width - small.shape[0]))[None]
    first = jnp.concatenate(
        [
            jnp.concatenate([qkv_weight, out_weight.T], axis=1),
            small_row,
            jnp.zeros((padded - shard - 1, joint + width), BF16),
        ],
        axis=0,
    )
    first = double(first, *far[0])

    quarter = -(-ff // (4 * TILE)) * TILE
    first, *pieces = after(first, *pack(block_arg, gate_weight, up_weight, down_weight.T, quarter))
    pieces = [to_plane(piece, slot) for slot, piece in enumerate(pieces)]
    for axis, bit in far[1:]:
        first = double(first, axis, bit)

    within = jnp.arange(padded, dtype=jnp.int32)
    owner = me ^ doubling_offsets(far + [("cx", 0), ("fy", 0), ("cc", 0)])
    target = jnp.where(within[None, :] < shard, owner[:, None] * shard + within[None, :], -1).reshape(1, -1)
    order = (jnp.arange(dim, dtype=jnp.int32)[:, None] == target).astype(BF16)
    place = jnp.where(within[None, :] == shard, owner[:, None], -1).reshape(1, -1)
    spread = (jnp.arange(world, dtype=jnp.int32)[:, None] == place).astype(BF16)

    at_row = lax.dynamic_slice_in_dim(segments, offset, rows, axis=1)
    zeros_before = jnp.sum((segments < 1).astype(jnp.int32), axis=1, keepdims=True)
    ones_before = jnp.sum((segments < 2).astype(jnp.int32), axis=1, keepdims=True)
    start = jnp.where(at_row == 0, 0, jnp.where(at_row == 1, zeros_before, ones_before))
    position = (offset + jnp.arange(rows, dtype=jnp.int32)[None, :] - start).reshape(count)
    lane = jnp.arange(LANES, dtype=jnp.int32)
    frequency = ROPE_BASE ** (-(lane % (HD // 2)).astype(F32) * 2.0 / HD)
    angle = position.astype(F32)[:, None] * frequency[None, :]
    cosine = jnp.cos(angle)
    sine = jnp.where(lane % HD < HD // 2, -1.0, 1.0)[None, :] * jnp.sin(angle)
    start_column = jnp.broadcast_to(start.reshape(count, 1), (count, LANES))
    start_row = jnp.broadcast_to(start[:, None, :], (seqs, 8, rows))

    first, cot_x, cot_y, order, spread, cosine, sine, start_column, *pieces = after(
        first, cot_x, cot_y, order, spread, cosine, sine, start_column, *pieces
    )
    w_joint = plane_gather(first[:, :joint])
    mlp_shard = assemble(plane_arg, pieces)
    mlp_weights = lax.all_gather(mlp_shard, WEIGHTS, axis=0, tiled=True)
    w_joint, far_0, far_1 = after(w_joint, cot_x[:rows], cot_y[rows:])
    w_joint = (w_joint, bit_swap(w_joint, "cc"))
    cot_far = [bit_swap(far_0, "fy"), bit_swap(far_1, "cx")]

    normed, q, kv, gain_attn, gain_mlp = prep(x, order, spread, w_joint, cosine, sine, rows)
    kv_all = gather_four(kv.reshape(seqs, rows, 2 * LANES), CTX)
    kv_all[3], out_rows = after(kv_all[3], first[:, joint:])
    w_out = plane_gather(out_rows)
    attended, levels, resid, normed_all = [], [], [], []
    for seq in range(seqs):
        turn = block_arg if seq == 0 else after(resid[0], block_arg)[1]
        attended_one, level_one = attend(turn, q, kv_all, start_column, rows, seq)
        if seq == 0:
            attended_one, w_out = after(attended_one, w_out)
            w_out = (w_out, bit_swap(w_out, "cc"))
        else:
            attended_one, *cot_far = after(attended_one, *cot_far)
        attended.append(attended_one)
        levels.append(level_one)
        resid_one, normed_one = project_out(attended[seq], x, w_out, order, gain_mlp, rows, seq)
        resid.append(resid_one)
        normed_all.append(gather_direct(normed_one, TOKENS))

    out_parts, d_terms, kept, turned = [], [], [], []
    for seq in range(seqs):
        if seq == 1:
            out_parts[0], normed_all[1] = lax.optimization_barrier((out_parts[0], normed_all[1]))
        result = mlp(normed_all[seq], [cot, cot_x, cot_y, cot_far[seq]], mlp_weights, seq)
        out_parts.append(result[:4])
        d_terms.append(sum_direct(TOKENS, *result[4:8]))
        kept.append(result[8])
        turned.append(result[9])
    d_resid, d_branch, d_attended, mlp_gain_grad, dq, dkv_terms, out_terms = [], [], [], [], [], [], []
    for seq in range(seqs):
        if seq == 0:
            _, *d_terms[0] = after(kept[1], *d_terms[0])
        else:
            dq[0], d_terms[1][0], *out_terms[0] = after(dq[0], d_terms[1][0], *out_terms[0])
        result = project_out_back(d_terms[seq], resid[seq], cot, w_out, order, gain_mlp, rows, seq)
        for place, value in zip((d_resid, d_branch, d_attended, mlp_gain_grad), result):
            place.append(value)
        out_terms.append(sum_direct(TOKENS, *after(d_terms[seq][1], *out_parts[seq])[1:]))
        if seq == 0:
            _, turned[1] = after(d_resid[0], turned[1])
            grads = mlp_grad(turned, kept)
            grads, d_attended[0], *d_terms[1] = after(grads, d_attended[0], *d_terms[1])
            grads = lax.psum_scatter(
                grads.reshape(world // 4, 4 * shard, 3 * quarter), WEIGHTS, scatter_dimension=0, tiled=False
            )
        else:
            out_grad = dot_tn(jnp.concatenate(d_branch, axis=0), jnp.concatenate(attended, axis=0)).astype(BF16)
            out_grad = halve(out_grad, "cc")
            d_attended[1], *dkv_terms[0] = after(d_attended[1], *dkv_terms[0])
        result = attend_back(
            block_arg, q, kv_all, d_attended[seq], attended[seq], levels[seq], start_row, cosine, sine, rows, seq
        )
        dq.append(result[0])
        dkv_terms.append(sum_direct(CTX, *result[1:]))
    dq[1], out_grad, *out_terms[1] = after(dq[1], out_grad, *out_terms[1])
    q_grad = dot_tn(normed, jnp.concatenate(dq, axis=0)).astype(BF16)
    q_grad = halve(q_grad, "cc")
    q_grad, *dkv_terms[1] = after(q_grad, *dkv_terms[1])
    q_grad = plane_sum(q_grad)
    d_resid = jnp.concatenate(d_resid, axis=0)
    d_kv, input_grad, attn_gain_grad, bias_grad = input_back(
        dq, dkv_terms, x, d_resid, w_joint, order, gain_attn, cosine, sine
    )
    d_kv, q_grad = after(d_kv, q_grad)

    output = []
    for seq in range(seqs):
        own, *away = out_terms[seq]
        output.append((resid[seq] + own + sum(term.astype(F32) for term in away)).astype(BF16))

    split_at = width + LANES
    bias_grad = bias_grad[0]
    small_grads = jnp.concatenate(
        [
            attn_gain_grad.reshape(world, -1),
            sum(mlp_gain_grad).reshape(world, -1),
            bias_grad[:split_at].reshape(world, -1),
            bias_grad[split_at:].reshape(world, -1),
        ],
        axis=1,
    ).astype(BF16)
    small_count = small_grads.shape[1]
    small_grads = jnp.pad(small_grads, ((0, 0), (0, 2 * LANES - small_count)))
    kv_grad = dot_tn(
        jnp.concatenate([normed, spread], axis=0), jnp.concatenate([d_kv, small_grads], axis=0)
    ).astype(BF16)
    pieces = cut(plane_arg, lax.optimization_barrier(grads))
    kv_grad, *pieces = after(halve(kv_grad, "cc"), *pieces)
    pieces = [from_plane(piece, slot) for slot, piece in enumerate(pieces)]
    kv_grad, out_grad = plane_sum(kv_grad), plane_sum(out_grad)
    first_sum = jnp.concatenate([q_grad, kv_grad, out_grad], axis=1)
    for axis, bit in reversed(far):
        first_sum = halve(first_sum, axis, bit)
    gate_grad, up_grad, down_grad_t = unpack(block_arg, pieces, ff)
    first_sum = first_sum.astype(F32)
    qkv_sum, out_sum = first_sum[:, :joint], first_sum[:, joint:]
    small_sum = qkv_sum[shard, width : width + small_count]
    at = (shard, 2 * shard, 2 * shard + split_at // world)

    return (
        jnp.stack(output),
        input_grad.reshape(hidden.shape),
        small_sum[: at[0]],
        qkv_sum[:shard],
        small_sum[at[1] : at[2]],
        small_sum[at[2] :],
        out_sum[:shard].T,
        small_sum[at[0] : at[1]],
        gate_grad,
        up_grad,
        down_grad_t.T,
    )


def solution(mesh):
    fsdp, ctx = mesh.shape["fsdp"], mesh.shape["ctx"]
    inner = Mesh(mesh.devices.reshape(fsdp // 2, 2, 2, ctx // 2), AXES)
    tokens = P(FSDP, CTX, None)
    vector = P(AXES)
    by_row = P(AXES, None)
    by_column = P(None, AXES)
    return jax.shard_map(
        on_device,
        mesh=inner,
        in_specs=(
            tokens,
            P(FSDP, None),
            vector,
            by_row,
            vector,
            by_column,
            vector,
            by_row,
            by_row,
            by_column,
            tokens,
        ),
        out_specs=(
            tokens,
            tokens,
            vector,
            by_row,
            vector,
            vector,
            by_column,
            vector,
            by_row,
            by_row,
            by_column,
        ),
        check_vma=False,
    )
```

```python
import functools

import jax
import jax.numpy as jnp
from jax import lax
from jax.experimental import pallas as pl
from jax.experimental.pallas import tpu as pltpu
from jax.sharding import Mesh
from jax.sharding import PartitionSpec as P

HD = 64
LANES = 128
EPSILON = 1e-06
ROPE_BASE = 1000000.0
MASKED = -1e30
SCALE = HD ** (-0.5)
TILE = 256
MIB = 1 << 20
VMEM_LIMIT = 60 * MIB
F32 = jnp.float32
BF16 = jnp.bfloat16
AXES = ("fz", "fy", "cx", "cc")
FSDP = ("fz", "fy")
CTX = ("cx", "cc")
TOKENS = ("fy", "cx")
WEIGHTS = ("fz", "cc")


def dot_nn(a, b):
    return lax.dot_general(a, b, (((1,), (0,)), ((), ())), preferred_element_type=F32)


def dot_nt(a, b):
    return lax.dot_general(a, b, (((1,), (1,)), ((), ())), preferred_element_type=F32)


def dot_tn(a, b):
    return lax.dot_general(a, b, (((0,), (0,)), ((), ())), preferred_element_type=F32)


def lane_of(shape):
    return lax.broadcasted_iota(jnp.int32, shape, len(shape) - 1)


def swap_halves(block):
    lead = lane_of(block.shape) % HD < HD // 2
    return jnp.where(
        lead, pltpu.roll(block, LANES - HD // 2, 1), pltpu.roll(block, HD // 2, 1)
    )


def other_head(block):
    return jnp.concatenate([block[:, HD:], block[:, :HD]], axis=1)


def read_out(extras, first, piece, total):
    owners, columns = extras.shape
    at = lax.broadcasted_iota(jnp.int32, (columns, total), 1) % piece + first
    chosen = (lax.broadcasted_iota(jnp.int32, (columns, total), 0) == at).astype(BF16)
    spread = dot_nn(extras, chosen)
    owner = lax.broadcasted_iota(jnp.int32, (owners, total), 1) // piece
    mine = owner == lax.broadcasted_iota(jnp.int32, (owners, total), 0)
    return jnp.sum(jnp.where(mine, spread, 0.0), axis=0, keepdims=True)


def prep_kernel(
    x_ref, order_ref, spread_ref, w_low_ref, w_high_ref, cos_ref, sin_ref,
    normed_low_ref, normed_high_ref, q_ref, kv_ref, gain_ref, gain_mlp_ref, bias_ref,
):
    x = x_ref[...].astype(F32)
    dim = x.shape[1]
    width = q_ref.shape[1]
    joint = w_low_ref.shape[1]
    middle = w_low_ref.shape[0]
    owners = spread_ref.shape[0]

    @pl.when(pl.program_id(0) == 0)
    def _():
        extras = dot_nn(spread_ref[:, :middle], w_low_ref[:, :LANES])
        extras = (extras + dot_nn(spread_ref[:, middle:], w_high_ref[:, :LANES])).astype(BF16)
        shard = dim // owners
        gain_ref[...] = read_out(extras, 0, shard, dim)
        gain_mlp_ref[...] = read_out(extras, shard, shard, dim)
        bias_ref[...] = read_out(extras, 2 * shard, joint // owners, joint)

    gain, bias = gain_ref[...], bias_ref[...]
    inverse = lax.rsqrt(jnp.mean(x * x, axis=-1, keepdims=True) + EPSILON)
    normed = (x * inverse * gain).astype(BF16)
    ordered = dot_nn(normed, order_ref[...]).astype(BF16)
    normed_low_ref[...] = ordered[:, :middle]
    normed_high_ref[...] = ordered[:, middle:]
    joined = dot_nn(ordered[:, :middle], w_low_ref[...])
    joined = joined + dot_nn(ordered[:, middle:], w_high_ref[...]) + bias
    cosine, sine = cos_ref[...], sin_ref[...]
    for begin in range(0, width + LANES, LANES):
        block = joined[:, begin : begin + LANES]
        turned = block * cosine + swap_halves(block) * sine
        if begin < width:
            q_ref[:, begin : begin + LANES] = (turned * SCALE).astype(BF16)
        else:
            kv_ref[:, :LANES] = turned.astype(BF16)
    kv_ref[:, LANES:] = joined[:, width + LANES :].astype(BF16)


def rows_of(rows, cols):
    return pl.BlockSpec((rows, cols), lambda i: (i, 0))


def whole(value):
    return pl.BlockSpec(value.shape, lambda i: (0,) * value.ndim)


def prep(x, order, spread, weights, cosine, sine, rows):
    count, dim = x.shape
    ordered = order.shape[1]
    joint = weights[0].shape[1]
    width = joint - 2 * LANES
    row = pl.BlockSpec((1, dim), lambda i: (0, 0))
    return pl.pallas_call(
        prep_kernel,
        grid=(count // rows,),
        in_specs=[
            rows_of(rows, dim),
            whole(order),
            whole(spread),
            whole(weights[0]),
            whole(weights[1]),
            rows_of(rows, LANES),
            rows_of(rows, LANES),
        ],
        out_specs=[
            rows_of(rows, ordered // 2),
            rows_of(rows, ordered // 2),
            rows_of(rows, width),
            rows_of(rows, 2 * LANES),
            row,
            row,
        ],
        out_shape=[
            jax.ShapeDtypeStruct((count, ordered // 2), BF16),
            jax.ShapeDtypeStruct((count, ordered // 2), BF16),
            jax.ShapeDtypeStruct((count, width), BF16),
            jax.ShapeDtypeStruct((count, 2 * LANES), BF16),
            jax.ShapeDtypeStruct((1, dim), F32),
            jax.ShapeDtypeStruct((1, dim), F32),
        ],
        scratch_shapes=[pltpu.VMEM((1, joint), F32)],
        compiler_params=pltpu.CompilerParams(vmem_limit_bytes=VMEM_LIMIT),
        cost_estimate=pl.CostEstimate(
            flops=2 * count * ordered * (joint + dim), bytes_accessed=12 * MIB, transcendentals=0
        ),
        name="norm_project_rotate",
    )(x, order, spread, weights[0], weights[1], cosine, sine)


def back_in_order(value, order):
    high = value.astype(BF16)
    low = (value - high.astype(F32)).astype(BF16)
    return dot_nt(high, order) + dot_nt(low, order)


def out_kernel(attended_ref, x_ref, w_low_ref, w_high_ref, order_ref, gain_ref, resid_ref, normed_ref):
    attended = attended_ref[...]
    branch = jnp.concatenate([dot_nt(attended, w_low_ref[...]), dot_nt(attended, w_high_ref[...])], axis=1)
    resid = x_ref[...].astype(F32) + back_in_order(branch, order_ref[...])
    inverse = lax.rsqrt(jnp.mean(resid * resid, axis=-1, keepdims=True) + EPSILON)
    resid_ref[...] = resid
    normed_ref[...] = (resid * inverse * gain_ref[...]).astype(BF16)


def project_out(attended, x, weights, order, gain, rows, seq):
    dim = x.shape[1]
    count = rows
    return pl.pallas_call(
        out_kernel,
        grid=(1,),
        in_specs=[
            rows_of(rows, attended.shape[1]),
            pl.BlockSpec((rows, dim), lambda i: (seq, 0)),
            whole(weights[0]),
            whole(weights[1]),
            whole(order),
            whole(gain),
        ],
        out_specs=[rows_of(rows, dim), rows_of(rows, dim)],
        out_shape=[jax.ShapeDtypeStruct((count, dim), F32), jax.ShapeDtypeStruct((count, dim), BF16)],
        compiler_params=pltpu.CompilerParams(vmem_limit_bytes=VMEM_LIMIT),
        cost_estimate=pl.CostEstimate(flops=6 * count * dim * dim, bytes_accessed=8 * MIB, transcendentals=0),
        name="project_out_norm",
    )(attended, x, weights[0], weights[1], order, gain)


def sum_rows(value):
    return jnp.sum(value, axis=0, keepdims=True)


def norm_back(values, inverse, gain, incoming):
    scaled = incoming * gain
    mean_term = jnp.mean(scaled * values, axis=-1, keepdims=True)
    return inverse * scaled - values * inverse**3 * mean_term


def total_of(own_ref, *away_refs):
    total = own_ref[...]
    for ref in away_refs:
        total = total + ref[...].astype(F32)
    return total


def out_back_kernel(
    own_ref, core_ref, x_ref, far_ref, resid_ref, cot_ref, w_low_ref, w_high_ref, order_ref, gain_ref,
    d_resid_ref, d_low_ref, d_high_ref, d_attended_ref, gain_grad_ref,
):
    middle = w_low_ref.shape[0]
    d_normed = total_of(own_ref, core_ref, x_ref, far_ref)
    resid = resid_ref[...]
    inverse = lax.rsqrt(jnp.mean(resid * resid, axis=-1, keepdims=True) + EPSILON)
    d_resid = cot_ref[...].astype(F32) + norm_back(resid, inverse, gain_ref[...], d_normed)
    d_resid_ref[...] = d_resid
    d_branch = dot_nn(d_resid.astype(BF16), order_ref[...]).astype(BF16)
    d_low_ref[...] = d_branch[:, :middle]
    d_high_ref[...] = d_branch[:, middle:]
    d_attended = dot_nn(d_branch[:, :middle], w_low_ref[...])
    d_attended = d_attended + dot_nn(d_branch[:, middle:], w_high_ref[...])
    d_attended_ref[...] = d_attended.astype(BF16)
    gain_grad_ref[...] = sum_rows(d_normed * resid * inverse)


def project_out_back(terms, resid, cot, weights, order, gain, rows, seq):
    count, dim = resid.shape
    ordered = order.shape[1]
    width = dim
    return pl.pallas_call(
        out_back_kernel,
        grid=(1,),
        in_specs=[
            rows_of(rows, dim),
            rows_of(rows, dim),
            rows_of(rows, dim),
            rows_of(rows, dim),
            rows_of(rows, dim),
            pl.BlockSpec((rows, dim), lambda i: (seq, 0)),
            whole(weights[0]),
            whole(weights[1]),
            whole(order),
            whole(gain),
        ],
        out_specs=[
            rows_of(rows, dim),
            rows_of(rows, ordered // 2),
            rows_of(rows, ordered // 2),
            rows_of(rows, width),
            pl.BlockSpec((1, dim), lambda i: (0, 0)),
        ],
        out_shape=[
            jax.ShapeDtypeStruct((count, dim), F32),
            jax.ShapeDtypeStruct((count, ordered // 2), BF16),
            jax.ShapeDtypeStruct((count, ordered // 2), BF16),
            jax.ShapeDtypeStruct((count, width), BF16),
            jax.ShapeDtypeStruct((1, dim), F32),
        ],
        compiler_params=pltpu.CompilerParams(vmem_limit_bytes=VMEM_LIMIT),
        cost_estimate=pl.CostEstimate(flops=4 * count * dim * dim, bytes_accessed=12 * MIB, transcendentals=0),
        name="norm_back_project",
    )(*terms, resid, cot, weights[0], weights[1], order, gain)


def call_whole(kernel, operands, out_shape, flops, name):
    return pl.pallas_call(
        kernel,
        in_specs=[pl.BlockSpec(memory_space=pltpu.VMEM)] * len(operands),
        out_specs=[pl.BlockSpec(memory_space=pltpu.VMEM)] * len(out_shape),
        out_shape=out_shape,
        compiler_params=pltpu.CompilerParams(vmem_limit_bytes=VMEM_LIMIT),
        cost_estimate=pl.CostEstimate(flops=flops, bytes_accessed=16 * MIB, transcendentals=0),
        name=name,
    )(*operands)


def input_back_kernel(*refs):
    dqs, terms = refs[:2], refs[2:10]
    x_ref, d_resid_ref, w_low_ref, w_high_ref, order_ref, gain_ref, cos_ref, sin_ref = refs[10:18]
    d_kv_ref, input_grad_ref, gain_grad_ref, bias_grad_ref = refs[18:]
    dkv = jnp.concatenate([total_of(*terms[:4]), total_of(*terms[4:])], axis=0)
    dk = dkv[:, :LANES]
    dk = dk * cos_ref[...] - swap_halves(dk) * sin_ref[...]
    d_kv = jnp.concatenate([dk.astype(BF16), dkv[:, LANES:].astype(BF16)], axis=1)
    d_kv_ref[...] = d_kv
    dq = jnp.concatenate([ref[...] for ref in dqs], axis=0)
    d_joined = jnp.concatenate([dq, d_kv], axis=1)
    d_normed = jnp.concatenate([dot_nt(d_joined, w_low_ref[...]), dot_nt(d_joined, w_high_ref[...])], axis=1)
    d_normed = back_in_order(d_normed, order_ref[...])
    x = x_ref[...].astype(F32)
    inverse = lax.rsqrt(jnp.mean(x * x, axis=-1, keepdims=True) + EPSILON)
    input_grad_ref[...] = (d_resid_ref[...] + norm_back(x, inverse, gain_ref[...], d_normed)).astype(BF16)
    gain_grad_ref[...] = sum_rows(d_normed * x * inverse)
    bias_grad_ref[...] = sum_rows(d_joined.astype(F32))


def input_back(dq, terms, x, d_resid, weights, order, gain, cosine, sine):
    count, dim = x.shape
    joint = dq[0].shape[1] + 2 * LANES
    return call_whole(
        input_back_kernel,
        (*dq, *terms[0], *terms[1], x, d_resid, *weights, order, gain, cosine, sine),
        [
            jax.ShapeDtypeStruct((count, 2 * LANES), BF16),
            jax.ShapeDtypeStruct((count, dim), BF16),
            jax.ShapeDtypeStruct((1, dim), F32),
            jax.ShapeDtypeStruct((1, joint), F32),
        ],
        6 * count * dim * joint,
        "input_gradient",
    )


def seq_rows(seq, rows, cols):
    return pl.BlockSpec((rows, cols), lambda i: (seq, 0))


def piece_of(seq, rows):
    return pl.BlockSpec((1, rows, 2 * LANES), lambda i: (seq, 0, 0))


def keys_and_values(piece_refs):
    joint = jnp.concatenate([ref[0] for ref in piece_refs], axis=0)
    key, value = joint[:, :LANES], joint[:, LANES:]
    return (key, other_head(key)), (value, other_head(value))


def attend_kernel(block_ref, q_ref, kv_0, kv_1, kv_2, kv_3, start_ref, out_ref, level_ref):
    rows, width = q_ref.shape
    length = 4 * rows
    heads = width // HD
    group = heads // 2
    keys, values = keys_and_values((kv_0, kv_1, kv_2, kv_3))
    upper_key = lane_of((length, LANES)) >= HD
    upper = lane_of((rows, LANES)) >= HD
    query_at = block_ref[0] * rows + lax.broadcasted_iota(jnp.int32, (rows, length), 0)
    key_at = jnp.concatenate(
        [
            (block_ref[0] ^ place) * rows + lax.broadcasted_iota(jnp.int32, (rows, rows), 1)
            for place in range(4)
        ],
        axis=1,
    )
    allowed = (key_at <= query_at) & (key_at >= start_ref[:, :1])
    bias = jnp.where(allowed, 0.0, MASKED)
    one = jnp.ones((), BF16)
    lane = lane_of((rows, LANES))
    levels = jnp.zeros((rows, LANES), F32)
    for pair in range(heads // 2):
        at = slice(pair * LANES, (pair + 1) * LANES)
        both = q_ref[:, at]
        parts = []
        for place in range(2):
            owner = (2 * pair + place) // group
            moved = int(owner != place)
            side = upper if place else ~upper
            side_key = upper_key if place else ~upper_key
            query = jnp.where(side, both, jnp.zeros_like(both))
            score = dot_nt(query, keys[moved]) + bias
            top = jnp.max(score, axis=1, keepdims=True)
            weight = jnp.exp(score - top).astype(BF16)
            mixed = dot_nn(weight, jnp.where(side_key, values[moved], one))
            total = pltpu.roll(mixed, HD, 1)
            parts.append(mixed / total)
            level = top + jnp.log(total[:, place * HD : place * HD + 1])
            levels = jnp.where(lane == 2 * pair + place, level, levels)
        out_ref[:, at] = jnp.where(upper, parts[1], parts[0]).astype(BF16)
    level_ref[...] = levels


def attend(block, q, kv_pieces, start, rows, seq):
    width = q.shape[1]
    heads = width // HD
    return pl.pallas_call(
        attend_kernel,
        grid=(1,),
        in_specs=[
            pl.BlockSpec(memory_space=pltpu.SMEM),
            seq_rows(seq, rows, width),
            *[piece_of(seq, rows)] * 4,
            seq_rows(seq, rows, LANES),
        ],
        out_specs=[seq_rows(0, rows, width), seq_rows(0, rows, LANES)],
        out_shape=[jax.ShapeDtypeStruct((rows, width), BF16), jax.ShapeDtypeStruct((rows, LANES), F32)],
        compiler_params=pltpu.CompilerParams(vmem_limit_bytes=VMEM_LIMIT),
        cost_estimate=pl.CostEstimate(
            flops=32 * rows * rows * LANES * heads,
            bytes_accessed=4 * rows * width,
            transcendentals=4 * rows * rows * heads,
        ),
        name="attention_forward",
    )(block, q, *kv_pieces, start)


def attend_back_kernel(
    block_ref, q_ref, kv_0, kv_1, kv_2, kv_3, back_ref, out_ref, level_ref, start_ref, cos_ref, sin_ref,
    dq_ref, own_ref, core_ref, x_ref, far_ref, dk_sum, dv_sum,
):
    rows, width = q_ref.shape
    heads = width // HD
    group = heads // 2
    keys, values = keys_and_values((kv_0, kv_1, kv_2, kv_3))
    key_t = keys[0].astype(F32).T.astype(BF16)
    keys_t = (key_t, jnp.concatenate([key_t[HD:], key_t[:HD]], axis=0))
    upper = lane_of((rows, LANES)) >= HD
    upper_t = lax.broadcasted_iota(jnp.int32, (LANES, rows), 0) >= HD
    query_at = block_ref[0] * rows + lax.broadcasted_iota(jnp.int32, (rows, rows), 1)
    key_at = lax.broadcasted_iota(jnp.int32, (rows, rows), 0)
    biases = []
    for place in range(4):
        at = (block_ref[0] ^ place) * rows + key_at
        biases.append(jnp.where((at <= query_at) & (at >= start_ref[0, :1, :]), 0.0, MASKED))
    head_of = lax.broadcasted_iota(jnp.int32, (width, LANES), 0) // HD
    by_head = (head_of == lane_of((width, LANES))).astype(BF16)
    product = back_ref[...].astype(F32) * out_ref[...].astype(F32)
    product_high = product.astype(BF16)
    product_low = (product - product_high.astype(F32)).astype(BF16)
    row_sums = (dot_nn(product_high, by_head) + dot_nn(product_low, by_head)).T
    levels = level_ref[...].T
    cosine, sine = cos_ref[...], sin_ref[...]
    dk_sum[...] = jnp.zeros_like(dk_sum)
    dv_sum[...] = jnp.zeros_like(dv_sum)
    for pair in range(heads // 2):
        at = slice(pair * LANES, (pair + 1) * LANES)
        both = q_ref[:, at]
        back_both = back_ref[:, at]
        zero = jnp.zeros_like(both)
        sides = (~upper, upper)
        queries = [jnp.where(side, both, zero) for side in sides]
        backs = [jnp.where(side, back_both, zero) for side in sides]
        owners = [(2 * pair + place) // group for place in range(2)]
        d_query_t = [jnp.zeros((LANES, rows), F32) for _ in range(2)]
        for piece in range(4):
            span = slice(piece * rows, (piece + 1) * rows)
            probs, d_scores = [], []
            for place in range(2):
                head = 2 * pair + place
                moved = int(owners[place] != place)
                score = dot_nt(keys[moved][span], queries[place]) + biases[piece]
                prob = jnp.exp(score - levels[head : head + 1])
                d_prob = dot_nt(values[moved][span], backs[place])
                d_score = (prob * (d_prob - row_sums[head : head + 1])).astype(BF16)
                d_query_t[place] = d_query_t[place] + dot_nn(keys_t[moved][:, span], d_score)
                probs.append(prob.astype(BF16))
                d_scores.append(d_score)
            if owners[0] == owners[1]:
                dv_sum[owners[0], span] += dot_nn(
                    jnp.concatenate(probs, axis=1), jnp.concatenate(backs, axis=0)
                )
                dk_sum[owners[0], span] += dot_nn(
                    jnp.concatenate(d_scores, axis=1), jnp.concatenate(queries, axis=0)
                )
            else:
                for place in range(2):
                    dv_sum[owners[place], span] += dot_nn(probs[place], backs[place])
                    dk_sum[owners[place], span] += dot_nn(d_scores[place], queries[place])
        d_query = jnp.where(upper_t, d_query_t[1], d_query_t[0]).T * SCALE
        dq_ref[:, at] = (d_query * cosine - swap_halves(d_query) * sine).astype(BF16)
    lower_key = lane_of((4 * rows, LANES)) < HD
    for total, begin in ((dk_sum, 0), (dv_sum, LANES)):
        first, second = total[0], total[1]
        first = first + pltpu.roll(first, HD, 1)
        second = second + pltpu.roll(second, HD, 1)
        both = jnp.where(lower_key, first, second)
        cols = slice(begin, begin + LANES)
        own_ref[:, cols] = both[:rows]
        for place, ref in enumerate((core_ref, x_ref, far_ref)):
            ref[:, cols] = both[(place + 1) * rows : (place + 2) * rows].astype(BF16)


def parts_of(rows, cols):
    shapes = [jax.ShapeDtypeStruct((rows, cols), F32)] + [jax.ShapeDtypeStruct((rows, cols), BF16)] * 3
    return [seq_rows(0, rows, cols)] * 4, shapes


def attend_back(block, q, kv_pieces, back, out, level, start, cosine, sine, rows, seq):
    width = q.shape[1]
    length = 4 * rows
    heads = width // HD
    specs, shapes = parts_of(rows, 2 * LANES)
    return pl.pallas_call(
        attend_back_kernel,
        grid=(1,),
        in_specs=[
            pl.BlockSpec(memory_space=pltpu.SMEM),
            seq_rows(seq, rows, width),
            *[piece_of(seq, rows)] * 4,
            seq_rows(0, rows, width),
            seq_rows(0, rows, width),
            seq_rows(0, rows, LANES),
            pl.BlockSpec((1, 8, rows), lambda i: (seq, 0, 0)),
            seq_rows(seq, rows, LANES),
            seq_rows(seq, rows, LANES),
        ],
        out_specs=[seq_rows(0, rows, width), *specs],
        out_shape=[jax.ShapeDtypeStruct((rows, width), BF16), *shapes],
        scratch_shapes=[
            pltpu.VMEM((2, length, LANES), F32),
            pltpu.VMEM((2, length, LANES), F32),
        ],
        compiler_params=pltpu.CompilerParams(vmem_limit_bytes=VMEM_LIMIT),
        cost_estimate=pl.CostEstimate(
            flops=80 * rows * rows * LANES * heads,
            bytes_accessed=8 * rows * width,
            transcendentals=4 * rows * rows * heads,
        ),
        name="attention_backward",
    )(block, q, *kv_pieces, back, out, level, start, cosine, sine)


def mlp_kernel(
    n_0, n_1, n_2, n_3, c_0, c_1, c_2, c_3, w_ref,
    own_ref, out_1, out_2, out_3, d_own_ref, d_1, d_2, d_3, kept_ref, turned_ref,
    normed_all, cot_all,
):
    step = pl.program_id(0)
    rows = own_ref.shape[0]
    columns = w_ref.shape[1] // 3

    @pl.when(step == 0)
    def _():
        for place, (n_ref, c_ref) in enumerate(zip((n_0, n_1, n_2, n_3), (c_0, c_1, c_2, c_3))):
            normed_all[place // 2, (place % 2) * rows : (place % 2 + 1) * rows] = n_ref[...]
            cot_all[place // 2, (place % 2) * rows : (place % 2 + 1) * rows] = c_ref[...]

    normed, cot = normed_all[step], cot_all[step]
    for begin in range(0, columns, TILE):
        at = slice(begin, begin + TILE)
        gate = dot_nn(normed, w_ref[:, begin : begin + TILE])
        up = dot_nn(normed, w_ref[:, columns + begin : columns + begin + TILE])
        d_act = dot_nn(cot, w_ref[:, 2 * columns + begin : 2 * columns + begin + TILE])
        sigmoid = 0.5 * jnp.tanh(0.5 * gate) + 0.5
        swish = gate * sigmoid
        kept_ref[0, :, at] = (d_act * up * (sigmoid + swish * (1.0 - sigmoid))).astype(BF16)
        kept_ref[1, :, at] = (d_act * swish).astype(BF16)
        kept_ref[2, :, at] = (swish * up).astype(BF16)
    turned_ref[0] = normed.T
    turned_ref[1] = cot.T
    out = dot_nt(kept_ref[2], w_ref[:, 2 * columns :])
    d_normed = dot_nt(kept_ref[0], w_ref[:, :columns]) + dot_nt(kept_ref[1], w_ref[:, columns : 2 * columns])

    @pl.when(step == 0)
    def _():
        own_ref[...] = out[:rows]
        out_1[...] = out[rows:].astype(BF16)
        d_own_ref[...] = d_normed[:rows]
        d_1[...] = d_normed[rows:].astype(BF16)

    @pl.when(step == 1)
    def _():
        out_2[...] = out[:rows].astype(BF16)
        out_3[...] = out[rows:].astype(BF16)
        d_2[...] = d_normed[:rows].astype(BF16)
        d_3[...] = d_normed[rows:].astype(BF16)


def mlp(normed, cot, weights, seq):
    rows, dim = normed[0].shape
    columns = weights.shape[1] // 3
    specs, shapes = parts_of(rows, dim)
    once = lambda at: pl.BlockSpec((rows, dim), lambda i: (at, 0), pipeline_mode=pl.Buffered(1))
    return pl.pallas_call(
        mlp_kernel,
        grid=(2,),
        in_specs=[
            *[once(0)] * 4,
            *[once(seq)] * 3,
            once(0),
            pl.BlockSpec(weights.shape, lambda i: (0, 0), pipeline_mode=pl.Buffered(1)),
        ],
        out_specs=[
            *specs,
            *specs,
            pl.BlockSpec((3, 2 * rows, columns), lambda i: (0, i, 0)),
            pl.BlockSpec((2, dim, 2 * rows), lambda i: (0, 0, i)),
        ],
        out_shape=[
            *shapes,
            *shapes,
            jax.ShapeDtypeStruct((3, 4 * rows, columns), BF16),
            jax.ShapeDtypeStruct((2, dim, 4 * rows), BF16),
        ],
        scratch_shapes=[
            pltpu.VMEM((2, 2 * rows, dim), BF16),
            pltpu.VMEM((2, 2 * rows, dim), BF16),
        ],
        compiler_params=pltpu.CompilerParams(vmem_limit_bytes=VMEM_LIMIT),
        cost_estimate=pl.CostEstimate(
            flops=48 * rows * dim * columns,
            bytes_accessed=6 * dim * columns + 24 * rows * columns,
            transcendentals=4 * rows * columns,
        ),
        name="feed_forward",
    )(*normed, *cot, weights)


def mlp_grad_kernel(turned_0, turned_1, kept_0, kept_1, grad_ref):
    grad_ref[...] = (dot_nn(turned_0[0], kept_0[0]) + dot_nn(turned_1[0], kept_1[0])).astype(BF16)


def mlp_grad(turned, kept):
    _, dim, count = turned[0].shape
    columns = kept[0].shape[2]
    turned_block = pl.BlockSpec((1, dim, count), lambda i: (i // 2, 0, 0))
    kept_block = pl.BlockSpec((1, count, columns), lambda i: (i, 0, 0))
    return pl.pallas_call(
        mlp_grad_kernel,
        grid=(3,),
        in_specs=[turned_block, turned_block, kept_block, kept_block],
        out_specs=pl.BlockSpec((dim, columns), lambda i: (0, i)),
        out_shape=jax.ShapeDtypeStruct((dim, 3 * columns), BF16),
        compiler_params=pltpu.CompilerParams(vmem_limit_bytes=VMEM_LIMIT),
        cost_estimate=pl.CostEstimate(
            flops=12 * count * dim * columns,
            bytes_accessed=6 * dim * columns + 12 * count * columns,
            transcendentals=0,
        ),
        name="feed_forward_gradients",
    )(*turned, *kept)


def pack_kernel(block_ref, gate_ref, up_ref, down_ref, *refs):
    out_refs, scratch = refs[:4], refs[4]
    shard, ff = gate_ref.shape
    quarter = scratch.shape[2] // 4
    for place, ref in enumerate((gate_ref, up_ref, down_ref)):
        scratch[place, :, :ff] = ref[...].astype(F32)
        scratch[place, :, ff:] = jnp.zeros((shard, 4 * quarter - ff), F32)
    for place, out_ref in enumerate(out_refs):
        begin = pl.multiple_of((block_ref[0] ^ place) * quarter, LANES)
        for part in range(3):
            out_ref[:, part * quarter : (part + 1) * quarter] = scratch[part, :, pl.ds(begin, quarter)].astype(BF16)


def pack(block, gate, up, down_t, quarter):
    shard = gate.shape[0]
    return pl.pallas_call(
        pack_kernel,
        in_specs=[pl.BlockSpec(memory_space=pltpu.SMEM)] + [pl.BlockSpec(memory_space=pltpu.VMEM)] * 3,
        out_specs=[pl.BlockSpec(memory_space=pltpu.VMEM)] * 4,
        out_shape=[jax.ShapeDtypeStruct((shard, 3 * quarter), BF16)] * 4,
        scratch_shapes=[pltpu.VMEM((3, shard, 4 * quarter), F32)],
        compiler_params=pltpu.CompilerParams(vmem_limit_bytes=VMEM_LIMIT),
        name="pack_columns",
    )(block, gate, up, down_t)


def pick(options, index):
    value = options[0]
    for place in range(1, len(options)):
        value = jnp.where(index == place, options[place], value)
    return value


def assemble_kernel(block_ref, *refs):
    pieces, out_ref, scratch = refs[:4], refs[4], refs[5]
    shard = pieces[0].shape[0]
    values = [ref[...].astype(F32) for ref in pieces]
    for owner in range(4):
        scratch[owner * shard : (owner + 1) * shard] = pick(values, block_ref[0] ^ owner)
    out_ref[...] = scratch[...].astype(BF16)


def assemble(block, pieces):
    shard, columns = pieces[0].shape
    return pl.pallas_call(
        assemble_kernel,
        in_specs=[pl.BlockSpec(memory_space=pltpu.SMEM)] + [pl.BlockSpec(memory_space=pltpu.VMEM)] * 4,
        out_specs=pl.BlockSpec(memory_space=pltpu.VMEM),
        out_shape=jax.ShapeDtypeStruct((4 * shard, columns), BF16),
        scratch_shapes=[pltpu.VMEM((4 * shard, columns), F32)],
        compiler_params=pltpu.CompilerParams(vmem_limit_bytes=VMEM_LIMIT),
        name="assemble_rows",
    )(block, *pieces)


def cut_kernel(block_ref, value_ref, *refs):
    out_refs, scratch = refs[:4], refs[4]
    shard = out_refs[0].shape[0]
    scratch[...] = value_ref[...].astype(F32)
    values = [scratch[owner * shard : (owner + 1) * shard] for owner in range(4)]
    for place, out_ref in enumerate(out_refs):
        out_ref[...] = pick(values, block_ref[0] ^ place).astype(BF16)


def cut(block, value):
    shard, columns = value.shape[0] // 4, value.shape[1]
    return pl.pallas_call(
        cut_kernel,
        in_specs=[pl.BlockSpec(memory_space=pltpu.SMEM), pl.BlockSpec(memory_space=pltpu.VMEM)],
        out_specs=[pl.BlockSpec(memory_space=pltpu.VMEM)] * 4,
        out_shape=[jax.ShapeDtypeStruct((shard, columns), BF16)] * 4,
        scratch_shapes=[pltpu.VMEM(value.shape, F32)],
        compiler_params=pltpu.CompilerParams(vmem_limit_bytes=VMEM_LIMIT),
        name="cut_rows",
    )(block, value)


def unpack_kernel(block_ref, *refs):
    pieces, out_refs, scratch = refs[:4], refs[4:7], refs[7]
    ff = out_refs[0].shape[1]
    quarter = scratch.shape[2] // 4
    for place, ref in enumerate(pieces):
        begin = pl.multiple_of((block_ref[0] ^ place) * quarter, LANES)
        for part in range(3):
            scratch[part, :, pl.ds(begin, quarter)] = ref[:, part * quarter : (part + 1) * quarter].astype(F32)
    for part, out_ref in enumerate(out_refs):
        out_ref[...] = scratch[part, :, :ff]


def unpack(block, pieces, ff):
    shard, columns = pieces[0].shape
    return pl.pallas_call(
        unpack_kernel,
        in_specs=[pl.BlockSpec(memory_space=pltpu.SMEM)] + [pl.BlockSpec(memory_space=pltpu.VMEM)] * 4,
        out_specs=[pl.BlockSpec(memory_space=pltpu.VMEM)] * 3,
        out_shape=[jax.ShapeDtypeStruct((shard, ff), F32)] * 3,
        scratch_shapes=[pltpu.VMEM((3, shard, columns // 3 * 4), F32)],
        compiler_params=pltpu.CompilerParams(vmem_limit_bytes=VMEM_LIMIT),
        name="unpack_columns",
    )(block, *pieces)


def bit_swap(value, axis, bit=0):
    size = lax.axis_size(axis)
    return lax.ppermute(value, axis, [(i, i ^ (1 << bit)) for i in range(size)])


def jump_swap(value, axes, jump):
    return lax.ppermute(value, axes, [(i, i ^ jump) for i in range(4)])


def to_plane(value, slot):
    high, low = slot >> 1, slot & 1
    pairs = [
        (4 * y + 2 * x + c, 4 * (c ^ low) + 2 * (x ^ high) + y) for y in range(2) for x in range(2) for c in range(2)
    ]
    return lax.ppermute(value, TOKENS + ("cc",), pairs)


def from_plane(value, slot):
    high, low = slot >> 1, slot & 1
    pairs = [
        (4 * y + 2 * x + c, 4 * c + 2 * (x ^ high) + (y ^ low)) for y in range(2) for x in range(2) for c in range(2)
    ]
    return lax.ppermute(value, TOKENS + ("cc",), pairs)


def after(first, *values):
    return lax.optimization_barrier((first, *values))


def gather_four(value, axes):
    from_first = bit_swap(value, axes[0])
    return [value, bit_swap(value, axes[1]), from_first, bit_swap(from_first, axes[1])]


def gather_direct(value, axes):
    return [value] + [jump_swap(value, axes, jump) for jump in range(1, 4)]


def sum_direct(axes, own, *away):
    return [own] + [jump_swap(value, axes, jump + 1) for jump, value in enumerate(away)]


def doubling_offsets(steps):
    weight = {"cc": 1, "cx": 2, "fy": 4, "fz": 8}
    offsets = [0]
    for axis, bit in steps:
        offsets += [offset ^ (weight[axis] << bit) for offset in offsets]
    return jnp.array(offsets, jnp.int32)


def double(value, axis, bit=0):
    return jnp.concatenate([value, bit_swap(value, axis, bit)], axis=0)


def plane_gather(value):
    return jnp.concatenate(gather_direct(value, TOKENS), axis=0)


def plane_sum(value):
    parts = jnp.split(value, 4, axis=0)
    terms = sum_direct(TOKENS, *parts)
    return sum(term.astype(F32) for term in terms).astype(BF16)


def core_sum(keep, send):
    return (keep.astype(F32) + bit_swap(send.astype(BF16), "cc").astype(F32)).astype(BF16)


def halve(value, axis, bit=0):
    middle = value.shape[0] // 2
    came = bit_swap(value[middle:], axis, bit)
    return (value[:middle].astype(F32) + came.astype(F32)).astype(BF16)


def on_device(
    hidden,
    segments,
    attn_gain,
    qkv_weight,
    qkv_bias,
    out_weight,
    mlp_gain,
    gate_weight,
    up_weight,
    down_weight,
    cotangent,
):
    seqs, rows, dim = hidden.shape
    count = seqs * rows
    shard = attn_gain.shape[0]
    world = dim // shard
    joint = qkv_weight.shape[1]
    width = joint - 2 * LANES
    ff = gate_weight.shape[1]
    block = lax.axis_index("cx") * lax.axis_size("cc") + lax.axis_index("cc")
    me = lax.axis_index(FSDP) * lax.axis_size(CTX) + block
    offset = block * rows
    block_arg = block.reshape(1).astype(jnp.int32)
    plane_arg = (lax.axis_index("cx") * 2 + lax.axis_index("fy")).reshape(1).astype(jnp.int32)
    x = hidden.reshape(count, dim)
    cot = cotangent.reshape(count, dim)

    cot_x = bit_swap(cot, "cx")

    far = [("fz", bit) for bit in reversed(range((lax.axis_size("fz")).bit_length() - 1))]
    padded = -(-(shard + 1) // 16) * 16
    small = jnp.concatenate([attn_gain, mlp_gain, qkv_bias])
    small_row = jnp.pad(small, (0, joint + width - small.shape[0]))[None]
    first = jnp.concatenate(
        [
            jnp.concatenate([qkv_weight, out_weight.T], axis=1),
            small_row,
            jnp.zeros((padded - shard - 1, joint + width), BF16),
        ],
        axis=0,
    )
    first = double(first, *far[0])

    quarter = -(-ff // (4 * TILE)) * TILE
    first, *pieces = after(first, *pack(block_arg, gate_weight, up_weight, down_weight.T, quarter))
    pieces = [to_plane(piece, slot) for slot, piece in enumerate(pieces)]
    for axis, bit in far[1:]:
        first = double(first, axis, bit)

    within = jnp.arange(padded, dtype=jnp.int32)
    owner = me ^ doubling_offsets(far + [("cx", 0), ("fy", 0), ("cc", 0)])
    target = jnp.where(within[None, :] < shard, owner[:, None] * shard + within[None, :], -1).reshape(1, -1)
    order = (jnp.arange(dim, dtype=jnp.int32)[:, None] == target).astype(BF16)
    place = jnp.where(within[None, :] == shard, owner[:, None], -1).reshape(1, -1)
    spread = (jnp.arange(world, dtype=jnp.int32)[:, None] == place).astype(BF16)

    at_row = lax.dynamic_slice_in_dim(segments, offset, rows, axis=1)
    zeros_before = jnp.sum((segments < 1).astype(jnp.int32), axis=1, keepdims=True)
    ones_before = jnp.sum((segments < 2).astype(jnp.int32), axis=1, keepdims=True)
    start = jnp.where(at_row == 0, 0, jnp.where(at_row == 1, zeros_before, ones_before))
    position = (offset + jnp.arange(rows, dtype=jnp.int32)[None, :] - start).reshape(count)
    lane = jnp.arange(LANES, dtype=jnp.int32)
    frequency = ROPE_BASE ** (-(lane % (HD // 2)).astype(F32) * 2.0 / HD)
    angle = position.astype(F32)[:, None] * frequency[None, :]
    cosine = jnp.cos(angle)
    sine = jnp.where(lane % HD < HD // 2, -1.0, 1.0)[None, :] * jnp.sin(angle)
    start_column = jnp.broadcast_to(start.reshape(count, 1), (count, LANES))
    start_row = jnp.broadcast_to(start[:, None, :], (seqs, 8, rows))

    first, cot_x, cot_late, order, spread, cosine, sine, start_column, *pieces = after(
        first, cot_x, cot, order, spread, cosine, sine, start_column, *pieces
    )
    w_joint = plane_gather(first[:, :joint])
    mlp_shard = assemble(plane_arg, pieces)
    mlp_weights = lax.all_gather(mlp_shard, WEIGHTS, axis=0, tiled=True)
    w_joint, cot_late = after(w_joint, cot_late)
    w_joint = (w_joint, bit_swap(w_joint, "cc"))
    cot_y = bit_swap(cot_late, "fy")

    normed_low, normed_high, q, kv, gain_attn, gain_mlp = prep(x, order, spread, w_joint, cosine, sine, rows)
    kv_all = gather_four(kv.reshape(seqs, rows, 2 * LANES), CTX)
    kv_all[3], out_rows, cot_y = after(kv_all[3], first[:, joint:], cot_y)
    w_out = plane_gather(out_rows)
    attended, levels, resid, normed_all = [], [], [], []
    for seq in range(seqs):
        turn = block_arg if seq == 0 else after(resid[0], block_arg)[1]
        attended_one, level_one = attend(turn, q, kv_all, start_column, rows, seq)
        if seq == 0:
            attended_one, w_out, far_0, far_1 = after(attended_one, w_out, cot_x[:rows], cot_y[rows:])
            cot_far = [bit_swap(far_0, "fy"), bit_swap(far_1, "cx")]
            w_out = (w_out, bit_swap(w_out, "cc"))
        else:
            attended_one, *cot_far = after(attended_one, *cot_far)
        attended.append(attended_one)
        levels.append(level_one)
        resid_one, normed_one = project_out(attended[seq], x, w_out, order, gain_mlp, rows, seq)
        resid.append(resid_one)
        normed_all.append(gather_direct(normed_one, TOKENS))

    out_parts, d_terms, kept, turned = [], [], [], []
    for seq in range(seqs):
        if seq == 1:
            out_parts[0], normed_all[1] = lax.optimization_barrier((out_parts[0], normed_all[1]))
        result = mlp(normed_all[seq], [cot, cot_x, cot_y, cot_far[seq]], mlp_weights, seq)
        out_parts.append(result[:4])
        d_terms.append(sum_direct(TOKENS, *result[4:8]))
        kept.append(result[8])
        turned.append(result[9])
    d_resid, d_low, d_high, d_attended, mlp_gain_grad, dq, dkv_terms, out_terms = [], [], [], [], [], [], [], []
    for seq in range(seqs):
        if seq == 0:
            _, *d_terms[0] = after(kept[1], *d_terms[0])
        else:
            dq[0], d_terms[1][0], *out_terms[0] = after(dq[0], d_terms[1][0], *out_terms[0])
        result = project_out_back(d_terms[seq], resid[seq], cot, w_out, order, gain_mlp, rows, seq)
        for place, value in zip((d_resid, d_low, d_high, d_attended, mlp_gain_grad), result):
            place.append(value)
        out_terms.append(sum_direct(TOKENS, *after(d_terms[seq][1], *out_parts[seq])[1:]))
        if seq == 0:
            _, turned[1] = after(d_resid[0], turned[1])
            grads = mlp_grad(turned, kept)
            grads, d_attended[0], *d_terms[1] = after(grads, d_attended[0], *d_terms[1])
            grads = lax.psum_scatter(
                grads.reshape(world // 4, 4 * shard, 3 * quarter), WEIGHTS, scatter_dimension=0, tiled=False
            )
        else:
            both = jnp.concatenate(attended, axis=0)
            out_grad = core_sum(
                dot_tn(jnp.concatenate(d_low, axis=0), both).astype(BF16), dot_tn(jnp.concatenate(d_high, axis=0), both)
            )
            d_attended[1], *dkv_terms[0] = after(d_attended[1], *dkv_terms[0])
        result = attend_back(
            block_arg, q, kv_all, d_attended[seq], attended[seq], levels[seq], start_row, cosine, sine, rows, seq
        )
        dq.append(result[0])
        dkv_terms.append(sum_direct(CTX, *result[1:]))
    dq[1], out_grad, *out_terms[1] = after(dq[1], out_grad, *out_terms[1])
    dq_both = jnp.concatenate(dq, axis=0)
    q_grad = core_sum(dot_tn(normed_low, dq_both).astype(BF16), dot_tn(normed_high, dq_both))
    q_grad, *dkv_terms[1] = after(q_grad, *dkv_terms[1])
    q_grad = plane_sum(q_grad)
    d_resid = jnp.concatenate(d_resid, axis=0)
    d_kv, input_grad, attn_gain_grad, bias_grad = input_back(
        dq, dkv_terms, x, d_resid, w_joint, order, gain_attn, cosine, sine
    )
    d_kv, q_grad, attn_gain_grad, bias_grad = after(d_kv, q_grad, attn_gain_grad, bias_grad)

    output = []
    for seq in range(seqs):
        own, *away = out_terms[seq]
        output.append((resid[seq] + own + sum(term.astype(F32) for term in away)).astype(BF16))

    split_at = width + LANES
    bias_grad = bias_grad[0]
    small_grads = jnp.concatenate(
        [
            attn_gain_grad.reshape(world, -1),
            sum(mlp_gain_grad).reshape(world, -1),
            bias_grad[:split_at].reshape(world, -1),
            bias_grad[split_at:].reshape(world, -1),
        ],
        axis=1,
    ).astype(BF16)
    small_count = small_grads.shape[1]
    small_grads = jnp.pad(small_grads, ((0, 0), (0, 2 * LANES - small_count)))
    middle = spread.shape[1] // 2
    kv_grad = core_sum(
        (dot_tn(normed_low, d_kv) + dot_tn(spread[:, :middle], small_grads)).astype(BF16),
        dot_tn(normed_high, d_kv) + dot_tn(spread[:, middle:], small_grads),
    )
    pieces = cut(plane_arg, lax.optimization_barrier(grads))
    kv_grad, *pieces = after(kv_grad, *pieces)
    pieces = [from_plane(piece, slot) for slot, piece in enumerate(pieces)]
    kv_grad, out_grad = plane_sum(kv_grad), plane_sum(out_grad)
    first_sum = jnp.concatenate([q_grad, kv_grad, out_grad], axis=1)
    for axis, bit in reversed(far):
        first_sum = halve(first_sum, axis, bit)
    gate_grad, up_grad, down_grad_t = unpack(block_arg, pieces, ff)
    first_sum = first_sum.astype(F32)
    qkv_sum, out_sum = first_sum[:, :joint], first_sum[:, joint:]
    small_sum = qkv_sum[shard, width : width + small_count]
    at = (shard, 2 * shard, 2 * shard + split_at // world)

    return (
        jnp.stack(output),
        input_grad.reshape(hidden.shape),
        small_sum[: at[0]],
        qkv_sum[:shard],
        small_sum[at[1] : at[2]],
        small_sum[at[2] :],
        out_sum[:shard].T,
        small_sum[at[0] : at[1]],
        gate_grad,
        up_grad,
        down_grad_t.T,
    )


def solution(mesh):
    fsdp, ctx = mesh.shape["fsdp"], mesh.shape["ctx"]
    inner = Mesh(mesh.devices.reshape(fsdp // 2, 2, 2, ctx // 2), AXES)
    tokens = P(FSDP, CTX, None)
    vector = P(AXES)
    by_row = P(AXES, None)
    by_column = P(None, AXES)
    return jax.shard_map(
        on_device,
        mesh=inner,
        in_specs=(
            tokens,
            P(FSDP, None),
            vector,
            by_row,
            vector,
            by_column,
            vector,
            by_row,
            by_row,
            by_column,
            tokens,
        ),
        out_specs=(
            tokens,
            tokens,
            vector,
            by_row,
            vector,
            vector,
            by_column,
            vector,
            by_row,
            by_row,
            by_column,
        ),
        check_vma=False,
    )
```

```python
import functools

import jax
import jax.numpy as jnp
from jax import lax
from jax.experimental import pallas as pl
from jax.experimental.pallas import tpu as pltpu
from jax.sharding import Mesh
from jax.sharding import PartitionSpec as P

HD = 64
LANES = 128
EPSILON = 1e-06
ROPE_BASE = 1000000.0
MASKED = -1e30
SCALE = HD ** (-0.5)
TILE = 256
MIB = 1 << 20
VMEM_LIMIT = 60 * MIB
F32 = jnp.float32
BF16 = jnp.bfloat16
AXES = ("fz", "fy", "cx", "cc")
FSDP = ("fz", "fy")
CTX = ("cx", "cc")
TOKENS = ("fy", "cx")
WEIGHTS = ("fz", "cc")


def dot_nn(a, b):
    return lax.dot_general(a, b, (((1,), (0,)), ((), ())), preferred_element_type=F32)


def dot_nt(a, b):
    return lax.dot_general(a, b, (((1,), (1,)), ((), ())), preferred_element_type=F32)


def dot_tn(a, b):
    return lax.dot_general(a, b, (((0,), (0,)), ((), ())), preferred_element_type=F32)


def lane_of(shape):
    return lax.broadcasted_iota(jnp.int32, shape, len(shape) - 1)


def swap_halves(block):
    lead = lane_of(block.shape) % HD < HD // 2
    return jnp.where(
        lead, pltpu.roll(block, LANES - HD // 2, 1), pltpu.roll(block, HD // 2, 1)
    )


def other_head(block):
    return jnp.concatenate([block[:, HD:], block[:, :HD]], axis=1)


def read_out(extras, first, piece, total):
    owners, columns = extras.shape
    at = lax.broadcasted_iota(jnp.int32, (columns, total), 1) % piece + first
    chosen = (lax.broadcasted_iota(jnp.int32, (columns, total), 0) == at).astype(BF16)
    spread = dot_nn(extras, chosen)
    owner = lax.broadcasted_iota(jnp.int32, (owners, total), 1) // piece
    mine = owner == lax.broadcasted_iota(jnp.int32, (owners, total), 0)
    return jnp.sum(jnp.where(mine, spread, 0.0), axis=0, keepdims=True)


def prep_kernel(
    x_ref, order_ref, spread_ref, w_low_ref, w_high_ref, cos_ref, sin_ref,
    normed_low_ref, normed_high_ref, q_ref, kv_ref, gain_ref, gain_mlp_ref, bias_ref,
):
    x = x_ref[...].astype(F32)
    dim = x.shape[1]
    width = q_ref.shape[1]
    joint = w_low_ref.shape[1]
    middle = w_low_ref.shape[0]
    owners = spread_ref.shape[0]

    @pl.when(pl.program_id(0) == 0)
    def _():
        extras = dot_nn(spread_ref[:, :middle], w_low_ref[:, :LANES])
        extras = (extras + dot_nn(spread_ref[:, middle:], w_high_ref[:, :LANES])).astype(BF16)
        shard = dim // owners
        gain_ref[...] = read_out(extras, 0, shard, dim)
        gain_mlp_ref[...] = read_out(extras, shard, shard, dim)
        bias_ref[...] = read_out(extras, 2 * shard, joint // owners, joint)

    gain, bias = gain_ref[...], bias_ref[...]
    inverse = lax.rsqrt(jnp.mean(x * x, axis=-1, keepdims=True) + EPSILON)
    normed = (x * inverse * gain).astype(BF16)
    ordered = dot_nn(normed, order_ref[...]).astype(BF16)
    normed_low_ref[...] = ordered[:, :middle]
    normed_high_ref[...] = ordered[:, middle:]
    joined = dot_nn(ordered[:, :middle], w_low_ref[...])
    joined = joined + dot_nn(ordered[:, middle:], w_high_ref[...]) + bias
    cosine, sine = cos_ref[...], sin_ref[...]
    for begin in range(0, width + LANES, LANES):
        block = joined[:, begin : begin + LANES]
        turned = block * cosine + swap_halves(block) * sine
        if begin < width:
            q_ref[:, begin : begin + LANES] = (turned * SCALE).astype(BF16)
        else:
            kv_ref[:, :LANES] = turned.astype(BF16)
    kv_ref[:, LANES:] = joined[:, width + LANES :].astype(BF16)


def rows_of(rows, cols):
    return pl.BlockSpec((rows, cols), lambda i: (i, 0))


def whole(value):
    return pl.BlockSpec(value.shape, lambda i: (0,) * value.ndim)


def prep(x, order, spread, weights, cosine, sine, rows):
    count, dim = x.shape
    ordered = order.shape[1]
    joint = weights[0].shape[1]
    width = joint - 2 * LANES
    row = pl.BlockSpec((1, dim), lambda i: (0, 0))
    return pl.pallas_call(
        prep_kernel,
        grid=(count // rows,),
        in_specs=[
            rows_of(rows, dim),
            whole(order),
            whole(spread),
            whole(weights[0]),
            whole(weights[1]),
            rows_of(rows, LANES),
            rows_of(rows, LANES),
        ],
        out_specs=[
            rows_of(rows, ordered // 2),
            rows_of(rows, ordered // 2),
            rows_of(rows, width),
            rows_of(rows, 2 * LANES),
            row,
            row,
        ],
        out_shape=[
            jax.ShapeDtypeStruct((count, ordered // 2), BF16),
            jax.ShapeDtypeStruct((count, ordered // 2), BF16),
            jax.ShapeDtypeStruct((count, width), BF16),
            jax.ShapeDtypeStruct((count, 2 * LANES), BF16),
            jax.ShapeDtypeStruct((1, dim), F32),
            jax.ShapeDtypeStruct((1, dim), F32),
        ],
        scratch_shapes=[pltpu.VMEM((1, joint), F32)],
        compiler_params=pltpu.CompilerParams(vmem_limit_bytes=VMEM_LIMIT),
        cost_estimate=pl.CostEstimate(
            flops=2 * count * ordered * (joint + dim), bytes_accessed=12 * MIB, transcendentals=0
        ),
        name="norm_project_rotate",
    )(x, order, spread, weights[0], weights[1], cosine, sine)


def back_in_order(value, order):
    high = value.astype(BF16)
    low = (value - high.astype(F32)).astype(BF16)
    return dot_nt(high, order) + dot_nt(low, order)


def out_kernel(attended_ref, x_ref, w_low_ref, w_high_ref, order_ref, gain_ref, resid_ref, normed_ref):
    attended = attended_ref[...]
    branch = jnp.concatenate([dot_nt(attended, w_low_ref[...]), dot_nt(attended, w_high_ref[...])], axis=1)
    resid = x_ref[...].astype(F32) + back_in_order(branch, order_ref[...])
    inverse = lax.rsqrt(jnp.mean(resid * resid, axis=-1, keepdims=True) + EPSILON)
    resid_ref[...] = resid
    normed_ref[...] = (resid * inverse * gain_ref[...]).astype(BF16)


def project_out(attended, x, weights, order, gain, rows, seq):
    dim = x.shape[1]
    count = rows
    return pl.pallas_call(
        out_kernel,
        grid=(1,),
        in_specs=[
            rows_of(rows, attended.shape[1]),
            pl.BlockSpec((rows, dim), lambda i: (seq, 0)),
            whole(weights[0]),
            whole(weights[1]),
            whole(order),
            whole(gain),
        ],
        out_specs=[rows_of(rows, dim), rows_of(rows, dim)],
        out_shape=[jax.ShapeDtypeStruct((count, dim), F32), jax.ShapeDtypeStruct((count, dim), BF16)],
        compiler_params=pltpu.CompilerParams(vmem_limit_bytes=VMEM_LIMIT),
        cost_estimate=pl.CostEstimate(flops=6 * count * dim * dim, bytes_accessed=8 * MIB, transcendentals=0),
        name="project_out_norm",
    )(attended, x, weights[0], weights[1], order, gain)


def sum_rows(value):
    return jnp.sum(value, axis=0, keepdims=True)


def norm_back(values, inverse, gain, incoming):
    scaled = incoming * gain
    mean_term = jnp.mean(scaled * values, axis=-1, keepdims=True)
    return inverse * scaled - values * inverse**3 * mean_term


def total_of(own_ref, *away_refs):
    total = own_ref[...]
    for ref in away_refs:
        total = total + ref[...].astype(F32)
    return total


def out_back_kernel(
    own_ref, core_ref, x_ref, far_ref, resid_ref, cot_ref, w_low_ref, w_high_ref, order_ref, gain_ref,
    d_resid_ref, d_low_ref, d_high_ref, d_attended_ref, gain_grad_ref,
):
    middle = w_low_ref.shape[0]
    d_normed = total_of(own_ref, core_ref, x_ref, far_ref)
    resid = resid_ref[...]
    inverse = lax.rsqrt(jnp.mean(resid * resid, axis=-1, keepdims=True) + EPSILON)
    d_resid = cot_ref[...].astype(F32) + norm_back(resid, inverse, gain_ref[...], d_normed)
    d_resid_ref[...] = d_resid
    d_branch = dot_nn(d_resid.astype(BF16), order_ref[...]).astype(BF16)
    d_low_ref[...] = d_branch[:, :middle]
    d_high_ref[...] = d_branch[:, middle:]
    d_attended = dot_nn(d_branch[:, :middle], w_low_ref[...])
    d_attended = d_attended + dot_nn(d_branch[:, middle:], w_high_ref[...])
    d_attended_ref[...] = d_attended.astype(BF16)
    gain_grad_ref[...] = sum_rows(d_normed * resid * inverse)


def project_out_back(terms, resid, cot, weights, order, gain, rows, seq):
    count, dim = resid.shape
    ordered = order.shape[1]
    width = dim
    return pl.pallas_call(
        out_back_kernel,
        grid=(1,),
        in_specs=[
            rows_of(rows, dim),
            rows_of(rows, dim),
            rows_of(rows, dim),
            rows_of(rows, dim),
            rows_of(rows, dim),
            pl.BlockSpec((rows, dim), lambda i: (seq, 0)),
            whole(weights[0]),
            whole(weights[1]),
            whole(order),
            whole(gain),
        ],
        out_specs=[
            rows_of(rows, dim),
            rows_of(rows, ordered // 2),
            rows_of(rows, ordered // 2),
            rows_of(rows, width),
            pl.BlockSpec((1, dim), lambda i: (0, 0)),
        ],
        out_shape=[
            jax.ShapeDtypeStruct((count, dim), F32),
            jax.ShapeDtypeStruct((count, ordered // 2), BF16),
            jax.ShapeDtypeStruct((count, ordered // 2), BF16),
            jax.ShapeDtypeStruct((count, width), BF16),
            jax.ShapeDtypeStruct((1, dim), F32),
        ],
        compiler_params=pltpu.CompilerParams(vmem_limit_bytes=VMEM_LIMIT),
        cost_estimate=pl.CostEstimate(flops=4 * count * dim * dim, bytes_accessed=12 * MIB, transcendentals=0),
        name="norm_back_project",
    )(*terms, resid, cot, weights[0], weights[1], order, gain)


def call_whole(kernel, operands, out_shape, flops, name):
    return pl.pallas_call(
        kernel,
        in_specs=[pl.BlockSpec(memory_space=pltpu.VMEM)] * len(operands),
        out_specs=[pl.BlockSpec(memory_space=pltpu.VMEM)] * len(out_shape),
        out_shape=out_shape,
        compiler_params=pltpu.CompilerParams(vmem_limit_bytes=VMEM_LIMIT),
        cost_estimate=pl.CostEstimate(flops=flops, bytes_accessed=16 * MIB, transcendentals=0),
        name=name,
    )(*operands)


def input_back_kernel(*refs):
    dqs, terms = refs[:2], refs[2:10]
    x_ref, d_resid_ref, w_low_ref, w_high_ref, order_ref, gain_ref, cos_ref, sin_ref = refs[10:18]
    d_kv_ref, input_grad_ref, gain_grad_ref, bias_grad_ref = refs[18:]
    dkv = jnp.concatenate([total_of(*terms[:4]), total_of(*terms[4:])], axis=0)
    dk = dkv[:, :LANES]
    dk = dk * cos_ref[...] - swap_halves(dk) * sin_ref[...]
    d_kv = jnp.concatenate([dk.astype(BF16), dkv[:, LANES:].astype(BF16)], axis=1)
    d_kv_ref[...] = d_kv
    dq = jnp.concatenate([ref[...] for ref in dqs], axis=0)
    d_joined = jnp.concatenate([dq, d_kv], axis=1)
    d_normed = jnp.concatenate([dot_nt(d_joined, w_low_ref[...]), dot_nt(d_joined, w_high_ref[...])], axis=1)
    d_normed = back_in_order(d_normed, order_ref[...])
    x = x_ref[...].astype(F32)
    inverse = lax.rsqrt(jnp.mean(x * x, axis=-1, keepdims=True) + EPSILON)
    input_grad_ref[...] = (d_resid_ref[...] + norm_back(x, inverse, gain_ref[...], d_normed)).astype(BF16)
    gain_grad_ref[...] = sum_rows(d_normed * x * inverse)
    bias_grad_ref[...] = sum_rows(d_joined.astype(F32))


def input_back(dq, terms, x, d_resid, weights, order, gain, cosine, sine):
    count, dim = x.shape
    joint = dq[0].shape[1] + 2 * LANES
    return call_whole(
        input_back_kernel,
        (*dq, *terms[0], *terms[1], x, d_resid, *weights, order, gain, cosine, sine),
        [
            jax.ShapeDtypeStruct((count, 2 * LANES), BF16),
            jax.ShapeDtypeStruct((count, dim), BF16),
            jax.ShapeDtypeStruct((1, dim), F32),
            jax.ShapeDtypeStruct((1, joint), F32),
        ],
        6 * count * dim * joint,
        "input_gradient",
    )


def seq_rows(seq, rows, cols):
    return pl.BlockSpec((rows, cols), lambda i: (seq, 0))


def piece_of(seq, rows):
    return pl.BlockSpec((1, rows, 2 * LANES), lambda i: (seq, 0, 0))


def keys_and_values(piece_refs):
    joint = jnp.concatenate([ref[0] for ref in piece_refs], axis=0)
    key, value = joint[:, :LANES], joint[:, LANES:]
    return (key, other_head(key)), (value, other_head(value))


def attend_kernel(block_ref, q_ref, kv_0, kv_1, kv_2, kv_3, start_ref, out_ref, level_ref):
    rows, width = q_ref.shape
    length = 4 * rows
    heads = width // HD
    group = heads // 2
    keys, values = keys_and_values((kv_0, kv_1, kv_2, kv_3))
    upper_key = lane_of((length, LANES)) >= HD
    upper = lane_of((rows, LANES)) >= HD
    query_at = block_ref[0] * rows + lax.broadcasted_iota(jnp.int32, (rows, length), 0)
    key_at = jnp.concatenate(
        [
            (block_ref[0] ^ place) * rows + lax.broadcasted_iota(jnp.int32, (rows, rows), 1)
            for place in range(4)
        ],
        axis=1,
    )
    allowed = (key_at <= query_at) & (key_at >= start_ref[:, :1])
    bias = jnp.where(allowed, 0.0, MASKED)
    one = jnp.ones((), BF16)
    lane = lane_of((rows, LANES))
    levels = jnp.zeros((rows, LANES), F32)
    for pair in range(heads // 2):
        at = slice(pair * LANES, (pair + 1) * LANES)
        both = q_ref[:, at]
        parts = []
        for place in range(2):
            owner = (2 * pair + place) // group
            moved = int(owner != place)
            side = upper if place else ~upper
            side_key = upper_key if place else ~upper_key
            query = jnp.where(side, both, jnp.zeros_like(both))
            score = dot_nt(query, keys[moved]) + bias
            top = jnp.max(score, axis=1, keepdims=True)
            weight = jnp.exp(score - top).astype(BF16)
            mixed = dot_nn(weight, jnp.where(side_key, values[moved], one))
            total = pltpu.roll(mixed, HD, 1)
            parts.append(mixed / total)
            level = top + jnp.log(total[:, place * HD : place * HD + 1])
            levels = jnp.where(lane == 2 * pair + place, level, levels)
        out_ref[:, at] = jnp.where(upper, parts[1], parts[0]).astype(BF16)
    level_ref[...] = levels


def attend(block, q, kv_pieces, start, rows, seq):
    width = q.shape[1]
    heads = width // HD
    return pl.pallas_call(
        attend_kernel,
        grid=(1,),
        in_specs=[
            pl.BlockSpec(memory_space=pltpu.SMEM),
            seq_rows(seq, rows, width),
            *[piece_of(seq, rows)] * 4,
            seq_rows(seq, rows, LANES),
        ],
        out_specs=[seq_rows(0, rows, width), seq_rows(0, rows, LANES)],
        out_shape=[jax.ShapeDtypeStruct((rows, width), BF16), jax.ShapeDtypeStruct((rows, LANES), F32)],
        compiler_params=pltpu.CompilerParams(vmem_limit_bytes=VMEM_LIMIT),
        cost_estimate=pl.CostEstimate(
            flops=32 * rows * rows * LANES * heads,
            bytes_accessed=4 * rows * width,
            transcendentals=4 * rows * rows * heads,
        ),
        name="attention_forward",
    )(block, q, *kv_pieces, start)


def attend_back_kernel(
    block_ref, q_ref, kv_0, kv_1, kv_2, kv_3, back_ref, out_ref, level_ref, start_ref, cos_ref, sin_ref,
    dq_ref, own_ref, core_ref, x_ref, far_ref, dk_sum, dv_sum,
):
    rows, width = q_ref.shape
    heads = width // HD
    group = heads // 2
    keys, values = keys_and_values((kv_0, kv_1, kv_2, kv_3))
    key_t = keys[0].astype(F32).T.astype(BF16)
    keys_t = (key_t, jnp.concatenate([key_t[HD:], key_t[:HD]], axis=0))
    upper = lane_of((rows, LANES)) >= HD
    upper_t = lax.broadcasted_iota(jnp.int32, (LANES, rows), 0) >= HD
    query_at = block_ref[0] * rows + lax.broadcasted_iota(jnp.int32, (rows, rows), 1)
    key_at = lax.broadcasted_iota(jnp.int32, (rows, rows), 0)
    biases = []
    for place in range(4):
        at = (block_ref[0] ^ place) * rows + key_at
        biases.append(jnp.where((at <= query_at) & (at >= start_ref[0, :1, :]), 0.0, MASKED))
    head_of = lax.broadcasted_iota(jnp.int32, (width, LANES), 0) // HD
    by_head = (head_of == lane_of((width, LANES))).astype(BF16)
    product = back_ref[...].astype(F32) * out_ref[...].astype(F32)
    product_high = product.astype(BF16)
    product_low = (product - product_high.astype(F32)).astype(BF16)
    row_sums = (dot_nn(product_high, by_head) + dot_nn(product_low, by_head)).T
    levels = level_ref[...].T
    cosine, sine = cos_ref[...], sin_ref[...]
    dk_sum[...] = jnp.zeros_like(dk_sum)
    dv_sum[...] = jnp.zeros_like(dv_sum)
    for pair in range(heads // 2):
        at = slice(pair * LANES, (pair + 1) * LANES)
        both = q_ref[:, at]
        back_both = back_ref[:, at]
        zero = jnp.zeros_like(both)
        sides = (~upper, upper)
        queries = [jnp.where(side, both, zero) for side in sides]
        backs = [jnp.where(side, back_both, zero) for side in sides]
        owners = [(2 * pair + place) // group for place in range(2)]
        d_query_t = [jnp.zeros((LANES, rows), F32) for _ in range(2)]
        for piece in range(4):
            span = slice(piece * rows, (piece + 1) * rows)
            probs, d_scores = [], []
            for place in range(2):
                head = 2 * pair + place
                moved = int(owners[place] != place)
                score = dot_nt(keys[moved][span], queries[place]) + biases[piece]
                prob = jnp.exp(score - levels[head : head + 1])
                d_prob = dot_nt(values[moved][span], backs[place])
                d_score = (prob * (d_prob - row_sums[head : head + 1])).astype(BF16)
                d_query_t[place] = d_query_t[place] + dot_nn(keys_t[moved][:, span], d_score)
                probs.append(prob.astype(BF16))
                d_scores.append(d_score)
            if owners[0] == owners[1]:
                dv_sum[owners[0], span] += dot_nn(
                    jnp.concatenate(probs, axis=1), jnp.concatenate(backs, axis=0)
                )
                dk_sum[owners[0], span] += dot_nn(
                    jnp.concatenate(d_scores, axis=1), jnp.concatenate(queries, axis=0)
                )
            else:
                for place in range(2):
                    dv_sum[owners[place], span] += dot_nn(probs[place], backs[place])
                    dk_sum[owners[place], span] += dot_nn(d_scores[place], queries[place])
        d_query = jnp.where(upper_t, d_query_t[1], d_query_t[0]).T * SCALE
        dq_ref[:, at] = (d_query * cosine - swap_halves(d_query) * sine).astype(BF16)
    lower_key = lane_of((4 * rows, LANES)) < HD
    for total, begin in ((dk_sum, 0), (dv_sum, LANES)):
        first, second = total[0], total[1]
        first = first + pltpu.roll(first, HD, 1)
        second = second + pltpu.roll(second, HD, 1)
        both = jnp.where(lower_key, first, second)
        cols = slice(begin, begin + LANES)
        own_ref[:, cols] = both[:rows]
        for place, ref in enumerate((core_ref, x_ref, far_ref)):
            ref[:, cols] = both[(place + 1) * rows : (place + 2) * rows].astype(BF16)


def parts_of(rows, cols):
    shapes = [jax.ShapeDtypeStruct((rows, cols), F32)] + [jax.ShapeDtypeStruct((rows, cols), BF16)] * 3
    return [seq_rows(0, rows, cols)] * 4, shapes


def attend_back(block, q, kv_pieces, back, out, level, start, cosine, sine, rows, seq):
    width = q.shape[1]
    length = 4 * rows
    heads = width // HD
    specs, shapes = parts_of(rows, 2 * LANES)
    return pl.pallas_call(
        attend_back_kernel,
        grid=(1,),
        in_specs=[
            pl.BlockSpec(memory_space=pltpu.SMEM),
            seq_rows(seq, rows, width),
            *[piece_of(seq, rows)] * 4,
            seq_rows(0, rows, width),
            seq_rows(0, rows, width),
            seq_rows(0, rows, LANES),
            pl.BlockSpec((1, 8, rows), lambda i: (seq, 0, 0)),
            seq_rows(seq, rows, LANES),
            seq_rows(seq, rows, LANES),
        ],
        out_specs=[seq_rows(0, rows, width), *specs],
        out_shape=[jax.ShapeDtypeStruct((rows, width), BF16), *shapes],
        scratch_shapes=[
            pltpu.VMEM((2, length, LANES), F32),
            pltpu.VMEM((2, length, LANES), F32),
        ],
        compiler_params=pltpu.CompilerParams(vmem_limit_bytes=VMEM_LIMIT),
        cost_estimate=pl.CostEstimate(
            flops=80 * rows * rows * LANES * heads,
            bytes_accessed=8 * rows * width,
            transcendentals=4 * rows * rows * heads,
        ),
        name="attention_backward",
    )(block, q, *kv_pieces, back, out, level, start, cosine, sine)


def mlp_kernel(
    n_0, n_1, n_2, n_3, c_0, c_1, c_2, c_3, w_ref,
    own_ref, out_1, out_2, out_3, d_own_ref, d_1, d_2, d_3, kept_ref, turned_ref,
    normed_all, cot_all,
):
    step = pl.program_id(0)
    rows = own_ref.shape[0]
    columns = w_ref.shape[1] // 3

    @pl.when(step == 0)
    def _():
        for place, (n_ref, c_ref) in enumerate(zip((n_0, n_1, n_2, n_3), (c_0, c_1, c_2, c_3))):
            normed_all[place // 2, (place % 2) * rows : (place % 2 + 1) * rows] = n_ref[...]
            cot_all[place // 2, (place % 2) * rows : (place % 2 + 1) * rows] = c_ref[...]

    normed, cot = normed_all[step], cot_all[step]
    for begin in range(0, columns, TILE):
        at = slice(begin, begin + TILE)
        gate = dot_nn(normed, w_ref[:, begin : begin + TILE])
        up = dot_nn(normed, w_ref[:, columns + begin : columns + begin + TILE])
        d_act = dot_nn(cot, w_ref[:, 2 * columns + begin : 2 * columns + begin + TILE])
        sigmoid = 0.5 * jnp.tanh(0.5 * gate) + 0.5
        swish = gate * sigmoid
        kept_ref[0, :, at] = (d_act * up * (sigmoid + swish * (1.0 - sigmoid))).astype(BF16)
        kept_ref[1, :, at] = (d_act * swish).astype(BF16)
        kept_ref[2, :, at] = (swish * up).astype(BF16)
    turned_ref[0] = normed.T
    turned_ref[1] = cot.T
    out = dot_nt(kept_ref[2], w_ref[:, 2 * columns :])
    d_normed = dot_nt(kept_ref[0], w_ref[:, :columns]) + dot_nt(kept_ref[1], w_ref[:, columns : 2 * columns])

    @pl.when(step == 0)
    def _():
        own_ref[...] = out[:rows]
        out_1[...] = out[rows:].astype(BF16)
        d_own_ref[...] = d_normed[:rows]
        d_1[...] = d_normed[rows:].astype(BF16)

    @pl.when(step == 1)
    def _():
        out_2[...] = out[:rows].astype(BF16)
        out_3[...] = out[rows:].astype(BF16)
        d_2[...] = d_normed[:rows].astype(BF16)
        d_3[...] = d_normed[rows:].astype(BF16)


def mlp(normed, cot, weights, seq):
    rows, dim = normed[0].shape
    columns = weights.shape[1] // 3
    specs, shapes = parts_of(rows, dim)
    once = lambda at: pl.BlockSpec((rows, dim), lambda i: (at, 0), pipeline_mode=pl.Buffered(1))
    return pl.pallas_call(
        mlp_kernel,
        grid=(2,),
        in_specs=[
            *[once(0)] * 4,
            *[once(seq)] * 3,
            once(0),
            pl.BlockSpec(weights.shape, lambda i: (0, 0), pipeline_mode=pl.Buffered(1)),
        ],
        out_specs=[
            *specs,
            *specs,
            pl.BlockSpec((3, 2 * rows, columns), lambda i: (0, i, 0)),
            pl.BlockSpec((2, dim, 2 * rows), lambda i: (0, 0, i)),
        ],
        out_shape=[
            *shapes,
            *shapes,
            jax.ShapeDtypeStruct((3, 4 * rows, columns), BF16),
            jax.ShapeDtypeStruct((2, dim, 4 * rows), BF16),
        ],
        scratch_shapes=[
            pltpu.VMEM((2, 2 * rows, dim), BF16),
            pltpu.VMEM((2, 2 * rows, dim), BF16),
        ],
        compiler_params=pltpu.CompilerParams(vmem_limit_bytes=VMEM_LIMIT),
        cost_estimate=pl.CostEstimate(
            flops=48 * rows * dim * columns,
            bytes_accessed=6 * dim * columns + 24 * rows * columns,
            transcendentals=4 * rows * columns,
        ),
        name="feed_forward",
    )(*normed, *cot, weights)


def mlp_grad_kernel(turned_0, turned_1, kept_0, kept_1, grad_ref):
    grad_ref[...] = (dot_nn(turned_0[0], kept_0[0]) + dot_nn(turned_1[0], kept_1[0])).astype(BF16)


def mlp_grad(turned, kept):
    _, dim, count = turned[0].shape
    columns = kept[0].shape[2]
    turned_block = pl.BlockSpec((1, dim, count), lambda i: (i // 2, 0, 0))
    kept_block = pl.BlockSpec((1, count, columns), lambda i: (i, 0, 0))
    return pl.pallas_call(
        mlp_grad_kernel,
        grid=(3,),
        in_specs=[turned_block, turned_block, kept_block, kept_block],
        out_specs=pl.BlockSpec((dim, columns), lambda i: (0, i)),
        out_shape=jax.ShapeDtypeStruct((dim, 3 * columns), BF16),
        compiler_params=pltpu.CompilerParams(vmem_limit_bytes=VMEM_LIMIT),
        cost_estimate=pl.CostEstimate(
            flops=12 * count * dim * columns,
            bytes_accessed=6 * dim * columns + 12 * count * columns,
            transcendentals=0,
        ),
        name="feed_forward_gradients",
    )(*turned, *kept)


def pack_kernel(block_ref, gate_ref, up_ref, down_ref, *refs):
    out_refs, scratch = refs[:4], refs[4]
    shard, ff = gate_ref.shape
    quarter = scratch.shape[2] // 4
    for place, ref in enumerate((gate_ref, up_ref, down_ref)):
        scratch[place, :, :ff] = ref[...].astype(F32)
        scratch[place, :, ff:] = jnp.zeros((shard, 4 * quarter - ff), F32)
    for place, out_ref in enumerate(out_refs):
        begin = pl.multiple_of((block_ref[0] ^ place) * quarter, LANES)
        for part in range(3):
            out_ref[:, part * quarter : (part + 1) * quarter] = scratch[part, :, pl.ds(begin, quarter)].astype(BF16)


def pack(block, gate, up, down_t, quarter):
    shard = gate.shape[0]
    return pl.pallas_call(
        pack_kernel,
        in_specs=[pl.BlockSpec(memory_space=pltpu.SMEM)] + [pl.BlockSpec(memory_space=pltpu.VMEM)] * 3,
        out_specs=[pl.BlockSpec(memory_space=pltpu.VMEM)] * 4,
        out_shape=[jax.ShapeDtypeStruct((shard, 3 * quarter), BF16)] * 4,
        scratch_shapes=[pltpu.VMEM((3, shard, 4 * quarter), F32)],
        compiler_params=pltpu.CompilerParams(vmem_limit_bytes=VMEM_LIMIT),
        name="pack_columns",
    )(block, gate, up, down_t)


def pick(options, index):
    value = options[0]
    for place in range(1, len(options)):
        value = jnp.where(index == place, options[place], value)
    return value


def assemble_kernel(block_ref, *refs):
    pieces, out_ref, scratch = refs[:4], refs[4], refs[5]
    shard = pieces[0].shape[0]
    values = [ref[...].astype(F32) for ref in pieces]
    for owner in range(4):
        scratch[owner * shard : (owner + 1) * shard] = pick(values, block_ref[0] ^ owner)
    out_ref[...] = scratch[...].astype(BF16)


def assemble(block, pieces):
    shard, columns = pieces[0].shape
    return pl.pallas_call(
        assemble_kernel,
        in_specs=[pl.BlockSpec(memory_space=pltpu.SMEM)] + [pl.BlockSpec(memory_space=pltpu.VMEM)] * 4,
        out_specs=pl.BlockSpec(memory_space=pltpu.VMEM),
        out_shape=jax.ShapeDtypeStruct((4 * shard, columns), BF16),
        scratch_shapes=[pltpu.VMEM((4 * shard, columns), F32)],
        compiler_params=pltpu.CompilerParams(vmem_limit_bytes=VMEM_LIMIT),
        name="assemble_rows",
    )(block, *pieces)


def cut_kernel(block_ref, value_ref, *refs):
    out_refs, scratch = refs[:4], refs[4]
    shard = out_refs[0].shape[0]
    scratch[...] = value_ref[...].astype(F32)
    values = [scratch[owner * shard : (owner + 1) * shard] for owner in range(4)]
    for place, out_ref in enumerate(out_refs):
        out_ref[...] = pick(values, block_ref[0] ^ place).astype(BF16)


def cut(block, value):
    shard, columns = value.shape[0] // 4, value.shape[1]
    return pl.pallas_call(
        cut_kernel,
        in_specs=[pl.BlockSpec(memory_space=pltpu.SMEM), pl.BlockSpec(memory_space=pltpu.VMEM)],
        out_specs=[pl.BlockSpec(memory_space=pltpu.VMEM)] * 4,
        out_shape=[jax.ShapeDtypeStruct((shard, columns), BF16)] * 4,
        scratch_shapes=[pltpu.VMEM(value.shape, F32)],
        compiler_params=pltpu.CompilerParams(vmem_limit_bytes=VMEM_LIMIT),
        name="cut_rows",
    )(block, value)


def unpack_kernel(block_ref, *refs):
    pieces, out_refs, scratch = refs[:4], refs[4:7], refs[7]
    ff = out_refs[0].shape[1]
    quarter = scratch.shape[2] // 4
    for place, ref in enumerate(pieces):
        begin = pl.multiple_of((block_ref[0] ^ place) * quarter, LANES)
        for part in range(3):
            scratch[part, :, pl.ds(begin, quarter)] = ref[:, part * quarter : (part + 1) * quarter].astype(F32)
    for part, out_ref in enumerate(out_refs):
        out_ref[...] = scratch[part, :, :ff]


def unpack(block, pieces, ff):
    shard, columns = pieces[0].shape
    return pl.pallas_call(
        unpack_kernel,
        in_specs=[pl.BlockSpec(memory_space=pltpu.SMEM)] + [pl.BlockSpec(memory_space=pltpu.VMEM)] * 4,
        out_specs=[pl.BlockSpec(memory_space=pltpu.VMEM)] * 3,
        out_shape=[jax.ShapeDtypeStruct((shard, ff), F32)] * 3,
        scratch_shapes=[pltpu.VMEM((3, shard, columns // 3 * 4), F32)],
        compiler_params=pltpu.CompilerParams(vmem_limit_bytes=VMEM_LIMIT),
        name="unpack_columns",
    )(block, *pieces)


def bit_swap(value, axis, bit=0):
    size = lax.axis_size(axis)
    return lax.ppermute(value, axis, [(i, i ^ (1 << bit)) for i in range(size)])


def jump_swap(value, axes, jump):
    return lax.ppermute(value, axes, [(i, i ^ jump) for i in range(4)])


def to_plane(value, slot):
    high, low = slot >> 1, slot & 1
    pairs = [
        (4 * y + 2 * x + c, 4 * (c ^ low) + 2 * (x ^ high) + y) for y in range(2) for x in range(2) for c in range(2)
    ]
    return lax.ppermute(value, TOKENS + ("cc",), pairs)


def from_plane(value, slot):
    high, low = slot >> 1, slot & 1
    pairs = [
        (4 * y + 2 * x + c, 4 * c + 2 * (x ^ high) + (y ^ low)) for y in range(2) for x in range(2) for c in range(2)
    ]
    return lax.ppermute(value, TOKENS + ("cc",), pairs)


def after(first, *values):
    return lax.optimization_barrier((first, *values))


def gather_four(value, axes):
    from_first = bit_swap(value, axes[0])
    return [value, bit_swap(value, axes[1]), from_first, bit_swap(from_first, axes[1])]


def gather_direct(value, axes):
    return [value] + [jump_swap(value, axes, jump) for jump in range(1, 4)]


def sum_direct(axes, own, *away):
    return [own] + [jump_swap(value, axes, jump + 1) for jump, value in enumerate(away)]


def doubling_offsets(steps):
    weight = {"cc": 1, "cx": 2, "fy": 4, "fz": 8}
    offsets = [0]
    for axis, bit in steps:
        offsets += [offset ^ (weight[axis] << bit) for offset in offsets]
    return jnp.array(offsets, jnp.int32)


def double(value, axis, bit=0):
    return jnp.concatenate([value, bit_swap(value, axis, bit)], axis=0)


def plane_gather(value):
    return jnp.concatenate(gather_direct(value, TOKENS), axis=0)


def plane_sum(value):
    parts = jnp.split(value, 4, axis=0)
    terms = sum_direct(TOKENS, *parts)
    return sum(term.astype(F32) for term in terms).astype(BF16)


def core_sum(keep, send):
    return (keep.astype(F32) + bit_swap(send.astype(BF16), "cc").astype(F32)).astype(BF16)


def halve(value, axis, bit=0):
    middle = value.shape[0] // 2
    came = bit_swap(value[middle:], axis, bit)
    return (value[:middle].astype(F32) + came.astype(F32)).astype(BF16)


def on_device(
    hidden,
    segments,
    attn_gain,
    qkv_weight,
    qkv_bias,
    out_weight,
    mlp_gain,
    gate_weight,
    up_weight,
    down_weight,
    cotangent,
):
    seqs, rows, dim = hidden.shape
    count = seqs * rows
    shard = attn_gain.shape[0]
    world = dim // shard
    joint = qkv_weight.shape[1]
    width = joint - 2 * LANES
    ff = gate_weight.shape[1]
    block = lax.axis_index("cx") * lax.axis_size("cc") + lax.axis_index("cc")
    me = lax.axis_index(FSDP) * lax.axis_size(CTX) + block
    offset = block * rows
    block_arg = block.reshape(1).astype(jnp.int32)
    plane_arg = (lax.axis_index("cx") * 2 + lax.axis_index("fy")).reshape(1).astype(jnp.int32)
    x = hidden.reshape(count, dim)
    cot = cotangent.reshape(count, dim)

    cot_x = bit_swap(cot, "cx")

    far = [("fz", bit) for bit in reversed(range((lax.axis_size("fz")).bit_length() - 1))]
    padded = -(-(shard + 1) // 16) * 16
    small = jnp.concatenate([attn_gain, mlp_gain, qkv_bias])
    small_row = jnp.pad(small, (0, joint + width - small.shape[0]))[None]
    first = jnp.concatenate(
        [
            jnp.concatenate([qkv_weight, out_weight.T], axis=1),
            small_row,
            jnp.zeros((padded - shard - 1, joint + width), BF16),
        ],
        axis=0,
    )
    first = double(first, *far[0])

    quarter = -(-ff // (4 * TILE)) * TILE
    first, *pieces = after(first, *pack(block_arg, gate_weight, up_weight, down_weight.T, quarter))
    pieces = [to_plane(piece, slot) for slot, piece in enumerate(pieces)]
    for axis, bit in far[1:]:
        first = double(first, axis, bit)

    within = jnp.arange(padded, dtype=jnp.int32)
    owner = me ^ doubling_offsets(far + [("cx", 0), ("fy", 0), ("cc", 0)])
    target = jnp.where(within[None, :] < shard, owner[:, None] * shard + within[None, :], -1).reshape(1, -1)
    order = (jnp.arange(dim, dtype=jnp.int32)[:, None] == target).astype(BF16)
    place = jnp.where(within[None, :] == shard, owner[:, None], -1).reshape(1, -1)
    spread = (jnp.arange(world, dtype=jnp.int32)[:, None] == place).astype(BF16)

    at_row = lax.dynamic_slice_in_dim(segments, offset, rows, axis=1)
    zeros_before = jnp.sum((segments < 1).astype(jnp.int32), axis=1, keepdims=True)
    ones_before = jnp.sum((segments < 2).astype(jnp.int32), axis=1, keepdims=True)
    start = jnp.where(at_row == 0, 0, jnp.where(at_row == 1, zeros_before, ones_before))
    position = (offset + jnp.arange(rows, dtype=jnp.int32)[None, :] - start).reshape(count)
    lane = jnp.arange(LANES, dtype=jnp.int32)
    frequency = ROPE_BASE ** (-(lane % (HD // 2)).astype(F32) * 2.0 / HD)
    angle = position.astype(F32)[:, None] * frequency[None, :]
    cosine = jnp.cos(angle)
    sine = jnp.where(lane % HD < HD // 2, -1.0, 1.0)[None, :] * jnp.sin(angle)
    start_column = jnp.broadcast_to(start.reshape(count, 1), (count, LANES))
    start_row = jnp.broadcast_to(start[:, None, :], (seqs, 8, rows))

    first, cot_x, cot_late, order, spread, cosine, sine, start_column, *pieces = after(
        first, cot_x, cot, order, spread, cosine, sine, start_column, *pieces
    )
    w_joint = plane_gather(first[:, :joint])
    mlp_shard = assemble(plane_arg, pieces)
    mlp_weights = lax.all_gather(mlp_shard, WEIGHTS, axis=0, tiled=True)
    w_joint, cot_late = after(w_joint, cot_late)
    w_joint = (w_joint, bit_swap(w_joint, "cc"))
    cot_y = bit_swap(cot_late, "fy")

    normed_low, normed_high, q, kv, gain_attn, gain_mlp = prep(x, order, spread, w_joint, cosine, sine, rows)
    kv_all = gather_four(kv.reshape(seqs, rows, 2 * LANES), CTX)
    kv_all[3], out_rows, cot_y = after(kv_all[3], first[:, joint:], cot_y)
    w_out = plane_gather(out_rows)
    attended, levels, resid, normed_all = [], [], [], []
    for seq in range(seqs):
        turn = block_arg if seq == 0 else after(resid[0], block_arg)[1]
        attended_one, level_one = attend(turn, q, kv_all, start_column, rows, seq)
        if seq == 0:
            attended_one, w_out, far_0, far_1 = after(attended_one, w_out, cot_x[:rows], cot_y[rows:])
            cot_far = [bit_swap(far_0, "fy"), bit_swap(far_1, "cx")]
            w_out = (w_out, bit_swap(w_out, "cc"))
        else:
            attended_one, *cot_far = after(attended_one, *cot_far)
        attended.append(attended_one)
        levels.append(level_one)
        resid_one, normed_one = project_out(attended[seq], x, w_out, order, gain_mlp, rows, seq)
        resid.append(resid_one)
        normed_all.append(gather_direct(normed_one, TOKENS))

    out_parts, d_terms, kept, turned = [], [], [], []
    for seq in range(seqs):
        if seq == 1:
            out_parts[0], normed_all[1] = lax.optimization_barrier((out_parts[0], normed_all[1]))
        result = mlp(normed_all[seq], [cot, cot_x, cot_y, cot_far[seq]], mlp_weights, seq)
        out_parts.append(result[:4])
        d_terms.append(sum_direct(TOKENS, *result[4:8]))
        kept.append(result[8])
        turned.append(result[9])
    d_resid, d_low, d_high, d_attended, mlp_gain_grad, dq, dkv_terms = [], [], [], [], [], [], []
    for seq in range(seqs):
        if seq == 0:
            _, *d_terms[0] = after(kept[1], *d_terms[0])
        else:
            dq[0], d_terms[1][0], *out_terms[0], out_terms[1][1], out_terms[1][2] = after(
                dq[0], d_terms[1][0], *out_terms[0], out_terms[1][1], out_terms[1][2]
            )
        result = project_out_back(d_terms[seq], resid[seq], cot, w_out, order, gain_mlp, rows, seq)
        for place, value in zip((d_resid, d_low, d_high, d_attended, mlp_gain_grad), result):
            place.append(value)
        if seq == 0:
            out_terms = [
                sum_direct(TOKENS, *after(terms[1], *parts)[1:]) for terms, parts in zip(d_terms, out_parts)
            ]
            _, turned[1] = after(d_resid[0], turned[1])
            grads = mlp_grad(turned, kept)
            grads, d_attended[0], *d_terms[1] = after(grads, d_attended[0], *d_terms[1])
            grads = lax.psum_scatter(
                grads.reshape(world // 4, 4 * shard, 3 * quarter), WEIGHTS, scatter_dimension=0, tiled=False
            )
        else:
            both = jnp.concatenate(attended, axis=0)
            out_grad = core_sum(
                dot_tn(jnp.concatenate(d_low, axis=0), both).astype(BF16), dot_tn(jnp.concatenate(d_high, axis=0), both)
            )
            d_attended[1], *dkv_terms[0] = after(d_attended[1], *dkv_terms[0])
            d_attended[1], out_grad = after(d_attended[1], out_grad)
            out_grad = plane_sum(out_grad)
        result = attend_back(
            block_arg, q, kv_all, d_attended[seq], attended[seq], levels[seq], start_row, cosine, sine, rows, seq
        )
        dq.append(result[0])
        dkv_terms.append(sum_direct(CTX, *result[1:]))
    dq[1], out_grad, *out_terms[1] = after(dq[1], out_grad, *out_terms[1])
    dq_both = jnp.concatenate(dq, axis=0)
    q_grad = core_sum(dot_tn(normed_low, dq_both).astype(BF16), dot_tn(normed_high, dq_both))
    q_grad, *dkv_terms[1] = after(q_grad, *dkv_terms[1])
    q_grad = plane_sum(q_grad)
    d_resid = jnp.concatenate(d_resid, axis=0)
    d_kv, input_grad, attn_gain_grad, bias_grad = input_back(
        dq, dkv_terms, x, d_resid, w_joint, order, gain_attn, cosine, sine
    )
    d_kv, q_grad, attn_gain_grad, bias_grad = after(d_kv, q_grad, attn_gain_grad, bias_grad)

    split_at = width + LANES
    bias_grad = bias_grad[0]
    small_grads = jnp.concatenate(
        [
            attn_gain_grad.reshape(world, -1),
            sum(mlp_gain_grad).reshape(world, -1),
            bias_grad[:split_at].reshape(world, -1),
            bias_grad[split_at:].reshape(world, -1),
        ],
        axis=1,
    ).astype(BF16)
    small_count = small_grads.shape[1]
    small_grads = jnp.pad(small_grads, ((0, 0), (0, 2 * LANES - small_count)))
    middle = spread.shape[1] // 2
    kv_grad = core_sum(
        (dot_tn(normed_low, d_kv) + dot_tn(spread[:, :middle], small_grads)).astype(BF16),
        dot_tn(normed_high, d_kv) + dot_tn(spread[:, middle:], small_grads),
    )
    pieces = cut(plane_arg, lax.optimization_barrier(grads))
    kv_grad, *pieces = after(kv_grad, *pieces)
    pieces = [from_plane(piece, slot) for slot, piece in enumerate(pieces)]
    first_sum = jnp.concatenate([q_grad, plane_sum(kv_grad), out_grad], axis=1)
    first_sum, out_terms = lax.optimization_barrier((first_sum, out_terms))
    for axis, bit in reversed(far):
        first_sum = halve(first_sum, axis, bit)
    output = []
    for seq in range(seqs):
        own, *away = out_terms[seq]
        output.append((resid[seq] + own + sum(term.astype(F32) for term in away)).astype(BF16))

    gate_grad, up_grad, down_grad_t = unpack(block_arg, pieces, ff)
    first_sum = first_sum.astype(F32)
    qkv_sum, out_sum = first_sum[:, :joint], first_sum[:, joint:]
    small_sum = qkv_sum[shard, width : width + small_count]
    at = (shard, 2 * shard, 2 * shard + split_at // world)

    return (
        jnp.stack(output),
        input_grad.reshape(hidden.shape),
        small_sum[: at[0]],
        qkv_sum[:shard],
        small_sum[at[1] : at[2]],
        small_sum[at[2] :],
        out_sum[:shard].T,
        small_sum[at[0] : at[1]],
        gate_grad,
        up_grad,
        down_grad_t.T,
    )


def solution(mesh):
    fsdp, ctx = mesh.shape["fsdp"], mesh.shape["ctx"]
    inner = Mesh(mesh.devices.reshape(fsdp // 2, 2, 2, ctx // 2), AXES)
    tokens = P(FSDP, CTX, None)
    vector = P(AXES)
    by_row = P(AXES, None)
    by_column = P(None, AXES)
    return jax.shard_map(
        on_device,
        mesh=inner,
        in_specs=(
            tokens,
            P(FSDP, None),
            vector,
            by_row,
            vector,
            by_column,
            vector,
            by_row,
            by_row,
            by_column,
            tokens,
        ),
        out_specs=(
            tokens,
            tokens,
            vector,
            by_row,
            vector,
            vector,
            by_column,
            vector,
            by_row,
            by_row,
            by_column,
        ),
        check_vma=False,
    )
```

```python
import functools

import jax
import jax.numpy as jnp
from jax import lax
from jax.experimental import pallas as pl
from jax.experimental.pallas import tpu as pltpu
from jax.sharding import Mesh
from jax.sharding import PartitionSpec as P

HD = 64
LANES = 128
EPSILON = 1e-06
ROPE_BASE = 1000000.0
MASKED = -1e30
SCALE = HD ** (-0.5)
TILE = 256
MIB = 1 << 20
VMEM_LIMIT = 60 * MIB
F32 = jnp.float32
BF16 = jnp.bfloat16
AXES = ("fz", "fy", "cx", "cc")
FSDP = ("fz", "fy")
CTX = ("cx", "cc")
TOKENS = ("fy", "cx")
WEIGHTS = ("fz", "cc")


def dot_nn(a, b):
    return lax.dot_general(a, b, (((1,), (0,)), ((), ())), preferred_element_type=F32)


def dot_nt(a, b):
    return lax.dot_general(a, b, (((1,), (1,)), ((), ())), preferred_element_type=F32)


def dot_tn(a, b):
    return lax.dot_general(a, b, (((0,), (0,)), ((), ())), preferred_element_type=F32)


def lane_of(shape):
    return lax.broadcasted_iota(jnp.int32, shape, len(shape) - 1)


def swap_halves(block):
    lead = lane_of(block.shape) % HD < HD // 2
    return jnp.where(
        lead, pltpu.roll(block, LANES - HD // 2, 1), pltpu.roll(block, HD // 2, 1)
    )


def other_head(block):
    return jnp.concatenate([block[:, HD:], block[:, :HD]], axis=1)


def read_out(extras, first, piece, total):
    owners, columns = extras.shape
    at = lax.broadcasted_iota(jnp.int32, (columns, total), 1) % piece + first
    chosen = (lax.broadcasted_iota(jnp.int32, (columns, total), 0) == at).astype(BF16)
    spread = dot_nn(extras, chosen)
    owner = lax.broadcasted_iota(jnp.int32, (owners, total), 1) // piece
    mine = owner == lax.broadcasted_iota(jnp.int32, (owners, total), 0)
    return jnp.sum(jnp.where(mine, spread, 0.0), axis=0, keepdims=True)


def prep_kernel(
    x_ref, order_ref, spread_ref, w_low_ref, w_high_ref, cos_ref, sin_ref,
    normed_low_ref, normed_high_ref, q_ref, kv_ref, gain_ref, gain_mlp_ref, bias_ref,
):
    x = x_ref[...].astype(F32)
    dim = x.shape[1]
    width = q_ref.shape[1]
    joint = w_low_ref.shape[1]
    middle = w_low_ref.shape[0]
    owners = spread_ref.shape[0]

    @pl.when(pl.program_id(0) == 0)
    def _():
        extras = dot_nn(spread_ref[:, :middle], w_low_ref[:, :LANES])
        extras = (extras + dot_nn(spread_ref[:, middle:], w_high_ref[:, :LANES])).astype(BF16)
        shard = dim // owners
        gain_ref[...] = read_out(extras, 0, shard, dim)
        gain_mlp_ref[...] = read_out(extras, shard, shard, dim)
        bias_ref[...] = read_out(extras, 2 * shard, joint // owners, joint)

    gain, bias = gain_ref[...], bias_ref[...]
    inverse = lax.rsqrt(jnp.mean(x * x, axis=-1, keepdims=True) + EPSILON)
    normed = (x * inverse * gain).astype(BF16)
    ordered = dot_nn(normed, order_ref[...]).astype(BF16)
    normed_low_ref[...] = ordered[:, :middle]
    normed_high_ref[...] = ordered[:, middle:]
    joined = dot_nn(ordered[:, :middle], w_low_ref[...])
    joined = joined + dot_nn(ordered[:, middle:], w_high_ref[...]) + bias
    cosine, sine = cos_ref[...], sin_ref[...]
    for begin in range(0, width + LANES, LANES):
        block = joined[:, begin : begin + LANES]
        turned = block * cosine + swap_halves(block) * sine
        if begin < width:
            q_ref[:, begin : begin + LANES] = (turned * SCALE).astype(BF16)
        else:
            kv_ref[:, :LANES] = turned.astype(BF16)
    kv_ref[:, LANES:] = joined[:, width + LANES :].astype(BF16)


def rows_of(rows, cols):
    return pl.BlockSpec((rows, cols), lambda i: (i, 0))


def whole(value):
    return pl.BlockSpec(value.shape, lambda i: (0,) * value.ndim)


def prep(x, order, spread, weights, cosine, sine, rows):
    count, dim = x.shape
    ordered = order.shape[1]
    joint = weights[0].shape[1]
    width = joint - 2 * LANES
    row = pl.BlockSpec((1, dim), lambda i: (0, 0))
    return pl.pallas_call(
        prep_kernel,
        grid=(count // rows,),
        in_specs=[
            rows_of(rows, dim),
            whole(order),
            whole(spread),
            whole(weights[0]),
            whole(weights[1]),
            rows_of(rows, LANES),
            rows_of(rows, LANES),
        ],
        out_specs=[
            rows_of(rows, ordered // 2),
            rows_of(rows, ordered // 2),
            rows_of(rows, width),
            rows_of(rows, 2 * LANES),
            row,
            row,
        ],
        out_shape=[
            jax.ShapeDtypeStruct((count, ordered // 2), BF16),
            jax.ShapeDtypeStruct((count, ordered // 2), BF16),
            jax.ShapeDtypeStruct((count, width), BF16),
            jax.ShapeDtypeStruct((count, 2 * LANES), BF16),
            jax.ShapeDtypeStruct((1, dim), F32),
            jax.ShapeDtypeStruct((1, dim), F32),
        ],
        scratch_shapes=[pltpu.VMEM((1, joint), F32)],
        compiler_params=pltpu.CompilerParams(vmem_limit_bytes=VMEM_LIMIT),
        cost_estimate=pl.CostEstimate(
            flops=2 * count * ordered * (joint + dim), bytes_accessed=12 * MIB, transcendentals=0
        ),
        name="norm_project_rotate",
    )(x, order, spread, weights[0], weights[1], cosine, sine)


def back_in_order(value, order):
    high = value.astype(BF16)
    low = (value - high.astype(F32)).astype(BF16)
    return dot_nt(high, order) + dot_nt(low, order)


def out_kernel(attended_ref, x_ref, w_low_ref, w_high_ref, order_ref, gain_ref, resid_ref, normed_ref):
    attended = attended_ref[...]
    branch = jnp.concatenate([dot_nt(attended, w_low_ref[...]), dot_nt(attended, w_high_ref[...])], axis=1)
    resid = x_ref[...].astype(F32) + back_in_order(branch, order_ref[...])
    inverse = lax.rsqrt(jnp.mean(resid * resid, axis=-1, keepdims=True) + EPSILON)
    resid_ref[...] = resid
    normed_ref[...] = (resid * inverse * gain_ref[...]).astype(BF16)


def project_out(attended, x, weights, order, gain, rows, seq):
    dim = x.shape[1]
    count = rows
    return pl.pallas_call(
        out_kernel,
        grid=(1,),
        in_specs=[
            rows_of(rows, attended.shape[1]),
            pl.BlockSpec((rows, dim), lambda i: (seq, 0)),
            whole(weights[0]),
            whole(weights[1]),
            whole(order),
            whole(gain),
        ],
        out_specs=[rows_of(rows, dim), rows_of(rows, dim)],
        out_shape=[jax.ShapeDtypeStruct((count, dim), F32), jax.ShapeDtypeStruct((count, dim), BF16)],
        compiler_params=pltpu.CompilerParams(vmem_limit_bytes=VMEM_LIMIT),
        cost_estimate=pl.CostEstimate(flops=6 * count * dim * dim, bytes_accessed=8 * MIB, transcendentals=0),
        name="project_out_norm",
    )(attended, x, weights[0], weights[1], order, gain)


def sum_rows(value):
    return jnp.sum(value, axis=0, keepdims=True)


def norm_back(values, inverse, gain, incoming):
    scaled = incoming * gain
    mean_term = jnp.mean(scaled * values, axis=-1, keepdims=True)
    return inverse * scaled - values * inverse**3 * mean_term


def total_of(own_ref, *away_refs):
    total = own_ref[...]
    for ref in away_refs:
        total = total + ref[...].astype(F32)
    return total


def out_back_kernel(
    own_ref, core_ref, x_ref, far_ref, resid_ref, cot_ref, w_low_ref, w_high_ref, order_ref, gain_ref,
    d_resid_ref, d_low_ref, d_high_ref, d_attended_ref, gain_grad_ref,
):
    middle = w_low_ref.shape[0]
    d_normed = total_of(own_ref, core_ref, x_ref, far_ref)
    resid = resid_ref[...]
    inverse = lax.rsqrt(jnp.mean(resid * resid, axis=-1, keepdims=True) + EPSILON)
    d_resid = cot_ref[...].astype(F32) + norm_back(resid, inverse, gain_ref[...], d_normed)
    d_resid_ref[...] = d_resid
    d_branch = dot_nn(d_resid.astype(BF16), order_ref[...]).astype(BF16)
    d_low_ref[...] = d_branch[:, :middle]
    d_high_ref[...] = d_branch[:, middle:]
    d_attended = dot_nn(d_branch[:, :middle], w_low_ref[...])
    d_attended = d_attended + dot_nn(d_branch[:, middle:], w_high_ref[...])
    d_attended_ref[...] = d_attended.astype(BF16)
    gain_grad_ref[...] = sum_rows(d_normed * resid * inverse)


def project_out_back(terms, resid, cot, weights, order, gain, rows, seq):
    count, dim = resid.shape
    ordered = order.shape[1]
    width = dim
    return pl.pallas_call(
        out_back_kernel,
        grid=(1,),
        in_specs=[
            rows_of(rows, dim),
            rows_of(rows, dim),
            rows_of(rows, dim),
            rows_of(rows, dim),
            rows_of(rows, dim),
            pl.BlockSpec((rows, dim), lambda i: (seq, 0)),
            whole(weights[0]),
            whole(weights[1]),
            whole(order),
            whole(gain),
        ],
        out_specs=[
            rows_of(rows, dim),
            rows_of(rows, ordered // 2),
            rows_of(rows, ordered // 2),
            rows_of(rows, width),
            pl.BlockSpec((1, dim), lambda i: (0, 0)),
        ],
        out_shape=[
            jax.ShapeDtypeStruct((count, dim), F32),
            jax.ShapeDtypeStruct((count, ordered // 2), BF16),
            jax.ShapeDtypeStruct((count, ordered // 2), BF16),
            jax.ShapeDtypeStruct((count, width), BF16),
            jax.ShapeDtypeStruct((1, dim), F32),
        ],
        compiler_params=pltpu.CompilerParams(vmem_limit_bytes=VMEM_LIMIT),
        cost_estimate=pl.CostEstimate(flops=4 * count * dim * dim, bytes_accessed=12 * MIB, transcendentals=0),
        name="norm_back_project",
    )(*terms, resid, cot, weights[0], weights[1], order, gain)


def call_whole(kernel, operands, out_shape, flops, name):
    return pl.pallas_call(
        kernel,
        in_specs=[pl.BlockSpec(memory_space=pltpu.VMEM)] * len(operands),
        out_specs=[pl.BlockSpec(memory_space=pltpu.VMEM)] * len(out_shape),
        out_shape=out_shape,
        compiler_params=pltpu.CompilerParams(vmem_limit_bytes=VMEM_LIMIT),
        cost_estimate=pl.CostEstimate(flops=flops, bytes_accessed=16 * MIB, transcendentals=0),
        name=name,
    )(*operands)


def input_back_kernel(*refs):
    dqs, terms = refs[:2], refs[2:10]
    x_ref, d_resid_ref, w_low_ref, w_high_ref, order_ref, gain_ref, cos_ref, sin_ref = refs[10:18]
    d_kv_ref, input_grad_ref, gain_grad_ref, bias_grad_ref = refs[18:]
    dkv = jnp.concatenate([total_of(*terms[:4]), total_of(*terms[4:])], axis=0)
    dk = dkv[:, :LANES]
    dk = dk * cos_ref[...] - swap_halves(dk) * sin_ref[...]
    d_kv = jnp.concatenate([dk.astype(BF16), dkv[:, LANES:].astype(BF16)], axis=1)
    d_kv_ref[...] = d_kv
    dq = jnp.concatenate([ref[...] for ref in dqs], axis=0)
    d_joined = jnp.concatenate([dq, d_kv], axis=1)
    d_normed = jnp.concatenate([dot_nt(d_joined, w_low_ref[...]), dot_nt(d_joined, w_high_ref[...])], axis=1)
    d_normed = back_in_order(d_normed, order_ref[...])
    x = x_ref[...].astype(F32)
    inverse = lax.rsqrt(jnp.mean(x * x, axis=-1, keepdims=True) + EPSILON)
    input_grad_ref[...] = (d_resid_ref[...] + norm_back(x, inverse, gain_ref[...], d_normed)).astype(BF16)
    gain_grad_ref[...] = sum_rows(d_normed * x * inverse)
    bias_grad_ref[...] = sum_rows(d_joined.astype(F32))


def input_back(dq, terms, x, d_resid, weights, order, gain, cosine, sine):
    count, dim = x.shape
    joint = dq[0].shape[1] + 2 * LANES
    return call_whole(
        input_back_kernel,
        (*dq, *terms[0], *terms[1], x, d_resid, *weights, order, gain, cosine, sine),
        [
            jax.ShapeDtypeStruct((count, 2 * LANES), BF16),
            jax.ShapeDtypeStruct((count, dim), BF16),
            jax.ShapeDtypeStruct((1, dim), F32),
            jax.ShapeDtypeStruct((1, joint), F32),
        ],
        6 * count * dim * joint,
        "input_gradient",
    )


def seq_rows(seq, rows, cols):
    return pl.BlockSpec((rows, cols), lambda i: (seq, 0))


def piece_of(seq, rows):
    return pl.BlockSpec((1, rows, 2 * LANES), lambda i: (seq, 0, 0))


def keys_and_values(piece_refs):
    joint = jnp.concatenate([ref[0] for ref in piece_refs], axis=0)
    key, value = joint[:, :LANES], joint[:, LANES:]
    return (key, other_head(key)), (value, other_head(value))


def attend_kernel(block_ref, q_ref, kv_0, kv_1, kv_2, kv_3, start_ref, out_ref, level_ref):
    rows, width = q_ref.shape
    length = 4 * rows
    heads = width // HD
    group = heads // 2
    keys, values = keys_and_values((kv_0, kv_1, kv_2, kv_3))
    upper_key = lane_of((length, LANES)) >= HD
    upper = lane_of((rows, LANES)) >= HD
    query_at = block_ref[0] * rows + lax.broadcasted_iota(jnp.int32, (rows, length), 0)
    key_at = jnp.concatenate(
        [
            (block_ref[0] ^ place) * rows + lax.broadcasted_iota(jnp.int32, (rows, rows), 1)
            for place in range(4)
        ],
        axis=1,
    )
    allowed = (key_at <= query_at) & (key_at >= start_ref[:, :1])
    bias = jnp.where(allowed, 0.0, MASKED)
    one = jnp.ones((), BF16)
    lane = lane_of((rows, LANES))
    levels = jnp.zeros((rows, LANES), F32)
    for pair in range(heads // 2):
        at = slice(pair * LANES, (pair + 1) * LANES)
        both = q_ref[:, at]
        parts = []
        for place in range(2):
            owner = (2 * pair + place) // group
            moved = int(owner != place)
            side = upper if place else ~upper
            side_key = upper_key if place else ~upper_key
            query = jnp.where(side, both, jnp.zeros_like(both))
            score = dot_nt(query, keys[moved]) + bias
            top = jnp.max(score, axis=1, keepdims=True)
            weight = jnp.exp(score - top).astype(BF16)
            mixed = dot_nn(weight, jnp.where(side_key, values[moved], one))
            total = pltpu.roll(mixed, HD, 1)
            parts.append(mixed / total)
            level = top + jnp.log(total[:, place * HD : place * HD + 1])
            levels = jnp.where(lane == 2 * pair + place, level, levels)
        out_ref[:, at] = jnp.where(upper, parts[1], parts[0]).astype(BF16)
    level_ref[...] = levels


def attend(block, q, kv_pieces, start, rows, seq):
    width = q.shape[1]
    heads = width // HD
    return pl.pallas_call(
        attend_kernel,
        grid=(1,),
        in_specs=[
            pl.BlockSpec(memory_space=pltpu.SMEM),
            seq_rows(seq, rows, width),
            *[piece_of(seq, rows)] * 4,
            seq_rows(seq, rows, LANES),
        ],
        out_specs=[seq_rows(0, rows, width), seq_rows(0, rows, LANES)],
        out_shape=[jax.ShapeDtypeStruct((rows, width), BF16), jax.ShapeDtypeStruct((rows, LANES), F32)],
        compiler_params=pltpu.CompilerParams(vmem_limit_bytes=VMEM_LIMIT),
        cost_estimate=pl.CostEstimate(
            flops=32 * rows * rows * LANES * heads,
            bytes_accessed=4 * rows * width,
            transcendentals=4 * rows * rows * heads,
        ),
        name="attention_forward",
    )(block, q, *kv_pieces, start)


def attend_back_kernel(
    block_ref, q_ref, kv_0, kv_1, kv_2, kv_3, back_ref, out_ref, level_ref, start_ref, cos_ref, sin_ref,
    dq_ref, own_ref, core_ref, x_ref, far_ref, dk_sum, dv_sum,
):
    rows, width = q_ref.shape
    heads = width // HD
    group = heads // 2
    keys, values = keys_and_values((kv_0, kv_1, kv_2, kv_3))
    key_t = keys[0].astype(F32).T.astype(BF16)
    keys_t = (key_t, jnp.concatenate([key_t[HD:], key_t[:HD]], axis=0))
    upper = lane_of((rows, LANES)) >= HD
    upper_t = lax.broadcasted_iota(jnp.int32, (LANES, rows), 0) >= HD
    query_at = block_ref[0] * rows + lax.broadcasted_iota(jnp.int32, (rows, rows), 1)
    key_at = lax.broadcasted_iota(jnp.int32, (rows, rows), 0)
    biases = []
    for place in range(4):
        at = (block_ref[0] ^ place) * rows + key_at
        biases.append(jnp.where((at <= query_at) & (at >= start_ref[0, :1, :]), 0.0, MASKED))
    head_of = lax.broadcasted_iota(jnp.int32, (width, LANES), 0) // HD
    by_head = (head_of == lane_of((width, LANES))).astype(BF16)
    product = back_ref[...].astype(F32) * out_ref[...].astype(F32)
    product_high = product.astype(BF16)
    product_low = (product - product_high.astype(F32)).astype(BF16)
    row_sums = (dot_nn(product_high, by_head) + dot_nn(product_low, by_head)).T
    levels = level_ref[...].T
    cosine, sine = cos_ref[...], sin_ref[...]
    dk_sum[...] = jnp.zeros_like(dk_sum)
    dv_sum[...] = jnp.zeros_like(dv_sum)
    for pair in range(heads // 2):
        at = slice(pair * LANES, (pair + 1) * LANES)
        both = q_ref[:, at]
        back_both = back_ref[:, at]
        zero = jnp.zeros_like(both)
        sides = (~upper, upper)
        queries = [jnp.where(side, both, zero) for side in sides]
        backs = [jnp.where(side, back_both, zero) for side in sides]
        owners = [(2 * pair + place) // group for place in range(2)]
        d_query_t = [jnp.zeros((LANES, rows), F32) for _ in range(2)]
        for piece in range(4):
            span = slice(piece * rows, (piece + 1) * rows)
            probs, d_scores = [], []
            for place in range(2):
                head = 2 * pair + place
                moved = int(owners[place] != place)
                score = dot_nt(keys[moved][span], queries[place]) + biases[piece]
                prob = jnp.exp(score - levels[head : head + 1])
                d_prob = dot_nt(values[moved][span], backs[place])
                d_score = (prob * (d_prob - row_sums[head : head + 1])).astype(BF16)
                d_query_t[place] = d_query_t[place] + dot_nn(keys_t[moved][:, span], d_score)
                probs.append(prob.astype(BF16))
                d_scores.append(d_score)
            if owners[0] == owners[1]:
                dv_sum[owners[0], span] += dot_nn(
                    jnp.concatenate(probs, axis=1), jnp.concatenate(backs, axis=0)
                )
                dk_sum[owners[0], span] += dot_nn(
                    jnp.concatenate(d_scores, axis=1), jnp.concatenate(queries, axis=0)
                )
            else:
                for place in range(2):
                    dv_sum[owners[place], span] += dot_nn(probs[place], backs[place])
                    dk_sum[owners[place], span] += dot_nn(d_scores[place], queries[place])
        d_query = jnp.where(upper_t, d_query_t[1], d_query_t[0]).T * SCALE
        dq_ref[:, at] = (d_query * cosine - swap_halves(d_query) * sine).astype(BF16)
    lower_key = lane_of((4 * rows, LANES)) < HD
    for total, begin in ((dk_sum, 0), (dv_sum, LANES)):
        first, second = total[0], total[1]
        first = first + pltpu.roll(first, HD, 1)
        second = second + pltpu.roll(second, HD, 1)
        both = jnp.where(lower_key, first, second)
        cols = slice(begin, begin + LANES)
        own_ref[:, cols] = both[:rows]
        for place, ref in enumerate((core_ref, x_ref, far_ref)):
            ref[:, cols] = both[(place + 1) * rows : (place + 2) * rows].astype(BF16)


def parts_of(rows, cols):
    shapes = [jax.ShapeDtypeStruct((rows, cols), F32)] + [jax.ShapeDtypeStruct((rows, cols), BF16)] * 3
    return [seq_rows(0, rows, cols)] * 4, shapes


def attend_back(block, q, kv_pieces, back, out, level, start, cosine, sine, rows, seq):
    width = q.shape[1]
    length = 4 * rows
    heads = width // HD
    specs, shapes = parts_of(rows, 2 * LANES)
    return pl.pallas_call(
        attend_back_kernel,
        grid=(1,),
        in_specs=[
            pl.BlockSpec(memory_space=pltpu.SMEM),
            seq_rows(seq, rows, width),
            *[piece_of(seq, rows)] * 4,
            seq_rows(0, rows, width),
            seq_rows(0, rows, width),
            seq_rows(0, rows, LANES),
            pl.BlockSpec((1, 8, rows), lambda i: (seq, 0, 0)),
            seq_rows(seq, rows, LANES),
            seq_rows(seq, rows, LANES),
        ],
        out_specs=[seq_rows(0, rows, width), *specs],
        out_shape=[jax.ShapeDtypeStruct((rows, width), BF16), *shapes],
        scratch_shapes=[
            pltpu.VMEM((2, length, LANES), F32),
            pltpu.VMEM((2, length, LANES), F32),
        ],
        compiler_params=pltpu.CompilerParams(vmem_limit_bytes=VMEM_LIMIT),
        cost_estimate=pl.CostEstimate(
            flops=80 * rows * rows * LANES * heads,
            bytes_accessed=8 * rows * width,
            transcendentals=4 * rows * rows * heads,
        ),
        name="attention_backward",
    )(block, q, *kv_pieces, back, out, level, start, cosine, sine)


def mlp_kernel(
    n_0, n_1, n_2, n_3, c_0, c_1, c_2, c_3, w_ref,
    own_ref, out_1, out_2, out_3, d_own_ref, d_1, d_2, d_3, kept_ref, turned_ref,
    normed_all, cot_all,
):
    step = pl.program_id(0)
    rows = own_ref.shape[0]
    columns = w_ref.shape[1] // 3

    @pl.when(step == 0)
    def _():
        for place, (n_ref, c_ref) in enumerate(zip((n_0, n_1, n_2, n_3), (c_0, c_1, c_2, c_3))):
            normed_all[place // 2, (place % 2) * rows : (place % 2 + 1) * rows] = n_ref[...]
            cot_all[place // 2, (place % 2) * rows : (place % 2 + 1) * rows] = c_ref[...]

    normed, cot = normed_all[step], cot_all[step]
    gate = dot_nn(normed, w_ref[:, :columns])
    up = dot_nn(normed, w_ref[:, columns : 2 * columns])
    d_act = dot_nn(cot, w_ref[:, 2 * columns :])
    sigmoid = 0.5 * jnp.tanh(0.5 * gate) + 0.5
    swish = gate * sigmoid
    kept_ref[0] = (d_act * up * (sigmoid + swish * (1.0 - sigmoid))).astype(BF16)
    kept_ref[1] = (d_act * swish).astype(BF16)
    kept_ref[2] = (swish * up).astype(BF16)
    turned_ref[0] = normed.T
    turned_ref[1] = cot.T
    out = dot_nt(kept_ref[2], w_ref[:, 2 * columns :])
    d_normed = dot_nt(kept_ref[0], w_ref[:, :columns]) + dot_nt(kept_ref[1], w_ref[:, columns : 2 * columns])

    @pl.when(step == 0)
    def _():
        own_ref[...] = out[:rows]
        out_1[...] = out[rows:].astype(BF16)
        d_own_ref[...] = d_normed[:rows]
        d_1[...] = d_normed[rows:].astype(BF16)

    @pl.when(step == 1)
    def _():
        out_2[...] = out[:rows].astype(BF16)
        out_3[...] = out[rows:].astype(BF16)
        d_2[...] = d_normed[:rows].astype(BF16)
        d_3[...] = d_normed[rows:].astype(BF16)


def mlp(normed, cot, weights, seq):
    rows, dim = normed[0].shape
    columns = weights.shape[1] // 3
    specs, shapes = parts_of(rows, dim)
    once = lambda at: pl.BlockSpec((rows, dim), lambda i: (at, 0), pipeline_mode=pl.Buffered(1))
    return pl.pallas_call(
        mlp_kernel,
        grid=(2,),
        in_specs=[
            *[once(0)] * 4,
            *[once(seq)] * 3,
            once(0),
            pl.BlockSpec(weights.shape, lambda i: (0, 0), pipeline_mode=pl.Buffered(1)),
        ],
        out_specs=[
            *specs,
            *specs,
            pl.BlockSpec((3, 2 * rows, columns), lambda i: (0, i, 0)),
            pl.BlockSpec((2, dim, 2 * rows), lambda i: (0, 0, i)),
        ],
        out_shape=[
            *shapes,
            *shapes,
            jax.ShapeDtypeStruct((3, 4 * rows, columns), BF16),
            jax.ShapeDtypeStruct((2, dim, 4 * rows), BF16),
        ],
        scratch_shapes=[
            pltpu.VMEM((2, 2 * rows, dim), BF16),
            pltpu.VMEM((2, 2 * rows, dim), BF16),
        ],
        compiler_params=pltpu.CompilerParams(vmem_limit_bytes=VMEM_LIMIT),
        cost_estimate=pl.CostEstimate(
            flops=48 * rows * dim * columns,
            bytes_accessed=6 * dim * columns + 24 * rows * columns,
            transcendentals=4 * rows * columns,
        ),
        name="feed_forward",
    )(*normed, *cot, weights)


def mlp_grad_kernel(turned_0, turned_1, kept_0, kept_1, grad_ref):
    grad_ref[...] = (dot_nn(turned_0[0], kept_0[0]) + dot_nn(turned_1[0], kept_1[0])).astype(BF16)


def mlp_grad(turned, kept):
    _, dim, count = turned[0].shape
    columns = kept[0].shape[2]
    turned_block = pl.BlockSpec((1, dim, count), lambda i: (i // 2, 0, 0))
    kept_block = pl.BlockSpec((1, count, columns), lambda i: (i, 0, 0))
    return pl.pallas_call(
        mlp_grad_kernel,
        grid=(3,),
        in_specs=[turned_block, turned_block, kept_block, kept_block],
        out_specs=pl.BlockSpec((dim, columns), lambda i: (0, i)),
        out_shape=jax.ShapeDtypeStruct((dim, 3 * columns), BF16),
        compiler_params=pltpu.CompilerParams(vmem_limit_bytes=VMEM_LIMIT),
        cost_estimate=pl.CostEstimate(
            flops=12 * count * dim * columns,
            bytes_accessed=6 * dim * columns + 12 * count * columns,
            transcendentals=0,
        ),
        name="feed_forward_gradients",
    )(*turned, *kept)


def pack_kernel(block_ref, gate_ref, up_ref, down_ref, *refs):
    out_refs, scratch = refs[:4], refs[4]
    shard, ff = gate_ref.shape
    quarter = scratch.shape[2] // 4
    for place, ref in enumerate((gate_ref, up_ref, down_ref)):
        scratch[place, :, :ff] = ref[...].astype(F32)
        scratch[place, :, ff:] = jnp.zeros((shard, 4 * quarter - ff), F32)
    for place, out_ref in enumerate(out_refs):
        begin = pl.multiple_of((block_ref[0] ^ place) * quarter, LANES)
        for part in range(3):
            out_ref[:, part * quarter : (part + 1) * quarter] = scratch[part, :, pl.ds(begin, quarter)].astype(BF16)


def pack(block, gate, up, down_t, quarter):
    shard = gate.shape[0]
    return pl.pallas_call(
        pack_kernel,
        in_specs=[pl.BlockSpec(memory_space=pltpu.SMEM)] + [pl.BlockSpec(memory_space=pltpu.VMEM)] * 3,
        out_specs=[pl.BlockSpec(memory_space=pltpu.VMEM)] * 4,
        out_shape=[jax.ShapeDtypeStruct((shard, 3 * quarter), BF16)] * 4,
        scratch_shapes=[pltpu.VMEM((3, shard, 4 * quarter), F32)],
        compiler_params=pltpu.CompilerParams(vmem_limit_bytes=VMEM_LIMIT),
        name="pack_columns",
    )(block, gate, up, down_t)


def pick(options, index):
    value = options[0]
    for place in range(1, len(options)):
        value = jnp.where(index == place, options[place], value)
    return value


def assemble_kernel(block_ref, *refs):
    pieces, out_ref, scratch = refs[:4], refs[4], refs[5]
    shard = pieces[0].shape[0]
    values = [ref[...].astype(F32) for ref in pieces]
    for owner in range(4):
        scratch[owner * shard : (owner + 1) * shard] = pick(values, block_ref[0] ^ owner)
    out_ref[...] = scratch[...].astype(BF16)


def assemble(block, pieces):
    shard, columns = pieces[0].shape
    return pl.pallas_call(
        assemble_kernel,
        in_specs=[pl.BlockSpec(memory_space=pltpu.SMEM)] + [pl.BlockSpec(memory_space=pltpu.VMEM)] * 4,
        out_specs=pl.BlockSpec(memory_space=pltpu.VMEM),
        out_shape=jax.ShapeDtypeStruct((4 * shard, columns), BF16),
        scratch_shapes=[pltpu.VMEM((4 * shard, columns), F32)],
        compiler_params=pltpu.CompilerParams(vmem_limit_bytes=VMEM_LIMIT),
        name="assemble_rows",
    )(block, *pieces)


def cut_kernel(block_ref, value_ref, *refs):
    out_refs, scratch = refs[:4], refs[4]
    shard = out_refs[0].shape[0]
    scratch[...] = value_ref[...].astype(F32)
    values = [scratch[owner * shard : (owner + 1) * shard] for owner in range(4)]
    for place, out_ref in enumerate(out_refs):
        out_ref[...] = pick(values, block_ref[0] ^ place).astype(BF16)


def cut(block, value):
    shard, columns = value.shape[0] // 4, value.shape[1]
    return pl.pallas_call(
        cut_kernel,
        in_specs=[pl.BlockSpec(memory_space=pltpu.SMEM), pl.BlockSpec(memory_space=pltpu.VMEM)],
        out_specs=[pl.BlockSpec(memory_space=pltpu.VMEM)] * 4,
        out_shape=[jax.ShapeDtypeStruct((shard, columns), BF16)] * 4,
        scratch_shapes=[pltpu.VMEM(value.shape, F32)],
        compiler_params=pltpu.CompilerParams(vmem_limit_bytes=VMEM_LIMIT),
        name="cut_rows",
    )(block, value)


def unpack_kernel(block_ref, *refs):
    pieces, out_refs, scratch = refs[:4], refs[4:7], refs[7]
    ff = out_refs[0].shape[1]
    quarter = scratch.shape[2] // 4
    for place, ref in enumerate(pieces):
        begin = pl.multiple_of((block_ref[0] ^ place) * quarter, LANES)
        for part in range(3):
            scratch[part, :, pl.ds(begin, quarter)] = ref[:, part * quarter : (part + 1) * quarter].astype(F32)
    for part, out_ref in enumerate(out_refs):
        out_ref[...] = scratch[part, :, :ff]


def unpack(block, pieces, ff):
    shard, columns = pieces[0].shape
    return pl.pallas_call(
        unpack_kernel,
        in_specs=[pl.BlockSpec(memory_space=pltpu.SMEM)] + [pl.BlockSpec(memory_space=pltpu.VMEM)] * 4,
        out_specs=[pl.BlockSpec(memory_space=pltpu.VMEM)] * 3,
        out_shape=[jax.ShapeDtypeStruct((shard, ff), F32)] * 3,
        scratch_shapes=[pltpu.VMEM((3, shard, columns // 3 * 4), F32)],
        compiler_params=pltpu.CompilerParams(vmem_limit_bytes=VMEM_LIMIT),
        name="unpack_columns",
    )(block, *pieces)


def bit_swap(value, axis, bit=0):
    size = lax.axis_size(axis)
    return lax.ppermute(value, axis, [(i, i ^ (1 << bit)) for i in range(size)])


def jump_swap(value, axes, jump):
    return lax.ppermute(value, axes, [(i, i ^ jump) for i in range(4)])


def to_plane(value, slot):
    high, low = slot >> 1, slot & 1
    pairs = [
        (4 * y + 2 * x + c, 4 * (c ^ low) + 2 * (x ^ high) + y) for y in range(2) for x in range(2) for c in range(2)
    ]
    return lax.ppermute(value, TOKENS + ("cc",), pairs)


def from_plane(value, slot):
    high, low = slot >> 1, slot & 1
    pairs = [
        (4 * y + 2 * x + c, 4 * c + 2 * (x ^ high) + (y ^ low)) for y in range(2) for x in range(2) for c in range(2)
    ]
    return lax.ppermute(value, TOKENS + ("cc",), pairs)


def after(first, *values):
    return lax.optimization_barrier((first, *values))


def gather_four(value, axes):
    from_first = bit_swap(value, axes[0])
    return [value, bit_swap(value, axes[1]), from_first, bit_swap(from_first, axes[1])]


def gather_direct(value, axes):
    return [value] + [jump_swap(value, axes, jump) for jump in range(1, 4)]


def sum_direct(axes, own, *away):
    return [own] + [jump_swap(value, axes, jump + 1) for jump, value in enumerate(away)]


def doubling_offsets(steps):
    weight = {"cc": 1, "cx": 2, "fy": 4, "fz": 8}
    offsets = [0]
    for axis, bit in steps:
        offsets += [offset ^ (weight[axis] << bit) for offset in offsets]
    return jnp.array(offsets, jnp.int32)


def double(value, axis, bit=0):
    return jnp.concatenate([value, bit_swap(value, axis, bit)], axis=0)


def plane_gather(value):
    return jnp.concatenate(gather_direct(value, TOKENS), axis=0)


def plane_sum(value):
    parts = jnp.split(value, 4, axis=0)
    terms = sum_direct(TOKENS, *parts)
    return sum(term.astype(F32) for term in terms).astype(BF16)


def core_sum(keep, send):
    return (keep.astype(F32) + bit_swap(send.astype(BF16), "cc").astype(F32)).astype(BF16)


def halve(value, axis, bit=0):
    middle = value.shape[0] // 2
    came = bit_swap(value[middle:], axis, bit)
    return (value[:middle].astype(F32) + came.astype(F32)).astype(BF16)


def on_device(
    hidden,
    segments,
    attn_gain,
    qkv_weight,
    qkv_bias,
    out_weight,
    mlp_gain,
    gate_weight,
    up_weight,
    down_weight,
    cotangent,
):
    seqs, rows, dim = hidden.shape
    count = seqs * rows
    shard = attn_gain.shape[0]
    world = dim // shard
    joint = qkv_weight.shape[1]
    width = joint - 2 * LANES
    ff = gate_weight.shape[1]
    block = lax.axis_index("cx") * lax.axis_size("cc") + lax.axis_index("cc")
    me = lax.axis_index(FSDP) * lax.axis_size(CTX) + block
    offset = block * rows
    block_arg = block.reshape(1).astype(jnp.int32)
    plane_arg = (lax.axis_index("cx") * 2 + lax.axis_index("fy")).reshape(1).astype(jnp.int32)
    x = hidden.reshape(count, dim)
    cot = cotangent.reshape(count, dim)

    cot_x = bit_swap(cot, "cx")

    far = [("fz", bit) for bit in reversed(range((lax.axis_size("fz")).bit_length() - 1))]
    padded = -(-(shard + 1) // 16) * 16
    small = jnp.concatenate([attn_gain, mlp_gain, qkv_bias])
    small_row = jnp.pad(small, (0, joint + width - small.shape[0]))[None]
    first = jnp.concatenate(
        [
            jnp.concatenate([qkv_weight, out_weight.T], axis=1),
            small_row,
            jnp.zeros((padded - shard - 1, joint + width), BF16),
        ],
        axis=0,
    )
    first = double(first, *far[0])

    quarter = -(-ff // (4 * TILE)) * TILE
    first, *pieces = after(first, *pack(block_arg, gate_weight, up_weight, down_weight.T, quarter))
    pieces = [to_plane(piece, slot) for slot, piece in enumerate(pieces)]
    for axis, bit in far[1:]:
        first = double(first, axis, bit)

    within = jnp.arange(padded, dtype=jnp.int32)
    owner = me ^ doubling_offsets(far + [("cx", 0), ("fy", 0), ("cc", 0)])
    target = jnp.where(within[None, :] < shard, owner[:, None] * shard + within[None, :], -1).reshape(1, -1)
    order = (jnp.arange(dim, dtype=jnp.int32)[:, None] == target).astype(BF16)
    place = jnp.where(within[None, :] == shard, owner[:, None], -1).reshape(1, -1)
    spread = (jnp.arange(world, dtype=jnp.int32)[:, None] == place).astype(BF16)

    at_row = lax.dynamic_slice_in_dim(segments, offset, rows, axis=1)
    zeros_before = jnp.sum((segments < 1).astype(jnp.int32), axis=1, keepdims=True)
    ones_before = jnp.sum((segments < 2).astype(jnp.int32), axis=1, keepdims=True)
    start = jnp.where(at_row == 0, 0, jnp.where(at_row == 1, zeros_before, ones_before))
    position = (offset + jnp.arange(rows, dtype=jnp.int32)[None, :] - start).reshape(count)
    lane = jnp.arange(LANES, dtype=jnp.int32)
    frequency = ROPE_BASE ** (-(lane % (HD // 2)).astype(F32) * 2.0 / HD)
    angle = position.astype(F32)[:, None] * frequency[None, :]
    cosine = jnp.cos(angle)
    sine = jnp.where(lane % HD < HD // 2, -1.0, 1.0)[None, :] * jnp.sin(angle)
    start_column = jnp.broadcast_to(start.reshape(count, 1), (count, LANES))
    start_row = jnp.broadcast_to(start[:, None, :], (seqs, 8, rows))

    first, cot_x, cot_late, order, spread, cosine, sine, start_column, *pieces = after(
        first, cot_x, cot, order, spread, cosine, sine, start_column, *pieces
    )
    w_joint = plane_gather(first[:, :joint])
    mlp_shard = assemble(plane_arg, pieces)
    mlp_weights = lax.all_gather(mlp_shard, WEIGHTS, axis=0, tiled=True)
    w_joint, cot_late = after(w_joint, cot_late)
    w_joint = (w_joint, bit_swap(w_joint, "cc"))
    cot_y = bit_swap(cot_late, "fy")

    normed_low, normed_high, q, kv, gain_attn, gain_mlp = prep(x, order, spread, w_joint, cosine, sine, rows)
    kv_all = gather_four(kv.reshape(seqs, rows, 2 * LANES), CTX)
    kv_all[3], out_rows, cot_y = after(kv_all[3], first[:, joint:], cot_y)
    w_out = plane_gather(out_rows)
    attended, levels, resid, normed_all = [], [], [], []
    for seq in range(seqs):
        turn = block_arg if seq == 0 else after(resid[0], block_arg)[1]
        attended_one, level_one = attend(turn, q, kv_all, start_column, rows, seq)
        if seq == 0:
            attended_one, w_out, far_0, far_1 = after(attended_one, w_out, cot_x[:rows], cot_y[rows:])
            cot_far = [bit_swap(far_0, "fy"), bit_swap(far_1, "cx")]
            w_out = (w_out, bit_swap(w_out, "cc"))
        else:
            attended_one, *cot_far = after(attended_one, *cot_far)
        attended.append(attended_one)
        levels.append(level_one)
        resid_one, normed_one = project_out(attended[seq], x, w_out, order, gain_mlp, rows, seq)
        resid.append(resid_one)
        normed_all.append(gather_direct(normed_one, TOKENS))

    out_parts, d_terms, kept, turned = [], [], [], []
    for seq in range(seqs):
        if seq == 1:
            out_parts[0], normed_all[1] = lax.optimization_barrier((out_parts[0], normed_all[1]))
        result = mlp(normed_all[seq], [cot, cot_x, cot_y, cot_far[seq]], mlp_weights, seq)
        out_parts.append(result[:4])
        d_terms.append(sum_direct(TOKENS, *result[4:8]))
        kept.append(result[8])
        turned.append(result[9])
    d_resid, d_low, d_high, d_attended, mlp_gain_grad, dq, dkv_terms, out_terms = [], [], [], [], [], [], [], []
    for seq in range(seqs):
        if seq == 0:
            _, *d_terms[0] = after(kept[1], *d_terms[0])
        else:
            dq[0], d_terms[1][0], *out_terms[0] = after(dq[0], d_terms[1][0], *out_terms[0])
        result = project_out_back(d_terms[seq], resid[seq], cot, w_out, order, gain_mlp, rows, seq)
        for place, value in zip((d_resid, d_low, d_high, d_attended, mlp_gain_grad), result):
            place.append(value)
        out_terms.append(sum_direct(TOKENS, *after(d_terms[seq][1], *out_parts[seq])[1:]))
        if seq == 0:
            _, turned[1] = after(d_resid[0], turned[1])
            grads = mlp_grad(turned, kept)
            grads, d_attended[0], *d_terms[1] = after(grads, d_attended[0], *d_terms[1])
            grads = lax.psum_scatter(
                grads.reshape(world // 4, 4 * shard, 3 * quarter), WEIGHTS, scatter_dimension=0, tiled=False
            )
        else:
            both = jnp.concatenate(attended, axis=0)
            out_grad = core_sum(
                dot_tn(jnp.concatenate(d_low, axis=0), both).astype(BF16), dot_tn(jnp.concatenate(d_high, axis=0), both)
            )
            d_attended[1], *dkv_terms[0] = after(d_attended[1], *dkv_terms[0])
        result = attend_back(
            block_arg, q, kv_all, d_attended[seq], attended[seq], levels[seq], start_row, cosine, sine, rows, seq
        )
        dq.append(result[0])
        dkv_terms.append(sum_direct(CTX, *result[1:]))
    dq[1], out_grad, *out_terms[1] = after(dq[1], out_grad, *out_terms[1])
    dq_both = jnp.concatenate(dq, axis=0)
    q_grad = core_sum(dot_tn(normed_low, dq_both).astype(BF16), dot_tn(normed_high, dq_both))
    q_grad, *dkv_terms[1] = after(q_grad, *dkv_terms[1])
    q_grad = plane_sum(q_grad)
    d_resid = jnp.concatenate(d_resid, axis=0)
    d_kv, input_grad, attn_gain_grad, bias_grad = input_back(
        dq, dkv_terms, x, d_resid, w_joint, order, gain_attn, cosine, sine
    )
    d_kv, q_grad, attn_gain_grad, bias_grad = after(d_kv, q_grad, attn_gain_grad, bias_grad)

    split_at = width + LANES
    bias_grad = bias_grad[0]
    small_grads = jnp.concatenate(
        [
            attn_gain_grad.reshape(world, -1),
            sum(mlp_gain_grad).reshape(world, -1),
            bias_grad[:split_at].reshape(world, -1),
            bias_grad[split_at:].reshape(world, -1),
        ],
        axis=1,
    ).astype(BF16)
    small_count = small_grads.shape[1]
    small_grads = jnp.pad(small_grads, ((0, 0), (0, 2 * LANES - small_count)))
    middle = spread.shape[1] // 2
    kv_grad = core_sum(
        (dot_tn(normed_low, d_kv) + dot_tn(spread[:, :middle], small_grads)).astype(BF16),
        dot_tn(normed_high, d_kv) + dot_tn(spread[:, middle:], small_grads),
    )
    pieces = cut(plane_arg, lax.optimization_barrier(grads))
    kv_grad, *pieces = after(kv_grad, *pieces)
    pieces = [from_plane(piece, slot) for slot, piece in enumerate(pieces)]
    kv_grad, out_grad = plane_sum(kv_grad), plane_sum(out_grad)
    first_sum = jnp.concatenate([q_grad, kv_grad, out_grad], axis=1)
    first_sum, out_terms = lax.optimization_barrier((first_sum, out_terms))
    for axis, bit in reversed(far):
        first_sum = halve(first_sum, axis, bit)
    output = []
    for seq in range(seqs):
        own, *away = out_terms[seq]
        output.append((resid[seq] + own + sum(term.astype(F32) for term in away)).astype(BF16))

    gate_grad, up_grad, down_grad_t = unpack(block_arg, pieces, ff)
    first_sum = first_sum.astype(F32)
    qkv_sum, out_sum = first_sum[:, :joint], first_sum[:, joint:]
    small_sum = qkv_sum[shard, width : width + small_count]
    at = (shard, 2 * shard, 2 * shard + split_at // world)

    return (
        jnp.stack(output),
        input_grad.reshape(hidden.shape),
        small_sum[: at[0]],
        qkv_sum[:shard],
        small_sum[at[1] : at[2]],
        small_sum[at[2] :],
        out_sum[:shard].T,
        small_sum[at[0] : at[1]],
        gate_grad,
        up_grad,
        down_grad_t.T,
    )


def solution(mesh):
    fsdp, ctx = mesh.shape["fsdp"], mesh.shape["ctx"]
    inner = Mesh(mesh.devices.reshape(fsdp // 2, 2, 2, ctx // 2), AXES)
    tokens = P(FSDP, CTX, None)
    vector = P(AXES)
    by_row = P(AXES, None)
    by_column = P(None, AXES)
    return jax.shard_map(
        on_device,
        mesh=inner,
        in_specs=(
            tokens,
            P(FSDP, None),
            vector,
            by_row,
            vector,
            by_column,
            vector,
            by_row,
            by_row,
            by_column,
            tokens,
        ),
        out_specs=(
            tokens,
            tokens,
            vector,
            by_row,
            vector,
            vector,
            by_column,
            vector,
            by_row,
            by_row,
            by_column,
        ),
        check_vma=False,
    )
```

```python
import functools

import jax
import jax.numpy as jnp
from jax import lax
from jax.experimental import pallas as pl
from jax.experimental.pallas import tpu as pltpu
from jax.sharding import Mesh
from jax.sharding import PartitionSpec as P

HD = 64
LANES = 128
EPSILON = 1e-06
ROPE_BASE = 1000000.0
MASKED = -1e30
SCALE = HD ** (-0.5)
TILE = 256
MIB = 1 << 20
VMEM_LIMIT = 60 * MIB
F32 = jnp.float32
BF16 = jnp.bfloat16
AXES = ("fz", "fy", "cx", "cc")
FSDP = ("fz", "fy")
CTX = ("cx", "cc")
TOKENS = ("fy", "cx")
WEIGHTS = ("fz", "cc")


def dot_nn(a, b):
    return lax.dot_general(a, b, (((1,), (0,)), ((), ())), preferred_element_type=F32)


def dot_nt(a, b):
    return lax.dot_general(a, b, (((1,), (1,)), ((), ())), preferred_element_type=F32)


def dot_tn(a, b):
    return lax.dot_general(a, b, (((0,), (0,)), ((), ())), preferred_element_type=F32)


def lane_of(shape):
    return lax.broadcasted_iota(jnp.int32, shape, len(shape) - 1)


def swap_halves(block):
    lead = lane_of(block.shape) % HD < HD // 2
    return jnp.where(
        lead, pltpu.roll(block, LANES - HD // 2, 1), pltpu.roll(block, HD // 2, 1)
    )


def other_head(block):
    return jnp.concatenate([block[:, HD:], block[:, :HD]], axis=1)


def read_out(extras, first, piece, total):
    owners, columns = extras.shape
    at = lax.broadcasted_iota(jnp.int32, (columns, total), 1) % piece + first
    chosen = (lax.broadcasted_iota(jnp.int32, (columns, total), 0) == at).astype(BF16)
    spread = dot_nn(extras, chosen)
    owner = lax.broadcasted_iota(jnp.int32, (owners, total), 1) // piece
    mine = owner == lax.broadcasted_iota(jnp.int32, (owners, total), 0)
    return jnp.sum(jnp.where(mine, spread, 0.0), axis=0, keepdims=True)


def prep_kernel(
    x_ref, order_ref, spread_ref, w_low_ref, w_high_ref, cos_ref, sin_ref,
    normed_low_ref, normed_high_ref, q_ref, kv_ref, gain_ref, gain_mlp_ref, bias_ref,
):
    x = x_ref[...].astype(F32)
    dim = x.shape[1]
    width = q_ref.shape[1]
    joint = w_low_ref.shape[1]
    middle = w_low_ref.shape[0]
    owners = spread_ref.shape[0]

    @pl.when(pl.program_id(0) == 0)
    def _():
        extras = dot_nn(spread_ref[:, :middle], w_low_ref[:, :LANES])
        extras = (extras + dot_nn(spread_ref[:, middle:], w_high_ref[:, :LANES])).astype(BF16)
        shard = dim // owners
        gain_ref[...] = read_out(extras, 0, shard, dim)
        gain_mlp_ref[...] = read_out(extras, shard, shard, dim)
        bias_ref[...] = read_out(extras, 2 * shard, joint // owners, joint)

    gain, bias = gain_ref[...], bias_ref[...]
    inverse = lax.rsqrt(jnp.mean(x * x, axis=-1, keepdims=True) + EPSILON)
    normed = (x * inverse * gain).astype(BF16)
    ordered = dot_nn(normed, order_ref[...]).astype(BF16)
    normed_low_ref[...] = ordered[:, :middle]
    normed_high_ref[...] = ordered[:, middle:]
    joined = dot_nn(ordered[:, :middle], w_low_ref[...])
    joined = joined + dot_nn(ordered[:, middle:], w_high_ref[...]) + bias
    cosine, sine = cos_ref[...], sin_ref[...]
    for begin in range(0, width + LANES, LANES):
        block = joined[:, begin : begin + LANES]
        turned = block * cosine + swap_halves(block) * sine
        if begin < width:
            q_ref[:, begin : begin + LANES] = (turned * SCALE).astype(BF16)
        else:
            kv_ref[:, :LANES] = turned.astype(BF16)
    kv_ref[:, LANES:] = joined[:, width + LANES :].astype(BF16)


def rows_of(rows, cols):
    return pl.BlockSpec((rows, cols), lambda i: (i, 0))


def whole(value):
    return pl.BlockSpec(value.shape, lambda i: (0,) * value.ndim)


def prep(x, order, spread, weights, cosine, sine, rows):
    count, dim = x.shape
    ordered = order.shape[1]
    joint = weights[0].shape[1]
    width = joint - 2 * LANES
    row = pl.BlockSpec((1, dim), lambda i: (0, 0))
    return pl.pallas_call(
        prep_kernel,
        grid=(count // rows,),
        in_specs=[
            rows_of(rows, dim),
            whole(order),
            whole(spread),
            whole(weights[0]),
            whole(weights[1]),
            rows_of(rows, LANES),
            rows_of(rows, LANES),
        ],
        out_specs=[
            rows_of(rows, ordered // 2),
            rows_of(rows, ordered // 2),
            rows_of(rows, width),
            rows_of(rows, 2 * LANES),
            row,
            row,
        ],
        out_shape=[
            jax.ShapeDtypeStruct((count, ordered // 2), BF16),
            jax.ShapeDtypeStruct((count, ordered // 2), BF16),
            jax.ShapeDtypeStruct((count, width), BF16),
            jax.ShapeDtypeStruct((count, 2 * LANES), BF16),
            jax.ShapeDtypeStruct((1, dim), F32),
            jax.ShapeDtypeStruct((1, dim), F32),
        ],
        scratch_shapes=[pltpu.VMEM((1, joint), F32)],
        compiler_params=pltpu.CompilerParams(vmem_limit_bytes=VMEM_LIMIT),
        cost_estimate=pl.CostEstimate(
            flops=2 * count * ordered * (joint + dim), bytes_accessed=12 * MIB, transcendentals=0
        ),
        name="norm_project_rotate",
    )(x, order, spread, weights[0], weights[1], cosine, sine)


def back_in_order(value, order):
    high = value.astype(BF16)
    low = (value - high.astype(F32)).astype(BF16)
    return dot_nt(high, order) + dot_nt(low, order)


def out_kernel(attended_ref, x_ref, w_low_ref, w_high_ref, order_ref, gain_ref, resid_ref, normed_ref):
    attended = attended_ref[...]
    branch = jnp.concatenate([dot_nt(attended, w_low_ref[...]), dot_nt(attended, w_high_ref[...])], axis=1)
    resid = x_ref[...].astype(F32) + back_in_order(branch, order_ref[...])
    inverse = lax.rsqrt(jnp.mean(resid * resid, axis=-1, keepdims=True) + EPSILON)
    resid_ref[...] = resid
    normed_ref[...] = (resid * inverse * gain_ref[...]).astype(BF16)


def project_out(attended, x, weights, order, gain, rows, seq):
    dim = x.shape[1]
    count = rows
    return pl.pallas_call(
        out_kernel,
        grid=(1,),
        in_specs=[
            rows_of(rows, attended.shape[1]),
            pl.BlockSpec((rows, dim), lambda i: (seq, 0)),
            whole(weights[0]),
            whole(weights[1]),
            whole(order),
            whole(gain),
        ],
        out_specs=[rows_of(rows, dim), rows_of(rows, dim)],
        out_shape=[jax.ShapeDtypeStruct((count, dim), F32), jax.ShapeDtypeStruct((count, dim), BF16)],
        compiler_params=pltpu.CompilerParams(vmem_limit_bytes=VMEM_LIMIT),
        cost_estimate=pl.CostEstimate(flops=6 * count * dim * dim, bytes_accessed=8 * MIB, transcendentals=0),
        name="project_out_norm",
    )(attended, x, weights[0], weights[1], order, gain)


def sum_rows(value):
    return jnp.sum(value, axis=0, keepdims=True)


def norm_back(values, inverse, gain, incoming):
    scaled = incoming * gain
    mean_term = jnp.mean(scaled * values, axis=-1, keepdims=True)
    return inverse * scaled - values * inverse**3 * mean_term


def total_of(own_ref, *away_refs):
    total = own_ref[...]
    for ref in away_refs:
        total = total + ref[...].astype(F32)
    return total


def out_back_kernel(
    own_ref, core_ref, x_ref, far_ref, resid_ref, cot_ref, w_low_ref, w_high_ref, order_ref, gain_ref,
    d_resid_ref, d_low_ref, d_high_ref, d_attended_ref, gain_grad_ref,
):
    middle = w_low_ref.shape[0]
    d_normed = total_of(own_ref, core_ref, x_ref, far_ref)
    resid = resid_ref[...]
    inverse = lax.rsqrt(jnp.mean(resid * resid, axis=-1, keepdims=True) + EPSILON)
    d_resid = cot_ref[...].astype(F32) + norm_back(resid, inverse, gain_ref[...], d_normed)
    d_resid_ref[...] = d_resid
    d_branch = dot_nn(d_resid.astype(BF16), order_ref[...]).astype(BF16)
    d_low_ref[...] = d_branch[:, :middle]
    d_high_ref[...] = d_branch[:, middle:]
    d_attended = dot_nn(d_branch[:, :middle], w_low_ref[...])
    d_attended = d_attended + dot_nn(d_branch[:, middle:], w_high_ref[...])
    d_attended_ref[...] = d_attended.astype(BF16)
    gain_grad_ref[...] = sum_rows(d_normed * resid * inverse)


def project_out_back(terms, resid, cot, weights, order, gain, rows, seq):
    count, dim = resid.shape
    ordered = order.shape[1]
    width = dim
    return pl.pallas_call(
        out_back_kernel,
        grid=(1,),
        in_specs=[
            rows_of(rows, dim),
            rows_of(rows, dim),
            rows_of(rows, dim),
            rows_of(rows, dim),
            rows_of(rows, dim),
            pl.BlockSpec((rows, dim), lambda i: (seq, 0)),
            whole(weights[0]),
            whole(weights[1]),
            whole(order),
            whole(gain),
        ],
        out_specs=[
            rows_of(rows, dim),
            rows_of(rows, ordered // 2),
            rows_of(rows, ordered // 2),
            rows_of(rows, width),
            pl.BlockSpec((1, dim), lambda i: (0, 0)),
        ],
        out_shape=[
            jax.ShapeDtypeStruct((count, dim), F32),
            jax.ShapeDtypeStruct((count, ordered // 2), BF16),
            jax.ShapeDtypeStruct((count, ordered // 2), BF16),
            jax.ShapeDtypeStruct((count, width), BF16),
            jax.ShapeDtypeStruct((1, dim), F32),
        ],
        compiler_params=pltpu.CompilerParams(vmem_limit_bytes=VMEM_LIMIT),
        cost_estimate=pl.CostEstimate(flops=4 * count * dim * dim, bytes_accessed=12 * MIB, transcendentals=0),
        name="norm_back_project",
    )(*terms, resid, cot, weights[0], weights[1], order, gain)


def call_whole(kernel, operands, out_shape, flops, name):
    return pl.pallas_call(
        kernel,
        in_specs=[pl.BlockSpec(memory_space=pltpu.VMEM)] * len(operands),
        out_specs=[pl.BlockSpec(memory_space=pltpu.VMEM)] * len(out_shape),
        out_shape=out_shape,
        compiler_params=pltpu.CompilerParams(vmem_limit_bytes=VMEM_LIMIT),
        cost_estimate=pl.CostEstimate(flops=flops, bytes_accessed=16 * MIB, transcendentals=0),
        name=name,
    )(*operands)


def input_back_kernel(*refs):
    dqs, terms = refs[:2], refs[2:10]
    x_ref, d_resid_ref, w_low_ref, w_high_ref, order_ref, gain_ref, cos_ref, sin_ref = refs[10:18]
    d_kv_ref, input_grad_ref, gain_grad_ref, bias_grad_ref = refs[18:]
    dkv = jnp.concatenate([total_of(*terms[:4]), total_of(*terms[4:])], axis=0)
    dk = dkv[:, :LANES]
    dk = dk * cos_ref[...] - swap_halves(dk) * sin_ref[...]
    d_kv = jnp.concatenate([dk.astype(BF16), dkv[:, LANES:].astype(BF16)], axis=1)
    d_kv_ref[...] = d_kv
    dq = jnp.concatenate([ref[...] for ref in dqs], axis=0)
    d_joined = jnp.concatenate([dq, d_kv], axis=1)
    d_normed = jnp.concatenate([dot_nt(d_joined, w_low_ref[...]), dot_nt(d_joined, w_high_ref[...])], axis=1)
    d_normed = back_in_order(d_normed, order_ref[...])
    x = x_ref[...].astype(F32)
    inverse = lax.rsqrt(jnp.mean(x * x, axis=-1, keepdims=True) + EPSILON)
    input_grad_ref[...] = (d_resid_ref[...] + norm_back(x, inverse, gain_ref[...], d_normed)).astype(BF16)
    gain_grad_ref[...] = sum_rows(d_normed * x * inverse)
    bias_grad_ref[...] = sum_rows(d_joined.astype(F32))


def input_back(dq, terms, x, d_resid, weights, order, gain, cosine, sine):
    count, dim = x.shape
    joint = dq[0].shape[1] + 2 * LANES
    return call_whole(
        input_back_kernel,
        (*dq, *terms[0], *terms[1], x, d_resid, *weights, order, gain, cosine, sine),
        [
            jax.ShapeDtypeStruct((count, 2 * LANES), BF16),
            jax.ShapeDtypeStruct((count, dim), BF16),
            jax.ShapeDtypeStruct((1, dim), F32),
            jax.ShapeDtypeStruct((1, joint), F32),
        ],
        6 * count * dim * joint,
        "input_gradient",
    )


def seq_rows(seq, rows, cols):
    return pl.BlockSpec((rows, cols), lambda i: (seq, 0))


def piece_of(seq, rows):
    return pl.BlockSpec((1, rows, 2 * LANES), lambda i: (seq, 0, 0))


def keys_and_values(piece_refs):
    joint = jnp.concatenate([ref[0] for ref in piece_refs], axis=0)
    key, value = joint[:, :LANES], joint[:, LANES:]
    return (key, other_head(key)), (value, other_head(value))


def attend_kernel(block_ref, q_ref, kv_0, kv_1, kv_2, kv_3, start_ref, out_ref, level_ref):
    rows, width = q_ref.shape
    length = 4 * rows
    heads = width // HD
    group = heads // 2
    keys, values = keys_and_values((kv_0, kv_1, kv_2, kv_3))
    upper_key = lane_of((length, LANES)) >= HD
    upper = lane_of((rows, LANES)) >= HD
    query_at = block_ref[0] * rows + lax.broadcasted_iota(jnp.int32, (rows, length), 0)
    key_at = jnp.concatenate(
        [
            (block_ref[0] ^ place) * rows + lax.broadcasted_iota(jnp.int32, (rows, rows), 1)
            for place in range(4)
        ],
        axis=1,
    )
    allowed = (key_at <= query_at) & (key_at >= start_ref[:, :1])
    bias = jnp.where(allowed, 0.0, MASKED)
    one = jnp.ones((), BF16)
    lane = lane_of((rows, LANES))
    levels = jnp.zeros((rows, LANES), F32)
    for pair in range(heads // 2):
        at = slice(pair * LANES, (pair + 1) * LANES)
        both = q_ref[:, at]
        parts = []
        for place in range(2):
            owner = (2 * pair + place) // group
            moved = int(owner != place)
            side = upper if place else ~upper
            side_key = upper_key if place else ~upper_key
            query = jnp.where(side, both, jnp.zeros_like(both))
            score = dot_nt(query, keys[moved]) + bias
            top = jnp.max(score, axis=1, keepdims=True)
            weight = jnp.exp(score - top).astype(BF16)
            mixed = dot_nn(weight, jnp.where(side_key, values[moved], one))
            total = pltpu.roll(mixed, HD, 1)
            parts.append(mixed / total)
            level = top + jnp.log(total[:, place * HD : place * HD + 1])
            levels = jnp.where(lane == 2 * pair + place, level, levels)
        out_ref[:, at] = jnp.where(upper, parts[1], parts[0]).astype(BF16)
    level_ref[...] = levels


def attend(block, q, kv_pieces, start, rows, seq):
    width = q.shape[1]
    heads = width // HD
    return pl.pallas_call(
        attend_kernel,
        grid=(1,),
        in_specs=[
            pl.BlockSpec(memory_space=pltpu.SMEM),
            seq_rows(seq, rows, width),
            *[piece_of(seq, rows)] * 4,
            seq_rows(seq, rows, LANES),
        ],
        out_specs=[seq_rows(0, rows, width), seq_rows(0, rows, LANES)],
        out_shape=[jax.ShapeDtypeStruct((rows, width), BF16), jax.ShapeDtypeStruct((rows, LANES), F32)],
        compiler_params=pltpu.CompilerParams(vmem_limit_bytes=VMEM_LIMIT),
        cost_estimate=pl.CostEstimate(
            flops=32 * rows * rows * LANES * heads,
            bytes_accessed=4 * rows * width,
            transcendentals=4 * rows * rows * heads,
        ),
        name="attention_forward",
    )(block, q, *kv_pieces, start)


def attend_back_kernel(
    block_ref, q_ref, kv_0, kv_1, kv_2, kv_3, back_ref, out_ref, level_ref, start_ref, cos_ref, sin_ref,
    dq_ref, own_ref, core_ref, x_ref, far_ref, dk_sum, dv_sum,
):
    rows, width = q_ref.shape
    heads = width // HD
    group = heads // 2
    keys, values = keys_and_values((kv_0, kv_1, kv_2, kv_3))
    key_t = keys[0].astype(F32).T.astype(BF16)
    keys_t = (key_t, jnp.concatenate([key_t[HD:], key_t[:HD]], axis=0))
    upper = lane_of((rows, LANES)) >= HD
    upper_t = lax.broadcasted_iota(jnp.int32, (LANES, rows), 0) >= HD
    query_at = block_ref[0] * rows + lax.broadcasted_iota(jnp.int32, (rows, rows), 1)
    key_at = lax.broadcasted_iota(jnp.int32, (rows, rows), 0)
    biases = []
    for place in range(4):
        at = (block_ref[0] ^ place) * rows + key_at
        biases.append(jnp.where((at <= query_at) & (at >= start_ref[0, :1, :]), 0.0, MASKED))
    head_of = lax.broadcasted_iota(jnp.int32, (width, LANES), 0) // HD
    by_head = (head_of == lane_of((width, LANES))).astype(BF16)
    product = back_ref[...].astype(F32) * out_ref[...].astype(F32)
    product_high = product.astype(BF16)
    product_low = (product - product_high.astype(F32)).astype(BF16)
    row_sums = (dot_nn(product_high, by_head) + dot_nn(product_low, by_head)).T
    levels = level_ref[...].T
    cosine, sine = cos_ref[...], sin_ref[...]
    dk_sum[...] = jnp.zeros_like(dk_sum)
    dv_sum[...] = jnp.zeros_like(dv_sum)
    for pair in range(heads // 2):
        at = slice(pair * LANES, (pair + 1) * LANES)
        both = q_ref[:, at]
        back_both = back_ref[:, at]
        zero = jnp.zeros_like(both)
        sides = (~upper, upper)
        queries = [jnp.where(side, both, zero) for side in sides]
        backs = [jnp.where(side, back_both, zero) for side in sides]
        owners = [(2 * pair + place) // group for place in range(2)]
        d_query_t = [jnp.zeros((LANES, rows), F32) for _ in range(2)]
        for piece in range(4):
            span = slice(piece * rows, (piece + 1) * rows)
            probs, d_scores = [], []
            for place in range(2):
                head = 2 * pair + place
                moved = int(owners[place] != place)
                score = dot_nt(keys[moved][span], queries[place]) + biases[piece]
                prob = jnp.exp(score - levels[head : head + 1])
                d_prob = dot_nt(values[moved][span], backs[place])
                d_score = (prob * (d_prob - row_sums[head : head + 1])).astype(BF16)
                d_query_t[place] = d_query_t[place] + dot_nn(keys_t[moved][:, span], d_score)
                probs.append(prob.astype(BF16))
                d_scores.append(d_score)
            if owners[0] == owners[1]:
                dv_sum[owners[0], span] += dot_nn(
                    jnp.concatenate(probs, axis=1), jnp.concatenate(backs, axis=0)
                )
                dk_sum[owners[0], span] += dot_nn(
                    jnp.concatenate(d_scores, axis=1), jnp.concatenate(queries, axis=0)
                )
            else:
                for place in range(2):
                    dv_sum[owners[place], span] += dot_nn(probs[place], backs[place])
                    dk_sum[owners[place], span] += dot_nn(d_scores[place], queries[place])
        d_query = jnp.where(upper_t, d_query_t[1], d_query_t[0]).T * SCALE
        dq_ref[:, at] = (d_query * cosine - swap_halves(d_query) * sine).astype(BF16)
    lower_key = lane_of((4 * rows, LANES)) < HD
    for total, begin in ((dk_sum, 0), (dv_sum, LANES)):
        first, second = total[0], total[1]
        first = first + pltpu.roll(first, HD, 1)
        second = second + pltpu.roll(second, HD, 1)
        both = jnp.where(lower_key, first, second)
        cols = slice(begin, begin + LANES)
        own_ref[:, cols] = both[:rows]
        for place, ref in enumerate((core_ref, x_ref, far_ref)):
            ref[:, cols] = both[(place + 1) * rows : (place + 2) * rows].astype(BF16)


def parts_of(rows, cols):
    shapes = [jax.ShapeDtypeStruct((rows, cols), F32)] + [jax.ShapeDtypeStruct((rows, cols), BF16)] * 3
    return [seq_rows(0, rows, cols)] * 4, shapes


def attend_back(block, q, kv_pieces, back, out, level, start, cosine, sine, rows, seq):
    width = q.shape[1]
    length = 4 * rows
    heads = width // HD
    specs, shapes = parts_of(rows, 2 * LANES)
    return pl.pallas_call(
        attend_back_kernel,
        grid=(1,),
        in_specs=[
            pl.BlockSpec(memory_space=pltpu.SMEM),
            seq_rows(seq, rows, width),
            *[piece_of(seq, rows)] * 4,
            seq_rows(0, rows, width),
            seq_rows(0, rows, width),
            seq_rows(0, rows, LANES),
            pl.BlockSpec((1, 8, rows), lambda i: (seq, 0, 0)),
            seq_rows(seq, rows, LANES),
            seq_rows(seq, rows, LANES),
        ],
        out_specs=[seq_rows(0, rows, width), *specs],
        out_shape=[jax.ShapeDtypeStruct((rows, width), BF16), *shapes],
        scratch_shapes=[
            pltpu.VMEM((2, length, LANES), F32),
            pltpu.VMEM((2, length, LANES), F32),
        ],
        compiler_params=pltpu.CompilerParams(vmem_limit_bytes=VMEM_LIMIT),
        cost_estimate=pl.CostEstimate(
            flops=80 * rows * rows * LANES * heads,
            bytes_accessed=8 * rows * width,
            transcendentals=4 * rows * rows * heads,
        ),
        name="attention_backward",
    )(block, q, *kv_pieces, back, out, level, start, cosine, sine)


def mlp_kernel(
    n_0, n_1, n_2, n_3, c_0, c_1, c_2, c_3, w_ref,
    own_ref, out_1, out_2, out_3, d_own_ref, d_1, d_2, d_3, kept_ref, turned_ref,
    normed_all, cot_all,
):
    step = pl.program_id(0)
    rows = own_ref.shape[0]
    columns = w_ref.shape[1] // 3

    @pl.when(step == 0)
    def _():
        for place, (n_ref, c_ref) in enumerate(zip((n_0, n_1, n_2, n_3), (c_0, c_1, c_2, c_3))):
            normed_all[place // 2, (place % 2) * rows : (place % 2 + 1) * rows] = n_ref[...]
            cot_all[place // 2, (place % 2) * rows : (place % 2 + 1) * rows] = c_ref[...]

    normed, cot = normed_all[step], cot_all[step]
    gate = dot_nn(normed, w_ref[:, :columns])
    up = dot_nn(normed, w_ref[:, columns : 2 * columns])
    d_act = dot_nn(cot, w_ref[:, 2 * columns :])
    sigmoid = 0.5 * jnp.tanh(0.5 * gate) + 0.5
    swish = gate * sigmoid
    kept_ref[0] = (d_act * up * (sigmoid + swish * (1.0 - sigmoid))).astype(BF16)
    kept_ref[1] = (d_act * swish).astype(BF16)
    kept_ref[2] = (swish * up).astype(BF16)
    turned_ref[0] = normed.T
    turned_ref[1] = cot.T
    out = dot_nt(kept_ref[2], w_ref[:, 2 * columns :])
    d_normed = dot_nt(kept_ref[0], w_ref[:, :columns]) + dot_nt(kept_ref[1], w_ref[:, columns : 2 * columns])

    @pl.when(step == 0)
    def _():
        own_ref[...] = out[:rows]
        out_1[...] = out[rows:].astype(BF16)
        d_own_ref[...] = d_normed[:rows]
        d_1[...] = d_normed[rows:].astype(BF16)

    @pl.when(step == 1)
    def _():
        out_2[...] = out[:rows].astype(BF16)
        out_3[...] = out[rows:].astype(BF16)
        d_2[...] = d_normed[:rows].astype(BF16)
        d_3[...] = d_normed[rows:].astype(BF16)


def mlp(normed, cot, weights, seq):
    rows, dim = normed[0].shape
    columns = weights.shape[1] // 3
    specs, shapes = parts_of(rows, dim)
    once = lambda at: pl.BlockSpec((rows, dim), lambda i: (at, 0), pipeline_mode=pl.Buffered(1))
    return pl.pallas_call(
        mlp_kernel,
        grid=(2,),
        in_specs=[
            *[once(0)] * 4,
            *[once(seq)] * 3,
            once(0),
            pl.BlockSpec(weights.shape, lambda i: (0, 0), pipeline_mode=pl.Buffered(1)),
        ],
        out_specs=[
            *specs,
            *specs,
            pl.BlockSpec((3, 2 * rows, columns), lambda i: (0, i, 0)),
            pl.BlockSpec((2, dim, 2 * rows), lambda i: (0, 0, i)),
        ],
        out_shape=[
            *shapes,
            *shapes,
            jax.ShapeDtypeStruct((3, 4 * rows, columns), BF16),
            jax.ShapeDtypeStruct((2, dim, 4 * rows), BF16),
        ],
        scratch_shapes=[
            pltpu.VMEM((2, 2 * rows, dim), BF16),
            pltpu.VMEM((2, 2 * rows, dim), BF16),
        ],
        compiler_params=pltpu.CompilerParams(vmem_limit_bytes=VMEM_LIMIT),
        cost_estimate=pl.CostEstimate(
            flops=48 * rows * dim * columns,
            bytes_accessed=6 * dim * columns + 24 * rows * columns,
            transcendentals=4 * rows * columns,
        ),
        name="feed_forward",
    )(*normed, *cot, weights)


def mlp_grad_kernel(turned_0, turned_1, kept_0, kept_1, grad_ref):
    grad_ref[...] = (dot_nn(turned_0[0], kept_0[0]) + dot_nn(turned_1[0], kept_1[0])).astype(BF16)


def mlp_grad(turned, kept):
    _, dim, count = turned[0].shape
    columns = kept[0].shape[2]
    turned_block = pl.BlockSpec((1, dim, count), lambda i: (i // 2, 0, 0))
    kept_block = pl.BlockSpec((1, count, columns), lambda i: (i, 0, 0))
    return pl.pallas_call(
        mlp_grad_kernel,
        grid=(3,),
        in_specs=[turned_block, turned_block, kept_block, kept_block],
        out_specs=pl.BlockSpec((dim, columns), lambda i: (0, i)),
        out_shape=jax.ShapeDtypeStruct((dim, 3 * columns), BF16),
        compiler_params=pltpu.CompilerParams(vmem_limit_bytes=VMEM_LIMIT),
        cost_estimate=pl.CostEstimate(
            flops=12 * count * dim * columns,
            bytes_accessed=6 * dim * columns + 12 * count * columns,
            transcendentals=0,
        ),
        name="feed_forward_gradients",
    )(*turned, *kept)


def pack_kernel(block_ref, gate_ref, up_ref, down_ref, *refs):
    out_refs, scratch = refs[:4], refs[4]
    shard, ff = gate_ref.shape
    quarter = scratch.shape[2] // 4
    for place, ref in enumerate((gate_ref, up_ref, down_ref)):
        scratch[place, :, :ff] = ref[...].astype(F32)
        scratch[place, :, ff:] = jnp.zeros((shard, 4 * quarter - ff), F32)
    for place, out_ref in enumerate(out_refs):
        begin = pl.multiple_of((block_ref[0] ^ place) * quarter, LANES)
        for part in range(3):
            out_ref[:, part * quarter : (part + 1) * quarter] = scratch[part, :, pl.ds(begin, quarter)].astype(BF16)


def pack(block, gate, up, down_t, quarter):
    shard = gate.shape[0]
    return pl.pallas_call(
        pack_kernel,
        in_specs=[pl.BlockSpec(memory_space=pltpu.SMEM)] + [pl.BlockSpec(memory_space=pltpu.VMEM)] * 3,
        out_specs=[pl.BlockSpec(memory_space=pltpu.VMEM)] * 4,
        out_shape=[jax.ShapeDtypeStruct((shard, 3 * quarter), BF16)] * 4,
        scratch_shapes=[pltpu.VMEM((3, shard, 4 * quarter), F32)],
        compiler_params=pltpu.CompilerParams(vmem_limit_bytes=VMEM_LIMIT),
        name="pack_columns",
    )(block, gate, up, down_t)


def pick(options, index):
    value = options[0]
    for place in range(1, len(options)):
        value = jnp.where(index == place, options[place], value)
    return value


def assemble_kernel(block_ref, *refs):
    pieces, out_ref, scratch = refs[:4], refs[4], refs[5]
    shard = pieces[0].shape[0]
    values = [ref[...].astype(F32) for ref in pieces]
    for owner in range(4):
        scratch[owner * shard : (owner + 1) * shard] = pick(values, block_ref[0] ^ owner)
    out_ref[...] = scratch[...].astype(BF16)


def assemble(block, pieces):
    shard, columns = pieces[0].shape
    return pl.pallas_call(
        assemble_kernel,
        in_specs=[pl.BlockSpec(memory_space=pltpu.SMEM)] + [pl.BlockSpec(memory_space=pltpu.VMEM)] * 4,
        out_specs=pl.BlockSpec(memory_space=pltpu.VMEM),
        out_shape=jax.ShapeDtypeStruct((4 * shard, columns), BF16),
        scratch_shapes=[pltpu.VMEM((4 * shard, columns), F32)],
        compiler_params=pltpu.CompilerParams(vmem_limit_bytes=VMEM_LIMIT),
        name="assemble_rows",
    )(block, *pieces)


def cut_kernel(block_ref, value_ref, *refs):
    out_refs, scratch = refs[:4], refs[4]
    shard = out_refs[0].shape[0]
    scratch[...] = value_ref[...].astype(F32)
    values = [scratch[owner * shard : (owner + 1) * shard] for owner in range(4)]
    for place, out_ref in enumerate(out_refs):
        out_ref[...] = pick(values, block_ref[0] ^ place).astype(BF16)


def cut(block, value):
    shard, columns = value.shape[0] // 4, value.shape[1]
    return pl.pallas_call(
        cut_kernel,
        in_specs=[pl.BlockSpec(memory_space=pltpu.SMEM), pl.BlockSpec(memory_space=pltpu.VMEM)],
        out_specs=[pl.BlockSpec(memory_space=pltpu.VMEM)] * 4,
        out_shape=[jax.ShapeDtypeStruct((shard, columns), BF16)] * 4,
        scratch_shapes=[pltpu.VMEM(value.shape, F32)],
        compiler_params=pltpu.CompilerParams(vmem_limit_bytes=VMEM_LIMIT),
        name="cut_rows",
    )(block, value)


def unpack_kernel(block_ref, *refs):
    pieces, out_refs, scratch = refs[:4], refs[4:7], refs[7]
    ff = out_refs[0].shape[1]
    quarter = scratch.shape[2] // 4
    for place, ref in enumerate(pieces):
        begin = pl.multiple_of((block_ref[0] ^ place) * quarter, LANES)
        for part in range(3):
            scratch[part, :, pl.ds(begin, quarter)] = ref[:, part * quarter : (part + 1) * quarter].astype(F32)
    for part, out_ref in enumerate(out_refs):
        out_ref[...] = scratch[part, :, :ff]


def unpack(block, pieces, ff):
    shard, columns = pieces[0].shape
    return pl.pallas_call(
        unpack_kernel,
        in_specs=[pl.BlockSpec(memory_space=pltpu.SMEM)] + [pl.BlockSpec(memory_space=pltpu.VMEM)] * 4,
        out_specs=[pl.BlockSpec(memory_space=pltpu.VMEM)] * 3,
        out_shape=[jax.ShapeDtypeStruct((shard, ff), F32)] * 3,
        scratch_shapes=[pltpu.VMEM((3, shard, columns // 3 * 4), F32)],
        compiler_params=pltpu.CompilerParams(vmem_limit_bytes=VMEM_LIMIT),
        name="unpack_columns",
    )(block, *pieces)


def bit_swap(value, axis, bit=0):
    size = lax.axis_size(axis)
    return lax.ppermute(value, axis, [(i, i ^ (1 << bit)) for i in range(size)])


def jump_swap(value, axes, jump):
    return lax.ppermute(value, axes, [(i, i ^ jump) for i in range(4)])


def to_plane(value, slot):
    high, low = slot >> 1, slot & 1
    pairs = [
        (4 * y + 2 * x + c, 4 * (c ^ low) + 2 * (x ^ high) + y) for y in range(2) for x in range(2) for c in range(2)
    ]
    return lax.ppermute(value, TOKENS + ("cc",), pairs)


def from_plane(value, slot):
    high, low = slot >> 1, slot & 1
    pairs = [
        (4 * y + 2 * x + c, 4 * c + 2 * (x ^ high) + (y ^ low)) for y in range(2) for x in range(2) for c in range(2)
    ]
    return lax.ppermute(value, TOKENS + ("cc",), pairs)


def after(first, *values):
    return lax.optimization_barrier((first, *values))


def gather_four(value, axes):
    from_first = bit_swap(value, axes[0])
    return [value, bit_swap(value, axes[1]), from_first, bit_swap(from_first, axes[1])]


def gather_direct(value, axes):
    return [value] + [jump_swap(value, axes, jump) for jump in range(1, 4)]


def sum_direct(axes, own, *away):
    return [own] + [jump_swap(value, axes, jump + 1) for jump, value in enumerate(away)]


def doubling_offsets(steps):
    weight = {"cc": 1, "cx": 2, "fy": 4, "fz": 8}
    offsets = [0]
    for axis, bit in steps:
        offsets += [offset ^ (weight[axis] << bit) for offset in offsets]
    return jnp.array(offsets, jnp.int32)


def double(value, axis, bit=0):
    return jnp.concatenate([value, bit_swap(value, axis, bit)], axis=0)


def plane_gather(value):
    return jnp.concatenate(gather_direct(value, TOKENS), axis=0)


def plane_sum(value):
    parts = jnp.split(value, 4, axis=0)
    terms = sum_direct(TOKENS, *parts)
    return sum(term.astype(F32) for term in terms).astype(BF16)


def core_sum(keep, send):
    return (keep.astype(F32) + bit_swap(send.astype(BF16), "cc").astype(F32)).astype(BF16)


def halve(value, axis, bit=0):
    middle = value.shape[0] // 2
    came = bit_swap(value[middle:], axis, bit)
    return (value[:middle].astype(F32) + came.astype(F32)).astype(BF16)


def on_device(
    hidden,
    segments,
    attn_gain,
    qkv_weight,
    qkv_bias,
    out_weight,
    mlp_gain,
    gate_weight,
    up_weight,
    down_weight,
    cotangent,
):
    seqs, rows, dim = hidden.shape
    count = seqs * rows
    shard = attn_gain.shape[0]
    world = dim // shard
    joint = qkv_weight.shape[1]
    width = joint - 2 * LANES
    ff = gate_weight.shape[1]
    block = lax.axis_index("cx") * lax.axis_size("cc") + lax.axis_index("cc")
    me = lax.axis_index(FSDP) * lax.axis_size(CTX) + block
    offset = block * rows
    block_arg = block.reshape(1).astype(jnp.int32)
    plane_arg = (lax.axis_index("cx") * 2 + lax.axis_index("fy")).reshape(1).astype(jnp.int32)
    x = hidden.reshape(count, dim)
    cot = cotangent.reshape(count, dim)

    cot_x = bit_swap(cot, "cx")

    far = [("fz", bit) for bit in reversed(range((lax.axis_size("fz")).bit_length() - 1))]
    padded = -(-(shard + 1) // 16) * 16
    small = jnp.concatenate([attn_gain, mlp_gain, qkv_bias])
    small_row = jnp.pad(small, (0, joint + width - small.shape[0]))[None]
    first = jnp.concatenate(
        [
            jnp.concatenate([qkv_weight, out_weight.T], axis=1),
            small_row,
            jnp.zeros((padded - shard - 1, joint + width), BF16),
        ],
        axis=0,
    )
    first = double(first, *far[0])

    quarter = -(-ff // (4 * TILE)) * TILE
    first, *pieces = after(first, *pack(block_arg, gate_weight, up_weight, down_weight.T, quarter))
    pieces = [to_plane(piece, slot) for slot, piece in enumerate(pieces)]
    for axis, bit in far[1:]:
        first = double(first, axis, bit)

    within = jnp.arange(padded, dtype=jnp.int32)
    owner = me ^ doubling_offsets(far + [("cx", 0), ("fy", 0), ("cc", 0)])
    target = jnp.where(within[None, :] < shard, owner[:, None] * shard + within[None, :], -1).reshape(1, -1)
    order = (jnp.arange(dim, dtype=jnp.int32)[:, None] == target).astype(BF16)
    place = jnp.where(within[None, :] == shard, owner[:, None], -1).reshape(1, -1)
    spread = (jnp.arange(world, dtype=jnp.int32)[:, None] == place).astype(BF16)

    at_row = lax.dynamic_slice_in_dim(segments, offset, rows, axis=1)
    zeros_before = jnp.sum((segments < 1).astype(jnp.int32), axis=1, keepdims=True)
    ones_before = jnp.sum((segments < 2).astype(jnp.int32), axis=1, keepdims=True)
    start = jnp.where(at_row == 0, 0, jnp.where(at_row == 1, zeros_before, ones_before))
    position = (offset + jnp.arange(rows, dtype=jnp.int32)[None, :] - start).reshape(count)
    lane = jnp.arange(LANES, dtype=jnp.int32)
    frequency = ROPE_BASE ** (-(lane % (HD // 2)).astype(F32) * 2.0 / HD)
    angle = position.astype(F32)[:, None] * frequency[None, :]
    cosine = jnp.cos(angle)
    sine = jnp.where(lane % HD < HD // 2, -1.0, 1.0)[None, :] * jnp.sin(angle)
    start_column = jnp.broadcast_to(start.reshape(count, 1), (count, LANES))
    start_row = jnp.broadcast_to(start[:, None, :], (seqs, 8, rows))

    first, cot_x, cot_late, order, spread, cosine, sine, start_column, *pieces = after(
        first, cot_x, cot, order, spread, cosine, sine, start_column, *pieces
    )
    w_joint = plane_gather(first[:, :joint])
    mlp_shard = assemble(plane_arg, pieces)
    mlp_weights = lax.all_gather(mlp_shard, WEIGHTS, axis=0, tiled=True)
    w_joint, cot_late = after(w_joint, cot_late)
    w_joint = (w_joint, bit_swap(w_joint, "cc"))
    cot_y = bit_swap(cot_late, "fy")

    normed_low, normed_high, q, kv, gain_attn, gain_mlp = prep(x, order, spread, w_joint, cosine, sine, rows)
    kv_all = gather_four(kv.reshape(seqs, rows, 2 * LANES), CTX)
    kv_all[3], out_rows, cot_y = after(kv_all[3], first[:, joint:], cot_y)
    cot_far = [bit_swap(cot_x[:rows], "fy"), bit_swap(cot_y[rows:], "cx")]
    w_out = plane_gather(out_rows)
    attended, levels, resid, normed_all = [], [], [], []
    for seq in range(seqs):
        turn = block_arg if seq == 0 else after(resid[0], block_arg)[1]
        attended_one, level_one = attend(turn, q, kv_all, start_column, rows, seq)
        if seq == 0:
            attended_one, w_out = after(attended_one, w_out)
            w_out = (w_out, bit_swap(w_out, "cc"))
        attended.append(attended_one)
        levels.append(level_one)
        resid_one, normed_one = project_out(attended[seq], x, w_out, order, gain_mlp, rows, seq)
        if seq == 0:
            resid_one, normed_one, *cot_far = after(resid_one, normed_one, *cot_far)
        resid.append(resid_one)
        normed_all.append(gather_direct(normed_one, TOKENS))

    out_parts, d_terms, kept, turned = [], [], [], []
    for seq in range(seqs):
        if seq == 1:
            out_parts[0], normed_all[1] = lax.optimization_barrier((out_parts[0], normed_all[1]))
        result = mlp(normed_all[seq], [cot, cot_x, cot_y, cot_far[seq]], mlp_weights, seq)
        out_parts.append(result[:4])
        d_terms.append(sum_direct(TOKENS, *result[4:8]))
        kept.append(result[8])
        turned.append(result[9])
    d_resid, d_low, d_high, d_attended, mlp_gain_grad, dq, dkv_terms, out_terms = [], [], [], [], [], [], [], []
    for seq in range(seqs):
        if seq == 0:
            _, *d_terms[0] = after(kept[1], *d_terms[0])
        else:
            dq[0], d_terms[1][0], *out_terms[0] = after(dq[0], d_terms[1][0], *out_terms[0])
        result = project_out_back(d_terms[seq], resid[seq], cot, w_out, order, gain_mlp, rows, seq)
        for place, value in zip((d_resid, d_low, d_high, d_attended, mlp_gain_grad), result):
            place.append(value)
        out_terms.append(sum_direct(TOKENS, *after(d_terms[seq][1], *out_parts[seq])[1:]))
        if seq == 0:
            _, turned[1] = after(d_resid[0], turned[1])
            grads = mlp_grad(turned, kept)
            grads, d_attended[0], *d_terms[1] = after(grads, d_attended[0], *d_terms[1])
            grads = lax.psum_scatter(
                grads.reshape(world // 4, 4 * shard, 3 * quarter), WEIGHTS, scatter_dimension=0, tiled=False
            )
        else:
            both = jnp.concatenate(attended, axis=0)
            out_grad = core_sum(
                dot_tn(jnp.concatenate(d_low, axis=0), both).astype(BF16), dot_tn(jnp.concatenate(d_high, axis=0), both)
            )
            d_attended[1], *dkv_terms[0] = after(d_attended[1], *dkv_terms[0])
        result = attend_back(
            block_arg, q, kv_all, d_attended[seq], attended[seq], levels[seq], start_row, cosine, sine, rows, seq
        )
        dq.append(result[0])
        dkv_terms.append(sum_direct(CTX, *result[1:]))
    dq[1], out_grad, *out_terms[1] = after(dq[1], out_grad, *out_terms[1])
    dq_both = jnp.concatenate(dq, axis=0)
    q_grad = core_sum(dot_tn(normed_low, dq_both).astype(BF16), dot_tn(normed_high, dq_both))
    q_grad, *dkv_terms[1] = after(q_grad, *dkv_terms[1])
    q_grad = plane_sum(q_grad)
    d_resid = jnp.concatenate(d_resid, axis=0)
    d_kv, input_grad, attn_gain_grad, bias_grad = input_back(
        dq, dkv_terms, x, d_resid, w_joint, order, gain_attn, cosine, sine
    )
    d_kv, q_grad, attn_gain_grad, bias_grad = after(d_kv, q_grad, attn_gain_grad, bias_grad)

    split_at = width + LANES
    bias_grad = bias_grad[0]
    small_grads = jnp.concatenate(
        [
            attn_gain_grad.reshape(world, -1),
            sum(mlp_gain_grad).reshape(world, -1),
            bias_grad[:split_at].reshape(world, -1),
            bias_grad[split_at:].reshape(world, -1),
        ],
        axis=1,
    ).astype(BF16)
    small_count = small_grads.shape[1]
    small_grads = jnp.pad(small_grads, ((0, 0), (0, 2 * LANES - small_count)))
    middle = spread.shape[1] // 2
    kv_grad = core_sum(
        (dot_tn(normed_low, d_kv) + dot_tn(spread[:, :middle], small_grads)).astype(BF16),
        dot_tn(normed_high, d_kv) + dot_tn(spread[:, middle:], small_grads),
    )
    pieces = cut(plane_arg, lax.optimization_barrier(grads))
    kv_grad, *pieces = after(kv_grad, *pieces)
    pieces = [from_plane(piece, slot) for slot, piece in enumerate(pieces)]
    kv_grad, out_grad = plane_sum(kv_grad), plane_sum(out_grad)
    first_sum = jnp.concatenate([q_grad, kv_grad, out_grad], axis=1)
    first_sum, out_terms = lax.optimization_barrier((first_sum, out_terms))
    for axis, bit in reversed(far):
        first_sum = halve(first_sum, axis, bit)
    output = []
    for seq in range(seqs):
        own, *away = out_terms[seq]
        output.append((resid[seq] + own + sum(term.astype(F32) for term in away)).astype(BF16))

    gate_grad, up_grad, down_grad_t = unpack(block_arg, pieces, ff)
    first_sum = first_sum.astype(F32)
    qkv_sum, out_sum = first_sum[:, :joint], first_sum[:, joint:]
    small_sum = qkv_sum[shard, width : width + small_count]
    at = (shard, 2 * shard, 2 * shard + split_at // world)

    return (
        jnp.stack(output),
        input_grad.reshape(hidden.shape),
        small_sum[: at[0]],
        qkv_sum[:shard],
        small_sum[at[1] : at[2]],
        small_sum[at[2] :],
        out_sum[:shard].T,
        small_sum[at[0] : at[1]],
        gate_grad,
        up_grad,
        down_grad_t.T,
    )


def solution(mesh):
    fsdp, ctx = mesh.shape["fsdp"], mesh.shape["ctx"]
    inner = Mesh(mesh.devices.reshape(fsdp // 2, 2, 2, ctx // 2), AXES)
    tokens = P(FSDP, CTX, None)
    vector = P(AXES)
    by_row = P(AXES, None)
    by_column = P(None, AXES)
    return jax.shard_map(
        on_device,
        mesh=inner,
        in_specs=(
            tokens,
            P(FSDP, None),
            vector,
            by_row,
            vector,
            by_column,
            vector,
            by_row,
            by_row,
            by_column,
            tokens,
        ),
        out_specs=(
            tokens,
            tokens,
            vector,
            by_row,
            vector,
            vector,
            by_column,
            vector,
            by_row,
            by_row,
            by_column,
        ),
        check_vma=False,
    )
```

```python
import functools

import jax
import jax.numpy as jnp
from jax import lax
from jax.experimental import pallas as pl
from jax.experimental.pallas import tpu as pltpu
from jax.sharding import Mesh
from jax.sharding import PartitionSpec as P

HD = 64
LANES = 128
EPSILON = 1e-06
ROPE_BASE = 1000000.0
MASKED = -1e30
SCALE = HD ** (-0.5)
TILE = 256
MIB = 1 << 20
VMEM_LIMIT = 54 * MIB
F32 = jnp.float32
BF16 = jnp.bfloat16
AXES = ("fz", "fy", "cx", "cc")
FSDP = ("fz", "fy")
CTX = ("cx", "cc")
TOKENS = ("fy", "cx")
WEIGHTS = ("fz", "cc")


def dot_nn(a, b):
    return lax.dot_general(a, b, (((1,), (0,)), ((), ())), preferred_element_type=F32)


def dot_nt(a, b):
    return lax.dot_general(a, b, (((1,), (1,)), ((), ())), preferred_element_type=F32)


def dot_tn(a, b):
    return lax.dot_general(a, b, (((0,), (0,)), ((), ())), preferred_element_type=F32)


def lane_of(shape):
    return lax.broadcasted_iota(jnp.int32, shape, len(shape) - 1)


def swap_halves(block):
    lead = lane_of(block.shape) % HD < HD // 2
    return jnp.where(
        lead, pltpu.roll(block, LANES - HD // 2, 1), pltpu.roll(block, HD // 2, 1)
    )


def other_head(block):
    return jnp.concatenate([block[:, HD:], block[:, :HD]], axis=1)


def read_out(extras, first, piece, total):
    owners, columns = extras.shape
    at = lax.broadcasted_iota(jnp.int32, (columns, total), 1) % piece + first
    chosen = (lax.broadcasted_iota(jnp.int32, (columns, total), 0) == at).astype(BF16)
    spread = dot_nn(extras, chosen)
    owner = lax.broadcasted_iota(jnp.int32, (owners, total), 1) // piece
    mine = owner == lax.broadcasted_iota(jnp.int32, (owners, total), 0)
    return jnp.sum(jnp.where(mine, spread, 0.0), axis=0, keepdims=True)


def prep_kernel(
    x_ref, order_ref, spread_ref, w_low_ref, w_high_ref, cos_ref, sin_ref,
    normed_low_ref, normed_high_ref, q_ref, kv_ref, gain_ref, gain_mlp_ref, bias_ref,
):
    x = x_ref[...].astype(F32)
    dim = x.shape[1]
    width = q_ref.shape[1]
    joint = w_low_ref.shape[1]
    middle = w_low_ref.shape[0]
    owners = spread_ref.shape[0]

    @pl.when(pl.program_id(0) == 0)
    def _():
        extras = dot_nn(spread_ref[:, :middle], w_low_ref[:, :LANES])
        extras = (extras + dot_nn(spread_ref[:, middle:], w_high_ref[:, :LANES])).astype(BF16)
        shard = dim // owners
        gain_ref[...] = read_out(extras, 0, shard, dim)
        gain_mlp_ref[...] = read_out(extras, shard, shard, dim)
        bias_ref[...] = read_out(extras, 2 * shard, joint // owners, joint)

    gain, bias = gain_ref[...], bias_ref[...]
    inverse = lax.rsqrt(jnp.mean(x * x, axis=-1, keepdims=True) + EPSILON)
    normed = (x * inverse * gain).astype(BF16)
    ordered = dot_nn(normed, order_ref[...]).astype(BF16)
    normed_low_ref[...] = ordered[:, :middle]
    normed_high_ref[...] = ordered[:, middle:]
    joined = dot_nn(ordered[:, :middle], w_low_ref[...])
    joined = joined + dot_nn(ordered[:, middle:], w_high_ref[...]) + bias
    cosine, sine = cos_ref[...], sin_ref[...]
    for begin in range(0, width + LANES, LANES):
        block = joined[:, begin : begin + LANES]
        turned = block * cosine + swap_halves(block) * sine
        if begin < width:
            q_ref[:, begin : begin + LANES] = (turned * SCALE).astype(BF16)
        else:
            kv_ref[:, :LANES] = turned.astype(BF16)
    kv_ref[:, LANES:] = joined[:, width + LANES :].astype(BF16)


def rows_of(rows, cols):
    return pl.BlockSpec((rows, cols), lambda i: (i, 0))


def whole(value):
    return pl.BlockSpec(value.shape, lambda i: (0,) * value.ndim)


def prep(x, order, spread, weights, cosine, sine, rows):
    count, dim = x.shape
    ordered = order.shape[1]
    joint = weights[0].shape[1]
    width = joint - 2 * LANES
    row = pl.BlockSpec((1, dim), lambda i: (0, 0))
    return pl.pallas_call(
        prep_kernel,
        grid=(count // rows,),
        in_specs=[
            rows_of(rows, dim),
            whole(order),
            whole(spread),
            whole(weights[0]),
            whole(weights[1]),
            rows_of(rows, LANES),
            rows_of(rows, LANES),
        ],
        out_specs=[
            rows_of(rows, ordered // 2),
            rows_of(rows, ordered // 2),
            rows_of(rows, width),
            rows_of(rows, 2 * LANES),
            row,
            row,
        ],
        out_shape=[
            jax.ShapeDtypeStruct((count, ordered // 2), BF16),
            jax.ShapeDtypeStruct((count, ordered // 2), BF16),
            jax.ShapeDtypeStruct((count, width), BF16),
            jax.ShapeDtypeStruct((count, 2 * LANES), BF16),
            jax.ShapeDtypeStruct((1, dim), F32),
            jax.ShapeDtypeStruct((1, dim), F32),
        ],
        scratch_shapes=[pltpu.VMEM((1, joint), F32)],
        compiler_params=pltpu.CompilerParams(vmem_limit_bytes=VMEM_LIMIT),
        cost_estimate=pl.CostEstimate(
            flops=2 * count * ordered * (joint + dim), bytes_accessed=12 * MIB, transcendentals=0
        ),
        name="norm_project_rotate",
    )(x, order, spread, weights[0], weights[1], cosine, sine)


def back_in_order(value, order):
    high = value.astype(BF16)
    low = (value - high.astype(F32)).astype(BF16)
    return dot_nt(high, order) + dot_nt(low, order)


def out_kernel(attended_ref, x_ref, w_low_ref, w_high_ref, order_ref, gain_ref, resid_ref, normed_ref):
    attended = attended_ref[...]
    branch = jnp.concatenate([dot_nt(attended, w_low_ref[...]), dot_nt(attended, w_high_ref[...])], axis=1)
    resid = x_ref[...].astype(F32) + back_in_order(branch, order_ref[...])
    inverse = lax.rsqrt(jnp.mean(resid * resid, axis=-1, keepdims=True) + EPSILON)
    resid_ref[...] = resid
    normed_ref[...] = (resid * inverse * gain_ref[...]).astype(BF16)


def project_out(attended, x, weights, order, gain, rows, seq):
    dim = x.shape[1]
    count = rows
    return pl.pallas_call(
        out_kernel,
        grid=(1,),
        in_specs=[
            rows_of(rows, attended.shape[1]),
            pl.BlockSpec((rows, dim), lambda i: (seq, 0)),
            whole(weights[0]),
            whole(weights[1]),
            whole(order),
            whole(gain),
        ],
        out_specs=[rows_of(rows, dim), rows_of(rows, dim)],
        out_shape=[jax.ShapeDtypeStruct((count, dim), F32), jax.ShapeDtypeStruct((count, dim), BF16)],
        compiler_params=pltpu.CompilerParams(vmem_limit_bytes=VMEM_LIMIT),
        cost_estimate=pl.CostEstimate(flops=6 * count * dim * dim, bytes_accessed=8 * MIB, transcendentals=0),
        name="project_out_norm",
    )(attended, x, weights[0], weights[1], order, gain)


def sum_rows(value):
    return jnp.sum(value, axis=0, keepdims=True)


def norm_back(values, inverse, gain, incoming):
    scaled = incoming * gain
    mean_term = jnp.mean(scaled * values, axis=-1, keepdims=True)
    return inverse * scaled - values * inverse**3 * mean_term


def total_of(own_ref, *away_refs):
    total = own_ref[...]
    for ref in away_refs:
        total = total + ref[...].astype(F32)
    return total


def out_back_kernel(
    own_ref, core_ref, x_ref, far_ref, resid_ref, cot_ref, w_low_ref, w_high_ref, order_ref, gain_ref,
    d_resid_ref, d_low_ref, d_high_ref, d_attended_ref, gain_grad_ref,
):
    middle = w_low_ref.shape[0]
    d_normed = total_of(own_ref, core_ref, x_ref, far_ref)
    resid = resid_ref[...]
    inverse = lax.rsqrt(jnp.mean(resid * resid, axis=-1, keepdims=True) + EPSILON)
    d_resid = cot_ref[...].astype(F32) + norm_back(resid, inverse, gain_ref[...], d_normed)
    d_resid_ref[...] = d_resid
    d_branch = dot_nn(d_resid.astype(BF16), order_ref[...]).astype(BF16)
    d_low_ref[...] = d_branch[:, :middle]
    d_high_ref[...] = d_branch[:, middle:]
    d_attended = dot_nn(d_branch[:, :middle], w_low_ref[...])
    d_attended = d_attended + dot_nn(d_branch[:, middle:], w_high_ref[...])
    d_attended_ref[...] = d_attended.astype(BF16)
    gain_grad_ref[...] = sum_rows(d_normed * resid * inverse)


def project_out_back(terms, resid, cot, weights, order, gain, rows, seq):
    count, dim = resid.shape
    ordered = order.shape[1]
    width = dim
    return pl.pallas_call(
        out_back_kernel,
        grid=(1,),
        in_specs=[
            rows_of(rows, dim),
            rows_of(rows, dim),
            rows_of(rows, dim),
            rows_of(rows, dim),
            rows_of(rows, dim),
            pl.BlockSpec((rows, dim), lambda i: (seq, 0)),
            whole(weights[0]),
            whole(weights[1]),
            whole(order),
            whole(gain),
        ],
        out_specs=[
            rows_of(rows, dim),
            rows_of(rows, ordered // 2),
            rows_of(rows, ordered // 2),
            rows_of(rows, width),
            pl.BlockSpec((1, dim), lambda i: (0, 0)),
        ],
        out_shape=[
            jax.ShapeDtypeStruct((count, dim), F32),
            jax.ShapeDtypeStruct((count, ordered // 2), BF16),
            jax.ShapeDtypeStruct((count, ordered // 2), BF16),
            jax.ShapeDtypeStruct((count, width), BF16),
            jax.ShapeDtypeStruct((1, dim), F32),
        ],
        compiler_params=pltpu.CompilerParams(vmem_limit_bytes=VMEM_LIMIT),
        cost_estimate=pl.CostEstimate(flops=4 * count * dim * dim, bytes_accessed=12 * MIB, transcendentals=0),
        name="norm_back_project",
    )(*terms, resid, cot, weights[0], weights[1], order, gain)


def call_whole(kernel, operands, out_shape, flops, name):
    return pl.pallas_call(
        kernel,
        in_specs=[pl.BlockSpec(memory_space=pltpu.VMEM)] * len(operands),
        out_specs=[pl.BlockSpec(memory_space=pltpu.VMEM)] * len(out_shape),
        out_shape=out_shape,
        compiler_params=pltpu.CompilerParams(vmem_limit_bytes=VMEM_LIMIT),
        cost_estimate=pl.CostEstimate(flops=flops, bytes_accessed=16 * MIB, transcendentals=0),
        name=name,
    )(*operands)


def input_back_kernel(*refs):
    dqs, terms = refs[:2], refs[2:10]
    x_ref, d_resid_ref, w_low_ref, w_high_ref, order_ref, gain_ref, cos_ref, sin_ref = refs[10:18]
    d_kv_ref, input_grad_ref, gain_grad_ref, bias_grad_ref = refs[18:]
    dkv = jnp.concatenate([total_of(*terms[:4]), total_of(*terms[4:])], axis=0)
    dk = dkv[:, :LANES]
    dk = dk * cos_ref[...] - swap_halves(dk) * sin_ref[...]
    d_kv = jnp.concatenate([dk.astype(BF16), dkv[:, LANES:].astype(BF16)], axis=1)
    d_kv_ref[...] = d_kv
    dq = jnp.concatenate([ref[...] for ref in dqs], axis=0)
    d_joined = jnp.concatenate([dq, d_kv], axis=1)
    d_normed = jnp.concatenate([dot_nt(d_joined, w_low_ref[...]), dot_nt(d_joined, w_high_ref[...])], axis=1)
    d_normed = back_in_order(d_normed, order_ref[...])
    x = x_ref[...].astype(F32)
    inverse = lax.rsqrt(jnp.mean(x * x, axis=-1, keepdims=True) + EPSILON)
    input_grad_ref[...] = (d_resid_ref[...] + norm_back(x, inverse, gain_ref[...], d_normed)).astype(BF16)
    gain_grad_ref[...] = sum_rows(d_normed * x * inverse)
    bias_grad_ref[...] = sum_rows(d_joined.astype(F32))


def input_back(dq, terms, x, d_resid, weights, order, gain, cosine, sine):
    count, dim = x.shape
    joint = dq[0].shape[1] + 2 * LANES
    return call_whole(
        input_back_kernel,
        (*dq, *terms[0], *terms[1], x, d_resid, *weights, order, gain, cosine, sine),
        [
            jax.ShapeDtypeStruct((count, 2 * LANES), BF16),
            jax.ShapeDtypeStruct((count, dim), BF16),
            jax.ShapeDtypeStruct((1, dim), F32),
            jax.ShapeDtypeStruct((1, joint), F32),
        ],
        6 * count * dim * joint,
        "input_gradient",
    )


def seq_rows(seq, rows, cols):
    return pl.BlockSpec((rows, cols), lambda i: (seq, 0))


def piece_of(seq, rows):
    return pl.BlockSpec((1, rows, 2 * LANES), lambda i: (seq, 0, 0))


def keys_and_values(piece_refs):
    joint = jnp.concatenate([ref[0] for ref in piece_refs], axis=0)
    key, value = joint[:, :LANES], joint[:, LANES:]
    return (key, other_head(key)), (value, other_head(value))


def attend_kernel(block_ref, q_ref, kv_0, kv_1, kv_2, kv_3, start_ref, out_ref, level_ref):
    rows, width = q_ref.shape
    length = 4 * rows
    heads = width // HD
    group = heads // 2
    keys, values = keys_and_values((kv_0, kv_1, kv_2, kv_3))
    upper_key = lane_of((length, LANES)) >= HD
    upper = lane_of((rows, LANES)) >= HD
    query_at = block_ref[0] * rows + lax.broadcasted_iota(jnp.int32, (rows, length), 0)
    key_at = jnp.concatenate(
        [
            (block_ref[0] ^ place) * rows + lax.broadcasted_iota(jnp.int32, (rows, rows), 1)
            for place in range(4)
        ],
        axis=1,
    )
    allowed = (key_at <= query_at) & (key_at >= start_ref[:, :1])
    bias = jnp.where(allowed, 0.0, MASKED)
    one = jnp.ones((), BF16)
    lane = lane_of((rows, LANES))
    levels = jnp.zeros((rows, LANES), F32)
    for pair in range(heads // 2):
        at = slice(pair * LANES, (pair + 1) * LANES)
        both = q_ref[:, at]
        parts = []
        for place in range(2):
            owner = (2 * pair + place) // group
            moved = int(owner != place)
            side = upper if place else ~upper
            side_key = upper_key if place else ~upper_key
            query = jnp.where(side, both, jnp.zeros_like(both))
            score = dot_nt(query, keys[moved]) + bias
            top = jnp.max(score, axis=1, keepdims=True)
            weight = jnp.exp(score - top).astype(BF16)
            mixed = dot_nn(weight, jnp.where(side_key, values[moved], one))
            total = pltpu.roll(mixed, HD, 1)
            parts.append(mixed / total)
            level = top + jnp.log(total[:, place * HD : place * HD + 1])
            levels = jnp.where(lane == 2 * pair + place, level, levels)
        out_ref[:, at] = jnp.where(upper, parts[1], parts[0]).astype(BF16)
    level_ref[...] = levels


def attend(block, q, kv_pieces, start, rows, seq):
    width = q.shape[1]
    heads = width // HD
    return pl.pallas_call(
        attend_kernel,
        grid=(1,),
        in_specs=[
            pl.BlockSpec(memory_space=pltpu.SMEM),
            seq_rows(seq, rows, width),
            *[piece_of(seq, rows)] * 4,
            seq_rows(seq, rows, LANES),
        ],
        out_specs=[seq_rows(0, rows, width), seq_rows(0, rows, LANES)],
        out_shape=[jax.ShapeDtypeStruct((rows, width), BF16), jax.ShapeDtypeStruct((rows, LANES), F32)],
        compiler_params=pltpu.CompilerParams(vmem_limit_bytes=VMEM_LIMIT),
        cost_estimate=pl.CostEstimate(
            flops=32 * rows * rows * LANES * heads,
            bytes_accessed=4 * rows * width,
            transcendentals=4 * rows * rows * heads,
        ),
        name="attention_forward",
    )(block, q, *kv_pieces, start)


def attend_back_kernel(
    block_ref, q_ref, kv_0, kv_1, kv_2, kv_3, back_ref, out_ref, level_ref, start_ref, cos_ref, sin_ref,
    dq_ref, own_ref, core_ref, x_ref, far_ref, dk_sum, dv_sum,
):
    rows, width = q_ref.shape
    heads = width // HD
    group = heads // 2
    keys, values = keys_and_values((kv_0, kv_1, kv_2, kv_3))
    key_t = keys[0].astype(F32).T.astype(BF16)
    keys_t = (key_t, jnp.concatenate([key_t[HD:], key_t[:HD]], axis=0))
    upper = lane_of((rows, LANES)) >= HD
    upper_t = lax.broadcasted_iota(jnp.int32, (LANES, rows), 0) >= HD
    query_at = block_ref[0] * rows + lax.broadcasted_iota(jnp.int32, (rows, rows), 1)
    key_at = lax.broadcasted_iota(jnp.int32, (rows, rows), 0)
    biases = []
    for place in range(4):
        at = (block_ref[0] ^ place) * rows + key_at
        biases.append(jnp.where((at <= query_at) & (at >= start_ref[0, :1, :]), 0.0, MASKED))
    head_of = lax.broadcasted_iota(jnp.int32, (width, LANES), 0) // HD
    by_head = (head_of == lane_of((width, LANES))).astype(BF16)
    product = back_ref[...].astype(F32) * out_ref[...].astype(F32)
    product_high = product.astype(BF16)
    product_low = (product - product_high.astype(F32)).astype(BF16)
    row_sums = (dot_nn(product_high, by_head) + dot_nn(product_low, by_head)).T
    levels = level_ref[...].T
    cosine, sine = cos_ref[...], sin_ref[...]
    dk_sum[...] = jnp.zeros_like(dk_sum)
    dv_sum[...] = jnp.zeros_like(dv_sum)
    for pair in range(heads // 2):
        at = slice(pair * LANES, (pair + 1) * LANES)
        both = q_ref[:, at]
        back_both = back_ref[:, at]
        zero = jnp.zeros_like(both)
        sides = (~upper, upper)
        queries = [jnp.where(side, both, zero) for side in sides]
        backs = [jnp.where(side, back_both, zero) for side in sides]
        owners = [(2 * pair + place) // group for place in range(2)]
        d_query_t = [jnp.zeros((LANES, rows), F32) for _ in range(2)]
        for piece in range(4):
            span = slice(piece * rows, (piece + 1) * rows)
            probs, d_scores = [], []
            for place in range(2):
                head = 2 * pair + place
                moved = int(owners[place] != place)
                score = dot_nt(keys[moved][span], queries[place]) + biases[piece]
                prob = jnp.exp(score - levels[head : head + 1])
                d_prob = dot_nt(values[moved][span], backs[place])
                d_score = (prob * (d_prob - row_sums[head : head + 1])).astype(BF16)
                d_query_t[place] = d_query_t[place] + dot_nn(keys_t[moved][:, span], d_score)
                probs.append(prob.astype(BF16))
                d_scores.append(d_score)
            if owners[0] == owners[1]:
                dv_sum[owners[0], span] += dot_nn(
                    jnp.concatenate(probs, axis=1), jnp.concatenate(backs, axis=0)
                )
                dk_sum[owners[0], span] += dot_nn(
                    jnp.concatenate(d_scores, axis=1), jnp.concatenate(queries, axis=0)
                )
            else:
                for place in range(2):
                    dv_sum[owners[place], span] += dot_nn(probs[place], backs[place])
                    dk_sum[owners[place], span] += dot_nn(d_scores[place], queries[place])
        d_query = jnp.where(upper_t, d_query_t[1], d_query_t[0]).T * SCALE
        dq_ref[:, at] = (d_query * cosine - swap_halves(d_query) * sine).astype(BF16)
    lower_key = lane_of((4 * rows, LANES)) < HD
    for total, begin in ((dk_sum, 0), (dv_sum, LANES)):
        first, second = total[0], total[1]
        first = first + pltpu.roll(first, HD, 1)
        second = second + pltpu.roll(second, HD, 1)
        both = jnp.where(lower_key, first, second)
        cols = slice(begin, begin + LANES)
        own_ref[:, cols] = both[:rows]
        for place, ref in enumerate((core_ref, x_ref, far_ref)):
            ref[:, cols] = both[(place + 1) * rows : (place + 2) * rows].astype(BF16)


def parts_of(rows, cols):
    shapes = [jax.ShapeDtypeStruct((rows, cols), F32)] + [jax.ShapeDtypeStruct((rows, cols), BF16)] * 3
    return [seq_rows(0, rows, cols)] * 4, shapes


def attend_back(block, q, kv_pieces, back, out, level, start, cosine, sine, rows, seq):
    width = q.shape[1]
    length = 4 * rows
    heads = width // HD
    specs, shapes = parts_of(rows, 2 * LANES)
    return pl.pallas_call(
        attend_back_kernel,
        grid=(1,),
        in_specs=[
            pl.BlockSpec(memory_space=pltpu.SMEM),
            seq_rows(seq, rows, width),
            *[piece_of(seq, rows)] * 4,
            seq_rows(0, rows, width),
            seq_rows(0, rows, width),
            seq_rows(0, rows, LANES),
            pl.BlockSpec((1, 8, rows), lambda i: (seq, 0, 0)),
            seq_rows(seq, rows, LANES),
            seq_rows(seq, rows, LANES),
        ],
        out_specs=[seq_rows(0, rows, width), *specs],
        out_shape=[jax.ShapeDtypeStruct((rows, width), BF16), *shapes],
        scratch_shapes=[
            pltpu.VMEM((2, length, LANES), F32),
            pltpu.VMEM((2, length, LANES), F32),
        ],
        compiler_params=pltpu.CompilerParams(vmem_limit_bytes=VMEM_LIMIT),
        cost_estimate=pl.CostEstimate(
            flops=80 * rows * rows * LANES * heads,
            bytes_accessed=8 * rows * width,
            transcendentals=4 * rows * rows * heads,
        ),
        name="attention_backward",
    )(block, q, *kv_pieces, back, out, level, start, cosine, sine)


def mlp_kernel(
    n_0, n_1, n_2, n_3, c_0, c_1, c_2, c_3, w_ref,
    own_ref, out_1, out_2, out_3, d_own_ref, d_1, d_2, d_3, kept_ref, turned_ref,
    normed_all, cot_all,
):
    step = pl.program_id(0)
    rows = own_ref.shape[0]
    columns = w_ref.shape[1] // 3

    @pl.when(step == 0)
    def _():
        for place, (n_ref, c_ref) in enumerate(zip((n_0, n_1, n_2, n_3), (c_0, c_1, c_2, c_3))):
            normed_all[place // 2, (place % 2) * rows : (place % 2 + 1) * rows] = n_ref[...]
            cot_all[place // 2, (place % 2) * rows : (place % 2 + 1) * rows] = c_ref[...]

    normed, cot = normed_all[step], cot_all[step]
    gate = dot_nn(normed, w_ref[:, :columns])
    up = dot_nn(normed, w_ref[:, columns : 2 * columns])
    d_act = dot_nn(cot, w_ref[:, 2 * columns :])
    sigmoid = 0.5 * jnp.tanh(0.5 * gate) + 0.5
    swish = gate * sigmoid
    kept_ref[0] = (d_act * up * (sigmoid + swish * (1.0 - sigmoid))).astype(BF16)
    kept_ref[1] = (d_act * swish).astype(BF16)
    kept_ref[2] = (swish * up).astype(BF16)
    turned_ref[0] = normed.T
    turned_ref[1] = cot.T
    out = dot_nt(kept_ref[2], w_ref[:, 2 * columns :])
    d_normed = dot_nt(kept_ref[0], w_ref[:, :columns]) + dot_nt(kept_ref[1], w_ref[:, columns : 2 * columns])

    @pl.when(step == 0)
    def _():
        own_ref[...] = out[:rows]
        out_1[...] = out[rows:].astype(BF16)
        d_own_ref[...] = d_normed[:rows]
        d_1[...] = d_normed[rows:].astype(BF16)

    @pl.when(step == 1)
    def _():
        out_2[...] = out[:rows].astype(BF16)
        out_3[...] = out[rows:].astype(BF16)
        d_2[...] = d_normed[:rows].astype(BF16)
        d_3[...] = d_normed[rows:].astype(BF16)


def mlp(normed, cot, weights, seq):
    rows, dim = normed[0].shape
    columns = weights.shape[1] // 3
    specs, shapes = parts_of(rows, dim)
    once = lambda at: pl.BlockSpec((rows, dim), lambda i: (at, 0), pipeline_mode=pl.Buffered(1))
    return pl.pallas_call(
        mlp_kernel,
        grid=(2,),
        in_specs=[
            *[once(0)] * 4,
            *[once(seq)] * 3,
            once(0),
            pl.BlockSpec(weights.shape, lambda i: (0, 0), pipeline_mode=pl.Buffered(1)),
        ],
        out_specs=[
            *specs,
            *specs,
            pl.BlockSpec((3, 2 * rows, columns), lambda i: (0, i, 0)),
            pl.BlockSpec((2, dim, 2 * rows), lambda i: (0, 0, i)),
        ],
        out_shape=[
            *shapes,
            *shapes,
            jax.ShapeDtypeStruct((3, 4 * rows, columns), BF16),
            jax.ShapeDtypeStruct((2, dim, 4 * rows), BF16),
        ],
        scratch_shapes=[
            pltpu.VMEM((2, 2 * rows, dim), BF16),
            pltpu.VMEM((2, 2 * rows, dim), BF16),
        ],
        compiler_params=pltpu.CompilerParams(vmem_limit_bytes=VMEM_LIMIT),
        cost_estimate=pl.CostEstimate(
            flops=48 * rows * dim * columns,
            bytes_accessed=6 * dim * columns + 24 * rows * columns,
            transcendentals=4 * rows * columns,
        ),
        name="feed_forward",
    )(*normed, *cot, weights)


def mlp_grad_kernel(turned_0, turned_1, kept_0, kept_1, grad_ref):
    grad_ref[...] = (dot_nn(turned_0[0], kept_0[0]) + dot_nn(turned_1[0], kept_1[0])).astype(BF16)


def mlp_grad(turned, kept):
    _, dim, count = turned[0].shape
    columns = kept[0].shape[2]
    turned_block = pl.BlockSpec((1, dim, count), lambda i: (i // 2, 0, 0))
    kept_block = pl.BlockSpec((1, count, columns), lambda i: (i, 0, 0))
    return pl.pallas_call(
        mlp_grad_kernel,
        grid=(3,),
        in_specs=[turned_block, turned_block, kept_block, kept_block],
        out_specs=pl.BlockSpec((dim, columns), lambda i: (0, i)),
        out_shape=jax.ShapeDtypeStruct((dim, 3 * columns), BF16),
        compiler_params=pltpu.CompilerParams(vmem_limit_bytes=VMEM_LIMIT),
        cost_estimate=pl.CostEstimate(
            flops=12 * count * dim * columns,
            bytes_accessed=6 * dim * columns + 12 * count * columns,
            transcendentals=0,
        ),
        name="feed_forward_gradients",
    )(*turned, *kept)


def pack_kernel(block_ref, gate_ref, up_ref, down_ref, *refs):
    out_refs, scratch = refs[:4], refs[4]
    shard, ff = gate_ref.shape
    quarter = scratch.shape[2] // 4
    for place, ref in enumerate((gate_ref, up_ref, down_ref)):
        scratch[place, :, :ff] = ref[...].astype(F32)
        scratch[place, :, ff:] = jnp.zeros((shard, 4 * quarter - ff), F32)
    for place, out_ref in enumerate(out_refs):
        begin = pl.multiple_of((block_ref[0] ^ place) * quarter, LANES)
        for part in range(3):
            out_ref[:, part * quarter : (part + 1) * quarter] = scratch[part, :, pl.ds(begin, quarter)].astype(BF16)


def pack(block, gate, up, down_t, quarter):
    shard = gate.shape[0]
    return pl.pallas_call(
        pack_kernel,
        in_specs=[pl.BlockSpec(memory_space=pltpu.SMEM)] + [pl.BlockSpec(memory_space=pltpu.VMEM)] * 3,
        out_specs=[pl.BlockSpec(memory_space=pltpu.VMEM)] * 4,
        out_shape=[jax.ShapeDtypeStruct((shard, 3 * quarter), BF16)] * 4,
        scratch_shapes=[pltpu.VMEM((3, shard, 4 * quarter), F32)],
        compiler_params=pltpu.CompilerParams(vmem_limit_bytes=VMEM_LIMIT),
        name="pack_columns",
    )(block, gate, up, down_t)


def pick(options, index):
    value = options[0]
    for place in range(1, len(options)):
        value = jnp.where(index == place, options[place], value)
    return value


def assemble_kernel(block_ref, *refs):
    pieces, out_ref, scratch = refs[:4], refs[4], refs[5]
    shard = pieces[0].shape[0]
    values = [ref[...].astype(F32) for ref in pieces]
    for owner in range(4):
        scratch[owner * shard : (owner + 1) * shard] = pick(values, block_ref[0] ^ owner)
    out_ref[...] = scratch[...].astype(BF16)


def assemble(block, pieces):
    shard, columns = pieces[0].shape
    return pl.pallas_call(
        assemble_kernel,
        in_specs=[pl.BlockSpec(memory_space=pltpu.SMEM)] + [pl.BlockSpec(memory_space=pltpu.VMEM)] * 4,
        out_specs=pl.BlockSpec(memory_space=pltpu.VMEM),
        out_shape=jax.ShapeDtypeStruct((4 * shard, columns), BF16),
        scratch_shapes=[pltpu.VMEM((4 * shard, columns), F32)],
        compiler_params=pltpu.CompilerParams(vmem_limit_bytes=VMEM_LIMIT),
        name="assemble_rows",
    )(block, *pieces)


def cut_kernel(block_ref, value_ref, *refs):
    out_refs, scratch = refs[:4], refs[4]
    shard = out_refs[0].shape[0]
    scratch[...] = value_ref[...].astype(F32)
    values = [scratch[owner * shard : (owner + 1) * shard] for owner in range(4)]
    for place, out_ref in enumerate(out_refs):
        out_ref[...] = pick(values, block_ref[0] ^ place).astype(BF16)


def cut(block, value):
    shard, columns = value.shape[0] // 4, value.shape[1]
    return pl.pallas_call(
        cut_kernel,
        in_specs=[pl.BlockSpec(memory_space=pltpu.SMEM), pl.BlockSpec(memory_space=pltpu.VMEM)],
        out_specs=[pl.BlockSpec(memory_space=pltpu.VMEM)] * 4,
        out_shape=[jax.ShapeDtypeStruct((shard, columns), BF16)] * 4,
        scratch_shapes=[pltpu.VMEM(value.shape, F32)],
        compiler_params=pltpu.CompilerParams(vmem_limit_bytes=VMEM_LIMIT),
        name="cut_rows",
    )(block, value)


def unpack_kernel(block_ref, *refs):
    pieces, out_refs, scratch = refs[:4], refs[4:7], refs[7]
    ff = out_refs[0].shape[1]
    quarter = scratch.shape[2] // 4
    for place, ref in enumerate(pieces):
        begin = pl.multiple_of((block_ref[0] ^ place) * quarter, LANES)
        for part in range(3):
            scratch[part, :, pl.ds(begin, quarter)] = ref[:, part * quarter : (part + 1) * quarter].astype(F32)
    for part, out_ref in enumerate(out_refs):
        out_ref[...] = scratch[part, :, :ff]


def unpack(block, pieces, ff):
    shard, columns = pieces[0].shape
    return pl.pallas_call(
        unpack_kernel,
        in_specs=[pl.BlockSpec(memory_space=pltpu.SMEM)] + [pl.BlockSpec(memory_space=pltpu.VMEM)] * 4,
        out_specs=[pl.BlockSpec(memory_space=pltpu.VMEM)] * 3,
        out_shape=[jax.ShapeDtypeStruct((shard, ff), F32)] * 3,
        scratch_shapes=[pltpu.VMEM((3, shard, columns // 3 * 4), F32)],
        compiler_params=pltpu.CompilerParams(vmem_limit_bytes=VMEM_LIMIT),
        name="unpack_columns",
    )(block, *pieces)


def bit_swap(value, axis, bit=0):
    size = lax.axis_size(axis)
    return lax.ppermute(value, axis, [(i, i ^ (1 << bit)) for i in range(size)])


def jump_swap(value, axes, jump):
    return lax.ppermute(value, axes, [(i, i ^ jump) for i in range(4)])


def to_plane(value, slot):
    high, low = slot >> 1, slot & 1
    pairs = [
        (4 * y + 2 * x + c, 4 * (c ^ low) + 2 * (x ^ high) + y) for y in range(2) for x in range(2) for c in range(2)
    ]
    return lax.ppermute(value, TOKENS + ("cc",), pairs)


def from_plane(value, slot):
    high, low = slot >> 1, slot & 1
    pairs = [
        (4 * y + 2 * x + c, 4 * c + 2 * (x ^ high) + (y ^ low)) for y in range(2) for x in range(2) for c in range(2)
    ]
    return lax.ppermute(value, TOKENS + ("cc",), pairs)


def after(first, *values):
    return lax.optimization_barrier((first, *values))


def gather_four(value, axes):
    from_first = bit_swap(value, axes[0])
    return [value, bit_swap(value, axes[1]), from_first, bit_swap(from_first, axes[1])]


def gather_direct(value, axes):
    return [value] + [jump_swap(value, axes, jump) for jump in range(1, 4)]


def sum_direct(axes, own, *away):
    return [own] + [jump_swap(value, axes, jump + 1) for jump, value in enumerate(away)]


def doubling_offsets(steps):
    weight = {"cc": 1, "cx": 2, "fy": 4, "fz": 8}
    offsets = [0]
    for axis, bit in steps:
        offsets += [offset ^ (weight[axis] << bit) for offset in offsets]
    return jnp.array(offsets, jnp.int32)


def double(value, axis, bit=0):
    return jnp.concatenate([value, bit_swap(value, axis, bit)], axis=0)


def plane_gather(value):
    return jnp.concatenate(gather_direct(value, TOKENS), axis=0)


def plane_sum(value):
    parts = jnp.split(value, 4, axis=0)
    terms = sum_direct(TOKENS, *parts)
    return sum(term.astype(F32) for term in terms).astype(BF16)


def core_sum(keep, send):
    return (keep.astype(F32) + bit_swap(send.astype(BF16), "cc").astype(F32)).astype(BF16)


def halve(value, axis, bit=0):
    middle = value.shape[0] // 2
    came = bit_swap(value[middle:], axis, bit)
    return (value[:middle].astype(F32) + came.astype(F32)).astype(BF16)


def on_device(
    hidden,
    segments,
    attn_gain,
    qkv_weight,
    qkv_bias,
    out_weight,
    mlp_gain,
    gate_weight,
    up_weight,
    down_weight,
    cotangent,
):
    seqs, rows, dim = hidden.shape
    count = seqs * rows
    shard = attn_gain.shape[0]
    world = dim // shard
    joint = qkv_weight.shape[1]
    width = joint - 2 * LANES
    ff = gate_weight.shape[1]
    block = lax.axis_index("cx") * lax.axis_size("cc") + lax.axis_index("cc")
    me = lax.axis_index(FSDP) * lax.axis_size(CTX) + block
    offset = block * rows
    block_arg = block.reshape(1).astype(jnp.int32)
    plane_arg = (lax.axis_index("cx") * 2 + lax.axis_index("fy")).reshape(1).astype(jnp.int32)
    x = hidden.reshape(count, dim)
    cot = cotangent.reshape(count, dim)

    cot_x = bit_swap(cot, "cx")

    far = [("fz", bit) for bit in reversed(range((lax.axis_size("fz")).bit_length() - 1))]
    padded = -(-(shard + 1) // 16) * 16
    small = jnp.concatenate([attn_gain, mlp_gain, qkv_bias])
    small_row = jnp.pad(small, (0, joint + width - small.shape[0]))[None]
    first = jnp.concatenate(
        [
            jnp.concatenate([qkv_weight, out_weight.T], axis=1),
            small_row,
            jnp.zeros((padded - shard - 1, joint + width), BF16),
        ],
        axis=0,
    )
    first = double(first, *far[0])

    quarter = -(-ff // (4 * TILE)) * TILE
    first, *pieces = after(first, *pack(block_arg, gate_weight, up_weight, down_weight.T, quarter))
    pieces = [to_plane(piece, slot) for slot, piece in enumerate(pieces)]
    for axis, bit in far[1:]:
        first = double(first, axis, bit)

    within = jnp.arange(padded, dtype=jnp.int32)
    owner = me ^ doubling_offsets(far + [("cx", 0), ("fy", 0), ("cc", 0)])
    target = jnp.where(within[None, :] < shard, owner[:, None] * shard + within[None, :], -1).reshape(1, -1)
    order = (jnp.arange(dim, dtype=jnp.int32)[:, None] == target).astype(BF16)
    place = jnp.where(within[None, :] == shard, owner[:, None], -1).reshape(1, -1)
    spread = (jnp.arange(world, dtype=jnp.int32)[:, None] == place).astype(BF16)

    at_row = lax.dynamic_slice_in_dim(segments, offset, rows, axis=1)
    zeros_before = jnp.sum((segments < 1).astype(jnp.int32), axis=1, keepdims=True)
    ones_before = jnp.sum((segments < 2).astype(jnp.int32), axis=1, keepdims=True)
    start = jnp.where(at_row == 0, 0, jnp.where(at_row == 1, zeros_before, ones_before))
    position = (offset + jnp.arange(rows, dtype=jnp.int32)[None, :] - start).reshape(count)
    lane = jnp.arange(LANES, dtype=jnp.int32)
    frequency = ROPE_BASE ** (-(lane % (HD // 2)).astype(F32) * 2.0 / HD)
    angle = position.astype(F32)[:, None] * frequency[None, :]
    cosine = jnp.cos(angle)
    sine = jnp.where(lane % HD < HD // 2, -1.0, 1.0)[None, :] * jnp.sin(angle)
    start_column = jnp.broadcast_to(start.reshape(count, 1), (count, LANES))
    start_row = jnp.broadcast_to(start[:, None, :], (seqs, 8, rows))

    first, cot_x, cot_late, order, spread, cosine, sine, start_column, *pieces = after(
        first, cot_x, cot, order, spread, cosine, sine, start_column, *pieces
    )
    w_joint = plane_gather(first[:, :joint])
    mlp_shard = assemble(plane_arg, pieces)
    mlp_weights = lax.all_gather(mlp_shard, WEIGHTS, axis=0, tiled=True)
    w_joint, cot_late = after(w_joint, cot_late)
    w_joint = (w_joint, bit_swap(w_joint, "cc"))
    cot_y = bit_swap(cot_late, "fy")

    normed_low, normed_high, q, kv, gain_attn, gain_mlp = prep(x, order, spread, w_joint, cosine, sine, rows)
    kv_all = gather_four(kv.reshape(seqs, rows, 2 * LANES), CTX)
    kv_all[3], out_rows, cot_y = after(kv_all[3], first[:, joint:], cot_y)
    w_out = plane_gather(out_rows)
    attended, levels, resid, normed_all = [], [], [], []
    for seq in range(seqs):
        turn = block_arg if seq == 0 else after(resid[0], block_arg)[1]
        attended_one, level_one = attend(turn, q, kv_all, start_column, rows, seq)
        if seq == 0:
            attended_one, w_out, far_0, far_1 = after(attended_one, w_out, cot_x[:rows], cot_y[rows:])
            cot_far = [bit_swap(far_0, "fy"), bit_swap(far_1, "cx")]
            w_out = (w_out, bit_swap(w_out, "cc"))
        else:
            attended_one, *cot_far = after(attended_one, *cot_far)
        attended.append(attended_one)
        levels.append(level_one)
        resid_one, normed_one = project_out(attended[seq], x, w_out, order, gain_mlp, rows, seq)
        resid.append(resid_one)
        normed_all.append(gather_direct(normed_one, TOKENS))

    out_parts, d_terms, kept, turned = [], [], [], []
    for seq in range(seqs):
        if seq == 1:
            out_parts[0], normed_all[1] = lax.optimization_barrier((out_parts[0], normed_all[1]))
        result = mlp(normed_all[seq], [cot, cot_x, cot_y, cot_far[seq]], mlp_weights, seq)
        out_parts.append(result[:4])
        d_terms.append(sum_direct(TOKENS, *result[4:8]))
        kept.append(result[8])
        turned.append(result[9])
    d_resid, d_low, d_high, d_attended, mlp_gain_grad, dq, dkv_terms, out_terms = [], [], [], [], [], [], [], []
    for seq in range(seqs):
        if seq == 0:
            _, *d_terms[0] = after(kept[1], *d_terms[0])
        else:
            dq[0], d_terms[1][0], *out_terms[0] = after(dq[0], d_terms[1][0], *out_terms[0])
        result = project_out_back(d_terms[seq], resid[seq], cot, w_out, order, gain_mlp, rows, seq)
        for place, value in zip((d_resid, d_low, d_high, d_attended, mlp_gain_grad), result):
            place.append(value)
        out_terms.append(sum_direct(TOKENS, *after(d_terms[seq][1], *out_parts[seq])[1:]))
        if seq == 0:
            _, turned[1] = after(d_resid[0], turned[1])
            grads = mlp_grad(turned, kept)
            grads, d_attended[0], *d_terms[1] = after(grads, d_attended[0], *d_terms[1])
            grads = lax.psum_scatter(
                grads.reshape(world // 4, 4 * shard, 3 * quarter), WEIGHTS, scatter_dimension=0, tiled=False
            )
        else:
            both = jnp.concatenate(attended, axis=0)
            out_grad = core_sum(
                dot_tn(jnp.concatenate(d_low, axis=0), both).astype(BF16), dot_tn(jnp.concatenate(d_high, axis=0), both)
            )
            d_attended[1], *dkv_terms[0] = after(d_attended[1], *dkv_terms[0])
        result = attend_back(
            block_arg, q, kv_all, d_attended[seq], attended[seq], levels[seq], start_row, cosine, sine, rows, seq
        )
        dq.append(result[0])
        dkv_terms.append(sum_direct(CTX, *result[1:]))
    dq[1], out_grad, *out_terms[1] = after(dq[1], out_grad, *out_terms[1])
    dq_both = jnp.concatenate(dq, axis=0)
    q_grad = core_sum(dot_tn(normed_low, dq_both).astype(BF16), dot_tn(normed_high, dq_both))
    q_grad, *dkv_terms[1] = after(q_grad, *dkv_terms[1])
    q_grad = plane_sum(q_grad)
    d_resid = jnp.concatenate(d_resid, axis=0)
    d_kv, input_grad, attn_gain_grad, bias_grad = input_back(
        dq, dkv_terms, x, d_resid, w_joint, order, gain_attn, cosine, sine
    )
    d_kv, q_grad, attn_gain_grad, bias_grad = after(d_kv, q_grad, attn_gain_grad, bias_grad)

    split_at = width + LANES
    bias_grad = bias_grad[0]
    small_grads = jnp.concatenate(
        [
            attn_gain_grad.reshape(world, -1),
            sum(mlp_gain_grad).reshape(world, -1),
            bias_grad[:split_at].reshape(world, -1),
            bias_grad[split_at:].reshape(world, -1),
        ],
        axis=1,
    ).astype(BF16)
    small_count = small_grads.shape[1]
    small_grads = jnp.pad(small_grads, ((0, 0), (0, 2 * LANES - small_count)))
    middle = spread.shape[1] // 2
    kv_grad = core_sum(
        (dot_tn(normed_low, d_kv) + dot_tn(spread[:, :middle], small_grads)).astype(BF16),
        dot_tn(normed_high, d_kv) + dot_tn(spread[:, middle:], small_grads),
    )
    pieces = cut(plane_arg, lax.optimization_barrier(grads))
    kv_grad, *pieces = after(kv_grad, *pieces)
    pieces = [from_plane(piece, slot) for slot, piece in enumerate(pieces)]
    kv_grad, out_grad = plane_sum(kv_grad), plane_sum(out_grad)
    first_sum = jnp.concatenate([q_grad, kv_grad, out_grad], axis=1)
    first_sum, out_terms = lax.optimization_barrier((first_sum, out_terms))
    for axis, bit in reversed(far):
        first_sum = halve(first_sum, axis, bit)
    output = []
    for seq in range(seqs):
        own, *away = out_terms[seq]
        output.append((resid[seq] + own + sum(term.astype(F32) for term in away)).astype(BF16))

    gate_grad, up_grad, down_grad_t = unpack(block_arg, pieces, ff)
    first_sum = first_sum.astype(F32)
    qkv_sum, out_sum = first_sum[:, :joint], first_sum[:, joint:]
    small_sum = qkv_sum[shard, width : width + small_count]
    at = (shard, 2 * shard, 2 * shard + split_at // world)

    return (
        jnp.stack(output),
        input_grad.reshape(hidden.shape),
        small_sum[: at[0]],
        qkv_sum[:shard],
        small_sum[at[1] : at[2]],
        small_sum[at[2] :],
        out_sum[:shard].T,
        small_sum[at[0] : at[1]],
        gate_grad,
        up_grad,
        down_grad_t.T,
    )


def solution(mesh):
    fsdp, ctx = mesh.shape["fsdp"], mesh.shape["ctx"]
    inner = Mesh(mesh.devices.reshape(fsdp // 2, 2, 2, ctx // 2), AXES)
    tokens = P(FSDP, CTX, None)
    vector = P(AXES)
    by_row = P(AXES, None)
    by_column = P(None, AXES)
    return jax.shard_map(
        on_device,
        mesh=inner,
        in_specs=(
            tokens,
            P(FSDP, None),
            vector,
            by_row,
            vector,
            by_column,
            vector,
            by_row,
            by_row,
            by_column,
            tokens,
        ),
        out_specs=(
            tokens,
            tokens,
            vector,
            by_row,
            vector,
            vector,
            by_column,
            vector,
            by_row,
            by_row,
            by_column,
        ),
        check_vma=False,
    )
```
